32 devices in a mesh: tower: 2 (over core), dp: 16 (over z, y, x).
Axes of the slice: x: 2, y: 2, z: 4, core: 2. Of those that a mesh axis runs over, the one named last changes fastest.
Arguments:
- latent: bfloat16 [32768, 256], P('dp'), may hold values from -6 to 6
- codes: int32 [2, 32768], P('tower', 'dp'), may hold values from 0 to 31, as said below
- targets: int32 [2, 3, 32768], P('tower', None, 'dp'), may hold values from 0 to 600, as said below
- visits: int32 [2, 32768, 4], P('tower', 'dp'), may hold values from 1 to 64
- importance: int32 [32768], P('dp'), may hold values from 1 to 1536
- params: float32 [2, 1054464], P('tower', 'dp'), as said below
- first_moment: float32 [2, 1054464], P('tower', 'dp')
- second_moment: float32 [2, 1054464], P('tower', 'dp'), as said below
Outputs:
- states: bfloat16 [2, 32768, 256], P('tower', 'dp')
- input_grad: float32 [2, 32768, 256], P('tower', 'dp')
- new_first: float32 [2, 1054464], P('tower', 'dp')
- new_second: float32 [2, 1054464], P('tower', 'dp')
- new_params: float32 [2, 1054464], P('tower', 'dp')
- params_low: bfloat16 [2, 1054464], P('tower', 'dp')
- norms: float32 [2, 2, 12], P('tower')
The draws below stay inside these ranges and needn't reach their ends.
Inputs may be any that keep to these rules, and one draw needn't show every extreme that they name: codes[0] holds actions below 4, codes[1] chance codes. targets[t, 2] lies below 32. `params`: flat master parameters in the stated layout. `second_moment`: positive.
All inputs are finite; a program needn't handle non-finite values.
Results may differ from the reference program's by a relative error of at most 0.01.
The reference program's roundings to bfloat16 on the way count: a program that leaves them out, or rounds other values in their place, can miss the bound.
Values may be sent and summed in bfloat16 or wider, within the bound.
A program may use at most 320 MiB of HBM per device.

```python
import math
import jax
import jax.numpy as jnp
from jax import lax

D = 256
CODES = 32
ACTIONS = 4
BINS = 601
BLOCKS = 10
MICRO = 4
STEP = 5
ROWS_DEV = 2048
TOKENS = 32768
HEADS = 1238
MATS = 12
P_SIZE = 1054464


def region_ends():
    first_end = (D + CODES) * D
    block_end = first_end + BLOCKS * D * D
    head_end = block_end + D * HEADS
    return (first_end, block_end, head_end)


def grad_size(position):
    first_end, block_end, head_end = region_ends()
    factor = jnp.where(position < block_end, 1.0, jnp.where(position < head_end, 0.15, 3.0))
    return factor * (2.0 / math.sqrt(TOKENS))


def draw_params(key, part):
    key = jax.random.fold_in(key, 11)
    noise = jax.random.normal(key, (2, P_SIZE), jnp.float32)
    first_end, block_end, head_end = region_ends()
    position = jnp.arange(P_SIZE)[None, :]
    matrix_scale = jnp.where(position < D * D, D ** (-0.5), jnp.where(position < first_end, 0.5, D ** (-0.5)))
    inner = position - head_end
    kind_index = inner // ((BLOCKS + 1) * D)
    column = (inner % D).astype(jnp.float32)
    gain_value = (0.5 + column / D) * (1.0 + 0.1 * noise)
    vector_part = jnp.where(kind_index == 0, gain_value, 0.3 * noise)
    return jnp.where(position < head_end, matrix_scale * noise, vector_part).astype(jnp.float32)


def draw_first_moment(key, part):
    key = jax.random.fold_in(key, 12)
    noise = jax.random.normal(key, (2, P_SIZE), jnp.float32)
    return (noise * grad_size(jnp.arange(P_SIZE))[None, :]).astype(jnp.float32)


def draw_second_moment(key, part):
    key = jax.random.fold_in(key, 13)
    spread = jnp.exp(jax.random.uniform(key, (2, P_SIZE), jnp.float32, 0.0, math.log(4.0)))
    scale_now = grad_size(jnp.arange(P_SIZE))[None, :]
    return (spread * scale_now * scale_now).astype(jnp.float32)


def draw_codes(key, part):
    key = jax.random.fold_in(key, 21)
    raw_codes = jax.random.randint(key, (2, TOKENS), 0, CODES)
    tower_row = jnp.arange(2)[:, None]
    return jnp.where(tower_row == 0, raw_codes % ACTIONS, raw_codes).astype(jnp.int32)


def draw_targets(key, part):
    key = jax.random.fold_in(key, 22)
    raw_bins = jax.random.randint(key, (2, 3, TOKENS), 0, BINS)
    group_row = jnp.arange(3)[None, :, None]
    return jnp.where(group_row == 2, raw_bins % CODES, raw_bins).astype(jnp.int32)


def draw_importance(key, part):
    key = jax.random.fold_in(key, 23)
    first_key, second_key = jax.random.split(key)
    base_value = jax.random.randint(first_key, (TOKENS,), 1, 9)
    power = jax.random.randint(second_key, (TOKENS,), 0, 7)
    band = 1 + 3 * jnp.arange(TOKENS) // TOKENS
    values = base_value * jnp.left_shift(jnp.ones_like(power), power) * band
    values = values.at[0].set(1).at[TOKENS - 1].set(1536)
    return values.astype(jnp.int32)


def place_ends(result, stream_key, smallest, largest):
    longest = result.shape.index(max(result.shape))
    spots = []
    for shift in (0, 1):
        where = [jax.random.randint(jax.random.fold_in(stream_key, axis), (), 0, length) for axis, length in enumerate(result.shape)]
        where[longest] = (where[longest] + shift) % result.shape[longest]
        spots.append(tuple(where))
    return result.at[spots[0]].set(smallest).at[spots[1]].set(largest)


def block_levels(rng, dims, cuts, least, high):
    def one(dim, blocks):
        heights = jax.random.uniform(jax.random.fold_in(jax.random.fold_in(rng, 6), dim), (blocks,), jnp.float32, least / len(cuts), high / len(cuts))
        return jnp.repeat(jnp.exp(heights), dims[dim] // blocks).reshape((-1,) + (1,) * (len(dims) - dim - 1))

    level = one(*cuts[0])
    for cut in cuts[1:]:
        level = level * one(*cut)
    return level


def bell_draw(own_key, dims, scale, reach, shards=(), dtype=jnp.bfloat16):
    loudness = block_levels(own_key, dims, shards, -0.22, 0.18) if shards else 1.0
    result = jax.random.normal(own_key, dims, jnp.float32) * scale * loudness
    return jnp.minimum(jnp.maximum(result, -reach), reach).astype(dtype)


def setup_inputs(seed: int = 0) -> dict:
    splits = jax.random.split(jax.random.key(seed), 9)
    latent = bell_draw(splits[0], (TOKENS, D), 1.0, 6.0, ((0, 16),))
    codes = draw_codes(jax.random.fold_in(splits[8], 71), 0)
    targets = draw_targets(jax.random.fold_in(splits[8], 71), 0)
    visits = place_ends(jax.random.randint(splits[3], (2, TOKENS, ACTIONS), 1, 65), jax.random.fold_in(splits[3], 1), 1, 64).astype(jnp.int32)
    importance = draw_importance(jax.random.fold_in(splits[8], 71), 0)
    params = draw_params(jax.random.fold_in(splits[8], 71), 0)
    first_moment = draw_first_moment(jax.random.fold_in(splits[8], 71), 0)
    second_moment = draw_second_moment(jax.random.fold_in(splits[8], 71), 0)
    return {"latent": latent, "codes": codes, "targets": targets, "visits": visits, "importance": importance, "params": params, "first_moment": first_moment, "second_moment": second_moment}


@jax.custom_vjp
def low(v):
    return lax.optimization_barrier(v.astype(jnp.bfloat16)).astype(jnp.float32)

@jax.custom_vjp
def low_back(v):
    return v

def low_keep(v):
    return (low(v), None)

def low_pass(kept, grad):
    return (grad,)

def back_keep(v):
    return (v, None)

def back_low(kept, grad):
    return (low(grad),)
low.defvjp(low_keep, low_pass)
low_back.defvjp(back_keep, back_low)
learn_rate = 0.5

def matmul(left, right):
    return jnp.dot(left, right, precision=lax.Precision.HIGHEST, preferred_element_type=jnp.float32)

def layer_norm(values):
    center = values - lax.optimization_barrier(jnp.mean(values, -1, keepdims=True))
    return center * lax.rsqrt(lax.optimization_barrier(jnp.mean(center * center, -1, keepdims=True)) + 1e-05)

def activate(values):
    return jax.nn.gelu(values, approximate=True)

def unpack(flat_params):
    first_end = (D + CODES) * D
    block_end = first_end + BLOCKS * D * D
    head_end = block_end + D * HEADS
    w_cat = flat_params[:first_end].reshape(D + CODES, D)
    w_blocks = flat_params[first_end:block_end].reshape(BLOCKS, D, D)
    w_head = flat_params[block_end:head_end].reshape(D, HEADS)
    vectors = flat_params[head_end:].reshape(3, BLOCKS + 1, D)
    return (w_cat, w_blocks, w_head, vectors)

def segment_of(position):
    first_end = (D + CODES) * D
    block_end = first_end + BLOCKS * D * D
    head_end = block_end + D * HEADS
    inner = jnp.where(position < block_end, 1 + (position - first_end) // (D * D), BLOCKS + 1)
    return jnp.where(position < first_end, 0, jnp.where(position < head_end, inner, BLOCKS + 2)).astype(jnp.int32)

def tower_pass(flat_params, inputs_now, code_now):
    w_cat, w_blocks, w_head, vectors = unpack(flat_params)
    onehot = (code_now[:, None] == jnp.arange(CODES)[None, :]).astype(jnp.float32)
    joined = jnp.concatenate([inputs_now, onehot], 1)
    pre_norm = low_back(matmul(joined, w_cat)) + vectors[2, 0]
    stream = activate(layer_norm(pre_norm) * vectors[0, 0] + vectors[1, 0])
    for phase_no in range(BLOCKS):
        mixed = low(activate(layer_norm(stream) * vectors[0, phase_no + 1] + vectors[1, phase_no + 1]))
        stream = stream + low_back(matmul(mixed, w_blocks[phase_no])) + vectors[2, phase_no + 1]
    return stream

def log_sum(section):
    top_value = lax.optimization_barrier(jnp.max(section, -1, keepdims=True))
    return (top_value + jnp.log(lax.optimization_barrier(jnp.sum(jnp.exp(section - top_value), -1, keepdims=True))))[:, 0]

def head_loss(flat_params, head_input, target_now, visit_now, weight_now):
    w_head = unpack(flat_params)[2]
    logits = low_back(matmul(head_input, w_head))
    starts = (0, BINS, 2 * BINS)
    widths = (BINS, BINS, CODES)
    per_row = jnp.zeros((head_input.shape[0],), jnp.float32)
    for group_no in range(3):
        section = logits[:, starts[group_no]:starts[group_no] + widths[group_no]]
        chosen = (target_now[group_no][:, None] == jnp.arange(widths[group_no])[None, :]).astype(jnp.float32)
        per_row = per_row + log_sum(section) - lax.optimization_barrier(jnp.sum(chosen * section, -1))
    policy = logits[:, 2 * BINS + CODES:]
    counts = visit_now.astype(jnp.float32)
    shares = counts / lax.optimization_barrier(jnp.sum(counts, -1, keepdims=True))
    per_row = per_row + log_sum(policy) - lax.optimization_barrier(jnp.sum(shares * policy, -1))
    return jnp.sum(weight_now * per_row)

def reference(latent, codes, targets, visits, importance, params, first_moment, second_moment):
    block_rows = ROWS_DEV // MICRO
    block_count = TOKENS // block_rows
    weight_sum = jnp.sum(importance.astype(jnp.float32))
    row_weight = importance.astype(jnp.float32) / weight_sum
    latent_full = latent.astype(jnp.float32)
    nudge = jnp.zeros_like(latent_full)

    def whole(param_full, latent_in, nudge_in):
        low_params = low(param_full)

        def one_block(carry, pieces):
            inputs_now, nudge_now, code_now, target_now, visit_now, weight_now = pieces
            after = low(tower_pass(low_params[0], low(inputs_now), code_now[0]))
            loss_first = head_loss(low_params[0], after, target_now[0], visit_now[0], weight_now)
            chance_in = after + nudge_now
            following = low(tower_pass(low_params[1], chance_in, code_now[1]))
            loss_second = head_loss(low_params[1], following, target_now[1], visit_now[1], weight_now)
            return (carry + loss_first + loss_second, jnp.stack([after, following]))
        pieces = (latent_in.reshape(block_count, block_rows, D), nudge_in.reshape(block_count, block_rows, D), codes.reshape(2, block_count, block_rows).transpose(1, 0, 2), targets.reshape(2, 3, block_count, block_rows).transpose(2, 0, 1, 3), visits.reshape(2, block_count, block_rows, ACTIONS).transpose(1, 0, 2, 3), row_weight.reshape(block_count, block_rows))
        loss, stacked = lax.scan(jax.checkpoint(one_block), jnp.zeros((), jnp.float32), pieces)
        return (loss, stacked)
    loss, pullback, stacked = jax.vjp(whole, params, latent_full, nudge, has_aux=True)
    grad_params, grad_latent, grad_nudge = pullback(jnp.ones((), jnp.float32))
    states = stacked.transpose(1, 0, 2, 3).reshape(2, TOKENS, D).astype(jnp.bfloat16)
    input_grad = jnp.stack([grad_latent, grad_nudge])
    first_new = 0.5 * first_moment + 0.5 * grad_params
    second_new = 0.5 * second_moment + 0.5 * grad_params * grad_params
    correction = 1.0 - 0.5 ** STEP
    segment = segment_of(jnp.arange(P_SIZE))
    is_matrix = (segment < MATS)[None, :]
    update = first_new / correction / (jnp.sqrt(second_new / correction) + 1e-06) + jnp.where(is_matrix, 0.01 * params, 0.0)
    member = (segment[:, None] == jnp.arange(MATS)[None, :]).astype(jnp.float32)
    weight_norm = jnp.sqrt(matmul(params * params, member))
    update_norm = jnp.sqrt(matmul(update * update, member))
    ratio = jnp.where(is_matrix, matmul(weight_norm / update_norm, member.T), 1.0)
    new_params = params - learn_rate * ratio * update
    norms = jnp.stack([weight_norm, update_norm], 1)
    return (states, input_grad, first_new, second_new, new_params, new_params.astype(jnp.bfloat16), norms)
```

```python
import jax
import jax.numpy as jnp
from jax import lax
from jax.experimental import pallas as pl
from jax.experimental.pallas import tpu as pltpu
from jax.sharding import PartitionSpec as P

D = 256
CODES = 32
BINS = 601
BLOCKS = 10
STEP = 5
HEADS = 1238
MATS = 12
P_SIZE = 1054464
HPAD = 1280
CAT = D + CODES
A_ROWS = CAT + BLOCKS * D
BF = jnp.bfloat16
F32 = jnp.float32
GELU_C = 0.7978845608028654
GELU_K = 0.044715


def nn(a, b):
    return jnp.dot(a, b, preferred_element_type=F32)


def nt(a, b):
    return lax.dot_general(a, b, (((1,), (1,)), ((), ())), preferred_element_type=F32)


def identity(n):
    return (lax.broadcasted_iota(jnp.int32, (n, n), 0) == lax.broadcasted_iota(jnp.int32, (n, n), 1)).astype(BF)


def twice(v):
    return jnp.concatenate([v, v], 1)


def column_stats(ref, cs):
    total = jnp.sum(ref[:, cs], axis=0, keepdims=True)
    mean = total * (1.0 / D)
    square = jnp.zeros((8, mean.shape[1]), F32)
    for r in range(0, D, 32):
        cen = ref[r : r + 32, cs] - mean
        square = square + jnp.sum((cen * cen).reshape(4, 8, -1), axis=0)
    var = jnp.sum(square, axis=0, keepdims=True) * (1.0 / D)
    return mean, lax.rsqrt(var + 1e-05)


def norm_act(src, cs, gsb, xh_ref, gp_ref, rstd_ref, out):
    mean, rstd = column_stats(src, cs)
    rstd_ref[:, cs] = jnp.broadcast_to(rstd, (8, rstd.shape[1]))
    for r in range(0, D, 32):
        rs = slice(r, r + 32)
        xh = (src[rs, cs] - mean) * rstd
        xh_ref[rs, cs] = xh.astype(BF)
        y = xh * twice(gsb[rs, 0:128]) + twice(gsb[rs, 128:256])
        y2 = y * y
        p = y2 * (GELU_C * GELU_K) + GELU_C
        t = jnp.tanh(y * p)
        q = t * 0.5 + 0.5
        a = y * q
        out(rs, a)
        slope = q + (a - a * q) * (p * 6.0 - 4.0 * GELU_C)
        gp_ref[rs, cs] = slope.astype(BF)


def broadcast_vectors(vt, rows):
    k = lax.broadcasted_iota(jnp.int32, (128, 128), 0)
    picks = jnp.concatenate([(k == row).astype(BF) for row in rows], 1)
    return nn(vt, picks)


def head_stage(cs, lg, dl, ints, rw):
    width = rw.shape[1]
    it8 = lax.broadcasted_iota(jnp.int32, (8, width), 0)
    low = -jnp.inf
    b75, b150, b154 = lg[600:608], lg[1200:1208], lg[1232:1240]

    def top(block):
        return jnp.max(block, axis=0, keepdims=True)

    def top_range(lo, hi):
        best = lg[lo : lo + 8]
        for r in range(lo + 8, hi, 8):
            best = jnp.maximum(best, lg[r : r + 8])
        return best

    max_v = top(jnp.maximum(top_range(0, 600), jnp.where(it8 < 1, b75, low)))
    max_r = top(
        jnp.maximum(
            jnp.maximum(top_range(608, 1200), jnp.where(it8 >= 1, b75, low)),
            jnp.where(it8 < 2, b150, low),
        )
    )
    max_c = top(
        jnp.maximum(
            jnp.maximum(top_range(1208, 1232), jnp.where(it8 >= 2, b150, low)),
            jnp.where(it8 < 2, b154, low),
        )
    )
    in_policy = (it8 >= 2) & (it8 < 6)
    max_p = top(jnp.where(in_policy, b154, low))

    def exp_range(lo, hi, best):
        acc = jnp.zeros((8, width), F32)
        for r in range(lo, hi, 8):
            e = jnp.exp(lg[r : r + 8] - best)
            lg[r : r + 8] = e
            acc = acc + e
        return acc

    e75 = jnp.exp(b75 - jnp.where(it8 < 1, max_v, max_r))
    e150 = jnp.exp(b150 - jnp.where(it8 < 2, max_r, max_c))
    e154 = jnp.exp(b154 - jnp.where(it8 < 2, max_c, max_p))

    def total(acc):
        return rw / jnp.sum(acc, axis=0, keepdims=True)

    inv_v = total(exp_range(0, 600, max_v) + jnp.where(it8 < 1, e75, 0.0))
    inv_r = total(exp_range(608, 1200, max_r) + jnp.where(it8 >= 1, e75, 0.0) + jnp.where(it8 < 2, e150, 0.0))
    inv_c = total(exp_range(1208, 1232, max_c) + jnp.where(it8 >= 2, e150, 0.0) + jnp.where(it8 < 2, e154, 0.0))
    inv_p = total(jnp.where(in_policy, e154, 0.0))
    hit_v = ints[1:2]
    hit_r = ints[6:7] + BINS
    hit_c = ints[7:8] + 2 * BINS
    counts = jnp.where(in_policy, ints.astype(F32), 0.0)
    share = counts * (rw / jnp.sum(counts, axis=0, keepdims=True))

    def minus(value, lo, *hits):
        at = lax.broadcasted_iota(jnp.int32, value.shape, 0)
        for hit in hits:
            value = value - jnp.where(at == hit - lo, rw, 0.0)
        return value

    d75 = minus(e75 * jnp.where(it8 < 1, inv_v, inv_r), 600, hit_v, hit_r)
    d150 = minus(e150 * jnp.where(it8 < 2, inv_r, inv_c), 1200, hit_r, hit_c)
    d154 = minus(e154 * jnp.where(it8 < 2, inv_c, inv_p), 1232, hit_c) - share
    d154 = jnp.where(it8 < 6, d154, 0.0)

    def emit(lo, hi, inv, hit):
        for r in range(lo, hi, 16):
            dl[r : r + 16, cs] = minus(lg[r : r + 16] * inv, r, hit).astype(BF)

    def pair(first, second):
        return jnp.concatenate([first, second], 0).astype(BF)

    emit(0, 592, inv_v, hit_v)
    dl[592:608, cs] = pair(minus(lg[592:600] * inv_v, 592, hit_v), d75)
    emit(608, 1200, inv_r, hit_r)
    dl[1200:1216, cs] = pair(d150, minus(lg[1208:1216] * inv_c, 1208, hit_c))
    emit(1216, 1232, inv_c, hit_c)
    dl[1232:1248, cs] = pair(d154, jnp.zeros_like(d154))
    dl[1248:HPAD, cs] = jnp.zeros((HPAD - 1248, width), BF)


CB = 256


def forward_tower(t, refs):
    (eye, w, wh, vec, wct, wt, vt, gsb, xt, mix, xh, gp, rstd, stream, ints, width) = refs
    blocks = range(0, width, CB)
    for cs in (slice(c, c + CB) for c in blocks):
        it = lax.broadcasted_iota(jnp.int32, (CODES, CB), 0)
        xt[t, D:CAT, cs] = (it == ints[t, 0:1, cs]).astype(BF)
        xt[t, CAT : CAT + 16, cs] = jnp.ones((16, CB), BF)
    vt[...] = nt(eye[...], vec[t]).astype(BF)
    wt[...] = nt(eye[...], w[t, 0:D]).astype(BF)
    wct[...] = nt(eye[...], w[t, D:CAT]).astype(BF)
    gsb[...] = broadcast_vectors(vt[...], (0, BLOCKS + 1, 2 * BLOCKS + 2))
    for cs in (slice(c, c + CB) for c in blocks):
        pre = nn(wt[...], xt[t, 0:D, cs]) + nn(wct[...], xt[t, D:CAT, cs])
        stream[:, cs] = pre + twice(gsb[:, 256:384])

        def keep(rs, a):
            stream[rs, cs] = a

        norm_act(stream, cs, gsb, xh.at[t, 0], gp.at[t, 0], rstd.at[t, 0], keep)

    @pl.loop(1, BLOCKS + 1)
    def _(k):
        gsb[...] = broadcast_vectors(vt[...], (k, k + BLOCKS + 1, k + 2 * BLOCKS + 2))
        row = pl.multiple_of(CAT + (k - 1) * D, 32)
        wt[...] = nt(eye[...], w[t, pl.ds(row, D)]).astype(BF)
        for cs in (slice(c, c + CB) for c in blocks):

            def keep(rs, a):
                mix[t, k - 1, rs, cs] = a.astype(BF)

            norm_act(stream, cs, gsb, xh.at[t, k], gp.at[t, k], rstd.at[t, k], keep)
            pre = nn(wt[...], mix[t, k - 1, 0:D, cs])
            stream[:, cs] = stream[:, cs] + pre + twice(gsb[:, 256:384])
        mix[t, k - 1, D : D + 16, :] = jnp.ones((16, width), BF)

    for c in blocks:
        cs = slice(c, c + CB)
        xt[t + 1, 0:D, cs] = stream[:, cs].astype(BF)


def backward_act(cs, grad_ref, gp_ref, xh_ref, dy16, dyx16):
    for r in range(0, D, 32):
        rs = slice(r, r + 32)
        dy = grad_ref[rs, :] * gp_ref[rs, cs].astype(F32)
        grad_ref[rs, :] = dy
        dy16[rs, cs] = dy.astype(BF)
        dyx16[rs, cs] = (dy * xh_ref[rs, cs].astype(F32)).astype(BF)


def backward_tower(t, refs):
    (eye, w, wh, vec, wht, vt, gsb, xt, mix, xh, gp, rstd, ds, ex, br, dy16, dyx16, dm, lg, dl, ints, rw, gw, gh, gv, ig, width) = refs
    blocks = range(0, width, CB)
    vt[...] = nt(eye[...], vec[t]).astype(BF)
    for h in range(0, HPAD, D):
        wht[h : h + D, :] = nt(eye[...], wh[t, :, h : h + D]).astype(BF)

    @pl.loop(0, width // CB)
    def _(c):
        cs = pl.ds(pl.multiple_of(c * CB, CB), CB)
        lg[...] = nn(wht[...], xt[t + 1, 0:D, cs])
        head_stage(cs, lg, dl, ints[t, :, cs], rw[0:1, cs])
        ds[:, cs] = nn(wh[t], dl[:, cs]) + ex[:, cs]

    gh[t] = nt(xt[t + 1, 0:D, :], dl[...]).astype(BF)
    def stage(k, first):
        gsb[:, 0:128] = broadcast_vectors(vt[...], (k,))
        pick = (lax.broadcasted_iota(jnp.int32, (16, 128), 1) == k).astype(BF)
        g16 = nt(pick, vt[...]).astype(BF)
        for i, c in enumerate(blocks):
            cs = slice(c, c + CB)
            buf = dm.at[i % 2]
            if first:
                buf[...] = ds[:, cs]
            else:
                row = pl.multiple_of(CAT + (k - 1) * D, 32)
                br[:, cs] = ds[:, cs].astype(BF)
                buf[...] = nn(w[t, pl.ds(row, D)], br[:, cs])
            backward_act(cs, buf, gp.at[t, k], xh.at[t, k], dy16, dyx16)
            m1 = nn(g16, dy16[:, cs])[0:1] * (1.0 / D)
            m2 = nn(g16, dyx16[:, cs])[0:1] * (1.0 / D)
            rs1 = rstd[t, k, 0:1, cs]
            m1 = m1 * rs1
            m2 = m2 * rs1
            for r in range(0, D, 32):
                rs = slice(r, r + 32)
                back = (buf[rs, :] * twice(gsb[rs, 0:128])) * rs1 - m1 - xh[t, k, rs, cs].astype(F32) * m2
                if first:
                    br[rs, cs] = back.astype(BF)
                else:
                    ds[rs, cs] = ds[rs, cs] + back
        ones = jnp.ones((16, width), BF)
        gv[t, 0, pl.ds(k, 1), :] = nt(ones, dyx16[...])[0:1]
        gv[t, 1, pl.ds(k, 1), :] = nt(ones, dy16[...])[0:1]

    @pl.loop(0, BLOCKS)
    def _(i):
        k = BLOCKS - i
        stage(k, False)
        full = nt(mix[t, k - 1], br[...])
        row = pl.multiple_of(CAT + (k - 1) * D, 32)
        gw[t, pl.ds(row, D), :] = full[0:D].astype(BF)
        gv[t, 2, pl.ds(k, 1), :] = full[D : D + 1]

    stage(0, True)
    full = nt(xt[t], br[...])
    gw[t, 0:CAT, :] = full[0:CAT].astype(BF)
    gv[t, 2, 0:1, :] = full[CAT : CAT + 1]
    for c in blocks:
        cs = slice(c, c + CB)
        back = nn(w[t, 0:D], br[:, cs])
        ex[:, cs] = back
        ig[t, cs, :] = back.T


def compute_kernel(x_ref, ints, rw, w, wh, vec, st, ig, gw, gh, gv, eye, wct, wt, wht, vt, gsb, xt, mix, xh, gp, rstd, stream, ex, br, dy16, dyx16, dm, lg, dl):
    width = x_ref.shape[0]
    eye[...] = identity(D)
    for c in range(0, width, CB):
        cs = slice(c, c + CB)
        xt[0, 0:D, cs] = nt(eye[...], x_ref[cs, :]).astype(BF)
    fwd = (eye, w, wh, vec, wct, wt, vt, gsb, xt, mix, xh, gp, rstd, stream, ints, width)
    bwd = (eye, w, wh, vec, wht, vt, gsb, xt, mix, xh, gp, rstd, stream, ex, br, dy16, dyx16, dm, lg, dl, ints, rw, gw, gh, gv, ig, width)

    @pl.loop(0, 2)
    def _(t):
        forward_tower(t, fwd)

        @pl.loop(0, width // CB)
        def _(c):
            cs = pl.ds(pl.multiple_of(c * CB, CB), CB)
            st[t, cs, :] = nt(eye[...], xt[t + 1, 0:D, cs]).astype(BF)

    ex[...] = jnp.zeros_like(ex)

    @pl.loop(0, 2)
    def _(i):
        backward_tower(1 - i, bwd)


def compute(x, ints, rw, w, wh, vec):
    width = x.shape[0]
    vm = pl.BlockSpec(memory_space=pltpu.VMEM)
    return pl.pallas_call(
        compute_kernel,
        out_shape=(
            jax.ShapeDtypeStruct((2, width, D), BF),
            jax.ShapeDtypeStruct((2, width, D), F32),
            jax.ShapeDtypeStruct((2, A_ROWS, D), BF),
            jax.ShapeDtypeStruct((2, D, HPAD), BF),
            jax.ShapeDtypeStruct((2, 3, 16, D), F32),
        ),
        in_specs=[vm] * 6,
        out_specs=(vm,) * 5,
        scratch_shapes=[
            pltpu.VMEM((D, D), BF),
            pltpu.VMEM((D, CODES), BF),
            pltpu.VMEM((D, D), BF),
            pltpu.VMEM((HPAD, D), BF),
            pltpu.VMEM((D, 128), BF),
            pltpu.VMEM((D, 384), F32),
            pltpu.VMEM((3, CAT + 16, width), BF),
            pltpu.VMEM((2, BLOCKS, D + 16, width), BF),
            pltpu.VMEM((2, BLOCKS + 1, D, width), BF),
            pltpu.VMEM((2, BLOCKS + 1, D, width), BF),
            pltpu.VMEM((2, BLOCKS + 1, 8, width), F32),
            pltpu.VMEM((D, width), F32),
            pltpu.VMEM((D, width), F32),
            pltpu.VMEM((D, width), BF),
            pltpu.VMEM((D, width), BF),
            pltpu.VMEM((D, width), BF),
            pltpu.VMEM((2, D, CB), F32),
            pltpu.VMEM((HPAD, CB), F32),
            pltpu.VMEM((HPAD, width), BF),
        ],
        compiler_params=pltpu.CompilerParams(vmem_limit_bytes=62 * 1024 * 1024),
    )(x, ints, rw, w, wh, vec)


def segment_of(position):
    first_end = (D + CODES) * D
    block_end = first_end + BLOCKS * D * D
    head_end = block_end + D * HEADS
    inner = jnp.where(position < block_end, 1 + (position - first_end) // (D * D), BLOCKS + 1)
    return jnp.where(position < first_end, 0, jnp.where(position < head_end, inner, BLOCKS + 2))


def swap(x):
    return lax.ppermute(x, "tower", [(0, 1), (1, 0)])


def unpack_all(flat):
    block_end = A_ROWS * D
    head_end = block_end + D * HEADS
    w = flat[:, :block_end].reshape(2, A_ROWS, D)
    wh = jnp.pad(flat[:, block_end:head_end].reshape(2, D, HEADS), ((0, 0), (0, 0), (0, HPAD - HEADS)))
    vec = jnp.pad(flat[:, head_end:].reshape(2, 3 * BLOCKS + 3, D), ((0, 0), (0, 128 - 3 * BLOCKS - 3), (0, 0)))
    return w, wh, vec


def on_device(latent, codes, targets, visits, importance, params, first_moment, second_moment):
    me = lax.axis_index("tower")
    is_first = me == 0
    row_count = latent.shape[0]
    half = row_count // 2
    shard_len = params.shape[1]
    weight_sum = lax.psum(jnp.sum(importance.astype(F32)), "dp")
    low = params[0].astype(BF)
    flat = lax.all_gather(low, ("tower", "dp"), axis=0, tiled=True).reshape(2, P_SIZE)
    w, wh, vec = unpack_all(flat)
    ints = jnp.concatenate([codes, targets[0, :1], visits[0].T, targets[0, 1:]], 0)
    mine = lax.dynamic_slice_in_dim(ints, me * half, half, 1)
    other = swap(lax.dynamic_slice_in_dim(ints, (1 - me) * half, half, 1))
    both = jnp.where(is_first, jnp.stack([mine, other]), jnp.stack([other, mine]))
    x = lax.dynamic_slice_in_dim(latent, me * half, half, 0)
    rw = lax.dynamic_slice_in_dim(importance, me * half, half, 0).astype(F32) / weight_sum
    st, ig, gw, gh, gv = compute(x, both, jnp.broadcast_to(rw[None], (8, half)), w, wh, vec)

    def owned(parts):
        keep = lax.dynamic_index_in_dim(parts, me, 0, keepdims=False)
        got = swap(lax.dynamic_index_in_dim(parts, 1 - me, 0, keepdims=False))
        return jnp.where(is_first, jnp.concatenate([keep, got]), jnp.concatenate([got, keep]))

    states_out = owned(st)
    inputs_out = owned(ig)
    grads = jnp.concatenate(
        [
            gw.astype(F32).reshape(2, -1),
            gh[:, :, :HEADS].astype(F32).reshape(2, -1),
            gv[:, :, : BLOCKS + 1].reshape(2, -1),
        ],
        1,
    )
    grad_shard = lax.psum_scatter(grads.reshape(-1), ("tower", "dp"), scatter_dimension=0, tiled=True)
    master = params[0]
    correction = 1.0 - 0.5**STEP
    first_new = 0.5 * first_moment[0] + 0.5 * grad_shard
    second_new = 0.5 * second_moment[0] + 0.5 * grad_shard * grad_shard
    position = lax.axis_index("dp") * shard_len + jnp.arange(shard_len)
    segment = segment_of(position)
    is_matrix = segment < MATS
    update = first_new / correction / (jnp.sqrt(second_new / correction) + 1e-06) + jnp.where(
        is_matrix, 0.01 * master, 0.0
    )
    member = (segment[:, None] == jnp.arange(MATS)[None, :]).astype(F32)
    weight_part = jnp.dot(master * master, member, precision=lax.Precision.HIGHEST)
    update_part = jnp.dot(update * update, member, precision=lax.Precision.HIGHEST)
    weight_sq, update_sq = lax.psum((weight_part, update_part), "dp")
    weight_norm = jnp.sqrt(weight_sq)
    update_norm = jnp.sqrt(update_sq)
    ratio = jnp.where(
        is_matrix, jnp.dot(member, weight_norm / update_norm, precision=lax.Precision.HIGHEST), 1.0
    )
    new_params = master - 0.5 * ratio * update
    norms = jnp.stack([weight_norm, update_norm])[None]
    return (
        states_out[None],
        inputs_out[None],
        first_new[None],
        second_new[None],
        new_params[None],
        new_params.astype(BF)[None],
        norms,
    )


def solution(mesh):
    in_specs = (
        P("dp", None),
        P("tower", "dp"),
        P("tower", None, "dp"),
        P("tower", "dp", None),
        P("dp"),
        P("tower", "dp"),
        P("tower", "dp"),
        P("tower", "dp"),
    )
    out_specs = (
        P("tower", "dp", None),
        P("tower", "dp", None),
        P("tower", "dp"),
        P("tower", "dp"),
        P("tower", "dp"),
        P("tower", "dp"),
        P("tower", None, None),
    )
    return jax.shard_map(
        on_device, mesh=mesh, in_specs=in_specs, out_specs=out_specs, check_vma=False
    )
```

```python
import functools

import jax
import jax.numpy as jnp
from jax import lax
from jax.experimental import pallas as pl
from jax.experimental.pallas import tpu as pltpu
from jax.sharding import PartitionSpec as P

D = 256
CODES = 32
BINS = 601
BLOCKS = 10
STEP = 5
HEADS = 1238
MATS = 12
P_SIZE = 1054464
HPAD = 1280
CAT = D + CODES
A_ROWS = CAT + BLOCKS * D
BF = jnp.bfloat16
F32 = jnp.float32
GELU_C = 0.7978845608028654
GELU_K = 0.044715


def nn(a, b):
    return jnp.dot(a, b, preferred_element_type=F32)


def nt(a, b):
    return lax.dot_general(a, b, (((1,), (1,)), ((), ())), preferred_element_type=F32)


def identity(n):
    return (lax.broadcasted_iota(jnp.int32, (n, n), 0) == lax.broadcasted_iota(jnp.int32, (n, n), 1)).astype(BF)


def twice(v):
    return jnp.concatenate([v, v], 1)


def column_stats(ref, cs):
    total = jnp.sum(ref[:, cs], axis=0, keepdims=True)
    mean = total * (1.0 / D)
    square = jnp.zeros((8, mean.shape[1]), F32)
    for r in range(0, D, 32):
        cen = ref[r : r + 32, cs] - mean
        square = square + jnp.sum((cen * cen).reshape(4, 8, -1), axis=0)
    var = jnp.sum(square, axis=0, keepdims=True) * (1.0 / D)
    return mean, lax.rsqrt(var + 1e-05)


def norm_act(src, cs, gsb, xh_ref, gp_ref, rstd_ref, out):
    mean, rstd = column_stats(src, cs)
    rstd_ref[:, cs] = jnp.broadcast_to(rstd, (8, rstd.shape[1]))
    for r in range(0, D, 32):
        rs = slice(r, r + 32)
        xh = (src[rs, cs] - mean) * rstd
        xh_ref[rs, cs] = xh.astype(BF)
        y = xh * twice(gsb[rs, 0:128]) + twice(gsb[rs, 128:256])
        y2 = y * y
        p = y2 * (GELU_C * GELU_K) + GELU_C
        t = jnp.tanh(y * p)
        q = t * 0.5 + 0.5
        a = y * q
        out(rs, a)
        slope = q + (a - a * q) * (p * 6.0 - 4.0 * GELU_C)
        gp_ref[rs, cs] = slope.astype(BF)


def broadcast_vectors(vt, rows):
    k = lax.broadcasted_iota(jnp.int32, (128, 128), 0)
    picks = jnp.concatenate([(k == row).astype(BF) for row in rows], 1)
    return nn(vt, picks)


def head_stage(cs, lg, dl, ints, rw):
    width = rw.shape[1]
    it8 = lax.broadcasted_iota(jnp.int32, (8, width), 0)
    low = -jnp.inf
    b75, b150, b154 = lg[600:608], lg[1200:1208], lg[1232:1240]

    def top(block):
        return jnp.max(block, axis=0, keepdims=True)

    def top_range(lo, hi):
        best = lg[lo : lo + 8]
        for r in range(lo + 8, hi, 8):
            best = jnp.maximum(best, lg[r : r + 8])
        return best

    max_v = top(jnp.maximum(top_range(0, 600), jnp.where(it8 < 1, b75, low)))
    max_r = top(
        jnp.maximum(
            jnp.maximum(top_range(608, 1200), jnp.where(it8 >= 1, b75, low)),
            jnp.where(it8 < 2, b150, low),
        )
    )
    max_c = top(
        jnp.maximum(
            jnp.maximum(top_range(1208, 1232), jnp.where(it8 >= 2, b150, low)),
            jnp.where(it8 < 2, b154, low),
        )
    )
    in_policy = (it8 >= 2) & (it8 < 6)
    max_p = top(jnp.where(in_policy, b154, low))

    def exp_range(lo, hi, best):
        acc = jnp.zeros((8, width), F32)
        for r in range(lo, hi, 8):
            e = jnp.exp(lg[r : r + 8] - best)
            lg[r : r + 8] = e
            acc = acc + e
        return acc

    e75 = jnp.exp(b75 - jnp.where(it8 < 1, max_v, max_r))
    e150 = jnp.exp(b150 - jnp.where(it8 < 2, max_r, max_c))
    e154 = jnp.exp(b154 - jnp.where(it8 < 2, max_c, max_p))

    def total(acc):
        return rw / jnp.sum(acc, axis=0, keepdims=True)

    inv_v = total(exp_range(0, 600, max_v) + jnp.where(it8 < 1, e75, 0.0))
    inv_r = total(exp_range(608, 1200, max_r) + jnp.where(it8 >= 1, e75, 0.0) + jnp.where(it8 < 2, e150, 0.0))
    inv_c = total(exp_range(1208, 1232, max_c) + jnp.where(it8 >= 2, e150, 0.0) + jnp.where(it8 < 2, e154, 0.0))
    inv_p = total(jnp.where(in_policy, e154, 0.0))
    hit_v = ints[1:2]
    hit_r = ints[6:7] + BINS
    hit_c = ints[7:8] + 2 * BINS
    counts = jnp.where(in_policy, ints.astype(F32), 0.0)
    share = counts * (rw / jnp.sum(counts, axis=0, keepdims=True))

    def minus(value, lo, *hits):
        at = lax.broadcasted_iota(jnp.int32, value.shape, 0)
        for hit in hits:
            value = value - jnp.where(at == hit - lo, rw, 0.0)
        return value

    d75 = minus(e75 * jnp.where(it8 < 1, inv_v, inv_r), 600, hit_v, hit_r)
    d150 = minus(e150 * jnp.where(it8 < 2, inv_r, inv_c), 1200, hit_r, hit_c)
    d154 = minus(e154 * jnp.where(it8 < 2, inv_c, inv_p), 1232, hit_c) - share
    d154 = jnp.where(it8 < 6, d154, 0.0)

    def emit(lo, hi, inv, hit):
        for r in range(lo, hi, 16):
            dl[r : r + 16, cs] = minus(lg[r : r + 16] * inv, r, hit).astype(BF)

    def pair(first, second):
        return jnp.concatenate([first, second], 0).astype(BF)

    emit(0, 592, inv_v, hit_v)
    dl[592:608, cs] = pair(minus(lg[592:600] * inv_v, 592, hit_v), d75)
    emit(608, 1200, inv_r, hit_r)
    dl[1200:1216, cs] = pair(d150, minus(lg[1208:1216] * inv_c, 1208, hit_c))
    emit(1216, 1232, inv_c, hit_c)
    dl[1232:1248, cs] = pair(d154, jnp.zeros_like(d154))
    dl[1248:HPAD, cs] = jnp.zeros((HPAD - 1248, width), BF)


CB = 256


def forward_tower(t, refs):
    (eye, w, wh, vec, wct, wt, vt, gsb, xt, mix, xh, gp, rstd, stream, ints, width) = refs
    blocks = range(0, width, CB)
    for cs in (slice(c, c + CB) for c in blocks):
        it = lax.broadcasted_iota(jnp.int32, (CODES, CB), 0)
        xt[t, D:CAT, cs] = (it == ints[t, 0:1, cs]).astype(BF)
        xt[t, CAT : CAT + 16, cs] = jnp.ones((16, CB), BF)
    vt[...] = nt(eye[...], vec[t]).astype(BF)
    wt[...] = nt(eye[...], w[t, 0:D]).astype(BF)
    wct[...] = nt(eye[...], w[t, D:CAT]).astype(BF)
    gsb[...] = broadcast_vectors(vt[...], (0, BLOCKS + 1, 2 * BLOCKS + 2))
    for cs in (slice(c, c + CB) for c in blocks):
        pre = nn(wt[...], xt[t, 0:D, cs]) + nn(wct[...], xt[t, D:CAT, cs])
        stream[:, cs] = pre + twice(gsb[:, 256:384])

        def keep(rs, a):
            stream[rs, cs] = a

        norm_act(stream, cs, gsb, xh.at[t, 0], gp.at[t, 0], rstd.at[t, 0], keep)

    @pl.loop(1, BLOCKS + 1)
    def _(k):
        gsb[...] = broadcast_vectors(vt[...], (k, k + BLOCKS + 1, k + 2 * BLOCKS + 2))
        row = pl.multiple_of(CAT + (k - 1) * D, 32)
        wt[...] = nt(eye[...], w[t, pl.ds(row, D)]).astype(BF)
        for cs in (slice(c, c + CB) for c in blocks):

            def keep(rs, a):
                mix[t, k - 1, rs, cs] = a.astype(BF)

            norm_act(stream, cs, gsb, xh.at[t, k], gp.at[t, k], rstd.at[t, k], keep)
            pre = nn(wt[...], mix[t, k - 1, 0:D, cs])
            stream[:, cs] = stream[:, cs] + pre + twice(gsb[:, 256:384])
        mix[t, k - 1, D : D + 16, :] = jnp.ones((16, width), BF)

    for c in blocks:
        cs = slice(c, c + CB)
        xt[t + 1, 0:D, cs] = stream[:, cs].astype(BF)


def backward_act(cs, grad_ref, gp_ref, xh_ref, dy16, dyx16):
    for r in range(0, D, 32):
        rs = slice(r, r + 32)
        dy = grad_ref[rs, :] * gp_ref[rs, cs].astype(F32)
        grad_ref[rs, :] = dy
        dy16[rs, cs] = dy.astype(BF)
        dyx16[rs, cs] = (dy * xh_ref[rs, cs].astype(F32)).astype(BF)


def backward_tower(t, refs):
    (eye, w, wh, vec, wht, vt, gsb, xt, mix, xh, gp, rstd, ds, ex, br, dy16, dyx16, dm, lg, dl, ints, rw, gw, gh, gv, ig, width) = refs
    blocks = range(0, width, CB)
    vt[...] = nt(eye[...], vec[t]).astype(BF)
    for h in range(0, HPAD, D):
        wht[h : h + D, :] = nt(eye[...], wh[t, :, h : h + D]).astype(BF)

    @pl.loop(0, width // CB)
    def _(c):
        cs = pl.ds(pl.multiple_of(c * CB, CB), CB)
        lg[...] = nn(wht[...], xt[t + 1, 0:D, cs])
        head_stage(cs, lg, dl, ints[t, :, cs], rw[0:1, cs])
        ds[:, cs] = nn(wh[t], dl[:, cs]) + ex[:, cs]

    gh[t] = nt(xt[t + 1, 0:D, :], dl[...]).astype(BF)
    def stage(k, first):
        gsb[:, 0:128] = broadcast_vectors(vt[...], (k,))
        pick = (lax.broadcasted_iota(jnp.int32, (16, 128), 1) == k).astype(BF)
        g16 = nt(pick, vt[...]).astype(BF)
        for i, c in enumerate(blocks):
            cs = slice(c, c + CB)
            buf = dm.at[i % 2]
            if first:
                buf[...] = ds[:, cs]
            else:
                row = pl.multiple_of(CAT + (k - 1) * D, 32)
                br[:, cs] = ds[:, cs].astype(BF)
                buf[...] = nn(w[t, pl.ds(row, D)], br[:, cs])
            backward_act(cs, buf, gp.at[t, k], xh.at[t, k], dy16, dyx16)
            m1 = nn(g16, dy16[:, cs])[0:1] * (1.0 / D)
            m2 = nn(g16, dyx16[:, cs])[0:1] * (1.0 / D)
            rs1 = rstd[t, k, 0:1, cs]
            m1 = m1 * rs1
            m2 = m2 * rs1
            for r in range(0, D, 32):
                rs = slice(r, r + 32)
                back = (buf[rs, :] * twice(gsb[rs, 0:128])) * rs1 - m1 - xh[t, k, rs, cs].astype(F32) * m2
                if first:
                    br[rs, cs] = back.astype(BF)
                else:
                    ds[rs, cs] = ds[rs, cs] + back
        ones = jnp.ones((16, width), BF)
        gv[t, 0, pl.ds(k, 1), :] = nt(ones, dyx16[...])[0:1]
        gv[t, 1, pl.ds(k, 1), :] = nt(ones, dy16[...])[0:1]

    @pl.loop(0, BLOCKS)
    def _(i):
        k = BLOCKS - i
        stage(k, False)
        full = nt(mix[t, k - 1], br[...])
        row = pl.multiple_of(CAT + (k - 1) * D, 32)
        gw[t, pl.ds(row, D), :] = full[0:D].astype(BF)
        gv[t, 2, pl.ds(k, 1), :] = full[D : D + 1]

    stage(0, True)
    full = nt(xt[t], br[...])
    gw[t, 0:CAT, :] = full[0:CAT].astype(BF)
    gv[t, 2, 0:1, :] = full[CAT : CAT + 1]
    for c in blocks:
        cs = slice(c, c + CB)
        back = nn(w[t, 0:D], br[:, cs])
        ex[:, cs] = back
        ig[t, cs, :] = back.T


def compute_kernel(x_ref, ints, rw, w, wh, vec, st, ig, gw, gh, gv, eye, wct, wt, wht, vt, gsb, xt, mix, xh, gp, rstd, stream, ex, br, dy16, dyx16, dm, lg, dl):
    width = x_ref.shape[0]
    eye[...] = identity(D)
    for c in range(0, width, CB):
        cs = slice(c, c + CB)
        xt[0, 0:D, cs] = nt(eye[...], x_ref[cs, :]).astype(BF)
    fwd = (eye, w, wh, vec, wct, wt, vt, gsb, xt, mix, xh, gp, rstd, stream, ints, width)
    bwd = (eye, w, wh, vec, wht, vt, gsb, xt, mix, xh, gp, rstd, stream, ex, br, dy16, dyx16, dm, lg, dl, ints, rw, gw, gh, gv, ig, width)

    @pl.loop(0, 2)
    def _(t):
        forward_tower(t, fwd)

        @pl.loop(0, width // CB)
        def _(c):
            cs = pl.ds(pl.multiple_of(c * CB, CB), CB)
            st[t, cs, :] = nt(eye[...], xt[t + 1, 0:D, cs]).astype(BF)

    ex[...] = jnp.zeros_like(ex)

    @pl.loop(0, 2)
    def _(i):
        backward_tower(1 - i, bwd)


def compute(x, ints, rw, w, wh, vec):
    width = x.shape[0]
    vm = pl.BlockSpec(memory_space=pltpu.VMEM)
    return pl.pallas_call(
        compute_kernel,
        out_shape=(
            jax.ShapeDtypeStruct((2, width, D), BF),
            jax.ShapeDtypeStruct((2, width, D), F32),
            jax.ShapeDtypeStruct((2, A_ROWS, D), BF),
            jax.ShapeDtypeStruct((2, D, HPAD), BF),
            jax.ShapeDtypeStruct((2, 3, 16, D), F32),
        ),
        in_specs=[vm] * 6,
        out_specs=(vm,) * 5,
        scratch_shapes=[
            pltpu.VMEM((D, D), BF),
            pltpu.VMEM((D, CODES), BF),
            pltpu.VMEM((D, D), BF),
            pltpu.VMEM((HPAD, D), BF),
            pltpu.VMEM((D, 128), BF),
            pltpu.VMEM((D, 384), F32),
            pltpu.VMEM((3, CAT + 16, width), BF),
            pltpu.VMEM((2, BLOCKS, D + 16, width), BF),
            pltpu.VMEM((2, BLOCKS + 1, D, width), BF),
            pltpu.VMEM((2, BLOCKS + 1, D, width), BF),
            pltpu.VMEM((2, BLOCKS + 1, 8, width), F32),
            pltpu.VMEM((D, width), F32),
            pltpu.VMEM((D, width), F32),
            pltpu.VMEM((D, width), BF),
            pltpu.VMEM((D, width), BF),
            pltpu.VMEM((D, width), BF),
            pltpu.VMEM((2, D, CB), F32),
            pltpu.VMEM((HPAD, CB), F32),
            pltpu.VMEM((HPAD, width), BF),
        ],
        compiler_params=pltpu.CompilerParams(vmem_limit_bytes=62 * 1024 * 1024),
    )(x, ints, rw, w, wh, vec)


class Plan:
    def __init__(self, n, length):
        self.n, self.length = n, length
        self.rows128 = -(-length // 128)
        block_end, head_end = A_ROWS * D, A_ROWS * D + D * HEADS
        self.a_base, self.a_rows, self.h_first, self.h_rows, self.h_off, self.v_first, self.v_rows, self.v_off = ([] for _ in range(8))
        used = 0
        for i in range(n):
            lo, hi = i * length, (i + 1) * length
            base = min(lo, block_end) // D // 16 * 16
            top = -(-min(hi, block_end) // D)
            a_rows = -(-(top - base) // 16) * 16 if lo < block_end else 0
            first = min(max(lo - block_end, 0), D * HEADS) // HEADS
            last = -(-min(max(hi - block_end, 0), D * HEADS) // HEADS)
            h_rows = last - first if hi > block_end and lo < head_end else 0
            v_first = max(lo - head_end, 0) // D
            v_rows = -(-(hi - head_end) // D) - v_first if hi > head_end else 0
            self.a_base.append(base)
            self.a_rows.append(a_rows)
            self.h_first.append(first)
            self.h_rows.append(h_rows)
            self.h_off.append(a_rows)
            self.v_first.append(v_first)
            self.v_rows.append(v_rows)
            self.v_off.append(a_rows + 5 * h_rows)
            used = max(used, a_rows + 5 * h_rows + v_rows)
        self.slot = -(-(used + 1) // 32) * 32

    def at(self, table, me):
        value = jnp.int32(table[0])
        for i in range(1, self.n):
            if table[i] != table[i - 1]:
                value = value + (me >= i).astype(jnp.int32) * (table[i] - table[i - 1])
        return value


MESH = pl.DeviceIdType.MESH


def neighbours(n):
    core = lax.axis_index("tower")
    me = lax.axis_index("dp")
    near_x = me + 1 - 2 * (me % 2)
    near_y = me + 2 - 4 * ((me // 2) % 2)
    return core, me, near_x, near_y


def at(core, index):
    return {"tower": core, "dp": index}


def greet(core, me, near_x, near_y, n):
    barrier = pltpu.get_barrier_semaphore()
    pl.semaphore_signal(barrier, inc=1, device_id=at(1 - core, me), device_id_type=MESH)
    for near in (near_x, near_y):
        pl.semaphore_signal(barrier, inc=1, device_id=at(core, near), device_id_type=MESH)
    for k in range(1, n // 4):
        pl.semaphore_signal(barrier, inc=1, device_id=at(core, (me + 4 * k) % n), device_id_type=MESH)
    return barrier


def place_shard(plan, me, p_ref, slot128, shifted, rolled):
    rows = plan.rows128
    start = me * plan.length
    shift = start % 128
    first = start // 128
    tall = shifted.shape[0]
    height = p_ref.shape[0]
    lane = lax.broadcasted_iota(jnp.int32, (height, 128), 1)
    rolled[0:8] = jnp.zeros((8, 128), F32)
    rolled[8 : 8 + height] = pltpu.roll(p_ref[...], shift, 1)
    shifted[...] = jnp.zeros((tall, 128), F32)
    moved = jnp.where(lane >= shift, rolled[8 : 8 + height], rolled[7 : 7 + height])
    shifted[16 : 16 + height] = moved
    slot128[...] = jnp.zeros(slot128.shape, F32)
    row = lax.broadcasted_iota(jnp.int32, (height, 128), 0)
    base = plan.at(plan.a_base, me)

    @pl.when(plan.at(plan.a_rows, me) > 0)
    def _():
        slot128[pl.ds(first - 2 * base, height)] = jnp.where(row + first < 2 * A_ROWS, moved, 0.0)

    h_first, h_rows, h_off = (plan.at(t, me) for t in (plan.h_first, plan.h_rows, plan.h_off))
    it = lax.broadcasted_iota(jnp.int32, (10, 128), 0)
    lane10 = lax.broadcasted_iota(jnp.int32, (10, 128), 1)

    @pl.loop(0, h_rows)
    def _(k):
        begin = A_ROWS * D + HEADS * (h_first + k) - 128 * first + 128 * 16
        turn = begin % 128
        window = pltpu.roll(shifted[pl.ds(begin // 128, 16)], (128 - turn) % 128, 1)
        value = jnp.where(lane10 < 128 - turn, window[0:10], window[1:11])
        slot128[pl.ds(2 * h_off + 10 * k, 10)] = jnp.where(it * 128 + lane10 < HEADS, value, 0.0)

    v_start = (A_ROWS * D + D * HEADS) // 128
    v_rows, v_off, v_first = (plan.at(t, me) for t in (plan.v_rows, plan.v_off, plan.v_first))
    tall_v = min(height, -(-2 * max(plan.v_rows) // 8) * 8)

    @pl.when(v_rows > 0)
    def _():
        inside = plan.at([max(0, v_start - i * plan.length // 128) for i in range(plan.n)], me)
        to = 2 * v_off + first + inside - v_start - 2 * v_first
        slot128[pl.ds(to, tall_v)] = shifted[pl.ds(16 + inside, tall_v)]


def unpack_slot(plan, i, slot, w, whf, vecf, scratch):
    base, rows = plan.a_base[i], plan.a_rows[i]
    if rows:
        shared = i > 0 and base < plan.a_base[i - 1] + plan.a_rows[i - 1]
        lo = 0
        if shared:
            w[base : base + 16] = w[base : base + 16] + slot[0:16]
            lo = 16
        if rows > lo:
            w[base + lo : base + rows] = slot[lo:rows]
    h_rows, h_off, h_first = plan.h_rows[i], plan.h_off[i], plan.h_first[i]
    v_rows, v_off, v_first = plan.v_rows[i], plan.v_off[i], plan.v_first[i]
    if h_rows or v_rows:
        value = slot[...].astype(F32)
        scratch[0] = value[:, 0:128]
        scratch[1] = value[:, 128:D]
    if h_rows:
        shared = i > 0 and plan.h_rows[i - 1] and plan.h_first[i - 1] + plan.h_rows[i - 1] > h_first
        for j in range(5):
            for half in range(2):
                cols = slice(D * j + 128 * half, D * j + 128 * half + 128)
                value = scratch[half, pl.ds(h_off + j, h_rows, stride=5)]
                if shared:
                    whf[h_first : h_first + 1, cols] = whf[h_first : h_first + 1, cols] + value[0:1]
                    if h_rows > 1:
                        whf[h_first + 1 : h_first + h_rows, cols] = value[1:h_rows]
                else:
                    whf[h_first : h_first + h_rows, cols] = value
    if v_rows:
        shared = v_first and plan.v_first[i - 1] + plan.v_rows[i - 1] > v_first
        shared = shared or (i > 0 and plan.v_rows[i - 1] > 0 and v_first == 0)
        for half in range(2):
            cols = slice(128 * half, 128 * half + 128)
            value = scratch[half, v_off : v_off + v_rows]
            if shared:
                vecf[v_first : v_first + 1, cols] = vecf[v_first : v_first + 1, cols] + value[0:1]
                if v_rows > 1:
                    vecf[v_first + 1 : v_first + v_rows, cols] = value[1:v_rows]
            else:
                vecf[v_first : v_first + v_rows, cols] = value


def split3(value):
    hi = value.astype(BF).astype(F32)
    mid = (value - hi).astype(BF).astype(F32)
    return hi, mid, value - hi - mid


def gather_kernel(plan, p_ref, ints_ref, imp_ref, w, wh, vec, both, rw, slots, slot128, shifted, rolled, scratch, whf, vecf, send, recv):
    n = plan.n
    depth = n // 4
    core, me, near_x, near_y = neighbours(n)
    barrier = greet(core, me, near_x, near_y, n)
    place_shard(plan, me, p_ref, slot128, shifted, rolled)
    pl.semaphore_wait(barrier, depth + 2)
    half = rw.shape[1]
    started = []

    def copy(src, dst, slot, to):
        c = pltpu.make_async_remote_copy(
            src_ref=src, dst_ref=dst, send_sem=send.at[slot], recv_sem=recv.at[slot], device_id=to, device_id_type=MESH
        )
        c.start()
        started.append(c)
        return c

    mine = pl.multiple_of(core * half, half)
    theirs = pl.multiple_of((1 - core) * half, half)
    number = iter(range(1 << 20))
    ints_copy = copy(ints_ref.at[:, pl.ds(theirs, half)], both.at[core], next(number), at(1 - core, me))
    rows = plan.slot
    total = jnp.sum(imp_ref[...].astype(F32), axis=1, keepdims=True)
    lane = lax.broadcasted_iota(jnp.int32, (1, D), 1)
    hi, mid, lo = split3(total)
    left = slot128[pl.ds(0, rows, stride=2)]
    right = slot128[pl.ds(1, rows, stride=2)]
    own = jnp.concatenate([left, right], 1)
    last = jnp.where(lane == 0, hi, jnp.where(lane == 1, mid, jnp.where(lane == 2, lo, 0.0)))
    last_row = lax.broadcasted_iota(jnp.int32, (rows, D), 0) == rows - 1
    slots[core, me] = jnp.where(last_row, last, own).astype(BF)

    def column(index, k):
        return (index + n - 4 * k) % n

    def send_slot(origin, to, lo=0, hi=rows):
        ref = slots.at[core, origin, pl.ds(lo, hi - lo)]
        return copy(ref, ref, next(number), to)

    near_xy = near_x + near_y - me
    cut = rows // 2
    z_in, x_in, y_in, d_in, s_in = {}, {}, {}, {}, []
    for k in sorted(range(1, depth), key=lambda k: (min(k, depth - k), k)):
        z_in[k] = send_slot(me, at(core, (me + 4 * k) % n))
    order = [0] + list(z_in)
    for k in order:
        if k:
            z_in[k].wait_recv()
        x_in[k] = send_slot(column(me, k), at(core, near_x))
        y_in[k] = send_slot(column(me, k), at(core, near_y))
        s_in.append(send_slot(column(me, k), at(1 - core, me)))
    for k in order:
        x_in[k].wait_recv()
        first = send_slot(column(near_x, k), at(core, near_y), 0, cut)
        s_in.append(send_slot(column(near_x, k), at(1 - core, me)))
        y_in[k].wait_recv()
        second = send_slot(column(near_y, k), at(core, near_x), cut, rows)
        s_in.append(send_slot(column(near_y, k), at(1 - core, me)))
        d_in[k] = (first, second)
    for k in order:
        for c in d_in[k]:
            c.wait_recv()
        s_in.append(send_slot(column(near_xy, k), at(1 - core, me)))
    ints_copy.wait_recv()
    both[core] = ints_ref[:, pl.ds(mine, half)]
    for c in s_in:
        c.wait_recv()
    for c in started:
        c.wait_send()
    whf[:, 1152:HPAD] = jnp.zeros((D, 128), F32)
    for t in range(2):
        vecf[...] = jnp.zeros(vecf.shape, F32)
        for i in range(n):
            unpack_slot(plan, i, slots.at[t, i], w.at[t], whf, vecf, scratch)
        wh[t] = whf[...].astype(BF)
        vec[t] = vecf[...].astype(BF)
    total = jnp.zeros((1, D), F32)
    for i in range(n):
        tail = slots[0, i, rows - 16 : rows].astype(F32)
        total = total + tail[15:16]
    weight_sum = jnp.sum(jnp.where(lane < 3, total, 0.0), axis=1, keepdims=True)
    rw[...] = jnp.broadcast_to(imp_ref[:, pl.ds(mine, half)].astype(F32) / weight_sum, (8, half))


def gather(plan, p128, ints, imp):
    n, rows = plan.n, plan.slot
    half = ints.shape[1] // 2
    vm = pl.BlockSpec(memory_space=pltpu.VMEM)
    height = p128.shape[0]
    tall = max(2 * rows, height + 40) + 80
    copies = 1 + (n // 4 - 1) + 2 * (n // 4) + 2 * (n // 4) + n
    return pl.pallas_call(
        functools.partial(gather_kernel, plan),
        out_shape=(
            jax.ShapeDtypeStruct((2, A_ROWS, D), BF),
            jax.ShapeDtypeStruct((2, D, HPAD), BF),
            jax.ShapeDtypeStruct((2, 128, D), BF),
            jax.ShapeDtypeStruct((2, 8, half), jnp.int32),
            jax.ShapeDtypeStruct((8, half), F32),
        ),
        in_specs=[vm] * 3,
        out_specs=(vm,) * 5,
        scratch_shapes=[
            pltpu.VMEM((2, n, rows, D), BF),
            pltpu.VMEM((tall, 128), F32),
            pltpu.VMEM((height + 128, 128), F32),
            pltpu.VMEM((height + 8, 128), F32),
            pltpu.VMEM((2, rows, 128), F32),
            pltpu.VMEM((D, HPAD), F32),
            pltpu.VMEM((128, D), F32),
            pltpu.SemaphoreType.DMA((copies,)),
            pltpu.SemaphoreType.DMA((copies,)),
        ],
        compiler_params=pltpu.CompilerParams(
            collective_id=0, has_side_effects=True, vmem_limit_bytes=48 * 1024 * 1024
        ),
    )(p128, ints, imp)


def segment_of(position):
    first_end = (D + CODES) * D
    block_end = first_end + BLOCKS * D * D
    head_end = block_end + D * HEADS
    inner = jnp.where(position < block_end, 1 + (position - first_end) // (D * D), BLOCKS + 1)
    return jnp.where(position < first_end, 0, jnp.where(position < head_end, inner, BLOCKS + 2))


def swap(x):
    return lax.ppermute(x, "tower", [(0, 1), (1, 0)])


def on_device(latent, codes, targets, visits, importance, params, first_moment, second_moment):
    me = lax.axis_index("tower")
    is_first = me == 0
    row_count = latent.shape[0]
    half = row_count // 2
    shard_len = params.shape[1]
    plan = Plan(lax.axis_size("dp"), shard_len)
    height = -(-plan.rows128 // 8) * 8
    p128 = jnp.pad(params[0], (0, 128 * height - shard_len)).reshape(height, 128)
    ints = jnp.concatenate([codes, targets[0, :1], visits[0].T, targets[0, 1:]], 0)
    x = lax.dynamic_slice_in_dim(latent, me * half, half, 0)
    w, wh, vec, both, rw = gather(plan, p128, ints, importance[None])
    st, ig, gw, gh, gv = compute(x, both, rw, w, wh, vec)

    def owned(parts):
        keep = lax.dynamic_index_in_dim(parts, me, 0, keepdims=False)
        got = swap(lax.dynamic_index_in_dim(parts, 1 - me, 0, keepdims=False))
        return jnp.where(is_first, jnp.concatenate([keep, got]), jnp.concatenate([got, keep]))

    states_out = owned(st)
    inputs_out = owned(ig)
    grads = jnp.concatenate(
        [
            gw.astype(F32).reshape(2, -1),
            gh[:, :, :HEADS].astype(F32).reshape(2, -1),
            gv[:, :, : BLOCKS + 1].reshape(2, -1),
        ],
        1,
    )
    grad_shard = lax.psum_scatter(grads.reshape(-1), ("tower", "dp"), scatter_dimension=0, tiled=True)
    master = params[0]
    correction = 1.0 - 0.5**STEP
    first_new = 0.5 * first_moment[0] + 0.5 * grad_shard
    second_new = 0.5 * second_moment[0] + 0.5 * grad_shard * grad_shard
    position = lax.axis_index("dp") * shard_len + jnp.arange(shard_len)
    segment = segment_of(position)
    is_matrix = segment < MATS
    update = first_new / correction / (jnp.sqrt(second_new / correction) + 1e-06) + jnp.where(
        is_matrix, 0.01 * master, 0.0
    )
    member = (segment[:, None] == jnp.arange(MATS)[None, :]).astype(F32)
    weight_part = jnp.dot(master * master, member, precision=lax.Precision.HIGHEST)
    update_part = jnp.dot(update * update, member, precision=lax.Precision.HIGHEST)
    weight_sq, update_sq = lax.psum((weight_part, update_part), "dp")
    weight_norm = jnp.sqrt(weight_sq)
    update_norm = jnp.sqrt(update_sq)
    ratio = jnp.where(
        is_matrix, jnp.dot(member, weight_norm / update_norm, precision=lax.Precision.HIGHEST), 1.0
    )
    new_params = master - 0.5 * ratio * update
    norms = jnp.stack([weight_norm, update_norm])[None]
    return (
        states_out[None],
        inputs_out[None],
        first_new[None],
        second_new[None],
        new_params[None],
        new_params.astype(BF)[None],
        norms,
    )


def solution(mesh):
    in_specs = (
        P("dp", None),
        P("tower", "dp"),
        P("tower", None, "dp"),
        P("tower", "dp", None),
        P("dp"),
        P("tower", "dp"),
        P("tower", "dp"),
        P("tower", "dp"),
    )
    out_specs = (
        P("tower", "dp", None),
        P("tower", "dp", None),
        P("tower", "dp"),
        P("tower", "dp"),
        P("tower", "dp"),
        P("tower", "dp"),
        P("tower", None, None),
    )
    return jax.shard_map(
        on_device, mesh=mesh, in_specs=in_specs, out_specs=out_specs, check_vma=False
    )
```

```python
import functools

import jax
import jax.numpy as jnp
from jax import lax
from jax.experimental import pallas as pl
from jax.experimental.pallas import tpu as pltpu
from jax.sharding import PartitionSpec as P

D = 256
CODES = 32
BINS = 601
BLOCKS = 10
STEP = 5
HEADS = 1238
MATS = 12
P_SIZE = 1054464
HPAD = 1280
CAT = D + CODES
A_ROWS = CAT + BLOCKS * D
BF = jnp.bfloat16
F32 = jnp.float32
GELU_C = 0.7978845608028654
GELU_K = 0.044715


def nn(a, b):
    return jnp.dot(a, b, preferred_element_type=F32)


def nt(a, b):
    return lax.dot_general(a, b, (((1,), (1,)), ((), ())), preferred_element_type=F32)


def identity(n):
    return (lax.broadcasted_iota(jnp.int32, (n, n), 0) == lax.broadcasted_iota(jnp.int32, (n, n), 1)).astype(BF)


def twice(v):
    return jnp.concatenate([v, v], 1)


def column_stats(ref, cs):
    total = jnp.sum(ref[:, cs], axis=0, keepdims=True)
    mean = total * (1.0 / D)
    square = jnp.zeros((8, mean.shape[1]), F32)
    for r in range(0, D, 32):
        cen = ref[r : r + 32, cs] - mean
        square = square + jnp.sum((cen * cen).reshape(4, 8, -1), axis=0)
    var = jnp.sum(square, axis=0, keepdims=True) * (1.0 / D)
    return mean, lax.rsqrt(var + 1e-05)


def norm_act(src, cs, gsb, xh_ref, gp_ref, rstd_ref, out):
    mean, rstd = column_stats(src, cs)
    rstd_ref[:, cs] = jnp.broadcast_to(rstd, (8, rstd.shape[1]))
    for r in range(0, D, 32):
        rs = slice(r, r + 32)
        xh = (src[rs, cs] - mean) * rstd
        xh_ref[rs, cs] = xh.astype(BF)
        y = xh * twice(gsb[rs, 0:128]) + twice(gsb[rs, 128:256])
        y2 = y * y
        p = y2 * (GELU_C * GELU_K) + GELU_C
        t = jnp.tanh(y * p)
        q = t * 0.5 + 0.5
        a = y * q
        out(rs, a)
        slope = q + (a - a * q) * (p * 6.0 - 4.0 * GELU_C)
        gp_ref[rs, cs] = slope.astype(BF)


def broadcast_vectors(vt, rows):
    k = lax.broadcasted_iota(jnp.int32, (128, 128), 0)
    picks = jnp.concatenate([(k == row).astype(BF) for row in rows], 1)
    return nn(vt, picks)


def head_stage(cs, lg, dl, ints, rw):
    width = rw.shape[1]
    it8 = lax.broadcasted_iota(jnp.int32, (8, width), 0)
    low = -jnp.inf
    b75, b150, b154 = lg[600:608], lg[1200:1208], lg[1232:1240]

    def top(block):
        return jnp.max(block, axis=0, keepdims=True)

    def top_range(lo, hi):
        best = lg[lo : lo + 8]
        for r in range(lo + 8, hi, 8):
            best = jnp.maximum(best, lg[r : r + 8])
        return best

    max_v = top(jnp.maximum(top_range(0, 600), jnp.where(it8 < 1, b75, low)))
    max_r = top(
        jnp.maximum(
            jnp.maximum(top_range(608, 1200), jnp.where(it8 >= 1, b75, low)),
            jnp.where(it8 < 2, b150, low),
        )
    )
    max_c = top(
        jnp.maximum(
            jnp.maximum(top_range(1208, 1232), jnp.where(it8 >= 2, b150, low)),
            jnp.where(it8 < 2, b154, low),
        )
    )
    in_policy = (it8 >= 2) & (it8 < 6)
    max_p = top(jnp.where(in_policy, b154, low))

    def exp_range(lo, hi, best):
        acc = jnp.zeros((8, width), F32)
        for r in range(lo, hi, 8):
            e = jnp.exp(lg[r : r + 8] - best)
            lg[r : r + 8] = e
            acc = acc + e
        return acc

    e75 = jnp.exp(b75 - jnp.where(it8 < 1, max_v, max_r))
    e150 = jnp.exp(b150 - jnp.where(it8 < 2, max_r, max_c))
    e154 = jnp.exp(b154 - jnp.where(it8 < 2, max_c, max_p))

    def total(acc):
        return rw / jnp.sum(acc, axis=0, keepdims=True)

    inv_v = total(exp_range(0, 600, max_v) + jnp.where(it8 < 1, e75, 0.0))
    inv_r = total(exp_range(608, 1200, max_r) + jnp.where(it8 >= 1, e75, 0.0) + jnp.where(it8 < 2, e150, 0.0))
    inv_c = total(exp_range(1208, 1232, max_c) + jnp.where(it8 >= 2, e150, 0.0) + jnp.where(it8 < 2, e154, 0.0))
    inv_p = total(jnp.where(in_policy, e154, 0.0))
    hit_v = ints[1:2]
    hit_r = ints[6:7] + BINS
    hit_c = ints[7:8] + 2 * BINS
    counts = jnp.where(in_policy, ints.astype(F32), 0.0)
    share = counts * (rw / jnp.sum(counts, axis=0, keepdims=True))

    def minus(value, lo, *hits):
        at = lax.broadcasted_iota(jnp.int32, value.shape, 0)
        for hit in hits:
            value = value - jnp.where(at == hit - lo, rw, 0.0)
        return value

    d75 = minus(e75 * jnp.where(it8 < 1, inv_v, inv_r), 600, hit_v, hit_r)
    d150 = minus(e150 * jnp.where(it8 < 2, inv_r, inv_c), 1200, hit_r, hit_c)
    d154 = minus(e154 * jnp.where(it8 < 2, inv_c, inv_p), 1232, hit_c) - share
    d154 = jnp.where(it8 < 6, d154, 0.0)

    def emit(lo, hi, inv, hit):
        for r in range(lo, hi, 16):
            dl[r : r + 16, cs] = minus(lg[r : r + 16] * inv, r, hit).astype(BF)

    def pair(first, second):
        return jnp.concatenate([first, second], 0).astype(BF)

    emit(0, 592, inv_v, hit_v)
    dl[592:608, cs] = pair(minus(lg[592:600] * inv_v, 592, hit_v), d75)
    emit(608, 1200, inv_r, hit_r)
    dl[1200:1216, cs] = pair(d150, minus(lg[1208:1216] * inv_c, 1208, hit_c))
    emit(1216, 1232, inv_c, hit_c)
    dl[1232:1248, cs] = pair(d154, jnp.zeros_like(d154))
    dl[1248:HPAD, cs] = jnp.zeros((HPAD - 1248, width), BF)


CB = 256


def forward_tower(t, refs):
    (eye, w, wh, vec, wct, wt, vt, gsb, xt, mix, xh, gp, rstd, stream, ints, width) = refs
    blocks = range(0, width, CB)
    for cs in (slice(c, c + CB) for c in blocks):
        it = lax.broadcasted_iota(jnp.int32, (CODES, CB), 0)
        xt[t, D:CAT, cs] = (it == ints[t, 0:1, cs]).astype(BF)
        xt[t, CAT : CAT + 16, cs] = jnp.ones((16, CB), BF)
    vt[...] = nt(eye[...], vec[t]).astype(BF)
    wt[...] = nt(eye[...], w[t, 0:D]).astype(BF)
    wct[...] = nt(eye[...], w[t, D:CAT]).astype(BF)
    gsb[...] = broadcast_vectors(vt[...], (0, BLOCKS + 1, 2 * BLOCKS + 2))
    for cs in (slice(c, c + CB) for c in blocks):
        pre = nn(wt[...], xt[t, 0:D, cs]) + nn(wct[...], xt[t, D:CAT, cs])
        stream[:, cs] = pre + twice(gsb[:, 256:384])

        def keep(rs, a):
            stream[rs, cs] = a

        norm_act(stream, cs, gsb, xh.at[t, 0], gp.at[t, 0], rstd.at[t, 0], keep)

    @pl.loop(1, BLOCKS + 1)
    def _(k):
        gsb[...] = broadcast_vectors(vt[...], (k, k + BLOCKS + 1, k + 2 * BLOCKS + 2))
        row = pl.multiple_of(CAT + (k - 1) * D, 32)
        wt[...] = nt(eye[...], w[t, pl.ds(row, D)]).astype(BF)
        for cs in (slice(c, c + CB) for c in blocks):

            def keep(rs, a):
                mix[t, k - 1, rs, cs] = a.astype(BF)

            norm_act(stream, cs, gsb, xh.at[t, k], gp.at[t, k], rstd.at[t, k], keep)
            pre = nn(wt[...], mix[t, k - 1, 0:D, cs])
            stream[:, cs] = stream[:, cs] + pre + twice(gsb[:, 256:384])
        mix[t, k - 1, D : D + 16, :] = jnp.ones((16, width), BF)

    for c in blocks:
        cs = slice(c, c + CB)
        xt[t + 1, 0:D, cs] = stream[:, cs].astype(BF)


def backward_act(cs, grad_ref, gp_ref, xh_ref, dy16, dyx16):
    for r in range(0, D, 32):
        rs = slice(r, r + 32)
        dy = grad_ref[rs, :] * gp_ref[rs, cs].astype(F32)
        grad_ref[rs, :] = dy
        dy16[rs, cs] = dy.astype(BF)
        dyx16[rs, cs] = (dy * xh_ref[rs, cs].astype(F32)).astype(BF)


def backward_tower(t, refs):
    (eye, w, wh, vec, wht, vt, gsb, xt, mix, xh, gp, rstd, ds, ex, br, dy16, dyx16, dm, lg, dl, ints, rw, gw, gh, gv, ig, width) = refs
    blocks = range(0, width, CB)
    vt[...] = nt(eye[...], vec[t]).astype(BF)
    for h in range(0, HPAD, D):
        wht[h : h + D, :] = nt(eye[...], wh[t, :, h : h + D]).astype(BF)

    @pl.loop(0, width // CB)
    def _(c):
        cs = pl.ds(pl.multiple_of(c * CB, CB), CB)
        lg[...] = nn(wht[...], xt[t + 1, 0:D, cs])
        head_stage(cs, lg, dl, ints[t, :, cs], rw[0:1, cs])
        ds[:, cs] = nn(wh[t], dl[:, cs]) + ex[:, cs]

    gh[t] = nt(xt[t + 1, 0:D, :], dl[...]).astype(BF)
    def stage(k, first):
        gsb[:, 0:128] = broadcast_vectors(vt[...], (k,))
        pick = (lax.broadcasted_iota(jnp.int32, (16, 128), 1) == k).astype(BF)
        g16 = nt(pick, vt[...]).astype(BF)
        for i, c in enumerate(blocks):
            cs = slice(c, c + CB)
            buf = dm.at[i % 2]
            if first:
                buf[...] = ds[:, cs]
            else:
                row = pl.multiple_of(CAT + (k - 1) * D, 32)
                br[:, cs] = ds[:, cs].astype(BF)
                buf[...] = nn(w[t, pl.ds(row, D)], br[:, cs])
            backward_act(cs, buf, gp.at[t, k], xh.at[t, k], dy16, dyx16)
            m1 = nn(g16, dy16[:, cs])[0:1] * (1.0 / D)
            m2 = nn(g16, dyx16[:, cs])[0:1] * (1.0 / D)
            rs1 = rstd[t, k, 0:1, cs]
            m1 = m1 * rs1
            m2 = m2 * rs1
            for r in range(0, D, 32):
                rs = slice(r, r + 32)
                back = (buf[rs, :] * twice(gsb[rs, 0:128])) * rs1 - m1 - xh[t, k, rs, cs].astype(F32) * m2
                if first:
                    br[rs, cs] = back.astype(BF)
                else:
                    ds[rs, cs] = ds[rs, cs] + back
        ones = jnp.ones((16, width), BF)
        gv[t, 0, pl.ds(k, 1), :] = nt(ones, dyx16[...])[0:1]
        gv[t, 1, pl.ds(k, 1), :] = nt(ones, dy16[...])[0:1]

    @pl.loop(0, BLOCKS)
    def _(i):
        k = BLOCKS - i
        stage(k, False)
        full = nt(mix[t, k - 1], br[...])
        row = pl.multiple_of(CAT + (k - 1) * D, 32)
        gw[t, pl.ds(row, D), :] = full[0:D].astype(BF)
        gv[t, 2, pl.ds(k, 1), :] = full[D : D + 1]

    stage(0, True)
    full = nt(xt[t], br[...])
    gw[t, 0:CAT, :] = full[0:CAT].astype(BF)
    gv[t, 2, 0:1, :] = full[CAT : CAT + 1]
    for c in blocks:
        cs = slice(c, c + CB)
        back = nn(w[t, 0:D], br[:, cs])
        ex[:, cs] = back
        ig[t, cs, :] = back.T


def compute_kernel(x_ref, ints, rw, w, wh, vec, st, ig, gw, gh, gv, eye, wct, wt, wht, vt, gsb, xt, mix, xh, gp, rstd, stream, ex, br, dy16, dyx16, dm, lg, dl):
    width = x_ref.shape[0]
    eye[...] = identity(D)
    for c in range(0, width, CB):
        cs = slice(c, c + CB)
        xt[0, 0:D, cs] = nt(eye[...], x_ref[cs, :]).astype(BF)
    fwd = (eye, w, wh, vec, wct, wt, vt, gsb, xt, mix, xh, gp, rstd, stream, ints, width)
    bwd = (eye, w, wh, vec, wht, vt, gsb, xt, mix, xh, gp, rstd, stream, ex, br, dy16, dyx16, dm, lg, dl, ints, rw, gw, gh, gv, ig, width)

    @pl.loop(0, 2)
    def _(t):
        forward_tower(t, fwd)

        @pl.loop(0, width // CB)
        def _(c):
            cs = pl.ds(pl.multiple_of(c * CB, CB), CB)
            st[t, cs, :] = nt(eye[...], xt[t + 1, 0:D, cs]).astype(BF)

    ex[...] = jnp.zeros_like(ex)

    @pl.loop(0, 2)
    def _(i):
        backward_tower(1 - i, bwd)


def compute(x, ints, rw, w, wh, vec):
    width = x.shape[0]
    vm = pl.BlockSpec(memory_space=pltpu.VMEM)
    return pl.pallas_call(
        compute_kernel,
        out_shape=(
            jax.ShapeDtypeStruct((2, width, D), BF),
            jax.ShapeDtypeStruct((2, width, D), F32),
            jax.ShapeDtypeStruct((2, A_ROWS, D), BF),
            jax.ShapeDtypeStruct((2, D, HPAD), BF),
            jax.ShapeDtypeStruct((2, 3, 16, D), F32),
        ),
        in_specs=[vm] * 6,
        out_specs=(vm,) * 5,
        scratch_shapes=[
            pltpu.VMEM((D, D), BF),
            pltpu.VMEM((D, CODES), BF),
            pltpu.VMEM((D, D), BF),
            pltpu.VMEM((HPAD, D), BF),
            pltpu.VMEM((D, 128), BF),
            pltpu.VMEM((D, 384), F32),
            pltpu.VMEM((3, CAT + 16, width), BF),
            pltpu.VMEM((2, BLOCKS, D + 16, width), BF),
            pltpu.VMEM((2, BLOCKS + 1, D, width), BF),
            pltpu.VMEM((2, BLOCKS + 1, D, width), BF),
            pltpu.VMEM((2, BLOCKS + 1, 8, width), F32),
            pltpu.VMEM((D, width), F32),
            pltpu.VMEM((D, width), F32),
            pltpu.VMEM((D, width), BF),
            pltpu.VMEM((D, width), BF),
            pltpu.VMEM((D, width), BF),
            pltpu.VMEM((2, D, CB), F32),
            pltpu.VMEM((HPAD, CB), F32),
            pltpu.VMEM((HPAD, width), BF),
        ],
        compiler_params=pltpu.CompilerParams(vmem_limit_bytes=62 * 1024 * 1024),
    )(x, ints, rw, w, wh, vec)


class Plan:
    def __init__(self, n, length):
        self.n, self.length = n, length
        self.rows128 = -(-length // 128)
        block_end, head_end = A_ROWS * D, A_ROWS * D + D * HEADS
        self.a_base, self.a_rows, self.h_first, self.h_rows, self.h_off, self.v_first, self.v_rows, self.v_off = ([] for _ in range(8))
        used = 0
        for i in range(n):
            lo, hi = i * length, (i + 1) * length
            base = min(lo, block_end) // D // 16 * 16
            top = -(-min(hi, block_end) // D)
            a_rows = -(-(top - base) // 16) * 16 if lo < block_end else 0
            first = min(max(lo - block_end, 0), D * HEADS) // HEADS
            last = -(-min(max(hi - block_end, 0), D * HEADS) // HEADS)
            h_rows = last - first if hi > block_end and lo < head_end else 0
            v_first = max(lo - head_end, 0) // D
            v_rows = -(-(hi - head_end) // D) - v_first if hi > head_end else 0
            self.a_base.append(base)
            self.a_rows.append(a_rows)
            self.h_first.append(first)
            self.h_rows.append(h_rows)
            self.h_off.append(a_rows)
            self.v_first.append(v_first)
            self.v_rows.append(v_rows)
            self.v_off.append(a_rows + 5 * h_rows)
            used = max(used, a_rows + 5 * h_rows + v_rows)
        self.slot = -(-(used + 1) // 32) * 32

    def at(self, table, me):
        value = jnp.int32(table[0])
        for i in range(1, self.n):
            if table[i] != table[i - 1]:
                value = value + (me >= i).astype(jnp.int32) * (table[i] - table[i - 1])
        return value


MESH = pl.DeviceIdType.MESH


def neighbours(n):
    core = lax.axis_index("tower")
    me = lax.axis_index("dp")
    near_x = me + 1 - 2 * (me % 2)
    near_y = me + 2 - 4 * ((me // 2) % 2)
    return core, me, near_x, near_y


def at(core, index):
    return {"tower": core, "dp": index}


def greet(core, me, near_x, near_y, n):
    barrier = pltpu.get_barrier_semaphore()
    pl.semaphore_signal(barrier, inc=1, device_id=at(1 - core, me), device_id_type=MESH)
    for near in (near_x, near_y):
        pl.semaphore_signal(barrier, inc=1, device_id=at(core, near), device_id_type=MESH)
    for k in range(1, n // 4):
        pl.semaphore_signal(barrier, inc=1, device_id=at(core, (me + 4 * k) % n), device_id_type=MESH)
    return barrier


def place_shard(plan, me, p_ref, slot128, shifted, rolled):
    rows = plan.rows128
    start = me * plan.length
    shift = start % 128
    first = start // 128
    tall = shifted.shape[0]
    height = p_ref.shape[0]
    lane = lax.broadcasted_iota(jnp.int32, (height, 128), 1)
    rolled[0:8] = jnp.zeros((8, 128), F32)
    rolled[8 : 8 + height] = pltpu.roll(p_ref[...], shift, 1)
    shifted[...] = jnp.zeros((tall, 128), F32)
    moved = jnp.where(lane >= shift, rolled[8 : 8 + height], rolled[7 : 7 + height])
    shifted[16 : 16 + height] = moved
    slot128[...] = jnp.zeros(slot128.shape, F32)
    row = lax.broadcasted_iota(jnp.int32, (height, 128), 0)
    base = plan.at(plan.a_base, me)

    @pl.when(plan.at(plan.a_rows, me) > 0)
    def _():
        slot128[pl.ds(first - 2 * base, height)] = jnp.where(row + first < 2 * A_ROWS, moved, 0.0)

    h_first, h_rows, h_off = (plan.at(t, me) for t in (plan.h_first, plan.h_rows, plan.h_off))
    it = lax.broadcasted_iota(jnp.int32, (10, 128), 0)
    lane10 = lax.broadcasted_iota(jnp.int32, (10, 128), 1)

    @pl.loop(0, h_rows)
    def _(k):
        begin = A_ROWS * D + HEADS * (h_first + k) - 128 * first + 128 * 16
        turn = begin % 128
        window = pltpu.roll(shifted[pl.ds(begin // 128, 16)], (128 - turn) % 128, 1)
        value = jnp.where(lane10 < 128 - turn, window[0:10], window[1:11])
        slot128[pl.ds(2 * h_off + 10 * k, 10)] = jnp.where(it * 128 + lane10 < HEADS, value, 0.0)

    v_start = (A_ROWS * D + D * HEADS) // 128
    v_rows, v_off, v_first = (plan.at(t, me) for t in (plan.v_rows, plan.v_off, plan.v_first))
    tall_v = min(height, -(-2 * max(plan.v_rows) // 8) * 8)

    @pl.when(v_rows > 0)
    def _():
        inside = plan.at([max(0, v_start - i * plan.length // 128) for i in range(plan.n)], me)
        to = 2 * v_off + first + inside - v_start - 2 * v_first
        slot128[pl.ds(to, tall_v)] = shifted[pl.ds(16 + inside, tall_v)]


def unpack_slot(plan, i, slot, w, whf, vecf, scratch):
    base, rows = plan.a_base[i], plan.a_rows[i]
    if rows:
        shared = i > 0 and base < plan.a_base[i - 1] + plan.a_rows[i - 1]
        lo = 0
        if shared:
            w[base : base + 16] = w[base : base + 16] + slot[0:16]
            lo = 16
        if rows > lo:
            w[base + lo : base + rows] = slot[lo:rows]
    h_rows, h_off, h_first = plan.h_rows[i], plan.h_off[i], plan.h_first[i]
    v_rows, v_off, v_first = plan.v_rows[i], plan.v_off[i], plan.v_first[i]
    if h_rows or v_rows:
        value = slot[...].astype(F32)
        scratch[0] = value[:, 0:128]
        scratch[1] = value[:, 128:D]
    if h_rows:
        shared = i > 0 and plan.h_rows[i - 1] and plan.h_first[i - 1] + plan.h_rows[i - 1] > h_first
        for j in range(5):
            for half in range(2):
                cols = slice(D * j + 128 * half, D * j + 128 * half + 128)
                value = scratch[half, pl.ds(h_off + j, h_rows, stride=5)]
                if shared:
                    whf[h_first : h_first + 1, cols] = whf[h_first : h_first + 1, cols] + value[0:1]
                    if h_rows > 1:
                        whf[h_first + 1 : h_first + h_rows, cols] = value[1:h_rows]
                else:
                    whf[h_first : h_first + h_rows, cols] = value
    if v_rows:
        shared = v_first and plan.v_first[i - 1] + plan.v_rows[i - 1] > v_first
        shared = shared or (i > 0 and plan.v_rows[i - 1] > 0 and v_first == 0)
        for half in range(2):
            cols = slice(128 * half, 128 * half + 128)
            value = scratch[half, v_off : v_off + v_rows]
            if shared:
                vecf[v_first : v_first + 1, cols] = vecf[v_first : v_first + 1, cols] + value[0:1]
                if v_rows > 1:
                    vecf[v_first + 1 : v_first + v_rows, cols] = value[1:v_rows]
            else:
                vecf[v_first : v_first + v_rows, cols] = value


def split3(value):
    hi = value.astype(BF).astype(F32)
    mid = (value - hi).astype(BF).astype(F32)
    return hi, mid, value - hi - mid


def gather_kernel(plan, p_ref, ints_ref, imp_ref, w, wh, vec, both, rw, slots, slot128, shifted, rolled, scratch, whf, vecf, send, recv):
    n = plan.n
    depth = n // 4
    core, me, near_x, near_y = neighbours(n)
    barrier = greet(core, me, near_x, near_y, n)
    place_shard(plan, me, p_ref, slot128, shifted, rolled)
    pl.semaphore_wait(barrier, depth + 2)
    half = rw.shape[1]
    started = []

    def copy(src, dst, slot, to):
        c = pltpu.make_async_remote_copy(
            src_ref=src, dst_ref=dst, send_sem=send.at[slot], recv_sem=recv.at[slot], device_id=to, device_id_type=MESH
        )
        c.start()
        started.append(c)
        return c

    mine = pl.multiple_of(core * half, half)
    theirs = pl.multiple_of((1 - core) * half, half)
    number = iter(range(1 << 20))
    ints_copy = copy(ints_ref.at[:, pl.ds(theirs, half)], both.at[core], next(number), at(1 - core, me))
    rows = plan.slot
    total = jnp.sum(imp_ref[...].astype(F32), axis=1, keepdims=True)
    lane = lax.broadcasted_iota(jnp.int32, (1, D), 1)
    hi, mid, lo = split3(total)
    left = slot128[pl.ds(0, rows, stride=2)]
    right = slot128[pl.ds(1, rows, stride=2)]
    own = jnp.concatenate([left, right], 1)
    last = jnp.where(lane == 0, hi, jnp.where(lane == 1, mid, jnp.where(lane == 2, lo, 0.0)))
    last_row = lax.broadcasted_iota(jnp.int32, (rows, D), 0) == rows - 1
    slots[core, me] = jnp.where(last_row, last, own).astype(BF)

    def column(index, k):
        return (index + n - 4 * k) % n

    def send_slot(origin, to, lo=0, hi=rows):
        ref = slots.at[core, origin, pl.ds(lo, hi - lo)]
        return copy(ref, ref, next(number), to)

    near_xy = near_x + near_y - me
    cut = rows // 2
    z_in, x_in, y_in, d_in, s_in = {}, {}, {}, {}, []
    for k in sorted(range(1, depth), key=lambda k: (min(k, depth - k), k)):
        z_in[k] = send_slot(me, at(core, (me + 4 * k) % n))
    order = [0] + list(z_in)
    for k in order:
        if k:
            z_in[k].wait_recv()
        x_in[k] = send_slot(column(me, k), at(core, near_x))
        y_in[k] = send_slot(column(me, k), at(core, near_y))
        s_in.append(send_slot(column(me, k), at(1 - core, me)))
    for k in order:
        x_in[k].wait_recv()
        first = send_slot(column(near_x, k), at(core, near_y), 0, cut)
        s_in.append(send_slot(column(near_x, k), at(1 - core, me)))
        y_in[k].wait_recv()
        second = send_slot(column(near_y, k), at(core, near_x), cut, rows)
        s_in.append(send_slot(column(near_y, k), at(1 - core, me)))
        d_in[k] = (first, second)
    for k in order:
        for c in d_in[k]:
            c.wait_recv()
        s_in.append(send_slot(column(near_xy, k), at(1 - core, me)))
    ints_copy.wait_recv()
    both[core] = ints_ref[:, pl.ds(mine, half)]
    for c in s_in:
        c.wait_recv()
    for c in started:
        c.wait_send()
    whf[:, 1152:HPAD] = jnp.zeros((D, 128), F32)
    for t in range(2):
        vecf[...] = jnp.zeros(vecf.shape, F32)
        for i in range(n):
            unpack_slot(plan, i, slots.at[t, i], w.at[t], whf, vecf, scratch)
        wh[t] = whf[...].astype(BF)
        vec[t] = vecf[...].astype(BF)
    total = jnp.zeros((1, D), F32)
    for i in range(n):
        tail = slots[0, i, rows - 16 : rows].astype(F32)
        total = total + tail[15:16]
    weight_sum = jnp.sum(jnp.where(lane < 3, total, 0.0), axis=1, keepdims=True)
    rw[...] = jnp.broadcast_to(imp_ref[:, pl.ds(mine, half)].astype(F32) / weight_sum, (8, half))


def gather(plan, p128, ints, imp):
    n, rows = plan.n, plan.slot
    half = ints.shape[1] // 2
    vm = pl.BlockSpec(memory_space=pltpu.VMEM)
    height = p128.shape[0]
    tall = max(2 * rows, height + 40) + 80
    copies = 1 + (n // 4 - 1) + 2 * (n // 4) + 2 * (n // 4) + n
    return pl.pallas_call(
        functools.partial(gather_kernel, plan),
        out_shape=(
            jax.ShapeDtypeStruct((2, A_ROWS, D), BF),
            jax.ShapeDtypeStruct((2, D, HPAD), BF),
            jax.ShapeDtypeStruct((2, 128, D), BF),
            jax.ShapeDtypeStruct((2, 8, half), jnp.int32),
            jax.ShapeDtypeStruct((8, half), F32),
        ),
        in_specs=[vm] * 3,
        out_specs=(vm,) * 5,
        scratch_shapes=[
            pltpu.VMEM((2, n, rows, D), BF),
            pltpu.VMEM((tall, 128), F32),
            pltpu.VMEM((height + 128, 128), F32),
            pltpu.VMEM((height + 8, 128), F32),
            pltpu.VMEM((2, rows, 128), F32),
            pltpu.VMEM((D, HPAD), F32),
            pltpu.VMEM((128, D), F32),
            pltpu.SemaphoreType.DMA((copies,)),
            pltpu.SemaphoreType.DMA((copies,)),
        ],
        compiler_params=pltpu.CompilerParams(
            collective_id=0, has_side_effects=True, vmem_limit_bytes=48 * 1024 * 1024
        ),
    )(p128, ints, imp)


def lay_flat(plan, me, slot128, flat, rolled):
    height = rolled.shape[0] - 16
    start = me * plan.length
    shift = start % 128
    first = start // 128
    base = plan.at(plan.a_base, me)
    row = lax.broadcasted_iota(jnp.int32, (height + 8, 128), 0)
    flat[...] = jnp.zeros(flat.shape, F32)

    @pl.when(plan.at(plan.a_rows, me) > 0)
    def _():
        rows = slot128[pl.ds(first - 2 * base, height + 8)]
        flat[16 : 24 + height] = jnp.where(row + first < 2 * A_ROWS, rows, 0.0)

    h_first, h_rows, h_off = (plan.at(t, me) for t in (plan.h_first, plan.h_rows, plan.h_off))
    it = lax.broadcasted_iota(jnp.int32, (16, 128), 0)
    lane = lax.broadcasted_iota(jnp.int32, (16, 128), 1)

    @pl.loop(0, h_rows)
    def _(k):
        begin = A_ROWS * D + HEADS * (h_first + k) - 128 * first + 128 * 16
        turn = begin % 128
        value = slot128[pl.ds(2 * h_off + 10 * k, 16)]
        value = jnp.where(it * 128 + lane < HEADS, value, 0.0)
        value = pltpu.roll(value, turn, 1)
        above = jnp.concatenate([jnp.zeros((8, 128), F32), value], 0)[7:23]
        to = pl.ds(begin // 128, 16)
        flat[to] = flat[to] + jnp.where(lane >= turn, value, above)

    v_start = (A_ROWS * D + D * HEADS) // 128
    v_rows, v_off, v_first = (plan.at(t, me) for t in (plan.v_rows, plan.v_off, plan.v_first))
    tall_v = min(height, -(-2 * max(plan.v_rows) // 8) * 8)

    @pl.when(v_rows > 0)
    def _():
        inside = plan.at([max(0, v_start - i * plan.length // 128) for i in range(plan.n)], me)
        source = 2 * v_off + first + inside - v_start - 2 * v_first
        to = pl.ds(16 + inside, tall_v)
        flat[to] = flat[to] + slot128[pl.ds(source, tall_v)]

    rolled[0 : height + 8] = pltpu.roll(flat[16 : 24 + height], (128 - shift) % 128, 1)
    lane = lax.broadcasted_iota(jnp.int32, (height, 128), 1)
    return jnp.where(lane < 128 - shift, rolled[0:height], rolled[1 : height + 1])


def pack_slots(plan, core, gw, gh, gv, rgw, rgh, rgv, slots, sums, vsum, scratch):
    total = gv[core].astype(F32) + rgv[...]
    for kind in range(3):
        vsum[kind * (BLOCKS + 1) : (kind + 1) * (BLOCKS + 1)] = total[kind, 0 : BLOCKS + 1]
    sums[...] = gh[core].astype(F32) + rgh[...].astype(F32)
    for i in range(plan.n):
        base, rows = plan.a_base[i], plan.a_rows[i]
        h_rows, h_off, h_first = plan.h_rows[i], plan.h_off[i], plan.h_first[i]
        v_rows, v_off, v_first = plan.v_rows[i], plan.v_off[i], plan.v_first[i]
        slots[i, rows : plan.slot] = jnp.zeros((plan.slot - rows, D), BF)
        if rows:
            added = gw[core, base : base + rows].astype(F32) + rgw[base : base + rows].astype(F32)
            slots[i, 0:rows] = added.astype(BF)
        if h_rows or v_rows:
            scratch[...] = jnp.zeros(scratch.shape, F32)
            for half in range(2):
                for j in range(5 if h_rows else 0):
                    cols = slice(D * j + 128 * half, D * j + 128 * half + 128)
                    scratch[half, pl.ds(h_off + j, h_rows, stride=5)] = sums[h_first : h_first + h_rows, cols]
                if v_rows:
                    scratch[half, v_off : v_off + v_rows] = vsum[v_first : v_first + v_rows, 128 * half : 128 * half + 128]
            whole = jnp.concatenate([scratch[0], scratch[1]], 1)
            slots[i, rows : plan.slot] = whole[rows:].astype(BF)


def segment_bounds():
    first = [0] + [(CAT + j * D) * D for j in range(BLOCKS + 1)]
    return list(zip(first, first[1:] + [A_ROWS * D + D * HEADS]))


def reduce_kernel(
    plan, gw, gh, gv, st, ig, p_ref, m_ref, v_ref,
    st_out, ig_out, first_out, second_out, new_out, low_out, norm_out,
    rgw, rgh, rgv, slots, sums, vsum, scratch, in_d, in_x, in_y, in_z, slot128, flat, rolled, squares, sq_z, sq_y, sq_x,
    send, recv, local,
):
    n, rows = plan.n, plan.slot
    depth, cut = n // 4, plan.slot // 2
    core, me, near_x, near_y = neighbours(n)
    near_xy = near_x + near_y - me
    barrier = greet(core, me, near_x, near_y, n)
    pl.semaphore_wait(barrier, depth + 2)
    half = st.shape[1]
    number = iter(range(1 << 20))
    started = []

    def copy(src, dst, to):
        slot = next(number)
        c = pltpu.make_async_remote_copy(
            src_ref=src, dst_ref=dst, send_sem=send.at[slot], recv_sem=recv.at[slot], device_id=to, device_id_type=MESH
        )
        c.start()
        started.append(c)
        return c

    def column(index, k):
        return (index + n - 4 * k) % n

    sibling = at(1 - core, me)
    early = [
        copy(gw.at[1 - core], rgw, sibling),
        copy(gh.at[1 - core], rgh, sibling),
        copy(gv.at[1 - core], rgv, sibling),
    ]
    mine = pl.ds(pl.multiple_of(core * half, half), half)
    late = [
        copy(st.at[1 - core], st_out.at[mine], sibling),
        copy(ig.at[1 - core], ig_out.at[mine], sibling),
    ]
    stay = [
        pltpu.make_async_copy(st.at[core], st_out.at[mine], local.at[0]),
        pltpu.make_async_copy(ig.at[core], ig_out.at[mine], local.at[1]),
    ]
    for c in stay:
        c.start()
    for c in early:
        c.wait_recv()
    pack_slots(plan, core, gw, gh, gv, rgw, rgh, rgv, slots, sums, vsum, scratch)
    order = list(range(1, depth)) + [0]
    to_x, to_y = at(core, near_x), at(core, near_y)
    halves = {}
    for k in order:
        diagonal = column(near_xy, k)
        halves[k] = (
            copy(slots.at[diagonal, pl.ds(0, cut)], in_d.at[k, pl.ds(0, cut)], to_y),
            copy(slots.at[diagonal, pl.ds(cut, rows - cut)], in_d.at[k, pl.ds(cut, rows - cut)], to_x),
        )
    fulls = {}
    for k in order:
        ox, oy = column(near_x, k), column(near_y, k)
        halves[k][0].wait_recv()
        slots[ox, 0:cut] = (slots[ox, 0:cut].astype(F32) + in_d[k, 0:cut].astype(F32)).astype(BF)
        first = copy(slots.at[ox], in_x.at[k], to_x)
        halves[k][1].wait_recv()
        slots[oy, cut:rows] = (slots[oy, cut:rows].astype(F32) + in_d[k, cut:rows].astype(F32)).astype(BF)
        fulls[k] = (first, copy(slots.at[oy], in_y.at[k], to_y))
    along = {}
    for k in order:
        own = column(me, k)
        for c in fulls[k]:
            c.wait_recv()
        if k:
            total = slots[own].astype(F32) + in_x[k].astype(F32) + in_y[k].astype(F32)
            slots[own] = total.astype(BF)
            along[k] = copy(slots.at[own], in_z.at[k], at(core, own))
    for c in along.values():
        c.wait_recv()
    total = slots[me].astype(F32) + in_x[0].astype(F32) + in_y[0].astype(F32)
    for k in along:
        total = total + in_z[k].astype(F32)
    slot128[...] = jnp.zeros(slot128.shape, F32)
    slot128[pl.ds(0, rows, stride=2)] = total[:, 0:128]
    slot128[pl.ds(1, rows, stride=2)] = total[:, 128:D]
    grad = lay_flat(plan, me, slot128, flat, rolled)

    height = p_ref.shape[0]
    place = 128 * lax.broadcasted_iota(jnp.int32, (height, 128), 0) + lax.broadcasted_iota(jnp.int32, (height, 128), 1)
    grad = jnp.where(place < plan.length, grad, 0.0)
    position = place + me * plan.length
    master = p_ref[...]
    correction = 1.0 - 0.5**STEP
    first_new = 0.5 * m_ref[...] + 0.5 * grad
    second_new = 0.5 * v_ref[...] + 0.5 * grad * grad
    first_out[...] = first_new
    second_out[...] = second_new
    bounds = segment_bounds()
    is_matrix = position < bounds[-1][1]
    update = first_new / correction / (jnp.sqrt(second_new / correction) + 1e-06) + jnp.where(is_matrix, 0.01 * master, 0.0)
    update = jnp.where(place < plan.length, update, 0.0)
    p_square, u_square = master * master, update * update
    flat[0:height] = update
    squares[...] = jnp.zeros(squares.shape, F32)
    for j, (lo, hi) in enumerate(bounds):
        inside = (position >= lo) & (position < hi)
        squares[0, j : j + 1] = jnp.sum(jnp.where(inside, p_square, 0.0), axis=0, keepdims=True)
        squares[0, 16 + j : 17 + j] = jnp.sum(jnp.where(inside, u_square, 0.0), axis=0, keepdims=True)
    steps = [copy(squares.at[0], sq_z.at[k], at(core, column(me, k))) for k in range(1, depth)]
    for c in steps:
        c.wait_recv()
    total = squares[0]
    for k in range(1, depth):
        total = total + sq_z[k]
    squares[1] = total
    copy(squares.at[1], sq_y, to_y).wait_recv()
    squares[2] = squares[1] + sq_y[...]
    copy(squares.at[2], sq_x, to_x).wait_recv()
    norm = jnp.sqrt(jnp.sum(squares[2] + sq_x[...], axis=1, keepdims=True))
    norm_out[...] = jnp.broadcast_to(norm, (32, 128))
    ratio = norm[0:16] / norm[16:32]
    factor = jnp.ones((height, 128), F32)
    for j, (lo, hi) in enumerate(bounds):
        inside = (position >= lo) & (position < hi)
        factor = jnp.where(inside, ratio[j : j + 1], factor)
    new = p_ref[...] - 0.5 * factor * flat[0:height]
    new_out[...] = new
    low_out[...] = new.astype(BF)
    for c in late:
        c.wait_recv()
    for c in stay:
        c.wait()
    for c in started:
        c.wait_send()


def reduce_and_update(plan, gw, gh, gv, st, ig, p128, m128, v128):
    n, rows = plan.n, plan.slot
    depth = n // 4
    half = st.shape[1]
    height = p128.shape[0]
    vm = pl.BlockSpec(memory_space=pltpu.VMEM)
    hbm = pl.BlockSpec(memory_space=pl.ANY)
    copies = 5 + 2 * depth + 2 * depth + (depth - 1) + (depth - 1) + 2
    flat32 = jax.ShapeDtypeStruct((height, 128), F32)
    return pl.pallas_call(
        functools.partial(reduce_kernel, plan),
        out_shape=(
            jax.ShapeDtypeStruct((2 * half, D), BF),
            jax.ShapeDtypeStruct((2 * half, D), F32),
            flat32,
            flat32,
            flat32,
            jax.ShapeDtypeStruct((height, 128), BF),
            jax.ShapeDtypeStruct((32, 128), F32),
        ),
        in_specs=[vm] * 3 + [hbm] * 2 + [vm] * 3,
        out_specs=(hbm, hbm, vm, vm, vm, vm, vm),
        scratch_shapes=[
            pltpu.VMEM((A_ROWS, D), BF),
            pltpu.VMEM((D, HPAD), BF),
            pltpu.VMEM(gv.shape[1:], F32),
            pltpu.VMEM((n, rows, D), BF),
            pltpu.VMEM((D, HPAD), F32),
            pltpu.VMEM((40, D), F32),
            pltpu.VMEM((2, rows, 128), F32),
            pltpu.VMEM((depth, rows, D), BF),
            pltpu.VMEM((depth, rows, D), BF),
            pltpu.VMEM((depth, rows, D), BF),
            pltpu.VMEM((depth, rows, D), BF),
            pltpu.VMEM((max(2 * rows, height + 48) + 80, 128), F32),
            pltpu.VMEM((height + 128, 128), F32),
            pltpu.VMEM((height + 16, 128), F32),
            pltpu.VMEM((3, 32, 128), F32),
            pltpu.VMEM((depth, 32, 128), F32),
            pltpu.VMEM((32, 128), F32),
            pltpu.VMEM((32, 128), F32),
            pltpu.SemaphoreType.DMA((copies,)),
            pltpu.SemaphoreType.DMA((copies,)),
            pltpu.SemaphoreType.DMA((2,)),
        ],
        compiler_params=pltpu.CompilerParams(
            collective_id=1, has_side_effects=True, vmem_limit_bytes=48 * 1024 * 1024
        ),
    )(gw, gh, gv, st, ig, p128, m128, v128)


def on_device(latent, codes, targets, visits, importance, params, first_moment, second_moment):
    me = lax.axis_index("tower")
    row_count = latent.shape[0]
    half = row_count // 2
    shard_len = params.shape[1]
    plan = Plan(lax.axis_size("dp"), shard_len)
    height = -(-plan.rows128 // 8) * 8

    def to_rows(value):
        return jnp.pad(value[0], (0, 128 * height - shard_len)).reshape(height, 128)

    p128 = to_rows(params)
    ints = jnp.concatenate([codes, targets[0, :1], visits[0].T, targets[0, 1:]], 0)
    x = lax.dynamic_slice_in_dim(latent, me * half, half, 0)
    w, wh, vec, both, rw = gather(plan, p128, ints, importance[None])
    st, ig, gw, gh, gv = compute(x, both, rw, w, wh, vec)

    states_out, inputs_out, *flat, low, norm = reduce_and_update(
        plan, gw, gh, gv, st, ig, p128, to_rows(first_moment), to_rows(second_moment)
    )

    def shard(value):
        return value.reshape(1, -1)[:, :shard_len]

    norms = jnp.stack([norm[:MATS, 0], norm[16 : 16 + MATS, 0]])[None]
    return (states_out[None], inputs_out[None], *(shard(v) for v in flat), shard(low), norms)


def solution(mesh):
    in_specs = (
        P("dp", None),
        P("tower", "dp"),
        P("tower", None, "dp"),
        P("tower", "dp", None),
        P("dp"),
        P("tower", "dp"),
        P("tower", "dp"),
        P("tower", "dp"),
    )
    out_specs = (
        P("tower", "dp", None),
        P("tower", "dp", None),
        P("tower", "dp"),
        P("tower", "dp"),
        P("tower", "dp"),
        P("tower", "dp"),
        P("tower", None, None),
    )
    return jax.shard_map(
        on_device, mesh=mesh, in_specs=in_specs, out_specs=out_specs, check_vma=False
    )
```

```python
import functools

import jax
import jax.numpy as jnp
from jax import lax
from jax.experimental import pallas as pl
from jax.experimental.pallas import tpu as pltpu
from jax.sharding import PartitionSpec as P

D = 256
CODES = 32
BINS = 601
BLOCKS = 10
STEP = 5
HEADS = 1238
MATS = 12
P_SIZE = 1054464
HPAD = 1280
CAT = D + CODES
A_ROWS = CAT + BLOCKS * D
BF = jnp.bfloat16
F32 = jnp.float32
GELU_C = 0.7978845608028654
GELU_K = 0.044715


def nn(a, b):
    return jnp.dot(a, b, preferred_element_type=F32)


def nt(a, b):
    return lax.dot_general(a, b, (((1,), (1,)), ((), ())), preferred_element_type=F32)


def identity(n):
    return (lax.broadcasted_iota(jnp.int32, (n, n), 0) == lax.broadcasted_iota(jnp.int32, (n, n), 1)).astype(BF)


def twice(v):
    return jnp.concatenate([v, v], 1)


def column_stats(ref, cs):
    total = jnp.sum(ref[:, cs], axis=0, keepdims=True)
    mean = total * (1.0 / D)
    square = jnp.zeros((8, mean.shape[1]), F32)
    for r in range(0, D, 32):
        cen = ref[r : r + 32, cs] - mean
        square = square + jnp.sum((cen * cen).reshape(4, 8, -1), axis=0)
    var = jnp.sum(square, axis=0, keepdims=True) * (1.0 / D)
    return mean, lax.rsqrt(var + 1e-05)


def norm_act(src, cs, gsb, xh_ref, gp_ref, rstd_ref, out):
    mean, rstd = column_stats(src, cs)
    rstd_ref[:, cs] = jnp.broadcast_to(rstd, (8, rstd.shape[1]))
    for r in range(0, D, 32):
        rs = slice(r, r + 32)
        xh = (src[rs, cs] - mean) * rstd
        xh_ref[rs, cs] = xh.astype(BF)
        y = xh * twice(gsb[rs, 0:128]) + twice(gsb[rs, 128:256])
        y2 = y * y
        p = y2 * (GELU_C * GELU_K) + GELU_C
        t = jnp.tanh(y * p)
        q = t * 0.5 + 0.5
        a = y * q
        out(rs, a)
        slope = q + (a - a * q) * (p * 6.0 - 4.0 * GELU_C)
        gp_ref[rs, cs] = slope.astype(BF)


def broadcast_vectors(vt, rows):
    k = lax.broadcasted_iota(jnp.int32, (128, 128), 0)
    picks = jnp.concatenate([(k == row).astype(BF) for row in rows], 1)
    return nn(vt, picks)


def head_stage(cs, lg, dl, ints, rw):
    width = rw.shape[1]
    it8 = lax.broadcasted_iota(jnp.int32, (8, width), 0)
    low = -jnp.inf
    b75, b150, b154 = lg[600:608], lg[1200:1208], lg[1232:1240]

    def top(block):
        return jnp.max(block, axis=0, keepdims=True)

    def top_range(lo, hi):
        best = lg[lo : lo + 8]
        for r in range(lo + 8, hi, 8):
            best = jnp.maximum(best, lg[r : r + 8])
        return best

    max_v = top(jnp.maximum(top_range(0, 600), jnp.where(it8 < 1, b75, low)))
    max_r = top(
        jnp.maximum(
            jnp.maximum(top_range(608, 1200), jnp.where(it8 >= 1, b75, low)),
            jnp.where(it8 < 2, b150, low),
        )
    )
    max_c = top(
        jnp.maximum(
            jnp.maximum(top_range(1208, 1232), jnp.where(it8 >= 2, b150, low)),
            jnp.where(it8 < 2, b154, low),
        )
    )
    in_policy = (it8 >= 2) & (it8 < 6)
    max_p = top(jnp.where(in_policy, b154, low))

    def exp_range(lo, hi, best):
        acc = jnp.zeros((8, width), F32)
        for r in range(lo, hi, 8):
            e = jnp.exp(lg[r : r + 8] - best)
            lg[r : r + 8] = e
            acc = acc + e
        return acc

    e75 = jnp.exp(b75 - jnp.where(it8 < 1, max_v, max_r))
    e150 = jnp.exp(b150 - jnp.where(it8 < 2, max_r, max_c))
    e154 = jnp.exp(b154 - jnp.where(it8 < 2, max_c, max_p))

    def total(acc):
        return rw / jnp.sum(acc, axis=0, keepdims=True)

    inv_v = total(exp_range(0, 600, max_v) + jnp.where(it8 < 1, e75, 0.0))
    inv_r = total(exp_range(608, 1200, max_r) + jnp.where(it8 >= 1, e75, 0.0) + jnp.where(it8 < 2, e150, 0.0))
    inv_c = total(exp_range(1208, 1232, max_c) + jnp.where(it8 >= 2, e150, 0.0) + jnp.where(it8 < 2, e154, 0.0))
    inv_p = total(jnp.where(in_policy, e154, 0.0))
    hit_v = ints[1:2]
    hit_r = ints[6:7] + BINS
    hit_c = ints[7:8] + 2 * BINS
    counts = jnp.where(in_policy, ints.astype(F32), 0.0)
    share = counts * (rw / jnp.sum(counts, axis=0, keepdims=True))

    def minus(value, lo, *hits):
        at = lax.broadcasted_iota(jnp.int32, value.shape, 0)
        for hit in hits:
            value = value - jnp.where(at == hit - lo, rw, 0.0)
        return value

    d75 = minus(e75 * jnp.where(it8 < 1, inv_v, inv_r), 600, hit_v, hit_r)
    d150 = minus(e150 * jnp.where(it8 < 2, inv_r, inv_c), 1200, hit_r, hit_c)
    d154 = minus(e154 * jnp.where(it8 < 2, inv_c, inv_p), 1232, hit_c) - share
    d154 = jnp.where(it8 < 6, d154, 0.0)

    def emit(lo, hi, inv, hit):
        for r in range(lo, hi, 16):
            dl[r : r + 16, cs] = minus(lg[r : r + 16] * inv, r, hit).astype(BF)

    def pair(first, second):
        return jnp.concatenate([first, second], 0).astype(BF)

    emit(0, 592, inv_v, hit_v)
    dl[592:608, cs] = pair(minus(lg[592:600] * inv_v, 592, hit_v), d75)
    emit(608, 1200, inv_r, hit_r)
    dl[1200:1216, cs] = pair(d150, minus(lg[1208:1216] * inv_c, 1208, hit_c))
    emit(1216, 1232, inv_c, hit_c)
    dl[1232:1248, cs] = pair(d154, jnp.zeros_like(d154))
    dl[1248:HPAD, cs] = jnp.zeros((HPAD - 1248, width), BF)


CB = 256


def forward_tower(t, refs):
    (eye, w, wh, vec, wct, wt, vt, gsb, xt, mix, xh, gp, rstd, stream, ints, width) = refs
    blocks = [slice(c, c + CB) for c in range(0, width, CB)]
    last = len(blocks) - 1

    def prefetch(k):
        gsb[k % 2] = broadcast_vectors(vt[...], (k, k + BLOCKS + 1, k + 2 * BLOCKS + 2))
        row = pl.multiple_of(CAT + (k - 1) * D, 32)
        wt[k % 2] = nt(eye[...], w[t, pl.ds(row, D)]).astype(BF)

    def stage(k, c):
        cs = blocks[c]

        def keep(rs, a):
            mix[t, k - 1, rs, cs] = a.astype(BF)

        norm_act(stream, cs, gsb.at[k % 2], xh.at[t, k], gp.at[t, k], rstd.at[t, k], keep)

    def product(k, c):
        return nn(wt[k % 2], mix[t, k - 1, 0:D, blocks[c]])

    def add(k, c, pre):
        stream[:, blocks[c]] = stream[:, blocks[c]] + pre + twice(gsb[k % 2, :, 256:384])

    vt[...] = nt(eye[...], vec[t]).astype(BF)
    wt[0] = nt(eye[...], w[t, 0:D]).astype(BF)
    wct[...] = nt(eye[...], w[t, D:CAT]).astype(BF)
    gsb[0] = broadcast_vectors(vt[...], (0, BLOCKS + 1, 2 * BLOCKS + 2))
    prefetch(1)
    for cs in blocks:
        it = lax.broadcasted_iota(jnp.int32, (CODES, CB), 0)
        xt[t, D:CAT, cs] = (it == ints[t, 0:1, cs]).astype(BF)
        xt[t, CAT : CAT + 16, cs] = jnp.ones((16, CB), BF)
    for c, cs in enumerate(blocks):
        pre = nn(wt[0], xt[t, 0:D, cs]) + nn(wct[...], xt[t, D:CAT, cs])
        stream[:, cs] = pre + twice(gsb[0, :, 256:384])

        def keep(rs, a):
            stream[rs, cs] = a

        norm_act(stream, cs, gsb.at[0], xh.at[t, 0], gp.at[t, 0], rstd.at[t, 0], keep)

    def layer(k, more):
        if more:
            prefetch(k + 1)
        mix[t, k - 1, D : D + 16, :] = jnp.ones((16, width), BF)
        for c in range(last + 1):
            pre = product(k, c)
            if c < last:
                stage(k, c + 1)
            elif more:
                stage(k + 1, 0)
            add(k, c, pre)

    stage(1, 0)

    @pl.loop(1, BLOCKS)
    def _(k):
        layer(k, True)

    layer(BLOCKS, False)
    for cs in blocks:
        xt[t + 1, 0:D, cs] = stream[:, cs].astype(BF)


def backward_act(cs, grad, gain, gp_ref, xh_ref, acc):
    s1 = jnp.zeros((8, CB), F32)
    s2 = jnp.zeros((8, CB), F32)
    for r in range(0, D, 16):
        rs = slice(r, r + 16)
        g = twice(gain[rs])
        dy = grad[rs, :] * gp_ref[rs, cs].astype(F32)
        prod = dy * xh_ref[rs, cs].astype(F32)
        back = dy * g
        grad[rs, :] = back
        prod_g = prod * g
        s1 = s1 + (back[0:8] + back[8:16])
        s2 = s2 + (prod_g[0:8] + prod_g[8:16])
        acc[0, rs] = acc[0, rs] + (prod[:, 0:128] + prod[:, 128:CB])
        acc[1, rs] = acc[1, rs] + (dy[:, 0:128] + dy[:, 128:CB])
    m1 = jnp.sum(s1, axis=0, keepdims=True) * (1.0 / D)
    m2 = jnp.sum(s2, axis=0, keepdims=True) * (1.0 / D)
    return m1, m2


def backward_tower(t, refs):
    (eye, w, wh, vec, wht, vt, gsb, xt, mix, xh, gp, rstd, ds, ex, br, dm, acc, lg, dl, ints, rw, gw, gh, gv, ig, width) = refs
    blocks = [slice(c, c + CB) for c in range(0, width, CB)]
    last = len(blocks) - 1
    vt[...] = nt(eye[...], vec[t]).astype(BF)
    for h in range(0, HPAD, D):
        wht[h : h + D, :] = nt(eye[...], wh[t, :, h : h + D]).astype(BF)

    @pl.loop(0, width // CB)
    def _(c):
        cs = pl.ds(pl.multiple_of(c * CB, CB), CB)
        lg[...] = nn(wht[...], xt[t + 1, 0:D, cs])
        head_stage(cs, lg, dl, ints[t, :, cs], rw[0:1, cs])
        value = nn(wh[t], dl[:, cs]) + ex[:, cs]
        ds[:, cs] = value
        br[BLOCKS % 2, :, cs] = value.astype(BF)

    gh[t] = nt(xt[t + 1, 0:D, :], dl[...]).astype(BF)
    acc[...] = jnp.zeros(acc.shape, F32)
    ones = jnp.ones((16, 128), BF)

    def spread(k):
        gsb[k % 2, :, 0:128] = broadcast_vectors(vt[...], (k,))

    def row_sums(k):
        for kind in range(2):
            gv[t, kind, pl.ds(k, 1), :] = nt(ones, acc[k % 2, kind].astype(BF))[0:1]
        acc[k % 2] = jnp.zeros(acc.shape[1:], F32)

    def product(k, c):
        row = pl.multiple_of(CAT + (k - 1) * D, 32)
        dm[c] = nn(w[t, pl.ds(row, D)], br[k % 2, :, blocks[c]])

    def stage(k, c, first):
        cs = blocks[c]
        m1, m2 = backward_act(cs, dm.at[c], gsb.at[k % 2, :, 0:128], gp.at[t, k], xh.at[t, k], acc.at[k % 2])
        rs1 = rstd[t, k, 0:1, cs]
        m1 = m1 * rs1
        m2 = m2 * rs1
        for r in range(0, D, 32):
            rs = slice(r, r + 32)
            back = dm[c, rs, :] * rs1 - m1 - xh[t, k, rs, cs].astype(F32) * m2
            if first:
                br[0, rs, cs] = back.astype(BF)
            else:
                value = ds[rs, cs] + back
                ds[rs, cs] = value
                br[(k + 1) % 2, rs, cs] = value.astype(BF)

    spread(BLOCKS)
    product(BLOCKS, 0)

    @pl.loop(0, BLOCKS)
    def _(i):
        k = BLOCKS - i
        spread(k - 1)
        for c in range(last + 1):
            if c < last:
                product(k, c + 1)
            stage(k, c, False)
            if c == 0:
                full = nt(mix[t, k - 1], br[k % 2])
                row = pl.multiple_of(CAT + (k - 1) * D, 32)
                gw[t, pl.ds(row, D), :] = full[0:D].astype(BF)
                gv[t, 2, pl.ds(k, 1), :] = full[D : D + 1]
                row_sums(k + 1)
            if c == 1:
                product(k - 1, 0)

    for c, cs in enumerate(blocks):
        dm[c] = ds[:, cs]
        stage(0, c, True)
    row_sums(1)
    row_sums(0)
    full = nt(xt[t], br[0])
    gw[t, 0:CAT, :] = full[0:CAT].astype(BF)
    gv[t, 2, 0:1, :] = full[CAT : CAT + 1]
    for cs in blocks:
        back = nn(w[t, 0:D], br[0, :, cs])
        ex[:, cs] = back
        ig[t, cs, :] = back.T


def compute_kernel(x_ref, ints, rw, w, wh, vec, st, ig, gw, gh, gv, eye, wct, wt, wht, vt, gsb, xt, mix, xh, gp, rstd, stream, ex, br, dm, acc, lg, dl):
    width = x_ref.shape[0]
    eye[...] = identity(D)
    for c in range(0, width, CB):
        cs = slice(c, c + CB)
        xt[0, 0:D, cs] = nt(eye[...], x_ref[cs, :]).astype(BF)
    fwd = (eye, w, wh, vec, wct, wt, vt, gsb, xt, mix, xh, gp, rstd, stream, ints, width)
    bwd = (eye, w, wh, vec, wht, vt, gsb, xt, mix, xh, gp, rstd, stream, ex, br, dm, acc, lg, dl, ints, rw, gw, gh, gv, ig, width)

    @pl.loop(0, 2)
    def _(t):
        forward_tower(t, fwd)

        @pl.loop(0, width // CB)
        def _(c):
            cs = pl.ds(pl.multiple_of(c * CB, CB), CB)
            st[t, cs, :] = nt(eye[...], xt[t + 1, 0:D, cs]).astype(BF)

    ex[...] = jnp.zeros_like(ex)

    @pl.loop(0, 2)
    def _(i):
        backward_tower(1 - i, bwd)


def compute(x, ints, rw, w, wh, vec):
    width = x.shape[0]
    vm = pl.BlockSpec(memory_space=pltpu.VMEM)
    return pl.pallas_call(
        compute_kernel,
        out_shape=(
            jax.ShapeDtypeStruct((2, width, D), BF),
            jax.ShapeDtypeStruct((2, width, D), F32),
            jax.ShapeDtypeStruct((2, A_ROWS, D), BF),
            jax.ShapeDtypeStruct((2, D, HPAD), BF),
            jax.ShapeDtypeStruct((2, 3, 16, D), F32),
        ),
        in_specs=[vm] * 6,
        out_specs=(vm,) * 5,
        scratch_shapes=[
            pltpu.VMEM((D, D), BF),
            pltpu.VMEM((D, CODES), BF),
            pltpu.VMEM((2, D, D), BF),
            pltpu.VMEM((HPAD, D), BF),
            pltpu.VMEM((D, 128), BF),
            pltpu.VMEM((2, D, 384), F32),
            pltpu.VMEM((3, CAT + 16, width), BF),
            pltpu.VMEM((2, BLOCKS, D + 16, width), BF),
            pltpu.VMEM((2, BLOCKS + 1, D, width), BF),
            pltpu.VMEM((2, BLOCKS + 1, D, width), BF),
            pltpu.VMEM((2, BLOCKS + 1, 8, width), F32),
            pltpu.VMEM((D, width), F32),
            pltpu.VMEM((D, width), F32),
            pltpu.VMEM((2, D, width), BF),
            pltpu.VMEM((width // CB, D, CB), F32),
            pltpu.VMEM((2, 2, D, 128), F32),
            pltpu.VMEM((HPAD, CB), F32),
            pltpu.VMEM((HPAD, width), BF),
        ],
        compiler_params=pltpu.CompilerParams(vmem_limit_bytes=62 * 1024 * 1024),
    )(x, ints, rw, w, wh, vec)


class Plan:
    def __init__(self, n, length):
        self.n, self.length = n, length
        self.rows128 = -(-length // 128)
        block_end, head_end = A_ROWS * D, A_ROWS * D + D * HEADS
        self.a_base, self.a_rows, self.h_first, self.h_rows, self.h_off, self.v_first, self.v_rows, self.v_off = ([] for _ in range(8))
        used = 0
        for i in range(n):
            lo, hi = i * length, (i + 1) * length
            base = min(lo, block_end) // D // 16 * 16
            top = -(-min(hi, block_end) // D)
            a_rows = -(-(top - base) // 16) * 16 if lo < block_end else 0
            first = min(max(lo - block_end, 0), D * HEADS) // HEADS
            last = -(-min(max(hi - block_end, 0), D * HEADS) // HEADS)
            h_rows = last - first if hi > block_end and lo < head_end else 0
            v_first = max(lo - head_end, 0) // D
            v_rows = -(-(hi - head_end) // D) - v_first if hi > head_end else 0
            self.a_base.append(base)
            self.a_rows.append(a_rows)
            self.h_first.append(first)
            self.h_rows.append(h_rows)
            self.h_off.append(a_rows)
            self.v_first.append(v_first)
            self.v_rows.append(v_rows)
            self.v_off.append(a_rows + 5 * h_rows)
            used = max(used, a_rows + 5 * h_rows + v_rows)
        self.slot = -(-(used + 1) // 32) * 32

    def at(self, table, me):
        value = jnp.int32(table[0])
        for i in range(1, self.n):
            if table[i] != table[i - 1]:
                value = value + (me >= i).astype(jnp.int32) * (table[i] - table[i - 1])
        return value


MESH = pl.DeviceIdType.MESH


def neighbours(n):
    core = lax.axis_index("tower")
    me = lax.axis_index("dp")
    near_x = me + 1 - 2 * (me % 2)
    near_y = me + 2 - 4 * ((me // 2) % 2)
    return core, me, near_x, near_y


def at(core, index):
    return {"tower": core, "dp": index}


def greet(core, me, near_x, near_y, n):
    barrier = pltpu.get_barrier_semaphore()
    pl.semaphore_signal(barrier, inc=1, device_id=at(1 - core, me), device_id_type=MESH)
    for near in (near_x, near_y):
        pl.semaphore_signal(barrier, inc=1, device_id=at(core, near), device_id_type=MESH)
    for k in range(1, n // 4):
        pl.semaphore_signal(barrier, inc=1, device_id=at(core, (me + 4 * k) % n), device_id_type=MESH)
    return barrier


def place_shard(plan, me, p_ref, slot128, shifted, rolled):
    rows = plan.rows128
    start = me * plan.length
    shift = start % 128
    first = start // 128
    tall = shifted.shape[0]
    height = p_ref.shape[0]
    lane = lax.broadcasted_iota(jnp.int32, (height, 128), 1)
    rolled[0:8] = jnp.zeros((8, 128), F32)
    rolled[8 : 8 + height] = pltpu.roll(p_ref[...], shift, 1)
    shifted[...] = jnp.zeros((tall, 128), F32)
    moved = jnp.where(lane >= shift, rolled[8 : 8 + height], rolled[7 : 7 + height])
    shifted[16 : 16 + height] = moved
    slot128[...] = jnp.zeros(slot128.shape, F32)
    row = lax.broadcasted_iota(jnp.int32, (height, 128), 0)
    base = plan.at(plan.a_base, me)

    @pl.when(plan.at(plan.a_rows, me) > 0)
    def _():
        slot128[pl.ds(first - 2 * base, height)] = jnp.where(row + first < 2 * A_ROWS, moved, 0.0)

    h_first, h_rows, h_off = (plan.at(t, me) for t in (plan.h_first, plan.h_rows, plan.h_off))
    it = lax.broadcasted_iota(jnp.int32, (10, 128), 0)
    lane10 = lax.broadcasted_iota(jnp.int32, (10, 128), 1)

    @pl.loop(0, h_rows)
    def _(k):
        begin = A_ROWS * D + HEADS * (h_first + k) - 128 * first + 128 * 16
        turn = begin % 128
        window = pltpu.roll(shifted[pl.ds(begin // 128, 16)], (128 - turn) % 128, 1)
        value = jnp.where(lane10 < 128 - turn, window[0:10], window[1:11])
        slot128[pl.ds(2 * h_off + 10 * k, 10)] = jnp.where(it * 128 + lane10 < HEADS, value, 0.0)

    v_start = (A_ROWS * D + D * HEADS) // 128
    v_rows, v_off, v_first = (plan.at(t, me) for t in (plan.v_rows, plan.v_off, plan.v_first))
    tall_v = min(height, -(-2 * max(plan.v_rows) // 8) * 8)

    @pl.when(v_rows > 0)
    def _():
        inside = plan.at([max(0, v_start - i * plan.length // 128) for i in range(plan.n)], me)
        to = 2 * v_off + first + inside - v_start - 2 * v_first
        slot128[pl.ds(to, tall_v)] = shifted[pl.ds(16 + inside, tall_v)]


def unpack_slot(plan, i, slot, w, whf, vecf, scratch):
    base, rows = plan.a_base[i], plan.a_rows[i]
    if rows:
        shared = i > 0 and base < plan.a_base[i - 1] + plan.a_rows[i - 1]
        lo = 0
        if shared:
            w[base : base + 16] = w[base : base + 16] + slot[0:16]
            lo = 16
        if rows > lo:
            w[base + lo : base + rows] = slot[lo:rows]
    h_rows, h_off, h_first = plan.h_rows[i], plan.h_off[i], plan.h_first[i]
    v_rows, v_off, v_first = plan.v_rows[i], plan.v_off[i], plan.v_first[i]
    if h_rows or v_rows:
        value = slot[...].astype(F32)
        scratch[0] = value[:, 0:128]
        scratch[1] = value[:, 128:D]
    if h_rows:
        shared = i > 0 and plan.h_rows[i - 1] and plan.h_first[i - 1] + plan.h_rows[i - 1] > h_first
        for j in range(5):
            for half in range(2):
                cols = slice(D * j + 128 * half, D * j + 128 * half + 128)
                value = scratch[half, pl.ds(h_off + j, h_rows, stride=5)]
                if shared:
                    whf[h_first : h_first + 1, cols] = whf[h_first : h_first + 1, cols] + value[0:1]
                    if h_rows > 1:
                        whf[h_first + 1 : h_first + h_rows, cols] = value[1:h_rows]
                else:
                    whf[h_first : h_first + h_rows, cols] = value
    if v_rows:
        shared = v_first and plan.v_first[i - 1] + plan.v_rows[i - 1] > v_first
        shared = shared or (i > 0 and plan.v_rows[i - 1] > 0 and v_first == 0)
        for half in range(2):
            cols = slice(128 * half, 128 * half + 128)
            value = scratch[half, v_off : v_off + v_rows]
            if shared:
                vecf[v_first : v_first + 1, cols] = vecf[v_first : v_first + 1, cols] + value[0:1]
                if v_rows > 1:
                    vecf[v_first + 1 : v_first + v_rows, cols] = value[1:v_rows]
            else:
                vecf[v_first : v_first + v_rows, cols] = value


def split3(value):
    hi = value.astype(BF).astype(F32)
    mid = (value - hi).astype(BF).astype(F32)
    return hi, mid, value - hi - mid


def gather_kernel(plan, p_ref, ints_ref, imp_ref, w, wh, vec, both, rw, slots, slot128, shifted, rolled, scratch, whf, vecf, send, recv):
    n = plan.n
    depth = n // 4
    core, me, near_x, near_y = neighbours(n)
    barrier = greet(core, me, near_x, near_y, n)
    place_shard(plan, me, p_ref, slot128, shifted, rolled)
    pl.semaphore_wait(barrier, depth + 2)
    half = rw.shape[1]
    started = []

    def copy(src, dst, slot, to):
        c = pltpu.make_async_remote_copy(
            src_ref=src, dst_ref=dst, send_sem=send.at[slot], recv_sem=recv.at[slot], device_id=to, device_id_type=MESH
        )
        c.start()
        started.append(c)
        return c

    mine = pl.multiple_of(core * half, half)
    theirs = pl.multiple_of((1 - core) * half, half)
    number = iter(range(1 << 20))
    ints_copy = copy(ints_ref.at[:, pl.ds(theirs, half)], both.at[core], next(number), at(1 - core, me))
    rows = plan.slot
    total = jnp.sum(imp_ref[...].astype(F32), axis=1, keepdims=True)
    lane = lax.broadcasted_iota(jnp.int32, (1, D), 1)
    hi, mid, lo = split3(total)
    left = slot128[pl.ds(0, rows, stride=2)]
    right = slot128[pl.ds(1, rows, stride=2)]
    own = jnp.concatenate([left, right], 1)
    last = jnp.where(lane == 0, hi, jnp.where(lane == 1, mid, jnp.where(lane == 2, lo, 0.0)))
    last_row = lax.broadcasted_iota(jnp.int32, (rows, D), 0) == rows - 1
    slots[core, me] = jnp.where(last_row, last, own).astype(BF)

    def column(index, k):
        return (index + n - 4 * k) % n

    def send_slot(origin, to, lo=0, hi=rows):
        ref = slots.at[core, origin, pl.ds(lo, hi - lo)]
        return copy(ref, ref, next(number), to)

    near_xy = near_x + near_y - me
    cut = rows // 2
    z_in, x_in, y_in, d_in, s_in = {}, {}, {}, {}, []
    for k in sorted(range(1, depth), key=lambda k: (min(k, depth - k), k)):
        z_in[k] = send_slot(me, at(core, (me + 4 * k) % n))
    order = [0] + list(z_in)
    for k in order:
        if k:
            z_in[k].wait_recv()
        x_in[k] = send_slot(column(me, k), at(core, near_x))
        y_in[k] = send_slot(column(me, k), at(core, near_y))
        s_in.append(send_slot(column(me, k), at(1 - core, me)))
    for k in order:
        x_in[k].wait_recv()
        first = send_slot(column(near_x, k), at(core, near_y), 0, cut)
        s_in.append(send_slot(column(near_x, k), at(1 - core, me)))
        y_in[k].wait_recv()
        second = send_slot(column(near_y, k), at(core, near_x), cut, rows)
        s_in.append(send_slot(column(near_y, k), at(1 - core, me)))
        d_in[k] = (first, second)
    for k in order:
        for c in d_in[k]:
            c.wait_recv()
        s_in.append(send_slot(column(near_xy, k), at(1 - core, me)))
    ints_copy.wait_recv()
    both[core] = ints_ref[:, pl.ds(mine, half)]
    for c in s_in:
        c.wait_recv()
    for c in started:
        c.wait_send()
    whf[:, 1152:HPAD] = jnp.zeros((D, 128), F32)
    for t in range(2):
        vecf[...] = jnp.zeros(vecf.shape, F32)
        for i in range(n):
            unpack_slot(plan, i, slots.at[t, i], w.at[t], whf, vecf, scratch)
        wh[t] = whf[...].astype(BF)
        vec[t] = vecf[...].astype(BF)
    total = jnp.zeros((1, D), F32)
    for i in range(n):
        tail = slots[0, i, rows - 16 : rows].astype(F32)
        total = total + tail[15:16]
    weight_sum = jnp.sum(jnp.where(lane < 3, total, 0.0), axis=1, keepdims=True)
    rw[...] = jnp.broadcast_to(imp_ref[:, pl.ds(mine, half)].astype(F32) / weight_sum, (8, half))


def gather(plan, p128, ints, imp):
    n, rows = plan.n, plan.slot
    half = ints.shape[1] // 2
    vm = pl.BlockSpec(memory_space=pltpu.VMEM)
    height = p128.shape[0]
    tall = max(2 * rows, height + 40) + 80
    copies = 1 + (n // 4 - 1) + 2 * (n // 4) + 2 * (n // 4) + n
    return pl.pallas_call(
        functools.partial(gather_kernel, plan),
        out_shape=(
            jax.ShapeDtypeStruct((2, A_ROWS, D), BF),
            jax.ShapeDtypeStruct((2, D, HPAD), BF),
            jax.ShapeDtypeStruct((2, 128, D), BF),
            jax.ShapeDtypeStruct((2, 8, half), jnp.int32),
            jax.ShapeDtypeStruct((8, half), F32),
        ),
        in_specs=[vm] * 3,
        out_specs=(vm,) * 5,
        scratch_shapes=[
            pltpu.VMEM((2, n, rows, D), BF),
            pltpu.VMEM((tall, 128), F32),
            pltpu.VMEM((height + 128, 128), F32),
            pltpu.VMEM((height + 8, 128), F32),
            pltpu.VMEM((2, rows, 128), F32),
            pltpu.VMEM((D, HPAD), F32),
            pltpu.VMEM((128, D), F32),
            pltpu.SemaphoreType.DMA((copies,)),
            pltpu.SemaphoreType.DMA((copies,)),
        ],
        compiler_params=pltpu.CompilerParams(
            collective_id=0, has_side_effects=True, vmem_limit_bytes=48 * 1024 * 1024
        ),
    )(p128, ints, imp)


def lay_flat(plan, me, slot128, flat, rolled):
    height = rolled.shape[0] - 16
    start = me * plan.length
    shift = start % 128
    first = start // 128
    base = plan.at(plan.a_base, me)
    row = lax.broadcasted_iota(jnp.int32, (height + 8, 128), 0)
    flat[...] = jnp.zeros(flat.shape, F32)

    @pl.when(plan.at(plan.a_rows, me) > 0)
    def _():
        rows = slot128[pl.ds(first - 2 * base, height + 8)]
        flat[16 : 24 + height] = jnp.where(row + first < 2 * A_ROWS, rows, 0.0)

    h_first, h_rows, h_off = (plan.at(t, me) for t in (plan.h_first, plan.h_rows, plan.h_off))
    it = lax.broadcasted_iota(jnp.int32, (16, 128), 0)
    lane = lax.broadcasted_iota(jnp.int32, (16, 128), 1)

    @pl.loop(0, h_rows)
    def _(k):
        begin = A_ROWS * D + HEADS * (h_first + k) - 128 * first + 128 * 16
        turn = begin % 128
        value = slot128[pl.ds(2 * h_off + 10 * k, 16)]
        value = jnp.where(it * 128 + lane < HEADS, value, 0.0)
        value = pltpu.roll(value, turn, 1)
        above = jnp.concatenate([jnp.zeros((8, 128), F32), value], 0)[7:23]
        to = pl.ds(begin // 128, 16)
        flat[to] = flat[to] + jnp.where(lane >= turn, value, above)

    v_start = (A_ROWS * D + D * HEADS) // 128
    v_rows, v_off, v_first = (plan.at(t, me) for t in (plan.v_rows, plan.v_off, plan.v_first))
    tall_v = min(height, -(-2 * max(plan.v_rows) // 8) * 8)

    @pl.when(v_rows > 0)
    def _():
        inside = plan.at([max(0, v_start - i * plan.length // 128) for i in range(plan.n)], me)
        source = 2 * v_off + first + inside - v_start - 2 * v_first
        to = pl.ds(16 + inside, tall_v)
        flat[to] = flat[to] + slot128[pl.ds(source, tall_v)]

    rolled[0 : height + 8] = pltpu.roll(flat[16 : 24 + height], (128 - shift) % 128, 1)
    lane = lax.broadcasted_iota(jnp.int32, (height, 128), 1)
    return jnp.where(lane < 128 - shift, rolled[0:height], rolled[1 : height + 1])


def pack_slots(plan, core, gw, gh, gv, rgw, rgh, rgv, slots, sums, vsum, scratch):
    total = gv[core].astype(F32) + rgv[...]
    for kind in range(3):
        vsum[kind * (BLOCKS + 1) : (kind + 1) * (BLOCKS + 1)] = total[kind, 0 : BLOCKS + 1]
    sums[...] = gh[core].astype(F32) + rgh[...].astype(F32)
    for i in range(plan.n):
        base, rows = plan.a_base[i], plan.a_rows[i]
        h_rows, h_off, h_first = plan.h_rows[i], plan.h_off[i], plan.h_first[i]
        v_rows, v_off, v_first = plan.v_rows[i], plan.v_off[i], plan.v_first[i]
        slots[i, rows : plan.slot] = jnp.zeros((plan.slot - rows, D), BF)
        if rows:
            added = gw[core, base : base + rows].astype(F32) + rgw[base : base + rows].astype(F32)
            slots[i, 0:rows] = added.astype(BF)
        if h_rows or v_rows:
            scratch[...] = jnp.zeros(scratch.shape, F32)
            for half in range(2):
                for j in range(5 if h_rows else 0):
                    cols = slice(D * j + 128 * half, D * j + 128 * half + 128)
                    scratch[half, pl.ds(h_off + j, h_rows, stride=5)] = sums[h_first : h_first + h_rows, cols]
                if v_rows:
                    scratch[half, v_off : v_off + v_rows] = vsum[v_first : v_first + v_rows, 128 * half : 128 * half + 128]
            whole = jnp.concatenate([scratch[0], scratch[1]], 1)
            slots[i, rows : plan.slot] = whole[rows:].astype(BF)


def segment_bounds():
    first = [0] + [(CAT + j * D) * D for j in range(BLOCKS + 1)]
    return list(zip(first, first[1:] + [A_ROWS * D + D * HEADS]))


def reduce_kernel(
    plan, gw, gh, gv, st, ig, p_ref, m_ref, v_ref,
    st_out, ig_out, first_out, second_out, new_out, low_out, norm_out,
    rgw, rgh, rgv, slots, sums, vsum, scratch, in_d, in_x, in_y, in_z, slot128, flat, rolled, squares, sq_z, sq_y, sq_x,
    send, recv, local,
):
    n, rows = plan.n, plan.slot
    depth, cut = n // 4, plan.slot // 2
    core, me, near_x, near_y = neighbours(n)
    near_xy = near_x + near_y - me
    barrier = greet(core, me, near_x, near_y, n)
    pl.semaphore_wait(barrier, depth + 2)
    half = st.shape[1]
    number = iter(range(1 << 20))
    started = []

    def copy(src, dst, to):
        slot = next(number)
        c = pltpu.make_async_remote_copy(
            src_ref=src, dst_ref=dst, send_sem=send.at[slot], recv_sem=recv.at[slot], device_id=to, device_id_type=MESH
        )
        c.start()
        started.append(c)
        return c

    def column(index, k):
        return (index + n - 4 * k) % n

    sibling = at(1 - core, me)
    early = [
        copy(gw.at[1 - core], rgw, sibling),
        copy(gh.at[1 - core], rgh, sibling),
        copy(gv.at[1 - core], rgv, sibling),
    ]
    mine = pl.ds(pl.multiple_of(core * half, half), half)
    late = [
        copy(st.at[1 - core], st_out.at[mine], sibling),
        copy(ig.at[1 - core], ig_out.at[mine], sibling),
    ]
    stay = [
        pltpu.make_async_copy(st.at[core], st_out.at[mine], local.at[0]),
        pltpu.make_async_copy(ig.at[core], ig_out.at[mine], local.at[1]),
    ]
    for c in stay:
        c.start()
    for c in early:
        c.wait_recv()
    pack_slots(plan, core, gw, gh, gv, rgw, rgh, rgv, slots, sums, vsum, scratch)
    order = list(range(1, depth)) + [0]
    to_x, to_y = at(core, near_x), at(core, near_y)
    halves = {}
    for k in order:
        diagonal = column(near_xy, k)
        halves[k] = (
            copy(slots.at[diagonal, pl.ds(0, cut)], in_d.at[k, pl.ds(0, cut)], to_y),
            copy(slots.at[diagonal, pl.ds(cut, rows - cut)], in_d.at[k, pl.ds(cut, rows - cut)], to_x),
        )
    fulls = {}
    for k in order:
        ox, oy = column(near_x, k), column(near_y, k)
        halves[k][0].wait_recv()
        slots[ox, 0:cut] = (slots[ox, 0:cut].astype(F32) + in_d[k, 0:cut].astype(F32)).astype(BF)
        first = copy(slots.at[ox], in_x.at[k], to_x)
        halves[k][1].wait_recv()
        slots[oy, cut:rows] = (slots[oy, cut:rows].astype(F32) + in_d[k, cut:rows].astype(F32)).astype(BF)
        fulls[k] = (first, copy(slots.at[oy], in_y.at[k], to_y))
    along = {}
    for k in order:
        own = column(me, k)
        for c in fulls[k]:
            c.wait_recv()
        if k:
            total = slots[own].astype(F32) + in_x[k].astype(F32) + in_y[k].astype(F32)
            slots[own] = total.astype(BF)
            along[k] = copy(slots.at[own], in_z.at[k], at(core, own))
    for c in along.values():
        c.wait_recv()
    total = slots[me].astype(F32) + in_x[0].astype(F32) + in_y[0].astype(F32)
    for k in along:
        total = total + in_z[k].astype(F32)
    slot128[...] = jnp.zeros(slot128.shape, F32)
    slot128[pl.ds(0, rows, stride=2)] = total[:, 0:128]
    slot128[pl.ds(1, rows, stride=2)] = total[:, 128:D]
    grad = lay_flat(plan, me, slot128, flat, rolled)

    height = p_ref.shape[0]
    place = 128 * lax.broadcasted_iota(jnp.int32, (height, 128), 0) + lax.broadcasted_iota(jnp.int32, (height, 128), 1)
    grad = jnp.where(place < plan.length, grad, 0.0)
    position = place + me * plan.length
    master = p_ref[...]
    correction = 1.0 - 0.5**STEP
    first_new = 0.5 * m_ref[...] + 0.5 * grad
    second_new = 0.5 * v_ref[...] + 0.5 * grad * grad
    first_out[...] = first_new
    second_out[...] = second_new
    bounds = segment_bounds()
    is_matrix = position < bounds[-1][1]
    update = first_new / correction / (jnp.sqrt(second_new / correction) + 1e-06) + jnp.where(is_matrix, 0.01 * master, 0.0)
    update = jnp.where(place < plan.length, update, 0.0)
    p_square, u_square = master * master, update * update
    flat[0:height] = update
    squares[...] = jnp.zeros(squares.shape, F32)
    for j, (lo, hi) in enumerate(bounds):
        inside = (position >= lo) & (position < hi)
        squares[0, j : j + 1] = jnp.sum(jnp.where(inside, p_square, 0.0), axis=0, keepdims=True)
        squares[0, 16 + j : 17 + j] = jnp.sum(jnp.where(inside, u_square, 0.0), axis=0, keepdims=True)
    steps = [copy(squares.at[0], sq_z.at[k], at(core, column(me, k))) for k in range(1, depth)]
    for c in steps:
        c.wait_recv()
    total = squares[0]
    for k in range(1, depth):
        total = total + sq_z[k]
    squares[1] = total
    copy(squares.at[1], sq_y, to_y).wait_recv()
    squares[2] = squares[1] + sq_y[...]
    copy(squares.at[2], sq_x, to_x).wait_recv()
    norm = jnp.sqrt(jnp.sum(squares[2] + sq_x[...], axis=1, keepdims=True))
    norm_out[...] = jnp.broadcast_to(norm, (32, 128))
    ratio = norm[0:16] / norm[16:32]
    factor = jnp.ones((height, 128), F32)
    for j, (lo, hi) in enumerate(bounds):
        inside = (position >= lo) & (position < hi)
        factor = jnp.where(inside, ratio[j : j + 1], factor)
    new = p_ref[...] - 0.5 * factor * flat[0:height]
    new_out[...] = new
    low_out[...] = new.astype(BF)
    for c in late:
        c.wait_recv()
    for c in stay:
        c.wait()
    for c in started:
        c.wait_send()


def reduce_and_update(plan, gw, gh, gv, st, ig, p128, m128, v128):
    n, rows = plan.n, plan.slot
    depth = n // 4
    half = st.shape[1]
    height = p128.shape[0]
    vm = pl.BlockSpec(memory_space=pltpu.VMEM)
    hbm = pl.BlockSpec(memory_space=pl.ANY)
    copies = 5 + 2 * depth + 2 * depth + (depth - 1) + (depth - 1) + 2
    flat32 = jax.ShapeDtypeStruct((height, 128), F32)
    return pl.pallas_call(
        functools.partial(reduce_kernel, plan),
        out_shape=(
            jax.ShapeDtypeStruct((2 * half, D), BF),
            jax.ShapeDtypeStruct((2 * half, D), F32),
            flat32,
            flat32,
            flat32,
            jax.ShapeDtypeStruct((height, 128), BF),
            jax.ShapeDtypeStruct((32, 128), F32),
        ),
        in_specs=[vm] * 3 + [hbm] * 2 + [vm] * 3,
        out_specs=(hbm, hbm, vm, vm, vm, vm, vm),
        scratch_shapes=[
            pltpu.VMEM((A_ROWS, D), BF),
            pltpu.VMEM((D, HPAD), BF),
            pltpu.VMEM(gv.shape[1:], F32),
            pltpu.VMEM((n, rows, D), BF),
            pltpu.VMEM((D, HPAD), F32),
            pltpu.VMEM((40, D), F32),
            pltpu.VMEM((2, rows, 128), F32),
            pltpu.VMEM((depth, rows, D), BF),
            pltpu.VMEM((depth, rows, D), BF),
            pltpu.VMEM((depth, rows, D), BF),
            pltpu.VMEM((depth, rows, D), BF),
            pltpu.VMEM((max(2 * rows, height + 48) + 80, 128), F32),
            pltpu.VMEM((height + 128, 128), F32),
            pltpu.VMEM((height + 16, 128), F32),
            pltpu.VMEM((3, 32, 128), F32),
            pltpu.VMEM((depth, 32, 128), F32),
            pltpu.VMEM((32, 128), F32),
            pltpu.VMEM((32, 128), F32),
            pltpu.SemaphoreType.DMA((copies,)),
            pltpu.SemaphoreType.DMA((copies,)),
            pltpu.SemaphoreType.DMA((2,)),
        ],
        compiler_params=pltpu.CompilerParams(
            collective_id=1, has_side_effects=True, vmem_limit_bytes=48 * 1024 * 1024
        ),
    )(gw, gh, gv, st, ig, p128, m128, v128)


def on_device(latent, codes, targets, visits, importance, params, first_moment, second_moment):
    me = lax.axis_index("tower")
    row_count = latent.shape[0]
    half = row_count // 2
    shard_len = params.shape[1]
    plan = Plan(lax.axis_size("dp"), shard_len)
    height = -(-plan.rows128 // 8) * 8

    def to_rows(value):
        return jnp.pad(value[0], (0, 128 * height - shard_len)).reshape(height, 128)

    p128 = to_rows(params)
    ints = jnp.concatenate([codes, targets[0, :1], visits[0].T, targets[0, 1:]], 0)
    x = lax.dynamic_slice_in_dim(latent, me * half, half, 0)
    w, wh, vec, both, rw = gather(plan, p128, ints, importance[None])
    st, ig, gw, gh, gv = compute(x, both, rw, w, wh, vec)

    states_out, inputs_out, *flat, low, norm = reduce_and_update(
        plan, gw, gh, gv, st, ig, p128, to_rows(first_moment), to_rows(second_moment)
    )

    def shard(value):
        return value.reshape(1, -1)[:, :shard_len]

    norms = jnp.stack([norm[:MATS, 0], norm[16 : 16 + MATS, 0]])[None]
    return (states_out[None], inputs_out[None], *(shard(v) for v in flat), shard(low), norms)


def solution(mesh):
    in_specs = (
        P("dp", None),
        P("tower", "dp"),
        P("tower", None, "dp"),
        P("tower", "dp", None),
        P("dp"),
        P("tower", "dp"),
        P("tower", "dp"),
        P("tower", "dp"),
    )
    out_specs = (
        P("tower", "dp", None),
        P("tower", "dp", None),
        P("tower", "dp"),
        P("tower", "dp"),
        P("tower", "dp"),
        P("tower", "dp"),
        P("tower", None, None),
    )
    return jax.shard_map(
        on_device, mesh=mesh, in_specs=in_specs, out_specs=out_specs, check_vma=False
    )
```

```python
import functools

import jax
import jax.numpy as jnp
from jax import lax
from jax.experimental import pallas as pl
from jax.experimental.pallas import tpu as pltpu
from jax.sharding import PartitionSpec as P

D = 256
CODES = 32
BINS = 601
BLOCKS = 10
STEP = 5
HEADS = 1238
MATS = 12
P_SIZE = 1054464
HPAD = 1280
CAT = D + CODES
A_ROWS = CAT + BLOCKS * D
BF = jnp.bfloat16
F32 = jnp.float32
GELU_C = 0.7978845608028654
GELU_K = 0.044715


def nn(a, b):
    return jnp.dot(a, b, preferred_element_type=F32)


def nt(a, b):
    return lax.dot_general(a, b, (((1,), (1,)), ((), ())), preferred_element_type=F32)


def identity(n):
    return (lax.broadcasted_iota(jnp.int32, (n, n), 0) == lax.broadcasted_iota(jnp.int32, (n, n), 1)).astype(BF)


def twice(v):
    return jnp.concatenate([v, v], 1)


def column_stats(ref, cs):
    total = jnp.sum(ref[:, cs], axis=0, keepdims=True)
    mean = total * (1.0 / D)
    square = jnp.zeros((8, mean.shape[1]), F32)
    for r in range(0, D, 32):
        cen = ref[r : r + 32, cs] - mean
        square = square + jnp.sum((cen * cen).reshape(4, 8, -1), axis=0)
    var = jnp.sum(square, axis=0, keepdims=True) * (1.0 / D)
    return mean, lax.rsqrt(var + 1e-05)


def norm_act(src, cs, gsb, xh_ref, gp_ref, rstd_ref, out):
    mean, rstd = column_stats(src, cs)
    rstd_ref[:, cs] = rstd
    for r in range(0, D, 32):
        rs = slice(r, r + 32)
        xh = (src[rs, cs] - mean) * rstd
        xh_ref[rs, cs] = xh.astype(BF)
        y = xh * twice(gsb[rs, 0:128]) + twice(gsb[rs, 128:256])
        y2 = y * y
        p = y2 * (GELU_C * GELU_K) + GELU_C
        t = jnp.tanh(y * p)
        q = t * 0.5 + 0.5
        a = y * q
        out(rs, a)
        slope = q + (a - a * q) * (p * 6.0 - 4.0 * GELU_C)
        gp_ref[rs, cs] = slope.astype(BF)


def broadcast_vectors(vt, rows):
    k = lax.broadcasted_iota(jnp.int32, (128, 128), 0)
    picks = jnp.concatenate([(k == row).astype(BF) for row in rows], 1)
    return nn(vt, picks)


def head_stage(cs, lg, dl, ints, rw):
    width = rw.shape[1]
    it8 = lax.broadcasted_iota(jnp.int32, (8, width), 0)
    low = -jnp.inf
    b75, b150, b154 = lg[600:608], lg[1200:1208], lg[1232:1240]

    def top(block):
        return jnp.max(block, axis=0, keepdims=True)

    def top_range(lo, hi):
        best = lg[lo : lo + 8]
        for r in range(lo + 8, hi, 8):
            best = jnp.maximum(best, lg[r : r + 8])
        return best

    max_v = top(jnp.maximum(top_range(0, 600), jnp.where(it8 < 1, b75, low)))
    max_r = top(
        jnp.maximum(
            jnp.maximum(top_range(608, 1200), jnp.where(it8 >= 1, b75, low)),
            jnp.where(it8 < 2, b150, low),
        )
    )
    max_c = top(
        jnp.maximum(
            jnp.maximum(top_range(1208, 1232), jnp.where(it8 >= 2, b150, low)),
            jnp.where(it8 < 2, b154, low),
        )
    )
    in_policy = (it8 >= 2) & (it8 < 6)
    max_p = top(jnp.where(in_policy, b154, low))

    def exp_range(lo, hi, best):
        acc = jnp.zeros((8, width), F32)
        for r in range(lo, hi, 8):
            e = jnp.exp(lg[r : r + 8] - best)
            lg[r : r + 8] = e
            acc = acc + e
        return acc

    e75 = jnp.exp(b75 - jnp.where(it8 < 1, max_v, max_r))
    e150 = jnp.exp(b150 - jnp.where(it8 < 2, max_r, max_c))
    e154 = jnp.exp(b154 - jnp.where(it8 < 2, max_c, max_p))

    def total(acc):
        return rw / jnp.sum(acc, axis=0, keepdims=True)

    inv_v = total(exp_range(0, 600, max_v) + jnp.where(it8 < 1, e75, 0.0))
    inv_r = total(exp_range(608, 1200, max_r) + jnp.where(it8 >= 1, e75, 0.0) + jnp.where(it8 < 2, e150, 0.0))
    inv_c = total(exp_range(1208, 1232, max_c) + jnp.where(it8 >= 2, e150, 0.0) + jnp.where(it8 < 2, e154, 0.0))
    inv_p = total(jnp.where(in_policy, e154, 0.0))
    hit_v = ints[1:2]
    hit_r = ints[6:7] + BINS
    hit_c = ints[7:8] + 2 * BINS
    counts = jnp.where(in_policy, ints.astype(F32), 0.0)
    share = counts * (rw / jnp.sum(counts, axis=0, keepdims=True))

    def minus(value, lo, *hits):
        at = lax.broadcasted_iota(jnp.int32, value.shape, 0)
        for hit in hits:
            value = value - jnp.where(at == hit - lo, rw, 0.0)
        return value

    d75 = minus(e75 * jnp.where(it8 < 1, inv_v, inv_r), 600, hit_v, hit_r)
    d150 = minus(e150 * jnp.where(it8 < 2, inv_r, inv_c), 1200, hit_r, hit_c)
    d154 = minus(e154 * jnp.where(it8 < 2, inv_c, inv_p), 1232, hit_c) - share
    d154 = jnp.where(it8 < 6, d154, 0.0)

    def emit(lo, hi, inv, hit):
        for r in range(lo, hi, 16):
            dl[r : r + 16, cs] = minus(lg[r : r + 16] * inv, r, hit).astype(BF)

    def pair(first, second):
        return jnp.concatenate([first, second], 0).astype(BF)

    emit(0, 592, inv_v, hit_v)
    dl[592:608, cs] = pair(minus(lg[592:600] * inv_v, 592, hit_v), d75)
    emit(608, 1200, inv_r, hit_r)
    dl[1200:1216, cs] = pair(d150, minus(lg[1208:1216] * inv_c, 1208, hit_c))
    emit(1216, 1232, inv_c, hit_c)
    dl[1232:1248, cs] = pair(d154, jnp.zeros_like(d154))
    dl[1248:HPAD, cs] = jnp.zeros((HPAD - 1248, width), BF)


CB = 256


def saved_views(t, mix, xh):
    def mixed(k):
        return mix.at[pl.ds(pl.multiple_of((t * BLOCKS + k - 1) * (D + 16), 16), D + 16)]

    def unit(k):
        return xh.at[pl.ds(pl.multiple_of((t * (BLOCKS + 1) + k) * D, D), D)]

    return mixed, unit


def forward_tower(t, refs, during=None):
    (eye, w, wh, vec, wct, wt, vt, gsb, xt, mix, xh, gp, rstd, stream, ints, width) = refs
    blocks = [slice(c, c + CB) for c in range(0, width, CB)]
    last = len(blocks) - 1
    mixed, unit = saved_views(t, mix, xh)

    def prefetch(k):
        gsb[k % 2] = broadcast_vectors(vt[...], (k, k + BLOCKS + 1, k + 2 * BLOCKS + 2))
        row = pl.multiple_of(CAT + (k - 1) * D, 32)
        wt[k % 2] = nt(eye[...], w[t, pl.ds(row, D)]).astype(BF)

    def stage(k, c):
        cs = blocks[c]

        def keep(rs, a):
            mixed(k)[rs, cs] = a.astype(BF)

        norm_act(stream, cs, gsb.at[k % 2], unit(k), gp.at[t, k], rstd.at[pl.ds(t * (BLOCKS + 1) + k, 1)], keep)

    def product(k, c):
        return nn(wt[k % 2], mixed(k)[0:D, blocks[c]])

    def add(k, c, pre):
        stream[:, blocks[c]] = stream[:, blocks[c]] + pre + twice(gsb[k % 2, :, 256:384])

    vt[...] = nt(eye[...], vec[t]).astype(BF)
    wt[0] = nt(eye[...], w[t, 0:D]).astype(BF)
    wct[...] = nt(eye[...], w[t, D:CAT]).astype(BF)
    gsb[0] = broadcast_vectors(vt[...], (0, BLOCKS + 1, 2 * BLOCKS + 2))
    prefetch(1)
    for cs in blocks:
        it = lax.broadcasted_iota(jnp.int32, (CODES, CB), 0)
        xt[t, D:CAT, cs] = (it == ints[t, 0:1, cs]).astype(BF)
        xt[t, CAT : CAT + 16, cs] = jnp.ones((16, CB), BF)
    for c, cs in enumerate(blocks):
        pre = nn(wt[0], xt[t, 0:D, cs]) + nn(wct[...], xt[t, D:CAT, cs])
        stream[:, cs] = pre + twice(gsb[0, :, 256:384])

        def keep(rs, a):
            stream[rs, cs] = a

        norm_act(stream, cs, gsb.at[0], unit(0), gp.at[t, 0], rstd.at[pl.ds(t * (BLOCKS + 1), 1)], keep)

    def layer(k, more):
        if more:
            prefetch(k + 1)
        mixed(k)[D : D + 16, :] = jnp.ones((16, width), BF)
        for c in range(last + 1):
            pre = product(k, c)
            if c < last:
                stage(k, c + 1)
            elif more:
                stage(k + 1, 0)
            add(k, c, pre)

    stage(1, 0)

    @pl.loop(1, BLOCKS)
    def _(k):
        if during is not None:
            during(k)
        layer(k, True)

    layer(BLOCKS, False)
    for cs in blocks:
        xt[t + 1, 0:D, cs] = stream[:, cs].astype(BF)


def backward_act(cs, grad, gain, gp_ref, xh_ref, acc):
    s1 = jnp.zeros((8, CB), F32)
    s2 = jnp.zeros((8, CB), F32)
    for r in range(0, D, 16):
        rs = slice(r, r + 16)
        g = twice(gain[rs])
        dy = grad[rs, :] * gp_ref[rs, cs].astype(F32)
        prod = dy * xh_ref[rs, cs].astype(F32)
        back = dy * g
        grad[rs, :] = back
        prod_g = prod * g
        s1 = s1 + (back[0:8] + back[8:16])
        s2 = s2 + (prod_g[0:8] + prod_g[8:16])
        acc[0, rs] = acc[0, rs] + (prod[:, 0:128] + prod[:, 128:CB])
        acc[1, rs] = acc[1, rs] + (dy[:, 0:128] + dy[:, 128:CB])
    m1 = jnp.sum(s1, axis=0, keepdims=True) * (1.0 / D)
    m2 = jnp.sum(s2, axis=0, keepdims=True) * (1.0 / D)
    return m1, m2


def backward_tower(t, refs, after_head=None, during=None, before_product=None):
    (eye, w, wh, vec, wht, vt, gsb, xt, mix, xh, gp, rstd, ds, ex, br, dm, acc, lg, dl, ints, rw, gw, gh, gv, ig, width) = refs
    blocks = [slice(c, c + CB) for c in range(0, width, CB)]
    last = len(blocks) - 1
    mixed, unit = saved_views(t, mix, xh)
    vt[...] = nt(eye[...], vec[t]).astype(BF)
    for h in range(0, HPAD, D):
        wht[h : h + D, :] = nt(eye[...], wh[t, :, h : h + D]).astype(BF)

    @pl.loop(0, width // CB)
    def _(c):
        cs = pl.ds(pl.multiple_of(c * CB, CB), CB)
        lg[...] = nn(wht[...], xt[t + 1, 0:D, cs])
        head_stage(cs, lg, dl, ints[t, :, cs], rw[0:1, cs])
        value = nn(wh[t], dl[:, cs]) + ex[:, cs]
        ds[:, cs] = value
        br[BLOCKS % 2, :, cs] = value.astype(BF)

    for h in range(0, HPAD, D):
        gh[t, :, h : h + D] = nt(xt[t + 1, 0:D, :], dl[h : h + D]).astype(BF)
    if after_head is not None:
        after_head()
    acc[...] = jnp.zeros(acc.shape, F32)
    ones = jnp.ones((16, 128), BF)

    def part(c):
        return dm.at[c * D : c * D + D]

    def spread(k):
        gsb[k % 2, :, 0:128] = broadcast_vectors(vt[...], (k,))

    def row_sums(k):
        for kind in range(2):
            gv[t, kind, pl.ds(k, 1), :] = nt(ones, acc[k % 2, kind].astype(BF))[0:1]
        acc[k % 2] = jnp.zeros(acc.shape[1:], F32)

    def product(k, c):
        row = pl.multiple_of(CAT + (k - 1) * D, 32)
        part(c)[...] = nn(w[t, pl.ds(row, D)], br[k % 2, :, blocks[c]])

    def stage(k, c, first):
        cs = blocks[c]
        m1, m2 = backward_act(cs, part(c), gsb.at[k % 2, :, 0:128], gp.at[t, k], unit(k), acc.at[k % 2])
        rs1 = rstd[pl.ds(t * (BLOCKS + 1) + k, 1), cs]
        m1 = m1 * rs1
        m2 = m2 * rs1
        for r in range(0, D, 32):
            rs = slice(r, r + 32)
            back = part(c)[rs, :] * rs1 - m1 - unit(k)[rs, cs].astype(F32) * m2
            if first:
                br[0, rs, cs] = back.astype(BF)
            else:
                value = ds[rs, cs] + back
                ds[rs, cs] = value
                br[(k + 1) % 2, rs, cs] = value.astype(BF)

    if before_product is not None:
        before_product()
    spread(BLOCKS)
    product(BLOCKS, 0)

    @pl.loop(0, BLOCKS)
    def _(i):
        k = BLOCKS - i
        if during is not None:
            during(i)
        spread(k - 1)
        for c in range(last + 1):
            if c < last:
                product(k, c + 1)
            stage(k, c, False)
            if c == 0:
                full = nt(mixed(k)[...], br[k % 2])
                row = pl.multiple_of(CAT + (k - 1) * D, 32)
                gw[t, pl.ds(row, D), :] = full[0:D].astype(BF)
                gv[t, 2, pl.ds(k, 1), :] = full[D : D + 1]
                row_sums(k + 1)
            if c == 1:
                product(k - 1, 0)

    for c, cs in enumerate(blocks):
        part(c)[...] = ds[:, cs]
        stage(0, c, True)
    row_sums(1)
    row_sums(0)
    full = nt(xt[t], br[0])
    gw[t, 0:CAT, :] = full[0:CAT].astype(BF)
    gv[t, 2, 0:1, :] = full[CAT : CAT + 1]
    for cs in blocks:
        back = nn(w[t, 0:D], br[0, :, cs])
        ex[:, cs] = back
        ig[cs, :] = back.T


def compute_kernel(x_ref, ints, rw, w, wh, vec, st, ig, gw, gh, gv, eye, wct, wt, wht, vt, gsb, xt, mix, xh, gp, rstd, stream, ex, br, dm, acc, lg, dl):
    width = x_ref.shape[0]
    eye[...] = identity(D)
    for c in range(0, width, CB):
        cs = slice(c, c + CB)
        xt[0, 0:D, cs] = nt(eye[...], x_ref[cs, :]).astype(BF)
    fwd = (eye, w, wh, vec, wct, wt, vt, gsb, xt, mix, xh, gp, rstd, stream, ints, width)
    @pl.loop(0, 2)
    def _(t):
        forward_tower(t, fwd)

        @pl.loop(0, width // CB)
        def _(c):
            cs = pl.ds(pl.multiple_of(c * CB, CB), CB)
            st[t, cs, :] = nt(eye[...], xt[t + 1, 0:D, cs]).astype(BF)

    ex[...] = jnp.zeros_like(ex)

    @pl.loop(0, 2)
    def _(i):
        t = 1 - i
        backward_tower(
            t,
            (eye, w, wh, vec, wht, vt, gsb, xt, mix, xh, gp, rstd, stream, ex, br, dm, acc, lg, dl, ints, rw, gw, gh, gv, ig.at[t], width),
        )


def work_scratch(width):
    return [
        pltpu.VMEM((D, D), BF),
        pltpu.VMEM((D, CODES), BF),
        pltpu.VMEM((2, D, D), BF),
        pltpu.VMEM((HPAD, D), BF),
        pltpu.VMEM((D, 128), BF),
        pltpu.VMEM((2, D, 384), F32),
        pltpu.VMEM((3, CAT + 16, width), BF),
        pltpu.VMEM((2 * BLOCKS * (D + 16), width), BF),
        pltpu.VMEM((2 * (BLOCKS + 1) * D, width), BF),
        pltpu.VMEM((2, BLOCKS + 1, D, width), BF),
        pltpu.VMEM((24, width), F32),
        pltpu.VMEM((D, width), F32),
        pltpu.VMEM((D, width), F32),
        pltpu.VMEM((2, D, width), BF),
        pltpu.VMEM((width // CB * D, CB), F32),
        pltpu.VMEM((2, 2, D, 128), F32),
        pltpu.VMEM((HPAD, CB), F32),
        pltpu.VMEM((HPAD, width), BF),
    ]


def compute(x, ints, rw, w, wh, vec):
    width = x.shape[0]
    vm = pl.BlockSpec(memory_space=pltpu.VMEM)
    return pl.pallas_call(
        compute_kernel,
        out_shape=(
            jax.ShapeDtypeStruct((2, width, D), BF),
            jax.ShapeDtypeStruct((2, width, D), F32),
            jax.ShapeDtypeStruct((2, A_ROWS, D), BF),
            jax.ShapeDtypeStruct((2, D, HPAD), BF),
            jax.ShapeDtypeStruct((2, 3, 16, D), F32),
        ),
        in_specs=[vm] * 6,
        out_specs=(vm,) * 5,
        scratch_shapes=work_scratch(width),
        compiler_params=pltpu.CompilerParams(vmem_limit_bytes=62 * 1024 * 1024),
    )(x, ints, rw, w, wh, vec)


class Plan:
    def __init__(self, n, length):
        self.n, self.length = n, length
        self.rows128 = -(-length // 128)
        block_end, head_end = A_ROWS * D, A_ROWS * D + D * HEADS
        self.a_base, self.a_rows, self.h_first, self.h_rows, self.h_off, self.v_first, self.v_rows, self.v_off = ([] for _ in range(8))
        used = 0
        for i in range(n):
            lo, hi = i * length, (i + 1) * length
            base = min(lo, block_end) // D // 16 * 16
            top = -(-min(hi, block_end) // D)
            a_rows = -(-(top - base) // 16) * 16 if lo < block_end else 0
            first = min(max(lo - block_end, 0), D * HEADS) // HEADS
            last = -(-min(max(hi - block_end, 0), D * HEADS) // HEADS)
            h_rows = last - first if hi > block_end and lo < head_end else 0
            v_first = max(lo - head_end, 0) // D
            v_rows = -(-(hi - head_end) // D) - v_first if hi > head_end else 0
            self.a_base.append(base)
            self.a_rows.append(a_rows)
            self.h_first.append(first)
            self.h_rows.append(h_rows)
            self.h_off.append(a_rows)
            self.v_first.append(v_first)
            self.v_rows.append(v_rows)
            self.v_off.append(a_rows + 5 * h_rows)
            used = max(used, a_rows + 5 * h_rows + v_rows)
        self.slot = -(-(used + 1) // 32) * 32

    def at(self, table, me):
        value = jnp.int32(table[0])
        for i in range(1, self.n):
            if table[i] != table[i - 1]:
                value = value + (me >= i).astype(jnp.int32) * (table[i] - table[i - 1])
        return value


MESH = pl.DeviceIdType.MESH


def neighbours(n):
    core = lax.axis_index("tower")
    me = lax.axis_index("dp")
    near_x = me + 1 - 2 * (me % 2)
    near_y = me + 2 - 4 * ((me // 2) % 2)
    return core, me, near_x, near_y


def at(core, index):
    return {"tower": core, "dp": index}


def greet(core, me, near_x, near_y, n):
    barrier = pltpu.get_barrier_semaphore()
    pl.semaphore_signal(barrier, inc=1, device_id=at(1 - core, me), device_id_type=MESH)
    for near in (near_x, near_y):
        pl.semaphore_signal(barrier, inc=1, device_id=at(core, near), device_id_type=MESH)
    for k in range(1, n // 4):
        pl.semaphore_signal(barrier, inc=1, device_id=at(core, (me + 4 * k) % n), device_id_type=MESH)
    return barrier


def place_shard(plan, me, p_ref, slot128, shifted, rolled):
    rows = plan.rows128
    start = me * plan.length
    shift = start % 128
    first = start // 128
    tall = shifted.shape[0]
    height = p_ref.shape[0]
    lane = lax.broadcasted_iota(jnp.int32, (height, 128), 1)
    rolled[0:8] = jnp.zeros((8, 128), F32)
    rolled[8 : 8 + height] = pltpu.roll(p_ref[...], shift, 1)
    shifted[...] = jnp.zeros((tall, 128), F32)
    moved = jnp.where(lane >= shift, rolled[8 : 8 + height], rolled[7 : 7 + height])
    shifted[16 : 16 + height] = moved
    slot128[...] = jnp.zeros(slot128.shape, F32)
    row = lax.broadcasted_iota(jnp.int32, (height, 128), 0)
    base = plan.at(plan.a_base, me)

    @pl.when(plan.at(plan.a_rows, me) > 0)
    def _():
        slot128[pl.ds(first - 2 * base, height)] = jnp.where(row + first < 2 * A_ROWS, moved, 0.0)

    h_first, h_rows, h_off = (plan.at(t, me) for t in (plan.h_first, plan.h_rows, plan.h_off))
    it = lax.broadcasted_iota(jnp.int32, (10, 128), 0)
    lane10 = lax.broadcasted_iota(jnp.int32, (10, 128), 1)

    @pl.loop(0, h_rows)
    def _(k):
        begin = A_ROWS * D + HEADS * (h_first + k) - 128 * first + 128 * 16
        turn = begin % 128
        window = pltpu.roll(shifted[pl.ds(begin // 128, 16)], (128 - turn) % 128, 1)
        value = jnp.where(lane10 < 128 - turn, window[0:10], window[1:11])
        slot128[pl.ds(2 * h_off + 10 * k, 10)] = jnp.where(it * 128 + lane10 < HEADS, value, 0.0)

    v_start = (A_ROWS * D + D * HEADS) // 128
    v_rows, v_off, v_first = (plan.at(t, me) for t in (plan.v_rows, plan.v_off, plan.v_first))
    tall_v = min(height, -(-2 * max(plan.v_rows) // 8) * 8)

    @pl.when(v_rows > 0)
    def _():
        inside = plan.at([max(0, v_start - i * plan.length // 128) for i in range(plan.n)], me)
        to = 2 * v_off + first + inside - v_start - 2 * v_first
        slot128[pl.ds(to, tall_v)] = shifted[pl.ds(16 + inside, tall_v)]


def unpack_rows(plan, i, slot, w, heads, vectors, scratch):
    base, rows = plan.a_base[i], plan.a_rows[i]
    if rows:
        shared = i > 0 and base < plan.a_base[i - 1] + plan.a_rows[i - 1]
        lo = 0
        if shared:
            w[base : base + 16] = w[base : base + 16] + slot[0:16]
            lo = 16
        if rows > lo:
            w[base + lo : base + rows] = slot[lo:rows]
    h_rows, h_off, h_first = plan.h_rows[i], plan.h_off[i], plan.h_first[i]
    v_rows, v_off, v_first = plan.v_rows[i], plan.v_off[i], plan.v_first[i]
    if h_rows or v_rows:
        value = slot.astype(F32)
        scratch[0] = value[:, 0:128]
        scratch[1] = value[:, 128:D]
    if h_rows:
        shared = i > 0 and plan.h_rows[i - 1] and plan.h_first[i - 1] + plan.h_rows[i - 1] > h_first
        for j in range(5):
            for half in range(2):
                cols = slice(128 * half, 128 * half + 128)
                first = D * j + h_first
                value = scratch[half, pl.ds(h_off + j, h_rows, stride=5)]
                if shared:
                    heads[first : first + 1, cols] = heads[first : first + 1, cols] + value[0:1]
                    if h_rows > 1:
                        heads[first + 1 : first + h_rows, cols] = value[1:h_rows]
                else:
                    heads[first : first + h_rows, cols] = value
    if v_rows:
        shared = v_first and plan.v_first[i - 1] + plan.v_rows[i - 1] > v_first
        shared = shared or (i > 0 and plan.v_rows[i - 1] > 0 and v_first == 0)
        for half in range(2):
            cols = slice(128 * half, 128 * half + 128)
            value = scratch[half, v_off : v_off + v_rows]
            if shared:
                vectors[v_first : v_first + 1, cols] = vectors[v_first : v_first + 1, cols] + value[0:1]
                if v_rows > 1:
                    vectors[v_first + 1 : v_first + v_rows, cols] = value[1:v_rows]
            else:
                vectors[v_first : v_first + v_rows, cols] = value


def split3(value):
    hi = value.astype(BF).astype(F32)
    mid = (value - hi).astype(BF).astype(F32)
    return hi, mid, value - hi - mid


def gather_kernel(plan, p_ref, ints_ref, imp_ref, w, wh, vec, both, rw, slots, slot128, shifted, rolled, scratch, whf, vecf, send, recv):
    n = plan.n
    depth = n // 4
    core, me, near_x, near_y = neighbours(n)
    barrier = greet(core, me, near_x, near_y, n)
    place_shard(plan, me, p_ref, slot128, shifted, rolled)
    pl.semaphore_wait(barrier, depth + 2)
    half = rw.shape[1]
    started = []

    def copy(src, dst, slot, to):
        c = pltpu.make_async_remote_copy(
            src_ref=src, dst_ref=dst, send_sem=send.at[slot], recv_sem=recv.at[slot], device_id=to, device_id_type=MESH
        )
        c.start()
        started.append(c)
        return c

    mine = pl.multiple_of(core * half, half)
    theirs = pl.multiple_of((1 - core) * half, half)
    number = iter(range(1 << 20))
    ints_copy = copy(ints_ref.at[:, pl.ds(theirs, half)], both.at[core], next(number), at(1 - core, me))
    rows = plan.slot
    total = jnp.sum(imp_ref[...].astype(F32), axis=1, keepdims=True)
    lane = lax.broadcasted_iota(jnp.int32, (1, D), 1)
    hi, mid, lo = split3(total)
    left = slot128[pl.ds(0, rows, stride=2)]
    right = slot128[pl.ds(1, rows, stride=2)]
    own = jnp.concatenate([left, right], 1)
    last = jnp.where(lane == 0, hi, jnp.where(lane == 1, mid, jnp.where(lane == 2, lo, 0.0)))
    last_row = lax.broadcasted_iota(jnp.int32, (rows, D), 0) == rows - 1
    slots[core, me] = jnp.where(last_row, last, own).astype(BF)

    def column(index, k):
        return (index + n - 4 * k) % n

    def send_slot(origin, to, lo=0, hi=rows):
        ref = slots.at[core, origin, pl.ds(lo, hi - lo)]
        return copy(ref, ref, next(number), to)

    near_xy = near_x + near_y - me
    cut = rows // 2
    z_in, x_in, y_in, d_in, s_in = {}, {}, {}, {}, []
    for k in sorted(range(1, depth), key=lambda k: (min(k, depth - k), k)):
        z_in[k] = send_slot(me, at(core, (me + 4 * k) % n))
    order = [0] + list(z_in)
    for k in order:
        if k:
            z_in[k].wait_recv()
        x_in[k] = send_slot(column(me, k), at(core, near_x))
        y_in[k] = send_slot(column(me, k), at(core, near_y))
        s_in.append(send_slot(column(me, k), at(1 - core, me)))
    for k in order:
        x_in[k].wait_recv()
        first = send_slot(column(near_x, k), at(core, near_y), 0, cut)
        s_in.append(send_slot(column(near_x, k), at(1 - core, me)))
        y_in[k].wait_recv()
        second = send_slot(column(near_y, k), at(core, near_x), cut, rows)
        s_in.append(send_slot(column(near_y, k), at(1 - core, me)))
        d_in[k] = (first, second)
    for k in order:
        for c in d_in[k]:
            c.wait_recv()
        s_in.append(send_slot(column(near_xy, k), at(1 - core, me)))
    ints_copy.wait_recv()
    both[core] = ints_ref[:, pl.ds(mine, half)]
    for c in s_in:
        c.wait_recv()
    for c in started:
        c.wait_send()
    for t in range(2):
        vecf[...] = jnp.zeros(vecf.shape, F32)
        for i in range(n):
            unpack_rows(plan, i, slots[t, i], w.at[t], whf, vecf, scratch)
        for j in range(5):
            wh[t, :, D * j : D * j + D] = whf[D * j : D * j + D].astype(BF)
        vec[t] = vecf[...].astype(BF)
    total = jnp.zeros((1, D), F32)
    for i in range(n):
        tail = slots[0, i, rows - 16 : rows].astype(F32)
        total = total + tail[15:16]
    weight_sum = jnp.sum(jnp.where(lane < 3, total, 0.0), axis=1, keepdims=True)
    rw[...] = jnp.broadcast_to(imp_ref[:, pl.ds(mine, half)].astype(F32) / weight_sum, (8, half))


def gather(plan, p128, ints, imp):
    n, rows = plan.n, plan.slot
    half = ints.shape[1] // 2
    vm = pl.BlockSpec(memory_space=pltpu.VMEM)
    height = p128.shape[0]
    tall = max(2 * rows, height + 40) + 80
    copies = 1 + (n // 4 - 1) + 2 * (n // 4) + 2 * (n // 4) + n
    return pl.pallas_call(
        functools.partial(gather_kernel, plan),
        out_shape=(
            jax.ShapeDtypeStruct((2, A_ROWS, D), BF),
            jax.ShapeDtypeStruct((2, D, HPAD), BF),
            jax.ShapeDtypeStruct((2, 128, D), BF),
            jax.ShapeDtypeStruct((2, 8, half), jnp.int32),
            jax.ShapeDtypeStruct((8, half), F32),
        ),
        in_specs=[vm] * 3,
        out_specs=(vm,) * 5,
        scratch_shapes=[
            pltpu.VMEM((2, n, rows, D), BF),
            pltpu.VMEM((tall, 128), F32),
            pltpu.VMEM((height + 128, 128), F32),
            pltpu.VMEM((height + 8, 128), F32),
            pltpu.VMEM((2, rows, 128), F32),
            pltpu.VMEM((HPAD, D), F32),
            pltpu.VMEM((128, D), F32),
            pltpu.SemaphoreType.DMA((copies,)),
            pltpu.SemaphoreType.DMA((copies,)),
        ],
        compiler_params=pltpu.CompilerParams(
            collective_id=0, has_side_effects=True, vmem_limit_bytes=48 * 1024 * 1024
        ),
    )(p128, ints, imp)


def chunks(height):
    step = max(c for c in range(8, 113, 8) if height % c == 0)
    return [(lo, lo + step) for lo in range(0, height, step)]


def lay_flat(plan, me, slot128, flat, rolled):
    height = rolled.shape[0] - 16
    start = me * plan.length
    shift = start % 128
    first = start // 128
    base = plan.at(plan.a_base, me)
    row = lax.broadcasted_iota(jnp.int32, (height + 8, 128), 0)
    flat[...] = jnp.zeros(flat.shape, F32)

    @pl.when(plan.at(plan.a_rows, me) > 0)
    def _():
        rows = slot128[pl.ds(first - 2 * base, height + 8)]
        flat[16 : 24 + height] = jnp.where(row + first < 2 * A_ROWS, rows, 0.0)

    h_first, h_rows, h_off = (plan.at(t, me) for t in (plan.h_first, plan.h_rows, plan.h_off))
    it = lax.broadcasted_iota(jnp.int32, (16, 128), 0)
    lane = lax.broadcasted_iota(jnp.int32, (16, 128), 1)

    @pl.loop(0, h_rows)
    def _(k):
        begin = A_ROWS * D + HEADS * (h_first + k) - 128 * first + 128 * 16
        turn = begin % 128
        value = slot128[pl.ds(2 * h_off + 10 * k, 16)]
        value = jnp.where(it * 128 + lane < HEADS, value, 0.0)
        value = pltpu.roll(value, turn, 1)
        above = jnp.concatenate([jnp.zeros((8, 128), F32), value], 0)[7:23]
        to = pl.ds(begin // 128, 16)
        flat[to] = flat[to] + jnp.where(lane >= turn, value, above)

    v_start = (A_ROWS * D + D * HEADS) // 128
    v_rows, v_off, v_first = (plan.at(t, me) for t in (plan.v_rows, plan.v_off, plan.v_first))
    tall_v = min(height, -(-2 * max(plan.v_rows) // 8) * 8)

    @pl.when(v_rows > 0)
    def _():
        inside = plan.at([max(0, v_start - i * plan.length // 128) for i in range(plan.n)], me)
        source = 2 * v_off + first + inside - v_start - 2 * v_first
        to = pl.ds(16 + inside, tall_v)
        flat[to] = flat[to] + slot128[pl.ds(source, tall_v)]

    rolled[0 : height + 8] = pltpu.roll(flat[16 : 24 + height], (128 - shift) % 128, 1)
    for lo, hi in chunks(height):
        lane = lax.broadcasted_iota(jnp.int32, (hi - lo, 128), 1)
        flat[lo:hi] = jnp.where(lane < 128 - shift, rolled[lo:hi], rolled[lo + 1 : hi + 1])


def pack_slots(plan, core, gw, gh, gv, rgw, rgh, rgv, slots, sums, vsum, scratch):
    total = gv[core].astype(F32) + rgv[...]
    for kind in range(3):
        vsum[kind * (BLOCKS + 1) : (kind + 1) * (BLOCKS + 1)] = total[kind, 0 : BLOCKS + 1]
    sums[...] = gh[core].astype(F32) + rgh[...].astype(F32)
    for i in range(plan.n):
        base, rows = plan.a_base[i], plan.a_rows[i]
        h_rows, h_off, h_first = plan.h_rows[i], plan.h_off[i], plan.h_first[i]
        v_rows, v_off, v_first = plan.v_rows[i], plan.v_off[i], plan.v_first[i]
        slots[i, rows : plan.slot] = jnp.zeros((plan.slot - rows, D), BF)
        if rows:
            added = gw[core, base : base + rows].astype(F32) + rgw[base : base + rows].astype(F32)
            slots[i, 0:rows] = added.astype(BF)
        if h_rows or v_rows:
            scratch[...] = jnp.zeros(scratch.shape, F32)
            for half in range(2):
                for j in range(5 if h_rows else 0):
                    cols = slice(D * j + 128 * half, D * j + 128 * half + 128)
                    scratch[half, pl.ds(h_off + j, h_rows, stride=5)] = sums[h_first : h_first + h_rows, cols]
                if v_rows:
                    scratch[half, v_off : v_off + v_rows] = vsum[v_first : v_first + v_rows, 128 * half : 128 * half + 128]
            whole = jnp.concatenate([scratch[0], scratch[1]], 1)
            slots[i, rows : plan.slot] = whole[rows:].astype(BF)


def segment_bounds():
    first = [0] + [(CAT + j * D) * D for j in range(BLOCKS + 1)]
    return list(zip(first, first[1:] + [A_ROWS * D + D * HEADS]))


def update_shard(plan, me, p_ref, m_ref, v_ref, outs, flat, squares, sq_z, sq_y, sq_x, push, to_z, to_y, to_x):
    first_out, second_out, new_out, low_out, norm_out = outs
    height = p_ref.shape[0]
    start = me * plan.length
    correction = 1.0 - 0.5**STEP
    bounds = segment_bounds()

    def place(lo, hi):
        shape = (hi - lo, 128)
        return 128 * lo + 128 * lax.broadcasted_iota(jnp.int32, shape, 0) + lax.broadcasted_iota(jnp.int32, shape, 1)

    for lo, hi in chunks(height):
        spot = place(lo, hi)
        grad = jnp.where(spot < plan.length, flat[lo:hi], 0.0)
        first_new = 0.5 * m_ref[lo:hi] + 0.5 * grad
        second_new = 0.5 * v_ref[lo:hi] + 0.5 * grad * grad
        first_out[lo:hi] = first_new
        second_out[lo:hi] = second_new
        decay = jnp.where(spot < bounds[-1][1] - start, 0.01 * p_ref[lo:hi], 0.0)
        update = first_new / correction / (jnp.sqrt(second_new / correction) + 1e-06) + decay
        flat[lo:hi] = jnp.where(spot < plan.length, update, 0.0)
        new_out[lo:hi] = p_ref[lo:hi] - 0.5 * update
    squares[...] = jnp.zeros(squares.shape, F32)

    def each_segment(body):
        for j, (first, last) in enumerate(bounds):
            pl.when((first < start + plan.length) & (last > start))(lambda j=j, first=first, last=last: body(j, first, last))

    def square_sums(j, first, last):
        weight, change = jnp.zeros((8, 128), F32), jnp.zeros((8, 128), F32)
        for lo, hi in chunks(height):
            spot = place(lo, hi)
            inside = (spot >= first - start) & (spot < last - start)
            p, u = jnp.where(inside, p_ref[lo:hi], 0.0), jnp.where(inside, flat[lo:hi], 0.0)
            weight = weight + jnp.sum((p * p).reshape(-1, 8, 128), axis=0)
            change = change + jnp.sum((u * u).reshape(-1, 8, 128), axis=0)
        squares[0, j : j + 1] = jnp.sum(weight, axis=0, keepdims=True)
        squares[0, 16 + j : 17 + j] = jnp.sum(change, axis=0, keepdims=True)

    each_segment(square_sums)
    for c in [push(squares.at[0], sq_z.at[k], to) for k, to in enumerate(to_z, 1)]:
        c.wait_recv()
    total = squares[0]
    for k in range(1, len(to_z) + 1):
        total = total + sq_z[k]
    squares[1] = total
    push(squares.at[1], sq_y, to_y).wait_recv()
    squares[2] = squares[1] + sq_y[...]
    push(squares.at[2], sq_x, to_x).wait_recv()
    norm = jnp.sqrt(jnp.sum(squares[2] + sq_x[...], axis=1, keepdims=True))
    norm_out[...] = jnp.broadcast_to(norm, (32, 128))

    def scaled(j, first, last):
        ratio = norm_out[j : j + 1] / norm_out[16 + j : 17 + j]
        for lo, hi in chunks(height):
            spot = place(lo, hi)
            inside = (spot >= first - start) & (spot < last - start)
            new_out[lo:hi] = jnp.where(inside, p_ref[lo:hi] - 0.5 * ratio * flat[lo:hi], new_out[lo:hi])

    each_segment(scaled)
    for lo, hi in chunks(height):
        low_out[lo:hi] = new_out[lo:hi].astype(BF)


def reduce_kernel(
    plan, gw, gh, gv, st, ig, p_ref, m_ref, v_ref,
    st_out, ig_out, first_out, second_out, new_out, low_out, norm_out,
    rgw, rgh, rgv, slots, sums, vsum, scratch, in_d, in_x, in_y, in_z, slot128, flat, rolled, squares, sq_z, sq_y, sq_x,
    send, recv, local,
):
    n, rows = plan.n, plan.slot
    depth, cut = n // 4, plan.slot // 2
    core, me, near_x, near_y = neighbours(n)
    near_xy = near_x + near_y - me
    barrier = greet(core, me, near_x, near_y, n)
    pl.semaphore_wait(barrier, depth + 2)
    half = st.shape[1]
    number = iter(range(1 << 20))
    started = []

    def copy(src, dst, to):
        slot = next(number)
        c = pltpu.make_async_remote_copy(
            src_ref=src, dst_ref=dst, send_sem=send.at[slot], recv_sem=recv.at[slot], device_id=to, device_id_type=MESH
        )
        c.start()
        started.append(c)
        return c

    def column(index, k):
        return (index + n - 4 * k) % n

    sibling = at(1 - core, me)
    early = [
        copy(gw.at[1 - core], rgw, sibling),
        copy(gh.at[1 - core], rgh, sibling),
        copy(gv.at[1 - core], rgv, sibling),
    ]
    mine = pl.ds(pl.multiple_of(core * half, half), half)
    late = [
        copy(st.at[1 - core], st_out.at[mine], sibling),
        copy(ig.at[1 - core], ig_out.at[mine], sibling),
    ]
    stay = [
        pltpu.make_async_copy(st.at[core], st_out.at[mine], local.at[0]),
        pltpu.make_async_copy(ig.at[core], ig_out.at[mine], local.at[1]),
    ]
    for c in stay:
        c.start()
    for c in early:
        c.wait_recv()
    pack_slots(plan, core, gw, gh, gv, rgw, rgh, rgv, slots, sums, vsum, scratch)
    order = list(range(1, depth)) + [0]
    to_x, to_y = at(core, near_x), at(core, near_y)
    halves = {}
    for k in order:
        diagonal = column(near_xy, k)
        halves[k] = (
            copy(slots.at[diagonal, pl.ds(0, cut)], in_d.at[k, pl.ds(0, cut)], to_y),
            copy(slots.at[diagonal, pl.ds(cut, rows - cut)], in_d.at[k, pl.ds(cut, rows - cut)], to_x),
        )
    fulls = {}
    for k in order:
        ox, oy = column(near_x, k), column(near_y, k)
        halves[k][0].wait_recv()
        slots[ox, 0:cut] = (slots[ox, 0:cut].astype(F32) + in_d[k, 0:cut].astype(F32)).astype(BF)
        first = copy(slots.at[ox], in_x.at[k], to_x)
        halves[k][1].wait_recv()
        slots[oy, cut:rows] = (slots[oy, cut:rows].astype(F32) + in_d[k, cut:rows].astype(F32)).astype(BF)
        fulls[k] = (first, copy(slots.at[oy], in_y.at[k], to_y))
    along = {}
    for k in order:
        own = column(me, k)
        for c in fulls[k]:
            c.wait_recv()
        if k:
            total = slots[own].astype(F32) + in_x[k].astype(F32) + in_y[k].astype(F32)
            slots[own] = total.astype(BF)
            along[k] = copy(slots.at[own], in_z.at[k], at(core, own))
    for c in along.values():
        c.wait_recv()
    total = slots[me].astype(F32) + in_x[0].astype(F32) + in_y[0].astype(F32)
    for k in along:
        total = total + in_z[k].astype(F32)
    slot128[...] = jnp.zeros(slot128.shape, F32)
    slot128[pl.ds(0, rows, stride=2)] = total[:, 0:128]
    slot128[pl.ds(1, rows, stride=2)] = total[:, 128:D]
    lay_flat(plan, me, slot128, flat, rolled)

    to_z = [at(core, column(me, k)) for k in range(1, depth)]
    outs = (first_out, second_out, new_out, low_out, norm_out)
    update_shard(plan, me, p_ref, m_ref, v_ref, outs, flat, squares, sq_z, sq_y, sq_x, copy, to_z, to_y, to_x)
    for c in late:
        c.wait_recv()
    for c in stay:
        c.wait()
    for c in started:
        c.wait_send()


def reduce_and_update(plan, gw, gh, gv, st, ig, p128, m128, v128):
    n, rows = plan.n, plan.slot
    depth = n // 4
    half = st.shape[1]
    height = p128.shape[0]
    vm = pl.BlockSpec(memory_space=pltpu.VMEM)
    hbm = pl.BlockSpec(memory_space=pl.ANY)
    copies = 5 + 2 * depth + 2 * depth + (depth - 1) + (depth - 1) + 2
    flat32 = jax.ShapeDtypeStruct((height, 128), F32)
    return pl.pallas_call(
        functools.partial(reduce_kernel, plan),
        out_shape=(
            jax.ShapeDtypeStruct((2 * half, D), BF),
            jax.ShapeDtypeStruct((2 * half, D), F32),
            flat32,
            flat32,
            flat32,
            jax.ShapeDtypeStruct((height, 128), BF),
            jax.ShapeDtypeStruct((32, 128), F32),
        ),
        in_specs=[vm] * 3 + [hbm] * 2 + [vm] * 3,
        out_specs=(hbm, hbm, vm, vm, vm, vm, vm),
        scratch_shapes=[
            pltpu.VMEM((A_ROWS, D), BF),
            pltpu.VMEM((D, HPAD), BF),
            pltpu.VMEM(gv.shape[1:], F32),
            pltpu.VMEM((n, rows, D), BF),
            pltpu.VMEM((D, HPAD), F32),
            pltpu.VMEM((40, D), F32),
            pltpu.VMEM((2, rows, 128), F32),
            pltpu.VMEM((depth, rows, D), BF),
            pltpu.VMEM((depth, rows, D), BF),
            pltpu.VMEM((depth, rows, D), BF),
            pltpu.VMEM((depth, rows, D), BF),
            pltpu.VMEM((max(2 * rows, height + 48) + 80, 128), F32),
            pltpu.VMEM((height + 128, 128), F32),
            pltpu.VMEM((height + 16, 128), F32),
            pltpu.VMEM((3, 32, 128), F32),
            pltpu.VMEM((depth, 32, 128), F32),
            pltpu.VMEM((32, 128), F32),
            pltpu.VMEM((32, 128), F32),
            pltpu.SemaphoreType.DMA((copies,)),
            pltpu.SemaphoreType.DMA((copies,)),
            pltpu.SemaphoreType.DMA((2,)),
        ],
        compiler_params=pltpu.CompilerParams(
            collective_id=1, has_side_effects=True, vmem_limit_bytes=48 * 1024 * 1024
        ),
    )(gw, gh, gv, st, ig, p128, m128, v128)


class Copies:
    def __init__(self, send, recv):
        self.send, self.recv, self.made, self.sent = send, recv, [], set()

    def add(self, src, dst, to, recv_slot=None, only=None):
        self.made.append((src, dst, to, recv_slot, only))
        return len(self.made) - 1

    def get(self, number):
        src, dst, to, recv_slot, _ = self.made[number]
        return pltpu.make_async_remote_copy(
            src_ref=src(), dst_ref=dst(), send_sem=self.send.at[number],
            recv_sem=self.recv.at[number] if recv_slot is None else recv_slot(),
            device_id=to(), device_id_type=MESH,
        )

    def start(self, *numbers):
        for number in numbers:
            self.get(number).start()

    def arrive(self, *numbers):
        for number in numbers:
            self.get(number).wait_recv()

    def leave(self, *numbers):
        for number in numbers:
            only = self.made[number][4]
            if number not in self.sent and only is None:
                self.get(number).wait_send()
            elif number not in self.sent:
                pl.when(only())(lambda number=number: self.get(number).wait_send())
            self.sent.add(number)


def fused_fits(plan):
    depth = plan.n // 4
    blocks = 11 * depth + depth - 1
    half = plan.slot // 2
    plain = [b + plan.slot <= A_ROWS for b, h, v in zip(plan.a_base, plan.h_rows, plan.v_rows) if not (h or v)]
    vectors = [rows for rows in plan.v_rows if rows]
    return (
        all(plain)
        and vectors == [3 * (BLOCKS + 1)]
        and plan.n % 4 == 0
        and half >= 32
        and 2 * depth * plan.slot <= (BLOCKS + 1) * D
        and -(-blocks // 4) * half <= BLOCKS * (D + 16)
        and max(plan.a_rows) <= plan.slot
    )


def train_kernel(
    plan, x_ref, ints_ref, imp_ref, p_ref, m_ref, v_ref,
    st_out, ig_out, first_out, second_out, new_out, low_out, norm_out,
    w, wh, vec, both, rw, eye, wct, wt, wht, vt, gsb, xt, mix, xh, gp, rstd, stream, ex, br, dm, acc, lg, dl,
    gw, gh, gv, packed, st_stage, slot128, flat, rolled, scratch, vsum, vacc, vin, partial, final, squares, sq_z, sq_y, sq_x,
    send, recv, z_recv, local, ready,
):
    n, rows = plan.n, plan.slot
    depth, hrows = n // 4, plan.slot // 2
    cut = hrows // 32 * 16
    core, me, near_x, near_y = neighbours(n)
    near_xy = near_x + near_y - me
    width = both.shape[2]
    z_me, j_me = me // 4, me % 4
    copies = Copies(send, recv)
    barrier = greet(core, me, near_x, near_y, n)
    mine = pl.multiple_of(core * width, width)
    theirs = pl.multiple_of((1 - core) * width, width)
    x_copy = pltpu.make_async_copy(x_ref.at[pl.ds(mine, width)], st_stage.at[0], local.at[0])
    x_copy.start()
    place_shard(plan, me, p_ref, slot128, flat, rolled)

    spare = (BLOCKS + 1) * D

    def slot_part(t, i, lo, count):
        row = pl.multiple_of(spare + rows * (t * depth + i // 4) + lo, 16)
        return xh.at[pl.ds(row, count), pl.ds(pl.multiple_of((i % 4) * D, D), D)]

    def column(index, k):
        return (index + n - 4 * k) % n

    def sibling():
        return at(1 - core, me)

    def same(make, to):
        return copies.add(make, make, to)

    low = core * hrows
    other_low = (1 - core) * hrows
    swap_first = same(lambda: slot_part(core, me, other_low, hrows), sibling)
    swap_second = same(lambda: slot_part(core, me, low, hrows), sibling)
    swap_ints = copies.add(lambda: ints_ref.at[:, pl.ds(theirs, width)], lambda: both.at[core], sibling)
    order = [0] + sorted(range(1, depth), key=lambda k: (min(k, depth - k), k))
    to_x, to_y = (lambda: at(core, near_x)), (lambda: at(core, near_y))
    gathers = []
    for t in range(2):
        g = {"z": {}, "x": {}, "y": {}, "d": {}, "s": []}
        for k in order:
            if k:
                g["z"][k] = same(lambda t=t: slot_part(t, me, low, hrows), lambda k=k: at(core, (me + 4 * k) % n))
            g["x"][k] = same(lambda t=t, k=k: slot_part(t, column(me, k), low, hrows), to_x)
            g["y"][k] = same(lambda t=t, k=k: slot_part(t, column(me, k), low, hrows), to_y)
            g["d"][k] = (
                same(lambda t=t, k=k: slot_part(t, column(near_x, k), low, cut), to_y),
                same(lambda t=t, k=k: slot_part(t, column(near_y, k), low + cut, hrows - cut), to_x),
            )
            g["s", k] = [
                same(lambda t=t, k=k, index=index: slot_part(t, column(index, k), low, hrows), sibling) if index is not me or k else None
                for index in (me, near_x, near_y, near_xy)
            ]
        gathers.append(g)

    def gather_0(t):
        g = gathers[t]
        copies.start(*g["z"].values())
        copies.start(g["x"][0], g["y"][0])

    def gather_1(t):
        g = gathers[t]
        for k in order[1:]:
            copies.arrive(g["z"][k])
            copies.start(g["x"][k], g["y"][k], g["s", k][0])

    def gather_2(t):
        g = gathers[t]
        for k in order:
            copies.arrive(g["x"][k])
            copies.start(g["d"][k][0], g["s", k][1])
            copies.arrive(g["y"][k])
            copies.start(g["d"][k][1], g["s", k][2])

    def gather_3(t):
        g = gathers[t]
        for k in order:
            copies.arrive(*g["d"][k])
            copies.start(g["s", k][3])

    def gather_4(t):
        g = gathers[t]
        for k in order:
            copies.arrive(*(c for c in g["s", k] if c is not None))

    def unpack(t):
        lg[4 * D : 5 * D, 128:D] = jnp.zeros((D, 128), F32)
        vsum[...] = jnp.zeros(vsum.shape, F32)
        for i in range(n):
            row, lane = spare + rows * (t * depth + i // 4), (i % 4) * D
            unpack_rows(plan, i, xh[row : row + rows, lane : lane + D], w.at[t], lg, vsum, scratch)
        for j in range(5):
            wh[t, :, D * j : D * j + D] = lg[D * j : D * j + D].astype(BF)
        vec[t] = vsum[...].astype(BF)

    total = jnp.sum(imp_ref[...].astype(F32), axis=1, keepdims=True)
    lane_d = lax.broadcasted_iota(jnp.int32, (1, D), 1)
    hi, mid, lo = split3(total)
    left = slot128[pl.ds(0, rows, stride=2)]
    right = slot128[pl.ds(1, rows, stride=2)]
    own = jnp.concatenate([left, right], 1)
    last = jnp.where(lane_d == 0, hi, jnp.where(lane_d == 1, mid, jnp.where(lane_d == 2, lo, 0.0)))
    last_row = lax.broadcasted_iota(jnp.int32, (rows, D), 0) == rows - 1
    slot_part(core, me, 0, rows)[...] = jnp.where(last_row, last, own).astype(BF)
    pl.semaphore_wait(barrier, depth + 2)
    copies.start(swap_first, swap_second, swap_ints)
    eye[...] = identity(D)
    x_copy.wait()
    for c in range(0, width, CB):
        xt[0, 0:D, c : c + CB] = nt(eye[...], st_stage[0, c : c + CB, :]).astype(BF)
    both[core] = ints_ref[:, pl.ds(mine, width)]
    copies.arrive(swap_first)
    gather_0(0)
    gather_1(0)
    gather_2(0)
    gather_3(0)
    gather_0(1)
    copies.arrive(swap_second, swap_ints)
    gather_4(0)
    unpack(0)
    total = jnp.zeros((1, D), F32)
    for i in range(n):
        row, lane = spare + rows * (i // 4), (i % 4) * D
        total = total + xh[row + rows - 16 : row + rows, lane : lane + D].astype(F32)[15:16]
    weight_sum = jnp.sum(jnp.where(lane_d < 3, total, 0.0), axis=1, keepdims=True)
    rw[...] = jnp.broadcast_to(imp_ref[:, pl.ds(mine, width)].astype(F32) / weight_sum, (8, width))

    fwd = (eye, w, wh, vec, wct, wt, vt, gsb, xt, mix, xh, gp, rstd, stream, both, width)

    def during_forward(k):
        pl.when(k == 2)(lambda: gather_1(1))
        pl.when(k == 5)(lambda: gather_2(1))
        pl.when(k == 8)(lambda: gather_3(1))

    def emit_states(t):
        for c in range(0, width, CB):
            st_stage[t, c : c + CB, :] = nt(eye[...], xt[t + 1, 0:D, c : c + CB]).astype(BF)

    forward_tower(0, fwd, during_forward)
    gather_4(1)
    copies.leave(*range(len(copies.made)))
    unpack(1)
    forward_tower(1, fwd, None)
    emit_states(0)
    emit_states(1)
    out_rows = pl.ds(mine, width)
    st_copy = copies.add(lambda: st_stage.at[1 - core], lambda: st_out.at[out_rows], sibling)
    copies.start(st_copy)
    st_stay = pltpu.make_async_copy(st_stage.at[core], st_out.at[out_rows], local.at[1])
    st_stay.start()

    packed_of = [i for i in range(n) if plan.h_rows[i] or plan.v_rows[i]]
    owner = plan.v_rows.index(3 * (BLOCKS + 1))

    def block(t, q):
        arena, first = (xh, spare) if t == 0 else (mix, BLOCKS * (D + 16))
        row = pl.multiple_of(first + hrows * (q // 4), 16)
        return arena.at[pl.ds(row, hrows), pl.ds(pl.multiple_of((q % 4) * D, D), D)]

    def piece(t, q, lo, count):
        arena, first = (xh, spare) if t == 0 else (mix, BLOCKS * (D + 16))
        row = pl.multiple_of(first + hrows * (q // 4) + lo, 16)
        return arena.at[pl.ds(row, count), pl.ds(pl.multiple_of((q % 4) * D, D), D)]

    def slot_half(t, i, lo):
        if i in packed_of:
            return packed.at[t, packed_of.index(i), pl.ds(pl.multiple_of(lo, 16), hrows)]
        return gw.at[t, pl.ds(pl.multiple_of(plan.a_base[i] + lo, 16), hrows)]

    j_x, j_y, j_d = near_x % 4, near_y % 4, near_xy % 4
    jobs = {}
    for t in range(2):
        for zz in range(depth):
            q = 11 * zz
            job = {"q": q}
            job["swap"] = [
                copies.add(lambda t=t, i=4 * zz + j: slot_half(t, i, other_low), lambda t=t, q=q + j: block(t, q), sibling)
                for j in range(4)
            ]
            job["d"] = (
                copies.add(lambda t=t, q=q: piece(t, q + 4 + j_d, 0, cut), lambda t=t, q=q: piece(t, q + 8, 0, cut), to_y),
                copies.add(lambda t=t, q=q: piece(t, q + 4 + j_d, cut, hrows - cut), lambda t=t, q=q: piece(t, q + 8, cut, hrows - cut), to_x),
            )
            job["x"] = copies.add(lambda t=t, q=q: block(t, q + 4 + j_x), lambda t=t, q=q: block(t, q + 9), to_x)
            job["y"] = copies.add(lambda t=t, q=q: block(t, q + 4 + j_y), lambda t=t, q=q: block(t, q + 10), to_y)
            job["z"] = copies.add(
                lambda t=t, q=q: block(t, q + 4 + j_me),
                lambda t=t, zz=zz: block(t, 11 * depth + (zz + depth - z_me) % depth - 1),
                lambda zz=zz: at(core, 4 * zz + j_me),
                lambda t=t, zz=zz: z_recv.at[t * depth + (zz + depth - z_me) % depth],
                lambda zz=zz: z_me != zz,
            )
            jobs[t, zz] = job

    def pack(t, planes):
        wanted = [i for i in packed_of if i // 4 in planes]
        for i in wanted:
            a_rows, h_rows, h_off, h_first = plan.a_rows[i], plan.h_rows[i], plan.h_off[i], plan.h_first[i]
            to = packed.at[t, packed_of.index(i)]
            scratch[...] = jnp.zeros(scratch.shape, F32)
            lo16, hi16 = h_first // 16 * 16, -(-(h_first + h_rows) // 16) * 16
            for half in range(2):
                for j in range(5 if h_rows else 0):
                    cols = slice(D * j + 128 * half, D * j + 128 * half + 128)
                    value = gh[t, lo16:hi16, cols].astype(F32)[h_first - lo16 : h_first - lo16 + h_rows]
                    scratch[half, pl.ds(h_off + j, h_rows, stride=5)] = value
            whole = jnp.concatenate([scratch[0], scratch[1]], 1)
            to[a_rows:rows] = whole[a_rows:].astype(BF)
            if a_rows:
                to[0:a_rows] = gw[t, plan.a_base[i] : plan.a_base[i] + a_rows]

    def plus(*refs):
        value = refs[0][...].astype(F32)
        for ref in refs[1:]:
            value = value + ref[...].astype(F32)
        return value

    def sum_0(t, zz):
        copies.start(*jobs[t, zz]["swap"])

    def sum_1(t, zz):
        job = jobs[t, zz]
        for j in range(4):
            copies.arrive(job["swap"][j])
            block(t, job["q"] + 4 + j)[...] = plus(slot_half(t, 4 * zz + j, low), block(t, job["q"] + j)).astype(BF)
        copies.start(*job["d"])

    def sum_2(t, zz):
        job = jobs[t, zz]
        q = job["q"]
        copies.arrive(job["d"][0])
        target = piece(t, q + 4 + j_x, 0, cut)
        target[...] = plus(target, piece(t, q + 8, 0, cut)).astype(BF)
        copies.start(job["x"])
        copies.arrive(job["d"][1])
        target = piece(t, q + 4 + j_y, cut, hrows - cut)
        target[...] = plus(target, piece(t, q + 8, cut, hrows - cut)).astype(BF)
        copies.start(job["y"])

    def sum_3(t, zz):
        job = jobs[t, zz]
        q = job["q"]
        copies.arrive(job["x"], job["y"])
        value = plus(block(t, q + 4 + j_me), block(t, q + 9), block(t, q + 10))

        @pl.when(z_me == zz)
        def _():
            partial[t] = value

        @pl.when(z_me != zz)
        def _():
            block(t, q + 4 + j_me)[...] = value.astype(BF)
            copies.start(job["z"])

    def sum_4(t):
        for k in range(1, depth):
            src = block(t, 11 * depth + k - 1)
            pltpu.make_async_remote_copy(
                src_ref=src, dst_ref=src, send_sem=send.at[0], recv_sem=z_recv.at[t * depth + k], device_id=sibling(), device_id_type=MESH
            ).wait_recv()
            partial[t] = partial[t] + src[...].astype(F32)

    def vector_step(step):
        sources = [gv.at[1 - core], vacc.at[0], vacc.at[1], vacc.at[2]]
        targets = [[sibling], [to_x], [to_y], [lambda k=k: at(core, (me + 4 * k) % n) for k in range(1, depth)]]
        if step:
            base = gv[core] if step == 1 else vacc[step - 2]
            for number, k in vector_copies[-1]:
                copies.arrive(number)
                base = base + vin[k]
            vacc[step - 1] = base
        if step < 4:
            slots = range(step, step + 1) if step < 3 else range(3, 2 + depth)
            started = []
            for k, to in zip(slots, targets[step]):
                number = copies.add(lambda step=step: sources[step], lambda k=k: vin.at[k], to)
                copies.start(number)
                started.append((number, k))
            vector_copies.append(started)

    vector_copies = []
    last_swap = copies.add(lambda: partial.at[1 - core], lambda: final.at[core], sibling)
    peers = [(1 - core, me), (core, near_x), (core, near_y)] + [(core, (me + 4 * k) % n) for k in range(1, depth)]

    bwd = (eye, w, wh, vec, wht, vt, gsb, xt, mix, xh, gp, rstd, stream, ex, br, dm, acc, lg, dl, both, rw, gw, gh, gv, dm, width)
    ig_copies = [copies.add(lambda: dm, lambda: ig_out.at[out_rows], sibling, None, lambda t=t: core != t) for t in range(2)]

    def ig_local():
        return pltpu.make_async_copy(dm, ig_out.at[out_rows], local.at[2])

    def emit_inputs(t):
        pl.when(core == t)(lambda: ig_local().start())
        pl.when(core != t)(lambda: copies.start(ig_copies[t]))

    def free_inputs(t):
        pl.when(core == t)(lambda: ig_local().wait())
        pl.when(core != t)(lambda: copies.get(ig_copies[t]).wait_send())

    ex[...] = jnp.zeros_like(ex)
    backward_tower(1, bwd, None, None)
    emit_inputs(1)
    for to_core, to_index in peers:
        pl.semaphore_signal(ready, inc=1, device_id=at(to_core, to_index), device_id_type=MESH)

    def after_head():
        pl.semaphore_wait(ready, len(peers))
        pack(1, range(depth))
        for zz in range(depth):
            sum_0(1, zz)
        pack(0, (depth - 1,))
        sum_0(0, depth - 1)

    def during_backward(i):
        def at_step(step, *calls):
            def run():
                for f, *args in calls:
                    f(*args)

            pl.when(i == step)(run)

        planes = range(depth)
        at_step(1, *((sum_1, 1, zz) for zz in planes), (sum_1, 0, depth - 1))
        at_step(3, *((sum_2, 1, zz) for zz in planes), (sum_2, 0, depth - 1))
        for zz in range(1, depth - 1):
            done = BLOCKS + 1 - 4 * zz + 1
            if done < BLOCKS:
                at_step(done, (pack, 0, (zz,)), (sum_0, 0, zz))
            if done + 1 < BLOCKS:
                at_step(done + 1, (sum_1, 0, zz))
            if done + 2 < BLOCKS:
                at_step(done + 2, (sum_2, 0, zz))
        at_step(5, *((sum_3, 1, zz) for zz in planes), (sum_3, 0, depth - 1))
        at_step(8, (sum_4, 1))

    backward_tower(0, bwd, after_head, during_backward, lambda: free_inputs(1))
    emit_inputs(0)
    done = {zz: BLOCKS + 1 - 4 * zz + 1 for zz in range(1, depth - 1)}
    for zz in sorted(done, reverse=True):
        if done[zz] >= BLOCKS:
            pack(0, (zz,))
            sum_0(0, zz)
    pack(0, (0,))
    sum_0(0, 0)
    vector_step(0)
    for zz in sorted(done, reverse=True):
        if done[zz] + 1 >= BLOCKS:
            sum_1(0, zz)
        if done[zz] + 2 >= BLOCKS:
            sum_2(0, zz)
    sum_1(0, 0)
    vector_step(1)
    for zz in sorted(done, reverse=True):
        sum_3(0, zz)
    sum_2(0, 0)
    vector_step(2)
    sum_3(0, 0)
    vector_step(3)
    sum_4(0)
    copies.start(last_swap)
    final[core] = partial[core]
    vector_step(4)
    copies.arrive(last_swap)

    slot128[...] = jnp.zeros(slot128.shape, F32)
    for h in range(2):
        slot128[pl.ds(2 * hrows * h, hrows, stride=2)] = final[h, :, 0:128]
        slot128[pl.ds(2 * hrows * h + 1, hrows, stride=2)] = final[h, :, 128:D]

    @pl.when(me == owner)
    def _():
        for kind in range(3):
            first = 2 * (plan.v_off[owner] + kind * (BLOCKS + 1))
            for h in range(2):
                value = vacc[3, kind, 0 : BLOCKS + 1, 128 * h : 128 * h + 128]
                slot128[pl.ds(first + h, BLOCKS + 1, stride=2)] = value

    def push(src, dst, to):
        number = copies.add(lambda: src, lambda: dst, lambda: to)
        copies.start(number)
        return copies.get(number)

    lay_flat(plan, me, slot128, flat, rolled)
    update_shard(
        plan, me, p_ref, m_ref, v_ref, (first_out, second_out, new_out, low_out, norm_out),
        flat, squares, sq_z, sq_y, sq_x, push, [at(core, (me + 4 * k) % n) for k in range(1, depth)], to_y(), to_x(),
    )
    copies.arrive(st_copy)
    pl.when(core == 0)(lambda: copies.arrive(ig_copies[0]))
    pl.when(core == 1)(lambda: copies.arrive(ig_copies[1]))
    free_inputs(0)
    st_stay.wait()
    copies.sent.update(ig_copies)
    copies.leave(*range(len(copies.made)))


def train(plan, latent, ints, imp, p128, m128, v128):
    n, rows = plan.n, plan.slot
    depth, hrows = n // 4, rows // 2
    width = ints.shape[1] // 2
    height = p128.shape[0]
    vm = pl.BlockSpec(memory_space=pltpu.VMEM)
    hbm = pl.BlockSpec(memory_space=pl.ANY)
    flat32 = jax.ShapeDtypeStruct((height, 128), F32)
    packed = sum(1 for h, v in zip(plan.h_rows, plan.v_rows) if h or v)
    return pl.pallas_call(
        functools.partial(train_kernel, plan),
        out_shape=(
            jax.ShapeDtypeStruct((2 * width, D), BF),
            jax.ShapeDtypeStruct((2 * width, D), F32),
            flat32,
            flat32,
            flat32,
            jax.ShapeDtypeStruct((height, 128), BF),
            jax.ShapeDtypeStruct((32, 128), F32),
        ),
        in_specs=[hbm] + [vm] * 5,
        out_specs=(hbm, hbm, vm, vm, vm, vm, vm),
        scratch_shapes=[
            pltpu.VMEM((2, A_ROWS, D), BF),
            pltpu.VMEM((2, D, HPAD), BF),
            pltpu.VMEM((2, 128, D), BF),
            pltpu.VMEM((2, 8, width), jnp.int32),
            pltpu.VMEM((8, width), F32),
            *work_scratch(width),
            pltpu.VMEM((2, A_ROWS, D), BF),
            pltpu.VMEM((2, D, HPAD), BF),
            pltpu.VMEM((2, 3, 16, D), F32),
            pltpu.VMEM((2, packed, rows, D), BF),
            pltpu.VMEM((2, width, D), BF),
            pltpu.VMEM((max(2 * rows, height + 48) + 80, 128), F32),
            pltpu.VMEM((height + 128, 128), F32),
            pltpu.VMEM((height + 16, 128), F32),
            pltpu.VMEM((2, rows, 128), F32),
            pltpu.VMEM((128, D), F32),
            pltpu.VMEM((4, 3, 16, D), F32),
            pltpu.VMEM((2 + depth, 3, 16, D), F32),
            pltpu.VMEM((2, hrows, D), F32),
            pltpu.VMEM((2, hrows, D), F32),
            pltpu.VMEM((3, 32, 128), F32),
            pltpu.VMEM((depth, 32, 128), F32),
            pltpu.VMEM((32, 128), F32),
            pltpu.VMEM((32, 128), F32),
            pltpu.SemaphoreType.DMA((11 * n,)),
            pltpu.SemaphoreType.DMA((11 * n,)),
            pltpu.SemaphoreType.DMA((2 * depth,)),
            pltpu.SemaphoreType.DMA((3,)),
            pltpu.SemaphoreType.REGULAR,
        ],
        compiler_params=pltpu.CompilerParams(
            collective_id=2, has_side_effects=True, vmem_limit_bytes=63 * 1024 * 1024
        ),
    )(latent, ints, imp, p128, m128, v128)


def on_device(latent, codes, targets, visits, importance, params, first_moment, second_moment):
    me = lax.axis_index("tower")
    row_count = latent.shape[0]
    half = row_count // 2
    shard_len = params.shape[1]
    plan = Plan(lax.axis_size("dp"), shard_len)
    height = -(-plan.rows128 // 8) * 8

    def to_rows(value):
        return jnp.pad(value[0], (0, 128 * height - shard_len)).reshape(height, 128)

    p128 = to_rows(params)
    ints = jnp.concatenate([codes, targets[0, :1], visits[0].T, targets[0, 1:]], 0)
    if fused_fits(plan):
        states_out, inputs_out, *flat, low, norm = train(
            plan, latent, ints, importance[None], p128, to_rows(first_moment), to_rows(second_moment)
        )
    else:
        x = lax.dynamic_slice_in_dim(latent, me * half, half, 0)
        w, wh, vec, both, rw = gather(plan, p128, ints, importance[None])
        st, ig, gw, gh, gv = compute(x, both, rw, w, wh, vec)
        states_out, inputs_out, *flat, low, norm = reduce_and_update(
            plan, gw, gh, gv, st, ig, p128, to_rows(first_moment), to_rows(second_moment)
        )

    def shard(value):
        return value.reshape(1, -1)[:, :shard_len]

    norms = jnp.stack([norm[:MATS, 0], norm[16 : 16 + MATS, 0]])[None]
    return (states_out[None], inputs_out[None], *(shard(v) for v in flat), shard(low), norms)


def solution(mesh):
    in_specs = (
        P("dp", None),
        P("tower", "dp"),
        P("tower", None, "dp"),
        P("tower", "dp", None),
        P("dp"),
        P("tower", "dp"),
        P("tower", "dp"),
        P("tower", "dp"),
    )
    out_specs = (
        P("tower", "dp", None),
        P("tower", "dp", None),
        P("tower", "dp"),
        P("tower", "dp"),
        P("tower", "dp"),
        P("tower", "dp"),
        P("tower", None, None),
    )
    return jax.shard_map(
        on_device, mesh=mesh, in_specs=in_specs, out_specs=out_specs, check_vma=False
    )
```

```python
import functools

import jax
import jax.numpy as jnp
from jax import lax
from jax.experimental import pallas as pl
from jax.experimental.pallas import tpu as pltpu
from jax.sharding import PartitionSpec as P

D = 256
CODES = 32
BINS = 601
BLOCKS = 10
STEP = 5
HEADS = 1238
MATS = 12
P_SIZE = 1054464
HPAD = 1280
CAT = D + CODES
A_ROWS = CAT + BLOCKS * D
BF = jnp.bfloat16
F32 = jnp.float32
GELU_C = 0.7978845608028654
GELU_K = 0.044715


def nn(a, b):
    return jnp.dot(a, b, preferred_element_type=F32)


def nt(a, b):
    return lax.dot_general(a, b, (((1,), (1,)), ((), ())), preferred_element_type=F32)


def identity(n):
    return (lax.broadcasted_iota(jnp.int32, (n, n), 0) == lax.broadcasted_iota(jnp.int32, (n, n), 1)).astype(BF)


def twice(v):
    return jnp.concatenate([v, v], 1)


def column_stats(ref, cs):
    total = jnp.sum(ref[:, cs], axis=0, keepdims=True)
    mean = total * (1.0 / D)
    square = jnp.zeros((8, mean.shape[1]), F32)
    for r in range(0, D, 32):
        cen = ref[r : r + 32, cs] - mean
        square = square + jnp.sum((cen * cen).reshape(4, 8, -1), axis=0)
    var = jnp.sum(square, axis=0, keepdims=True) * (1.0 / D)
    return mean, lax.rsqrt(var + 1e-05)


def norm_act(src, cs, gsb, xh_ref, gp_ref, rstd_ref, out):
    mean, rstd = column_stats(src, cs)
    rstd_ref[:, cs] = rstd
    for r in range(0, D, 32):
        rs = slice(r, r + 32)
        xh = (src[rs, cs] - mean) * rstd
        xh_ref[rs, cs] = xh.astype(BF)
        y = xh * twice(gsb[rs, 0:128]) + twice(gsb[rs, 128:256])
        y2 = y * y
        p = y2 * (GELU_C * GELU_K) + GELU_C
        t = jnp.tanh(y * p)
        q = t * 0.5 + 0.5
        a = y * q
        out(rs, a)
        slope = q + (a - a * q) * (p * 6.0 - 4.0 * GELU_C)
        gp_ref[rs, cs] = slope.astype(BF)


def broadcast_vectors(vt, rows):
    k = lax.broadcasted_iota(jnp.int32, (128, 128), 0)
    picks = jnp.concatenate([(k == row).astype(BF) for row in rows], 1)
    return nn(vt, picks)


def head_stage(cs, lg, dl, ints, rw):
    width = rw.shape[1]
    it8 = lax.broadcasted_iota(jnp.int32, (8, width), 0)
    low = -jnp.inf
    b75, b150, b154 = lg[600:608], lg[1200:1208], lg[1232:1240]

    def top(block):
        return jnp.max(block, axis=0, keepdims=True)

    def top_range(lo, hi):
        best = lg[lo : lo + 8]
        for r in range(lo + 8, hi, 8):
            best = jnp.maximum(best, lg[r : r + 8])
        return best

    max_v = top(jnp.maximum(top_range(0, 600), jnp.where(it8 < 1, b75, low)))
    max_r = top(
        jnp.maximum(
            jnp.maximum(top_range(608, 1200), jnp.where(it8 >= 1, b75, low)),
            jnp.where(it8 < 2, b150, low),
        )
    )
    max_c = top(
        jnp.maximum(
            jnp.maximum(top_range(1208, 1232), jnp.where(it8 >= 2, b150, low)),
            jnp.where(it8 < 2, b154, low),
        )
    )
    in_policy = (it8 >= 2) & (it8 < 6)
    max_p = top(jnp.where(in_policy, b154, low))

    def exp_range(lo, hi, best):
        acc = jnp.zeros((8, width), F32)
        for r in range(lo, hi, 8):
            e = jnp.exp(lg[r : r + 8] - best)
            lg[r : r + 8] = e
            acc = acc + e
        return acc

    e75 = jnp.exp(b75 - jnp.where(it8 < 1, max_v, max_r))
    e150 = jnp.exp(b150 - jnp.where(it8 < 2, max_r, max_c))
    e154 = jnp.exp(b154 - jnp.where(it8 < 2, max_c, max_p))

    def total(acc):
        return rw / jnp.sum(acc, axis=0, keepdims=True)

    inv_v = total(exp_range(0, 600, max_v) + jnp.where(it8 < 1, e75, 0.0))
    inv_r = total(exp_range(608, 1200, max_r) + jnp.where(it8 >= 1, e75, 0.0) + jnp.where(it8 < 2, e150, 0.0))
    inv_c = total(exp_range(1208, 1232, max_c) + jnp.where(it8 >= 2, e150, 0.0) + jnp.where(it8 < 2, e154, 0.0))
    inv_p = total(jnp.where(in_policy, e154, 0.0))
    hit_v = ints[1:2]
    hit_r = ints[6:7] + BINS
    hit_c = ints[7:8] + 2 * BINS
    counts = jnp.where(in_policy, ints.astype(F32), 0.0)
    share = counts * (rw / jnp.sum(counts, axis=0, keepdims=True))

    def minus(value, lo, *hits):
        at = lax.broadcasted_iota(jnp.int32, value.shape, 0)
        for hit in hits:
            value = value - jnp.where(at == hit - lo, rw, 0.0)
        return value

    d75 = minus(e75 * jnp.where(it8 < 1, inv_v, inv_r), 600, hit_v, hit_r)
    d150 = minus(e150 * jnp.where(it8 < 2, inv_r, inv_c), 1200, hit_r, hit_c)
    d154 = minus(e154 * jnp.where(it8 < 2, inv_c, inv_p), 1232, hit_c) - share
    d154 = jnp.where(it8 < 6, d154, 0.0)

    def emit(lo, hi, inv, hit):
        for r in range(lo, hi, 16):
            dl[r : r + 16, cs] = minus(lg[r : r + 16] * inv, r, hit).astype(BF)

    def pair(first, second):
        return jnp.concatenate([first, second], 0).astype(BF)

    emit(0, 592, inv_v, hit_v)
    dl[592:608, cs] = pair(minus(lg[592:600] * inv_v, 592, hit_v), d75)
    emit(608, 1200, inv_r, hit_r)
    dl[1200:1216, cs] = pair(d150, minus(lg[1208:1216] * inv_c, 1208, hit_c))
    emit(1216, 1232, inv_c, hit_c)
    dl[1232:1248, cs] = pair(d154, jnp.zeros_like(d154))
    dl[1248:HPAD, cs] = jnp.zeros((HPAD - 1248, width), BF)


CB = 256
GROUP = 2


def spread(v, cs):
    return jnp.concatenate([v] * ((cs.stop - cs.start) // 128), 1)


def saved_views(t, mix, xh):
    def mixed(k):
        return mix.at[pl.ds(pl.multiple_of((t * BLOCKS + k - 1) * (D + 16), 16), D + 16)]

    def unit(k):
        return xh.at[pl.ds(pl.multiple_of((t * (BLOCKS + 1) + k) * D, D), D)]

    return mixed, unit


def forward_tower(t, refs, during=None):
    (eye, w, wh, vec, wct, wt, vt, gsb, xt, mix, xh, gp, rstd, stream, ints, width) = refs
    blocks = [slice(c, c + CB) for c in range(0, width, CB)]
    per = min(GROUP, len(blocks))
    groups = [slice(c, c + per * CB) for c in range(0, width, per * CB)]
    mixed, unit = saved_views(t, mix, xh)

    def prefetch(k):
        gsb[k % 2] = broadcast_vectors(vt[...], (k, k + BLOCKS + 1, k + 2 * BLOCKS + 2))
        row = pl.multiple_of(CAT + (k - 1) * D, 32)
        wt[k % 2] = nt(eye[...], w[t, pl.ds(row, D)]).astype(BF)

    def stage(k, c):
        cs = blocks[c]

        def keep(rs, a):
            mixed(k)[rs, cs] = a.astype(BF)

        norm_act(stream, cs, gsb.at[k % 2], unit(k), gp.at[t, k], rstd.at[pl.ds(t * (BLOCKS + 1) + k, 1)], keep)

    def product(k, group):
        return nn(wt[k % 2], mixed(k)[0:D, groups[group]])

    def add(k, group, pre):
        cs = groups[group]
        stream[:, cs] = stream[:, cs] + pre + spread(gsb[k % 2, :, 256:384], cs)

    vt[...] = nt(eye[...], vec[t]).astype(BF)
    wt[0] = nt(eye[...], w[t, 0:D]).astype(BF)
    wct[...] = nt(eye[...], w[t, D:CAT]).astype(BF)
    gsb[0] = broadcast_vectors(vt[...], (0, BLOCKS + 1, 2 * BLOCKS + 2))
    prefetch(1)
    for cs in blocks:
        it = lax.broadcasted_iota(jnp.int32, (CODES, CB), 0)
        xt[t, D:CAT, cs] = (it == ints[t, 0:1, cs]).astype(BF)
        xt[t, CAT : CAT + 16, cs] = jnp.ones((16, CB), BF)
    for c, cs in enumerate(blocks):
        pre = nn(wt[0], xt[t, 0:D, cs]) + nn(wct[...], xt[t, D:CAT, cs])
        stream[:, cs] = pre + twice(gsb[0, :, 256:384])

        def keep(rs, a):
            stream[rs, cs] = a

        norm_act(stream, cs, gsb.at[0], unit(0), gp.at[t, 0], rstd.at[pl.ds(t * (BLOCKS + 1), 1)], keep)

    def layer(k, more):
        if more:
            prefetch(k + 1)
        mixed(k)[D : D + 16, :] = jnp.ones((16, width), BF)
        for group in range(len(groups)):
            pre = product(k, group)
            ahead = group + 1 < len(groups)
            if ahead or more:
                for c in range(per):
                    stage(k if ahead else k + 1, (group + 1) % len(groups) * per + c)
            add(k, group, pre)

    for c in range(per):
        stage(1, c)

    @pl.loop(1, BLOCKS)
    def _(k):
        if during is not None:
            during(k)
        layer(k, True)

    layer(BLOCKS, False)
    for cs in blocks:
        xt[t + 1, 0:D, cs] = stream[:, cs].astype(BF)


def backward_act(cs, grad, gain, gp_ref, xh_ref, acc):
    s1 = jnp.zeros((8, CB), F32)
    s2 = jnp.zeros((8, CB), F32)
    for r in range(0, D, 16):
        rs = slice(r, r + 16)
        g = twice(gain[rs])
        dy = grad[rs, :] * gp_ref[rs, cs].astype(F32)
        prod = dy * xh_ref[rs, cs].astype(F32)
        back = dy * g
        grad[rs, :] = back
        prod_g = prod * g
        s1 = s1 + (back[0:8] + back[8:16])
        s2 = s2 + (prod_g[0:8] + prod_g[8:16])
        acc[0, rs] = acc[0, rs] + (prod[:, 0:128] + prod[:, 128:CB])
        acc[1, rs] = acc[1, rs] + (dy[:, 0:128] + dy[:, 128:CB])
    m1 = jnp.sum(s1, axis=0, keepdims=True) * (1.0 / D)
    m2 = jnp.sum(s2, axis=0, keepdims=True) * (1.0 / D)
    return m1, m2


def backward_tower(t, refs, after_head=None, during=None, before_product=None):
    (eye, w, wh, vec, wht, vt, gsb, xt, mix, xh, gp, rstd, ds, ex, br, dm, acc, lg, dl, ints, rw, gw, gh, gv, ig, width) = refs
    blocks = [slice(c, c + CB) for c in range(0, width, CB)]
    per = min(GROUP, len(blocks))
    groups = [slice(c, c + per * CB) for c in range(0, width, per * CB)]
    mixed, unit = saved_views(t, mix, xh)
    vt[...] = nt(eye[...], vec[t]).astype(BF)
    for h in range(0, HPAD, D):
        wht[h : h + D, :] = nt(eye[...], wh[t, :, h : h + D]).astype(BF)

    @pl.loop(0, width // CB)
    def _(c):
        cs = pl.ds(pl.multiple_of(c * CB, CB), CB)
        lg[...] = nn(wht[...], xt[t + 1, 0:D, cs])
        head_stage(cs, lg, dl, ints[t, :, cs], rw[0:1, cs])
        value = nn(wh[t], dl[:, cs]) + ex[:, cs]
        ds[:, cs] = value
        br[BLOCKS % 2, :, cs] = value.astype(BF)

    for h in range(0, HPAD, D):
        gh[t, :, h : h + D] = nt(xt[t + 1, 0:D, :], dl[h : h + D]).astype(BF)
    if after_head is not None:
        after_head()
    acc[...] = jnp.zeros(acc.shape, F32)
    ones = jnp.ones((16, 128), BF)

    def part(c):
        return dm.at[c * D : c * D + D]

    def gains(k):
        gsb[k % 2, :, 0:128] = broadcast_vectors(vt[...], (k,))

    def row_sums(k):
        for kind in range(2):
            gv[t, kind, pl.ds(k, 1), :] = nt(ones, acc[k % 2, kind].astype(BF))[0:1]
        acc[k % 2] = jnp.zeros(acc.shape[1:], F32)

    def product(k, group):
        row = pl.multiple_of(CAT + (k - 1) * D, 32)
        back = nn(w[t, pl.ds(row, D)], br[k % 2, :, groups[group]])
        for c in range(per):
            part(group * per + c)[...] = back[:, c * CB : c * CB + CB]

    def stage(k, c, first):
        cs = blocks[c]
        m1, m2 = backward_act(cs, part(c), gsb.at[k % 2, :, 0:128], gp.at[t, k], unit(k), acc.at[k % 2])
        rs1 = rstd[pl.ds(t * (BLOCKS + 1) + k, 1), cs]
        m1 = m1 * rs1
        m2 = m2 * rs1
        for r in range(0, D, 32):
            rs = slice(r, r + 32)
            back = part(c)[rs, :] * rs1 - m1 - unit(k)[rs, cs].astype(F32) * m2
            if first:
                br[0, rs, cs] = back.astype(BF)
            else:
                value = ds[rs, cs] + back
                ds[rs, cs] = value
                br[(k + 1) % 2, rs, cs] = value.astype(BF)

    if before_product is not None:
        before_product()
    gains(BLOCKS)
    product(BLOCKS, 0)

    @pl.loop(0, BLOCKS)
    def _(i):
        k = BLOCKS - i
        if during is not None:
            during(i)
        gains(k - 1)
        for group in range(len(groups)):
            if group + 1 < len(groups):
                product(k, group + 1)
            for c in range(per):
                stage(k, group * per + c, False)
            if group == 0:
                full = nt(mixed(k)[...], br[k % 2])
                row = pl.multiple_of(CAT + (k - 1) * D, 32)
                gw[t, pl.ds(row, D), :] = full[0:D].astype(BF)
                gv[t, 2, pl.ds(k, 1), :] = full[D : D + 1]
                row_sums(k + 1)
                product(k - 1, 0)

    for c, cs in enumerate(blocks):
        part(c)[...] = ds[:, cs]
        stage(0, c, True)
    row_sums(1)
    row_sums(0)
    full = nt(xt[t], br[0])
    gw[t, 0:CAT, :] = full[0:CAT].astype(BF)
    gv[t, 2, 0:1, :] = full[CAT : CAT + 1]
    for cs in blocks:
        back = nn(w[t, 0:D], br[0, :, cs])
        ex[:, cs] = back
        ig[cs, :] = back.T


def compute_kernel(x_ref, ints, rw, w, wh, vec, st, ig, gw, gh, gv, eye, wct, wt, wht, vt, gsb, xt, mix, xh, gp, rstd, stream, ex, br, dm, acc, lg, dl):
    width = x_ref.shape[0]
    eye[...] = identity(D)
    for c in range(0, width, CB):
        cs = slice(c, c + CB)
        xt[0, 0:D, cs] = nt(eye[...], x_ref[cs, :]).astype(BF)
    fwd = (eye, w, wh, vec, wct, wt, vt, gsb, xt, mix, xh, gp, rstd, stream, ints, width)
    @pl.loop(0, 2)
    def _(t):
        forward_tower(t, fwd)

        @pl.loop(0, width // CB)
        def _(c):
            cs = pl.ds(pl.multiple_of(c * CB, CB), CB)
            st[t, cs, :] = nt(eye[...], xt[t + 1, 0:D, cs]).astype(BF)

    ex[...] = jnp.zeros_like(ex)

    @pl.loop(0, 2)
    def _(i):
        t = 1 - i
        backward_tower(
            t,
            (eye, w, wh, vec, wht, vt, gsb, xt, mix, xh, gp, rstd, stream, ex, br, dm, acc, lg, dl, ints, rw, gw, gh, gv, ig.at[t], width),
        )


def work_scratch(width):
    return [
        pltpu.VMEM((D, D), BF),
        pltpu.VMEM((D, CODES), BF),
        pltpu.VMEM((2, D, D), BF),
        pltpu.VMEM((HPAD, D), BF),
        pltpu.VMEM((D, 128), BF),
        pltpu.VMEM((2, D, 384), F32),
        pltpu.VMEM((3, CAT + 16, width), BF),
        pltpu.VMEM((2 * BLOCKS * (D + 16), width), BF),
        pltpu.VMEM((2 * (BLOCKS + 1) * D, width), BF),
        pltpu.VMEM((2, BLOCKS + 1, D, width), BF),
        pltpu.VMEM((24, width), F32),
        pltpu.VMEM((D, width), F32),
        pltpu.VMEM((D, width), F32),
        pltpu.VMEM((2, D, width), BF),
        pltpu.VMEM((width // CB * D, CB), F32),
        pltpu.VMEM((2, 2, D, 128), F32),
        pltpu.VMEM((HPAD, CB), F32),
        pltpu.VMEM((HPAD, width), BF),
    ]


def compute(x, ints, rw, w, wh, vec):
    width = x.shape[0]
    vm = pl.BlockSpec(memory_space=pltpu.VMEM)
    return pl.pallas_call(
        compute_kernel,
        out_shape=(
            jax.ShapeDtypeStruct((2, width, D), BF),
            jax.ShapeDtypeStruct((2, width, D), F32),
            jax.ShapeDtypeStruct((2, A_ROWS, D), BF),
            jax.ShapeDtypeStruct((2, D, HPAD), BF),
            jax.ShapeDtypeStruct((2, 3, 16, D), F32),
        ),
        in_specs=[vm] * 6,
        out_specs=(vm,) * 5,
        scratch_shapes=work_scratch(width),
        compiler_params=pltpu.CompilerParams(vmem_limit_bytes=62 * 1024 * 1024),
    )(x, ints, rw, w, wh, vec)


class Plan:
    def __init__(self, n, length):
        self.n, self.length = n, length
        self.rows128 = -(-length // 128)
        block_end, head_end = A_ROWS * D, A_ROWS * D + D * HEADS
        self.a_base, self.a_rows, self.h_first, self.h_rows, self.h_off, self.v_first, self.v_rows, self.v_off = ([] for _ in range(8))
        used = 0
        for i in range(n):
            lo, hi = i * length, (i + 1) * length
            base = min(lo, block_end) // D // 16 * 16
            top = -(-min(hi, block_end) // D)
            a_rows = -(-(top - base) // 16) * 16 if lo < block_end else 0
            first = min(max(lo - block_end, 0), D * HEADS) // HEADS
            last = -(-min(max(hi - block_end, 0), D * HEADS) // HEADS)
            h_rows = last - first if hi > block_end and lo < head_end else 0
            v_first = max(lo - head_end, 0) // D
            v_rows = -(-(hi - head_end) // D) - v_first if hi > head_end else 0
            self.a_base.append(base)
            self.a_rows.append(a_rows)
            self.h_first.append(first)
            self.h_rows.append(h_rows)
            self.h_off.append(a_rows)
            self.v_first.append(v_first)
            self.v_rows.append(v_rows)
            self.v_off.append(a_rows + 5 * h_rows)
            used = max(used, a_rows + 5 * h_rows + v_rows)
        self.slot = -(-(used + 1) // 32) * 32

    def at(self, table, me):
        value = jnp.int32(table[0])
        for i in range(1, self.n):
            if table[i] != table[i - 1]:
                value = value + (me >= i).astype(jnp.int32) * (table[i] - table[i - 1])
        return value


MESH = pl.DeviceIdType.MESH


def neighbours(n):
    core = lax.axis_index("tower")
    me = lax.axis_index("dp")
    near_x = me + 1 - 2 * (me % 2)
    near_y = me + 2 - 4 * ((me // 2) % 2)
    return core, me, near_x, near_y


def at(core, index):
    return {"tower": core, "dp": index}


def greet(core, me, near_x, near_y, n):
    barrier = pltpu.get_barrier_semaphore()
    pl.semaphore_signal(barrier, inc=1, device_id=at(1 - core, me), device_id_type=MESH)
    for near in (near_x, near_y):
        pl.semaphore_signal(barrier, inc=1, device_id=at(core, near), device_id_type=MESH)
    for k in range(1, n // 4):
        pl.semaphore_signal(barrier, inc=1, device_id=at(core, (me + 4 * k) % n), device_id_type=MESH)
    return barrier


def place_shard(plan, me, p_ref, slot128, shifted, rolled):
    rows = plan.rows128
    start = me * plan.length
    shift = start % 128
    first = start // 128
    tall = shifted.shape[0]
    height = p_ref.shape[0]
    lane = lax.broadcasted_iota(jnp.int32, (height, 128), 1)
    rolled[0:8] = jnp.zeros((8, 128), F32)
    rolled[8 : 8 + height] = pltpu.roll(p_ref[...], shift, 1)
    shifted[...] = jnp.zeros((tall, 128), F32)
    moved = jnp.where(lane >= shift, rolled[8 : 8 + height], rolled[7 : 7 + height])
    shifted[16 : 16 + height] = moved
    slot128[...] = jnp.zeros(slot128.shape, F32)
    row = lax.broadcasted_iota(jnp.int32, (height, 128), 0)
    base = plan.at(plan.a_base, me)

    @pl.when(plan.at(plan.a_rows, me) > 0)
    def _():
        slot128[pl.ds(first - 2 * base, height)] = jnp.where(row + first < 2 * A_ROWS, moved, 0.0)

    h_first, h_rows, h_off = (plan.at(t, me) for t in (plan.h_first, plan.h_rows, plan.h_off))
    it = lax.broadcasted_iota(jnp.int32, (10, 128), 0)
    lane10 = lax.broadcasted_iota(jnp.int32, (10, 128), 1)

    @pl.loop(0, h_rows)
    def _(k):
        begin = A_ROWS * D + HEADS * (h_first + k) - 128 * first + 128 * 16
        turn = begin % 128
        window = pltpu.roll(shifted[pl.ds(begin // 128, 16)], (128 - turn) % 128, 1)
        value = jnp.where(lane10 < 128 - turn, window[0:10], window[1:11])
        slot128[pl.ds(2 * h_off + 10 * k, 10)] = jnp.where(it * 128 + lane10 < HEADS, value, 0.0)

    v_start = (A_ROWS * D + D * HEADS) // 128
    v_rows, v_off, v_first = (plan.at(t, me) for t in (plan.v_rows, plan.v_off, plan.v_first))
    tall_v = min(height, -(-2 * max(plan.v_rows) // 8) * 8)

    @pl.when(v_rows > 0)
    def _():
        inside = plan.at([max(0, v_start - i * plan.length // 128) for i in range(plan.n)], me)
        to = 2 * v_off + first + inside - v_start - 2 * v_first
        slot128[pl.ds(to, tall_v)] = shifted[pl.ds(16 + inside, tall_v)]


def unpack_rows(plan, i, slot, w, heads, vectors, scratch):
    base, rows = plan.a_base[i], plan.a_rows[i]
    if rows:
        shared = i > 0 and base < plan.a_base[i - 1] + plan.a_rows[i - 1]
        lo = 0
        if shared:
            w[base : base + 16] = w[base : base + 16] + slot[0:16]
            lo = 16
        if rows > lo:
            w[base + lo : base + rows] = slot[lo:rows]
    h_rows, h_off, h_first = plan.h_rows[i], plan.h_off[i], plan.h_first[i]
    v_rows, v_off, v_first = plan.v_rows[i], plan.v_off[i], plan.v_first[i]
    if h_rows or v_rows:
        value = slot.astype(F32)
        scratch[0] = value[:, 0:128]
        scratch[1] = value[:, 128:D]
    if h_rows:
        shared = i > 0 and plan.h_rows[i - 1] and plan.h_first[i - 1] + plan.h_rows[i - 1] > h_first
        for j in range(5):
            for half in range(2):
                cols = slice(128 * half, 128 * half + 128)
                first = D * j + h_first
                value = scratch[half, pl.ds(h_off + j, h_rows, stride=5)]
                if shared:
                    heads[first : first + 1, cols] = heads[first : first + 1, cols] + value[0:1]
                    if h_rows > 1:
                        heads[first + 1 : first + h_rows, cols] = value[1:h_rows]
                else:
                    heads[first : first + h_rows, cols] = value
    if v_rows:
        shared = v_first and plan.v_first[i - 1] + plan.v_rows[i - 1] > v_first
        shared = shared or (i > 0 and plan.v_rows[i - 1] > 0 and v_first == 0)
        for half in range(2):
            cols = slice(128 * half, 128 * half + 128)
            value = scratch[half, v_off : v_off + v_rows]
            if shared:
                vectors[v_first : v_first + 1, cols] = vectors[v_first : v_first + 1, cols] + value[0:1]
                if v_rows > 1:
                    vectors[v_first + 1 : v_first + v_rows, cols] = value[1:v_rows]
            else:
                vectors[v_first : v_first + v_rows, cols] = value


def split3(value):
    hi = value.astype(BF).astype(F32)
    mid = (value - hi).astype(BF).astype(F32)
    return hi, mid, value - hi - mid


def gather_kernel(plan, p_ref, ints_ref, imp_ref, w, wh, vec, both, rw, slots, slot128, shifted, rolled, scratch, whf, vecf, send, recv):
    n = plan.n
    depth = n // 4
    core, me, near_x, near_y = neighbours(n)
    barrier = greet(core, me, near_x, near_y, n)
    place_shard(plan, me, p_ref, slot128, shifted, rolled)
    pl.semaphore_wait(barrier, depth + 2)
    half = rw.shape[1]
    started = []

    def copy(src, dst, slot, to):
        c = pltpu.make_async_remote_copy(
            src_ref=src, dst_ref=dst, send_sem=send.at[slot], recv_sem=recv.at[slot], device_id=to, device_id_type=MESH
        )
        c.start()
        started.append(c)
        return c

    mine = pl.multiple_of(core * half, half)
    theirs = pl.multiple_of((1 - core) * half, half)
    number = iter(range(1 << 20))
    ints_copy = copy(ints_ref.at[:, pl.ds(theirs, half)], both.at[core], next(number), at(1 - core, me))
    rows = plan.slot
    total = jnp.sum(imp_ref[...].astype(F32), axis=1, keepdims=True)
    lane = lax.broadcasted_iota(jnp.int32, (1, D), 1)
    hi, mid, lo = split3(total)
    left = slot128[pl.ds(0, rows, stride=2)]
    right = slot128[pl.ds(1, rows, stride=2)]
    own = jnp.concatenate([left, right], 1)
    last = jnp.where(lane == 0, hi, jnp.where(lane == 1, mid, jnp.where(lane == 2, lo, 0.0)))
    last_row = lax.broadcasted_iota(jnp.int32, (rows, D), 0) == rows - 1
    slots[core, me] = jnp.where(last_row, last, own).astype(BF)

    def column(index, k):
        return (index + n - 4 * k) % n

    def send_slot(origin, to, lo=0, hi=rows):
        ref = slots.at[core, origin, pl.ds(lo, hi - lo)]
        return copy(ref, ref, next(number), to)

    near_xy = near_x + near_y - me
    cut = rows // 2
    z_in, x_in, y_in, d_in, s_in = {}, {}, {}, {}, []
    for k in sorted(range(1, depth), key=lambda k: (min(k, depth - k), k)):
        z_in[k] = send_slot(me, at(core, (me + 4 * k) % n))
    order = [0] + list(z_in)
    for k in order:
        if k:
            z_in[k].wait_recv()
        x_in[k] = send_slot(column(me, k), at(core, near_x))
        y_in[k] = send_slot(column(me, k), at(core, near_y))
        s_in.append(send_slot(column(me, k), at(1 - core, me)))
    for k in order:
        x_in[k].wait_recv()
        first = send_slot(column(near_x, k), at(core, near_y), 0, cut)
        s_in.append(send_slot(column(near_x, k), at(1 - core, me)))
        y_in[k].wait_recv()
        second = send_slot(column(near_y, k), at(core, near_x), cut, rows)
        s_in.append(send_slot(column(near_y, k), at(1 - core, me)))
        d_in[k] = (first, second)
    for k in order:
        for c in d_in[k]:
            c.wait_recv()
        s_in.append(send_slot(column(near_xy, k), at(1 - core, me)))
    ints_copy.wait_recv()
    both[core] = ints_ref[:, pl.ds(mine, half)]
    for c in s_in:
        c.wait_recv()
    for c in started:
        c.wait_send()
    for t in range(2):
        vecf[...] = jnp.zeros(vecf.shape, F32)
        for i in range(n):
            unpack_rows(plan, i, slots[t, i], w.at[t], whf, vecf, scratch)
        for j in range(5):
            wh[t, :, D * j : D * j + D] = whf[D * j : D * j + D].astype(BF)
        vec[t] = vecf[...].astype(BF)
    total = jnp.zeros((1, D), F32)
    for i in range(n):
        tail = slots[0, i, rows - 16 : rows].astype(F32)
        total = total + tail[15:16]
    weight_sum = jnp.sum(jnp.where(lane < 3, total, 0.0), axis=1, keepdims=True)
    rw[...] = jnp.broadcast_to(imp_ref[:, pl.ds(mine, half)].astype(F32) / weight_sum, (8, half))


def gather(plan, p128, ints, imp):
    n, rows = plan.n, plan.slot
    half = ints.shape[1] // 2
    vm = pl.BlockSpec(memory_space=pltpu.VMEM)
    height = p128.shape[0]
    tall = max(2 * rows, height + 40) + 80
    copies = 1 + (n // 4 - 1) + 2 * (n // 4) + 2 * (n // 4) + n
    return pl.pallas_call(
        functools.partial(gather_kernel, plan),
        out_shape=(
            jax.ShapeDtypeStruct((2, A_ROWS, D), BF),
            jax.ShapeDtypeStruct((2, D, HPAD), BF),
            jax.ShapeDtypeStruct((2, 128, D), BF),
            jax.ShapeDtypeStruct((2, 8, half), jnp.int32),
            jax.ShapeDtypeStruct((8, half), F32),
        ),
        in_specs=[vm] * 3,
        out_specs=(vm,) * 5,
        scratch_shapes=[
            pltpu.VMEM((2, n, rows, D), BF),
            pltpu.VMEM((tall, 128), F32),
            pltpu.VMEM((height + 128, 128), F32),
            pltpu.VMEM((height + 8, 128), F32),
            pltpu.VMEM((2, rows, 128), F32),
            pltpu.VMEM((HPAD, D), F32),
            pltpu.VMEM((128, D), F32),
            pltpu.SemaphoreType.DMA((copies,)),
            pltpu.SemaphoreType.DMA((copies,)),
        ],
        compiler_params=pltpu.CompilerParams(
            collective_id=0, has_side_effects=True, vmem_limit_bytes=48 * 1024 * 1024
        ),
    )(p128, ints, imp)


def chunks(height):
    step = max(c for c in range(8, 113, 8) if height % c == 0)
    return [(lo, lo + step) for lo in range(0, height, step)]


def lay_flat(plan, me, slot128, flat, rolled):
    height = rolled.shape[0] - 16
    start = me * plan.length
    shift = start % 128
    first = start // 128
    base = plan.at(plan.a_base, me)
    row = lax.broadcasted_iota(jnp.int32, (height + 8, 128), 0)
    flat[...] = jnp.zeros(flat.shape, F32)

    @pl.when(plan.at(plan.a_rows, me) > 0)
    def _():
        rows = slot128[pl.ds(first - 2 * base, height + 8)]
        flat[16 : 24 + height] = jnp.where(row + first < 2 * A_ROWS, rows, 0.0)

    h_first, h_rows, h_off = (plan.at(t, me) for t in (plan.h_first, plan.h_rows, plan.h_off))
    it = lax.broadcasted_iota(jnp.int32, (16, 128), 0)
    lane = lax.broadcasted_iota(jnp.int32, (16, 128), 1)

    @pl.loop(0, h_rows)
    def _(k):
        begin = A_ROWS * D + HEADS * (h_first + k) - 128 * first + 128 * 16
        turn = begin % 128
        value = slot128[pl.ds(2 * h_off + 10 * k, 16)]
        value = jnp.where(it * 128 + lane < HEADS, value, 0.0)
        value = pltpu.roll(value, turn, 1)
        above = jnp.concatenate([jnp.zeros((8, 128), F32), value], 0)[7:23]
        to = pl.ds(begin // 128, 16)
        flat[to] = flat[to] + jnp.where(lane >= turn, value, above)

    v_start = (A_ROWS * D + D * HEADS) // 128
    v_rows, v_off, v_first = (plan.at(t, me) for t in (plan.v_rows, plan.v_off, plan.v_first))
    tall_v = min(height, -(-2 * max(plan.v_rows) // 8) * 8)

    @pl.when(v_rows > 0)
    def _():
        inside = plan.at([max(0, v_start - i * plan.length // 128) for i in range(plan.n)], me)
        source = 2 * v_off + first + inside - v_start - 2 * v_first
        to = pl.ds(16 + inside, tall_v)
        flat[to] = flat[to] + slot128[pl.ds(source, tall_v)]

    rolled[0 : height + 8] = pltpu.roll(flat[16 : 24 + height], (128 - shift) % 128, 1)
    for lo, hi in chunks(height):
        lane = lax.broadcasted_iota(jnp.int32, (hi - lo, 128), 1)
        flat[lo:hi] = jnp.where(lane < 128 - shift, rolled[lo:hi], rolled[lo + 1 : hi + 1])


def pack_slots(plan, core, gw, gh, gv, rgw, rgh, rgv, slots, sums, vsum, scratch):
    total = gv[core].astype(F32) + rgv[...]
    for kind in range(3):
        vsum[kind * (BLOCKS + 1) : (kind + 1) * (BLOCKS + 1)] = total[kind, 0 : BLOCKS + 1]
    sums[...] = gh[core].astype(F32) + rgh[...].astype(F32)
    for i in range(plan.n):
        base, rows = plan.a_base[i], plan.a_rows[i]
        h_rows, h_off, h_first = plan.h_rows[i], plan.h_off[i], plan.h_first[i]
        v_rows, v_off, v_first = plan.v_rows[i], plan.v_off[i], plan.v_first[i]
        slots[i, rows : plan.slot] = jnp.zeros((plan.slot - rows, D), BF)
        if rows:
            added = gw[core, base : base + rows].astype(F32) + rgw[base : base + rows].astype(F32)
            slots[i, 0:rows] = added.astype(BF)
        if h_rows or v_rows:
            scratch[...] = jnp.zeros(scratch.shape, F32)
            for half in range(2):
                for j in range(5 if h_rows else 0):
                    cols = slice(D * j + 128 * half, D * j + 128 * half + 128)
                    scratch[half, pl.ds(h_off + j, h_rows, stride=5)] = sums[h_first : h_first + h_rows, cols]
                if v_rows:
                    scratch[half, v_off : v_off + v_rows] = vsum[v_first : v_first + v_rows, 128 * half : 128 * half + 128]
            whole = jnp.concatenate([scratch[0], scratch[1]], 1)
            slots[i, rows : plan.slot] = whole[rows:].astype(BF)


def segment_bounds():
    first = [0] + [(CAT + j * D) * D for j in range(BLOCKS + 1)]
    return list(zip(first, first[1:] + [A_ROWS * D + D * HEADS]))


def update_shard(plan, me, p_ref, m_ref, v_ref, outs, flat, squares, sq_z, sq_y, sq_x, push, to_z, to_y, to_x):
    first_out, second_out, new_out, low_out, norm_out = outs
    height = p_ref.shape[0]
    start = me * plan.length
    correction = 1.0 - 0.5**STEP
    bounds = segment_bounds()

    def place(lo, hi):
        shape = (hi - lo, 128)
        return 128 * lo + 128 * lax.broadcasted_iota(jnp.int32, shape, 0) + lax.broadcasted_iota(jnp.int32, shape, 1)

    for lo, hi in chunks(height):
        spot = place(lo, hi)
        grad = jnp.where(spot < plan.length, flat[lo:hi], 0.0)
        first_new = 0.5 * m_ref[lo:hi] + 0.5 * grad
        second_new = 0.5 * v_ref[lo:hi] + 0.5 * grad * grad
        first_out[lo:hi] = first_new
        second_out[lo:hi] = second_new
        decay = jnp.where(spot < bounds[-1][1] - start, 0.01 * p_ref[lo:hi], 0.0)
        update = first_new / correction / (jnp.sqrt(second_new / correction) + 1e-06) + decay
        flat[lo:hi] = jnp.where(spot < plan.length, update, 0.0)
        new_out[lo:hi] = p_ref[lo:hi] - 0.5 * update
    squares[...] = jnp.zeros(squares.shape, F32)

    def each_segment(body):
        for j, (first, last) in enumerate(bounds):
            pl.when((first < start + plan.length) & (last > start))(lambda j=j, first=first, last=last: body(j, first, last))

    def square_sums(j, first, last):
        weight, change = jnp.zeros((8, 128), F32), jnp.zeros((8, 128), F32)
        for lo, hi in chunks(height):
            spot = place(lo, hi)
            inside = (spot >= first - start) & (spot < last - start)
            p, u = jnp.where(inside, p_ref[lo:hi], 0.0), jnp.where(inside, flat[lo:hi], 0.0)
            weight = weight + jnp.sum((p * p).reshape(-1, 8, 128), axis=0)
            change = change + jnp.sum((u * u).reshape(-1, 8, 128), axis=0)
        squares[0, j : j + 1] = jnp.sum(weight, axis=0, keepdims=True)
        squares[0, 16 + j : 17 + j] = jnp.sum(change, axis=0, keepdims=True)

    each_segment(square_sums)
    for c in [push(squares.at[0], sq_z.at[k], to) for k, to in enumerate(to_z, 1)]:
        c.wait_recv()
    total = squares[0]
    for k in range(1, len(to_z) + 1):
        total = total + sq_z[k]
    squares[1] = total
    push(squares.at[1], sq_y, to_y).wait_recv()
    squares[2] = squares[1] + sq_y[...]
    push(squares.at[2], sq_x, to_x).wait_recv()
    norm = jnp.sqrt(jnp.sum(squares[2] + sq_x[...], axis=1, keepdims=True))
    norm_out[...] = jnp.broadcast_to(norm, (32, 128))

    def scaled(j, first, last):
        ratio = norm_out[j : j + 1] / norm_out[16 + j : 17 + j]
        for lo, hi in chunks(height):
            spot = place(lo, hi)
            inside = (spot >= first - start) & (spot < last - start)
            new_out[lo:hi] = jnp.where(inside, p_ref[lo:hi] - 0.5 * ratio * flat[lo:hi], new_out[lo:hi])

    each_segment(scaled)
    for lo, hi in chunks(height):
        low_out[lo:hi] = new_out[lo:hi].astype(BF)


def reduce_kernel(
    plan, gw, gh, gv, st, ig, p_ref, m_ref, v_ref,
    st_out, ig_out, first_out, second_out, new_out, low_out, norm_out,
    rgw, rgh, rgv, slots, sums, vsum, scratch, in_d, in_x, in_y, in_z, slot128, flat, rolled, squares, sq_z, sq_y, sq_x,
    send, recv, local,
):
    n, rows = plan.n, plan.slot
    depth, cut = n // 4, plan.slot // 2
    core, me, near_x, near_y = neighbours(n)
    near_xy = near_x + near_y - me
    barrier = greet(core, me, near_x, near_y, n)
    pl.semaphore_wait(barrier, depth + 2)
    half = st.shape[1]
    number = iter(range(1 << 20))
    started = []

    def copy(src, dst, to):
        slot = next(number)
        c = pltpu.make_async_remote_copy(
            src_ref=src, dst_ref=dst, send_sem=send.at[slot], recv_sem=recv.at[slot], device_id=to, device_id_type=MESH
        )
        c.start()
        started.append(c)
        return c

    def column(index, k):
        return (index + n - 4 * k) % n

    sibling = at(1 - core, me)
    early = [
        copy(gw.at[1 - core], rgw, sibling),
        copy(gh.at[1 - core], rgh, sibling),
        copy(gv.at[1 - core], rgv, sibling),
    ]
    mine = pl.ds(pl.multiple_of(core * half, half), half)
    late = [
        copy(st.at[1 - core], st_out.at[mine], sibling),
        copy(ig.at[1 - core], ig_out.at[mine], sibling),
    ]
    stay = [
        pltpu.make_async_copy(st.at[core], st_out.at[mine], local.at[0]),
        pltpu.make_async_copy(ig.at[core], ig_out.at[mine], local.at[1]),
    ]
    for c in stay:
        c.start()
    for c in early:
        c.wait_recv()
    pack_slots(plan, core, gw, gh, gv, rgw, rgh, rgv, slots, sums, vsum, scratch)
    order = list(range(1, depth)) + [0]
    to_x, to_y = at(core, near_x), at(core, near_y)
    halves = {}
    for k in order:
        diagonal = column(near_xy, k)
        halves[k] = (
            copy(slots.at[diagonal, pl.ds(0, cut)], in_d.at[k, pl.ds(0, cut)], to_y),
            copy(slots.at[diagonal, pl.ds(cut, rows - cut)], in_d.at[k, pl.ds(cut, rows - cut)], to_x),
        )
    fulls = {}
    for k in order:
        ox, oy = column(near_x, k), column(near_y, k)
        halves[k][0].wait_recv()
        slots[ox, 0:cut] = (slots[ox, 0:cut].astype(F32) + in_d[k, 0:cut].astype(F32)).astype(BF)
        first = copy(slots.at[ox], in_x.at[k], to_x)
        halves[k][1].wait_recv()
        slots[oy, cut:rows] = (slots[oy, cut:rows].astype(F32) + in_d[k, cut:rows].astype(F32)).astype(BF)
        fulls[k] = (first, copy(slots.at[oy], in_y.at[k], to_y))
    along = {}
    for k in order:
        own = column(me, k)
        for c in fulls[k]:
            c.wait_recv()
        if k:
            total = slots[own].astype(F32) + in_x[k].astype(F32) + in_y[k].astype(F32)
            slots[own] = total.astype(BF)
            along[k] = copy(slots.at[own], in_z.at[k], at(core, own))
    for c in along.values():
        c.wait_recv()
    total = slots[me].astype(F32) + in_x[0].astype(F32) + in_y[0].astype(F32)
    for k in along:
        total = total + in_z[k].astype(F32)
    slot128[...] = jnp.zeros(slot128.shape, F32)
    slot128[pl.ds(0, rows, stride=2)] = total[:, 0:128]
    slot128[pl.ds(1, rows, stride=2)] = total[:, 128:D]
    lay_flat(plan, me, slot128, flat, rolled)

    to_z = [at(core, column(me, k)) for k in range(1, depth)]
    outs = (first_out, second_out, new_out, low_out, norm_out)
    update_shard(plan, me, p_ref, m_ref, v_ref, outs, flat, squares, sq_z, sq_y, sq_x, copy, to_z, to_y, to_x)
    for c in late:
        c.wait_recv()
    for c in stay:
        c.wait()
    for c in started:
        c.wait_send()


def reduce_and_update(plan, gw, gh, gv, st, ig, p128, m128, v128):
    n, rows = plan.n, plan.slot
    depth = n // 4
    half = st.shape[1]
    height = p128.shape[0]
    vm = pl.BlockSpec(memory_space=pltpu.VMEM)
    hbm = pl.BlockSpec(memory_space=pl.ANY)
    copies = 5 + 2 * depth + 2 * depth + (depth - 1) + (depth - 1) + 2
    flat32 = jax.ShapeDtypeStruct((height, 128), F32)
    return pl.pallas_call(
        functools.partial(reduce_kernel, plan),
        out_shape=(
            jax.ShapeDtypeStruct((2 * half, D), BF),
            jax.ShapeDtypeStruct((2 * half, D), F32),
            flat32,
            flat32,
            flat32,
            jax.ShapeDtypeStruct((height, 128), BF),
            jax.ShapeDtypeStruct((32, 128), F32),
        ),
        in_specs=[vm] * 3 + [hbm] * 2 + [vm] * 3,
        out_specs=(hbm, hbm, vm, vm, vm, vm, vm),
        scratch_shapes=[
            pltpu.VMEM((A_ROWS, D), BF),
            pltpu.VMEM((D, HPAD), BF),
            pltpu.VMEM(gv.shape[1:], F32),
            pltpu.VMEM((n, rows, D), BF),
            pltpu.VMEM((D, HPAD), F32),
            pltpu.VMEM((40, D), F32),
            pltpu.VMEM((2, rows, 128), F32),
            pltpu.VMEM((depth, rows, D), BF),
            pltpu.VMEM((depth, rows, D), BF),
            pltpu.VMEM((depth, rows, D), BF),
            pltpu.VMEM((depth, rows, D), BF),
            pltpu.VMEM((max(2 * rows, height + 48) + 80, 128), F32),
            pltpu.VMEM((height + 128, 128), F32),
            pltpu.VMEM((height + 16, 128), F32),
            pltpu.VMEM((3, 32, 128), F32),
            pltpu.VMEM((depth, 32, 128), F32),
            pltpu.VMEM((32, 128), F32),
            pltpu.VMEM((32, 128), F32),
            pltpu.SemaphoreType.DMA((copies,)),
            pltpu.SemaphoreType.DMA((copies,)),
            pltpu.SemaphoreType.DMA((2,)),
        ],
        compiler_params=pltpu.CompilerParams(
            collective_id=1, has_side_effects=True, vmem_limit_bytes=48 * 1024 * 1024
        ),
    )(gw, gh, gv, st, ig, p128, m128, v128)


class Copies:
    def __init__(self, send, recv):
        self.send, self.recv, self.made, self.sent = send, recv, [], set()

    def add(self, src, dst, to, recv_slot=None, only=None):
        self.made.append((src, dst, to, recv_slot, only))
        return len(self.made) - 1

    def get(self, number):
        src, dst, to, recv_slot, _ = self.made[number]
        return pltpu.make_async_remote_copy(
            src_ref=src(), dst_ref=dst(), send_sem=self.send.at[number],
            recv_sem=self.recv.at[number] if recv_slot is None else recv_slot(),
            device_id=to(), device_id_type=MESH,
        )

    def start(self, *numbers):
        for number in numbers:
            self.get(number).start()

    def arrive(self, *numbers):
        for number in numbers:
            self.get(number).wait_recv()

    def leave(self, *numbers):
        for number in numbers:
            only = self.made[number][4]
            if number not in self.sent and only is None:
                self.get(number).wait_send()
            elif number not in self.sent:
                pl.when(only())(lambda number=number: self.get(number).wait_send())
            self.sent.add(number)


def fused_fits(plan):
    depth = plan.n // 4
    blocks = 11 * depth + depth - 1
    half = plan.slot // 2
    plain = [b + plan.slot <= A_ROWS for b, h, v in zip(plan.a_base, plan.h_rows, plan.v_rows) if not (h or v)]
    vectors = [rows for rows in plan.v_rows if rows]
    return (
        all(plain)
        and vectors == [3 * (BLOCKS + 1)]
        and plan.n % 4 == 0
        and half >= 32
        and 2 * depth * plan.slot <= (BLOCKS + 1) * D
        and -(-blocks // 4) * half <= BLOCKS * (D + 16)
        and max(plan.a_rows) <= plan.slot
    )


def train_kernel(
    plan, x_ref, ints_ref, imp_ref, pmv_ref, st_out, ig_out, flat_out, low_out, norm_out,
    w, wh, vec, both, rw, eye, wct, wt, wht, vt, gsb, xt, mix, xh, gp, rstd, stream, ex, br, dm, acc, lg, dl,
    gw, gh, gv, packed, st_stage, slot128, flat, rolled, scratch, vsum, vacc, vin, partial, final, squares, sq_z, sq_y, sq_x,
    send, recv, z_recv, local, ready,
):
    n, rows = plan.n, plan.slot
    depth, hrows = n // 4, plan.slot // 2
    cut = hrows // 32 * 16
    core, me, near_x, near_y = neighbours(n)
    near_xy = near_x + near_y - me
    width = both.shape[2]
    height = pmv_ref.shape[0] // 3
    p_ref, m_ref, v_ref = (pmv_ref.at[i * height : (i + 1) * height] for i in range(3))
    first_out, second_out, new_out = (flat_out.at[i * height : (i + 1) * height] for i in range(3))
    z_me, j_me = me // 4, me % 4
    copies = Copies(send, recv)
    barrier = greet(core, me, near_x, near_y, n)
    mine = pl.multiple_of(core * width, width)
    theirs = pl.multiple_of((1 - core) * width, width)
    x_copy = pltpu.make_async_copy(x_ref.at[pl.ds(mine, width)], st_stage.at[0], local.at[0])
    x_copy.start()
    place_shard(plan, me, p_ref, slot128, flat, rolled)

    spare = (BLOCKS + 1) * D

    def slot_part(t, i, lo, count):
        row = pl.multiple_of(spare + rows * (t * depth + i // 4) + lo, 16)
        return xh.at[pl.ds(row, count), pl.ds(pl.multiple_of((i % 4) * D, D), D)]

    def column(index, k):
        return (index + n - 4 * k) % n

    def sibling():
        return at(1 - core, me)

    def same(make, to):
        return copies.add(make, make, to)

    low = core * hrows
    other_low = (1 - core) * hrows
    swap_first = same(lambda: slot_part(core, me, other_low, hrows), sibling)
    swap_second = same(lambda: slot_part(core, me, low, hrows), sibling)
    swap_ints = copies.add(lambda: ints_ref.at[:, pl.ds(theirs, width)], lambda: both.at[core], sibling)
    order = [0] + sorted(range(1, depth), key=lambda k: (min(k, depth - k), k))
    to_x, to_y = (lambda: at(core, near_x)), (lambda: at(core, near_y))
    gathers = []
    for t in range(2):
        g = {"z": {}, "x": {}, "y": {}, "d": {}, "s": []}
        for k in order:
            if k:
                g["z"][k] = same(lambda t=t: slot_part(t, me, low, hrows), lambda k=k: at(core, (me + 4 * k) % n))
            g["x"][k] = same(lambda t=t, k=k: slot_part(t, column(me, k), low, hrows), to_x)
            g["y"][k] = same(lambda t=t, k=k: slot_part(t, column(me, k), low, hrows), to_y)
            g["d"][k] = (
                same(lambda t=t, k=k: slot_part(t, column(near_x, k), low, cut), to_y),
                same(lambda t=t, k=k: slot_part(t, column(near_y, k), low + cut, hrows - cut), to_x),
            )
            g["s", k] = [
                same(lambda t=t, k=k, index=index: slot_part(t, column(index, k), low, hrows), sibling) if index is not me or k else None
                for index in (me, near_x, near_y, near_xy)
            ]
        gathers.append(g)

    def gather_0(t):
        g = gathers[t]
        copies.start(*g["z"].values())
        copies.start(g["x"][0], g["y"][0])

    def gather_1(t):
        g = gathers[t]
        for k in order[1:]:
            copies.arrive(g["z"][k])
            copies.start(g["x"][k], g["y"][k], g["s", k][0])

    def gather_2(t):
        g = gathers[t]
        for k in order:
            copies.arrive(g["x"][k])
            copies.start(g["d"][k][0], g["s", k][1])
            copies.arrive(g["y"][k])
            copies.start(g["d"][k][1], g["s", k][2])

    def gather_3(t):
        g = gathers[t]
        for k in order:
            copies.arrive(*g["d"][k])
            copies.start(g["s", k][3])

    def gather_4(t):
        g = gathers[t]
        for k in order:
            copies.arrive(*(c for c in g["s", k] if c is not None))

    def unpack(t):
        lg[4 * D : 5 * D, 128:D] = jnp.zeros((D, 128), F32)
        vsum[...] = jnp.zeros(vsum.shape, F32)
        for i in range(n):
            row, lane = spare + rows * (t * depth + i // 4), (i % 4) * D
            unpack_rows(plan, i, xh[row : row + rows, lane : lane + D], w.at[t], lg, vsum, scratch)
        for j in range(5):
            wh[t, :, D * j : D * j + D] = lg[D * j : D * j + D].astype(BF)
        vec[t] = vsum[...].astype(BF)

    total = jnp.sum(imp_ref[...].astype(F32), axis=1, keepdims=True)
    lane_d = lax.broadcasted_iota(jnp.int32, (1, D), 1)
    hi, mid, lo = split3(total)
    left = slot128[pl.ds(0, rows, stride=2)]
    right = slot128[pl.ds(1, rows, stride=2)]
    own = jnp.concatenate([left, right], 1)
    last = jnp.where(lane_d == 0, hi, jnp.where(lane_d == 1, mid, jnp.where(lane_d == 2, lo, 0.0)))
    last_row = lax.broadcasted_iota(jnp.int32, (rows, D), 0) == rows - 1
    slot_part(core, me, 0, rows)[...] = jnp.where(last_row, last, own).astype(BF)
    pl.semaphore_wait(barrier, depth + 2)
    copies.start(swap_first, swap_second, swap_ints)
    eye[...] = identity(D)
    x_copy.wait()
    for c in range(0, width, CB):
        xt[0, 0:D, c : c + CB] = nt(eye[...], st_stage[0, c : c + CB, :]).astype(BF)
    both[core] = ints_ref[:, pl.ds(mine, width)]
    copies.arrive(swap_first)
    gather_0(0)
    gather_1(0)
    gather_2(0)
    gather_3(0)
    gather_0(1)
    copies.arrive(swap_second, swap_ints)
    gather_4(0)
    unpack(0)
    total = jnp.zeros((1, D), F32)
    for i in range(n):
        row, lane = spare + rows * (i // 4), (i % 4) * D
        total = total + xh[row + rows - 16 : row + rows, lane : lane + D].astype(F32)[15:16]
    weight_sum = jnp.sum(jnp.where(lane_d < 3, total, 0.0), axis=1, keepdims=True)
    rw[...] = jnp.broadcast_to(imp_ref[:, pl.ds(mine, width)].astype(F32) / weight_sum, (8, width))

    fwd = (eye, w, wh, vec, wct, wt, vt, gsb, xt, mix, xh, gp, rstd, stream, both, width)

    def during_forward(k):
        pl.when(k == 2)(lambda: gather_1(1))
        pl.when(k == 5)(lambda: gather_2(1))
        pl.when(k == 8)(lambda: gather_3(1))

    def emit_states(t):
        for c in range(0, width, CB):
            st_stage[t, c : c + CB, :] = nt(eye[...], xt[t + 1, 0:D, c : c + CB]).astype(BF)

    forward_tower(0, fwd, during_forward)
    gather_4(1)
    copies.leave(*range(len(copies.made)))
    unpack(1)
    forward_tower(1, fwd, None)
    emit_states(0)
    emit_states(1)
    out_rows = pl.ds(mine, width)
    st_copy = copies.add(lambda: st_stage.at[1 - core], lambda: st_out.at[out_rows], sibling)
    copies.start(st_copy)
    st_stay = pltpu.make_async_copy(st_stage.at[core], st_out.at[out_rows], local.at[1])
    st_stay.start()

    packed_of = [i for i in range(n) if plan.h_rows[i] or plan.v_rows[i]]
    owner = plan.v_rows.index(3 * (BLOCKS + 1))

    def block(t, q):
        arena, first = (xh, spare) if t == 0 else (mix, BLOCKS * (D + 16))
        row = pl.multiple_of(first + hrows * (q // 4), 16)
        return arena.at[pl.ds(row, hrows), pl.ds(pl.multiple_of((q % 4) * D, D), D)]

    def piece(t, q, lo, count):
        arena, first = (xh, spare) if t == 0 else (mix, BLOCKS * (D + 16))
        row = pl.multiple_of(first + hrows * (q // 4) + lo, 16)
        return arena.at[pl.ds(row, count), pl.ds(pl.multiple_of((q % 4) * D, D), D)]

    def slot_half(t, i, lo):
        if i in packed_of:
            return packed.at[t, packed_of.index(i), pl.ds(pl.multiple_of(lo, 16), hrows)]
        return gw.at[t, pl.ds(pl.multiple_of(plan.a_base[i] + lo, 16), hrows)]

    j_x, j_y, j_d = near_x % 4, near_y % 4, near_xy % 4
    jobs = {}
    for t in range(2):
        for zz in range(depth):
            q = 11 * zz
            job = {"q": q}
            job["swap"] = [
                copies.add(lambda t=t, i=4 * zz + j: slot_half(t, i, other_low), lambda t=t, q=q + j: block(t, q), sibling)
                for j in range(4)
            ]
            job["d"] = (
                copies.add(lambda t=t, q=q: piece(t, q + 4 + j_d, 0, cut), lambda t=t, q=q: piece(t, q + 8, 0, cut), to_y),
                copies.add(lambda t=t, q=q: piece(t, q + 4 + j_d, cut, hrows - cut), lambda t=t, q=q: piece(t, q + 8, cut, hrows - cut), to_x),
            )
            job["x"] = copies.add(lambda t=t, q=q: block(t, q + 4 + j_x), lambda t=t, q=q: block(t, q + 9), to_x)
            job["y"] = copies.add(lambda t=t, q=q: block(t, q + 4 + j_y), lambda t=t, q=q: block(t, q + 10), to_y)
            job["z"] = copies.add(
                lambda t=t, q=q: block(t, q + 4 + j_me),
                lambda t=t, zz=zz: block(t, 11 * depth + (zz + depth - z_me) % depth - 1),
                lambda zz=zz: at(core, 4 * zz + j_me),
                lambda t=t, zz=zz: z_recv.at[t * depth + (zz + depth - z_me) % depth],
                lambda zz=zz: z_me != zz,
            )
            jobs[t, zz] = job

    def pack(t, planes):
        wanted = [i for i in packed_of if i // 4 in planes]
        for i in wanted:
            a_rows, h_rows, h_off, h_first = plan.a_rows[i], plan.h_rows[i], plan.h_off[i], plan.h_first[i]
            to = packed.at[t, packed_of.index(i)]
            scratch[...] = jnp.zeros(scratch.shape, F32)
            lo16, hi16 = h_first // 16 * 16, -(-(h_first + h_rows) // 16) * 16
            for half in range(2):
                for j in range(5 if h_rows else 0):
                    cols = slice(D * j + 128 * half, D * j + 128 * half + 128)
                    value = gh[t, lo16:hi16, cols].astype(F32)[h_first - lo16 : h_first - lo16 + h_rows]
                    scratch[half, pl.ds(h_off + j, h_rows, stride=5)] = value
            whole = jnp.concatenate([scratch[0], scratch[1]], 1)
            to[a_rows:rows] = whole[a_rows:].astype(BF)
            if a_rows:
                to[0:a_rows] = gw[t, plan.a_base[i] : plan.a_base[i] + a_rows]

    def plus(*refs):
        value = refs[0][...].astype(F32)
        for ref in refs[1:]:
            value = value + ref[...].astype(F32)
        return value

    def sum_0(t, zz):
        copies.start(*jobs[t, zz]["swap"])

    def sum_1(t, zz):
        job = jobs[t, zz]
        for j in range(4):
            copies.arrive(job["swap"][j])
            block(t, job["q"] + 4 + j)[...] = plus(slot_half(t, 4 * zz + j, low), block(t, job["q"] + j)).astype(BF)
        copies.start(*job["d"])

    def sum_2(t, zz):
        job = jobs[t, zz]
        q = job["q"]
        copies.arrive(job["d"][0])
        target = piece(t, q + 4 + j_x, 0, cut)
        target[...] = plus(target, piece(t, q + 8, 0, cut)).astype(BF)
        copies.start(job["x"])
        copies.arrive(job["d"][1])
        target = piece(t, q + 4 + j_y, cut, hrows - cut)
        target[...] = plus(target, piece(t, q + 8, cut, hrows - cut)).astype(BF)
        copies.start(job["y"])

    def sum_3(t, zz):
        job = jobs[t, zz]
        q = job["q"]
        copies.arrive(job["x"], job["y"])
        value = plus(block(t, q + 4 + j_me), block(t, q + 9), block(t, q + 10))

        @pl.when(z_me == zz)
        def _():
            partial[t] = value

        @pl.when(z_me != zz)
        def _():
            block(t, q + 4 + j_me)[...] = value.astype(BF)
            copies.start(job["z"])

    def sum_4(t):
        for k in range(1, depth):
            src = block(t, 11 * depth + k - 1)
            pltpu.make_async_remote_copy(
                src_ref=src, dst_ref=src, send_sem=send.at[0], recv_sem=z_recv.at[t * depth + k], device_id=sibling(), device_id_type=MESH
            ).wait_recv()
            partial[t] = partial[t] + src[...].astype(F32)

    def vector_step(step):
        sources = [gv.at[1 - core], vacc.at[0], vacc.at[1], vacc.at[2]]
        targets = [[sibling], [to_x], [to_y], [lambda k=k: at(core, (me + 4 * k) % n) for k in range(1, depth)]]
        if step:
            base = gv[core] if step == 1 else vacc[step - 2]
            for number, k in vector_copies[-1]:
                copies.arrive(number)
                base = base + vin[k]
            vacc[step - 1] = base
        if step < 4:
            slots = range(step, step + 1) if step < 3 else range(3, 2 + depth)
            started = []
            for k, to in zip(slots, targets[step]):
                number = copies.add(lambda step=step: sources[step], lambda k=k: vin.at[k], to)
                copies.start(number)
                started.append((number, k))
            vector_copies.append(started)

    vector_copies = []
    last_swap = copies.add(lambda: partial.at[1 - core], lambda: final.at[core], sibling)
    peers = [(1 - core, me), (core, near_x), (core, near_y)] + [(core, (me + 4 * k) % n) for k in range(1, depth)]

    bwd = (eye, w, wh, vec, wht, vt, gsb, xt, mix, xh, gp, rstd, stream, ex, br, dm, acc, lg, dl, both, rw, gw, gh, gv, dm, width)
    ig_copies = [copies.add(lambda: dm, lambda: ig_out.at[out_rows], sibling, None, lambda t=t: core != t) for t in range(2)]

    def ig_local():
        return pltpu.make_async_copy(dm, ig_out.at[out_rows], local.at[2])

    def emit_inputs(t):
        pl.when(core == t)(lambda: ig_local().start())
        pl.when(core != t)(lambda: copies.start(ig_copies[t]))

    def free_inputs(t):
        pl.when(core == t)(lambda: ig_local().wait())
        pl.when(core != t)(lambda: copies.get(ig_copies[t]).wait_send())

    ex[...] = jnp.zeros_like(ex)
    backward_tower(1, bwd, None, None)
    emit_inputs(1)
    for to_core, to_index in peers:
        pl.semaphore_signal(ready, inc=1, device_id=at(to_core, to_index), device_id_type=MESH)

    def after_head():
        pl.semaphore_wait(ready, len(peers))
        pack(1, range(depth))
        for zz in range(depth):
            sum_0(1, zz)
        pack(0, (depth - 1,))
        sum_0(0, depth - 1)

    def during_backward(i):
        def at_step(step, *calls):
            def run():
                for f, *args in calls:
                    f(*args)

            pl.when(i == step)(run)

        planes = range(depth)
        at_step(1, *((sum_1, 1, zz) for zz in planes), (sum_1, 0, depth - 1))
        at_step(3, *((sum_2, 1, zz) for zz in planes), (sum_2, 0, depth - 1))
        for zz in range(1, depth - 1):
            done = BLOCKS + 1 - 4 * zz + 1
            if done < BLOCKS:
                at_step(done, (pack, 0, (zz,)), (sum_0, 0, zz))
            if done + 1 < BLOCKS:
                at_step(done + 1, (sum_1, 0, zz))
            if done + 2 < BLOCKS:
                at_step(done + 2, (sum_2, 0, zz))
        at_step(5, *((sum_3, 1, zz) for zz in planes), (sum_3, 0, depth - 1))
        at_step(8, (sum_4, 1))

    backward_tower(0, bwd, after_head, during_backward, lambda: free_inputs(1))
    emit_inputs(0)
    done = {zz: BLOCKS + 1 - 4 * zz + 1 for zz in range(1, depth - 1)}
    for zz in sorted(done, reverse=True):
        if done[zz] >= BLOCKS:
            pack(0, (zz,))
            sum_0(0, zz)
    pack(0, (0,))
    sum_0(0, 0)
    vector_step(0)
    for zz in sorted(done, reverse=True):
        if done[zz] + 1 >= BLOCKS:
            sum_1(0, zz)
        if done[zz] + 2 >= BLOCKS:
            sum_2(0, zz)
    sum_1(0, 0)
    vector_step(1)
    for zz in sorted(done, reverse=True):
        sum_3(0, zz)
    sum_2(0, 0)
    vector_step(2)
    sum_3(0, 0)
    vector_step(3)
    sum_4(0)
    copies.start(last_swap)
    final[core] = partial[core]
    vector_step(4)
    copies.arrive(last_swap)

    slot128[...] = jnp.zeros(slot128.shape, F32)
    for h in range(2):
        slot128[pl.ds(2 * hrows * h, hrows, stride=2)] = final[h, :, 0:128]
        slot128[pl.ds(2 * hrows * h + 1, hrows, stride=2)] = final[h, :, 128:D]

    @pl.when(me == owner)
    def _():
        for kind in range(3):
            first = 2 * (plan.v_off[owner] + kind * (BLOCKS + 1))
            for h in range(2):
                value = vacc[3, kind, 0 : BLOCKS + 1, 128 * h : 128 * h + 128]
                slot128[pl.ds(first + h, BLOCKS + 1, stride=2)] = value

    def push(src, dst, to):
        number = copies.add(lambda: src, lambda: dst, lambda: to)
        copies.start(number)
        return copies.get(number)

    lay_flat(plan, me, slot128, flat, rolled)
    update_shard(
        plan, me, p_ref, m_ref, v_ref, (first_out, second_out, new_out, low_out, norm_out),
        flat, squares, sq_z, sq_y, sq_x, push, [at(core, (me + 4 * k) % n) for k in range(1, depth)], to_y(), to_x(),
    )
    copies.arrive(st_copy)
    pl.when(core == 0)(lambda: copies.arrive(ig_copies[0]))
    pl.when(core == 1)(lambda: copies.arrive(ig_copies[1]))
    free_inputs(0)
    st_stay.wait()
    copies.sent.update(ig_copies)
    copies.leave(*range(len(copies.made)))


def train(plan, latent, ints, imp, pmv):
    n, rows = plan.n, plan.slot
    depth, hrows = n // 4, rows // 2
    width = ints.shape[1] // 2
    height = pmv.shape[0] // 3
    vm = pl.BlockSpec(memory_space=pltpu.VMEM)
    hbm = pl.BlockSpec(memory_space=pl.ANY)
    packed = sum(1 for h, v in zip(plan.h_rows, plan.v_rows) if h or v)
    return pl.pallas_call(
        functools.partial(train_kernel, plan),
        out_shape=(
            jax.ShapeDtypeStruct((2 * width, D), BF),
            jax.ShapeDtypeStruct((2 * width, D), F32),
            jax.ShapeDtypeStruct((3 * height, 128), F32),
            jax.ShapeDtypeStruct((height, 128), BF),
            jax.ShapeDtypeStruct((32, 128), F32),
        ),
        in_specs=[hbm] + [vm] * 3,
        out_specs=(hbm, hbm, vm, vm, vm),
        scratch_shapes=[
            pltpu.VMEM((2, A_ROWS, D), BF),
            pltpu.VMEM((2, D, HPAD), BF),
            pltpu.VMEM((2, 128, D), BF),
            pltpu.VMEM((2, 8, width), jnp.int32),
            pltpu.VMEM((8, width), F32),
            *work_scratch(width),
            pltpu.VMEM((2, A_ROWS, D), BF),
            pltpu.VMEM((2, D, HPAD), BF),
            pltpu.VMEM((2, 3, 16, D), F32),
            pltpu.VMEM((2, packed, rows, D), BF),
            pltpu.VMEM((2, width, D), BF),
            pltpu.VMEM((max(2 * rows, height + 48) + 80, 128), F32),
            pltpu.VMEM((height + 128, 128), F32),
            pltpu.VMEM((height + 16, 128), F32),
            pltpu.VMEM((2, rows, 128), F32),
            pltpu.VMEM((128, D), F32),
            pltpu.VMEM((4, 3, 16, D), F32),
            pltpu.VMEM((2 + depth, 3, 16, D), F32),
            pltpu.VMEM((2, hrows, D), F32),
            pltpu.VMEM((2, hrows, D), F32),
            pltpu.VMEM((3, 32, 128), F32),
            pltpu.VMEM((depth, 32, 128), F32),
            pltpu.VMEM((32, 128), F32),
            pltpu.VMEM((32, 128), F32),
            pltpu.SemaphoreType.DMA((11 * n,)),
            pltpu.SemaphoreType.DMA((11 * n,)),
            pltpu.SemaphoreType.DMA((2 * depth,)),
            pltpu.SemaphoreType.DMA((3,)),
            pltpu.SemaphoreType.REGULAR,
        ],
        compiler_params=pltpu.CompilerParams(
            collective_id=2, has_side_effects=True, vmem_limit_bytes=63 * 1024 * 1024
        ),
    )(latent, ints, imp, pmv)


def on_device(latent, codes, targets, visits, importance, params, first_moment, second_moment):
    me = lax.axis_index("tower")
    row_count = latent.shape[0]
    half = row_count // 2
    shard_len = params.shape[1]
    plan = Plan(lax.axis_size("dp"), shard_len)
    height = -(-plan.rows128 // 8) * 8
    size = 128 * height
    spread_out = [
        jnp.pad(v, ((0, 0), (i * size, (3 - i) * size - shard_len))) for i, v in enumerate((params, first_moment, second_moment))
    ]
    pmv = (spread_out[0] + spread_out[1] + spread_out[2]).reshape(3 * height, 128)
    ints = jnp.concatenate([codes, targets[0, :1], visits[0].T, targets[0, 1:]], 0)
    if fused_fits(plan):
        states_out, inputs_out, flat, low, norm = train(plan, latent, ints, importance[None], pmv)
    else:
        x = lax.dynamic_slice_in_dim(latent, me * half, half, 0)
        p128, m128, v128 = (pmv[i * height : (i + 1) * height] for i in range(3))
        w, wh, vec, both, rw = gather(plan, p128, ints, importance[None])
        st, ig, gw, gh, gv = compute(x, both, rw, w, wh, vec)
        states_out, inputs_out, *flat, low, norm = reduce_and_update(plan, gw, gh, gv, st, ig, p128, m128, v128)
        flat = jnp.concatenate(flat)
    flat = flat.reshape(1, -1)
    first, second, new = (flat[:, i * 128 * height : i * 128 * height + shard_len] for i in range(3))
    norms = jnp.stack([norm[:MATS, 0], norm[16 : 16 + MATS, 0]])[None]
    return (states_out[None], inputs_out[None], first, second, new, low.reshape(1, -1)[:, :shard_len], norms)


def solution(mesh):
    in_specs = (
        P("dp", None),
        P("tower", "dp"),
        P("tower", None, "dp"),
        P("tower", "dp", None),
        P("dp"),
        P("tower", "dp"),
        P("tower", "dp"),
        P("tower", "dp"),
    )
    out_specs = (
        P("tower", "dp", None),
        P("tower", "dp", None),
        P("tower", "dp"),
        P("tower", "dp"),
        P("tower", "dp"),
        P("tower", "dp"),
        P("tower", None, None),
    )
    return jax.shard_map(
        on_device, mesh=mesh, in_specs=in_specs, out_specs=out_specs, check_vma=False
    )
```

```python
import functools

import jax
import jax.numpy as jnp
from jax import lax
from jax.experimental import pallas as pl
from jax.experimental.pallas import tpu as pltpu
from jax.sharding import PartitionSpec as P

D = 256
CODES = 32
BINS = 601
BLOCKS = 10
STEP = 5
HEADS = 1238
MATS = 12
P_SIZE = 1054464
HPAD = 1280
CAT = D + CODES
A_ROWS = CAT + BLOCKS * D
BF = jnp.bfloat16
F32 = jnp.float32
GELU_C = 0.7978845608028654
GELU_K = 0.044715


def nn(a, b):
    return jnp.dot(a, b, preferred_element_type=F32)


def nt(a, b):
    return lax.dot_general(a, b, (((1,), (1,)), ((), ())), preferred_element_type=F32)


def identity(n):
    return (lax.broadcasted_iota(jnp.int32, (n, n), 0) == lax.broadcasted_iota(jnp.int32, (n, n), 1)).astype(BF)


ZETA = (GELU_C * GELU_K) ** (1.0 / 3.0)
B0 = GELU_C / ZETA
E0 = 0.5 / ZETA


def wide(v, cs):
    return jnp.concatenate([v] * ((cs.stop - cs.start) // v.shape[1]), 1)


def norm_act(src, cs, gs, unit, gp, rstd, out):
    for r in range(0, D, 32):
        rs = slice(r, r + 32)
        xh = src[rs, cs] * rstd
        unit[rs, cs] = xh.astype(BF)
        z = xh * wide(gs[rs, 0:128], cs) + wide(gs[rs, 128:256], cs)
        z2 = z * z
        t = jnp.tanh(z * (z2 + B0))
        q = t * E0 + E0
        a = z * q
        out(rs, a)
        gp[rs, cs] = (q + (a * (1.0 - t)) * (z2 * 3.0 + B0)).astype(BF)


def broadcast_vectors(vt, rows):
    k = lax.broadcasted_iota(jnp.int32, (128, 128), 0)
    picks = jnp.concatenate([(k == row).astype(BF) for row in rows], 1)
    return nn(vt, picks)


def head_stage(cs, lg, dl, ints, rw):
    width = rw.shape[1]
    it8 = lax.broadcasted_iota(jnp.int32, (8, width), 0)
    low = -jnp.inf
    b75, b150, b154 = lg[600:608], lg[1200:1208], lg[1232:1240]

    def top(block):
        return jnp.max(block, axis=0, keepdims=True)

    def top_range(lo, hi):
        best = lg[lo : lo + 8]
        for r in range(lo + 8, hi, 8):
            best = jnp.maximum(best, lg[r : r + 8])
        return best

    max_v = top(jnp.maximum(top_range(0, 600), jnp.where(it8 < 1, b75, low)))
    max_r = top(
        jnp.maximum(
            jnp.maximum(top_range(608, 1200), jnp.where(it8 >= 1, b75, low)),
            jnp.where(it8 < 2, b150, low),
        )
    )
    max_c = top(
        jnp.maximum(
            jnp.maximum(top_range(1208, 1232), jnp.where(it8 >= 2, b150, low)),
            jnp.where(it8 < 2, b154, low),
        )
    )
    in_policy = (it8 >= 2) & (it8 < 6)
    max_p = top(jnp.where(in_policy, b154, low))

    def exp_range(lo, hi, best):
        acc = jnp.zeros((8, width), F32)
        for r in range(lo, hi, 8):
            e = jnp.exp(lg[r : r + 8] - best)
            lg[r : r + 8] = e
            acc = acc + e
        return acc

    e75 = jnp.exp(b75 - jnp.where(it8 < 1, max_v, max_r))
    e150 = jnp.exp(b150 - jnp.where(it8 < 2, max_r, max_c))
    e154 = jnp.exp(b154 - jnp.where(it8 < 2, max_c, max_p))

    def total(acc):
        return rw / jnp.sum(acc, axis=0, keepdims=True)

    inv_v = total(exp_range(0, 600, max_v) + jnp.where(it8 < 1, e75, 0.0))
    inv_r = total(exp_range(608, 1200, max_r) + jnp.where(it8 >= 1, e75, 0.0) + jnp.where(it8 < 2, e150, 0.0))
    inv_c = total(exp_range(1208, 1232, max_c) + jnp.where(it8 >= 2, e150, 0.0) + jnp.where(it8 < 2, e154, 0.0))
    inv_p = total(jnp.where(in_policy, e154, 0.0))
    hit_v = ints[1:2]
    hit_r = ints[6:7] + BINS
    hit_c = ints[7:8] + 2 * BINS
    counts = jnp.where(in_policy, ints.astype(F32), 0.0)
    share = counts * (rw / jnp.sum(counts, axis=0, keepdims=True))

    def minus(value, lo, *hits):
        at = lax.broadcasted_iota(jnp.int32, value.shape, 0)
        for hit in hits:
            value = value - jnp.where(at == hit - lo, rw, 0.0)
        return value

    d75 = minus(e75 * jnp.where(it8 < 1, inv_v, inv_r), 600, hit_v, hit_r)
    d150 = minus(e150 * jnp.where(it8 < 2, inv_r, inv_c), 1200, hit_r, hit_c)
    d154 = minus(e154 * jnp.where(it8 < 2, inv_c, inv_p), 1232, hit_c) - share
    d154 = jnp.where(it8 < 6, d154, 0.0)

    def emit(lo, hi, inv, hit):
        for r in range(lo, hi, 16):
            dl[r : r + 16, cs] = minus(lg[r : r + 16] * inv, r, hit).astype(BF)

    def pair(first, second):
        return jnp.concatenate([first, second], 0).astype(BF)

    emit(0, 592, inv_v, hit_v)
    dl[592:608, cs] = pair(minus(lg[592:600] * inv_v, 592, hit_v), d75)
    emit(608, 1200, inv_r, hit_r)
    dl[1200:1216, cs] = pair(d150, minus(lg[1208:1216] * inv_c, 1208, hit_c))
    emit(1216, 1232, inv_c, hit_c)
    dl[1232:1248, cs] = pair(d154, jnp.zeros_like(d154))
    dl[1248:HPAD, cs] = jnp.zeros((HPAD - 1248, width), BF)


CB = 256
GROUP = 2


def saved_views(t, mix, xh):
    def mixed(k):
        return mix.at[pl.ds(pl.multiple_of((t * BLOCKS + k - 1) * (D + 16), 16), D + 16)]

    def unit(k):
        return xh.at[pl.ds(pl.multiple_of((t * (BLOCKS + 1) + k) * D, D), D)]

    return mixed, unit


def column_groups(width):
    blocks = [slice(c, c + CB) for c in range(0, width, CB)]
    per = min(GROUP, len(blocks))
    return blocks, per, [slice(c, c + per * CB) for c in range(0, width, per * CB)]


def forward_tower(t, refs, during=None):
    (eye, w, wh, vec, wt, vt, gsb, xt, mix, xh, gp, rstd, stream, mean, ints, width) = refs
    blocks, per, groups = column_groups(width)
    mixed, unit = saved_views(t, mix, xh)
    first_bias = 2 * (BLOCKS + 1)
    ones = jnp.ones((16, D), BF)

    def mean_rows(slot):
        value = nn(ones, wt[slot, 0:D])[0:8] * (1.0 / D)
        high = value.astype(BF).astype(F32)
        wt[slot, D : D + 16] = jnp.concatenate([high, value - high], 0).astype(BF)

    def vectors(k):
        gsb[k % 2] = broadcast_vectors(vt[...], (k, k + BLOCKS + 1)) * ZETA

    def prefetch(k):
        vectors(k)
        row = pl.multiple_of(CAT + (k - 1) * D, 32)
        wt[k % 2, 0:D, 0:D] = nt(eye[...], w[t, pl.ds(row, D)]).astype(BF)
        at_row = lax.broadcasted_iota(jnp.int32, (128, 128), 0) == k + first_bias
        at_lane = lax.broadcasted_iota(jnp.int32, (128, 128), 1) == 0
        wt[k % 2, 0:D, D:384] = nn(vt[...], (at_row & at_lane).astype(BF)).astype(BF)
        mean_rows(k % 2)

    def row_of(k):
        return pl.ds(t * (BLOCKS + 1) + k, 1)

    def stage(k, c):
        def keep(rs, a):
            mixed(k)[rs, blocks[c]] = a.astype(BF)

        norm_act(stream, blocks[c], gsb.at[k % 2], unit(k), gp.at[t, k], rstd[row_of(k), blocks[c]], keep)

    def spread(square, k, cs):
        var = jnp.sum(square, axis=0, keepdims=True) * (1.0 / D)
        rstd[row_of(k), cs] = lax.rsqrt(var + 1e-05)

    def add(k, cs, out, fresh):
        shift = out[D : D + 1] + out[D + 8 : D + 9]
        square = jnp.zeros((8, out.shape[1]), F32)
        for r in range(0, D, 16):
            value = out[r : r + 16] - shift
            if not fresh:
                value = stream[r : r + 16, cs] + value
            stream[r : r + 16, cs] = value
            square = square + (value[0:8] * value[0:8] + value[8:16] * value[8:16])
        if not fresh:
            mean[0:1, cs] = mean[0:1, cs] + shift
        spread(square, k + 1, cs)

    def centre(cs):
        total = jnp.zeros((8, CB), F32)
        for r in range(0, D, 8):
            total = total + stream[r : r + 8, cs]
        middle = jnp.sum(total, axis=0, keepdims=True) * (1.0 / D)
        mean[0:1, cs] = middle
        square = jnp.zeros((8, CB), F32)
        for r in range(0, D, 8):
            value = stream[r : r + 8, cs] - middle
            stream[r : r + 8, cs] = value
            square = square + value * value
        spread(square, 1, cs)

    vt[...] = nt(eye[...], vec[t]).astype(BF)
    vectors(0)
    wt[0, 0:D, 0:D] = nt(eye[...], w[t, 0:D]).astype(BF)
    tile = first_bias // 16 * 16
    picked = lax.broadcasted_iota(jnp.int32, (16, D), 0) == first_bias - tile
    bias = jnp.where(picked, vec[t, tile : tile + 16].astype(F32), 0.0).astype(BF)
    rest = jnp.concatenate([w[t, D:CAT], bias, jnp.zeros((128 - CODES - 16, D), BF)], 0)
    wt[0, 0:D, D:384] = nt(eye[...], rest).astype(BF)
    mean_rows(0)
    for cs in blocks:
        it = lax.broadcasted_iota(jnp.int32, (CODES, CB), 0)
        xt[t, D:CAT, cs] = (it == ints[t, 0:1, cs]).astype(BF)
        xt[t, CAT : CAT + 16, cs] = jnp.ones((16, CB), BF)
    first = [nn(wt[0, :, 0 : CAT + 16], xt[t, :, cs]) for cs in groups]
    prefetch(1)
    for group, cs in enumerate(groups):
        add(-1, cs, first[group], True)
    for cs in blocks:

        def keep(rs, a):
            stream[rs, cs] = a

        norm_act(stream, cs, gsb.at[0], unit(0), gp.at[t, 0], rstd[row_of(0), cs], keep)
        centre(cs)

    def layer(k, more):
        if more:
            prefetch(k + 1)
        mixed(k)[D : D + 16, :] = jnp.ones((16, width), BF)
        for group, cs in enumerate(groups):
            out = nn(wt[k % 2, :, 0 : D + 16], mixed(k)[:, cs])
            ahead = group + 1 < len(groups)
            if ahead or more:
                for c in range(per):
                    stage(k if ahead else k + 1, (group + 1) % len(groups) * per + c)
            add(k, cs, out, False)

    for c in range(per):
        stage(1, c)

    @pl.loop(1, BLOCKS)
    def _(k):
        if during is not None:
            during(k)
        layer(k, True)

    layer(BLOCKS, False)
    for cs in blocks:
        xt[t + 1, 0:D, cs] = (stream[:, cs] + mean[0:1, cs]).astype(BF)


def backward_tower(t, refs, after_head=None, during=None, before_product=None):
    (eye, w, wh, vec, wht, vt, gsb, xt, mix, xh, gp, rstd, ds, ex, br, dm, d2, lg, dl, ints, rw, gw, gh, gv, ig, width) = refs
    blocks, per, groups = column_groups(width)
    mixed, unit = saved_views(t, mix, xh)
    vt[...] = nt(eye[...], vec[t]).astype(BF)
    for h in range(0, HPAD, D):
        wht[h : h + D, :] = nt(eye[...], wh[t, :, h : h + D]).astype(BF)

    @pl.loop(0, width // CB)
    def _(c):
        cs = pl.ds(pl.multiple_of(c * CB, CB), CB)
        lg[...] = nn(wht[...], xt[t + 1, 0:D, cs])
        head_stage(cs, lg, dl, ints[t, :, cs], rw[0:1, cs])
        value = nn(wh[t], dl[:, cs]) + ex[:, cs]
        ds[:, cs] = value
        br[BLOCKS % 2, :, cs] = value.astype(BF)

    for h in range(0, HPAD, D):
        gh[t, :, h : h + D] = nt(xt[t + 1, 0:D, :], dl[h : h + D]).astype(BF)
    if after_head is not None:
        after_head()
    ones = jnp.ones((16, width), BF)

    def part(c):
        return dm.at[c * D : c * D + D]

    def gains(k):
        gsb[k % 2, :, 0:128] = broadcast_vectors(vt[...], (k,)) * ZETA

    def row_sums(k):
        for kind in range(2):
            gv[t, kind, pl.ds(k, 1), :] = nt(ones, d2[1 - kind])[0:1] * ZETA

    def product(k, group):
        row = pl.multiple_of(CAT + (k - 1) * D, 32)
        back = nn(w[t, pl.ds(row, D)], br[k % 2, :, groups[group]])
        for c in range(per):
            part(group * per + c)[...] = back[:, c * CB : c * CB + CB]

    def slopes(k, c):
        cs, grad = blocks[c], part(c)
        for r in range(0, D, 32):
            rs = slice(r, r + 32)
            dy = grad[rs, :] * gp[t, k, rs, cs].astype(F32)
            grad[rs, :] = dy
            low = dy.astype(BF)
            d2[0, rs, cs] = low
            d2[1, rs, cs] = low * unit(k)[rs, cs]

    def sums(k, group):
        pick = (lax.broadcasted_iota(jnp.int32, (16, 128), 1) == k).astype(BF)
        gain = nt(pick, vt[...]).astype(BF)
        scale = rstd[pl.ds(t * (BLOCKS + 1) + k, 1), groups[group]] * (ZETA / D)
        return [(nn(gain, d2[i, :, groups[group]]) * scale).astype(BF) for i in range(2)]

    def inputs(k, group, means, first):
        for c in range(per):
            cs = blocks[group * per + c]
            m1, m2 = (m[:, c * CB : c * CB + CB] for m in means)
            scale = rstd[pl.ds(t * (BLOCKS + 1) + k, 1), cs]
            for r in range(0, D, 16):
                rs = slice(r, r + 16)
                less = (m1 + unit(k)[rs, cs] * m2).astype(F32)
                back = part(group * per + c)[rs, :] * wide(gsb[k % 2, rs, 0:128], cs) * scale - less
                if first:
                    br[0, rs, cs] = back.astype(BF)
                else:
                    value = ds[rs, cs] + back
                    ds[rs, cs] = value
                    br[(k + 1) % 2, rs, cs] = value.astype(BF)

    def weight_sums(k):
        full = nt(mixed(k)[...], br[k % 2])
        row = pl.multiple_of(CAT + (k - 1) * D, 32)
        gw[t, pl.ds(row, D), :] = full[0:D].astype(BF)
        gv[t, 2, pl.ds(k, 1), :] = full[D : D + 1]

    def layer(k, first):
        means = []
        for group in range(len(groups)):
            if not first and group + 1 < len(groups):
                product(k, group + 1)
            for c in range(per):
                slopes(k, group * per + c)
            means.append(sums(k, group))
        if not first:
            weight_sums(k)
        for group in range(len(groups)):
            inputs(k, group, means[group], first)
            if not first and group == 0:
                product(k - 1, 0)
        row_sums(k)

    if before_product is not None:
        before_product()
    gains(BLOCKS)
    product(BLOCKS, 0)

    @pl.loop(0, BLOCKS)
    def _(i):
        k = BLOCKS - i
        if during is not None:
            during(i)
        gains(k - 1)
        layer(k, False)

    for c, cs in enumerate(blocks):
        part(c)[...] = ds[:, cs]
    layer(0, True)
    full = nt(xt[t], br[0])
    gw[t, 0:CAT, :] = full[0:CAT].astype(BF)
    gv[t, 2, 0:1, :] = full[CAT : CAT + 1]
    for cs in blocks:
        back = nn(w[t, 0:D], br[0, :, cs])
        ex[:, cs] = back
        ig[cs, :] = back.T


def compute_kernel(x_ref, ints, rw, w, wh, vec, st, ig, gw, gh, gv, eye, wt, wht, vt, gsb, xt, mix, xh, gp, rstd, mean, stream, ex, br, dm, d2, lg, dl):
    width = x_ref.shape[0]
    eye[...] = identity(D)
    for c in range(0, width, CB):
        cs = slice(c, c + CB)
        xt[0, 0:D, cs] = nt(eye[...], x_ref[cs, :]).astype(BF)
    fwd = (eye, w, wh, vec, wt, vt, gsb, xt, mix, xh, gp, rstd, stream, mean, ints, width)
    @pl.loop(0, 2)
    def _(t):
        forward_tower(t, fwd)

        @pl.loop(0, width // CB)
        def _(c):
            cs = pl.ds(pl.multiple_of(c * CB, CB), CB)
            st[t, cs, :] = nt(eye[...], xt[t + 1, 0:D, cs]).astype(BF)

    ex[...] = jnp.zeros_like(ex)

    @pl.loop(0, 2)
    def _(i):
        t = 1 - i
        backward_tower(
            t,
            (eye, w, wh, vec, wht, vt, gsb, xt, mix, xh, gp, rstd, stream, ex, br, dm, d2, lg, dl, ints, rw, gw, gh, gv, ig.at[t], width),
        )


def work_scratch(width):
    return [
        pltpu.VMEM((D, D), BF),
        pltpu.VMEM((2, D + 16, 384), BF),
        pltpu.VMEM((HPAD, D), BF),
        pltpu.VMEM((D, 128), BF),
        pltpu.VMEM((2, D, 256), F32),
        pltpu.VMEM((3, CAT + 16, width), BF),
        pltpu.VMEM((2 * BLOCKS * (D + 16), width), BF),
        pltpu.VMEM((2 * (BLOCKS + 1) * D, width), BF),
        pltpu.VMEM((2, BLOCKS + 1, D, width), BF),
        pltpu.VMEM((24, width), F32),
        pltpu.VMEM((8, width), F32),
        pltpu.VMEM((D, width), F32),
        pltpu.VMEM((D, width), F32),
        pltpu.VMEM((2, D, width), BF),
        pltpu.VMEM((width // CB * D, CB), F32),
        pltpu.VMEM((2, D, width), BF),
        pltpu.VMEM((HPAD, CB), F32),
        pltpu.VMEM((HPAD, width), BF),
    ]


def compute(x, ints, rw, w, wh, vec):
    width = x.shape[0]
    vm = pl.BlockSpec(memory_space=pltpu.VMEM)
    return pl.pallas_call(
        compute_kernel,
        out_shape=(
            jax.ShapeDtypeStruct((2, width, D), BF),
            jax.ShapeDtypeStruct((2, width, D), F32),
            jax.ShapeDtypeStruct((2, A_ROWS, D), BF),
            jax.ShapeDtypeStruct((2, D, HPAD), BF),
            jax.ShapeDtypeStruct((2, 3, 16, D), F32),
        ),
        in_specs=[vm] * 6,
        out_specs=(vm,) * 5,
        scratch_shapes=work_scratch(width),
        compiler_params=pltpu.CompilerParams(vmem_limit_bytes=62 * 1024 * 1024),
    )(x, ints, rw, w, wh, vec)


class Plan:
    def __init__(self, n, length):
        self.n, self.length = n, length
        self.rows128 = -(-length // 128)
        block_end, head_end = A_ROWS * D, A_ROWS * D + D * HEADS
        self.a_base, self.a_rows, self.h_first, self.h_rows, self.h_off, self.v_first, self.v_rows, self.v_off = ([] for _ in range(8))
        used = 0
        for i in range(n):
            lo, hi = i * length, (i + 1) * length
            base = min(lo, block_end) // D // 16 * 16
            top = -(-min(hi, block_end) // D)
            a_rows = -(-(top - base) // 16) * 16 if lo < block_end else 0
            first = min(max(lo - block_end, 0), D * HEADS) // HEADS
            last = -(-min(max(hi - block_end, 0), D * HEADS) // HEADS)
            h_rows = last - first if hi > block_end and lo < head_end else 0
            v_first = max(lo - head_end, 0) // D
            v_rows = -(-(hi - head_end) // D) - v_first if hi > head_end else 0
            self.a_base.append(base)
            self.a_rows.append(a_rows)
            self.h_first.append(first)
            self.h_rows.append(h_rows)
            self.h_off.append(a_rows)
            self.v_first.append(v_first)
            self.v_rows.append(v_rows)
            self.v_off.append(a_rows + 5 * h_rows)
            used = max(used, a_rows + 5 * h_rows + v_rows)
        self.slot = -(-(used + 1) // 32) * 32

    def at(self, table, me):
        value = jnp.int32(table[0])
        for i in range(1, self.n):
            if table[i] != table[i - 1]:
                value = value + (me >= i).astype(jnp.int32) * (table[i] - table[i - 1])
        return value


MESH = pl.DeviceIdType.MESH


def neighbours(n):
    core = lax.axis_index("tower")
    me = lax.axis_index("dp")
    near_x = me + 1 - 2 * (me % 2)
    near_y = me + 2 - 4 * ((me // 2) % 2)
    return core, me, near_x, near_y


def at(core, index):
    return {"tower": core, "dp": index}


def greet(core, me, near_x, near_y, n):
    barrier = pltpu.get_barrier_semaphore()
    pl.semaphore_signal(barrier, inc=1, device_id=at(1 - core, me), device_id_type=MESH)
    for near in (near_x, near_y):
        pl.semaphore_signal(barrier, inc=1, device_id=at(core, near), device_id_type=MESH)
    for k in range(1, n // 4):
        pl.semaphore_signal(barrier, inc=1, device_id=at(core, (me + 4 * k) % n), device_id_type=MESH)
    return barrier


def place_shard(plan, me, p_ref, slot128, shifted, rolled):
    rows = plan.rows128
    start = me * plan.length
    shift = start % 128
    first = start // 128
    tall = shifted.shape[0]
    height = p_ref.shape[0]
    lane = lax.broadcasted_iota(jnp.int32, (height, 128), 1)
    rolled[0:8] = jnp.zeros((8, 128), F32)
    rolled[8 : 8 + height] = pltpu.roll(p_ref[...], shift, 1)
    shifted[...] = jnp.zeros((tall, 128), F32)
    moved = jnp.where(lane >= shift, rolled[8 : 8 + height], rolled[7 : 7 + height])
    shifted[16 : 16 + height] = moved
    slot128[...] = jnp.zeros(slot128.shape, F32)
    row = lax.broadcasted_iota(jnp.int32, (height, 128), 0)
    base = plan.at(plan.a_base, me)

    @pl.when(plan.at(plan.a_rows, me) > 0)
    def _():
        slot128[pl.ds(first - 2 * base, height)] = jnp.where(row + first < 2 * A_ROWS, moved, 0.0)

    h_first, h_rows, h_off = (plan.at(t, me) for t in (plan.h_first, plan.h_rows, plan.h_off))
    it = lax.broadcasted_iota(jnp.int32, (10, 128), 0)
    lane10 = lax.broadcasted_iota(jnp.int32, (10, 128), 1)

    @pl.loop(0, h_rows)
    def _(k):
        begin = A_ROWS * D + HEADS * (h_first + k) - 128 * first + 128 * 16
        turn = begin % 128
        window = pltpu.roll(shifted[pl.ds(begin // 128, 16)], (128 - turn) % 128, 1)
        value = jnp.where(lane10 < 128 - turn, window[0:10], window[1:11])
        slot128[pl.ds(2 * h_off + 10 * k, 10)] = jnp.where(it * 128 + lane10 < HEADS, value, 0.0)

    v_start = (A_ROWS * D + D * HEADS) // 128
    v_rows, v_off, v_first = (plan.at(t, me) for t in (plan.v_rows, plan.v_off, plan.v_first))
    tall_v = min(height, -(-2 * max(plan.v_rows) // 8) * 8)

    @pl.when(v_rows > 0)
    def _():
        inside = plan.at([max(0, v_start - i * plan.length // 128) for i in range(plan.n)], me)
        to = 2 * v_off + first + inside - v_start - 2 * v_first
        slot128[pl.ds(to, tall_v)] = shifted[pl.ds(16 + inside, tall_v)]


def unpack_rows(plan, i, slot, w, heads, vectors, scratch):
    base, rows = plan.a_base[i], plan.a_rows[i]
    if rows:
        shared = i > 0 and base < plan.a_base[i - 1] + plan.a_rows[i - 1]
        lo = 0
        if shared:
            w[base : base + 16] = w[base : base + 16] + slot[0:16]
            lo = 16
        if rows > lo:
            w[base + lo : base + rows] = slot[lo:rows]
    h_rows, h_off, h_first = plan.h_rows[i], plan.h_off[i], plan.h_first[i]
    v_rows, v_off, v_first = plan.v_rows[i], plan.v_off[i], plan.v_first[i]
    if h_rows or v_rows:
        value = slot.astype(F32)
        scratch[0][...] = value[:, 0:128]
        scratch[1][...] = value[:, 128:D]
    if h_rows:
        shared = i > 0 and plan.h_rows[i - 1] and plan.h_first[i - 1] + plan.h_rows[i - 1] > h_first
        for j in range(5):
            for half in range(2):
                cols = slice(128 * half, 128 * half + 128)
                first = D * j + h_first
                value = scratch[half][pl.ds(h_off + j, h_rows, stride=5)]
                if shared:
                    heads[first : first + 1, cols] = heads[first : first + 1, cols] + value[0:1]
                    if h_rows > 1:
                        heads[first + 1 : first + h_rows, cols] = value[1:h_rows]
                else:
                    heads[first : first + h_rows, cols] = value
    if v_rows:
        shared = v_first and plan.v_first[i - 1] + plan.v_rows[i - 1] > v_first
        shared = shared or (i > 0 and plan.v_rows[i - 1] > 0 and v_first == 0)
        for half in range(2):
            cols = slice(128 * half, 128 * half + 128)
            value = scratch[half][v_off : v_off + v_rows]
            if shared:
                vectors[v_first : v_first + 1, cols] = vectors[v_first : v_first + 1, cols] + value[0:1]
                if v_rows > 1:
                    vectors[v_first + 1 : v_first + v_rows, cols] = value[1:v_rows]
            else:
                vectors[v_first : v_first + v_rows, cols] = value


def split3(value):
    hi = value.astype(BF).astype(F32)
    mid = (value - hi).astype(BF).astype(F32)
    return hi, mid, value - hi - mid


def gather_kernel(plan, p_ref, ints_ref, imp_ref, w, wh, vec, both, rw, slots, slot128, shifted, rolled, scratch, whf, vecf, send, recv):
    n = plan.n
    depth = n // 4
    core, me, near_x, near_y = neighbours(n)
    barrier = greet(core, me, near_x, near_y, n)
    place_shard(plan, me, p_ref, slot128, shifted, rolled)
    pl.semaphore_wait(barrier, depth + 2)
    half = rw.shape[1]
    started = []

    def copy(src, dst, slot, to):
        c = pltpu.make_async_remote_copy(
            src_ref=src, dst_ref=dst, send_sem=send.at[slot], recv_sem=recv.at[slot], device_id=to, device_id_type=MESH
        )
        c.start()
        started.append(c)
        return c

    mine = pl.multiple_of(core * half, half)
    theirs = pl.multiple_of((1 - core) * half, half)
    number = iter(range(1 << 20))
    ints_copy = copy(ints_ref.at[:, pl.ds(theirs, half)], both.at[core], next(number), at(1 - core, me))
    rows = plan.slot
    total = jnp.sum(imp_ref[...].astype(F32), axis=1, keepdims=True)
    lane = lax.broadcasted_iota(jnp.int32, (1, D), 1)
    hi, mid, lo = split3(total)
    left = slot128[pl.ds(0, rows, stride=2)]
    right = slot128[pl.ds(1, rows, stride=2)]
    own = jnp.concatenate([left, right], 1)
    last = jnp.where(lane == 0, hi, jnp.where(lane == 1, mid, jnp.where(lane == 2, lo, 0.0)))
    last_row = lax.broadcasted_iota(jnp.int32, (rows, D), 0) == rows - 1
    slots[core, me] = jnp.where(last_row, last, own).astype(BF)

    def column(index, k):
        return (index + n - 4 * k) % n

    def send_slot(origin, to, lo=0, hi=rows):
        ref = slots.at[core, origin, pl.ds(lo, hi - lo)]
        return copy(ref, ref, next(number), to)

    near_xy = near_x + near_y - me
    cut = rows // 2
    z_in, x_in, y_in, d_in, s_in = {}, {}, {}, {}, []
    for k in sorted(range(1, depth), key=lambda k: (min(k, depth - k), k)):
        z_in[k] = send_slot(me, at(core, (me + 4 * k) % n))
    order = [0] + list(z_in)
    for k in order:
        if k:
            z_in[k].wait_recv()
        x_in[k] = send_slot(column(me, k), at(core, near_x))
        y_in[k] = send_slot(column(me, k), at(core, near_y))
        s_in.append(send_slot(column(me, k), at(1 - core, me)))
    for k in order:
        x_in[k].wait_recv()
        first = send_slot(column(near_x, k), at(core, near_y), 0, cut)
        s_in.append(send_slot(column(near_x, k), at(1 - core, me)))
        y_in[k].wait_recv()
        second = send_slot(column(near_y, k), at(core, near_x), cut, rows)
        s_in.append(send_slot(column(near_y, k), at(1 - core, me)))
        d_in[k] = (first, second)
    for k in order:
        for c in d_in[k]:
            c.wait_recv()
        s_in.append(send_slot(column(near_xy, k), at(1 - core, me)))
    ints_copy.wait_recv()
    both[core] = ints_ref[:, pl.ds(mine, half)]
    for c in s_in:
        c.wait_recv()
    for c in started:
        c.wait_send()
    for t in range(2):
        vecf[...] = jnp.zeros(vecf.shape, F32)
        for i in range(n):
            unpack_rows(plan, i, slots[t, i], w.at[t], whf, vecf, [scratch.at[0], scratch.at[1]])
        for j in range(5):
            wh[t, :, D * j : D * j + D] = whf[D * j : D * j + D].astype(BF)
        vec[t] = vecf[...].astype(BF)
    total = jnp.zeros((1, D), F32)
    for i in range(n):
        tail = slots[0, i, rows - 16 : rows].astype(F32)
        total = total + tail[15:16]
    weight_sum = jnp.sum(jnp.where(lane < 3, total, 0.0), axis=1, keepdims=True)
    rw[...] = jnp.broadcast_to(imp_ref[:, pl.ds(mine, half)].astype(F32) / weight_sum, (8, half))


def gather(plan, p128, ints, imp):
    n, rows = plan.n, plan.slot
    half = ints.shape[1] // 2
    vm = pl.BlockSpec(memory_space=pltpu.VMEM)
    height = p128.shape[0]
    tall = max(2 * rows, height + 40) + 80
    copies = 1 + (n // 4 - 1) + 2 * (n // 4) + 2 * (n // 4) + n
    return pl.pallas_call(
        functools.partial(gather_kernel, plan),
        out_shape=(
            jax.ShapeDtypeStruct((2, A_ROWS, D), BF),
            jax.ShapeDtypeStruct((2, D, HPAD), BF),
            jax.ShapeDtypeStruct((2, 128, D), BF),
            jax.ShapeDtypeStruct((2, 8, half), jnp.int32),
            jax.ShapeDtypeStruct((8, half), F32),
        ),
        in_specs=[vm] * 3,
        out_specs=(vm,) * 5,
        scratch_shapes=[
            pltpu.VMEM((2, n, rows, D), BF),
            pltpu.VMEM((tall, 128), F32),
            pltpu.VMEM((height + 128, 128), F32),
            pltpu.VMEM((height + 8, 128), F32),
            pltpu.VMEM((2, rows, 128), F32),
            pltpu.VMEM((HPAD, D), F32),
            pltpu.VMEM((128, D), F32),
            pltpu.SemaphoreType.DMA((copies,)),
            pltpu.SemaphoreType.DMA((copies,)),
        ],
        compiler_params=pltpu.CompilerParams(
            collective_id=0, has_side_effects=True, vmem_limit_bytes=48 * 1024 * 1024
        ),
    )(p128, ints, imp)


def chunks(height):
    step = max(c for c in range(8, 113, 8) if height % c == 0)
    return [(lo, lo + step) for lo in range(0, height, step)]


def lay_flat(plan, me, slot128, flat, rolled):
    height = rolled.shape[0] - 16
    start = me * plan.length
    shift = start % 128
    first = start // 128
    base = plan.at(plan.a_base, me)
    row = lax.broadcasted_iota(jnp.int32, (height + 8, 128), 0)
    flat[...] = jnp.zeros(flat.shape, F32)

    @pl.when(plan.at(plan.a_rows, me) > 0)
    def _():
        rows = slot128[pl.ds(first - 2 * base, height + 8)]
        flat[16 : 24 + height] = jnp.where(row + first < 2 * A_ROWS, rows, 0.0)

    h_first, h_rows, h_off = (plan.at(t, me) for t in (plan.h_first, plan.h_rows, plan.h_off))
    it = lax.broadcasted_iota(jnp.int32, (16, 128), 0)
    lane = lax.broadcasted_iota(jnp.int32, (16, 128), 1)

    @pl.loop(0, h_rows)
    def _(k):
        begin = A_ROWS * D + HEADS * (h_first + k) - 128 * first + 128 * 16
        turn = begin % 128
        value = slot128[pl.ds(2 * h_off + 10 * k, 16)]
        value = jnp.where(it * 128 + lane < HEADS, value, 0.0)
        value = pltpu.roll(value, turn, 1)
        above = jnp.concatenate([jnp.zeros((8, 128), F32), value], 0)[7:23]
        to = pl.ds(begin // 128, 16)
        flat[to] = flat[to] + jnp.where(lane >= turn, value, above)

    v_start = (A_ROWS * D + D * HEADS) // 128
    v_rows, v_off, v_first = (plan.at(t, me) for t in (plan.v_rows, plan.v_off, plan.v_first))
    tall_v = min(height, -(-2 * max(plan.v_rows) // 8) * 8)

    @pl.when(v_rows > 0)
    def _():
        inside = plan.at([max(0, v_start - i * plan.length // 128) for i in range(plan.n)], me)
        source = 2 * v_off + first + inside - v_start - 2 * v_first
        to = pl.ds(16 + inside, tall_v)
        flat[to] = flat[to] + slot128[pl.ds(source, tall_v)]

    rolled[0 : height + 8] = pltpu.roll(flat[16 : 24 + height], (128 - shift) % 128, 1)
    for lo, hi in chunks(height):
        lane = lax.broadcasted_iota(jnp.int32, (hi - lo, 128), 1)
        flat[lo:hi] = jnp.where(lane < 128 - shift, rolled[lo:hi], rolled[lo + 1 : hi + 1])


def pack_slots(plan, core, gw, gh, gv, rgw, rgh, rgv, slots, sums, vsum, scratch):
    total = gv[core].astype(F32) + rgv[...]
    for kind in range(3):
        vsum[kind * (BLOCKS + 1) : (kind + 1) * (BLOCKS + 1)] = total[kind, 0 : BLOCKS + 1]
    sums[...] = gh[core].astype(F32) + rgh[...].astype(F32)
    for i in range(plan.n):
        base, rows = plan.a_base[i], plan.a_rows[i]
        h_rows, h_off, h_first = plan.h_rows[i], plan.h_off[i], plan.h_first[i]
        v_rows, v_off, v_first = plan.v_rows[i], plan.v_off[i], plan.v_first[i]
        slots[i, rows : plan.slot] = jnp.zeros((plan.slot - rows, D), BF)
        if rows:
            added = gw[core, base : base + rows].astype(F32) + rgw[base : base + rows].astype(F32)
            slots[i, 0:rows] = added.astype(BF)
        if h_rows or v_rows:
            scratch[...] = jnp.zeros(scratch.shape, F32)
            for half in range(2):
                for j in range(5 if h_rows else 0):
                    cols = slice(D * j + 128 * half, D * j + 128 * half + 128)
                    scratch[half, pl.ds(h_off + j, h_rows, stride=5)] = sums[h_first : h_first + h_rows, cols]
                if v_rows:
                    scratch[half, v_off : v_off + v_rows] = vsum[v_first : v_first + v_rows, 128 * half : 128 * half + 128]
            whole = jnp.concatenate([scratch[0], scratch[1]], 1)
            slots[i, rows : plan.slot] = whole[rows:].astype(BF)


def segment_bounds():
    first = [0] + [(CAT + j * D) * D for j in range(BLOCKS + 1)]
    return list(zip(first, first[1:] + [A_ROWS * D + D * HEADS]))


def update_shard(plan, me, p_ref, m_ref, v_ref, outs, flat, squares, sq_z, sq_y, sq_x, push, to_z, to_y, to_x):
    first_out, second_out, new_out, norm_out = outs
    height = p_ref.shape[0]
    start = me * plan.length
    correction = 1.0 - 0.5**STEP
    bounds = segment_bounds()

    def place(lo, hi):
        shape = (hi - lo, 128)
        return 128 * lo + 128 * lax.broadcasted_iota(jnp.int32, shape, 0) + lax.broadcasted_iota(jnp.int32, shape, 1)

    for lo, hi in chunks(height):
        spot = place(lo, hi)
        grad = jnp.where(spot < plan.length, flat[lo:hi], 0.0)
        first_new = 0.5 * m_ref[lo:hi] + 0.5 * grad
        second_new = 0.5 * v_ref[lo:hi] + 0.5 * grad * grad
        first_out[lo:hi] = first_new
        second_out[lo:hi] = second_new
        decay = jnp.where(spot < bounds[-1][1] - start, 0.01 * p_ref[lo:hi], 0.0)
        update = first_new / correction / (jnp.sqrt(second_new / correction) + 1e-06) + decay
        flat[lo:hi] = jnp.where(spot < plan.length, update, 0.0)
        new_out[lo:hi] = p_ref[lo:hi] - 0.5 * update
    squares[...] = jnp.zeros(squares.shape, F32)

    def each_segment(body):
        for j, (first, last) in enumerate(bounds):
            pl.when((first < start + plan.length) & (last > start))(lambda j=j, first=first, last=last: body(j, first, last))

    def square_sums(j, first, last):
        weight, change = jnp.zeros((8, 128), F32), jnp.zeros((8, 128), F32)
        for lo, hi in chunks(height):
            spot = place(lo, hi)
            inside = (spot >= first - start) & (spot < last - start)
            p, u = jnp.where(inside, p_ref[lo:hi], 0.0), jnp.where(inside, flat[lo:hi], 0.0)
            weight = weight + jnp.sum((p * p).reshape(-1, 8, 128), axis=0)
            change = change + jnp.sum((u * u).reshape(-1, 8, 128), axis=0)
        squares[0, j : j + 1] = jnp.sum(weight, axis=0, keepdims=True)
        squares[0, 16 + j : 17 + j] = jnp.sum(change, axis=0, keepdims=True)

    each_segment(square_sums)
    for c in [push(squares.at[0], sq_z.at[k], to) for k, to in enumerate(to_z, 1)]:
        c.wait_recv()
    total = squares[0]
    for k in range(1, len(to_z) + 1):
        total = total + sq_z[k]
    squares[1] = total
    push(squares.at[1], sq_y, to_y).wait_recv()
    squares[2] = squares[1] + sq_y[...]
    push(squares.at[2], sq_x, to_x).wait_recv()
    total = squares[2] + sq_x[...]
    norm = jnp.sqrt(jnp.sum(total, axis=1, keepdims=True))
    sq_y[...] = jnp.broadcast_to(norm, (32, 128))
    line = jnp.sqrt(jnp.sum(jnp.concatenate([total, jnp.zeros((96, 128), F32)], 0).T, axis=0, keepdims=True))
    norm_out[0:1] = line[:, 0:MATS]
    norm_out[1:2] = pltpu.roll(line, 112, 1)[:, 0:MATS]

    def scaled(j, first, last):
        ratio = sq_y[j : j + 1] / sq_y[16 + j : 17 + j]
        for lo, hi in chunks(height):
            spot = place(lo, hi)
            inside = (spot >= first - start) & (spot < last - start)
            new_out[lo:hi] = jnp.where(inside, p_ref[lo:hi] - 0.5 * ratio * flat[lo:hi], new_out[lo:hi])

    each_segment(scaled)


def reduce_kernel(
    plan, gw, gh, gv, st, ig, p_ref, m_ref, v_ref,
    st_out, ig_out, first_out, second_out, new_out, norm_out,
    rgw, rgh, rgv, slots, sums, vsum, scratch, in_d, in_x, in_y, in_z, slot128, flat, rolled, squares, sq_z, sq_y, sq_x,
    send, recv, local,
):
    n, rows = plan.n, plan.slot
    depth, cut = n // 4, plan.slot // 2
    core, me, near_x, near_y = neighbours(n)
    near_xy = near_x + near_y - me
    barrier = greet(core, me, near_x, near_y, n)
    pl.semaphore_wait(barrier, depth + 2)
    half = st.shape[1]
    number = iter(range(1 << 20))
    started = []

    def copy(src, dst, to):
        slot = next(number)
        c = pltpu.make_async_remote_copy(
            src_ref=src, dst_ref=dst, send_sem=send.at[slot], recv_sem=recv.at[slot], device_id=to, device_id_type=MESH
        )
        c.start()
        started.append(c)
        return c

    def column(index, k):
        return (index + n - 4 * k) % n

    sibling = at(1 - core, me)
    early = [
        copy(gw.at[1 - core], rgw, sibling),
        copy(gh.at[1 - core], rgh, sibling),
        copy(gv.at[1 - core], rgv, sibling),
    ]
    mine = pl.ds(pl.multiple_of(core * half, half), half)
    late = [
        copy(st.at[1 - core], st_out.at[mine], sibling),
        copy(ig.at[1 - core], ig_out.at[mine], sibling),
    ]
    stay = [
        pltpu.make_async_copy(st.at[core], st_out.at[mine], local.at[0]),
        pltpu.make_async_copy(ig.at[core], ig_out.at[mine], local.at[1]),
    ]
    for c in stay:
        c.start()
    for c in early:
        c.wait_recv()
    pack_slots(plan, core, gw, gh, gv, rgw, rgh, rgv, slots, sums, vsum, scratch)
    order = list(range(1, depth)) + [0]
    to_x, to_y = at(core, near_x), at(core, near_y)
    halves = {}
    for k in order:
        diagonal = column(near_xy, k)
        halves[k] = (
            copy(slots.at[diagonal, pl.ds(0, cut)], in_d.at[k, pl.ds(0, cut)], to_y),
            copy(slots.at[diagonal, pl.ds(cut, rows - cut)], in_d.at[k, pl.ds(cut, rows - cut)], to_x),
        )
    fulls = {}
    for k in order:
        ox, oy = column(near_x, k), column(near_y, k)
        halves[k][0].wait_recv()
        slots[ox, 0:cut] = (slots[ox, 0:cut].astype(F32) + in_d[k, 0:cut].astype(F32)).astype(BF)
        first = copy(slots.at[ox], in_x.at[k], to_x)
        halves[k][1].wait_recv()
        slots[oy, cut:rows] = (slots[oy, cut:rows].astype(F32) + in_d[k, cut:rows].astype(F32)).astype(BF)
        fulls[k] = (first, copy(slots.at[oy], in_y.at[k], to_y))
    along = {}
    for k in order:
        own = column(me, k)
        for c in fulls[k]:
            c.wait_recv()
        if k:
            total = slots[own].astype(F32) + in_x[k].astype(F32) + in_y[k].astype(F32)
            slots[own] = total.astype(BF)
            along[k] = copy(slots.at[own], in_z.at[k], at(core, own))
    for c in along.values():
        c.wait_recv()
    total = slots[me].astype(F32) + in_x[0].astype(F32) + in_y[0].astype(F32)
    for k in along:
        total = total + in_z[k].astype(F32)
    slot128[...] = jnp.zeros(slot128.shape, F32)
    slot128[pl.ds(0, rows, stride=2)] = total[:, 0:128]
    slot128[pl.ds(1, rows, stride=2)] = total[:, 128:D]
    lay_flat(plan, me, slot128, flat, rolled)

    to_z = [at(core, column(me, k)) for k in range(1, depth)]
    outs = (first_out, second_out, new_out, norm_out)
    update_shard(plan, me, p_ref, m_ref, v_ref, outs, flat, squares, sq_z, sq_y, sq_x, copy, to_z, to_y, to_x)
    for c in late:
        c.wait_recv()
    for c in stay:
        c.wait()
    for c in started:
        c.wait_send()


def reduce_and_update(plan, gw, gh, gv, st, ig, p128, m128, v128):
    n, rows = plan.n, plan.slot
    depth = n // 4
    half = st.shape[1]
    height = p128.shape[0]
    vm = pl.BlockSpec(memory_space=pltpu.VMEM)
    hbm = pl.BlockSpec(memory_space=pl.ANY)
    copies = 5 + 2 * depth + 2 * depth + (depth - 1) + (depth - 1) + 2
    flat32 = jax.ShapeDtypeStruct((height, 128), F32)
    return pl.pallas_call(
        functools.partial(reduce_kernel, plan),
        out_shape=(
            jax.ShapeDtypeStruct((2 * half, D), BF),
            jax.ShapeDtypeStruct((2 * half, D), F32),
            flat32,
            flat32,
            flat32,
            jax.ShapeDtypeStruct((2, MATS), F32),
        ),
        in_specs=[vm] * 3 + [hbm] * 2 + [vm] * 3,
        out_specs=(hbm, hbm, vm, vm, vm, vm),
        scratch_shapes=[
            pltpu.VMEM((A_ROWS, D), BF),
            pltpu.VMEM((D, HPAD), BF),
            pltpu.VMEM(gv.shape[1:], F32),
            pltpu.VMEM((n, rows, D), BF),
            pltpu.VMEM((D, HPAD), F32),
            pltpu.VMEM((40, D), F32),
            pltpu.VMEM((2, rows, 128), F32),
            pltpu.VMEM((depth, rows, D), BF),
            pltpu.VMEM((depth, rows, D), BF),
            pltpu.VMEM((depth, rows, D), BF),
            pltpu.VMEM((depth, rows, D), BF),
            pltpu.VMEM((max(2 * rows, height + 48) + 80, 128), F32),
            pltpu.VMEM((height + 128, 128), F32),
            pltpu.VMEM((height + 16, 128), F32),
            pltpu.VMEM((3, 32, 128), F32),
            pltpu.VMEM((depth, 32, 128), F32),
            pltpu.VMEM((32, 128), F32),
            pltpu.VMEM((32, 128), F32),
            pltpu.SemaphoreType.DMA((copies,)),
            pltpu.SemaphoreType.DMA((copies,)),
            pltpu.SemaphoreType.DMA((2,)),
        ],
        compiler_params=pltpu.CompilerParams(
            collective_id=1, has_side_effects=True, vmem_limit_bytes=48 * 1024 * 1024
        ),
    )(gw, gh, gv, st, ig, p128, m128, v128)


class Copies:
    def __init__(self, send, recv):
        self.send, self.recv, self.made, self.sent = send, recv, [], set()

    def add(self, src, dst, to, recv_slot=None, only=None):
        self.made.append((src, dst, to, recv_slot, only))
        return len(self.made) - 1

    def get(self, number):
        src, dst, to, recv_slot, _ = self.made[number]
        return pltpu.make_async_remote_copy(
            src_ref=src(), dst_ref=dst(), send_sem=self.send.at[number],
            recv_sem=self.recv.at[number] if recv_slot is None else recv_slot(),
            device_id=to(), device_id_type=MESH,
        )

    def start(self, *numbers):
        for number in numbers:
            self.get(number).start()

    def arrive(self, *numbers):
        for number in numbers:
            self.get(number).wait_recv()

    def leave(self, *numbers):
        for number in numbers:
            only = self.made[number][4]
            if number not in self.sent and only is None:
                self.get(number).wait_send()
            elif number not in self.sent:
                pl.when(only())(lambda number=number: self.get(number).wait_send())
            self.sent.add(number)


def fused_fits(plan):
    depth = plan.n // 4
    blocks = 11 * depth + depth - 1
    half = plan.slot // 2
    plain = [b + plan.slot <= A_ROWS for b, h, v in zip(plan.a_base, plan.h_rows, plan.v_rows) if not (h or v)]
    vectors = [rows for rows in plan.v_rows if rows]
    return (
        all(plain)
        and vectors == [3 * (BLOCKS + 1)]
        and plan.n % 4 == 0
        and half >= 32
        and 4 * half <= HPAD
        and 2 * depth * plan.slot <= (BLOCKS + 1) * D
        and -(-blocks // 4) * half <= BLOCKS * (D + 16)
        and max(plan.a_rows) <= plan.slot
    )


def train_kernel(
    plan, x_ref, codes_ref, targets_ref, visits_ref, imp_ref, p_ref, m_ref, v_ref, st_out, ig_out, flat_out, norm_out,
    w, wh, vec, both, away, rw, eye, wt, wht, vt, gsb, xt, mix, xh, gp, rstd, mean, stream, ex, br, dm, d2, lg, dl,
    gw, gh, gv, packed, st_stage, slot128, flat, rolled, vsum, vacc, vin, squares, sq_z, sq_y, sq_x,
    send, recv, z_recv, local, ready,
):
    n, rows = plan.n, plan.slot
    depth, hrows = n // 4, plan.slot // 2
    cut = hrows // 32 * 16
    core, me, near_x, near_y = neighbours(n)
    near_xy = near_x + near_y - me
    width = both.shape[2]
    height = p_ref.shape[0]
    first_out, second_out, new_out = (flat_out.at[i * height : (i + 1) * height] for i in range(3))
    moments = [
        pltpu.make_async_copy(src, dst, local.at[3 + i])
        for i, (src, dst) in enumerate(((m_ref, first_out), (v_ref, second_out)))
    ]
    z_me, j_me = me // 4, me % 4
    copies = Copies(send, recv)
    scratch = [slot128.at[0:rows], slot128.at[rows : 2 * rows]]
    barrier = greet(core, me, near_x, near_y, n)
    mine = pl.multiple_of(core * width, width)
    theirs = pl.multiple_of((1 - core) * width, width)
    x_copy = pltpu.make_async_copy(x_ref.at[pl.ds(mine, width)], st_stage.at[0], local.at[0])
    x_copy.start()
    for c in moments:
        c.start()
    for to, half in ((both.at[core], mine), (away, theirs)):
        cols = pl.ds(half, width)
        to[0:1] = codes_ref[:, cols]
        to[1:2] = targets_ref[0, :, cols]
        to[2:6] = visits_ref[:, cols]
        to[6:7] = targets_ref[1, :, cols]
        to[7:8] = targets_ref[2, :, cols]
    place_shard(plan, me, p_ref, slot128, flat, rolled)

    spare = (BLOCKS + 1) * D

    def slot_part(t, i, lo, count):
        row = pl.multiple_of(spare + rows * (t * depth + i // 4) + lo, 16)
        return xh.at[pl.ds(row, count), pl.ds(pl.multiple_of((i % 4) * D, D), D)]

    def column(index, k):
        return (index + n - 4 * k) % n

    def sibling():
        return at(1 - core, me)

    def same(make, to):
        return copies.add(make, make, to)

    low = core * hrows
    other_low = (1 - core) * hrows
    swap_first = same(lambda: slot_part(core, me, other_low, hrows), sibling)
    swap_second = same(lambda: slot_part(core, me, low, hrows), sibling)
    swap_ints = copies.add(lambda: away, lambda: both.at[core], sibling)
    order = [0] + sorted(range(1, depth), key=lambda k: (min(k, depth - k), k))
    to_x, to_y = (lambda: at(core, near_x)), (lambda: at(core, near_y))
    gathers = []
    for t in range(2):
        g = {"z": {}, "x": {}, "y": {}, "d": {}, "s": []}
        for k in order:
            if k:
                g["z"][k] = same(lambda t=t: slot_part(t, me, low, hrows), lambda k=k: at(core, (me + 4 * k) % n))
            g["x"][k] = same(lambda t=t, k=k: slot_part(t, column(me, k), low, hrows), to_x)
            g["y"][k] = same(lambda t=t, k=k: slot_part(t, column(me, k), low, hrows), to_y)
            g["d"][k] = (
                same(lambda t=t, k=k: slot_part(t, column(near_x, k), low, cut), to_y),
                same(lambda t=t, k=k: slot_part(t, column(near_y, k), low + cut, hrows - cut), to_x),
            )
            g["s", k] = [
                same(lambda t=t, k=k, index=index: slot_part(t, column(index, k), low, hrows), sibling) if index is not me or k else None
                for index in (me, near_x, near_y, near_xy)
            ]
        gathers.append(g)

    def gather_0(t):
        g = gathers[t]
        copies.start(*g["z"].values())
        copies.start(g["x"][0], g["y"][0])

    def gather_1(t):
        g = gathers[t]
        for k in order[1:]:
            copies.arrive(g["z"][k])
            copies.start(g["x"][k], g["y"][k], g["s", k][0])

    def gather_2(t):
        g = gathers[t]
        for k in order:
            copies.arrive(g["x"][k])
            copies.start(g["d"][k][0], g["s", k][1])
            copies.arrive(g["y"][k])
            copies.start(g["d"][k][1], g["s", k][2])

    def gather_3(t):
        g = gathers[t]
        for k in order:
            copies.arrive(*g["d"][k])
            copies.start(g["s", k][3])

    def gather_4(t):
        g = gathers[t]
        for k in order:
            copies.arrive(*(c for c in g["s", k] if c is not None))

    def unpack(t):
        lg[4 * D : 5 * D, 128:D] = jnp.zeros((D, 128), F32)
        vsum[...] = jnp.zeros(vsum.shape, F32)
        for i in range(n):
            row, lane = spare + rows * (t * depth + i // 4), (i % 4) * D
            unpack_rows(plan, i, xh[row : row + rows, lane : lane + D], w.at[t], lg, vsum, scratch)
        for j in range(5):
            wh[t, :, D * j : D * j + D] = lg[D * j : D * j + D].astype(BF)
        vec[t] = vsum[...].astype(BF)

    total = jnp.sum(imp_ref[...].astype(F32), axis=1, keepdims=True)
    lane_d = lax.broadcasted_iota(jnp.int32, (1, D), 1)
    hi, mid, lo = split3(total)
    left = slot128[pl.ds(0, rows, stride=2)]
    right = slot128[pl.ds(1, rows, stride=2)]
    own = jnp.concatenate([left, right], 1)
    last = jnp.where(lane_d == 0, hi, jnp.where(lane_d == 1, mid, jnp.where(lane_d == 2, lo, 0.0)))
    last_row = lax.broadcasted_iota(jnp.int32, (rows, D), 0) == rows - 1
    slot_part(core, me, 0, rows)[...] = jnp.where(last_row, last, own).astype(BF)
    pl.semaphore_wait(barrier, depth + 2)
    copies.start(swap_first, swap_second, swap_ints)
    eye[...] = identity(D)
    x_copy.wait()
    for c in range(0, width, CB):
        xt[0, 0:D, c : c + CB] = nt(eye[...], st_stage[0, c : c + CB, :]).astype(BF)
    copies.arrive(swap_first)
    gather_0(0)
    gather_1(0)
    gather_2(0)
    gather_3(0)
    gather_0(1)
    copies.arrive(swap_second, swap_ints)
    gather_4(0)
    unpack(0)
    total = jnp.zeros((1, D), F32)
    for i in range(n):
        row, lane = spare + rows * (i // 4), (i % 4) * D
        total = total + xh[row + rows - 16 : row + rows, lane : lane + D].astype(F32)[15:16]
    weight_sum = jnp.sum(jnp.where(lane_d < 3, total, 0.0), axis=1, keepdims=True)
    rw[...] = jnp.broadcast_to(imp_ref[:, pl.ds(mine, width)].astype(F32) / weight_sum, (8, width))

    fwd = (eye, w, wh, vec, wt, vt, gsb, xt, mix, xh, gp, rstd, stream, mean, both, width)

    def during_forward(k):
        pl.when(k == 2)(lambda: gather_1(1))
        pl.when(k == 5)(lambda: gather_2(1))
        pl.when(k == 8)(lambda: gather_3(1))

    def emit_states(t):
        for c in range(0, width, CB):
            st_stage[t, c : c + CB, :] = nt(eye[...], xt[t + 1, 0:D, c : c + CB]).astype(BF)

    forward_tower(0, fwd, during_forward)
    gather_4(1)
    copies.leave(*range(len(copies.made)))
    unpack(1)
    forward_tower(1, fwd, None)
    emit_states(0)
    emit_states(1)
    out_rows = pl.ds(mine, width)
    st_copy = copies.add(lambda: st_stage.at[1 - core], lambda: st_out.at[out_rows], sibling)
    copies.start(st_copy)
    st_stay = pltpu.make_async_copy(st_stage.at[core], st_out.at[out_rows], local.at[1])
    st_stay.start()

    packed_of = [i for i in range(n) if plan.h_rows[i] or plan.v_rows[i]]
    owner = plan.v_rows.index(3 * (BLOCKS + 1))

    def block(t, q):
        arena, first = (xh, spare) if t == 0 else (mix, BLOCKS * (D + 16))
        row = pl.multiple_of(first + hrows * (q // 4), 16)
        return arena.at[pl.ds(row, hrows), pl.ds(pl.multiple_of((q % 4) * D, D), D)]

    def piece(t, q, lo, count):
        arena, first = (xh, spare) if t == 0 else (mix, BLOCKS * (D + 16))
        row = pl.multiple_of(first + hrows * (q // 4) + lo, 16)
        return arena.at[pl.ds(row, count), pl.ds(pl.multiple_of((q % 4) * D, D), D)]

    def slot_half(t, i, lo):
        if i in packed_of:
            return packed.at[packed_of.index(i), pl.ds(pl.multiple_of(lo, 16), hrows)]
        return gw.at[t, pl.ds(pl.multiple_of(plan.a_base[i] + lo, 16), hrows)]

    j_x, j_y, j_d = near_x % 4, near_y % 4, near_xy % 4
    jobs = {}
    for t in range(2):
        for zz in range(depth):
            q = 11 * zz
            job = {"q": q}
            job["swap"] = [
                copies.add(lambda t=t, i=4 * zz + j: slot_half(t, i, other_low), lambda t=t, q=q + j: block(t, q), sibling)
                for j in range(4)
            ]
            job["d"] = (
                copies.add(lambda t=t, q=q: piece(t, q + 4 + j_d, 0, cut), lambda t=t, q=q: piece(t, q + 8, 0, cut), to_y),
                copies.add(lambda t=t, q=q: piece(t, q + 4 + j_d, cut, hrows - cut), lambda t=t, q=q: piece(t, q + 8, cut, hrows - cut), to_x),
            )
            job["x"] = copies.add(lambda t=t, q=q: block(t, q + 4 + j_x), lambda t=t, q=q: block(t, q + 9), to_x)
            job["y"] = copies.add(lambda t=t, q=q: block(t, q + 4 + j_y), lambda t=t, q=q: block(t, q + 10), to_y)
            job["z"] = copies.add(
                lambda t=t, q=q: block(t, q + 4 + j_me),
                lambda t=t, zz=zz: block(t, 11 * depth + (zz + depth - z_me) % depth - 1),
                lambda zz=zz: at(core, 4 * zz + j_me),
                lambda t=t, zz=zz: z_recv.at[t * depth + (zz + depth - z_me) % depth],
                lambda zz=zz: z_me != zz,
            )
            jobs[t, zz] = job

    def pack(t, planes):
        wanted = [i for i in packed_of if i // 4 in planes]
        for i in wanted:
            a_rows, h_rows, h_off, h_first = plan.a_rows[i], plan.h_rows[i], plan.h_off[i], plan.h_first[i]
            to = packed.at[packed_of.index(i)]
            for part in scratch:
                part[...] = jnp.zeros(part.shape, F32)
            lo16, hi16 = h_first // 16 * 16, -(-(h_first + h_rows) // 16) * 16
            for half in range(2):
                for j in range(5 if h_rows else 0):
                    cols = slice(D * j + 128 * half, D * j + 128 * half + 128)
                    value = gh[t, lo16:hi16, cols].astype(F32)[h_first - lo16 : h_first - lo16 + h_rows]
                    scratch[half][pl.ds(h_off + j, h_rows, stride=5)] = value
            whole = jnp.concatenate([scratch[0][...], scratch[1][...]], 1)
            to[a_rows:rows] = whole[a_rows:].astype(BF)
            if a_rows:
                to[0:a_rows] = gw[t, plan.a_base[i] : plan.a_base[i] + a_rows]

    def plus(*refs):
        value = refs[0][...].astype(F32)
        for ref in refs[1:]:
            value = value + ref[...].astype(F32)
        return value

    def sum_0(t, zz):
        copies.start(*jobs[t, zz]["swap"])

    def sum_1(t, zz):
        job = jobs[t, zz]
        for j in range(4):
            copies.arrive(job["swap"][j])
            block(t, job["q"] + 4 + j)[...] = plus(slot_half(t, 4 * zz + j, low), block(t, job["q"] + j)).astype(BF)
        copies.start(*job["d"])

    def sum_2(t, zz):
        job = jobs[t, zz]
        q = job["q"]
        copies.arrive(job["d"][0])
        target = piece(t, q + 4 + j_x, 0, cut)
        target[...] = plus(target, piece(t, q + 8, 0, cut)).astype(BF)
        copies.start(job["x"])
        copies.arrive(job["d"][1])
        target = piece(t, q + 4 + j_y, cut, hrows - cut)
        target[...] = plus(target, piece(t, q + 8, cut, hrows - cut)).astype(BF)
        copies.start(job["y"])

    def sum_3(t, zz):
        job = jobs[t, zz]
        q = job["q"]
        copies.arrive(job["x"], job["y"])
        value = plus(block(t, q + 4 + j_me), block(t, q + 9), block(t, q + 10))

        @pl.when(z_me == zz)
        def _():
            partial(t)[...] = value

        @pl.when(z_me != zz)
        def _():
            block(t, q + 4 + j_me)[...] = value.astype(BF)
            copies.start(job["z"])

    def sum_4(t):
        for k in range(1, depth):
            src = block(t, 11 * depth + k - 1)
            pltpu.make_async_remote_copy(
                src_ref=src, dst_ref=src, send_sem=send.at[0], recv_sem=z_recv.at[t * depth + k], device_id=sibling(), device_id_type=MESH
            ).wait_recv()
            partial(t)[...] = partial(t)[...] + src[...].astype(F32)

    def final(h):
        return lg.at[pl.ds(pl.multiple_of(h * hrows, 8), hrows)]

    def partial(t):
        return lg.at[pl.ds(pl.multiple_of((2 + t) * hrows, 8), hrows)]

    def vector_step(step):
        sources = [gv.at[1 - core], vacc.at[0], vacc.at[1], vacc.at[2]]
        targets = [[sibling], [to_x], [to_y], [lambda k=k: at(core, (me + 4 * k) % n) for k in range(1, depth)]]
        if step:
            base = gv[core] if step == 1 else vacc[step - 2]
            for number, k in vector_copies[-1]:
                copies.arrive(number)
                base = base + vin[k]
            vacc[step - 1] = base
        if step < 4:
            slots = range(step, step + 1) if step < 3 else range(3, 2 + depth)
            started = []
            for k, to in zip(slots, targets[step]):
                number = copies.add(lambda step=step: sources[step], lambda k=k: vin.at[k], to)
                copies.start(number)
                started.append((number, k))
            vector_copies.append(started)

    vector_copies = []
    last_swap = copies.add(lambda: partial(1 - core), lambda: final(core), sibling)
    peers = [(1 - core, me), (core, near_x), (core, near_y)] + [(core, (me + 4 * k) % n) for k in range(1, depth)]

    bwd = (eye, w, wh, vec, wht, vt, gsb, xt, mix, xh, gp, rstd, stream, ex, br, dm, d2, lg, dl, both, rw, gw, gh, gv, dm, width)
    ig_copies = [copies.add(lambda: dm, lambda: ig_out.at[out_rows], sibling, None, lambda t=t: core != t) for t in range(2)]

    def ig_local():
        return pltpu.make_async_copy(dm, ig_out.at[out_rows], local.at[2])

    def emit_inputs(t):
        pl.when(core == t)(lambda: ig_local().start())
        pl.when(core != t)(lambda: copies.start(ig_copies[t]))

    def free_inputs(t):
        pl.when(core == t)(lambda: ig_local().wait())
        pl.when(core != t)(lambda: copies.get(ig_copies[t]).wait_send())

    ex[...] = jnp.zeros_like(ex)
    backward_tower(1, bwd, None, None)
    emit_inputs(1)
    for to_core, to_index in peers:
        pl.semaphore_signal(ready, inc=1, device_id=at(to_core, to_index), device_id_type=MESH)

    def after_head():
        pl.semaphore_wait(ready, len(peers))
        pack(1, range(depth))
        for zz in range(depth):
            sum_0(1, zz)

    def during_backward(i):
        def at_step(step, *calls):
            def run():
                for f, *args in calls:
                    f(*args)

            pl.when(i == step)(run)

        planes = range(depth)

        def release():
            copies.leave(*(jobs[1, i // 4]["swap"][i % 4] for i in packed_of))

        at_step(1, *((sum_1, 1, zz) for zz in planes))
        at_step(2, (release,), (pack, 0, (depth - 1,)), (sum_0, 0, depth - 1))
        at_step(3, *((sum_2, 1, zz) for zz in planes))
        for zz in range(1, depth - 1):
            done = BLOCKS + 1 - 4 * zz + 1
            if done < BLOCKS:
                at_step(done, (pack, 0, (zz,)), (sum_0, 0, zz))
            if done + 1 < BLOCKS:
                at_step(done + 1, (sum_1, 0, zz))
            if done + 2 < BLOCKS:
                at_step(done + 2, (sum_2, 0, zz))
        at_step(4, (sum_1, 0, depth - 1))
        at_step(5, *((sum_3, 1, zz) for zz in planes))
        at_step(6, (sum_2, 0, depth - 1))
        at_step(8, (sum_4, 1), (sum_3, 0, depth - 1))

    backward_tower(0, bwd, after_head, during_backward, lambda: free_inputs(1))
    emit_inputs(0)
    done = {zz: BLOCKS + 1 - 4 * zz + 1 for zz in range(1, depth - 1)}
    for zz in sorted(done, reverse=True):
        if done[zz] >= BLOCKS:
            pack(0, (zz,))
            sum_0(0, zz)
    pack(0, (0,))
    sum_0(0, 0)
    vector_step(0)
    for zz in sorted(done, reverse=True):
        if done[zz] + 1 >= BLOCKS:
            sum_1(0, zz)
        if done[zz] + 2 >= BLOCKS:
            sum_2(0, zz)
    sum_1(0, 0)
    vector_step(1)
    for zz in sorted(done, reverse=True):
        sum_3(0, zz)
    sum_2(0, 0)
    vector_step(2)
    sum_3(0, 0)
    vector_step(3)
    sum_4(0)
    copies.start(last_swap)
    final(core)[...] = partial(core)[...]
    vector_step(4)
    copies.arrive(last_swap)

    slot128[...] = jnp.zeros(slot128.shape, F32)
    for h in range(2):
        slot128[pl.ds(2 * hrows * h, hrows, stride=2)] = final(h)[:, 0:128]
        slot128[pl.ds(2 * hrows * h + 1, hrows, stride=2)] = final(h)[:, 128:D]

    @pl.when(me == owner)
    def _():
        for kind in range(3):
            first = 2 * (plan.v_off[owner] + kind * (BLOCKS + 1))
            for h in range(2):
                value = vacc[3, kind, 0 : BLOCKS + 1, 128 * h : 128 * h + 128]
                slot128[pl.ds(first + h, BLOCKS + 1, stride=2)] = value

    def push(src, dst, to):
        number = copies.add(lambda: src, lambda: dst, lambda: to)
        copies.start(number)
        return copies.get(number)

    lay_flat(plan, me, slot128, flat, rolled)
    for c in moments:
        c.wait()
    update_shard(
        plan, me, p_ref, first_out, second_out, (first_out, second_out, new_out, norm_out),
        flat, squares, sq_z, sq_y, sq_x, push, [at(core, (me + 4 * k) % n) for k in range(1, depth)], to_y(), to_x(),
    )
    copies.arrive(st_copy)
    pl.when(core == 0)(lambda: copies.arrive(ig_copies[0]))
    pl.when(core == 1)(lambda: copies.arrive(ig_copies[1]))
    free_inputs(0)
    st_stay.wait()
    copies.sent.update(ig_copies)
    copies.leave(*range(len(copies.made)))


def train(plan, latent, codes, targets, visits, imp, p128, m128, v128):
    n, rows = plan.n, plan.slot
    depth, hrows = n // 4, rows // 2
    width = codes.shape[1] // 2
    height = p128.shape[0]
    vm = pl.BlockSpec(memory_space=pltpu.VMEM)
    hbm = pl.BlockSpec(memory_space=pl.ANY)
    packed = sum(1 for h, v in zip(plan.h_rows, plan.v_rows) if h or v)
    return pl.pallas_call(
        functools.partial(train_kernel, plan),
        out_shape=(
            jax.ShapeDtypeStruct((2 * width, D), BF),
            jax.ShapeDtypeStruct((2 * width, D), F32),
            jax.ShapeDtypeStruct((3 * height, 128), F32),
            jax.ShapeDtypeStruct((2, MATS), F32),
        ),
        in_specs=[hbm] + [vm] * 5 + [hbm] * 2,
        out_specs=(hbm, hbm, vm, vm),
        scratch_shapes=[
            pltpu.VMEM((2, A_ROWS, D), BF),
            pltpu.VMEM((2, D, HPAD), BF),
            pltpu.VMEM((2, 128, D), BF),
            pltpu.VMEM((2, 8, width), jnp.int32),
            pltpu.VMEM((8, width), jnp.int32),
            pltpu.VMEM((8, width), F32),
            *work_scratch(width),
            pltpu.VMEM((2, A_ROWS, D), BF),
            pltpu.VMEM((2, D, HPAD), BF),
            pltpu.VMEM((2, 3, 16, D), F32),
            pltpu.VMEM((packed, rows, D), BF),
            pltpu.VMEM((2, width, D), BF),
            pltpu.VMEM((max(2 * rows, height + 48) + 80, 128), F32),
            pltpu.VMEM((height + 128, 128), F32),
            pltpu.VMEM((height + 16, 128), F32),
            pltpu.VMEM((128, D), F32),
            pltpu.VMEM((4, 3, 16, D), F32),
            pltpu.VMEM((2 + depth, 3, 16, D), F32),
            pltpu.VMEM((3, 32, 128), F32),
            pltpu.VMEM((depth, 32, 128), F32),
            pltpu.VMEM((32, 128), F32),
            pltpu.VMEM((32, 128), F32),
            pltpu.SemaphoreType.DMA((11 * n,)),
            pltpu.SemaphoreType.DMA((11 * n,)),
            pltpu.SemaphoreType.DMA((2 * depth,)),
            pltpu.SemaphoreType.DMA((5,)),
            pltpu.SemaphoreType.REGULAR,
        ],
        compiler_params=pltpu.CompilerParams(
            collective_id=2, has_side_effects=True, vmem_limit_bytes=63 * 1024 * 1024
        ),
    )(latent, codes, targets, visits, imp, p128, m128, v128)


def on_device(latent, codes, targets, visits, importance, params, first_moment, second_moment):
    me = lax.axis_index("tower")
    row_count = latent.shape[0]
    half = row_count // 2
    shard_len = params.shape[1]
    plan = Plan(lax.axis_size("dp"), shard_len)
    height = -(-plan.rows128 // 8) * 8
    p128, m128, v128 = (
        jnp.pad(v, ((0, 0), (0, 128 * height - shard_len))).reshape(height, 128) for v in (params, first_moment, second_moment)
    )
    if fused_fits(plan):
        states_out, inputs_out, flat, norms = train(
            plan, latent, codes, targets.transpose(1, 0, 2), visits[0].T, importance[None], p128, m128, v128
        )
    else:
        ints = jnp.concatenate([codes, targets[0, :1], visits[0].T, targets[0, 1:]], 0)
        x = lax.dynamic_slice_in_dim(latent, me * half, half, 0)
        w, wh, vec, both, rw = gather(plan, p128, ints, importance[None])
        st, ig, gw, gh, gv = compute(x, both, rw, w, wh, vec)
        states_out, inputs_out, *flat, norms = reduce_and_update(plan, gw, gh, gv, st, ig, p128, m128, v128)
        flat = jnp.concatenate(flat)
    flat = flat.reshape(1, -1)
    first, second, new = (flat[:, i * 128 * height : i * 128 * height + shard_len] for i in range(3))
    return (states_out[None], inputs_out[None], first, second, new, new.astype(BF), norms[None])


def solution(mesh):
    in_specs = (
        P("dp", None),
        P("tower", "dp"),
        P("tower", None, "dp"),
        P("tower", "dp", None),
        P("dp"),
        P("tower", "dp"),
        P("tower", "dp"),
        P("tower", "dp"),
    )
    out_specs = (
        P("tower", "dp", None),
        P("tower", "dp", None),
        P("tower", "dp"),
        P("tower", "dp"),
        P("tower", "dp"),
        P("tower", "dp"),
        P("tower", None, None),
    )
    return jax.shard_map(
        on_device, mesh=mesh, in_specs=in_specs, out_specs=out_specs, check_vma=False
    )
```

```python
import functools

import jax
import jax.numpy as jnp
from jax import lax
from jax.experimental import pallas as pl
from jax.experimental.pallas import tpu as pltpu
from jax.sharding import PartitionSpec as P

D = 256
CODES = 32
BINS = 601
BLOCKS = 10
STEP = 5
HEADS = 1238
MATS = 12
P_SIZE = 1054464
HPAD = 1280
CAT = D + CODES
A_ROWS = CAT + BLOCKS * D
BF = jnp.bfloat16
F32 = jnp.float32
GELU_C = 0.7978845608028654
GELU_K = 0.044715


def nn(a, b):
    return jnp.dot(a, b, preferred_element_type=F32)


def nt(a, b):
    return lax.dot_general(a, b, (((1,), (1,)), ((), ())), preferred_element_type=F32)


def identity(n):
    return (lax.broadcasted_iota(jnp.int32, (n, n), 0) == lax.broadcasted_iota(jnp.int32, (n, n), 1)).astype(BF)


ZETA = (GELU_C * GELU_K) ** (1.0 / 3.0)
B0 = GELU_C / ZETA
E0 = 0.5 / ZETA


def wide(v, cs):
    return jnp.concatenate([v] * ((cs.stop - cs.start) // v.shape[1]), 1)


class Later:
    def __init__(self, depth=1):
        self.depth, self.held = depth, []

    def put(self, *stores):
        self.held.append(stores)
        if len(self.held) > self.depth:
            self.flush(self.depth)

    def flush(self, keep=0):
        while len(self.held) > keep:
            for store in self.held.pop(0):
                store()


def put(ref, rs, cs, value):
    ref[rs, cs] = value


def norm_act(src, cs, gs, unit, gp, rstd, out, later, kind=BF):
    for r in range(0, D, 32):
        rs = slice(r, r + 32)
        xh = src[rs, cs] * rstd
        z = xh * wide(gs[rs, 0:128], cs) + wide(gs[rs, 128:256], cs)
        z2 = z * z
        t = jnp.tanh(z * (z2 + B0))
        q = t * E0 + E0
        a = z * q
        slope = (q + (a * (1.0 - t)) * (z2 * 3.0 + B0)).astype(BF)
        later.put(
            functools.partial(put, unit, rs, cs, xh.astype(BF)),
            functools.partial(out, rs, a.astype(kind)),
            functools.partial(put, gp, rs, cs, slope),
        )


def broadcast_vectors(vt, rows):
    k = lax.broadcasted_iota(jnp.int32, (128, 128), 0)
    picks = jnp.concatenate([(k == row).astype(BF) for row in rows], 1)
    return nn(vt, picks)


def head_stage(cs, lg, dl, ints, rw):
    width = rw.shape[1]
    it8 = lax.broadcasted_iota(jnp.int32, (8, width), 0)
    low = -jnp.inf
    b75, b150, b154 = lg[600:608], lg[1200:1208], lg[1232:1240]

    def top(block):
        return jnp.max(block, axis=0, keepdims=True)

    def top_range(lo, hi):
        best = lg[lo : lo + 8]
        for r in range(lo + 8, hi, 8):
            best = jnp.maximum(best, lg[r : r + 8])
        return best

    max_v = top(jnp.maximum(top_range(0, 600), jnp.where(it8 < 1, b75, low)))
    max_r = top(
        jnp.maximum(
            jnp.maximum(top_range(608, 1200), jnp.where(it8 >= 1, b75, low)),
            jnp.where(it8 < 2, b150, low),
        )
    )
    max_c = top(
        jnp.maximum(
            jnp.maximum(top_range(1208, 1232), jnp.where(it8 >= 2, b150, low)),
            jnp.where(it8 < 2, b154, low),
        )
    )
    in_policy = (it8 >= 2) & (it8 < 6)
    max_p = top(jnp.where(in_policy, b154, low))

    def exp_range(lo, hi, best):
        acc = jnp.zeros((8, width), F32)
        for r in range(lo, hi, 8):
            e = jnp.exp(lg[r : r + 8] - best)
            lg[r : r + 8] = e
            acc = acc + e
        return acc

    e75 = jnp.exp(b75 - jnp.where(it8 < 1, max_v, max_r))
    e150 = jnp.exp(b150 - jnp.where(it8 < 2, max_r, max_c))
    e154 = jnp.exp(b154 - jnp.where(it8 < 2, max_c, max_p))

    def total(acc):
        return rw / jnp.sum(acc, axis=0, keepdims=True)

    inv_v = total(exp_range(0, 600, max_v) + jnp.where(it8 < 1, e75, 0.0))
    inv_r = total(exp_range(608, 1200, max_r) + jnp.where(it8 >= 1, e75, 0.0) + jnp.where(it8 < 2, e150, 0.0))
    inv_c = total(exp_range(1208, 1232, max_c) + jnp.where(it8 >= 2, e150, 0.0) + jnp.where(it8 < 2, e154, 0.0))
    inv_p = total(jnp.where(in_policy, e154, 0.0))
    hit_v = ints[1:2]
    hit_r = ints[6:7] + BINS
    hit_c = ints[7:8] + 2 * BINS
    counts = jnp.where(in_policy, ints.astype(F32), 0.0)
    share = counts * (rw / jnp.sum(counts, axis=0, keepdims=True))

    def minus(value, lo, *hits):
        at = lax.broadcasted_iota(jnp.int32, value.shape, 0)
        for hit in hits:
            value = value - jnp.where(at == hit - lo, rw, 0.0)
        return value

    d75 = minus(e75 * jnp.where(it8 < 1, inv_v, inv_r), 600, hit_v, hit_r)
    d150 = minus(e150 * jnp.where(it8 < 2, inv_r, inv_c), 1200, hit_r, hit_c)
    d154 = minus(e154 * jnp.where(it8 < 2, inv_c, inv_p), 1232, hit_c) - share
    d154 = jnp.where(it8 < 6, d154, 0.0)

    def emit(lo, hi, inv, hit):
        for r in range(lo, hi, 16):
            dl[r : r + 16, cs] = minus(lg[r : r + 16] * inv, r, hit).astype(BF)

    def pair(first, second):
        return jnp.concatenate([first, second], 0).astype(BF)

    emit(0, 592, inv_v, hit_v)
    dl[592:608, cs] = pair(minus(lg[592:600] * inv_v, 592, hit_v), d75)
    emit(608, 1200, inv_r, hit_r)
    dl[1200:1216, cs] = pair(d150, minus(lg[1208:1216] * inv_c, 1208, hit_c))
    emit(1216, 1232, inv_c, hit_c)
    dl[1232:1248, cs] = pair(d154, jnp.zeros_like(d154))
    dl[1248:HPAD, cs] = jnp.zeros((HPAD - 1248, width), BF)


CB = 256
GROUP = 2


def saved_views(t, mix, xh):
    def mixed(k):
        return mix.at[pl.ds(pl.multiple_of((t * BLOCKS + k - 1) * (D + 16), 16), D + 16)]

    def unit(k):
        return xh.at[pl.ds(pl.multiple_of((t * (BLOCKS + 1) + k) * D, D), D)]

    return mixed, unit


def column_groups(width):
    blocks = [slice(c, c + CB) for c in range(0, width, CB)]
    per = min(GROUP, len(blocks))
    return blocks, per, [slice(c, c + per * CB) for c in range(0, width, per * CB)]


def forward_tower(t, refs, during=None):
    (eye, w, wh, vec, wt, vt, gsb, xt, mix, xh, gp, rstd, stream, mean, ints, width) = refs
    blocks, per, groups = column_groups(width)
    mixed, unit = saved_views(t, mix, xh)
    first_bias = 2 * (BLOCKS + 1)
    ones = jnp.ones((16, D), BF)

    def mean_rows(slot):
        value = nn(ones, wt[slot, 0:D])[0:8] * (1.0 / D)
        high = value.astype(BF).astype(F32)
        wt[slot, D : D + 16] = jnp.concatenate([high, value - high], 0).astype(BF)

    def vectors(k):
        gsb[k % 2] = broadcast_vectors(vt[...], (k, k + BLOCKS + 1)) * ZETA

    def prefetch(k):
        vectors(k)
        row = pl.multiple_of(CAT + (k - 1) * D, 32)
        wt[k % 2, 0:D, 0:D] = nt(eye[...], w[t, pl.ds(row, D)]).astype(BF)
        at_row = lax.broadcasted_iota(jnp.int32, (128, 128), 0) == k + first_bias
        at_lane = lax.broadcasted_iota(jnp.int32, (128, 128), 1) == 0
        wt[k % 2, 0:D, D:384] = nn(vt[...], (at_row & at_lane).astype(BF)).astype(BF)
        mean_rows(k % 2)

    def row_of(k):
        return pl.ds(t * (BLOCKS + 1) + k, 1)

    def stage(k, c):
        def keep(rs, a):
            mixed(k)[rs, blocks[c]] = a

        later = Later()
        norm_act(stream, blocks[c], gsb.at[k % 2], unit(k), gp.at[t, k], rstd[row_of(k), blocks[c]], keep, later)
        later.flush()

    def spread(square, k, cs):
        var = jnp.sum(square, axis=0, keepdims=True) * (1.0 / D)
        rstd[row_of(k), cs] = lax.rsqrt(var + 1e-05)

    def add(k, cs, out, fresh):
        shift = out[D : D + 1] + out[D + 8 : D + 9]
        square = jnp.zeros((8, out.shape[1]), F32)
        for r in range(0, D, 32):
            value = out[r : r + 32] - shift
            if not fresh:
                value = stream[r : r + 32, cs] + value
            stream[r : r + 32, cs] = value
            square = square + jnp.sum((value * value).reshape(4, 8, -1), axis=0)
        if not fresh:
            mean[0:1, cs] = mean[0:1, cs] + shift
        spread(square, k + 1, cs)

    def centre(cs):
        total = jnp.zeros((8, CB), F32)
        for r in range(0, D, 32):
            total = total + jnp.sum(stream[r : r + 32, cs].reshape(4, 8, -1), axis=0)
        middle = jnp.sum(total, axis=0, keepdims=True) * (1.0 / D)
        mean[0:1, cs] = middle
        square = jnp.zeros((8, CB), F32)
        for r in range(0, D, 32):
            value = stream[r : r + 32, cs] - middle
            stream[r : r + 32, cs] = value
            square = square + jnp.sum((value * value).reshape(4, 8, -1), axis=0)
        spread(square, 1, cs)

    vt[...] = nt(eye[...], vec[t]).astype(BF)
    vectors(0)
    wt[0, 0:D, 0:D] = nt(eye[...], w[t, 0:D]).astype(BF)
    tile = first_bias // 16 * 16
    picked = lax.broadcasted_iota(jnp.int32, (16, D), 0) == first_bias - tile
    bias = jnp.where(picked, vec[t, tile : tile + 16].astype(F32), 0.0).astype(BF)
    rest = jnp.concatenate([w[t, D:CAT], bias, jnp.zeros((128 - CODES - 16, D), BF)], 0)
    wt[0, 0:D, D:384] = nt(eye[...], rest).astype(BF)
    mean_rows(0)
    for cs in blocks:
        it = lax.broadcasted_iota(jnp.int32, (CODES, CB), 0)
        xt[t, D:CAT, cs] = (it == ints[t, 0:1, cs]).astype(BF)
        xt[t, CAT : CAT + 16, cs] = jnp.ones((16, CB), BF)
    first = [nn(wt[0, :, 0 : CAT + 16], xt[t, :, cs]) for cs in groups]
    prefetch(1)
    for group, cs in enumerate(groups):
        add(-1, cs, first[group], True)
    for cs in blocks:

        def keep(rs, a):
            stream[rs, cs] = a

        later = Later()
        norm_act(stream, cs, gsb.at[0], unit(0), gp.at[t, 0], rstd[row_of(0), cs], keep, later, F32)
        later.flush()
        centre(cs)

    def layer(k, more):
        if more:
            prefetch(k + 1)
        mixed(k)[D : D + 16, :] = jnp.ones((16, width), BF)
        for group, cs in enumerate(groups):
            out = nn(wt[k % 2, :, 0 : D + 16], mixed(k)[:, cs])
            ahead = group + 1 < len(groups)
            if ahead or more:
                for c in range(per):
                    stage(k if ahead else k + 1, (group + 1) % len(groups) * per + c)
            add(k, cs, out, False)

    for c in range(per):
        stage(1, c)

    @pl.loop(1, BLOCKS)
    def _(k):
        if during is not None:
            during(k)
        layer(k, True)

    layer(BLOCKS, False)
    for cs in blocks:
        xt[t + 1, 0:D, cs] = (stream[:, cs] + mean[0:1, cs]).astype(BF)


def backward_tower(t, refs, after_head=None, during=None, before_product=None):
    (eye, w, wh, vec, wht, vt, gsb, xt, mix, xh, gp, rstd, ds, ex, br, dm, d2, lg, dl, ints, rw, gw, gh, gv, ig, width) = refs
    blocks, per, groups = column_groups(width)
    mixed, unit = saved_views(t, mix, xh)
    vt[...] = nt(eye[...], vec[t]).astype(BF)
    for h in range(0, HPAD, D):
        wht[h : h + D, :] = nt(eye[...], wh[t, :, h : h + D]).astype(BF)

    @pl.loop(0, width // CB)
    def _(c):
        cs = pl.ds(pl.multiple_of(c * CB, CB), CB)
        lg[...] = nn(wht[...], xt[t + 1, 0:D, cs])
        head_stage(cs, lg, dl, ints[t, :, cs], rw[0:1, cs])
        value = nn(wh[t], dl[:, cs]) + ex[:, cs]
        ds[:, cs] = value
        br[BLOCKS % 2, :, cs] = value.astype(BF)

    for h in range(0, HPAD, D):
        gh[t, :, h : h + D] = nt(xt[t + 1, 0:D, :], dl[h : h + D]).astype(BF)
    if after_head is not None:
        after_head()
    ones = jnp.ones((16, width), BF)

    def part(c):
        return dm.at[c * D : c * D + D]

    def gains(k):
        gsb[k % 2, :, 0:128] = broadcast_vectors(vt[...], (k,)) * ZETA

    def row_sums(k):
        for kind in range(2):
            gv[t, kind, pl.ds(k, 1), :] = nt(ones, d2[1 - kind])[0:1] * ZETA

    def product(k, group):
        row = pl.multiple_of(CAT + (k - 1) * D, 32)
        back = nn(w[t, pl.ds(row, D)], br[k % 2, :, groups[group]])
        for c in range(per):
            part(group * per + c)[...] = back[:, c * CB : c * CB + CB]

    def slopes(k, c):
        cs, grad = blocks[c], part(c)
        later = Later()
        for r in range(0, D, 32):
            rs = slice(r, r + 32)
            dy = grad[rs, :] * gp[t, k, rs, cs].astype(F32)
            low = dy.astype(BF)
            later.put(
                functools.partial(put, grad, rs, slice(None), dy),
                functools.partial(put, d2.at[0], rs, cs, low),
                functools.partial(put, d2.at[1], rs, cs, low * unit(k)[rs, cs]),
            )
        later.flush()

    def sums(k, group):
        pick = (lax.broadcasted_iota(jnp.int32, (16, 128), 1) == k).astype(BF)
        gain = nt(pick, vt[...]).astype(BF)
        scale = rstd[pl.ds(t * (BLOCKS + 1) + k, 1), groups[group]] * (ZETA / D)
        return [(nn(gain, d2[i, :, groups[group]]) * scale).astype(BF) for i in range(2)]

    def inputs(k, group, means, first):
        later = Later()
        for c in range(per):
            cs = blocks[group * per + c]
            m1, m2 = (m[:, c * CB : c * CB + CB] for m in means)
            scale = rstd[pl.ds(t * (BLOCKS + 1) + k, 1), cs]
            m1, m2 = (jnp.concatenate([m, m], 0) for m in (m1, m2))
            for r in range(0, D, 32):
                rs = slice(r, r + 32)
                less = (m1 + unit(k)[rs, cs] * m2).astype(F32)
                back = part(group * per + c)[rs, :] * wide(gsb[k % 2, rs, 0:128], cs) * scale - less
                if first:
                    later.put(functools.partial(put, br.at[0], rs, cs, back.astype(BF)))
                else:
                    value = ds[rs, cs] + back
                    later.put(
                        functools.partial(put, ds, rs, cs, value),
                        functools.partial(put, br.at[(k + 1) % 2], rs, cs, value.astype(BF)),
                    )
        later.flush()

    def weight_sums(k):
        full = nt(mixed(k)[...], br[k % 2])
        row = pl.multiple_of(CAT + (k - 1) * D, 32)
        gw[t, pl.ds(row, D), :] = full[0:D].astype(BF)
        gv[t, 2, pl.ds(k, 1), :] = full[D : D + 1]

    def layer(k, first):
        means = []
        for group in range(len(groups)):
            if not first and group + 1 < len(groups):
                product(k, group + 1)
            for c in range(per):
                slopes(k, group * per + c)
            means.append(sums(k, group))
        if not first:
            weight_sums(k)
        for group in range(len(groups)):
            inputs(k, group, means[group], first)
            if not first and group == 0:
                product(k - 1, 0)
        row_sums(k)

    if before_product is not None:
        before_product()
    gains(BLOCKS)
    product(BLOCKS, 0)

    @pl.loop(0, BLOCKS)
    def _(i):
        k = BLOCKS - i
        if during is not None:
            during(i)
        gains(k - 1)
        layer(k, False)

    for c, cs in enumerate(blocks):
        part(c)[...] = ds[:, cs]
    layer(0, True)
    full = nt(xt[t], br[0])
    gw[t, 0:CAT, :] = full[0:CAT].astype(BF)
    gv[t, 2, 0:1, :] = full[CAT : CAT + 1]
    for cs in blocks:
        back = nn(w[t, 0:D], br[0, :, cs])
        ex[:, cs] = back
        ig[cs, :] = back.T


def compute_kernel(x_ref, ints, rw, w, wh, vec, st, ig, gw, gh, gv, eye, wt, wht, vt, gsb, xt, mix, xh, gp, rstd, mean, stream, ex, br, dm, d2, lg, dl):
    width = x_ref.shape[0]
    eye[...] = identity(D)
    for c in range(0, width, CB):
        cs = slice(c, c + CB)
        xt[0, 0:D, cs] = nt(eye[...], x_ref[cs, :]).astype(BF)
    fwd = (eye, w, wh, vec, wt, vt, gsb, xt, mix, xh, gp, rstd, stream, mean, ints, width)
    @pl.loop(0, 2)
    def _(t):
        forward_tower(t, fwd)

        @pl.loop(0, width // CB)
        def _(c):
            cs = pl.ds(pl.multiple_of(c * CB, CB), CB)
            st[t, cs, :] = nt(eye[...], xt[t + 1, 0:D, cs]).astype(BF)

    ex[...] = jnp.zeros_like(ex)

    @pl.loop(0, 2)
    def _(i):
        t = 1 - i
        backward_tower(
            t,
            (eye, w, wh, vec, wht, vt, gsb, xt, mix, xh, gp, rstd, stream, ex, br, dm, d2, lg, dl, ints, rw, gw, gh, gv, ig.at[t], width),
        )


def work_scratch(width):
    return [
        pltpu.VMEM((D, D), BF),
        pltpu.VMEM((2, D + 16, 384), BF),
        pltpu.VMEM((HPAD, D), BF),
        pltpu.VMEM((D, 128), BF),
        pltpu.VMEM((2, D, 256), F32),
        pltpu.VMEM((3, CAT + 16, width), BF),
        pltpu.VMEM((2 * BLOCKS * (D + 16), width), BF),
        pltpu.VMEM((2 * (BLOCKS + 1) * D, width), BF),
        pltpu.VMEM((2, BLOCKS + 1, D, width), BF),
        pltpu.VMEM((24, width), F32),
        pltpu.VMEM((8, width), F32),
        pltpu.VMEM((D, width), F32),
        pltpu.VMEM((D, width), F32),
        pltpu.VMEM((2, D, width), BF),
        pltpu.VMEM((width // CB * D, CB), F32),
        pltpu.VMEM((2, D, width), BF),
        pltpu.VMEM((HPAD, CB), F32),
        pltpu.VMEM((HPAD, width), BF),
    ]


def compute(x, ints, rw, w, wh, vec):
    width = x.shape[0]
    vm = pl.BlockSpec(memory_space=pltpu.VMEM)
    return pl.pallas_call(
        compute_kernel,
        out_shape=(
            jax.ShapeDtypeStruct((2, width, D), BF),
            jax.ShapeDtypeStruct((2, width, D), F32),
            jax.ShapeDtypeStruct((2, A_ROWS, D), BF),
            jax.ShapeDtypeStruct((2, D, HPAD), BF),
            jax.ShapeDtypeStruct((2, 3, 16, D), F32),
        ),
        in_specs=[vm] * 6,
        out_specs=(vm,) * 5,
        scratch_shapes=work_scratch(width),
        compiler_params=pltpu.CompilerParams(vmem_limit_bytes=62 * 1024 * 1024),
    )(x, ints, rw, w, wh, vec)


class Plan:
    def __init__(self, n, length):
        self.n, self.length = n, length
        self.rows128 = -(-length // 128)
        block_end, head_end = A_ROWS * D, A_ROWS * D + D * HEADS
        self.a_base, self.a_rows, self.h_first, self.h_rows, self.h_off, self.v_first, self.v_rows, self.v_off = ([] for _ in range(8))
        used = 0
        for i in range(n):
            lo, hi = i * length, (i + 1) * length
            base = min(lo, block_end) // D // 16 * 16
            top = -(-min(hi, block_end) // D)
            a_rows = -(-(top - base) // 16) * 16 if lo < block_end else 0
            first = min(max(lo - block_end, 0), D * HEADS) // HEADS
            last = -(-min(max(hi - block_end, 0), D * HEADS) // HEADS)
            h_rows = last - first if hi > block_end and lo < head_end else 0
            v_first = max(lo - head_end, 0) // D
            v_rows = -(-(hi - head_end) // D) - v_first if hi > head_end else 0
            self.a_base.append(base)
            self.a_rows.append(a_rows)
            self.h_first.append(first)
            self.h_rows.append(h_rows)
            self.h_off.append(a_rows)
            self.v_first.append(v_first)
            self.v_rows.append(v_rows)
            self.v_off.append(a_rows + 5 * h_rows)
            used = max(used, a_rows + 5 * h_rows + v_rows)
        self.slot = -(-(used + 1) // 32) * 32

    def at(self, table, me):
        value = jnp.int32(table[0])
        for i in range(1, self.n):
            if table[i] != table[i - 1]:
                value = value + (me >= i).astype(jnp.int32) * (table[i] - table[i - 1])
        return value


MESH = pl.DeviceIdType.MESH


def neighbours(n):
    core = lax.axis_index("tower")
    me = lax.axis_index("dp")
    near_x = me + 1 - 2 * (me % 2)
    near_y = me + 2 - 4 * ((me // 2) % 2)
    return core, me, near_x, near_y


def at(core, index):
    return {"tower": core, "dp": index}


def greet(core, me, near_x, near_y, n):
    barrier = pltpu.get_barrier_semaphore()
    pl.semaphore_signal(barrier, inc=1, device_id=at(1 - core, me), device_id_type=MESH)
    for near in (near_x, near_y):
        pl.semaphore_signal(barrier, inc=1, device_id=at(core, near), device_id_type=MESH)
    for k in range(1, n // 4):
        pl.semaphore_signal(barrier, inc=1, device_id=at(core, (me + 4 * k) % n), device_id_type=MESH)
    return barrier


def place_shard(plan, me, p_ref, slot128, shifted, rolled):
    rows = plan.rows128
    start = me * plan.length
    shift = start % 128
    first = start // 128
    tall = shifted.shape[0]
    height = p_ref.shape[0]
    lane = lax.broadcasted_iota(jnp.int32, (height, 128), 1)
    rolled[0:8] = jnp.zeros((8, 128), F32)
    rolled[8 : 8 + height] = pltpu.roll(p_ref[...], shift, 1)
    shifted[...] = jnp.zeros((tall, 128), F32)
    moved = jnp.where(lane >= shift, rolled[8 : 8 + height], rolled[7 : 7 + height])
    shifted[16 : 16 + height] = moved
    slot128[...] = jnp.zeros(slot128.shape, F32)
    row = lax.broadcasted_iota(jnp.int32, (height, 128), 0)
    base = plan.at(plan.a_base, me)

    @pl.when(plan.at(plan.a_rows, me) > 0)
    def _():
        slot128[pl.ds(first - 2 * base, height)] = jnp.where(row + first < 2 * A_ROWS, moved, 0.0)

    h_first, h_rows, h_off = (plan.at(t, me) for t in (plan.h_first, plan.h_rows, plan.h_off))
    it = lax.broadcasted_iota(jnp.int32, (10, 128), 0)
    lane10 = lax.broadcasted_iota(jnp.int32, (10, 128), 1)

    @pl.loop(0, h_rows)
    def _(k):
        begin = A_ROWS * D + HEADS * (h_first + k) - 128 * first + 128 * 16
        turn = begin % 128
        window = pltpu.roll(shifted[pl.ds(begin // 128, 16)], (128 - turn) % 128, 1)
        value = jnp.where(lane10 < 128 - turn, window[0:10], window[1:11])
        slot128[pl.ds(2 * h_off + 10 * k, 10)] = jnp.where(it * 128 + lane10 < HEADS, value, 0.0)

    v_start = (A_ROWS * D + D * HEADS) // 128
    v_rows, v_off, v_first = (plan.at(t, me) for t in (plan.v_rows, plan.v_off, plan.v_first))
    tall_v = min(height, -(-2 * max(plan.v_rows) // 8) * 8)

    @pl.when(v_rows > 0)
    def _():
        inside = plan.at([max(0, v_start - i * plan.length // 128) for i in range(plan.n)], me)
        to = 2 * v_off + first + inside - v_start - 2 * v_first
        slot128[pl.ds(to, tall_v)] = shifted[pl.ds(16 + inside, tall_v)]


def unpack_rows(plan, i, slot, w, heads, vectors, scratch):
    base, rows = plan.a_base[i], plan.a_rows[i]
    if rows:
        shared = i > 0 and base < plan.a_base[i - 1] + plan.a_rows[i - 1]
        lo = 0
        if shared:
            w[base : base + 16] = w[base : base + 16] + slot[0:16]
            lo = 16
        if rows > lo:
            w[base + lo : base + rows] = slot[lo:rows]
    h_rows, h_off, h_first = plan.h_rows[i], plan.h_off[i], plan.h_first[i]
    v_rows, v_off, v_first = plan.v_rows[i], plan.v_off[i], plan.v_first[i]
    if h_rows or v_rows:
        value = slot.astype(F32)
        scratch[0][...] = value[:, 0:128]
        scratch[1][...] = value[:, 128:D]
    if h_rows:
        shared = i > 0 and plan.h_rows[i - 1] and plan.h_first[i - 1] + plan.h_rows[i - 1] > h_first
        for j in range(5):
            for half in range(2):
                cols = slice(128 * half, 128 * half + 128)
                first = D * j + h_first
                value = scratch[half][pl.ds(h_off + j, h_rows, stride=5)]
                if shared:
                    heads[first : first + 1, cols] = heads[first : first + 1, cols] + value[0:1]
                    if h_rows > 1:
                        heads[first + 1 : first + h_rows, cols] = value[1:h_rows]
                else:
                    heads[first : first + h_rows, cols] = value
    if v_rows:
        shared = v_first and plan.v_first[i - 1] + plan.v_rows[i - 1] > v_first
        shared = shared or (i > 0 and plan.v_rows[i - 1] > 0 and v_first == 0)
        for half in range(2):
            cols = slice(128 * half, 128 * half + 128)
            value = scratch[half][v_off : v_off + v_rows]
            if shared:
                vectors[v_first : v_first + 1, cols] = vectors[v_first : v_first + 1, cols] + value[0:1]
                if v_rows > 1:
                    vectors[v_first + 1 : v_first + v_rows, cols] = value[1:v_rows]
            else:
                vectors[v_first : v_first + v_rows, cols] = value


def split3(value):
    hi = value.astype(BF).astype(F32)
    mid = (value - hi).astype(BF).astype(F32)
    return hi, mid, value - hi - mid


def gather_kernel(plan, p_ref, ints_ref, imp_ref, w, wh, vec, both, rw, slots, slot128, shifted, rolled, scratch, whf, vecf, send, recv):
    n = plan.n
    depth = n // 4
    core, me, near_x, near_y = neighbours(n)
    barrier = greet(core, me, near_x, near_y, n)
    place_shard(plan, me, p_ref, slot128, shifted, rolled)
    pl.semaphore_wait(barrier, depth + 2)
    half = rw.shape[1]
    started = []

    def copy(src, dst, slot, to):
        c = pltpu.make_async_remote_copy(
            src_ref=src, dst_ref=dst, send_sem=send.at[slot], recv_sem=recv.at[slot], device_id=to, device_id_type=MESH
        )
        c.start()
        started.append(c)
        return c

    mine = pl.multiple_of(core * half, half)
    theirs = pl.multiple_of((1 - core) * half, half)
    number = iter(range(1 << 20))
    ints_copy = copy(ints_ref.at[:, pl.ds(theirs, half)], both.at[core], next(number), at(1 - core, me))
    rows = plan.slot
    total = jnp.sum(imp_ref[...].astype(F32), axis=1, keepdims=True)
    lane = lax.broadcasted_iota(jnp.int32, (1, D), 1)
    hi, mid, lo = split3(total)
    left = slot128[pl.ds(0, rows, stride=2)]
    right = slot128[pl.ds(1, rows, stride=2)]
    own = jnp.concatenate([left, right], 1)
    last = jnp.where(lane == 0, hi, jnp.where(lane == 1, mid, jnp.where(lane == 2, lo, 0.0)))
    last_row = lax.broadcasted_iota(jnp.int32, (rows, D), 0) == rows - 1
    slots[core, me] = jnp.where(last_row, last, own).astype(BF)

    def column(index, k):
        return (index + n - 4 * k) % n

    def send_slot(origin, to, lo=0, hi=rows):
        ref = slots.at[core, origin, pl.ds(lo, hi - lo)]
        return copy(ref, ref, next(number), to)

    near_xy = near_x + near_y - me
    cut = rows // 2
    z_in, x_in, y_in, d_in, s_in = {}, {}, {}, {}, []
    for k in sorted(range(1, depth), key=lambda k: (min(k, depth - k), k)):
        z_in[k] = send_slot(me, at(core, (me + 4 * k) % n))
    order = [0] + list(z_in)
    for k in order:
        if k:
            z_in[k].wait_recv()
        x_in[k] = send_slot(column(me, k), at(core, near_x))
        y_in[k] = send_slot(column(me, k), at(core, near_y))
        s_in.append(send_slot(column(me, k), at(1 - core, me)))
    for k in order:
        x_in[k].wait_recv()
        first = send_slot(column(near_x, k), at(core, near_y), 0, cut)
        s_in.append(send_slot(column(near_x, k), at(1 - core, me)))
        y_in[k].wait_recv()
        second = send_slot(column(near_y, k), at(core, near_x), cut, rows)
        s_in.append(send_slot(column(near_y, k), at(1 - core, me)))
        d_in[k] = (first, second)
    for k in order:
        for c in d_in[k]:
            c.wait_recv()
        s_in.append(send_slot(column(near_xy, k), at(1 - core, me)))
    ints_copy.wait_recv()
    both[core] = ints_ref[:, pl.ds(mine, half)]
    for c in s_in:
        c.wait_recv()
    for c in started:
        c.wait_send()
    for t in range(2):
        vecf[...] = jnp.zeros(vecf.shape, F32)
        for i in range(n):
            unpack_rows(plan, i, slots[t, i], w.at[t], whf, vecf, [scratch.at[0], scratch.at[1]])
        for j in range(5):
            wh[t, :, D * j : D * j + D] = whf[D * j : D * j + D].astype(BF)
        vec[t] = vecf[...].astype(BF)
    total = jnp.zeros((1, D), F32)
    for i in range(n):
        tail = slots[0, i, rows - 16 : rows].astype(F32)
        total = total + tail[15:16]
    weight_sum = jnp.sum(jnp.where(lane < 3, total, 0.0), axis=1, keepdims=True)
    rw[...] = jnp.broadcast_to(imp_ref[:, pl.ds(mine, half)].astype(F32) / weight_sum, (8, half))


def gather(plan, p128, ints, imp):
    n, rows = plan.n, plan.slot
    half = ints.shape[1] // 2
    vm = pl.BlockSpec(memory_space=pltpu.VMEM)
    height = p128.shape[0]
    tall = max(2 * rows, height + 40) + 80
    copies = 1 + (n // 4 - 1) + 2 * (n // 4) + 2 * (n // 4) + n
    return pl.pallas_call(
        functools.partial(gather_kernel, plan),
        out_shape=(
            jax.ShapeDtypeStruct((2, A_ROWS, D), BF),
            jax.ShapeDtypeStruct((2, D, HPAD), BF),
            jax.ShapeDtypeStruct((2, 128, D), BF),
            jax.ShapeDtypeStruct((2, 8, half), jnp.int32),
            jax.ShapeDtypeStruct((8, half), F32),
        ),
        in_specs=[vm] * 3,
        out_specs=(vm,) * 5,
        scratch_shapes=[
            pltpu.VMEM((2, n, rows, D), BF),
            pltpu.VMEM((tall, 128), F32),
            pltpu.VMEM((height + 128, 128), F32),
            pltpu.VMEM((height + 8, 128), F32),
            pltpu.VMEM((2, rows, 128), F32),
            pltpu.VMEM((HPAD, D), F32),
            pltpu.VMEM((128, D), F32),
            pltpu.SemaphoreType.DMA((copies,)),
            pltpu.SemaphoreType.DMA((copies,)),
        ],
        compiler_params=pltpu.CompilerParams(
            collective_id=0, has_side_effects=True, vmem_limit_bytes=48 * 1024 * 1024
        ),
    )(p128, ints, imp)


def chunks(height):
    step = max(c for c in range(8, 113, 8) if height % c == 0)
    return [(lo, lo + step) for lo in range(0, height, step)]


def lay_flat(plan, me, slot128, flat, rolled):
    height = rolled.shape[0] - 16
    start = me * plan.length
    shift = start % 128
    first = start // 128
    base = plan.at(plan.a_base, me)
    row = lax.broadcasted_iota(jnp.int32, (height + 8, 128), 0)
    flat[...] = jnp.zeros(flat.shape, F32)

    @pl.when(plan.at(plan.a_rows, me) > 0)
    def _():
        rows = slot128[pl.ds(first - 2 * base, height + 8)]
        flat[16 : 24 + height] = jnp.where(row + first < 2 * A_ROWS, rows, 0.0)

    h_first, h_rows, h_off = (plan.at(t, me) for t in (plan.h_first, plan.h_rows, plan.h_off))
    it = lax.broadcasted_iota(jnp.int32, (16, 128), 0)
    lane = lax.broadcasted_iota(jnp.int32, (16, 128), 1)

    @pl.loop(0, h_rows)
    def _(k):
        begin = A_ROWS * D + HEADS * (h_first + k) - 128 * first + 128 * 16
        turn = begin % 128
        value = slot128[pl.ds(2 * h_off + 10 * k, 16)]
        value = jnp.where(it * 128 + lane < HEADS, value, 0.0)
        value = pltpu.roll(value, turn, 1)
        above = jnp.concatenate([jnp.zeros((8, 128), F32), value], 0)[7:23]
        to = pl.ds(begin // 128, 16)
        flat[to] = flat[to] + jnp.where(lane >= turn, value, above)

    v_start = (A_ROWS * D + D * HEADS) // 128
    v_rows, v_off, v_first = (plan.at(t, me) for t in (plan.v_rows, plan.v_off, plan.v_first))
    tall_v = min(height, -(-2 * max(plan.v_rows) // 8) * 8)

    @pl.when(v_rows > 0)
    def _():
        inside = plan.at([max(0, v_start - i * plan.length // 128) for i in range(plan.n)], me)
        source = 2 * v_off + first + inside - v_start - 2 * v_first
        to = pl.ds(16 + inside, tall_v)
        flat[to] = flat[to] + slot128[pl.ds(source, tall_v)]

    rolled[0 : height + 8] = pltpu.roll(flat[16 : 24 + height], (128 - shift) % 128, 1)
    for lo, hi in chunks(height):
        lane = lax.broadcasted_iota(jnp.int32, (hi - lo, 128), 1)
        flat[lo:hi] = jnp.where(lane < 128 - shift, rolled[lo:hi], rolled[lo + 1 : hi + 1])


def pack_slots(plan, core, gw, gh, gv, rgw, rgh, rgv, slots, sums, vsum, scratch):
    total = gv[core].astype(F32) + rgv[...]
    for kind in range(3):
        vsum[kind * (BLOCKS + 1) : (kind + 1) * (BLOCKS + 1)] = total[kind, 0 : BLOCKS + 1]
    sums[...] = gh[core].astype(F32) + rgh[...].astype(F32)
    for i in range(plan.n):
        base, rows = plan.a_base[i], plan.a_rows[i]
        h_rows, h_off, h_first = plan.h_rows[i], plan.h_off[i], plan.h_first[i]
        v_rows, v_off, v_first = plan.v_rows[i], plan.v_off[i], plan.v_first[i]
        slots[i, rows : plan.slot] = jnp.zeros((plan.slot - rows, D), BF)
        if rows:
            added = gw[core, base : base + rows].astype(F32) + rgw[base : base + rows].astype(F32)
            slots[i, 0:rows] = added.astype(BF)
        if h_rows or v_rows:
            scratch[...] = jnp.zeros(scratch.shape, F32)
            for half in range(2):
                for j in range(5 if h_rows else 0):
                    cols = slice(D * j + 128 * half, D * j + 128 * half + 128)
                    scratch[half, pl.ds(h_off + j, h_rows, stride=5)] = sums[h_first : h_first + h_rows, cols]
                if v_rows:
                    scratch[half, v_off : v_off + v_rows] = vsum[v_first : v_first + v_rows, 128 * half : 128 * half + 128]
            whole = jnp.concatenate([scratch[0], scratch[1]], 1)
            slots[i, rows : plan.slot] = whole[rows:].astype(BF)


def segment_bounds():
    first = [0] + [(CAT + j * D) * D for j in range(BLOCKS + 1)]
    return list(zip(first, first[1:] + [A_ROWS * D + D * HEADS]))


def update_shard(plan, me, p_ref, m_ref, v_ref, outs, flat, squares, sq_z, sq_y, sq_x, push, to_z, to_y, to_x):
    first_out, second_out, new_out, norm_out = outs
    height = p_ref.shape[0]
    start = me * plan.length
    correction = 1.0 - 0.5**STEP
    bounds = segment_bounds()

    def place(lo, hi):
        shape = (hi - lo, 128)
        return 128 * lo + 128 * lax.broadcasted_iota(jnp.int32, shape, 0) + lax.broadcasted_iota(jnp.int32, shape, 1)

    for lo, hi in chunks(height):
        spot = place(lo, hi)
        grad = jnp.where(spot < plan.length, flat[lo:hi], 0.0)
        first_new = 0.5 * m_ref[lo:hi] + 0.5 * grad
        second_new = 0.5 * v_ref[lo:hi] + 0.5 * grad * grad
        first_out[lo:hi] = first_new
        second_out[lo:hi] = second_new
        decay = jnp.where(spot < bounds[-1][1] - start, 0.01 * p_ref[lo:hi], 0.0)
        update = first_new / correction / (jnp.sqrt(second_new / correction) + 1e-06) + decay
        flat[lo:hi] = jnp.where(spot < plan.length, update, 0.0)
        new_out[lo:hi] = p_ref[lo:hi] - 0.5 * update
    squares[...] = jnp.zeros(squares.shape, F32)

    def each_segment(body):
        for j, (first, last) in enumerate(bounds):
            pl.when((first < start + plan.length) & (last > start))(lambda j=j, first=first, last=last: body(j, first, last))

    def square_sums(j, first, last):
        weight, change = jnp.zeros((8, 128), F32), jnp.zeros((8, 128), F32)
        for lo, hi in chunks(height):
            spot = place(lo, hi)
            inside = (spot >= first - start) & (spot < last - start)
            p, u = jnp.where(inside, p_ref[lo:hi], 0.0), jnp.where(inside, flat[lo:hi], 0.0)
            weight = weight + jnp.sum((p * p).reshape(-1, 8, 128), axis=0)
            change = change + jnp.sum((u * u).reshape(-1, 8, 128), axis=0)
        squares[0, j : j + 1] = jnp.sum(weight, axis=0, keepdims=True)
        squares[0, 16 + j : 17 + j] = jnp.sum(change, axis=0, keepdims=True)

    each_segment(square_sums)
    for c in [push(squares.at[0], sq_z.at[k], to) for k, to in enumerate(to_z, 1)]:
        c.wait_recv()
    total = squares[0]
    for k in range(1, len(to_z) + 1):
        total = total + sq_z[k]
    squares[1] = total
    push(squares.at[1], sq_y, to_y).wait_recv()
    squares[2] = squares[1] + sq_y[...]
    push(squares.at[2], sq_x, to_x).wait_recv()
    total = squares[2] + sq_x[...]
    norm = jnp.sqrt(jnp.sum(total, axis=1, keepdims=True))
    sq_y[...] = jnp.broadcast_to(norm, (32, 128))
    line = jnp.sqrt(jnp.sum(jnp.concatenate([total, jnp.zeros((96, 128), F32)], 0).T, axis=0, keepdims=True))
    norm_out[0:1] = line[:, 0:MATS]
    norm_out[1:2] = pltpu.roll(line, 112, 1)[:, 0:MATS]

    def scaled(j, first, last):
        ratio = sq_y[j : j + 1] / sq_y[16 + j : 17 + j]
        for lo, hi in chunks(height):
            spot = place(lo, hi)
            inside = (spot >= first - start) & (spot < last - start)
            new_out[lo:hi] = jnp.where(inside, p_ref[lo:hi] - 0.5 * ratio * flat[lo:hi], new_out[lo:hi])

    each_segment(scaled)


def reduce_kernel(
    plan, gw, gh, gv, st, ig, p_ref, m_ref, v_ref,
    st_out, ig_out, first_out, second_out, new_out, norm_out,
    rgw, rgh, rgv, slots, sums, vsum, scratch, in_d, in_x, in_y, in_z, slot128, flat, rolled, squares, sq_z, sq_y, sq_x,
    send, recv, local,
):
    n, rows = plan.n, plan.slot
    depth, cut = n // 4, plan.slot // 2
    core, me, near_x, near_y = neighbours(n)
    near_xy = near_x + near_y - me
    barrier = greet(core, me, near_x, near_y, n)
    pl.semaphore_wait(barrier, depth + 2)
    half = st.shape[1]
    number = iter(range(1 << 20))
    started = []

    def copy(src, dst, to):
        slot = next(number)
        c = pltpu.make_async_remote_copy(
            src_ref=src, dst_ref=dst, send_sem=send.at[slot], recv_sem=recv.at[slot], device_id=to, device_id_type=MESH
        )
        c.start()
        started.append(c)
        return c

    def column(index, k):
        return (index + n - 4 * k) % n

    sibling = at(1 - core, me)
    early = [
        copy(gw.at[1 - core], rgw, sibling),
        copy(gh.at[1 - core], rgh, sibling),
        copy(gv.at[1 - core], rgv, sibling),
    ]
    mine = pl.ds(pl.multiple_of(core * half, half), half)
    late = [
        copy(st.at[1 - core], st_out.at[mine], sibling),
        copy(ig.at[1 - core], ig_out.at[mine], sibling),
    ]
    stay = [
        pltpu.make_async_copy(st.at[core], st_out.at[mine], local.at[0]),
        pltpu.make_async_copy(ig.at[core], ig_out.at[mine], local.at[1]),
    ]
    for c in stay:
        c.start()
    for c in early:
        c.wait_recv()
    pack_slots(plan, core, gw, gh, gv, rgw, rgh, rgv, slots, sums, vsum, scratch)
    order = list(range(1, depth)) + [0]
    to_x, to_y = at(core, near_x), at(core, near_y)
    halves = {}
    for k in order:
        diagonal = column(near_xy, k)
        halves[k] = (
            copy(slots.at[diagonal, pl.ds(0, cut)], in_d.at[k, pl.ds(0, cut)], to_y),
            copy(slots.at[diagonal, pl.ds(cut, rows - cut)], in_d.at[k, pl.ds(cut, rows - cut)], to_x),
        )
    fulls = {}
    for k in order:
        ox, oy = column(near_x, k), column(near_y, k)
        halves[k][0].wait_recv()
        slots[ox, 0:cut] = (slots[ox, 0:cut].astype(F32) + in_d[k, 0:cut].astype(F32)).astype(BF)
        first = copy(slots.at[ox], in_x.at[k], to_x)
        halves[k][1].wait_recv()
        slots[oy, cut:rows] = (slots[oy, cut:rows].astype(F32) + in_d[k, cut:rows].astype(F32)).astype(BF)
        fulls[k] = (first, copy(slots.at[oy], in_y.at[k], to_y))
    along = {}
    for k in order:
        own = column(me, k)
        for c in fulls[k]:
            c.wait_recv()
        if k:
            total = slots[own].astype(F32) + in_x[k].astype(F32) + in_y[k].astype(F32)
            slots[own] = total.astype(BF)
            along[k] = copy(slots.at[own], in_z.at[k], at(core, own))
    for c in along.values():
        c.wait_recv()
    total = slots[me].astype(F32) + in_x[0].astype(F32) + in_y[0].astype(F32)
    for k in along:
        total = total + in_z[k].astype(F32)
    slot128[...] = jnp.zeros(slot128.shape, F32)
    slot128[pl.ds(0, rows, stride=2)] = total[:, 0:128]
    slot128[pl.ds(1, rows, stride=2)] = total[:, 128:D]
    lay_flat(plan, me, slot128, flat, rolled)

    to_z = [at(core, column(me, k)) for k in range(1, depth)]
    outs = (first_out, second_out, new_out, norm_out)
    update_shard(plan, me, p_ref, m_ref, v_ref, outs, flat, squares, sq_z, sq_y, sq_x, copy, to_z, to_y, to_x)
    for c in late:
        c.wait_recv()
    for c in stay:
        c.wait()
    for c in started:
        c.wait_send()


def reduce_and_update(plan, gw, gh, gv, st, ig, p128, m128, v128):
    n, rows = plan.n, plan.slot
    depth = n // 4
    half = st.shape[1]
    height = p128.shape[0]
    vm = pl.BlockSpec(memory_space=pltpu.VMEM)
    hbm = pl.BlockSpec(memory_space=pl.ANY)
    copies = 5 + 2 * depth + 2 * depth + (depth - 1) + (depth - 1) + 2
    flat32 = jax.ShapeDtypeStruct((height, 128), F32)
    return pl.pallas_call(
        functools.partial(reduce_kernel, plan),
        out_shape=(
            jax.ShapeDtypeStruct((2 * half, D), BF),
            jax.ShapeDtypeStruct((2 * half, D), F32),
            flat32,
            flat32,
            flat32,
            jax.ShapeDtypeStruct((2, MATS), F32),
        ),
        in_specs=[vm] * 3 + [hbm] * 2 + [vm] * 3,
        out_specs=(hbm, hbm, vm, vm, vm, vm),
        scratch_shapes=[
            pltpu.VMEM((A_ROWS, D), BF),
            pltpu.VMEM((D, HPAD), BF),
            pltpu.VMEM(gv.shape[1:], F32),
            pltpu.VMEM((n, rows, D), BF),
            pltpu.VMEM((D, HPAD), F32),
            pltpu.VMEM((40, D), F32),
            pltpu.VMEM((2, rows, 128), F32),
            pltpu.VMEM((depth, rows, D), BF),
            pltpu.VMEM((depth, rows, D), BF),
            pltpu.VMEM((depth, rows, D), BF),
            pltpu.VMEM((depth, rows, D), BF),
            pltpu.VMEM((max(2 * rows, height + 48) + 80, 128), F32),
            pltpu.VMEM((height + 128, 128), F32),
            pltpu.VMEM((height + 16, 128), F32),
            pltpu.VMEM((3, 32, 128), F32),
            pltpu.VMEM((depth, 32, 128), F32),
            pltpu.VMEM((32, 128), F32),
            pltpu.VMEM((32, 128), F32),
            pltpu.SemaphoreType.DMA((copies,)),
            pltpu.SemaphoreType.DMA((copies,)),
            pltpu.SemaphoreType.DMA((2,)),
        ],
        compiler_params=pltpu.CompilerParams(
            collective_id=1, has_side_effects=True, vmem_limit_bytes=48 * 1024 * 1024
        ),
    )(gw, gh, gv, st, ig, p128, m128, v128)


class Copies:
    def __init__(self, send, recv):
        self.send, self.recv, self.made, self.sent = send, recv, [], set()

    def add(self, src, dst, to, recv_slot=None, only=None):
        self.made.append((src, dst, to, recv_slot, only))
        return len(self.made) - 1

    def get(self, number):
        src, dst, to, recv_slot, _ = self.made[number]
        return pltpu.make_async_remote_copy(
            src_ref=src(), dst_ref=dst(), send_sem=self.send.at[number],
            recv_sem=self.recv.at[number] if recv_slot is None else recv_slot(),
            device_id=to(), device_id_type=MESH,
        )

    def start(self, *numbers):
        for number in numbers:
            self.get(number).start()

    def arrive(self, *numbers):
        for number in numbers:
            self.get(number).wait_recv()

    def leave(self, *numbers):
        for number in numbers:
            only = self.made[number][4]
            if number not in self.sent and only is None:
                self.get(number).wait_send()
            elif number not in self.sent:
                pl.when(only())(lambda number=number: self.get(number).wait_send())
            self.sent.add(number)


def fused_fits(plan):
    depth = plan.n // 4
    blocks = 11 * depth + depth - 1
    half = plan.slot // 2
    plain = [b + plan.slot <= A_ROWS for b, h, v in zip(plan.a_base, plan.h_rows, plan.v_rows) if not (h or v)]
    vectors = [rows for rows in plan.v_rows if rows]
    return (
        all(plain)
        and vectors == [3 * (BLOCKS + 1)]
        and plan.n % 4 == 0
        and half >= 32
        and 4 * half <= HPAD
        and 2 * depth * plan.slot <= (BLOCKS + 1) * D
        and -(-blocks // 4) * half <= BLOCKS * (D + 16)
        and max(plan.a_rows) <= plan.slot
    )


def train_kernel(
    plan, x_ref, codes_ref, targets_ref, visits_ref, imp_ref, p_ref, m_ref, v_ref, st_out, ig_out, flat_out, norm_out,
    w, wh, vec, both, away, rw, eye, wt, wht, vt, gsb, xt, mix, xh, gp, rstd, mean, stream, ex, br, dm, d2, lg, dl,
    gw, gh, gv, packed, st_stage, slot128, flat, rolled, vsum, vacc, vin, squares, sq_z, sq_y, sq_x,
    send, recv, z_recv, local, ready,
):
    n, rows = plan.n, plan.slot
    depth, hrows = n // 4, plan.slot // 2
    cut = hrows // 32 * 16
    core, me, near_x, near_y = neighbours(n)
    near_xy = near_x + near_y - me
    width = both.shape[2]
    height = p_ref.shape[0]
    first_out, second_out, new_out = (flat_out.at[i * height : (i + 1) * height] for i in range(3))
    moments = [
        pltpu.make_async_copy(src, dst, local.at[3 + i])
        for i, (src, dst) in enumerate(((m_ref, first_out), (v_ref, second_out)))
    ]
    z_me, j_me = me // 4, me % 4
    copies = Copies(send, recv)
    scratch = [slot128.at[0:rows], slot128.at[rows : 2 * rows]]
    barrier = greet(core, me, near_x, near_y, n)
    mine = pl.multiple_of(core * width, width)
    theirs = pl.multiple_of((1 - core) * width, width)
    x_copy = pltpu.make_async_copy(x_ref.at[pl.ds(mine, width)], st_stage.at[0], local.at[0])
    x_copy.start()
    for c in moments:
        c.start()
    for to, half in ((both.at[core], mine), (away, theirs)):
        cols = pl.ds(half, width)
        to[0:1] = codes_ref[:, cols]
        to[1:2] = targets_ref[0, :, cols]
        to[2:6] = visits_ref[:, cols]
        to[6:7] = targets_ref[1, :, cols]
        to[7:8] = targets_ref[2, :, cols]
    place_shard(plan, me, p_ref, slot128, flat, rolled)

    spare = (BLOCKS + 1) * D

    def slot_part(t, i, lo, count):
        row = pl.multiple_of(spare + rows * (t * depth + i // 4) + lo, 16)
        return xh.at[pl.ds(row, count), pl.ds(pl.multiple_of((i % 4) * D, D), D)]

    def column(index, k):
        return (index + n - 4 * k) % n

    def sibling():
        return at(1 - core, me)

    def same(make, to):
        return copies.add(make, make, to)

    low = core * hrows
    other_low = (1 - core) * hrows
    swap_first = same(lambda: slot_part(core, me, other_low, hrows), sibling)
    swap_second = same(lambda: slot_part(core, me, low, hrows), sibling)
    swap_ints = copies.add(lambda: away, lambda: both.at[core], sibling)
    order = [0] + sorted(range(1, depth), key=lambda k: (min(k, depth - k), k))
    to_x, to_y = (lambda: at(core, near_x)), (lambda: at(core, near_y))
    gathers = []
    for t in range(2):
        g = {"z": {}, "x": {}, "y": {}, "d": {}, "s": []}
        for k in order:
            if k:
                g["z"][k] = same(lambda t=t: slot_part(t, me, low, hrows), lambda k=k: at(core, (me + 4 * k) % n))
            g["x"][k] = same(lambda t=t, k=k: slot_part(t, column(me, k), low, hrows), to_x)
            g["y"][k] = same(lambda t=t, k=k: slot_part(t, column(me, k), low, hrows), to_y)
            g["d"][k] = (
                same(lambda t=t, k=k: slot_part(t, column(near_x, k), low, cut), to_y),
                same(lambda t=t, k=k: slot_part(t, column(near_y, k), low + cut, hrows - cut), to_x),
            )
            g["s", k] = [
                same(lambda t=t, k=k, index=index: slot_part(t, column(index, k), low, hrows), sibling) if index is not me or k else None
                for index in (me, near_x, near_y, near_xy)
            ]
        gathers.append(g)

    def gather_0(t):
        g = gathers[t]
        copies.start(*g["z"].values())
        copies.start(g["x"][0], g["y"][0])

    def gather_1(t):
        g = gathers[t]
        for k in order[1:]:
            copies.arrive(g["z"][k])
            copies.start(g["x"][k], g["y"][k], g["s", k][0])

    def gather_2(t):
        g = gathers[t]
        for k in order:
            copies.arrive(g["x"][k])
            copies.start(g["d"][k][0], g["s", k][1])
            copies.arrive(g["y"][k])
            copies.start(g["d"][k][1], g["s", k][2])

    def gather_3(t):
        g = gathers[t]
        for k in order:
            copies.arrive(*g["d"][k])
            copies.start(g["s", k][3])

    def gather_4(t):
        g = gathers[t]
        for k in order:
            copies.arrive(*(c for c in g["s", k] if c is not None))

    def unpack(t):
        lg[4 * D : 5 * D, 128:D] = jnp.zeros((D, 128), F32)
        vsum[...] = jnp.zeros(vsum.shape, F32)
        for i in range(n):
            row, lane = spare + rows * (t * depth + i // 4), (i % 4) * D
            unpack_rows(plan, i, xh[row : row + rows, lane : lane + D], w.at[t], lg, vsum, scratch)
        for j in range(5):
            wh[t, :, D * j : D * j + D] = lg[D * j : D * j + D].astype(BF)
        vec[t] = vsum[...].astype(BF)

    total = jnp.sum(imp_ref[...].astype(F32), axis=1, keepdims=True)
    lane_d = lax.broadcasted_iota(jnp.int32, (1, D), 1)
    hi, mid, lo = split3(total)
    left = slot128[pl.ds(0, rows, stride=2)]
    right = slot128[pl.ds(1, rows, stride=2)]
    own = jnp.concatenate([left, right], 1)
    last = jnp.where(lane_d == 0, hi, jnp.where(lane_d == 1, mid, jnp.where(lane_d == 2, lo, 0.0)))
    last_row = lax.broadcasted_iota(jnp.int32, (rows, D), 0) == rows - 1
    slot_part(core, me, 0, rows)[...] = jnp.where(last_row, last, own).astype(BF)
    pl.semaphore_wait(barrier, depth + 2)
    copies.start(swap_first, swap_second, swap_ints)
    eye[...] = identity(D)
    x_copy.wait()
    for c in range(0, width, CB):
        xt[0, 0:D, c : c + CB] = nt(eye[...], st_stage[0, c : c + CB, :]).astype(BF)
    copies.arrive(swap_first)
    gather_0(0)
    gather_1(0)
    gather_2(0)
    gather_3(0)
    gather_0(1)
    copies.arrive(swap_second, swap_ints)
    gather_4(0)
    unpack(0)
    total = jnp.zeros((1, D), F32)
    for i in range(n):
        row, lane = spare + rows * (i // 4), (i % 4) * D
        total = total + xh[row + rows - 16 : row + rows, lane : lane + D].astype(F32)[15:16]
    weight_sum = jnp.sum(jnp.where(lane_d < 3, total, 0.0), axis=1, keepdims=True)
    rw[...] = jnp.broadcast_to(imp_ref[:, pl.ds(mine, width)].astype(F32) / weight_sum, (8, width))

    fwd = (eye, w, wh, vec, wt, vt, gsb, xt, mix, xh, gp, rstd, stream, mean, both, width)

    def during_forward(k):
        pl.when(k == 2)(lambda: gather_1(1))
        pl.when(k == 5)(lambda: gather_2(1))
        pl.when(k == 8)(lambda: gather_3(1))

    def emit_states(t):
        for c in range(0, width, CB):
            st_stage[t, c : c + CB, :] = nt(eye[...], xt[t + 1, 0:D, c : c + CB]).astype(BF)

    forward_tower(0, fwd, during_forward)
    gather_4(1)
    copies.leave(*range(len(copies.made)))
    unpack(1)
    forward_tower(1, fwd, None)
    emit_states(0)
    emit_states(1)
    out_rows = pl.ds(mine, width)
    st_copy = copies.add(lambda: st_stage.at[1 - core], lambda: st_out.at[out_rows], sibling)
    copies.start(st_copy)
    st_stay = pltpu.make_async_copy(st_stage.at[core], st_out.at[out_rows], local.at[1])
    st_stay.start()

    packed_of = [i for i in range(n) if plan.h_rows[i] or plan.v_rows[i]]
    owner = plan.v_rows.index(3 * (BLOCKS + 1))

    def block(t, q):
        arena, first = (xh, spare) if t == 0 else (mix, BLOCKS * (D + 16))
        row = pl.multiple_of(first + hrows * (q // 4), 16)
        return arena.at[pl.ds(row, hrows), pl.ds(pl.multiple_of((q % 4) * D, D), D)]

    def piece(t, q, lo, count):
        arena, first = (xh, spare) if t == 0 else (mix, BLOCKS * (D + 16))
        row = pl.multiple_of(first + hrows * (q // 4) + lo, 16)
        return arena.at[pl.ds(row, count), pl.ds(pl.multiple_of((q % 4) * D, D), D)]

    def slot_half(t, i, lo):
        if i in packed_of:
            return packed.at[packed_of.index(i), pl.ds(pl.multiple_of(lo, 16), hrows)]
        return gw.at[t, pl.ds(pl.multiple_of(plan.a_base[i] + lo, 16), hrows)]

    j_x, j_y, j_d = near_x % 4, near_y % 4, near_xy % 4
    jobs = {}
    for t in range(2):
        for zz in range(depth):
            q = 11 * zz
            job = {"q": q}
            job["swap"] = [
                copies.add(lambda t=t, i=4 * zz + j: slot_half(t, i, other_low), lambda t=t, q=q + j: block(t, q), sibling)
                for j in range(4)
            ]
            job["d"] = (
                copies.add(lambda t=t, q=q: piece(t, q + 4 + j_d, 0, cut), lambda t=t, q=q: piece(t, q + 8, 0, cut), to_y),
                copies.add(lambda t=t, q=q: piece(t, q + 4 + j_d, cut, hrows - cut), lambda t=t, q=q: piece(t, q + 8, cut, hrows - cut), to_x),
            )
            job["x"] = copies.add(lambda t=t, q=q: block(t, q + 4 + j_x), lambda t=t, q=q: block(t, q + 9), to_x)
            job["y"] = copies.add(lambda t=t, q=q: block(t, q + 4 + j_y), lambda t=t, q=q: block(t, q + 10), to_y)
            job["z"] = copies.add(
                lambda t=t, q=q: block(t, q + 4 + j_me),
                lambda t=t, zz=zz: block(t, 11 * depth + (zz + depth - z_me) % depth - 1),
                lambda zz=zz: at(core, 4 * zz + j_me),
                lambda t=t, zz=zz: z_recv.at[t * depth + (zz + depth - z_me) % depth],
                lambda zz=zz: z_me != zz,
            )
            jobs[t, zz] = job

    def pack(t, planes):
        wanted = [i for i in packed_of if i // 4 in planes]
        for i in wanted:
            a_rows, h_rows, h_off, h_first = plan.a_rows[i], plan.h_rows[i], plan.h_off[i], plan.h_first[i]
            to = packed.at[packed_of.index(i)]
            for part in scratch:
                part[...] = jnp.zeros(part.shape, F32)
            lo16, hi16 = h_first // 16 * 16, -(-(h_first + h_rows) // 16) * 16
            for half in range(2):
                for j in range(5 if h_rows else 0):
                    cols = slice(D * j + 128 * half, D * j + 128 * half + 128)
                    value = gh[t, lo16:hi16, cols].astype(F32)[h_first - lo16 : h_first - lo16 + h_rows]
                    scratch[half][pl.ds(h_off + j, h_rows, stride=5)] = value
            whole = jnp.concatenate([scratch[0][...], scratch[1][...]], 1)
            to[a_rows:rows] = whole[a_rows:].astype(BF)
            if a_rows:
                to[0:a_rows] = gw[t, plan.a_base[i] : plan.a_base[i] + a_rows]

    def plus(*refs):
        value = refs[0][...].astype(F32)
        for ref in refs[1:]:
            value = value + ref[...].astype(F32)
        return value

    def sum_0(t, zz):
        copies.start(*jobs[t, zz]["swap"])

    def sum_1(t, zz):
        job = jobs[t, zz]
        for j in range(4):
            copies.arrive(job["swap"][j])
            block(t, job["q"] + 4 + j)[...] = plus(slot_half(t, 4 * zz + j, low), block(t, job["q"] + j)).astype(BF)
        copies.start(*job["d"])

    def sum_2(t, zz):
        job = jobs[t, zz]
        q = job["q"]
        copies.arrive(job["d"][0])
        target = piece(t, q + 4 + j_x, 0, cut)
        target[...] = plus(target, piece(t, q + 8, 0, cut)).astype(BF)
        copies.start(job["x"])
        copies.arrive(job["d"][1])
        target = piece(t, q + 4 + j_y, cut, hrows - cut)
        target[...] = plus(target, piece(t, q + 8, cut, hrows - cut)).astype(BF)
        copies.start(job["y"])

    def sum_3(t, zz):
        job = jobs[t, zz]
        q = job["q"]
        copies.arrive(job["x"], job["y"])
        value = plus(block(t, q + 4 + j_me), block(t, q + 9), block(t, q + 10))

        @pl.when(z_me == zz)
        def _():
            partial(t)[...] = value

        @pl.when(z_me != zz)
        def _():
            block(t, q + 4 + j_me)[...] = value.astype(BF)
            copies.start(job["z"])

    def sum_4(t):
        for k in range(1, depth):
            src = block(t, 11 * depth + k - 1)
            pltpu.make_async_remote_copy(
                src_ref=src, dst_ref=src, send_sem=send.at[0], recv_sem=z_recv.at[t * depth + k], device_id=sibling(), device_id_type=MESH
            ).wait_recv()
            partial(t)[...] = partial(t)[...] + src[...].astype(F32)

    def final(h):
        return lg.at[pl.ds(pl.multiple_of(h * hrows, 8), hrows)]

    def partial(t):
        return lg.at[pl.ds(pl.multiple_of((2 + t) * hrows, 8), hrows)]

    def vector_step(step):
        sources = [gv.at[1 - core], vacc.at[0], vacc.at[1], vacc.at[2]]
        targets = [[sibling], [to_x], [to_y], [lambda k=k: at(core, (me + 4 * k) % n) for k in range(1, depth)]]
        if step:
            base = gv[core] if step == 1 else vacc[step - 2]
            for number, k in vector_copies[-1]:
                copies.arrive(number)
                base = base + vin[k]
            vacc[step - 1] = base
        if step < 4:
            slots = range(step, step + 1) if step < 3 else range(3, 2 + depth)
            started = []
            for k, to in zip(slots, targets[step]):
                number = copies.add(lambda step=step: sources[step], lambda k=k: vin.at[k], to)
                copies.start(number)
                started.append((number, k))
            vector_copies.append(started)

    vector_copies = []
    last_swap = copies.add(lambda: partial(1 - core), lambda: final(core), sibling)
    peers = [(1 - core, me), (core, near_x), (core, near_y)] + [(core, (me + 4 * k) % n) for k in range(1, depth)]

    bwd = (eye, w, wh, vec, wht, vt, gsb, xt, mix, xh, gp, rstd, stream, ex, br, dm, d2, lg, dl, both, rw, gw, gh, gv, dm, width)
    ig_copies = [copies.add(lambda: dm, lambda: ig_out.at[out_rows], sibling, None, lambda t=t: core != t) for t in range(2)]

    def ig_local():
        return pltpu.make_async_copy(dm, ig_out.at[out_rows], local.at[2])

    def emit_inputs(t):
        pl.when(core == t)(lambda: ig_local().start())
        pl.when(core != t)(lambda: copies.start(ig_copies[t]))

    def free_inputs(t):
        pl.when(core == t)(lambda: ig_local().wait())
        pl.when(core != t)(lambda: copies.get(ig_copies[t]).wait_send())

    ex[...] = jnp.zeros_like(ex)
    backward_tower(1, bwd, None, None)
    emit_inputs(1)
    for to_core, to_index in peers:
        pl.semaphore_signal(ready, inc=1, device_id=at(to_core, to_index), device_id_type=MESH)

    def after_head():
        pl.semaphore_wait(ready, len(peers))
        pack(1, range(depth))
        for zz in range(depth):
            sum_0(1, zz)

    def during_backward(i):
        def at_step(step, *calls):
            def run():
                for f, *args in calls:
                    f(*args)

            pl.when(i == step)(run)

        planes = range(depth)

        def release():
            copies.leave(*(jobs[1, i // 4]["swap"][i % 4] for i in packed_of))

        at_step(1, *((sum_1, 1, zz) for zz in planes))
        at_step(2, (release,), (pack, 0, (depth - 1,)), (sum_0, 0, depth - 1))
        at_step(3, *((sum_2, 1, zz) for zz in planes))
        for zz in range(1, depth - 1):
            done = BLOCKS + 1 - 4 * zz + 1
            if done < BLOCKS:
                at_step(done, (pack, 0, (zz,)), (sum_0, 0, zz))
            if done + 1 < BLOCKS:
                at_step(done + 1, (sum_1, 0, zz))
            if done + 2 < BLOCKS:
                at_step(done + 2, (sum_2, 0, zz))
        at_step(4, (sum_1, 0, depth - 1))
        at_step(5, *((sum_3, 1, zz) for zz in planes))
        at_step(6, (sum_2, 0, depth - 1))
        at_step(8, (sum_4, 1), (sum_3, 0, depth - 1))

    backward_tower(0, bwd, after_head, during_backward, lambda: free_inputs(1))
    emit_inputs(0)
    done = {zz: BLOCKS + 1 - 4 * zz + 1 for zz in range(1, depth - 1)}
    for zz in sorted(done, reverse=True):
        if done[zz] >= BLOCKS:
            pack(0, (zz,))
            sum_0(0, zz)
    pack(0, (0,))
    sum_0(0, 0)
    vector_step(0)
    for zz in sorted(done, reverse=True):
        if done[zz] + 1 >= BLOCKS:
            sum_1(0, zz)
        if done[zz] + 2 >= BLOCKS:
            sum_2(0, zz)
    sum_1(0, 0)
    vector_step(1)
    for zz in sorted(done, reverse=True):
        sum_3(0, zz)
    sum_2(0, 0)
    vector_step(2)
    sum_3(0, 0)
    vector_step(3)
    sum_4(0)
    copies.start(last_swap)
    final(core)[...] = partial(core)[...]
    vector_step(4)
    copies.arrive(last_swap)

    slot128[...] = jnp.zeros(slot128.shape, F32)
    for h in range(2):
        slot128[pl.ds(2 * hrows * h, hrows, stride=2)] = final(h)[:, 0:128]
        slot128[pl.ds(2 * hrows * h + 1, hrows, stride=2)] = final(h)[:, 128:D]

    @pl.when(me == owner)
    def _():
        for kind in range(3):
            first = 2 * (plan.v_off[owner] + kind * (BLOCKS + 1))
            for h in range(2):
                value = vacc[3, kind, 0 : BLOCKS + 1, 128 * h : 128 * h + 128]
                slot128[pl.ds(first + h, BLOCKS + 1, stride=2)] = value

    def push(src, dst, to):
        number = copies.add(lambda: src, lambda: dst, lambda: to)
        copies.start(number)
        return copies.get(number)

    lay_flat(plan, me, slot128, flat, rolled)
    for c in moments:
        c.wait()
    update_shard(
        plan, me, p_ref, first_out, second_out, (first_out, second_out, new_out, norm_out),
        flat, squares, sq_z, sq_y, sq_x, push, [at(core, (me + 4 * k) % n) for k in range(1, depth)], to_y(), to_x(),
    )
    copies.arrive(st_copy)
    pl.when(core == 0)(lambda: copies.arrive(ig_copies[0]))
    pl.when(core == 1)(lambda: copies.arrive(ig_copies[1]))
    free_inputs(0)
    st_stay.wait()
    copies.sent.update(ig_copies)
    copies.leave(*range(len(copies.made)))


def train(plan, latent, codes, targets, visits, imp, p128, m128, v128):
    n, rows = plan.n, plan.slot
    depth, hrows = n // 4, rows // 2
    width = codes.shape[1] // 2
    height = p128.shape[0]
    vm = pl.BlockSpec(memory_space=pltpu.VMEM)
    hbm = pl.BlockSpec(memory_space=pl.ANY)
    packed = sum(1 for h, v in zip(plan.h_rows, plan.v_rows) if h or v)
    return pl.pallas_call(
        functools.partial(train_kernel, plan),
        out_shape=(
            jax.ShapeDtypeStruct((2 * width, D), BF),
            jax.ShapeDtypeStruct((2 * width, D), F32),
            jax.ShapeDtypeStruct((3 * height, 128), F32),
            jax.ShapeDtypeStruct((2, MATS), F32),
        ),
        in_specs=[hbm] + [vm] * 5 + [hbm] * 2,
        out_specs=(hbm, hbm, vm, vm),
        scratch_shapes=[
            pltpu.VMEM((2, A_ROWS, D), BF),
            pltpu.VMEM((2, D, HPAD), BF),
            pltpu.VMEM((2, 128, D), BF),
            pltpu.VMEM((2, 8, width), jnp.int32),
            pltpu.VMEM((8, width), jnp.int32),
            pltpu.VMEM((8, width), F32),
            *work_scratch(width),
            pltpu.VMEM((2, A_ROWS, D), BF),
            pltpu.VMEM((2, D, HPAD), BF),
            pltpu.VMEM((2, 3, 16, D), F32),
            pltpu.VMEM((packed, rows, D), BF),
            pltpu.VMEM((2, width, D), BF),
            pltpu.VMEM((max(2 * rows, height + 48) + 80, 128), F32),
            pltpu.VMEM((height + 128, 128), F32),
            pltpu.VMEM((height + 16, 128), F32),
            pltpu.VMEM((128, D), F32),
            pltpu.VMEM((4, 3, 16, D), F32),
            pltpu.VMEM((2 + depth, 3, 16, D), F32),
            pltpu.VMEM((3, 32, 128), F32),
            pltpu.VMEM((depth, 32, 128), F32),
            pltpu.VMEM((32, 128), F32),
            pltpu.VMEM((32, 128), F32),
            pltpu.SemaphoreType.DMA((11 * n,)),
            pltpu.SemaphoreType.DMA((11 * n,)),
            pltpu.SemaphoreType.DMA((2 * depth,)),
            pltpu.SemaphoreType.DMA((5,)),
            pltpu.SemaphoreType.REGULAR,
        ],
        compiler_params=pltpu.CompilerParams(
            collective_id=2, has_side_effects=True, vmem_limit_bytes=63 * 1024 * 1024
        ),
    )(latent, codes, targets, visits, imp, p128, m128, v128)


def on_device(latent, codes, targets, visits, importance, params, first_moment, second_moment):
    me = lax.axis_index("tower")
    row_count = latent.shape[0]
    half = row_count // 2
    shard_len = params.shape[1]
    plan = Plan(lax.axis_size("dp"), shard_len)
    height = -(-plan.rows128 // 8) * 8
    p128, m128, v128 = (
        jnp.pad(v, ((0, 0), (0, 128 * height - shard_len))).reshape(height, 128) for v in (params, first_moment, second_moment)
    )
    if fused_fits(plan):
        states_out, inputs_out, flat, norms = train(
            plan, latent, codes, targets.transpose(1, 0, 2), visits[0].T, importance[None], p128, m128, v128
        )
    else:
        ints = jnp.concatenate([codes, targets[0, :1], visits[0].T, targets[0, 1:]], 0)
        x = lax.dynamic_slice_in_dim(latent, me * half, half, 0)
        w, wh, vec, both, rw = gather(plan, p128, ints, importance[None])
        st, ig, gw, gh, gv = compute(x, both, rw, w, wh, vec)
        states_out, inputs_out, *flat, norms = reduce_and_update(plan, gw, gh, gv, st, ig, p128, m128, v128)
        flat = jnp.concatenate(flat)
    flat = flat.reshape(1, -1)
    first, second, new = (flat[:, i * 128 * height : i * 128 * height + shard_len] for i in range(3))
    return (states_out[None], inputs_out[None], first, second, new, new.astype(BF), norms[None])


def solution(mesh):
    in_specs = (
        P("dp", None),
        P("tower", "dp"),
        P("tower", None, "dp"),
        P("tower", "dp", None),
        P("dp"),
        P("tower", "dp"),
        P("tower", "dp"),
        P("tower", "dp"),
    )
    out_specs = (
        P("tower", "dp", None),
        P("tower", "dp", None),
        P("tower", "dp"),
        P("tower", "dp"),
        P("tower", "dp"),
        P("tower", "dp"),
        P("tower", None, None),
    )
    return jax.shard_map(
        on_device, mesh=mesh, in_specs=in_specs, out_specs=out_specs, check_vma=False
    )
```

```python
import functools

import jax
import jax.numpy as jnp
from jax import lax
from jax.experimental import pallas as pl
from jax.experimental.pallas import tpu as pltpu
from jax.sharding import PartitionSpec as P

D = 256
CODES = 32
BINS = 601
BLOCKS = 10
STEP = 5
HEADS = 1238
MATS = 12
P_SIZE = 1054464
HPAD = 1280
CAT = D + CODES
A_ROWS = CAT + BLOCKS * D
BF = jnp.bfloat16
F32 = jnp.float32
GELU_C = 0.7978845608028654
GELU_K = 0.044715


def nn(a, b):
    return jnp.dot(a, b, preferred_element_type=F32)


def nt(a, b):
    return lax.dot_general(a, b, (((1,), (1,)), ((), ())), preferred_element_type=F32)


def identity(n):
    return (lax.broadcasted_iota(jnp.int32, (n, n), 0) == lax.broadcasted_iota(jnp.int32, (n, n), 1)).astype(BF)


def twice(v):
    return jnp.concatenate([v, v], 1)


def column_stats(ref, cs):
    total = jnp.sum(ref[:, cs], axis=0, keepdims=True)
    mean = total * (1.0 / D)
    square = jnp.zeros((8, mean.shape[1]), F32)
    for r in range(0, D, 32):
        cen = ref[r : r + 32, cs] - mean
        square = square + jnp.sum((cen * cen).reshape(4, 8, -1), axis=0)
    var = jnp.sum(square, axis=0, keepdims=True) * (1.0 / D)
    return mean, lax.rsqrt(var + 1e-05)


def norm_act(src, cs, gsb, xh_ref, gp_ref, rstd_ref, out):
    mean, rstd = column_stats(src, cs)
    rstd_ref[:, cs] = rstd
    for r in range(0, D, 32):
        rs = slice(r, r + 32)
        xh = (src[rs, cs] - mean) * rstd
        xh_ref[rs, cs] = xh.astype(BF)
        y = xh * twice(gsb[rs, 0:128]) + twice(gsb[rs, 128:256])
        y2 = y * y
        p = y2 * (GELU_C * GELU_K) + GELU_C
        t = jnp.tanh(y * p)
        q = t * 0.5 + 0.5
        a = y * q
        out(rs, a)
        slope = q + (a - a * q) * (p * 6.0 - 4.0 * GELU_C)
        gp_ref[rs, cs] = slope.astype(BF)


def broadcast_vectors(vt, rows):
    k = lax.broadcasted_iota(jnp.int32, (128, 128), 0)
    picks = jnp.concatenate([(k == row).astype(BF) for row in rows], 1)
    return nn(vt, picks)


def head_stage(cs, lg, dl, ints, rw):
    width = rw.shape[1]
    it8 = lax.broadcasted_iota(jnp.int32, (8, width), 0)
    low = -jnp.inf
    b75, b150, b154 = lg[600:608], lg[1200:1208], lg[1232:1240]

    def top(block):
        return jnp.max(block, axis=0, keepdims=True)

    def top_range(lo, hi):
        best = lg[lo : lo + 8]
        for r in range(lo + 8, hi, 8):
            best = jnp.maximum(best, lg[r : r + 8])
        return best

    max_v = top(jnp.maximum(top_range(0, 600), jnp.where(it8 < 1, b75, low)))
    max_r = top(
        jnp.maximum(
            jnp.maximum(top_range(608, 1200), jnp.where(it8 >= 1, b75, low)),
            jnp.where(it8 < 2, b150, low),
        )
    )
    max_c = top(
        jnp.maximum(
            jnp.maximum(top_range(1208, 1232), jnp.where(it8 >= 2, b150, low)),
            jnp.where(it8 < 2, b154, low),
        )
    )
    in_policy = (it8 >= 2) & (it8 < 6)
    max_p = top(jnp.where(in_policy, b154, low))

    def exp_range(lo, hi, best):
        acc = jnp.zeros((8, width), F32)
        for r in range(lo, hi, 8):
            e = jnp.exp(lg[r : r + 8] - best)
            lg[r : r + 8] = e
            acc = acc + e
        return acc

    e75 = jnp.exp(b75 - jnp.where(it8 < 1, max_v, max_r))
    e150 = jnp.exp(b150 - jnp.where(it8 < 2, max_r, max_c))
    e154 = jnp.exp(b154 - jnp.where(it8 < 2, max_c, max_p))

    def total(acc):
        return rw / jnp.sum(acc, axis=0, keepdims=True)

    inv_v = total(exp_range(0, 600, max_v) + jnp.where(it8 < 1, e75, 0.0))
    inv_r = total(exp_range(608, 1200, max_r) + jnp.where(it8 >= 1, e75, 0.0) + jnp.where(it8 < 2, e150, 0.0))
    inv_c = total(exp_range(1208, 1232, max_c) + jnp.where(it8 >= 2, e150, 0.0) + jnp.where(it8 < 2, e154, 0.0))
    inv_p = total(jnp.where(in_policy, e154, 0.0))
    hit_v = ints[1:2]
    hit_r = ints[6:7] + BINS
    hit_c = ints[7:8] + 2 * BINS
    counts = jnp.where(in_policy, ints.astype(F32), 0.0)
    share = counts * (rw / jnp.sum(counts, axis=0, keepdims=True))

    def minus(value, lo, *hits):
        at = lax.broadcasted_iota(jnp.int32, value.shape, 0)
        for hit in hits:
            value = value - jnp.where(at == hit - lo, rw, 0.0)
        return value

    d75 = minus(e75 * jnp.where(it8 < 1, inv_v, inv_r), 600, hit_v, hit_r)
    d150 = minus(e150 * jnp.where(it8 < 2, inv_r, inv_c), 1200, hit_r, hit_c)
    d154 = minus(e154 * jnp.where(it8 < 2, inv_c, inv_p), 1232, hit_c) - share
    d154 = jnp.where(it8 < 6, d154, 0.0)

    def emit(lo, hi, inv, hit):
        for r in range(lo, hi, 16):
            dl[r : r + 16, cs] = minus(lg[r : r + 16] * inv, r, hit).astype(BF)

    def pair(first, second):
        return jnp.concatenate([first, second], 0).astype(BF)

    emit(0, 592, inv_v, hit_v)
    dl[592:608, cs] = pair(minus(lg[592:600] * inv_v, 592, hit_v), d75)
    emit(608, 1200, inv_r, hit_r)
    dl[1200:1216, cs] = pair(d150, minus(lg[1208:1216] * inv_c, 1208, hit_c))
    emit(1216, 1232, inv_c, hit_c)
    dl[1232:1248, cs] = pair(d154, jnp.zeros_like(d154))
    dl[1248:HPAD, cs] = jnp.zeros((HPAD - 1248, width), BF)


CB = 256
GROUP = 2


def spread(v, cs):
    return jnp.concatenate([v] * ((cs.stop - cs.start) // 128), 1)


def saved_views(t, mix, xh):
    def mixed(k):
        return mix.at[pl.ds(pl.multiple_of((t * BLOCKS + k - 1) * (D + 16), 16), D + 16)]

    def unit(k):
        return xh.at[pl.ds(pl.multiple_of((t * (BLOCKS + 1) + k) * D, D), D)]

    return mixed, unit


def forward_tower(t, refs, during=None):
    (eye, w, wh, vec, wct, wt, vt, gsb, xt, mix, xh, gp, rstd, stream, ints, width) = refs
    blocks = [slice(c, c + CB) for c in range(0, width, CB)]
    per = min(GROUP, len(blocks))
    groups = [slice(c, c + per * CB) for c in range(0, width, per * CB)]
    mixed, unit = saved_views(t, mix, xh)

    def prefetch(k):
        gsb[k % 2] = broadcast_vectors(vt[...], (k, k + BLOCKS + 1, k + 2 * BLOCKS + 2))
        row = pl.multiple_of(CAT + (k - 1) * D, 32)
        wt[k % 2] = nt(eye[...], w[t, pl.ds(row, D)]).astype(BF)

    def stage(k, c):
        cs = blocks[c]

        def keep(rs, a):
            mixed(k)[rs, cs] = a.astype(BF)

        norm_act(stream, cs, gsb.at[k % 2], unit(k), gp.at[t, k], rstd.at[pl.ds(t * (BLOCKS + 1) + k, 1)], keep)

    def product(k, group):
        return nn(wt[k % 2], mixed(k)[0:D, groups[group]])

    def add(k, group, pre):
        cs = groups[group]
        stream[:, cs] = stream[:, cs] + pre + spread(gsb[k % 2, :, 256:384], cs)

    vt[...] = nt(eye[...], vec[t]).astype(BF)
    wt[0] = nt(eye[...], w[t, 0:D]).astype(BF)
    wct[...] = nt(eye[...], w[t, D:CAT]).astype(BF)
    gsb[0] = broadcast_vectors(vt[...], (0, BLOCKS + 1, 2 * BLOCKS + 2))
    prefetch(1)
    for cs in blocks:
        it = lax.broadcasted_iota(jnp.int32, (CODES, CB), 0)
        xt[t, D:CAT, cs] = (it == ints[t, 0:1, cs]).astype(BF)
        xt[t, CAT : CAT + 16, cs] = jnp.ones((16, CB), BF)
    for c, cs in enumerate(blocks):
        pre = nn(wt[0], xt[t, 0:D, cs]) + nn(wct[...], xt[t, D:CAT, cs])
        stream[:, cs] = pre + twice(gsb[0, :, 256:384])

        def keep(rs, a):
            stream[rs, cs] = a

        norm_act(stream, cs, gsb.at[0], unit(0), gp.at[t, 0], rstd.at[pl.ds(t * (BLOCKS + 1), 1)], keep)

    def layer(k, more):
        if more:
            prefetch(k + 1)
        mixed(k)[D : D + 16, :] = jnp.ones((16, width), BF)
        for group in range(len(groups)):
            pre = product(k, group)
            ahead = group + 1 < len(groups)
            if ahead or more:
                for c in range(per):
                    stage(k if ahead else k + 1, (group + 1) % len(groups) * per + c)
            add(k, group, pre)

    for c in range(per):
        stage(1, c)

    @pl.loop(1, BLOCKS)
    def _(k):
        if during is not None:
            during(k)
        layer(k, True)

    layer(BLOCKS, False)
    for cs in blocks:
        xt[t + 1, 0:D, cs] = stream[:, cs].astype(BF)


def backward_act(cs, grad, gain, gp_ref, xh_ref, acc):
    s1 = jnp.zeros((8, CB), F32)
    s2 = jnp.zeros((8, CB), F32)
    for r in range(0, D, 16):
        rs = slice(r, r + 16)
        g = twice(gain[rs])
        dy = grad[rs, :] * gp_ref[rs, cs].astype(F32)
        prod = dy * xh_ref[rs, cs].astype(F32)
        back = dy * g
        grad[rs, :] = back
        prod_g = prod * g
        s1 = s1 + (back[0:8] + back[8:16])
        s2 = s2 + (prod_g[0:8] + prod_g[8:16])
        acc[0, rs] = acc[0, rs] + (prod[:, 0:128] + prod[:, 128:CB])
        acc[1, rs] = acc[1, rs] + (dy[:, 0:128] + dy[:, 128:CB])
    m1 = jnp.sum(s1, axis=0, keepdims=True) * (1.0 / D)
    m2 = jnp.sum(s2, axis=0, keepdims=True) * (1.0 / D)
    return m1, m2


def backward_tower(t, refs, after_head=None, during=None, before_product=None, after_weights=None):
    (eye, w, wh, vec, wht, vt, gsb, xt, mix, xh, gp, rstd, ds, ex, br, dm, acc, lg, dl, ints, rw, gw, gh, gv, ig, width) = refs
    blocks = [slice(c, c + CB) for c in range(0, width, CB)]
    per = min(GROUP, len(blocks))
    groups = [slice(c, c + per * CB) for c in range(0, width, per * CB)]
    mixed, unit = saved_views(t, mix, xh)
    vt[...] = nt(eye[...], vec[t]).astype(BF)
    for h in range(0, HPAD, D):
        wht[h : h + D, :] = nt(eye[...], wh[t, :, h : h + D]).astype(BF)

    @pl.loop(0, width // CB)
    def _(c):
        cs = pl.ds(pl.multiple_of(c * CB, CB), CB)
        lg[...] = nn(wht[...], xt[t + 1, 0:D, cs])
        head_stage(cs, lg, dl, ints[t, :, cs], rw[0:1, cs])
        value = nn(wh[t], dl[:, cs]) + ex[:, cs]
        ds[:, cs] = value
        br[BLOCKS % 2, :, cs] = value.astype(BF)

    for h in range(0, HPAD, D):
        gh[t, :, h : h + D] = nt(xt[t + 1, 0:D, :], dl[h : h + D]).astype(BF)
    if after_head is not None:
        after_head()
    acc[...] = jnp.zeros(acc.shape, F32)
    ones = jnp.ones((16, 128), BF)

    def part(c):
        return dm.at[c * D : c * D + D]

    def gains(k):
        gsb[k % 2, :, 0:128] = broadcast_vectors(vt[...], (k,))

    def row_sums(k):
        for kind in range(2):
            gv[t, kind, pl.ds(k, 1), :] = nt(ones, acc[k % 2, kind].astype(BF))[0:1]
        acc[k % 2] = jnp.zeros(acc.shape[1:], F32)

    def product(k, group):
        row = pl.multiple_of(CAT + (k - 1) * D, 32)
        back = nn(w[t, pl.ds(row, D)], br[k % 2, :, groups[group]])
        for c in range(per):
            part(group * per + c)[...] = back[:, c * CB : c * CB + CB]

    def stage(k, c, first):
        cs = blocks[c]
        m1, m2 = backward_act(cs, part(c), gsb.at[k % 2, :, 0:128], gp.at[t, k], unit(k), acc.at[k % 2])
        rs1 = rstd[pl.ds(t * (BLOCKS + 1) + k, 1), cs]
        m1 = m1 * rs1
        m2 = m2 * rs1
        for r in range(0, D, 32):
            rs = slice(r, r + 32)
            back = part(c)[rs, :] * rs1 - m1 - unit(k)[rs, cs].astype(F32) * m2
            if first:
                br[0, rs, cs] = back.astype(BF)
            else:
                value = ds[rs, cs] + back
                ds[rs, cs] = value
                br[(k + 1) % 2, rs, cs] = value.astype(BF)

    if before_product is not None:
        before_product()
    gains(BLOCKS)
    product(BLOCKS, 0)

    @pl.loop(0, BLOCKS)
    def _(i):
        k = BLOCKS - i
        if during is not None:
            during(i)
        gains(k - 1)
        for group in range(len(groups)):
            if group + 1 < len(groups):
                product(k, group + 1)
            for c in range(per):
                stage(k, group * per + c, False)
            if group == 0:
                full = nt(mixed(k)[...], br[k % 2])
                row = pl.multiple_of(CAT + (k - 1) * D, 32)
                gw[t, pl.ds(row, D), :] = full[0:D].astype(BF)
                gv[t, 2, pl.ds(k, 1), :] = full[D : D + 1]
                row_sums(k + 1)
                product(k - 1, 0)

    for c, cs in enumerate(blocks):
        part(c)[...] = ds[:, cs]
        stage(0, c, True)
    row_sums(1)
    row_sums(0)
    full = nt(xt[t], br[0])
    gw[t, 0:CAT, :] = full[0:CAT].astype(BF)
    gv[t, 2, 0:1, :] = full[CAT : CAT + 1]
    if after_weights is not None:
        after_weights()
    for cs in blocks:
        back = nn(w[t, 0:D], br[0, :, cs])
        ex[:, cs] = back
        ig[cs, :] = back.T


def compute_kernel(x_ref, ints, rw, w, wh, vec, st, ig, gw, gh, gv, eye, wct, wt, wht, vt, gsb, xt, mix, xh, gp, rstd, stream, ex, br, dm, acc, lg, dl):
    width = x_ref.shape[0]
    eye[...] = identity(D)
    for c in range(0, width, CB):
        cs = slice(c, c + CB)
        xt[0, 0:D, cs] = nt(eye[...], x_ref[cs, :]).astype(BF)
    fwd = (eye, w, wh, vec, wct, wt, vt, gsb, xt, mix, xh, gp, rstd, stream, ints, width)
    @pl.loop(0, 2)
    def _(t):
        forward_tower(t, fwd)

        @pl.loop(0, width // CB)
        def _(c):
            cs = pl.ds(pl.multiple_of(c * CB, CB), CB)
            st[t, cs, :] = nt(eye[...], xt[t + 1, 0:D, cs]).astype(BF)

    ex[...] = jnp.zeros_like(ex)

    @pl.loop(0, 2)
    def _(i):
        t = 1 - i
        backward_tower(
            t,
            (eye, w, wh, vec, wht, vt, gsb, xt, mix, xh, gp, rstd, stream, ex, br, dm, acc, lg, dl, ints, rw, gw, gh, gv, ig.at[t], width),
        )


def work_scratch(width):
    return [
        pltpu.VMEM((D, D), BF),
        pltpu.VMEM((D, CODES), BF),
        pltpu.VMEM((2, D, D), BF),
        pltpu.VMEM((HPAD, D), BF),
        pltpu.VMEM((D, 128), BF),
        pltpu.VMEM((2, D, 384), F32),
        pltpu.VMEM((3, CAT + 16, width), BF),
        pltpu.VMEM((2 * BLOCKS * (D + 16), width), BF),
        pltpu.VMEM((2 * (BLOCKS + 1) * D, width), BF),
        pltpu.VMEM((2, BLOCKS + 1, D, width), BF),
        pltpu.VMEM((24, width), F32),
        pltpu.VMEM((D, width), F32),
        pltpu.VMEM((D, width), F32),
        pltpu.VMEM((2, D, width), BF),
        pltpu.VMEM((width // CB * D, CB), F32),
        pltpu.VMEM((2, 2, D, 128), F32),
        pltpu.VMEM((HPAD, CB), F32),
        pltpu.VMEM((HPAD, width), BF),
    ]


def compute(x, ints, rw, w, wh, vec):
    width = x.shape[0]
    vm = pl.BlockSpec(memory_space=pltpu.VMEM)
    return pl.pallas_call(
        compute_kernel,
        out_shape=(
            jax.ShapeDtypeStruct((2, width, D), BF),
            jax.ShapeDtypeStruct((2, width, D), F32),
            jax.ShapeDtypeStruct((2, A_ROWS, D), BF),
            jax.ShapeDtypeStruct((2, D, HPAD), BF),
            jax.ShapeDtypeStruct((2, 3, 16, D), F32),
        ),
        in_specs=[vm] * 6,
        out_specs=(vm,) * 5,
        scratch_shapes=work_scratch(width),
        compiler_params=pltpu.CompilerParams(vmem_limit_bytes=62 * 1024 * 1024),
    )(x, ints, rw, w, wh, vec)


class Plan:
    def __init__(self, n, length):
        self.n, self.length = n, length
        self.rows128 = -(-length // 128)
        block_end, head_end = A_ROWS * D, A_ROWS * D + D * HEADS
        self.a_base, self.a_rows, self.h_first, self.h_rows, self.h_off, self.v_first, self.v_rows, self.v_off = ([] for _ in range(8))
        used = 0
        for i in range(n):
            lo, hi = i * length, (i + 1) * length
            base = min(lo, block_end) // D // 16 * 16
            top = -(-min(hi, block_end) // D)
            a_rows = -(-(top - base) // 16) * 16 if lo < block_end else 0
            first = min(max(lo - block_end, 0), D * HEADS) // HEADS
            last = -(-min(max(hi - block_end, 0), D * HEADS) // HEADS)
            h_rows = last - first if hi > block_end and lo < head_end else 0
            v_first = max(lo - head_end, 0) // D
            v_rows = -(-(hi - head_end) // D) - v_first if hi > head_end else 0
            self.a_base.append(base)
            self.a_rows.append(a_rows)
            self.h_first.append(first)
            self.h_rows.append(h_rows)
            self.h_off.append(a_rows)
            self.v_first.append(v_first)
            self.v_rows.append(v_rows)
            self.v_off.append(a_rows + 5 * h_rows)
            used = max(used, a_rows + 5 * h_rows + v_rows)
        self.heads = max(self.h_rows)
        self.image = (HEADS * self.heads // 128 + 24) // 8 * 8
        self.slot = -(-(used + 1) // 32) * 32

    def at(self, table, me):
        value = jnp.int32(table[0])
        for i in range(1, self.n):
            if table[i] != table[i - 1]:
                value = value + (me >= i).astype(jnp.int32) * (table[i] - table[i - 1])
        return value


MESH = pl.DeviceIdType.MESH


def neighbours(n):
    core = lax.axis_index("tower")
    me = lax.axis_index("dp")
    near_x = me + 1 - 2 * (me % 2)
    near_y = me + 2 - 4 * ((me // 2) % 2)
    return core, me, near_x, near_y


def at(core, index):
    return {"tower": core, "dp": index}


def greet(core, me, near_x, near_y, n, crossed=False):
    barrier = pltpu.get_barrier_semaphore()
    pl.semaphore_signal(barrier, inc=1, device_id=at(1 - core, me), device_id_type=MESH)
    for near in (near_x, near_y, near_x + near_y - me):
        pl.semaphore_signal(barrier, inc=1, device_id=at(core, near), device_id_type=MESH)
    for k in range(1, n // 4):
        pl.semaphore_signal(barrier, inc=1, device_id=at(core, (me + 4 * k) % n), device_id_type=MESH)
    for near in [near_x, near_y] + [(me + 4 * k) % n for k in range(1, n // 4)] if crossed else []:
        pl.semaphore_signal(barrier, inc=1, device_id=at(1 - core, near), device_id_type=MESH)
    return barrier


def place_shard(plan, me, p_ref, slot128, shifted, rolled):
    rows = plan.rows128
    start = me * plan.length
    shift = start % 128
    first = start // 128
    tall = shifted.shape[0]
    height = p_ref.shape[0]
    lane = lax.broadcasted_iota(jnp.int32, (height, 128), 1)
    rolled[0:8] = jnp.zeros((8, 128), F32)
    rolled[8 : 8 + height] = pltpu.roll(p_ref[...], shift, 1)
    shifted[...] = jnp.zeros((tall, 128), F32)
    moved = jnp.where(lane >= shift, rolled[8 : 8 + height], rolled[7 : 7 + height])
    shifted[16 : 16 + height] = moved
    slot128[...] = jnp.zeros(slot128.shape, F32)
    row = lax.broadcasted_iota(jnp.int32, (height, 128), 0)
    base = plan.at(plan.a_base, me)

    @pl.when(plan.at(plan.a_rows, me) > 0)
    def _():
        slot128[pl.ds(first - 2 * base, height)] = jnp.where(row + first < 2 * A_ROWS, moved, 0.0)

    v_start = (A_ROWS * D + D * HEADS) // 128
    v_rows, v_off, v_first = (plan.at(t, me) for t in (plan.v_rows, plan.v_off, plan.v_first))
    tall_v = min(height, -(-2 * max(plan.v_rows) // 8) * 8)

    @pl.when(v_rows > 0)
    def _():
        inside = plan.at([max(0, v_start - i * plan.length // 128) for i in range(plan.n)], me)
        to = 2 * v_off + first + inside - v_start - 2 * v_first
        slot128[pl.ds(to, tall_v)] = shifted[pl.ds(16 + inside, tall_v)]

    h_first, h_rows, h_off = (plan.at(t, me) for t in (plan.h_first, plan.h_rows, plan.h_off))

    @pl.when(h_rows > 0)
    def _():
        tall_h = plan.image
        begin = A_ROWS * D + HEADS * h_first - 128 * first + 128 * 16
        turn = begin % 128
        rolled[0:tall_h] = pltpu.roll(shifted[pl.ds(begin // 128, tall_h)], (128 - turn) % 128, 1)
        rolled[tall_h : tall_h + 8] = jnp.zeros((8, 128), F32)
        lane = lax.broadcasted_iota(jnp.int32, (tall_h, 128), 1)
        shifted[0:tall_h] = jnp.where(lane < 128 - turn, rolled[0:tall_h], rolled[1 : tall_h + 1])
        to = slot128.at[pl.ds(pl.multiple_of(2 * h_off, 8), 10 * plan.heads)]
        it = lax.broadcasted_iota(jnp.int32, (10, 128), 0)
        lane = lax.broadcasted_iota(jnp.int32, (10, 128), 1)
        for k in range(plan.heads):
            row, turn = HEADS * k // 128, HEADS * k % 128
            window = pltpu.roll(shifted[row : row + 16], (128 - turn) % 128, 1)
            value = jnp.where(lane < 128 - turn, window[0:10], window[1:11])
            kept = (it * 128 + lane < HEADS) & (k < h_rows)
            to[10 * k : 10 * k + 10] = to[10 * k : 10 * k + 10] + jnp.where(kept, value, 0.0)


def unpack_rows(plan, i, slot, w, heads, vectors, scratch):
    base, rows = plan.a_base[i], plan.a_rows[i]
    if rows:
        shared = i > 0 and base < plan.a_base[i - 1] + plan.a_rows[i - 1]
        lo = 0
        if shared:
            w[base : base + 16] = w[base : base + 16] + slot[0:16]
            lo = 16
        if rows > lo:
            w[base + lo : base + rows] = slot[lo:rows]
    h_rows, h_off, h_first = plan.h_rows[i], plan.h_off[i], plan.h_first[i]
    v_rows, v_off, v_first = plan.v_rows[i], plan.v_off[i], plan.v_first[i]
    if h_rows or v_rows:
        value = slot.astype(F32)
        scratch[0][...] = value[:, 0:128]
        scratch[1][...] = value[:, 128:D]
    if h_rows:
        shared = i > 0 and plan.h_rows[i - 1] and plan.h_first[i - 1] + plan.h_rows[i - 1] > h_first
        for j in range(5):
            for half in range(2):
                cols = slice(128 * half, 128 * half + 128)
                first = D * j + h_first
                value = scratch[half][pl.ds(h_off + j, h_rows, stride=5)]
                if shared:
                    heads[first : first + 1, cols] = heads[first : first + 1, cols] + value[0:1]
                    if h_rows > 1:
                        heads[first + 1 : first + h_rows, cols] = value[1:h_rows]
                else:
                    heads[first : first + h_rows, cols] = value
    if v_rows:
        shared = v_first and plan.v_first[i - 1] + plan.v_rows[i - 1] > v_first
        shared = shared or (i > 0 and plan.v_rows[i - 1] > 0 and v_first == 0)
        for half in range(2):
            cols = slice(128 * half, 128 * half + 128)
            value = scratch[half][v_off : v_off + v_rows]
            if shared:
                vectors[v_first : v_first + 1, cols] = vectors[v_first : v_first + 1, cols] + value[0:1]
                if v_rows > 1:
                    vectors[v_first + 1 : v_first + v_rows, cols] = value[1:v_rows]
            else:
                vectors[v_first : v_first + v_rows, cols] = value


def split3(value):
    hi = value.astype(BF).astype(F32)
    mid = (value - hi).astype(BF).astype(F32)
    return hi, mid, value - hi - mid


def gather_kernel(plan, p_ref, ints_ref, imp_ref, w, wh, vec, both, rw, slots, slot128, shifted, rolled, scratch, whf, vecf, send, recv):
    n = plan.n
    depth = n // 4
    core, me, near_x, near_y = neighbours(n)
    barrier = greet(core, me, near_x, near_y, n)
    place_shard(plan, me, p_ref, slot128, shifted, rolled)
    pl.semaphore_wait(barrier, depth + 3)
    half = rw.shape[1]
    started = []

    def copy(src, dst, slot, to):
        c = pltpu.make_async_remote_copy(
            src_ref=src, dst_ref=dst, send_sem=send.at[slot], recv_sem=recv.at[slot], device_id=to, device_id_type=MESH
        )
        c.start()
        started.append(c)
        return c

    mine = pl.multiple_of(core * half, half)
    theirs = pl.multiple_of((1 - core) * half, half)
    number = iter(range(1 << 20))
    ints_copy = copy(ints_ref.at[:, pl.ds(theirs, half)], both.at[core], next(number), at(1 - core, me))
    rows = plan.slot
    total = jnp.sum(imp_ref[...].astype(F32), axis=1, keepdims=True)
    lane = lax.broadcasted_iota(jnp.int32, (1, D), 1)
    hi, mid, lo = split3(total)
    left = slot128[pl.ds(0, rows, stride=2)]
    right = slot128[pl.ds(1, rows, stride=2)]
    own = jnp.concatenate([left, right], 1)
    last = jnp.where(lane == 0, hi, jnp.where(lane == 1, mid, jnp.where(lane == 2, lo, 0.0)))
    last_row = lax.broadcasted_iota(jnp.int32, (rows, D), 0) == rows - 1
    slots[core, me] = jnp.where(last_row, last, own).astype(BF)

    def column(index, k):
        return (index + n - 4 * k) % n

    def send_slot(origin, to, lo=0, hi=rows):
        ref = slots.at[core, origin, pl.ds(lo, hi - lo)]
        return copy(ref, ref, next(number), to)

    near_xy = near_x + near_y - me
    cut = rows // 2
    z_in, x_in, y_in, d_in, s_in = {}, {}, {}, {}, []
    for k in sorted(range(1, depth), key=lambda k: (min(k, depth - k), k)):
        z_in[k] = send_slot(me, at(core, (me + 4 * k) % n))
    order = [0] + list(z_in)
    for k in order:
        if k:
            z_in[k].wait_recv()
        x_in[k] = send_slot(column(me, k), at(core, near_x))
        y_in[k] = send_slot(column(me, k), at(core, near_y))
        s_in.append(send_slot(column(me, k), at(1 - core, me)))
    for k in order:
        x_in[k].wait_recv()
        first = send_slot(column(near_x, k), at(core, near_y), 0, cut)
        s_in.append(send_slot(column(near_x, k), at(1 - core, me)))
        y_in[k].wait_recv()
        second = send_slot(column(near_y, k), at(core, near_x), cut, rows)
        s_in.append(send_slot(column(near_y, k), at(1 - core, me)))
        d_in[k] = (first, second)
    for k in order:
        for c in d_in[k]:
            c.wait_recv()
        s_in.append(send_slot(column(near_xy, k), at(1 - core, me)))
    ints_copy.wait_recv()
    both[core] = ints_ref[:, pl.ds(mine, half)]
    for c in s_in:
        c.wait_recv()
    for c in started:
        c.wait_send()
    for t in range(2):
        vecf[...] = jnp.zeros(vecf.shape, F32)
        for i in range(n):
            unpack_rows(plan, i, slots[t, i], w.at[t], whf, vecf, [scratch.at[0], scratch.at[1]])
        for j in range(5):
            wh[t, :, D * j : D * j + D] = whf[D * j : D * j + D].astype(BF)
        vec[t] = vecf[...].astype(BF)
    total = jnp.zeros((1, D), F32)
    for i in range(n):
        tail = slots[0, i, rows - 16 : rows].astype(F32)
        total = total + tail[15:16]
    weight_sum = jnp.sum(jnp.where(lane < 3, total, 0.0), axis=1, keepdims=True)
    rw[...] = jnp.broadcast_to(imp_ref[:, pl.ds(mine, half)].astype(F32) / weight_sum, (8, half))


def gather(plan, p128, ints, imp):
    n, rows = plan.n, plan.slot
    half = ints.shape[1] // 2
    vm = pl.BlockSpec(memory_space=pltpu.VMEM)
    height = p128.shape[0]
    tall = max(2 * rows, height + 40) + 80
    copies = 1 + (n // 4 - 1) + 2 * (n // 4) + 2 * (n // 4) + n
    return pl.pallas_call(
        functools.partial(gather_kernel, plan),
        out_shape=(
            jax.ShapeDtypeStruct((2, A_ROWS, D), BF),
            jax.ShapeDtypeStruct((2, D, HPAD), BF),
            jax.ShapeDtypeStruct((2, 128, D), BF),
            jax.ShapeDtypeStruct((2, 8, half), jnp.int32),
            jax.ShapeDtypeStruct((8, half), F32),
        ),
        in_specs=[vm] * 3,
        out_specs=(vm,) * 5,
        scratch_shapes=[
            pltpu.VMEM((2, n, rows, D), BF),
            pltpu.VMEM((tall, 128), F32),
            pltpu.VMEM((height + 128, 128), F32),
            pltpu.VMEM((height + 40, 128), F32),
            pltpu.VMEM((2, rows, 128), F32),
            pltpu.VMEM((HPAD, D), F32),
            pltpu.VMEM((128, D), F32),
            pltpu.SemaphoreType.DMA((copies,)),
            pltpu.SemaphoreType.DMA((copies,)),
        ],
        compiler_params=pltpu.CompilerParams(
            collective_id=0, has_side_effects=True, vmem_limit_bytes=48 * 1024 * 1024
        ),
    )(p128, ints, imp)


def chunks(height):
    step = max(c for c in range(8, 113, 8) if height % c == 0)
    return [(lo, lo + step) for lo in range(0, height, step)]


def lay_flat(plan, me, slot128, flat, rolled):
    height = rolled.shape[0] - 40
    start = me * plan.length
    shift = start % 128
    first = start // 128
    base = plan.at(plan.a_base, me)
    row = lax.broadcasted_iota(jnp.int32, (height + 8, 128), 0)
    flat[...] = jnp.zeros(flat.shape, F32)

    @pl.when(plan.at(plan.a_rows, me) > 0)
    def _():
        rows = slot128[pl.ds(first - 2 * base, height + 8)]
        flat[16 : 24 + height] = jnp.where(row + first < 2 * A_ROWS, rows, 0.0)

    v_start = (A_ROWS * D + D * HEADS) // 128
    v_rows, v_off, v_first = (plan.at(t, me) for t in (plan.v_rows, plan.v_off, plan.v_first))
    tall_v = min(height, -(-2 * max(plan.v_rows) // 8) * 8)

    @pl.when(v_rows > 0)
    def _():
        inside = plan.at([max(0, v_start - i * plan.length // 128) for i in range(plan.n)], me)
        source = 2 * v_off + first + inside - v_start - 2 * v_first
        to = pl.ds(16 + inside, tall_v)
        flat[to] = flat[to] + slot128[pl.ds(source, tall_v)]

    h_first, h_rows, h_off = (plan.at(t, me) for t in (plan.h_first, plan.h_rows, plan.h_off))

    @pl.when(h_rows > 0)
    def _():
        tall_h = plan.image
        source = slot128.at[pl.ds(pl.multiple_of(2 * h_off, 8), 10 * plan.heads + 6)]
        it = lax.broadcasted_iota(jnp.int32, (16, 128), 0)
        lane = lax.broadcasted_iota(jnp.int32, (16, 128), 1)
        rolled[0 : tall_h + 8] = jnp.zeros((tall_h + 8, 128), F32)
        for k in range(plan.heads):
            row, turn = HEADS * k // 128, HEADS * k % 128
            kept = (it * 128 + lane < HEADS) & (k < h_rows)
            value = pltpu.roll(jnp.where(kept, source[10 * k : 10 * k + 16], 0.0), turn, 1)
            above = jnp.concatenate([jnp.zeros((8, 128), F32), value], 0)[7:23]
            rolled[row : row + 16] = rolled[row : row + 16] + jnp.where(lane >= turn, value, above)
        begin = A_ROWS * D + HEADS * h_first - 128 * first + 128 * 16
        turn = begin % 128
        slot128[0:8] = jnp.zeros((8, 128), F32)
        slot128[8 : 8 + tall_h] = pltpu.roll(rolled[0:tall_h], turn, 1)
        lane = lax.broadcasted_iota(jnp.int32, (tall_h, 128), 1)
        moved = jnp.where(lane >= turn, slot128[8 : 8 + tall_h], slot128[7 : 7 + tall_h])
        to = pl.ds(begin // 128, tall_h)
        flat[to] = flat[to] + moved

    rolled[0 : height + 8] = pltpu.roll(flat[16 : 24 + height], (128 - shift) % 128, 1)
    for lo, hi in chunks(height):
        lane = lax.broadcasted_iota(jnp.int32, (hi - lo, 128), 1)
        flat[lo:hi] = jnp.where(lane < 128 - shift, rolled[lo:hi], rolled[lo + 1 : hi + 1])


def pack_slots(plan, core, gw, gh, gv, rgw, rgh, rgv, slots, sums, vsum, scratch):
    total = gv[core].astype(F32) + rgv[...]
    for kind in range(3):
        vsum[kind * (BLOCKS + 1) : (kind + 1) * (BLOCKS + 1)] = total[kind, 0 : BLOCKS + 1]
    sums[...] = gh[core].astype(F32) + rgh[...].astype(F32)
    for i in range(plan.n):
        base, rows = plan.a_base[i], plan.a_rows[i]
        h_rows, h_off, h_first = plan.h_rows[i], plan.h_off[i], plan.h_first[i]
        v_rows, v_off, v_first = plan.v_rows[i], plan.v_off[i], plan.v_first[i]
        slots[i, rows : plan.slot] = jnp.zeros((plan.slot - rows, D), BF)
        if rows:
            added = gw[core, base : base + rows].astype(F32) + rgw[base : base + rows].astype(F32)
            slots[i, 0:rows] = added.astype(BF)
        if h_rows or v_rows:
            scratch[...] = jnp.zeros(scratch.shape, F32)
            for half in range(2):
                for j in range(5 if h_rows else 0):
                    cols = slice(D * j + 128 * half, D * j + 128 * half + 128)
                    scratch[half, pl.ds(h_off + j, h_rows, stride=5)] = sums[h_first : h_first + h_rows, cols]
                if v_rows:
                    scratch[half, v_off : v_off + v_rows] = vsum[v_first : v_first + v_rows, 128 * half : 128 * half + 128]
            whole = jnp.concatenate([scratch[0], scratch[1]], 1)
            slots[i, rows : plan.slot] = whole[rows:].astype(BF)


def segment_bounds():
    first = [0] + [(CAT + j * D) * D for j in range(BLOCKS + 1)]
    return list(zip(first, first[1:] + [A_ROWS * D + D * HEADS]))


def update_shard(plan, me, p_ref, m_ref, v_ref, outs, flat, squares, sq_in, push, to_plane, to_z):
    first_out, second_out, new_out, norm_out = outs
    height = p_ref.shape[0]
    start = me * plan.length
    correction = 1.0 - 0.5**STEP
    bounds = segment_bounds()

    def place(lo, hi):
        shape = (hi - lo, 128)
        return 128 * lo + 128 * lax.broadcasted_iota(jnp.int32, shape, 0) + lax.broadcasted_iota(jnp.int32, shape, 1)

    for lo, hi in chunks(height):
        spot = place(lo, hi)
        grad = jnp.where(spot < plan.length, flat[lo:hi], 0.0)
        first_new = 0.5 * m_ref[lo:hi] + 0.5 * grad
        second_new = 0.5 * v_ref[lo:hi] + 0.5 * grad * grad
        first_out[lo:hi] = first_new
        second_out[lo:hi] = second_new
        decay = jnp.where(spot < bounds[-1][1] - start, 0.01 * p_ref[lo:hi], 0.0)
        update = first_new / correction / (jnp.sqrt(second_new / correction) + 1e-06) + decay
        flat[lo:hi] = jnp.where(spot < plan.length, update, 0.0)
        new_out[lo:hi] = p_ref[lo:hi] - 0.5 * update
    squares[...] = jnp.zeros(squares.shape, F32)

    def each_segment(body):
        for j, (first, last) in enumerate(bounds):
            pl.when((first < start + plan.length) & (last > start))(lambda j=j, first=first, last=last: body(j, first, last))

    def square_sums(j, first, last):
        weight, change = jnp.zeros((8, 128), F32), jnp.zeros((8, 128), F32)
        for lo, hi in chunks(height):
            spot = place(lo, hi)
            inside = (spot >= first - start) & (spot < last - start)
            p, u = jnp.where(inside, p_ref[lo:hi], 0.0), jnp.where(inside, flat[lo:hi], 0.0)
            weight = weight + jnp.sum((p * p).reshape(-1, 8, 128), axis=0)
            change = change + jnp.sum((u * u).reshape(-1, 8, 128), axis=0)
        squares[0, j : j + 1] = jnp.sum(weight, axis=0, keepdims=True)
        squares[0, 16 + j : 17 + j] = jnp.sum(change, axis=0, keepdims=True)

    each_segment(square_sums)
    total = squares[0]
    for hop, targets in enumerate((to_plane, to_z)):
        lands = range(3) if hop == 0 else range(3, 3 + len(to_z))
        for c in [push(squares.at[hop], sq_in.at[k], to) for k, to in zip(lands, targets)]:
            c.wait_recv()
        for k in lands:
            total = total + sq_in[k]
        squares[hop + 1] = total
    norm = jnp.sqrt(jnp.sum(total, axis=1, keepdims=True))
    squares[3] = jnp.broadcast_to(norm, (32, 128))
    line = jnp.sqrt(jnp.sum(jnp.concatenate([total, jnp.zeros((96, 128), F32)], 0).T, axis=0, keepdims=True))
    norm_out[0:1] = line[:, 0:MATS]
    norm_out[1:2] = pltpu.roll(line, 112, 1)[:, 0:MATS]

    def scaled(j, first, last):
        ratio = squares[3, j : j + 1] / squares[3, 16 + j : 17 + j]
        for lo, hi in chunks(height):
            spot = place(lo, hi)
            inside = (spot >= first - start) & (spot < last - start)
            new_out[lo:hi] = jnp.where(inside, p_ref[lo:hi] - 0.5 * ratio * flat[lo:hi], new_out[lo:hi])

    each_segment(scaled)


def reduce_kernel(
    plan, gw, gh, gv, st, ig, p_ref, m_ref, v_ref,
    st_out, ig_out, first_out, second_out, new_out, norm_out,
    rgw, rgh, rgv, slots, sums, vsum, scratch, in_d, in_x, in_y, in_z, slot128, flat, rolled, squares, sq_in,
    send, recv, local,
):
    n, rows = plan.n, plan.slot
    depth, cut = n // 4, plan.slot // 2
    core, me, near_x, near_y = neighbours(n)
    near_xy = near_x + near_y - me
    barrier = greet(core, me, near_x, near_y, n)
    pl.semaphore_wait(barrier, depth + 3)
    half = st.shape[1]
    number = iter(range(1 << 20))
    started = []

    def copy(src, dst, to):
        slot = next(number)
        c = pltpu.make_async_remote_copy(
            src_ref=src, dst_ref=dst, send_sem=send.at[slot], recv_sem=recv.at[slot], device_id=to, device_id_type=MESH
        )
        c.start()
        started.append(c)
        return c

    def column(index, k):
        return (index + n - 4 * k) % n

    sibling = at(1 - core, me)
    early = [
        copy(gw.at[1 - core], rgw, sibling),
        copy(gh.at[1 - core], rgh, sibling),
        copy(gv.at[1 - core], rgv, sibling),
    ]
    mine = pl.ds(pl.multiple_of(core * half, half), half)
    late = [
        copy(st.at[1 - core], st_out.at[mine], sibling),
        copy(ig.at[1 - core], ig_out.at[mine], sibling),
    ]
    stay = [
        pltpu.make_async_copy(st.at[core], st_out.at[mine], local.at[0]),
        pltpu.make_async_copy(ig.at[core], ig_out.at[mine], local.at[1]),
    ]
    for c in stay:
        c.start()
    for c in early:
        c.wait_recv()
    pack_slots(plan, core, gw, gh, gv, rgw, rgh, rgv, slots, sums, vsum, scratch)
    order = list(range(1, depth)) + [0]
    to_x, to_y = at(core, near_x), at(core, near_y)
    halves = {}
    for k in order:
        diagonal = column(near_xy, k)
        halves[k] = (
            copy(slots.at[diagonal, pl.ds(0, cut)], in_d.at[k, pl.ds(0, cut)], to_y),
            copy(slots.at[diagonal, pl.ds(cut, rows - cut)], in_d.at[k, pl.ds(cut, rows - cut)], to_x),
        )
    fulls = {}
    for k in order:
        ox, oy = column(near_x, k), column(near_y, k)
        halves[k][0].wait_recv()
        slots[ox, 0:cut] = (slots[ox, 0:cut].astype(F32) + in_d[k, 0:cut].astype(F32)).astype(BF)
        first = copy(slots.at[ox], in_x.at[k], to_x)
        halves[k][1].wait_recv()
        slots[oy, cut:rows] = (slots[oy, cut:rows].astype(F32) + in_d[k, cut:rows].astype(F32)).astype(BF)
        fulls[k] = (first, copy(slots.at[oy], in_y.at[k], to_y))
    along = {}
    for k in order:
        own = column(me, k)
        for c in fulls[k]:
            c.wait_recv()
        if k:
            total = slots[own].astype(F32) + in_x[k].astype(F32) + in_y[k].astype(F32)
            slots[own] = total.astype(BF)
            along[k] = copy(slots.at[own], in_z.at[k], at(core, own))
    for c in along.values():
        c.wait_recv()
    total = slots[me].astype(F32) + in_x[0].astype(F32) + in_y[0].astype(F32)
    for k in along:
        total = total + in_z[k].astype(F32)
    slot128[...] = jnp.zeros(slot128.shape, F32)
    slot128[pl.ds(0, rows, stride=2)] = total[:, 0:128]
    slot128[pl.ds(1, rows, stride=2)] = total[:, 128:D]
    lay_flat(plan, me, slot128, flat, rolled)

    to_z = [at(core, column(me, k)) for k in range(1, depth)]
    outs = (first_out, second_out, new_out, norm_out)
    to_plane = [to_x, to_y, at(core, near_xy)]
    update_shard(plan, me, p_ref, m_ref, v_ref, outs, flat, squares, sq_in, copy, to_plane, to_z)
    for c in late:
        c.wait_recv()
    for c in stay:
        c.wait()
    for c in started:
        c.wait_send()


def reduce_and_update(plan, gw, gh, gv, st, ig, p128, m128, v128):
    n, rows = plan.n, plan.slot
    depth = n // 4
    half = st.shape[1]
    height = p128.shape[0]
    vm = pl.BlockSpec(memory_space=pltpu.VMEM)
    hbm = pl.BlockSpec(memory_space=pl.ANY)
    copies = 5 + 2 * depth + 2 * depth + (depth - 1) + (depth - 1) + 3
    flat32 = jax.ShapeDtypeStruct((height, 128), F32)
    return pl.pallas_call(
        functools.partial(reduce_kernel, plan),
        out_shape=(
            jax.ShapeDtypeStruct((2 * half, D), BF),
            jax.ShapeDtypeStruct((2 * half, D), F32),
            flat32,
            flat32,
            flat32,
            jax.ShapeDtypeStruct((2, MATS), F32),
        ),
        in_specs=[vm] * 3 + [hbm] * 2 + [vm] * 3,
        out_specs=(hbm, hbm, vm, vm, vm, vm),
        scratch_shapes=[
            pltpu.VMEM((A_ROWS, D), BF),
            pltpu.VMEM((D, HPAD), BF),
            pltpu.VMEM(gv.shape[1:], F32),
            pltpu.VMEM((n, rows, D), BF),
            pltpu.VMEM((D, HPAD), F32),
            pltpu.VMEM((40, D), F32),
            pltpu.VMEM((2, rows, 128), F32),
            pltpu.VMEM((depth, rows, D), BF),
            pltpu.VMEM((depth, rows, D), BF),
            pltpu.VMEM((depth, rows, D), BF),
            pltpu.VMEM((depth, rows, D), BF),
            pltpu.VMEM((max(2 * rows, height + 48) + 80, 128), F32),
            pltpu.VMEM((height + 128, 128), F32),
            pltpu.VMEM((height + 40, 128), F32),
            pltpu.VMEM((4, 32, 128), F32),
            pltpu.VMEM((2 + depth, 32, 128), F32),
            pltpu.SemaphoreType.DMA((copies,)),
            pltpu.SemaphoreType.DMA((copies,)),
            pltpu.SemaphoreType.DMA((2,)),
        ],
        compiler_params=pltpu.CompilerParams(
            collective_id=1, has_side_effects=True, vmem_limit_bytes=48 * 1024 * 1024
        ),
    )(gw, gh, gv, st, ig, p128, m128, v128)


class Copies:
    def __init__(self, send, recv):
        self.send, self.recv, self.made, self.sent = send, recv, [], set()

    def add(self, src, dst, to, recv_slot=None, only=None):
        self.made.append((src, dst, to, recv_slot, only))
        return len(self.made) - 1

    def get(self, number):
        src, dst, to, recv_slot, _ = self.made[number]
        return pltpu.make_async_remote_copy(
            src_ref=src(), dst_ref=dst(), send_sem=self.send.at[number],
            recv_sem=self.recv.at[number] if recv_slot is None else recv_slot(),
            device_id=to(), device_id_type=MESH,
        )

    def start(self, *numbers):
        for number in numbers:
            self.get(number).start()

    def arrive(self, *numbers):
        for number in numbers:
            self.get(number).wait_recv()

    def leave(self, *numbers):
        for number in numbers:
            only = self.made[number][4]
            if number not in self.sent and only is None:
                self.get(number).wait_send()
            elif number not in self.sent:
                pl.when(only())(lambda number=number: self.get(number).wait_send())
            self.sent.add(number)


def fused_fits(plan):
    depth = plan.n // 4
    blocks = 11 * depth + 2 * (depth - 1)
    half = plan.slot // 2
    plain = [b + plan.slot <= A_ROWS for b, h, v in zip(plan.a_base, plan.h_rows, plan.v_rows) if not (h or v)]
    vectors = [rows for rows in plan.v_rows if rows]
    return (
        all(plain)
        and vectors == [3 * (BLOCKS + 1)]
        and plan.n % 4 == 0
        and half >= 32
        and 4 * half <= HPAD
        and 2 * depth * plan.slot <= (BLOCKS + 1) * D
        and -(-blocks // 4) * half <= BLOCKS * (D + 16)
        and max(plan.a_rows) <= plan.slot
    )


def train_kernel(
    plan, x_ref, codes_ref, targets_ref, visits_ref, imp_ref, p_ref, m_ref, v_ref, st_out, ig_out, flat_out, norm_out,
    w, wh, vec, both, away, rw, eye, wct, wt, wht, vt, gsb, xt, mix, xh, gp, rstd, stream, ex, br, dm, acc, lg, dl,
    gw, gh, gv, packed, st_stage, slot128, flat, rolled, vsum, vacc, vin, squares, sq_in,
    send, recv, z_recv, own_recv, local, ready,
):
    n, rows = plan.n, plan.slot
    depth, hrows = n // 4, plan.slot // 2
    cut = hrows // 32 * 16
    core, me, near_x, near_y = neighbours(n)
    near_xy = near_x + near_y - me
    width = both.shape[2]
    height = p_ref.shape[0]
    first_out, second_out, new_out = (flat_out.at[i * height : (i + 1) * height] for i in range(3))
    moments = [
        pltpu.make_async_copy(src, dst, local.at[3 + i])
        for i, (src, dst) in enumerate(((m_ref, first_out), (v_ref, second_out)))
    ]
    z_me, j_me = me // 4, me % 4
    copies = Copies(send, recv)
    scratch = [slot128.at[0:rows], slot128.at[rows : 2 * rows]]
    barrier = greet(core, me, near_x, near_y, n, True)
    mine = pl.multiple_of(core * width, width)
    theirs = pl.multiple_of((1 - core) * width, width)
    x_copy = pltpu.make_async_copy(x_ref.at[pl.ds(mine, width)], st_stage.at[0], local.at[0])
    x_copy.start()
    for c in moments:
        c.start()
    for to, half in ((both.at[core], mine), (away, theirs)):
        cols = pl.ds(half, width)
        to[0:1] = codes_ref[:, cols]
        to[1:2] = targets_ref[0, :, cols]
        to[2:6] = visits_ref[:, cols]
        to[6:7] = targets_ref[1, :, cols]
        to[7:8] = targets_ref[2, :, cols]
    place_shard(plan, me, p_ref, slot128, flat, rolled)

    spare = (BLOCKS + 1) * D

    def slot_part(t, i, lo, count):
        row = pl.multiple_of(spare + rows * (t * depth + i // 4) + lo, 16)
        return xh.at[pl.ds(row, count), pl.ds(pl.multiple_of((i % 4) * D, D), D)]

    def column(index, k):
        return (index + n - 4 * k) % n

    def sibling():
        return at(1 - core, me)

    def same(make, to):
        return copies.add(make, make, to)

    low = core * hrows
    other_low = (1 - core) * hrows
    order = [0] + sorted(range(1, depth), key=lambda k: (min(k, depth - k), k))
    to_x, to_y, to_d = (lambda: at(core, near_x)), (lambda: at(core, near_y)), (lambda: at(core, near_xy))
    swap_ints = copies.add(lambda: away, lambda: both.at[core], sibling)

    def arrival(t, number):
        return own_recv.at[t * (depth + 2) + number]

    own_targets = [(lambda: near_x), (lambda: near_y)] + [lambda k=k: (me + 4 * k) % n for k in order[1:]]
    own_sends = [copies.add(lambda: slot_part(core, me, 0, rows), lambda: slot_part(core, me, 0, rows), sibling, lambda: arrival(core, 0))]
    for number, target in enumerate(own_targets, 1):
        for h in range(2):
            make = lambda h=h: slot_part(core, me, h * hrows, hrows)
            own_sends.append(
                copies.add(make, make, lambda h=h, target=target: at(h, target()), lambda number=number: arrival(core, number))
            )
    own_sends = own_sends[3 + 2 :] + own_sends[1:5] + own_sends[:1]

    def own_arrive(t, number, make):
        pltpu.make_async_remote_copy(
            src_ref=make(), dst_ref=make(), send_sem=send.at[0], recv_sem=arrival(t, number), device_id=sibling(), device_id_type=MESH
        ).wait_recv()

    gathers = []
    for t in range(2):
        g = {}
        for k in order:
            if k:
                g["x", k] = same(lambda t=t, k=k: slot_part(t, column(me, k), low, hrows), to_x)
                g["y", k] = same(lambda t=t, k=k: slot_part(t, column(me, k), low, hrows), to_y)
            g["d", k] = (
                same(lambda t=t, k=k: slot_part(t, column(near_x, k), low, cut), to_y),
                same(lambda t=t, k=k: slot_part(t, column(near_y, k), low + cut, hrows - cut), to_x),
            )
            g["s", k] = [
                same(lambda t=t, k=k, index=index: slot_part(t, column(index, k), low, hrows), sibling) if index is not me or k else None
                for index in (me, near_x, near_y, near_xy)
            ]
        gathers.append(g)

    def gather_0(t):
        pl.when(core == t)(lambda: copies.start(*own_sends))

    def gather_1(t):
        g = gathers[t]
        for number, k in enumerate(order[1:], 3):
            own_arrive(t, number, lambda: slot_part(t, me, low, hrows))
            copies.start(g["x", k], g["y", k], g["s", k][0])

    def gather_2(t):
        g = gathers[t]
        for k in order:
            if k:
                copies.arrive(g["x", k])
            else:
                own_arrive(t, 1, lambda: slot_part(t, me, low, hrows))
            copies.start(g["d", k][0], g["s", k][1])
            if k:
                copies.arrive(g["y", k])
            else:
                own_arrive(t, 2, lambda: slot_part(t, me, low, hrows))
            copies.start(g["d", k][1], g["s", k][2])

    def gather_3(t):
        g = gathers[t]
        for k in order:
            copies.arrive(*g["d", k])
            copies.start(g["s", k][3])

    def gather_4(t):
        g = gathers[t]
        pl.when(core != t)(lambda: own_arrive(t, 0, lambda: slot_part(t, me, 0, rows)))
        for k in order:
            copies.arrive(*(c for c in g["s", k] if c is not None))

    def unpack(t):
        lg[4 * D : 5 * D, 128:D] = jnp.zeros((D, 128), F32)
        vsum[...] = jnp.zeros(vsum.shape, F32)
        for i in range(n):
            row, lane = spare + rows * (t * depth + i // 4), (i % 4) * D
            unpack_rows(plan, i, xh[row : row + rows, lane : lane + D], w.at[t], lg, vsum, scratch)
        for j in range(5):
            wh[t, :, D * j : D * j + D] = lg[D * j : D * j + D].astype(BF)
        vec[t] = vsum[...].astype(BF)

    total = jnp.sum(imp_ref[...].astype(F32), axis=1, keepdims=True)
    lane_d = lax.broadcasted_iota(jnp.int32, (1, D), 1)
    hi, mid, lo = split3(total)
    left = slot128[pl.ds(0, rows, stride=2)]
    right = slot128[pl.ds(1, rows, stride=2)]
    own = jnp.concatenate([left, right], 1)
    last = jnp.where(lane_d == 0, hi, jnp.where(lane_d == 1, mid, jnp.where(lane_d == 2, lo, 0.0)))
    last_row = lax.broadcasted_iota(jnp.int32, (rows, D), 0) == rows - 1
    slot_part(core, me, 0, rows)[...] = jnp.where(last_row, last, own).astype(BF)
    pl.semaphore_wait(barrier, depth + 3 + 2 + depth - 1)
    gather_0(0)
    copies.start(swap_ints)
    eye[...] = identity(D)
    x_copy.wait()
    for c in range(0, width, CB):
        xt[0, 0:D, c : c + CB] = nt(eye[...], st_stage[0, c : c + CB, :]).astype(BF)
    gather_1(0)
    gather_0(1)
    gather_2(0)
    gather_3(0)
    copies.arrive(swap_ints)
    gather_4(0)
    unpack(0)
    total = jnp.zeros((1, D), F32)
    for i in range(n):
        row, lane = spare + rows * (i // 4), (i % 4) * D
        total = total + xh[row + rows - 16 : row + rows, lane : lane + D].astype(F32)[15:16]
    weight_sum = jnp.sum(jnp.where(lane_d < 3, total, 0.0), axis=1, keepdims=True)
    rw[...] = jnp.broadcast_to(imp_ref[:, pl.ds(mine, width)].astype(F32) / weight_sum, (8, width))

    fwd = (eye, w, wh, vec, wct, wt, vt, gsb, xt, mix, xh, gp, rstd, stream, both, width)

    def during_forward(k):
        pl.when(k == 1)(lambda: gather_1(1))
        pl.when(k == 4)(lambda: gather_2(1))
        pl.when(k == 7)(lambda: gather_3(1))

    def emit_states(t):
        for c in range(0, width, CB):
            st_stage[t, c : c + CB, :] = nt(eye[...], xt[t + 1, 0:D, c : c + CB]).astype(BF)

    forward_tower(0, fwd, during_forward)
    gather_4(1)
    copies.leave(*range(len(copies.made)))
    unpack(1)
    forward_tower(1, fwd, None)
    emit_states(0)
    emit_states(1)
    out_rows = pl.ds(mine, width)
    st_copy = copies.add(lambda: st_stage.at[1 - core], lambda: st_out.at[out_rows], sibling)
    copies.start(st_copy)
    st_stay = pltpu.make_async_copy(st_stage.at[core], st_out.at[out_rows], local.at[1])
    st_stay.start()

    packed_of = [i for i in range(n) if plan.h_rows[i] or plan.v_rows[i]]
    owner = plan.v_rows.index(3 * (BLOCKS + 1))

    def block(t, q):
        arena, first = (xh, spare) if t == 0 else (mix, BLOCKS * (D + 16))
        row = pl.multiple_of(first + hrows * (q // 4), 16)
        return arena.at[pl.ds(row, hrows), pl.ds(pl.multiple_of((q % 4) * D, D), D)]

    def slot_half(t, i, lo):
        if i in packed_of:
            return packed.at[packed_of.index(i), pl.ds(pl.multiple_of(lo, 16), hrows)]
        return gw.at[t, pl.ds(pl.multiple_of(plan.a_base[i] + lo, 16), hrows)]

    def z_block(h, k):
        return 11 * depth + h * (depth - 1) + k - 1

    j_x, j_y, j_d = near_x % 4, near_y % 4, near_xy % 4
    jobs = {}
    for t in range(2):
        for zz in range(depth):
            q = 11 * zz
            job = {"q": q}
            job["swap"] = [
                copies.add(lambda t=t, i=4 * zz + j: slot_half(t, i, other_low), lambda t=t, q=q + j: block(t, q), sibling)
                for j in range(4)
            ]
            for number, (side, j, to) in enumerate((("x", j_x, to_x), ("y", j_y, to_y), ("d", j_d, to_d))):
                job[side] = copies.add(lambda t=t, q=q, j=j: block(t, q + 4 + j), lambda t=t, q=q, b=8 + number: block(t, q + b), to)
            job["z"] = copies.add(
                lambda t=t, q=q: block(t, q + 4 + j_me),
                lambda t=t, zz=zz: block(t, z_block(core, (zz + depth - z_me) % depth)),
                lambda t=t, zz=zz: at(t, 4 * zz + j_me),
                lambda zz=zz: z_recv.at[core * depth + (zz + depth - z_me) % depth],
                lambda zz=zz: z_me != zz,
            )
            jobs[t, zz] = job

    def pack(t, planes):
        wanted = [i for i in packed_of if i // 4 in planes]
        for i in wanted:
            a_rows, h_rows, h_off, h_first = plan.a_rows[i], plan.h_rows[i], plan.h_off[i], plan.h_first[i]
            to = packed.at[packed_of.index(i)]
            for part in scratch:
                part[...] = jnp.zeros(part.shape, F32)
            lo16, hi16 = h_first // 16 * 16, -(-(h_first + h_rows) // 16) * 16
            for half in range(2):
                for j in range(5 if h_rows else 0):
                    cols = slice(D * j + 128 * half, D * j + 128 * half + 128)
                    value = gh[t, lo16:hi16, cols].astype(F32)[h_first - lo16 : h_first - lo16 + h_rows]
                    scratch[half][pl.ds(h_off + j, h_rows, stride=5)] = value
            whole = jnp.concatenate([scratch[0][...], scratch[1][...]], 1)
            to[a_rows:rows] = whole[a_rows:].astype(BF)
            if a_rows:
                to[0:a_rows] = gw[t, plan.a_base[i] : plan.a_base[i] + a_rows]

    def plus(*refs):
        value = refs[0][...].astype(F32)
        for ref in refs[1:]:
            value = value + ref[...].astype(F32)
        return value

    def sum_0(t, zz):
        copies.start(*jobs[t, zz]["swap"])

    def sum_1(t, zz):
        job = jobs[t, zz]
        for j in range(4):
            copies.arrive(job["swap"][j])
            block(t, job["q"] + 4 + j)[...] = plus(slot_half(t, 4 * zz + j, low), block(t, job["q"] + j)).astype(BF)
        copies.start(job["x"], job["y"], job["d"])

    def sum_3(t, zz):
        job = jobs[t, zz]
        q = job["q"]
        copies.arrive(job["x"], job["y"], job["d"])
        value = plus(block(t, q + 4 + j_me), block(t, q + 8), block(t, q + 9), block(t, q + 10))

        @pl.when(z_me != zz)
        def _():
            block(t, q + 4 + j_me)[...] = value.astype(BF)
            copies.start(job["z"])

        @pl.when((z_me == zz) & (core == t))
        def _():
            final(core)[...] = value

        @pl.when((z_me == zz) & (core != t))
        def _():
            outgo[...] = value
            copies.start(hand_over)

    def sum_4(t):
        copies.arrive(hand_over)
        for h in range(2):
            for k in range(1, depth):
                src = block(t, z_block(h, k))
                pltpu.make_async_remote_copy(
                    src_ref=src, dst_ref=src, send_sem=send.at[0], recv_sem=z_recv.at[h * depth + k], device_id=sibling(), device_id_type=MESH
                ).wait_recv()
                final(h)[...] = final(h)[...] + src[...].astype(F32)

    def final(h):
        return lg.at[pl.ds(pl.multiple_of(h * hrows, 8), hrows)]

    outgo = lg.at[2 * hrows : 3 * hrows]

    def vector_step(step):
        sources = [gv.at[1 - core], vacc.at[0], vacc.at[1]]
        along = [lambda k=k: at(core, (me + 4 * k) % n) for k in range(1, depth)]
        targets = [[sibling], [to_x, to_y, to_d], along]
        if step:
            base = gv[core] if step == 1 else vacc[step - 2]
            for number, k in vector_copies[-1]:
                copies.arrive(number)
                base = base + vin[k]
            vacc[step - 1] = base
        if step < 3:
            started = []
            for k, to in enumerate(targets[step], (0, 1, 4)[step]):
                number = copies.add(lambda step=step: sources[step], lambda k=k: vin.at[k], to)
                copies.start(number)
                started.append((number, k))
            vector_copies.append(started)

    vector_copies = []
    hand_over = copies.add(lambda: outgo, lambda: final(core), sibling)
    peers = [(1 - core, me), (core, near_x), (core, near_y), (core, near_xy)] + [(1 - core, (me + 4 * k) % n) for k in range(1, depth)] + [(core, (me + 4 * k) % n) for k in range(1, depth)]

    bwd = (eye, w, wh, vec, wht, vt, gsb, xt, mix, xh, gp, rstd, stream, ex, br, dm, acc, lg, dl, both, rw, gw, gh, gv, dm, width)
    ig_copies = [copies.add(lambda: dm, lambda: ig_out.at[out_rows], sibling, None, lambda t=t: core != t) for t in range(2)]

    def ig_local():
        return pltpu.make_async_copy(dm, ig_out.at[out_rows], local.at[2])

    def emit_inputs(t):
        pl.when(core == t)(lambda: ig_local().start())
        pl.when(core != t)(lambda: copies.start(ig_copies[t]))

    def free_inputs(t):
        pl.when(core == t)(lambda: ig_local().wait())
        pl.when(core != t)(lambda: copies.get(ig_copies[t]).wait_send())

    ex[...] = jnp.zeros_like(ex)
    backward_tower(1, bwd, None, None)
    emit_inputs(1)
    for to_core, to_index in peers:
        pl.semaphore_signal(ready, inc=1, device_id=at(to_core, to_index), device_id_type=MESH)

    def after_head():
        pl.semaphore_wait(ready, len(peers))
        pack(1, range(depth))
        for zz in range(depth):
            sum_0(1, zz)

    def during_backward(i):
        def at_step(step, *calls):
            def run():
                for f, *args in calls:
                    f(*args)

            pl.when(i == step)(run)

        planes = range(depth)

        def release():
            copies.leave(*(jobs[1, i // 4]["swap"][i % 4] for i in packed_of))

        at_step(1, *((sum_1, 1, zz) for zz in planes))
        at_step(2, (release,), (pack, 0, (depth - 1,)), (sum_0, 0, depth - 1))
        at_step(3, (sum_1, 0, depth - 1))
        for zz in range(1, depth - 1):
            done = BLOCKS + 1 - 4 * zz + 1
            if done < BLOCKS:
                at_step(done, (pack, 0, (zz,)), (sum_0, 0, zz))
            if done + 1 < BLOCKS:
                at_step(done + 1, (sum_1, 0, zz))
        at_step(4, *((sum_3, 1, zz) for zz in planes))
        at_step(6, (sum_3, 0, depth - 1))
        for zz in range(1, depth - 1):
            done = BLOCKS + 1 - 4 * zz + 1
            if done + 3 < BLOCKS:
                at_step(done + 3, (sum_3, 0, zz))

    def after_weights():
        late = [zz for zz in range(1, depth - 1) if BLOCKS + 1 - 4 * zz + 1 >= BLOCKS]
        for zz in [*late, 0]:
            pack(0, (zz,))
            sum_0(0, zz)
        vector_step(0)

    backward_tower(0, bwd, after_head, during_backward, lambda: free_inputs(1), after_weights)
    emit_inputs(0)
    steps = {zz: BLOCKS + 1 - 4 * zz + 1 for zz in range(1, depth - 1)}
    for zz in sorted(steps, reverse=True):
        if steps[zz] + 1 >= BLOCKS:
            sum_1(0, zz)
    sum_1(0, 0)
    vector_step(1)
    for zz in sorted(steps, reverse=True):
        if steps[zz] + 3 >= BLOCKS:
            sum_3(0, zz)
    sum_3(0, 0)
    vector_step(2)
    pl.when(core == 0)(lambda: sum_4(0))
    pl.when(core == 1)(lambda: sum_4(1))
    vector_step(3)

    slot128[...] = jnp.zeros(slot128.shape, F32)
    for h in range(2):
        slot128[pl.ds(2 * hrows * h, hrows, stride=2)] = final(h)[:, 0:128]
        slot128[pl.ds(2 * hrows * h + 1, hrows, stride=2)] = final(h)[:, 128:D]

    @pl.when(me == owner)
    def _():
        for kind in range(3):
            first = 2 * (plan.v_off[owner] + kind * (BLOCKS + 1))
            for h in range(2):
                value = vacc[2, kind, 0 : BLOCKS + 1, 128 * h : 128 * h + 128]
                slot128[pl.ds(first + h, BLOCKS + 1, stride=2)] = value

    def push(src, dst, to):
        number = copies.add(lambda: src, lambda: dst, lambda: to)
        copies.start(number)
        return copies.get(number)

    lay_flat(plan, me, slot128, flat, rolled)
    for c in moments:
        c.wait()
    update_shard(
        plan, me, p_ref, first_out, second_out, (first_out, second_out, new_out, norm_out),
        flat, squares, sq_in, push, [to_x(), to_y(), to_d()], [at(core, (me + 4 * k) % n) for k in range(1, depth)],
    )
    copies.arrive(st_copy)
    pl.when(core == 0)(lambda: copies.arrive(ig_copies[0]))
    pl.when(core == 1)(lambda: copies.arrive(ig_copies[1]))
    free_inputs(0)
    st_stay.wait()
    copies.sent.update(ig_copies)
    copies.leave(*range(len(copies.made)))


def train(plan, latent, codes, targets, visits, imp, p128, m128, v128):
    n, rows = plan.n, plan.slot
    depth, hrows = n // 4, rows // 2
    width = codes.shape[1] // 2
    height = p128.shape[0]
    vm = pl.BlockSpec(memory_space=pltpu.VMEM)
    hbm = pl.BlockSpec(memory_space=pl.ANY)
    packed = sum(1 for h, v in zip(plan.h_rows, plan.v_rows) if h or v)
    return pl.pallas_call(
        functools.partial(train_kernel, plan),
        out_shape=(
            jax.ShapeDtypeStruct((2 * width, D), BF),
            jax.ShapeDtypeStruct((2 * width, D), F32),
            jax.ShapeDtypeStruct((3 * height, 128), F32),
            jax.ShapeDtypeStruct((2, MATS), F32),
        ),
        in_specs=[hbm] + [vm] * 5 + [hbm] * 2,
        out_specs=(hbm, hbm, vm, vm),
        scratch_shapes=[
            pltpu.VMEM((2, A_ROWS, D), BF),
            pltpu.VMEM((2, D, HPAD), BF),
            pltpu.VMEM((2, 128, D), BF),
            pltpu.VMEM((2, 8, width), jnp.int32),
            pltpu.VMEM((8, width), jnp.int32),
            pltpu.VMEM((8, width), F32),
            *work_scratch(width),
            pltpu.VMEM((2, A_ROWS, D), BF),
            pltpu.VMEM((2, D, HPAD), BF),
            pltpu.VMEM((2, 3, 16, D), F32),
            pltpu.VMEM((packed, rows, D), BF),
            pltpu.VMEM((2, width, D), BF),
            pltpu.VMEM((max(2 * rows, height + 48) + 80, 128), F32),
            pltpu.VMEM((height + 128, 128), F32),
            pltpu.VMEM((height + 40, 128), F32),
            pltpu.VMEM((128, D), F32),
            pltpu.VMEM((3, 3, 16, D), F32),
            pltpu.VMEM((3 + depth, 3, 16, D), F32),
            pltpu.VMEM((4, 32, 128), F32),
            pltpu.VMEM((2 + depth, 32, 128), F32),
            pltpu.SemaphoreType.DMA((11 * n,)),
            pltpu.SemaphoreType.DMA((11 * n,)),
            pltpu.SemaphoreType.DMA((2 * depth,)),
            pltpu.SemaphoreType.DMA((2 * (depth + 2),)),
            pltpu.SemaphoreType.DMA((5,)),
            pltpu.SemaphoreType.REGULAR,
        ],
        compiler_params=pltpu.CompilerParams(
            collective_id=2, has_side_effects=True, vmem_limit_bytes=63 * 1024 * 1024
        ),
    )(latent, codes, targets, visits, imp, p128, m128, v128)


def on_device(latent, codes, targets, visits, importance, params, first_moment, second_moment):
    me = lax.axis_index("tower")
    row_count = latent.shape[0]
    half = row_count // 2
    shard_len = params.shape[1]
    plan = Plan(lax.axis_size("dp"), shard_len)
    height = -(-plan.rows128 // 8) * 8
    p128, m128, v128 = (
        jnp.pad(v, ((0, 0), (0, 128 * height - shard_len))).reshape(height, 128) for v in (params, first_moment, second_moment)
    )
    if fused_fits(plan):
        states_out, inputs_out, flat, norms = train(
            plan, latent, codes, targets.transpose(1, 0, 2), visits[0].T, importance[None], p128, m128, v128
        )
    else:
        ints = jnp.concatenate([codes, targets[0, :1], visits[0].T, targets[0, 1:]], 0)
        x = lax.dynamic_slice_in_dim(latent, me * half, half, 0)
        w, wh, vec, both, rw = gather(plan, p128, ints, importance[None])
        st, ig, gw, gh, gv = compute(x, both, rw, w, wh, vec)
        states_out, inputs_out, *flat, norms = reduce_and_update(plan, gw, gh, gv, st, ig, p128, m128, v128)
        flat = jnp.concatenate(flat)
    flat = flat.reshape(1, -1)
    first, second, new = (flat[:, i * 128 * height : i * 128 * height + shard_len] for i in range(3))
    return (states_out[None], inputs_out[None], first, second, new, new.astype(BF), norms[None])


def solution(mesh):
    in_specs = (
        P("dp", None),
        P("tower", "dp"),
        P("tower", None, "dp"),
        P("tower", "dp", None),
        P("dp"),
        P("tower", "dp"),
        P("tower", "dp"),
        P("tower", "dp"),
    )
    out_specs = (
        P("tower", "dp", None),
        P("tower", "dp", None),
        P("tower", "dp"),
        P("tower", "dp"),
        P("tower", "dp"),
        P("tower", "dp"),
        P("tower", None, None),
    )
    return jax.shard_map(
        on_device, mesh=mesh, in_specs=in_specs, out_specs=out_specs, check_vma=False
    )
```

```python
import functools

import jax
import jax.numpy as jnp
from jax import lax
from jax.experimental import pallas as pl
from jax.experimental.pallas import tpu as pltpu
from jax.sharding import PartitionSpec as P

D = 256
CODES = 32
BINS = 601
BLOCKS = 10
STEP = 5
HEADS = 1238
MATS = 12
P_SIZE = 1054464
HPAD = 1280
CAT = D + CODES
A_ROWS = CAT + BLOCKS * D
BF = jnp.bfloat16
F32 = jnp.float32
GELU_C = 0.7978845608028654
GELU_K = 0.044715


def nn(a, b):
    return jnp.dot(a, b, preferred_element_type=F32)


def nt(a, b):
    return lax.dot_general(a, b, (((1,), (1,)), ((), ())), preferred_element_type=F32)


def identity(n):
    return (lax.broadcasted_iota(jnp.int32, (n, n), 0) == lax.broadcasted_iota(jnp.int32, (n, n), 1)).astype(BF)


def twice(v):
    return jnp.concatenate([v, v], 1)


def column_stats(ref, cs):
    total = jnp.sum(ref[:, cs], axis=0, keepdims=True)
    mean = total * (1.0 / D)
    square = jnp.zeros((8, mean.shape[1]), F32)
    for r in range(0, D, 32):
        cen = ref[r : r + 32, cs] - mean
        square = square + jnp.sum((cen * cen).reshape(4, 8, -1), axis=0)
    var = jnp.sum(square, axis=0, keepdims=True) * (1.0 / D)
    return mean, lax.rsqrt(var + 1e-05)


def norm_act(src, cs, gsb, xh_ref, gp_ref, rstd_ref, out):
    mean, rstd = column_stats(src, cs)
    rstd_ref[:, cs] = rstd
    for r in range(0, D, 32):
        rs = slice(r, r + 32)
        xh = (src[rs, cs] - mean) * rstd
        xh_ref[rs, cs] = xh.astype(BF)
        y = xh * twice(gsb[rs, 0:128]) + twice(gsb[rs, 128:256])
        y2 = y * y
        p = y2 * (GELU_C * GELU_K) + GELU_C
        t = jnp.tanh(y * p)
        q = t * 0.5 + 0.5
        a = y * q
        out(rs, a)
        slope = q + (a - a * q) * (p * 6.0 - 4.0 * GELU_C)
        gp_ref[rs, cs] = slope.astype(BF)


def broadcast_vectors(vt, rows):
    k = lax.broadcasted_iota(jnp.int32, (128, 128), 0)
    picks = jnp.concatenate([(k == row).astype(BF) for row in rows], 1)
    return nn(vt, picks)


def head_stage(cs, lg, dl, ints, rw):
    width = rw.shape[1]
    it8 = lax.broadcasted_iota(jnp.int32, (8, width), 0)
    low = -jnp.inf
    b75, b150, b154 = lg[600:608], lg[1200:1208], lg[1232:1240]

    def top(block):
        return jnp.max(block, axis=0, keepdims=True)

    def top_range(lo, hi):
        best = lg[lo : lo + 8]
        for r in range(lo + 8, hi, 8):
            best = jnp.maximum(best, lg[r : r + 8])
        return best

    max_v = top(jnp.maximum(top_range(0, 600), jnp.where(it8 < 1, b75, low)))
    max_r = top(
        jnp.maximum(
            jnp.maximum(top_range(608, 1200), jnp.where(it8 >= 1, b75, low)),
            jnp.where(it8 < 2, b150, low),
        )
    )
    max_c = top(
        jnp.maximum(
            jnp.maximum(top_range(1208, 1232), jnp.where(it8 >= 2, b150, low)),
            jnp.where(it8 < 2, b154, low),
        )
    )
    in_policy = (it8 >= 2) & (it8 < 6)
    max_p = top(jnp.where(in_policy, b154, low))

    def exp_range(lo, hi, best):
        acc = jnp.zeros((8, width), F32)
        for r in range(lo, hi, 8):
            e = jnp.exp(lg[r : r + 8] - best)
            lg[r : r + 8] = e
            acc = acc + e
        return acc

    e75 = jnp.exp(b75 - jnp.where(it8 < 1, max_v, max_r))
    e150 = jnp.exp(b150 - jnp.where(it8 < 2, max_r, max_c))
    e154 = jnp.exp(b154 - jnp.where(it8 < 2, max_c, max_p))

    def total(acc):
        return rw / jnp.sum(acc, axis=0, keepdims=True)

    inv_v = total(exp_range(0, 600, max_v) + jnp.where(it8 < 1, e75, 0.0))
    inv_r = total(exp_range(608, 1200, max_r) + jnp.where(it8 >= 1, e75, 0.0) + jnp.where(it8 < 2, e150, 0.0))
    inv_c = total(exp_range(1208, 1232, max_c) + jnp.where(it8 >= 2, e150, 0.0) + jnp.where(it8 < 2, e154, 0.0))
    inv_p = total(jnp.where(in_policy, e154, 0.0))
    hit_v = ints[1:2]
    hit_r = ints[6:7] + BINS
    hit_c = ints[7:8] + 2 * BINS
    counts = jnp.where(in_policy, ints.astype(F32), 0.0)
    share = counts * (rw / jnp.sum(counts, axis=0, keepdims=True))

    def minus(value, lo, *hits):
        at = lax.broadcasted_iota(jnp.int32, value.shape, 0)
        for hit in hits:
            value = value - jnp.where(at == hit - lo, rw, 0.0)
        return value

    d75 = minus(e75 * jnp.where(it8 < 1, inv_v, inv_r), 600, hit_v, hit_r)
    d150 = minus(e150 * jnp.where(it8 < 2, inv_r, inv_c), 1200, hit_r, hit_c)
    d154 = minus(e154 * jnp.where(it8 < 2, inv_c, inv_p), 1232, hit_c) - share
    d154 = jnp.where(it8 < 6, d154, 0.0)

    def emit(lo, hi, inv, hit):
        for r in range(lo, hi, 16):
            dl[r : r + 16, cs] = minus(lg[r : r + 16] * inv, r, hit).astype(BF)

    def pair(first, second):
        return jnp.concatenate([first, second], 0).astype(BF)

    emit(0, 592, inv_v, hit_v)
    dl[592:608, cs] = pair(minus(lg[592:600] * inv_v, 592, hit_v), d75)
    emit(608, 1200, inv_r, hit_r)
    dl[1200:1216, cs] = pair(d150, minus(lg[1208:1216] * inv_c, 1208, hit_c))
    emit(1216, 1232, inv_c, hit_c)
    dl[1232:1248, cs] = pair(d154, jnp.zeros_like(d154))
    dl[1248:HPAD, cs] = jnp.zeros((HPAD - 1248, width), BF)


CB = 256
GROUP = 2


def spread(v, cs):
    return jnp.concatenate([v] * ((cs.stop - cs.start) // 128), 1)


def saved_views(t, mix, xh):
    def mixed(k):
        return mix.at[pl.ds(pl.multiple_of((t * BLOCKS + k - 1) * (D + 16), 16), D + 16)]

    def unit(k):
        return xh.at[pl.ds(pl.multiple_of((t * (BLOCKS + 1) + k) * D, D), D)]

    return mixed, unit


def forward_tower(t, refs, during=None):
    (eye, w, wh, vec, wct, wt, vt, gsb, xt, mix, xh, gp, rstd, stream, ints, width) = refs
    blocks = [slice(c, c + CB) for c in range(0, width, CB)]
    per = min(GROUP, len(blocks))
    groups = [slice(c, c + per * CB) for c in range(0, width, per * CB)]
    mixed, unit = saved_views(t, mix, xh)

    def prefetch(k):
        gsb[k % 2] = broadcast_vectors(vt[...], (k, k + BLOCKS + 1, k + 2 * BLOCKS + 2))
        row = pl.multiple_of(CAT + (k - 1) * D, 32)
        wt[k % 2] = nt(eye[...], w[t, pl.ds(row, D)]).astype(BF)

    def stage(k, c):
        cs = blocks[c]

        def keep(rs, a):
            mixed(k)[rs, cs] = a.astype(BF)

        norm_act(stream, cs, gsb.at[k % 2], unit(k), gp.at[t, k], rstd.at[pl.ds(t * (BLOCKS + 1) + k, 1)], keep)

    def product(k, group):
        return nn(wt[k % 2], mixed(k)[0:D, groups[group]])

    def add(k, group, pre):
        cs = groups[group]
        stream[:, cs] = stream[:, cs] + pre + spread(gsb[k % 2, :, 256:384], cs)

    vt[...] = nt(eye[...], vec[t]).astype(BF)
    wt[0] = nt(eye[...], w[t, 0:D]).astype(BF)
    wct[...] = nt(eye[...], w[t, D:CAT]).astype(BF)
    gsb[0] = broadcast_vectors(vt[...], (0, BLOCKS + 1, 2 * BLOCKS + 2))
    prefetch(1)
    for cs in blocks:
        it = lax.broadcasted_iota(jnp.int32, (CODES, CB), 0)
        xt[t, D:CAT, cs] = (it == ints[t, 0:1, cs]).astype(BF)
        xt[t, CAT : CAT + 16, cs] = jnp.ones((16, CB), BF)
    for c, cs in enumerate(blocks):
        pre = nn(wt[0], xt[t, 0:D, cs]) + nn(wct[...], xt[t, D:CAT, cs])
        stream[:, cs] = pre + twice(gsb[0, :, 256:384])

        def keep(rs, a):
            stream[rs, cs] = a

        norm_act(stream, cs, gsb.at[0], unit(0), gp.at[t, 0], rstd.at[pl.ds(t * (BLOCKS + 1), 1)], keep)

    def layer(k, more):
        if more:
            prefetch(k + 1)
        mixed(k)[D : D + 16, :] = jnp.ones((16, width), BF)
        for group in range(len(groups)):
            pre = product(k, group)
            ahead = group + 1 < len(groups)
            if ahead or more:
                for c in range(per):
                    stage(k if ahead else k + 1, (group + 1) % len(groups) * per + c)
            add(k, group, pre)

    for c in range(per):
        stage(1, c)

    @pl.loop(1, BLOCKS)
    def _(k):
        if during is not None:
            during(k)
        layer(k, True)

    layer(BLOCKS, False)
    for cs in blocks:
        xt[t + 1, 0:D, cs] = stream[:, cs].astype(BF)


def backward_act(cs, grad, gain, gp_ref, xh_ref, acc):
    s1 = jnp.zeros((8, CB), F32)
    s2 = jnp.zeros((8, CB), F32)
    for r in range(0, D, 16):
        rs = slice(r, r + 16)
        g = twice(gain[rs])
        dy = grad[rs, :] * gp_ref[rs, cs].astype(F32)
        prod = dy * xh_ref[rs, cs].astype(F32)
        back = dy * g
        grad[rs, :] = back
        prod_g = prod * g
        s1 = s1 + (back[0:8] + back[8:16])
        s2 = s2 + (prod_g[0:8] + prod_g[8:16])
        acc[0, rs] = acc[0, rs] + (prod[:, 0:128] + prod[:, 128:CB])
        acc[1, rs] = acc[1, rs] + (dy[:, 0:128] + dy[:, 128:CB])
    m1 = jnp.sum(s1, axis=0, keepdims=True) * (1.0 / D)
    m2 = jnp.sum(s2, axis=0, keepdims=True) * (1.0 / D)
    return m1, m2


def backward_tower(t, refs, after_head=None, during=None, before_product=None, after_weights=None):
    (eye, w, wh, vec, wht, vt, gsb, xt, mix, xh, gp, rstd, ds, ex, br, dm, acc, lg, dl, ints, rw, gw, gh, gv, ig, width) = refs
    blocks = [slice(c, c + CB) for c in range(0, width, CB)]
    per = min(GROUP, len(blocks))
    groups = [slice(c, c + per * CB) for c in range(0, width, per * CB)]
    mixed, unit = saved_views(t, mix, xh)
    vt[...] = nt(eye[...], vec[t]).astype(BF)
    for h in range(0, HPAD, D):
        wht[h : h + D, :] = nt(eye[...], wh[t, :, h : h + D]).astype(BF)

    @pl.loop(0, width // CB)
    def _(c):
        cs = pl.ds(pl.multiple_of(c * CB, CB), CB)
        lg[...] = nn(wht[...], xt[t + 1, 0:D, cs])
        head_stage(cs, lg, dl, ints[t, :, cs], rw[0:1, cs])
        value = nn(wh[t], dl[:, cs]) + ex[:, cs]
        ds[:, cs] = value
        br[BLOCKS % 2, :, cs] = value.astype(BF)

    for h in range(0, HPAD, D):
        gh[t, :, h : h + D] = nt(xt[t + 1, 0:D, :], dl[h : h + D]).astype(BF)
    if after_head is not None:
        after_head()
    acc[...] = jnp.zeros(acc.shape, F32)
    ones = jnp.ones((16, 128), BF)

    def part(c):
        return dm.at[c * D : c * D + D]

    def gains(k):
        gsb[k % 2, :, 0:128] = broadcast_vectors(vt[...], (k,))

    def row_sums(k):
        for kind in range(2):
            gv[t, kind, pl.ds(k, 1), :] = nt(ones, acc[k % 2, kind].astype(BF))[0:1]
        acc[k % 2] = jnp.zeros(acc.shape[1:], F32)

    def product(k, group):
        row = pl.multiple_of(CAT + (k - 1) * D, 32)
        back = nn(w[t, pl.ds(row, D)], br[k % 2, :, groups[group]])
        for c in range(per):
            part(group * per + c)[...] = back[:, c * CB : c * CB + CB]

    def stage(k, c, first):
        cs = blocks[c]
        m1, m2 = backward_act(cs, part(c), gsb.at[k % 2, :, 0:128], gp.at[t, k], unit(k), acc.at[k % 2])
        rs1 = rstd[pl.ds(t * (BLOCKS + 1) + k, 1), cs]
        m1 = m1 * rs1
        m2 = m2 * rs1
        for r in range(0, D, 32):
            rs = slice(r, r + 32)
            back = part(c)[rs, :] * rs1 - m1 - unit(k)[rs, cs].astype(F32) * m2
            if first:
                br[0, rs, cs] = back.astype(BF)
            else:
                value = ds[rs, cs] + back
                ds[rs, cs] = value
                br[(k + 1) % 2, rs, cs] = value.astype(BF)

    if before_product is not None:
        before_product()
    gains(BLOCKS)
    product(BLOCKS, 0)

    @pl.loop(0, BLOCKS)
    def _(i):
        k = BLOCKS - i
        if during is not None:
            during(i)
        gains(k - 1)
        for group in range(len(groups)):
            if group + 1 < len(groups):
                product(k, group + 1)
            for c in range(per):
                stage(k, group * per + c, False)
            if group == 0:
                full = nt(mixed(k)[...], br[k % 2])
                row = pl.multiple_of(CAT + (k - 1) * D, 32)
                gw[t, pl.ds(row, D), :] = full[0:D].astype(BF)
                gv[t, 2, pl.ds(k, 1), :] = full[D : D + 1]
                row_sums(k + 1)
                product(k - 1, 0)

    for c, cs in enumerate(blocks):
        part(c)[...] = ds[:, cs]
        stage(0, c, True)
    row_sums(1)
    row_sums(0)
    full = nt(xt[t], br[0])
    gw[t, 0:CAT, :] = full[0:CAT].astype(BF)
    gv[t, 2, 0:1, :] = full[CAT : CAT + 1]
    if after_weights is not None:
        after_weights()
    for cs in blocks:
        back = nn(w[t, 0:D], br[0, :, cs])
        ex[:, cs] = back
        ig[cs, :] = back.T


def compute_kernel(x_ref, ints, rw, w, wh, vec, st, ig, gw, gh, gv, eye, wct, wt, wht, vt, gsb, xt, mix, xh, gp, rstd, stream, ex, br, dm, acc, lg, dl):
    width = x_ref.shape[0]
    eye[...] = identity(D)
    for c in range(0, width, CB):
        cs = slice(c, c + CB)
        xt[0, 0:D, cs] = nt(eye[...], x_ref[cs, :]).astype(BF)
    fwd = (eye, w, wh, vec, wct, wt, vt, gsb, xt, mix, xh, gp, rstd, stream, ints, width)
    @pl.loop(0, 2)
    def _(t):
        forward_tower(t, fwd)

        @pl.loop(0, width // CB)
        def _(c):
            cs = pl.ds(pl.multiple_of(c * CB, CB), CB)
            st[t, cs, :] = nt(eye[...], xt[t + 1, 0:D, cs]).astype(BF)

    ex[...] = jnp.zeros_like(ex)

    @pl.loop(0, 2)
    def _(i):
        t = 1 - i
        backward_tower(
            t,
            (eye, w, wh, vec, wht, vt, gsb, xt, mix, xh, gp, rstd, stream, ex, br, dm, acc, lg, dl, ints, rw, gw, gh, gv, ig.at[t], width),
        )


def work_scratch(width):
    return [
        pltpu.VMEM((D, D), BF),
        pltpu.VMEM((D, CODES), BF),
        pltpu.VMEM((2, D, D), BF),
        pltpu.VMEM((HPAD, D), BF),
        pltpu.VMEM((D, 128), BF),
        pltpu.VMEM((2, D, 384), F32),
        pltpu.VMEM((3, CAT + 16, width), BF),
        pltpu.VMEM((2 * BLOCKS * (D + 16), width), BF),
        pltpu.VMEM((2 * (BLOCKS + 1) * D, width), BF),
        pltpu.VMEM((2, BLOCKS + 1, D, width), BF),
        pltpu.VMEM((24, width), F32),
        pltpu.VMEM((D, width), F32),
        pltpu.VMEM((D, width), F32),
        pltpu.VMEM((2, D, width), BF),
        pltpu.VMEM((width // CB * D, CB), F32),
        pltpu.VMEM((2, 2, D, 128), F32),
        pltpu.VMEM((HPAD, CB), F32),
        pltpu.VMEM((HPAD, width), BF),
    ]


def compute(x, ints, rw, w, wh, vec):
    width = x.shape[0]
    vm = pl.BlockSpec(memory_space=pltpu.VMEM)
    return pl.pallas_call(
        compute_kernel,
        out_shape=(
            jax.ShapeDtypeStruct((2, width, D), BF),
            jax.ShapeDtypeStruct((2, width, D), F32),
            jax.ShapeDtypeStruct((2, A_ROWS, D), BF),
            jax.ShapeDtypeStruct((2, D, HPAD), BF),
            jax.ShapeDtypeStruct((2, 3, 16, D), F32),
        ),
        in_specs=[vm] * 6,
        out_specs=(vm,) * 5,
        scratch_shapes=work_scratch(width),
        compiler_params=pltpu.CompilerParams(vmem_limit_bytes=62 * 1024 * 1024),
    )(x, ints, rw, w, wh, vec)


class Plan:
    def __init__(self, n, length):
        self.n, self.length = n, length
        self.rows128 = -(-length // 128)
        block_end, head_end = A_ROWS * D, A_ROWS * D + D * HEADS
        self.a_base, self.a_rows, self.h_first, self.h_rows, self.h_off, self.v_first, self.v_rows, self.v_off = ([] for _ in range(8))
        used = 0
        for i in range(n):
            lo, hi = i * length, (i + 1) * length
            base = min(lo, block_end) // D // 16 * 16
            top = -(-min(hi, block_end) // D)
            a_rows = -(-(top - base) // 16) * 16 if lo < block_end else 0
            first = min(max(lo - block_end, 0), D * HEADS) // HEADS
            last = -(-min(max(hi - block_end, 0), D * HEADS) // HEADS)
            h_rows = last - first if hi > block_end and lo < head_end else 0
            v_first = max(lo - head_end, 0) // D
            v_rows = -(-(hi - head_end) // D) - v_first if hi > head_end else 0
            self.a_base.append(base)
            self.a_rows.append(a_rows)
            self.h_first.append(first)
            self.h_rows.append(h_rows)
            self.h_off.append(a_rows)
            self.v_first.append(v_first)
            self.v_rows.append(v_rows)
            self.v_off.append(a_rows + 5 * h_rows)
            used = max(used, a_rows + 5 * h_rows + v_rows)
        self.heads = max(self.h_rows)
        self.image = (HEADS * self.heads // 128 + 24) // 8 * 8
        self.slot = -(-(used + 1) // 32) * 32

    def at(self, table, me):
        value = jnp.int32(table[0])
        for i in range(1, self.n):
            if table[i] != table[i - 1]:
                value = value + (me >= i).astype(jnp.int32) * (table[i] - table[i - 1])
        return value


MESH = pl.DeviceIdType.MESH


def neighbours(n):
    core = lax.axis_index("tower")
    me = lax.axis_index("dp")
    near_x = me + 1 - 2 * (me % 2)
    near_y = me + 2 - 4 * ((me // 2) % 2)
    return core, me, near_x, near_y


def at(core, index):
    return {"tower": core, "dp": index}


def greet(core, me, near_x, near_y, n, crossed=False):
    barrier = pltpu.get_barrier_semaphore()
    pl.semaphore_signal(barrier, inc=1, device_id=at(1 - core, me), device_id_type=MESH)
    for near in (near_x, near_y, near_x + near_y - me):
        pl.semaphore_signal(barrier, inc=1, device_id=at(core, near), device_id_type=MESH)
    for k in range(1, n // 4):
        pl.semaphore_signal(barrier, inc=1, device_id=at(core, (me + 4 * k) % n), device_id_type=MESH)
    for near in [near_x, near_y] + [(me + 4 * k) % n for k in range(1, n // 4)] if crossed else []:
        pl.semaphore_signal(barrier, inc=1, device_id=at(1 - core, near), device_id_type=MESH)
    return barrier


def place_shard(plan, me, p_ref, slot128, shifted, rolled):
    rows = plan.rows128
    start = me * plan.length
    shift = start % 128
    first = start // 128
    tall = shifted.shape[0]
    height = p_ref.shape[0]
    lane = lax.broadcasted_iota(jnp.int32, (height, 128), 1)
    rolled[0:8] = jnp.zeros((8, 128), F32)
    rolled[8 : 8 + height] = pltpu.roll(p_ref[...], shift, 1)
    shifted[...] = jnp.zeros((tall, 128), F32)
    moved = jnp.where(lane >= shift, rolled[8 : 8 + height], rolled[7 : 7 + height])
    shifted[16 : 16 + height] = moved
    slot128[...] = jnp.zeros(slot128.shape, F32)
    row = lax.broadcasted_iota(jnp.int32, (height, 128), 0)
    base = plan.at(plan.a_base, me)

    @pl.when(plan.at(plan.a_rows, me) > 0)
    def _():
        slot128[pl.ds(first - 2 * base, height)] = jnp.where(row + first < 2 * A_ROWS, moved, 0.0)

    v_start = (A_ROWS * D + D * HEADS) // 128
    v_rows, v_off, v_first = (plan.at(t, me) for t in (plan.v_rows, plan.v_off, plan.v_first))
    tall_v = min(height, -(-2 * max(plan.v_rows) // 8) * 8)

    @pl.when(v_rows > 0)
    def _():
        inside = plan.at([max(0, v_start - i * plan.length // 128) for i in range(plan.n)], me)
        to = 2 * v_off + first + inside - v_start - 2 * v_first
        slot128[pl.ds(to, tall_v)] = shifted[pl.ds(16 + inside, tall_v)]

    h_first, h_rows, h_off = (plan.at(t, me) for t in (plan.h_first, plan.h_rows, plan.h_off))

    @pl.when(h_rows > 0)
    def _():
        tall_h = plan.image
        begin = A_ROWS * D + HEADS * h_first - 128 * first + 128 * 16
        turn = begin % 128
        rolled[0:tall_h] = pltpu.roll(shifted[pl.ds(begin // 128, tall_h)], (128 - turn) % 128, 1)
        rolled[tall_h : tall_h + 8] = jnp.zeros((8, 128), F32)
        lane = lax.broadcasted_iota(jnp.int32, (tall_h, 128), 1)
        shifted[0:tall_h] = jnp.where(lane < 128 - turn, rolled[0:tall_h], rolled[1 : tall_h + 1])
        to = slot128.at[pl.ds(pl.multiple_of(2 * h_off, 8), 10 * plan.heads)]
        it = lax.broadcasted_iota(jnp.int32, (10, 128), 0)
        lane = lax.broadcasted_iota(jnp.int32, (10, 128), 1)
        for k in range(plan.heads):
            row, turn = HEADS * k // 128, HEADS * k % 128
            window = pltpu.roll(shifted[row : row + 16], (128 - turn) % 128, 1)
            value = jnp.where(lane < 128 - turn, window[0:10], window[1:11])
            kept = (it * 128 + lane < HEADS) & (k < h_rows)
            to[10 * k : 10 * k + 10] = to[10 * k : 10 * k + 10] + jnp.where(kept, value, 0.0)


def unpack_rows(plan, i, slot, w, heads, vectors, scratch):
    base, rows = plan.a_base[i], plan.a_rows[i]
    if rows:
        shared = i > 0 and base < plan.a_base[i - 1] + plan.a_rows[i - 1]
        lo = 0
        if shared:
            w[base : base + 16] = w[base : base + 16] + slot[0:16]
            lo = 16
        if rows > lo:
            w[base + lo : base + rows] = slot[lo:rows]
    h_rows, h_off, h_first = plan.h_rows[i], plan.h_off[i], plan.h_first[i]
    v_rows, v_off, v_first = plan.v_rows[i], plan.v_off[i], plan.v_first[i]
    if h_rows or v_rows:
        value = slot.astype(F32)
        scratch[0][...] = value[:, 0:128]
        scratch[1][...] = value[:, 128:D]
    if h_rows:
        shared = i > 0 and plan.h_rows[i - 1] and plan.h_first[i - 1] + plan.h_rows[i - 1] > h_first
        for j in range(5):
            for half in range(2):
                cols = slice(128 * half, 128 * half + 128)
                first = D * j + h_first
                value = scratch[half][pl.ds(h_off + j, h_rows, stride=5)]
                if shared:
                    heads[first : first + 1, cols] = heads[first : first + 1, cols] + value[0:1]
                    if h_rows > 1:
                        heads[first + 1 : first + h_rows, cols] = value[1:h_rows]
                else:
                    heads[first : first + h_rows, cols] = value
    if v_rows:
        shared = v_first and plan.v_first[i - 1] + plan.v_rows[i - 1] > v_first
        shared = shared or (i > 0 and plan.v_rows[i - 1] > 0 and v_first == 0)
        for half in range(2):
            cols = slice(128 * half, 128 * half + 128)
            value = scratch[half][v_off : v_off + v_rows]
            if shared:
                vectors[v_first : v_first + 1, cols] = vectors[v_first : v_first + 1, cols] + value[0:1]
                if v_rows > 1:
                    vectors[v_first + 1 : v_first + v_rows, cols] = value[1:v_rows]
            else:
                vectors[v_first : v_first + v_rows, cols] = value


def split3(value):
    hi = value.astype(BF).astype(F32)
    mid = (value - hi).astype(BF).astype(F32)
    return hi, mid, value - hi - mid


def gather_kernel(plan, p_ref, ints_ref, imp_ref, w, wh, vec, both, rw, slots, slot128, shifted, rolled, scratch, whf, vecf, send, recv):
    n = plan.n
    depth = n // 4
    core, me, near_x, near_y = neighbours(n)
    barrier = greet(core, me, near_x, near_y, n)
    place_shard(plan, me, p_ref, slot128, shifted, rolled)
    pl.semaphore_wait(barrier, depth + 3)
    half = rw.shape[1]
    started = []

    def copy(src, dst, slot, to):
        c = pltpu.make_async_remote_copy(
            src_ref=src, dst_ref=dst, send_sem=send.at[slot], recv_sem=recv.at[slot], device_id=to, device_id_type=MESH
        )
        c.start()
        started.append(c)
        return c

    mine = pl.multiple_of(core * half, half)
    theirs = pl.multiple_of((1 - core) * half, half)
    number = iter(range(1 << 20))
    ints_copy = copy(ints_ref.at[:, pl.ds(theirs, half)], both.at[core], next(number), at(1 - core, me))
    rows = plan.slot
    total = jnp.sum(imp_ref[...].astype(F32), axis=1, keepdims=True)
    lane = lax.broadcasted_iota(jnp.int32, (1, D), 1)
    hi, mid, lo = split3(total)
    left = slot128[pl.ds(0, rows, stride=2)]
    right = slot128[pl.ds(1, rows, stride=2)]
    own = jnp.concatenate([left, right], 1)
    last = jnp.where(lane == 0, hi, jnp.where(lane == 1, mid, jnp.where(lane == 2, lo, 0.0)))
    last_row = lax.broadcasted_iota(jnp.int32, (rows, D), 0) == rows - 1
    slots[core, me] = jnp.where(last_row, last, own).astype(BF)

    def column(index, k):
        return (index + n - 4 * k) % n

    def send_slot(origin, to, lo=0, hi=rows):
        ref = slots.at[core, origin, pl.ds(lo, hi - lo)]
        return copy(ref, ref, next(number), to)

    near_xy = near_x + near_y - me
    cut = rows // 2
    z_in, x_in, y_in, d_in, s_in = {}, {}, {}, {}, []
    for k in sorted(range(1, depth), key=lambda k: (min(k, depth - k), k)):
        z_in[k] = send_slot(me, at(core, (me + 4 * k) % n))
    order = [0] + list(z_in)
    for k in order:
        if k:
            z_in[k].wait_recv()
        x_in[k] = send_slot(column(me, k), at(core, near_x))
        y_in[k] = send_slot(column(me, k), at(core, near_y))
        s_in.append(send_slot(column(me, k), at(1 - core, me)))
    for k in order:
        x_in[k].wait_recv()
        first = send_slot(column(near_x, k), at(core, near_y), 0, cut)
        s_in.append(send_slot(column(near_x, k), at(1 - core, me)))
        y_in[k].wait_recv()
        second = send_slot(column(near_y, k), at(core, near_x), cut, rows)
        s_in.append(send_slot(column(near_y, k), at(1 - core, me)))
        d_in[k] = (first, second)
    for k in order:
        for c in d_in[k]:
            c.wait_recv()
        s_in.append(send_slot(column(near_xy, k), at(1 - core, me)))
    ints_copy.wait_recv()
    both[core] = ints_ref[:, pl.ds(mine, half)]
    for c in s_in:
        c.wait_recv()
    for c in started:
        c.wait_send()
    for t in range(2):
        vecf[...] = jnp.zeros(vecf.shape, F32)
        for i in range(n):
            unpack_rows(plan, i, slots[t, i], w.at[t], whf, vecf, [scratch.at[0], scratch.at[1]])
        for j in range(5):
            wh[t, :, D * j : D * j + D] = whf[D * j : D * j + D].astype(BF)
        vec[t] = vecf[...].astype(BF)
    total = jnp.zeros((1, D), F32)
    for i in range(n):
        tail = slots[0, i, rows - 16 : rows].astype(F32)
        total = total + tail[15:16]
    weight_sum = jnp.sum(jnp.where(lane < 3, total, 0.0), axis=1, keepdims=True)
    rw[...] = jnp.broadcast_to(imp_ref[:, pl.ds(mine, half)].astype(F32) / weight_sum, (8, half))


def gather(plan, p128, ints, imp):
    n, rows = plan.n, plan.slot
    half = ints.shape[1] // 2
    vm = pl.BlockSpec(memory_space=pltpu.VMEM)
    height = p128.shape[0]
    tall = max(2 * rows, height + 40) + 80
    copies = 1 + (n // 4 - 1) + 2 * (n // 4) + 2 * (n // 4) + n
    return pl.pallas_call(
        functools.partial(gather_kernel, plan),
        out_shape=(
            jax.ShapeDtypeStruct((2, A_ROWS, D), BF),
            jax.ShapeDtypeStruct((2, D, HPAD), BF),
            jax.ShapeDtypeStruct((2, 128, D), BF),
            jax.ShapeDtypeStruct((2, 8, half), jnp.int32),
            jax.ShapeDtypeStruct((8, half), F32),
        ),
        in_specs=[vm] * 3,
        out_specs=(vm,) * 5,
        scratch_shapes=[
            pltpu.VMEM((2, n, rows, D), BF),
            pltpu.VMEM((tall, 128), F32),
            pltpu.VMEM((height + 128, 128), F32),
            pltpu.VMEM((height + 40, 128), F32),
            pltpu.VMEM((2, rows, 128), F32),
            pltpu.VMEM((HPAD, D), F32),
            pltpu.VMEM((128, D), F32),
            pltpu.SemaphoreType.DMA((copies,)),
            pltpu.SemaphoreType.DMA((copies,)),
        ],
        compiler_params=pltpu.CompilerParams(
            collective_id=0, has_side_effects=True, vmem_limit_bytes=48 * 1024 * 1024
        ),
    )(p128, ints, imp)


def chunks(height):
    step = max(c for c in range(8, 113, 8) if height % c == 0)
    return [(lo, lo + step) for lo in range(0, height, step)]


def lay_flat(plan, me, slot128, flat, rolled):
    height = rolled.shape[0] - 40
    start = me * plan.length
    shift = start % 128
    first = start // 128
    base = plan.at(plan.a_base, me)
    row = lax.broadcasted_iota(jnp.int32, (height + 8, 128), 0)
    flat[...] = jnp.zeros(flat.shape, F32)

    @pl.when(plan.at(plan.a_rows, me) > 0)
    def _():
        rows = slot128[pl.ds(first - 2 * base, height + 8)]
        flat[16 : 24 + height] = jnp.where(row + first < 2 * A_ROWS, rows, 0.0)

    v_start = (A_ROWS * D + D * HEADS) // 128
    v_rows, v_off, v_first = (plan.at(t, me) for t in (plan.v_rows, plan.v_off, plan.v_first))
    tall_v = min(height, -(-2 * max(plan.v_rows) // 8) * 8)

    @pl.when(v_rows > 0)
    def _():
        inside = plan.at([max(0, v_start - i * plan.length // 128) for i in range(plan.n)], me)
        source = 2 * v_off + first + inside - v_start - 2 * v_first
        to = pl.ds(16 + inside, tall_v)
        flat[to] = flat[to] + slot128[pl.ds(source, tall_v)]

    h_first, h_rows, h_off = (plan.at(t, me) for t in (plan.h_first, plan.h_rows, plan.h_off))

    @pl.when(h_rows > 0)
    def _():
        tall_h = plan.image
        source = slot128.at[pl.ds(pl.multiple_of(2 * h_off, 8), 10 * plan.heads + 6)]
        it = lax.broadcasted_iota(jnp.int32, (16, 128), 0)
        lane = lax.broadcasted_iota(jnp.int32, (16, 128), 1)
        rolled[0 : tall_h + 8] = jnp.zeros((tall_h + 8, 128), F32)
        for k in range(plan.heads):
            row, turn = HEADS * k // 128, HEADS * k % 128
            kept = (it * 128 + lane < HEADS) & (k < h_rows)
            value = pltpu.roll(jnp.where(kept, source[10 * k : 10 * k + 16], 0.0), turn, 1)
            above = jnp.concatenate([jnp.zeros((8, 128), F32), value], 0)[7:23]
            rolled[row : row + 16] = rolled[row : row + 16] + jnp.where(lane >= turn, value, above)
        begin = A_ROWS * D + HEADS * h_first - 128 * first + 128 * 16
        turn = begin % 128
        slot128[0:8] = jnp.zeros((8, 128), F32)
        slot128[8 : 8 + tall_h] = pltpu.roll(rolled[0:tall_h], turn, 1)
        lane = lax.broadcasted_iota(jnp.int32, (tall_h, 128), 1)
        moved = jnp.where(lane >= turn, slot128[8 : 8 + tall_h], slot128[7 : 7 + tall_h])
        to = pl.ds(begin // 128, tall_h)
        flat[to] = flat[to] + moved

    rolled[0 : height + 8] = pltpu.roll(flat[16 : 24 + height], (128 - shift) % 128, 1)
    for lo, hi in chunks(height):
        lane = lax.broadcasted_iota(jnp.int32, (hi - lo, 128), 1)
        flat[lo:hi] = jnp.where(lane < 128 - shift, rolled[lo:hi], rolled[lo + 1 : hi + 1])


def pack_slots(plan, core, gw, gh, gv, rgw, rgh, rgv, slots, sums, vsum, scratch):
    total = gv[core].astype(F32) + rgv[...]
    for kind in range(3):
        vsum[kind * (BLOCKS + 1) : (kind + 1) * (BLOCKS + 1)] = total[kind, 0 : BLOCKS + 1]
    sums[...] = gh[core].astype(F32) + rgh[...].astype(F32)
    for i in range(plan.n):
        base, rows = plan.a_base[i], plan.a_rows[i]
        h_rows, h_off, h_first = plan.h_rows[i], plan.h_off[i], plan.h_first[i]
        v_rows, v_off, v_first = plan.v_rows[i], plan.v_off[i], plan.v_first[i]
        slots[i, rows : plan.slot] = jnp.zeros((plan.slot - rows, D), BF)
        if rows:
            added = gw[core, base : base + rows].astype(F32) + rgw[base : base + rows].astype(F32)
            slots[i, 0:rows] = added.astype(BF)
        if h_rows or v_rows:
            scratch[...] = jnp.zeros(scratch.shape, F32)
            for half in range(2):
                for j in range(5 if h_rows else 0):
                    cols = slice(D * j + 128 * half, D * j + 128 * half + 128)
                    scratch[half, pl.ds(h_off + j, h_rows, stride=5)] = sums[h_first : h_first + h_rows, cols]
                if v_rows:
                    scratch[half, v_off : v_off + v_rows] = vsum[v_first : v_first + v_rows, 128 * half : 128 * half + 128]
            whole = jnp.concatenate([scratch[0], scratch[1]], 1)
            slots[i, rows : plan.slot] = whole[rows:].astype(BF)


def segment_bounds():
    first = [0] + [(CAT + j * D) * D for j in range(BLOCKS + 1)]
    return list(zip(first, first[1:] + [A_ROWS * D + D * HEADS]))


def update_shard(plan, me, p_ref, m_ref, v_ref, outs, flat, squares, sq_in, push, to_plane, to_z):
    first_out, second_out, new_out, norm_out = outs
    height = p_ref.shape[0]
    start = me * plan.length
    correction = 1.0 - 0.5**STEP
    bounds = segment_bounds()

    def place(lo, hi):
        shape = (hi - lo, 128)
        return 128 * lo + 128 * lax.broadcasted_iota(jnp.int32, shape, 0) + lax.broadcasted_iota(jnp.int32, shape, 1)

    for lo, hi in chunks(height):
        spot = place(lo, hi)
        grad = jnp.where(spot < plan.length, flat[lo:hi], 0.0)
        first_new = 0.5 * m_ref[lo:hi] + 0.5 * grad
        second_new = 0.5 * v_ref[lo:hi] + 0.5 * grad * grad
        first_out[lo:hi] = first_new
        second_out[lo:hi] = second_new
        decay = jnp.where(spot < bounds[-1][1] - start, 0.01 * p_ref[lo:hi], 0.0)
        update = first_new / correction / (jnp.sqrt(second_new / correction) + 1e-06) + decay
        flat[lo:hi] = jnp.where(spot < plan.length, update, 0.0)
        new_out[lo:hi] = p_ref[lo:hi] - 0.5 * update
    squares[...] = jnp.zeros(squares.shape, F32)

    def each_segment(body):
        for j, (first, last) in enumerate(bounds):
            pl.when((first < start + plan.length) & (last > start))(lambda j=j, first=first, last=last: body(j, first, last))

    def square_sums(j, first, last):
        weight, change = jnp.zeros((8, 128), F32), jnp.zeros((8, 128), F32)
        for lo, hi in chunks(height):
            spot = place(lo, hi)
            inside = (spot >= first - start) & (spot < last - start)
            p, u = jnp.where(inside, p_ref[lo:hi], 0.0), jnp.where(inside, flat[lo:hi], 0.0)
            weight = weight + jnp.sum((p * p).reshape(-1, 8, 128), axis=0)
            change = change + jnp.sum((u * u).reshape(-1, 8, 128), axis=0)
        squares[0, j : j + 1] = jnp.sum(weight, axis=0, keepdims=True)
        squares[0, 16 + j : 17 + j] = jnp.sum(change, axis=0, keepdims=True)

    each_segment(square_sums)
    total = squares[0]
    for hop, targets in enumerate((to_plane, to_z)):
        lands = range(3) if hop == 0 else range(3, 3 + len(to_z))
        for c in [push(squares.at[hop], sq_in.at[k], to) for k, to in zip(lands, targets)]:
            c.wait_recv()
        for k in lands:
            total = total + sq_in[k]
        squares[hop + 1] = total
    norm = jnp.sqrt(jnp.sum(total, axis=1, keepdims=True))
    squares[3] = jnp.broadcast_to(norm, (32, 128))
    line = jnp.sqrt(jnp.sum(jnp.concatenate([total, jnp.zeros((96, 128), F32)], 0).T, axis=0, keepdims=True))
    norm_out[0:1] = line[:, 0:MATS]
    norm_out[1:2] = pltpu.roll(line, 112, 1)[:, 0:MATS]

    def scaled(j, first, last):
        ratio = squares[3, j : j + 1] / squares[3, 16 + j : 17 + j]
        for lo, hi in chunks(height):
            spot = place(lo, hi)
            inside = (spot >= first - start) & (spot < last - start)
            new_out[lo:hi] = jnp.where(inside, p_ref[lo:hi] - 0.5 * ratio * flat[lo:hi], new_out[lo:hi])

    each_segment(scaled)


def reduce_kernel(
    plan, gw, gh, gv, st, ig, p_ref, m_ref, v_ref,
    st_out, ig_out, first_out, second_out, new_out, norm_out,
    rgw, rgh, rgv, slots, sums, vsum, scratch, in_d, in_x, in_y, in_z, slot128, flat, rolled, squares, sq_in,
    send, recv, local,
):
    n, rows = plan.n, plan.slot
    depth, cut = n // 4, plan.slot // 2
    core, me, near_x, near_y = neighbours(n)
    near_xy = near_x + near_y - me
    barrier = greet(core, me, near_x, near_y, n)
    pl.semaphore_wait(barrier, depth + 3)
    half = st.shape[1]
    number = iter(range(1 << 20))
    started = []

    def copy(src, dst, to):
        slot = next(number)
        c = pltpu.make_async_remote_copy(
            src_ref=src, dst_ref=dst, send_sem=send.at[slot], recv_sem=recv.at[slot], device_id=to, device_id_type=MESH
        )
        c.start()
        started.append(c)
        return c

    def column(index, k):
        return (index + n - 4 * k) % n

    sibling = at(1 - core, me)
    early = [
        copy(gw.at[1 - core], rgw, sibling),
        copy(gh.at[1 - core], rgh, sibling),
        copy(gv.at[1 - core], rgv, sibling),
    ]
    mine = pl.ds(pl.multiple_of(core * half, half), half)
    late = [
        copy(st.at[1 - core], st_out.at[mine], sibling),
        copy(ig.at[1 - core], ig_out.at[mine], sibling),
    ]
    stay = [
        pltpu.make_async_copy(st.at[core], st_out.at[mine], local.at[0]),
        pltpu.make_async_copy(ig.at[core], ig_out.at[mine], local.at[1]),
    ]
    for c in stay:
        c.start()
    for c in early:
        c.wait_recv()
    pack_slots(plan, core, gw, gh, gv, rgw, rgh, rgv, slots, sums, vsum, scratch)
    order = list(range(1, depth)) + [0]
    to_x, to_y = at(core, near_x), at(core, near_y)
    halves = {}
    for k in order:
        diagonal = column(near_xy, k)
        halves[k] = (
            copy(slots.at[diagonal, pl.ds(0, cut)], in_d.at[k, pl.ds(0, cut)], to_y),
            copy(slots.at[diagonal, pl.ds(cut, rows - cut)], in_d.at[k, pl.ds(cut, rows - cut)], to_x),
        )
    fulls = {}
    for k in order:
        ox, oy = column(near_x, k), column(near_y, k)
        halves[k][0].wait_recv()
        slots[ox, 0:cut] = (slots[ox, 0:cut].astype(F32) + in_d[k, 0:cut].astype(F32)).astype(BF)
        first = copy(slots.at[ox], in_x.at[k], to_x)
        halves[k][1].wait_recv()
        slots[oy, cut:rows] = (slots[oy, cut:rows].astype(F32) + in_d[k, cut:rows].astype(F32)).astype(BF)
        fulls[k] = (first, copy(slots.at[oy], in_y.at[k], to_y))
    along = {}
    for k in order:
        own = column(me, k)
        for c in fulls[k]:
            c.wait_recv()
        if k:
            total = slots[own].astype(F32) + in_x[k].astype(F32) + in_y[k].astype(F32)
            slots[own] = total.astype(BF)
            along[k] = copy(slots.at[own], in_z.at[k], at(core, own))
    for c in along.values():
        c.wait_recv()
    total = slots[me].astype(F32) + in_x[0].astype(F32) + in_y[0].astype(F32)
    for k in along:
        total = total + in_z[k].astype(F32)
    slot128[...] = jnp.zeros(slot128.shape, F32)
    slot128[pl.ds(0, rows, stride=2)] = total[:, 0:128]
    slot128[pl.ds(1, rows, stride=2)] = total[:, 128:D]
    lay_flat(plan, me, slot128, flat, rolled)

    to_z = [at(core, column(me, k)) for k in range(1, depth)]
    outs = (first_out, second_out, new_out, norm_out)
    to_plane = [to_x, to_y, at(core, near_xy)]
    update_shard(plan, me, p_ref, m_ref, v_ref, outs, flat, squares, sq_in, copy, to_plane, to_z)
    for c in late:
        c.wait_recv()
    for c in stay:
        c.wait()
    for c in started:
        c.wait_send()


def reduce_and_update(plan, gw, gh, gv, st, ig, p128, m128, v128):
    n, rows = plan.n, plan.slot
    depth = n // 4
    half = st.shape[1]
    height = p128.shape[0]
    vm = pl.BlockSpec(memory_space=pltpu.VMEM)
    hbm = pl.BlockSpec(memory_space=pl.ANY)
    copies = 5 + 2 * depth + 2 * depth + (depth - 1) + (depth - 1) + 3
    flat32 = jax.ShapeDtypeStruct((height, 128), F32)
    return pl.pallas_call(
        functools.partial(reduce_kernel, plan),
        out_shape=(
            jax.ShapeDtypeStruct((2 * half, D), BF),
            jax.ShapeDtypeStruct((2 * half, D), F32),
            flat32,
            flat32,
            flat32,
            jax.ShapeDtypeStruct((2, MATS), F32),
        ),
        in_specs=[vm] * 3 + [hbm] * 2 + [vm] * 3,
        out_specs=(hbm, hbm, vm, vm, vm, vm),
        scratch_shapes=[
            pltpu.VMEM((A_ROWS, D), BF),
            pltpu.VMEM((D, HPAD), BF),
            pltpu.VMEM(gv.shape[1:], F32),
            pltpu.VMEM((n, rows, D), BF),
            pltpu.VMEM((D, HPAD), F32),
            pltpu.VMEM((40, D), F32),
            pltpu.VMEM((2, rows, 128), F32),
            pltpu.VMEM((depth, rows, D), BF),
            pltpu.VMEM((depth, rows, D), BF),
            pltpu.VMEM((depth, rows, D), BF),
            pltpu.VMEM((depth, rows, D), BF),
            pltpu.VMEM((max(2 * rows, height + 48) + 80, 128), F32),
            pltpu.VMEM((height + 128, 128), F32),
            pltpu.VMEM((height + 40, 128), F32),
            pltpu.VMEM((4, 32, 128), F32),
            pltpu.VMEM((2 + depth, 32, 128), F32),
            pltpu.SemaphoreType.DMA((copies,)),
            pltpu.SemaphoreType.DMA((copies,)),
            pltpu.SemaphoreType.DMA((2,)),
        ],
        compiler_params=pltpu.CompilerParams(
            collective_id=1, has_side_effects=True, vmem_limit_bytes=48 * 1024 * 1024
        ),
    )(gw, gh, gv, st, ig, p128, m128, v128)


class Copies:
    def __init__(self, send, recv):
        self.send, self.recv, self.made, self.sent = send, recv, [], set()

    def add(self, src, dst, to, recv_slot=None, only=None):
        self.made.append((src, dst, to, recv_slot, only))
        return len(self.made) - 1

    def get(self, number):
        src, dst, to, recv_slot, _ = self.made[number]
        return pltpu.make_async_remote_copy(
            src_ref=src(), dst_ref=dst(), send_sem=self.send.at[number],
            recv_sem=self.recv.at[number] if recv_slot is None else recv_slot(),
            device_id=to(), device_id_type=MESH,
        )

    def start(self, *numbers):
        for number in numbers:
            self.get(number).start()

    def arrive(self, *numbers):
        for number in numbers:
            self.get(number).wait_recv()

    def leave(self, *numbers):
        for number in numbers:
            only = self.made[number][4]
            if number not in self.sent and only is None:
                self.get(number).wait_send()
            elif number not in self.sent:
                pl.when(only())(lambda number=number: self.get(number).wait_send())
            self.sent.add(number)


def fused_fits(plan):
    depth, half = plan.n // 4, plan.slot // 2
    plain = [b + plan.slot <= A_ROWS for b, h, v in zip(plan.a_base, plan.h_rows, plan.v_rows) if not (h or v)]
    vectors = [rows for rows in plan.v_rows if rows]
    return (
        all(plain)
        and vectors == [3 * (BLOCKS + 1)]
        and plan.n % 4 == 0
        and half >= 32
        and 4 * half <= HPAD
        and 2 * depth * plan.slot <= (BLOCKS + 1) * D
        and depth == 4
        and max(plan.a_rows) <= plan.slot
    )


def train_kernel(
    plan, x_ref, codes_ref, targets_ref, visits_ref, imp_ref, p_ref, m_ref, v_ref, st_out, ig_out, flat_out, norm_out,
    w, wh, vec, both, away, rw, eye, wct, wt, wht, vt, gsb, xt, mix, xh, gp, rstd, stream, ex, br, dm, acc, lg, dl,
    gw, gh, gv, packed, st_stage, slot128, flat, rolled, vsum, vacc, vin, owned, squares, sq_in,
    send, recv, z_recv, own_recv, local, ready,
):
    n, rows = plan.n, plan.slot
    depth, hrows = n // 4, plan.slot // 2
    cut = hrows // 32 * 16
    core, me, near_x, near_y = neighbours(n)
    near_xy = near_x + near_y - me
    width = both.shape[2]
    height = p_ref.shape[0]
    first_out, second_out, new_out = (flat_out.at[i * height : (i + 1) * height] for i in range(3))
    moments = [
        pltpu.make_async_copy(src, dst, local.at[3 + i])
        for i, (src, dst) in enumerate(((m_ref, first_out), (v_ref, second_out)))
    ]
    z_me, j_me = me // 4, me % 4
    copies = Copies(send, recv)
    scratch = [slot128.at[0:rows], slot128.at[rows : 2 * rows]]
    barrier = greet(core, me, near_x, near_y, n, True)
    mine = pl.multiple_of(core * width, width)
    theirs = pl.multiple_of((1 - core) * width, width)
    x_copy = pltpu.make_async_copy(x_ref.at[pl.ds(mine, width)], st_stage.at[0], local.at[0])
    x_copy.start()
    for c in moments:
        c.start()
    for to, half in ((both.at[core], mine), (away, theirs)):
        cols = pl.ds(half, width)
        to[0:1] = codes_ref[:, cols]
        to[1:2] = targets_ref[0, :, cols]
        to[2:6] = visits_ref[:, cols]
        to[6:7] = targets_ref[1, :, cols]
        to[7:8] = targets_ref[2, :, cols]
    place_shard(plan, me, p_ref, slot128, flat, rolled)

    spare = (BLOCKS + 1) * D

    def slot_part(t, i, lo, count):
        row = pl.multiple_of(spare + rows * (t * depth + i // 4) + lo, 16)
        return xh.at[pl.ds(row, count), pl.ds(pl.multiple_of((i % 4) * D, D), D)]

    def column(index, k):
        return (index + n - 4 * k) % n

    def sibling():
        return at(1 - core, me)

    def same(make, to):
        return copies.add(make, make, to)

    low = core * hrows
    other_low = (1 - core) * hrows
    order = [0] + sorted(range(1, depth), key=lambda k: (min(k, depth - k), k))
    to_x, to_y, to_d = (lambda: at(core, near_x)), (lambda: at(core, near_y)), (lambda: at(core, near_xy))
    swap_ints = copies.add(lambda: away, lambda: both.at[core], sibling)

    def arrival(t, number):
        return own_recv.at[t * (depth + 2) + number]

    own_targets = [(lambda: near_x), (lambda: near_y)] + [lambda k=k: (me + 4 * k) % n for k in order[1:]]
    own_sends = [copies.add(lambda: slot_part(core, me, 0, rows), lambda: slot_part(core, me, 0, rows), sibling, lambda: arrival(core, 0))]
    for number, target in enumerate(own_targets, 1):
        for h in range(2):
            make = lambda h=h: slot_part(core, me, h * hrows, hrows)
            own_sends.append(
                copies.add(make, make, lambda h=h, target=target: at(h, target()), lambda number=number: arrival(core, number))
            )
    own_sends = own_sends[3 + 2 :] + own_sends[1:5] + own_sends[:1]

    def own_arrive(t, number, make):
        pltpu.make_async_remote_copy(
            src_ref=make(), dst_ref=make(), send_sem=send.at[0], recv_sem=arrival(t, number), device_id=sibling(), device_id_type=MESH
        ).wait_recv()

    gathers = []
    for t in range(2):
        g = {}
        for k in order:
            if k:
                g["x", k] = same(lambda t=t, k=k: slot_part(t, column(me, k), low, hrows), to_x)
                g["y", k] = same(lambda t=t, k=k: slot_part(t, column(me, k), low, hrows), to_y)
            g["d", k] = (
                same(lambda t=t, k=k: slot_part(t, column(near_x, k), low, cut), to_y),
                same(lambda t=t, k=k: slot_part(t, column(near_y, k), low + cut, hrows - cut), to_x),
            )
            g["s", k] = [
                same(lambda t=t, k=k, index=index: slot_part(t, column(index, k), low, hrows), sibling) if index is not me or k else None
                for index in (me, near_x, near_y, near_xy)
            ]
        gathers.append(g)

    def gather_0(t):
        pl.when(core == t)(lambda: copies.start(*own_sends))

    def gather_1(t):
        g = gathers[t]
        for number, k in enumerate(order[1:], 3):
            own_arrive(t, number, lambda: slot_part(t, me, low, hrows))
            copies.start(g["x", k], g["y", k], g["s", k][0])

    def gather_2(t):
        g = gathers[t]
        for k in order:
            if k:
                copies.arrive(g["x", k])
            else:
                own_arrive(t, 1, lambda: slot_part(t, me, low, hrows))
            copies.start(g["d", k][0], g["s", k][1])
            if k:
                copies.arrive(g["y", k])
            else:
                own_arrive(t, 2, lambda: slot_part(t, me, low, hrows))
            copies.start(g["d", k][1], g["s", k][2])

    def gather_3(t):
        g = gathers[t]
        for k in order:
            copies.arrive(*g["d", k])
            copies.start(g["s", k][3])

    def gather_4(t):
        g = gathers[t]
        pl.when(core != t)(lambda: own_arrive(t, 0, lambda: slot_part(t, me, 0, rows)))
        for k in order:
            copies.arrive(*(c for c in g["s", k] if c is not None))

    def unpack(t):
        lg[4 * D : 5 * D, 128:D] = jnp.zeros((D, 128), F32)
        vsum[...] = jnp.zeros(vsum.shape, F32)
        for i in range(n):
            row, lane = spare + rows * (t * depth + i // 4), (i % 4) * D
            unpack_rows(plan, i, xh[row : row + rows, lane : lane + D], w.at[t], lg, vsum, scratch)
        for j in range(5):
            wh[t, :, D * j : D * j + D] = lg[D * j : D * j + D].astype(BF)
        vec[t] = vsum[...].astype(BF)

    total = jnp.sum(imp_ref[...].astype(F32), axis=1, keepdims=True)
    lane_d = lax.broadcasted_iota(jnp.int32, (1, D), 1)
    hi, mid, lo = split3(total)
    left = slot128[pl.ds(0, rows, stride=2)]
    right = slot128[pl.ds(1, rows, stride=2)]
    own = jnp.concatenate([left, right], 1)
    last = jnp.where(lane_d == 0, hi, jnp.where(lane_d == 1, mid, jnp.where(lane_d == 2, lo, 0.0)))
    last_row = lax.broadcasted_iota(jnp.int32, (rows, D), 0) == rows - 1
    slot_part(core, me, 0, rows)[...] = jnp.where(last_row, last, own).astype(BF)
    pl.semaphore_wait(barrier, depth + 3 + 2 + depth - 1)
    gather_0(0)
    copies.start(swap_ints)
    eye[...] = identity(D)
    x_copy.wait()
    for c in range(0, width, CB):
        xt[0, 0:D, c : c + CB] = nt(eye[...], st_stage[0, c : c + CB, :]).astype(BF)
    gather_1(0)
    gather_0(1)
    gather_2(0)
    gather_3(0)
    copies.arrive(swap_ints)
    gather_4(0)
    unpack(0)
    total = jnp.zeros((1, D), F32)
    for i in range(n):
        row, lane = spare + rows * (i // 4), (i % 4) * D
        total = total + xh[row + rows - 16 : row + rows, lane : lane + D].astype(F32)[15:16]
    weight_sum = jnp.sum(jnp.where(lane_d < 3, total, 0.0), axis=1, keepdims=True)
    rw[...] = jnp.broadcast_to(imp_ref[:, pl.ds(mine, width)].astype(F32) / weight_sum, (8, width))

    fwd = (eye, w, wh, vec, wct, wt, vt, gsb, xt, mix, xh, gp, rstd, stream, both, width)

    def during_forward(k):
        pl.when(k == 1)(lambda: gather_1(1))
        pl.when(k == 4)(lambda: gather_2(1))
        pl.when(k == 7)(lambda: gather_3(1))

    def emit_states(t):
        for c in range(0, width, CB):
            st_stage[t, c : c + CB, :] = nt(eye[...], xt[t + 1, 0:D, c : c + CB]).astype(BF)

    forward_tower(0, fwd, during_forward)
    gather_4(1)
    copies.leave(*range(len(copies.made)))
    unpack(1)
    forward_tower(1, fwd, None)
    emit_states(0)
    emit_states(1)
    out_rows = pl.ds(mine, width)
    st_copy = copies.add(lambda: st_stage.at[1 - core], lambda: st_out.at[out_rows], sibling)
    copies.start(st_copy)
    st_stay = pltpu.make_async_copy(st_stage.at[core], st_out.at[out_rows], local.at[1])
    st_stay.start()

    packed_of = [i for i in range(n) if plan.h_rows[i] or plan.v_rows[i]]
    owner = plan.v_rows.index(3 * (BLOCKS + 1))

    early = (2, 3)

    def piece(t, zz, b, lo, count):
        if t == 1 and zz in early:
            arena, first, q = dl, 0, 7 * early.index(zz) + b
        elif t == 1:
            arena, first, q = mix, BLOCKS * (D + 16), 7 * zz + b
        else:
            arena, first, q = xh, spare, 7 * zz + b
        row = pl.multiple_of(first + hrows * (q // 4) + lo, 16)
        return arena.at[pl.ds(row, count), pl.ds(pl.multiple_of((q % 4) * D, D), D)]

    def block(t, zz, b):
        return piece(t, zz, b, 0, hrows)

    def z_in(h, k):
        return st_stage.at[0, pl.ds(pl.multiple_of(hrows * (h * (depth - 1) + k - 1), 16), hrows)]

    def z_out(t, zz):
        if t == 1 and zz in early:
            return st_stage.at[1, pl.ds(hrows * early.index(zz), hrows)]
        return block(t, zz, j_me)

    def slot_half(t, i, lo):
        if i in packed_of:
            return packed.at[packed_of.index(i), pl.ds(pl.multiple_of(lo, 16), hrows)]
        return gw.at[t, pl.ds(pl.multiple_of(plan.a_base[i] + lo, 16), hrows)]

    j_x, j_y, j_d = near_x % 4, near_y % 4, near_xy % 4
    direct = ((0, 0),)
    jobs = {}
    for t in range(2):
        for zz in range(depth):
            job = {}
            job["swap"] = [
                copies.add(lambda t=t, i=4 * zz + j: slot_half(t, i, other_low), lambda t=t, zz=zz, j=j: block(t, zz, j), sibling)
                for j in range(4)
            ]
            if (t, zz) in direct:
                job["d"] = [copies.add(lambda t=t, zz=zz: block(t, zz, j_d), lambda t=t, zz=zz: block(t, zz, 4), to_d)]
            else:
                job["d"] = [
                    copies.add(
                        lambda t=t, zz=zz, lo=lo, count=count: piece(t, zz, j_d, lo, count),
                        lambda t=t, zz=zz, lo=lo, count=count: piece(t, zz, 4, lo, count),
                        to,
                    )
                    for to, lo, count in ((to_y, 0, cut), (to_x, cut, hrows - cut))
                ]
            job["x"] = copies.add(lambda t=t, zz=zz: block(t, zz, j_x), lambda t=t, zz=zz: block(t, zz, 5), to_x)
            job["y"] = copies.add(lambda t=t, zz=zz: block(t, zz, j_y), lambda t=t, zz=zz: block(t, zz, 6), to_y)
            job["z"] = copies.add(
                lambda t=t, zz=zz: z_out(t, zz),
                lambda zz=zz: z_in(core, (zz + depth - z_me) % depth),
                lambda t=t, zz=zz: at(t, 4 * zz + j_me),
                lambda zz=zz: z_recv.at[core * depth + (zz + depth - z_me) % depth],
                lambda zz=zz: z_me != zz,
            )
            jobs[t, zz] = job

    def pack(t, planes):
        wanted = [i for i in packed_of if i // 4 in planes]
        for i in wanted:
            a_rows, h_rows, h_off, h_first = plan.a_rows[i], plan.h_rows[i], plan.h_off[i], plan.h_first[i]
            to = packed.at[packed_of.index(i)]
            for part in scratch:
                part[...] = jnp.zeros(part.shape, F32)
            lo16, hi16 = h_first // 16 * 16, -(-(h_first + h_rows) // 16) * 16
            for half in range(2):
                for j in range(5 if h_rows else 0):
                    cols = slice(D * j + 128 * half, D * j + 128 * half + 128)
                    value = gh[t, lo16:hi16, cols].astype(F32)[h_first - lo16 : h_first - lo16 + h_rows]
                    scratch[half][pl.ds(h_off + j, h_rows, stride=5)] = value
            whole = jnp.concatenate([scratch[0][...], scratch[1][...]], 1)
            to[a_rows:rows] = whole[a_rows:].astype(BF)
            if a_rows:
                to[0:a_rows] = gw[t, plan.a_base[i] : plan.a_base[i] + a_rows]

    def plus(*refs):
        value = refs[0][...].astype(F32)
        for ref in refs[1:]:
            value = value + ref[...].astype(F32)
        return value

    def sum_0(t, zz):
        copies.start(*jobs[t, zz]["swap"])

    def sum_1(t, zz):
        job = jobs[t, zz]
        for j in range(4):
            copies.arrive(job["swap"][j])
            target = block(t, zz, j)
            target[...] = plus(slot_half(t, 4 * zz + j, low), target).astype(BF)
        copies.start(*job["d"])
        if (t, zz) in direct:
            copies.start(job["x"], job["y"])

    def sum_2(t, zz):
        job = jobs[t, zz]
        for side, copy, j, lo, count in (("x", job["d"][0], j_x, 0, cut), ("y", job["d"][1], j_y, cut, hrows - cut)):
            copies.arrive(copy)
            target = piece(t, zz, j, lo, count)
            target[...] = plus(target, piece(t, zz, 4, lo, count)).astype(BF)
            copies.start(job[side])

    def sum_3(t, zz):
        job = jobs[t, zz]
        copies.arrive(job["x"], job["y"])
        value = plus(block(t, zz, j_me), block(t, zz, 5), block(t, zz, 6))
        if (t, zz) in direct:
            copies.arrive(*job["d"])
            value = value + block(t, zz, 4)[...].astype(F32)

        @pl.when(z_me != zz)
        def _():
            z_out(t, zz)[...] = value.astype(BF)
            copies.start(job["z"])

        @pl.when((z_me == zz) & (core == t))
        def _():
            final(core)[...] = value

        @pl.when((z_me == zz) & (core != t))
        def _():
            outgo[...] = value
            copies.start(hand_over)

    def sum_4():
        copies.arrive(hand_over)
        for h in range(2):
            for k in range(1, depth):
                src = z_in(h, k)
                pltpu.make_async_remote_copy(
                    src_ref=src, dst_ref=src, send_sem=send.at[0], recv_sem=z_recv.at[h * depth + k], device_id=sibling(), device_id_type=MESH
                ).wait_recv()
                final(h)[...] = final(h)[...] + src[...].astype(F32)

    def final(h):
        return owned.at[h]

    outgo = owned.at[2]

    def vector_step(step):
        sources = [gv.at[1 - core], vacc.at[0], vacc.at[1]]
        along = [lambda k=k: at(core, (me + 4 * k) % n) for k in range(1, depth)]
        targets = [[sibling], [to_x, to_y, to_d], along]
        if step:
            base = gv[core] if step == 1 else vacc[step - 2]
            for number, k in vector_copies[-1]:
                copies.arrive(number)
                base = base + vin[k]
            vacc[step - 1] = base
        if step < 3:
            started = []
            for k, to in enumerate(targets[step], (0, 1, 4)[step]):
                number = copies.add(lambda step=step: sources[step], lambda k=k: vin.at[k], to)
                copies.start(number)
                started.append((number, k))
            vector_copies.append(started)

    vector_copies = []
    hand_over = copies.add(lambda: outgo, lambda: final(core), sibling)
    peers = [(1 - core, me), (core, near_x), (core, near_y), (core, near_xy)] + [(1 - core, (me + 4 * k) % n) for k in range(1, depth)] + [(core, (me + 4 * k) % n) for k in range(1, depth)]

    bwd = (eye, w, wh, vec, wht, vt, gsb, xt, mix, xh, gp, rstd, stream, ex, br, dm, acc, lg, dl, both, rw, gw, gh, gv, dm, width)
    ig_copies = [copies.add(lambda: dm, lambda: ig_out.at[out_rows], sibling, None, lambda t=t: core != t) for t in range(2)]

    def ig_local():
        return pltpu.make_async_copy(dm, ig_out.at[out_rows], local.at[2])

    def emit_inputs(t):
        pl.when(core == t)(lambda: ig_local().start())
        pl.when(core != t)(lambda: copies.start(ig_copies[t]))

    def free_inputs(t):
        pl.when(core == t)(lambda: ig_local().wait())
        pl.when(core != t)(lambda: copies.get(ig_copies[t]).wait_send())

    def signal_ready(which):
        for to_core, to_index in peers:
            pl.semaphore_signal(ready.at[which], inc=1, device_id=at(to_core, to_index), device_id_type=MESH)

    def wait_ready(which):
        pl.semaphore_wait(ready.at[which], len(peers))

    def schedule(i, steps):
        for step in sorted({s[0] for s in steps}):

            def run(step=step):
                for s, f, *args in steps:
                    if s == step:
                        f(*args)

            pl.when(i == step)(run)

    def after_head_1():
        copies.leave(st_copy)
        st_stay.wait()
        signal_ready(0)

    def during_backward_1(i):
        schedule(i, [
            (1, wait_ready, 0), (1, pack, 1, (3,)), (1, sum_0, 1, 3),
            (2, sum_1, 1, 3),
            (4, pack, 1, (2,)), (4, sum_0, 1, 2), (4, sum_2, 1, 3),
            (5, sum_1, 1, 2),
            (7, sum_2, 1, 2), (7, sum_3, 1, 3),
        ])

    ex[...] = jnp.zeros_like(ex)
    backward_tower(1, bwd, after_head_1, during_backward_1, None, lambda: sum_3(1, 2))
    emit_inputs(1)
    signal_ready(1)
    for zz in early:
        job = jobs[1, zz]
        copies.leave(*job["swap"], *job["d"], job["x"], job["y"])

    def after_head_0():
        wait_ready(1)
        sum_0(1, 1)
        sum_0(1, 0)
        pack(0, (3,))
        sum_0(0, 3)

    def during_backward_0(i):
        schedule(i, [
            (0, sum_1, 1, 1), (0, sum_1, 1, 0),
            (1, sum_1, 0, 3),
            (3, sum_2, 1, 1), (3, sum_2, 1, 0),
            (4, pack, 0, (2,)), (4, sum_0, 0, 2), (4, sum_2, 0, 3),
            (5, sum_1, 0, 2),
            (7, sum_3, 1, 1), (7, sum_3, 1, 0),
            (8, sum_0, 0, 1), (8, sum_2, 0, 2), (8, sum_3, 0, 3),
            (9, sum_1, 0, 1),
        ])

    def after_weights():
        sum_0(0, 0)
        vector_step(0)
        sum_2(0, 1)

    backward_tower(0, bwd, after_head_0, during_backward_0, lambda: free_inputs(1), after_weights)
    emit_inputs(0)
    sum_1(0, 0)
    vector_step(1)
    sum_3(0, 2)
    sum_3(0, 1)
    sum_3(0, 0)
    vector_step(2)
    sum_4()
    vector_step(3)

    slot128[...] = jnp.zeros(slot128.shape, F32)
    for h in range(2):
        slot128[pl.ds(2 * hrows * h, hrows, stride=2)] = final(h)[:, 0:128]
        slot128[pl.ds(2 * hrows * h + 1, hrows, stride=2)] = final(h)[:, 128:D]

    @pl.when(me == owner)
    def _():
        for kind in range(3):
            first = 2 * (plan.v_off[owner] + kind * (BLOCKS + 1))
            for h in range(2):
                value = vacc[2, kind, 0 : BLOCKS + 1, 128 * h : 128 * h + 128]
                slot128[pl.ds(first + h, BLOCKS + 1, stride=2)] = value

    def push(src, dst, to):
        number = copies.add(lambda: src, lambda: dst, lambda: to)
        copies.start(number)
        return copies.get(number)

    lay_flat(plan, me, slot128, flat, rolled)
    for c in moments:
        c.wait()
    update_shard(
        plan, me, p_ref, first_out, second_out, (first_out, second_out, new_out, norm_out),
        flat, squares, sq_in, push, [to_x(), to_y(), to_d()], [at(core, (me + 4 * k) % n) for k in range(1, depth)],
    )
    copies.arrive(st_copy)
    pl.when(core == 0)(lambda: copies.arrive(ig_copies[0]))
    pl.when(core == 1)(lambda: copies.arrive(ig_copies[1]))
    free_inputs(0)
    copies.sent.update(ig_copies)
    copies.leave(*range(len(copies.made)))


def train(plan, latent, codes, targets, visits, imp, p128, m128, v128):
    n, rows = plan.n, plan.slot
    depth, hrows = n // 4, rows // 2
    width = codes.shape[1] // 2
    height = p128.shape[0]
    vm = pl.BlockSpec(memory_space=pltpu.VMEM)
    hbm = pl.BlockSpec(memory_space=pl.ANY)
    packed = sum(1 for h, v in zip(plan.h_rows, plan.v_rows) if h or v)
    return pl.pallas_call(
        functools.partial(train_kernel, plan),
        out_shape=(
            jax.ShapeDtypeStruct((2 * width, D), BF),
            jax.ShapeDtypeStruct((2 * width, D), F32),
            jax.ShapeDtypeStruct((3 * height, 128), F32),
            jax.ShapeDtypeStruct((2, MATS), F32),
        ),
        in_specs=[hbm] + [vm] * 5 + [hbm] * 2,
        out_specs=(hbm, hbm, vm, vm),
        scratch_shapes=[
            pltpu.VMEM((2, A_ROWS, D), BF),
            pltpu.VMEM((2, D, HPAD), BF),
            pltpu.VMEM((2, 128, D), BF),
            pltpu.VMEM((2, 8, width), jnp.int32),
            pltpu.VMEM((8, width), jnp.int32),
            pltpu.VMEM((8, width), F32),
            *work_scratch(width),
            pltpu.VMEM((2, A_ROWS, D), BF),
            pltpu.VMEM((2, D, HPAD), BF),
            pltpu.VMEM((2, 3, 16, D), F32),
            pltpu.VMEM((packed, rows, D), BF),
            pltpu.VMEM((2, width, D), BF),
            pltpu.VMEM((max(2 * rows, height + 48) + 80, 128), F32),
            pltpu.VMEM((height + 128, 128), F32),
            pltpu.VMEM((height + 40, 128), F32),
            pltpu.VMEM((128, D), F32),
            pltpu.VMEM((3, 3, 16, D), F32),
            pltpu.VMEM((3 + depth, 3, 16, D), F32),
            pltpu.VMEM((3, hrows, D), F32),
            pltpu.VMEM((4, 32, 128), F32),
            pltpu.VMEM((2 + depth, 32, 128), F32),
            pltpu.SemaphoreType.DMA((11 * n,)),
            pltpu.SemaphoreType.DMA((11 * n,)),
            pltpu.SemaphoreType.DMA((2 * depth,)),
            pltpu.SemaphoreType.DMA((2 * (depth + 2),)),
            pltpu.SemaphoreType.DMA((5,)),
            pltpu.SemaphoreType.REGULAR((2,)),
        ],
        compiler_params=pltpu.CompilerParams(
            collective_id=2, has_side_effects=True, vmem_limit_bytes=63 * 1024 * 1024
        ),
    )(latent, codes, targets, visits, imp, p128, m128, v128)


def on_device(latent, codes, targets, visits, importance, params, first_moment, second_moment):
    me = lax.axis_index("tower")
    row_count = latent.shape[0]
    half = row_count // 2
    shard_len = params.shape[1]
    plan = Plan(lax.axis_size("dp"), shard_len)
    height = -(-plan.rows128 // 8) * 8
    p128, m128, v128 = (
        jnp.pad(v, ((0, 0), (0, 128 * height - shard_len))).reshape(height, 128) for v in (params, first_moment, second_moment)
    )
    if fused_fits(plan):
        states_out, inputs_out, flat, norms = train(
            plan, latent, codes, targets.transpose(1, 0, 2), visits[0].T, importance[None], p128, m128, v128
        )
    else:
        ints = jnp.concatenate([codes, targets[0, :1], visits[0].T, targets[0, 1:]], 0)
        x = lax.dynamic_slice_in_dim(latent, me * half, half, 0)
        w, wh, vec, both, rw = gather(plan, p128, ints, importance[None])
        st, ig, gw, gh, gv = compute(x, both, rw, w, wh, vec)
        states_out, inputs_out, *flat, norms = reduce_and_update(plan, gw, gh, gv, st, ig, p128, m128, v128)
        flat = jnp.concatenate(flat)
    flat = flat.reshape(1, -1)
    first, second, new = (flat[:, i * 128 * height : i * 128 * height + shard_len] for i in range(3))
    return (states_out[None], inputs_out[None], first, second, new, new.astype(BF), norms[None])


def solution(mesh):
    in_specs = (
        P("dp", None),
        P("tower", "dp"),
        P("tower", None, "dp"),
        P("tower", "dp", None),
        P("dp"),
        P("tower", "dp"),
        P("tower", "dp"),
        P("tower", "dp"),
    )
    out_specs = (
        P("tower", "dp", None),
        P("tower", "dp", None),
        P("tower", "dp"),
        P("tower", "dp"),
        P("tower", "dp"),
        P("tower", "dp"),
        P("tower", None, None),
    )
    return jax.shard_map(
        on_device, mesh=mesh, in_specs=in_specs, out_specs=out_specs, check_vma=False
    )
```

```python
import functools

import jax
import jax.numpy as jnp
from jax import lax
from jax.experimental import pallas as pl
from jax.experimental.pallas import tpu as pltpu
from jax.sharding import PartitionSpec as P

D = 256
CODES = 32
BINS = 601
BLOCKS = 10
STEP = 5
HEADS = 1238
MATS = 12
P_SIZE = 1054464
HPAD = 1280
CAT = D + CODES
A_ROWS = CAT + BLOCKS * D
BF = jnp.bfloat16
F32 = jnp.float32
GELU_C = 0.7978845608028654
GELU_K = 0.044715


def nn(a, b):
    return jnp.dot(a, b, preferred_element_type=F32)


def nt(a, b):
    return lax.dot_general(a, b, (((1,), (1,)), ((), ())), preferred_element_type=F32)


def identity(n):
    return (lax.broadcasted_iota(jnp.int32, (n, n), 0) == lax.broadcasted_iota(jnp.int32, (n, n), 1)).astype(BF)


def twice(v):
    return jnp.concatenate([v, v], 1)


def column_stats(ref, cs):
    total = jnp.sum(ref[:, cs], axis=0, keepdims=True)
    mean = total * (1.0 / D)
    square = jnp.zeros((8, mean.shape[1]), F32)
    for r in range(0, D, 32):
        cen = ref[r : r + 32, cs] - mean
        square = square + jnp.sum((cen * cen).reshape(4, 8, -1), axis=0)
    var = jnp.sum(square, axis=0, keepdims=True) * (1.0 / D)
    return mean, lax.rsqrt(var + 1e-05)


def norm_act(src, cs, gsb, xh_ref, gp_ref, rstd_ref, out):
    mean, rstd = column_stats(src, cs)
    rstd_ref[:, cs] = rstd
    for r in range(0, D, 32):
        rs = slice(r, r + 32)
        xh = (src[rs, cs] - mean) * rstd
        xh_ref[rs, cs] = xh.astype(BF)
        y = xh * twice(gsb[rs, 0:128]) + twice(gsb[rs, 128:256])
        y2 = y * y
        p = y2 * (GELU_C * GELU_K) + GELU_C
        t = jnp.tanh(y * p)
        q = t * 0.5 + 0.5
        a = y * q
        out(rs, a)
        slope = q + (a - a * q) * (p * 6.0 - 4.0 * GELU_C)
        gp_ref[rs, cs] = slope.astype(BF)


def broadcast_vectors(vt, rows):
    k = lax.broadcasted_iota(jnp.int32, (128, 128), 0)
    picks = jnp.concatenate([(k == row).astype(BF) for row in rows], 1)
    return nn(vt, picks)


def head_stage(cs, lg, dl, ints, rw):
    width = rw.shape[1]
    it8 = lax.broadcasted_iota(jnp.int32, (8, width), 0)
    low = -jnp.inf
    b75, b150, b154 = lg[600:608], lg[1200:1208], lg[1232:1240]

    def top(block):
        return jnp.max(block, axis=0, keepdims=True)

    def top_range(lo, hi):
        best = lg[lo : lo + 8]
        for r in range(lo + 8, hi, 8):
            best = jnp.maximum(best, lg[r : r + 8])
        return best

    max_v = top(jnp.maximum(top_range(0, 600), jnp.where(it8 < 1, b75, low)))
    max_r = top(
        jnp.maximum(
            jnp.maximum(top_range(608, 1200), jnp.where(it8 >= 1, b75, low)),
            jnp.where(it8 < 2, b150, low),
        )
    )
    max_c = top(
        jnp.maximum(
            jnp.maximum(top_range(1208, 1232), jnp.where(it8 >= 2, b150, low)),
            jnp.where(it8 < 2, b154, low),
        )
    )
    in_policy = (it8 >= 2) & (it8 < 6)
    max_p = top(jnp.where(in_policy, b154, low))

    def exp_range(lo, hi, best):
        acc = jnp.zeros((8, width), F32)
        for r in range(lo, hi, 8):
            e = jnp.exp(lg[r : r + 8] - best)
            lg[r : r + 8] = e
            acc = acc + e
        return acc

    e75 = jnp.exp(b75 - jnp.where(it8 < 1, max_v, max_r))
    e150 = jnp.exp(b150 - jnp.where(it8 < 2, max_r, max_c))
    e154 = jnp.exp(b154 - jnp.where(it8 < 2, max_c, max_p))

    def total(acc):
        return rw / jnp.sum(acc, axis=0, keepdims=True)

    inv_v = total(exp_range(0, 600, max_v) + jnp.where(it8 < 1, e75, 0.0))
    inv_r = total(exp_range(608, 1200, max_r) + jnp.where(it8 >= 1, e75, 0.0) + jnp.where(it8 < 2, e150, 0.0))
    inv_c = total(exp_range(1208, 1232, max_c) + jnp.where(it8 >= 2, e150, 0.0) + jnp.where(it8 < 2, e154, 0.0))
    inv_p = total(jnp.where(in_policy, e154, 0.0))
    hit_v = ints[1:2]
    hit_r = ints[6:7] + BINS
    hit_c = ints[7:8] + 2 * BINS
    counts = jnp.where(in_policy, ints.astype(F32), 0.0)
    share = counts * (rw / jnp.sum(counts, axis=0, keepdims=True))

    def minus(value, lo, *hits):
        at = lax.broadcasted_iota(jnp.int32, value.shape, 0)
        for hit in hits:
            value = value - jnp.where(at == hit - lo, rw, 0.0)
        return value

    d75 = minus(e75 * jnp.where(it8 < 1, inv_v, inv_r), 600, hit_v, hit_r)
    d150 = minus(e150 * jnp.where(it8 < 2, inv_r, inv_c), 1200, hit_r, hit_c)
    d154 = minus(e154 * jnp.where(it8 < 2, inv_c, inv_p), 1232, hit_c) - share
    d154 = jnp.where(it8 < 6, d154, 0.0)

    def emit(lo, hi, inv, hit):
        for r in range(lo, hi, 16):
            dl[r : r + 16, cs] = minus(lg[r : r + 16] * inv, r, hit).astype(BF)

    def pair(first, second):
        return jnp.concatenate([first, second], 0).astype(BF)

    emit(0, 592, inv_v, hit_v)
    dl[592:608, cs] = pair(minus(lg[592:600] * inv_v, 592, hit_v), d75)
    emit(608, 1200, inv_r, hit_r)
    dl[1200:1216, cs] = pair(d150, minus(lg[1208:1216] * inv_c, 1208, hit_c))
    emit(1216, 1232, inv_c, hit_c)
    dl[1232:1248, cs] = pair(d154, jnp.zeros_like(d154))
    dl[1248:HPAD, cs] = jnp.zeros((HPAD - 1248, width), BF)


CB = 256
GROUP = 2


def spread(v, cs):
    return jnp.concatenate([v] * ((cs.stop - cs.start) // 128), 1)


def saved_views(t, mix, xh):
    def mixed(k):
        return mix.at[pl.ds(pl.multiple_of((t * BLOCKS + k - 1) * (D + 16), 16), D + 16)]

    def unit(k):
        return xh.at[pl.ds(pl.multiple_of((t * (BLOCKS + 1) + k) * D, D), D)]

    return mixed, unit


def forward_tower(t, refs, during=None):
    (eye, w, wh, vec, wct, wt, vt, gsb, xt, mix, xh, gp, rstd, stream, ints, width) = refs
    blocks = [slice(c, c + CB) for c in range(0, width, CB)]
    per = min(GROUP, len(blocks))
    groups = [slice(c, c + per * CB) for c in range(0, width, per * CB)]
    mixed, unit = saved_views(t, mix, xh)

    def prefetch(k):
        gsb[k % 2] = broadcast_vectors(vt[...], (k, k + BLOCKS + 1, k + 2 * BLOCKS + 2))
        row = pl.multiple_of(CAT + (k - 1) * D, 32)
        wt[k % 2] = nt(eye[...], w[t, pl.ds(row, D)]).astype(BF)

    def stage(k, c):
        cs = blocks[c]

        def keep(rs, a):
            mixed(k)[rs, cs] = a.astype(BF)

        norm_act(stream, cs, gsb.at[k % 2], unit(k), gp.at[t, k], rstd.at[pl.ds(t * (BLOCKS + 1) + k, 1)], keep)

    def product(k, group):
        return nn(wt[k % 2], mixed(k)[0:D, groups[group]])

    def add(k, group, pre):
        cs = groups[group]
        stream[:, cs] = stream[:, cs] + pre + spread(gsb[k % 2, :, 256:384], cs)

    vt[...] = nt(eye[...], vec[t]).astype(BF)
    wt[0] = nt(eye[...], w[t, 0:D]).astype(BF)
    wct[...] = nt(eye[...], w[t, D:CAT]).astype(BF)
    gsb[0] = broadcast_vectors(vt[...], (0, BLOCKS + 1, 2 * BLOCKS + 2))
    prefetch(1)
    for cs in blocks:
        it = lax.broadcasted_iota(jnp.int32, (CODES, CB), 0)
        xt[t, D:CAT, cs] = (it == ints[t, 0:1, cs]).astype(BF)
        xt[t, CAT : CAT + 16, cs] = jnp.ones((16, CB), BF)
    for c, cs in enumerate(blocks):
        pre = nn(wt[0], xt[t, 0:D, cs]) + nn(wct[...], xt[t, D:CAT, cs])
        stream[:, cs] = pre + twice(gsb[0, :, 256:384])

        def keep(rs, a):
            stream[rs, cs] = a

        norm_act(stream, cs, gsb.at[0], unit(0), gp.at[t, 0], rstd.at[pl.ds(t * (BLOCKS + 1), 1)], keep)

    def layer(k, more):
        if more:
            prefetch(k + 1)
        mixed(k)[D : D + 16, :] = jnp.ones((16, width), BF)
        for group in range(len(groups)):
            pre = product(k, group)
            ahead = group + 1 < len(groups)
            if ahead or more:
                for c in range(per):
                    stage(k if ahead else k + 1, (group + 1) % len(groups) * per + c)
            add(k, group, pre)

    for c in range(per):
        stage(1, c)

    @pl.loop(1, BLOCKS)
    def _(k):
        if during is not None:
            during(k)
        layer(k, True)

    layer(BLOCKS, False)
    for cs in blocks:
        xt[t + 1, 0:D, cs] = stream[:, cs].astype(BF)


def backward_act(cs, grad, gain, gp_ref, xh_ref, acc):
    s1 = jnp.zeros((8, CB), F32)
    s2 = jnp.zeros((8, CB), F32)
    for r in range(0, D, 16):
        rs = slice(r, r + 16)
        g = twice(gain[rs])
        dy = grad[rs, :] * gp_ref[rs, cs].astype(F32)
        prod = dy * xh_ref[rs, cs].astype(F32)
        back = dy * g
        grad[rs, :] = back
        prod_g = prod * g
        s1 = s1 + (back[0:8] + back[8:16])
        s2 = s2 + (prod_g[0:8] + prod_g[8:16])
        acc[0, rs] = acc[0, rs] + (prod[:, 0:128] + prod[:, 128:CB])
        acc[1, rs] = acc[1, rs] + (dy[:, 0:128] + dy[:, 128:CB])
    m1 = jnp.sum(s1, axis=0, keepdims=True) * (1.0 / D)
    m2 = jnp.sum(s2, axis=0, keepdims=True) * (1.0 / D)
    return m1, m2


def backward_tower(t, refs, after_head=None, during=None, before_product=None, after_weights=None):
    (eye, w, wh, vec, wht, vt, gsb, xt, mix, xh, gp, rstd, ds, ex, br, dm, acc, lg, dl, ints, rw, gw, gh, gv, ig, width) = refs
    blocks = [slice(c, c + CB) for c in range(0, width, CB)]
    per = min(GROUP, len(blocks))
    groups = [slice(c, c + per * CB) for c in range(0, width, per * CB)]
    mixed, unit = saved_views(t, mix, xh)
    vt[...] = nt(eye[...], vec[t]).astype(BF)
    for h in range(0, HPAD, D):
        wht[h : h + D, :] = nt(eye[...], wh[t, :, h : h + D]).astype(BF)

    @pl.loop(0, width // CB)
    def _(c):
        cs = pl.ds(pl.multiple_of(c * CB, CB), CB)
        lg[...] = nn(wht[...], xt[t + 1, 0:D, cs])
        head_stage(cs, lg, dl, ints[t, :, cs], rw[0:1, cs])
        value = nn(wh[t], dl[:, cs]) + ex[:, cs]
        ds[:, cs] = value
        br[BLOCKS % 2, :, cs] = value.astype(BF)

    for h in range(0, HPAD, D):
        gh[t, :, h : h + D] = nt(xt[t + 1, 0:D, :], dl[h : h + D]).astype(BF)
    if after_head is not None:
        after_head()
    acc[...] = jnp.zeros(acc.shape, F32)
    ones = jnp.ones((16, 128), BF)

    def part(c):
        return dm.at[c * D : c * D + D]

    def gains(k):
        gsb[k % 2, :, 0:128] = broadcast_vectors(vt[...], (k,))

    def row_sums(k):
        for kind in range(2):
            gv[t, kind, pl.ds(k, 1), :] = nt(ones, acc[k % 2, kind].astype(BF))[0:1]
        acc[k % 2] = jnp.zeros(acc.shape[1:], F32)

    def product(k, group):
        row = pl.multiple_of(CAT + (k - 1) * D, 32)
        back = nn(w[t, pl.ds(row, D)], br[k % 2, :, groups[group]])
        for c in range(per):
            part(group * per + c)[...] = back[:, c * CB : c * CB + CB]

    def stage(k, c, first):
        cs = blocks[c]
        m1, m2 = backward_act(cs, part(c), gsb.at[k % 2, :, 0:128], gp.at[t, k], unit(k), acc.at[k % 2])
        rs1 = rstd[pl.ds(t * (BLOCKS + 1) + k, 1), cs]
        m1 = m1 * rs1
        m2 = m2 * rs1
        for r in range(0, D, 32):
            rs = slice(r, r + 32)
            back = part(c)[rs, :] * rs1 - m1 - unit(k)[rs, cs].astype(F32) * m2
            if first:
                br[0, rs, cs] = back.astype(BF)
            else:
                value = ds[rs, cs] + back
                ds[rs, cs] = value
                br[(k + 1) % 2, rs, cs] = value.astype(BF)

    if before_product is not None:
        before_product()
    gains(BLOCKS)
    product(BLOCKS, 0)

    @pl.loop(0, BLOCKS)
    def _(i):
        k = BLOCKS - i
        if during is not None:
            during(i)
        gains(k - 1)
        for group in range(len(groups)):
            if group + 1 < len(groups):
                product(k, group + 1)
            for c in range(per):
                stage(k, group * per + c, False)
            if group == 0:
                full = nt(mixed(k)[...], br[k % 2])
                row = pl.multiple_of(CAT + (k - 1) * D, 32)
                gw[t, pl.ds(row, D), :] = full[0:D].astype(BF)
                gv[t, 2, pl.ds(k, 1), :] = full[D : D + 1]
                row_sums(k + 1)
                product(k - 1, 0)

    for c, cs in enumerate(blocks):
        part(c)[...] = ds[:, cs]
        stage(0, c, True)
    row_sums(1)
    row_sums(0)
    full = nt(xt[t], br[0])
    gw[t, 0:CAT, :] = full[0:CAT].astype(BF)
    gv[t, 2, 0:1, :] = full[CAT : CAT + 1]
    if after_weights is not None:
        after_weights()
    for cs in blocks:
        back = nn(w[t, 0:D], br[0, :, cs])
        ex[:, cs] = back
        ig[cs, :] = back.T


def compute_kernel(x_ref, ints, rw, w, wh, vec, st, ig, gw, gh, gv, eye, wct, wt, wht, vt, gsb, xt, mix, xh, gp, rstd, stream, ex, br, dm, acc, lg, dl):
    width = x_ref.shape[0]
    eye[...] = identity(D)
    for c in range(0, width, CB):
        cs = slice(c, c + CB)
        xt[0, 0:D, cs] = nt(eye[...], x_ref[cs, :]).astype(BF)
    fwd = (eye, w, wh, vec, wct, wt, vt, gsb, xt, mix, xh, gp, rstd, stream, ints, width)
    @pl.loop(0, 2)
    def _(t):
        forward_tower(t, fwd)

        @pl.loop(0, width // CB)
        def _(c):
            cs = pl.ds(pl.multiple_of(c * CB, CB), CB)
            st[t, cs, :] = nt(eye[...], xt[t + 1, 0:D, cs]).astype(BF)

    ex[...] = jnp.zeros_like(ex)

    @pl.loop(0, 2)
    def _(i):
        t = 1 - i
        backward_tower(
            t,
            (eye, w, wh, vec, wht, vt, gsb, xt, mix, xh, gp, rstd, stream, ex, br, dm, acc, lg, dl, ints, rw, gw, gh, gv, ig.at[t], width),
        )


def work_scratch(width):
    return [
        pltpu.VMEM((D, D), BF),
        pltpu.VMEM((D, CODES), BF),
        pltpu.VMEM((2, D, D), BF),
        pltpu.VMEM((HPAD, D), BF),
        pltpu.VMEM((D, 128), BF),
        pltpu.VMEM((2, D, 384), F32),
        pltpu.VMEM((3, CAT + 16, width), BF),
        pltpu.VMEM((2 * BLOCKS * (D + 16), width), BF),
        pltpu.VMEM((2 * (BLOCKS + 1) * D, width), BF),
        pltpu.VMEM((2, BLOCKS + 1, D, width), BF),
        pltpu.VMEM((24, width), F32),
        pltpu.VMEM((D, width), F32),
        pltpu.VMEM((D, width), F32),
        pltpu.VMEM((2, D, width), BF),
        pltpu.VMEM((width // CB * D, CB), F32),
        pltpu.VMEM((2, 2, D, 128), F32),
        pltpu.VMEM((HPAD, CB), F32),
        pltpu.VMEM((HPAD, width), BF),
    ]


def compute(x, ints, rw, w, wh, vec):
    width = x.shape[0]
    vm = pl.BlockSpec(memory_space=pltpu.VMEM)
    return pl.pallas_call(
        compute_kernel,
        out_shape=(
            jax.ShapeDtypeStruct((2, width, D), BF),
            jax.ShapeDtypeStruct((2, width, D), F32),
            jax.ShapeDtypeStruct((2, A_ROWS, D), BF),
            jax.ShapeDtypeStruct((2, D, HPAD), BF),
            jax.ShapeDtypeStruct((2, 3, 16, D), F32),
        ),
        in_specs=[vm] * 6,
        out_specs=(vm,) * 5,
        scratch_shapes=work_scratch(width),
        compiler_params=pltpu.CompilerParams(vmem_limit_bytes=62 * 1024 * 1024),
    )(x, ints, rw, w, wh, vec)


class Plan:
    def __init__(self, n, length):
        self.n, self.length = n, length
        self.rows128 = -(-length // 128)
        block_end, head_end = A_ROWS * D, A_ROWS * D + D * HEADS
        self.a_base, self.a_rows, self.h_first, self.h_rows, self.h_off, self.v_first, self.v_rows, self.v_off = ([] for _ in range(8))
        used = 0
        for i in range(n):
            lo, hi = i * length, (i + 1) * length
            base = min(lo, block_end) // D // 16 * 16
            top = -(-min(hi, block_end) // D)
            a_rows = -(-(top - base) // 16) * 16 if lo < block_end else 0
            first = min(max(lo - block_end, 0), D * HEADS) // HEADS
            last = -(-min(max(hi - block_end, 0), D * HEADS) // HEADS)
            h_rows = last - first if hi > block_end and lo < head_end else 0
            v_first = max(lo - head_end, 0) // D
            v_rows = -(-(hi - head_end) // D) - v_first if hi > head_end else 0
            self.a_base.append(base)
            self.a_rows.append(a_rows)
            self.h_first.append(first)
            self.h_rows.append(h_rows)
            self.h_off.append(a_rows)
            self.v_first.append(v_first)
            self.v_rows.append(v_rows)
            self.v_off.append(a_rows + 5 * h_rows)
            used = max(used, a_rows + 5 * h_rows + v_rows)
        self.heads = max(self.h_rows)
        self.image = (HEADS * self.heads // 128 + 24) // 8 * 8
        self.slot = -(-(used + 1) // 32) * 32

    def at(self, table, me):
        value = jnp.int32(table[0])
        for i in range(1, self.n):
            if table[i] != table[i - 1]:
                value = value + (me >= i).astype(jnp.int32) * (table[i] - table[i - 1])
        return value


MESH = pl.DeviceIdType.MESH


def neighbours(n):
    core = lax.axis_index("tower")
    me = lax.axis_index("dp")
    near_x = me + 1 - 2 * (me % 2)
    near_y = me + 2 - 4 * ((me // 2) % 2)
    return core, me, near_x, near_y


def at(core, index):
    return {"tower": core, "dp": index}


def greet(core, me, near_x, near_y, n, crossed=False):
    barrier = pltpu.get_barrier_semaphore()
    pl.semaphore_signal(barrier, inc=1, device_id=at(1 - core, me), device_id_type=MESH)
    for near in (near_x, near_y, near_x + near_y - me):
        pl.semaphore_signal(barrier, inc=1, device_id=at(core, near), device_id_type=MESH)
    for k in range(1, n // 4):
        pl.semaphore_signal(barrier, inc=1, device_id=at(core, (me + 4 * k) % n), device_id_type=MESH)
    for near in [near_x, near_y] + [(me + 4 * k) % n for k in range(1, n // 4)] if crossed else []:
        pl.semaphore_signal(barrier, inc=1, device_id=at(1 - core, near), device_id_type=MESH)
    return barrier


def place_shard(plan, me, p_ref, slot128, shifted, rolled):
    rows = plan.rows128
    start = me * plan.length
    shift = start % 128
    first = start // 128
    tall = shifted.shape[0]
    height = p_ref.shape[0]
    lane = lax.broadcasted_iota(jnp.int32, (height, 128), 1)
    rolled[0:8] = jnp.zeros((8, 128), F32)
    rolled[8 : 8 + height] = pltpu.roll(p_ref[...], shift, 1)
    shifted[...] = jnp.zeros((tall, 128), F32)
    moved = jnp.where(lane >= shift, rolled[8 : 8 + height], rolled[7 : 7 + height])
    shifted[16 : 16 + height] = moved
    slot128[...] = jnp.zeros(slot128.shape, F32)
    row = lax.broadcasted_iota(jnp.int32, (height, 128), 0)
    base = plan.at(plan.a_base, me)

    @pl.when(plan.at(plan.a_rows, me) > 0)
    def _():
        slot128[pl.ds(first - 2 * base, height)] = jnp.where(row + first < 2 * A_ROWS, moved, 0.0)

    v_start = (A_ROWS * D + D * HEADS) // 128
    v_rows, v_off, v_first = (plan.at(t, me) for t in (plan.v_rows, plan.v_off, plan.v_first))
    tall_v = min(height, -(-2 * max(plan.v_rows) // 8) * 8)

    @pl.when(v_rows > 0)
    def _():
        inside = plan.at([max(0, v_start - i * plan.length // 128) for i in range(plan.n)], me)
        to = 2 * v_off + first + inside - v_start - 2 * v_first
        slot128[pl.ds(to, tall_v)] = shifted[pl.ds(16 + inside, tall_v)]

    h_first, h_rows, h_off = (plan.at(t, me) for t in (plan.h_first, plan.h_rows, plan.h_off))

    @pl.when(h_rows > 0)
    def _():
        tall_h = plan.image
        begin = A_ROWS * D + HEADS * h_first - 128 * first + 128 * 16
        turn = begin % 128
        rolled[0:tall_h] = pltpu.roll(shifted[pl.ds(begin // 128, tall_h)], (128 - turn) % 128, 1)
        rolled[tall_h : tall_h + 8] = jnp.zeros((8, 128), F32)
        lane = lax.broadcasted_iota(jnp.int32, (tall_h, 128), 1)
        shifted[0:tall_h] = jnp.where(lane < 128 - turn, rolled[0:tall_h], rolled[1 : tall_h + 1])
        to = slot128.at[pl.ds(pl.multiple_of(2 * h_off, 8), 10 * plan.heads)]
        it = lax.broadcasted_iota(jnp.int32, (10, 128), 0)
        lane = lax.broadcasted_iota(jnp.int32, (10, 128), 1)
        for k in range(plan.heads):
            row, turn = HEADS * k // 128, HEADS * k % 128
            window = pltpu.roll(shifted[row : row + 16], (128 - turn) % 128, 1)
            value = jnp.where(lane < 128 - turn, window[0:10], window[1:11])
            kept = (it * 128 + lane < HEADS) & (k < h_rows)
            to[10 * k : 10 * k + 10] = to[10 * k : 10 * k + 10] + jnp.where(kept, value, 0.0)


def unpack_rows(plan, i, slot, w, heads, vectors, scratch):
    base, rows = plan.a_base[i], plan.a_rows[i]
    if rows:
        shared = i > 0 and base < plan.a_base[i - 1] + plan.a_rows[i - 1]
        lo = 0
        if shared:
            w[base : base + 16] = w[base : base + 16] + slot[0:16]
            lo = 16
        if rows > lo:
            w[base + lo : base + rows] = slot[lo:rows]
    h_rows, h_off, h_first = plan.h_rows[i], plan.h_off[i], plan.h_first[i]
    v_rows, v_off, v_first = plan.v_rows[i], plan.v_off[i], plan.v_first[i]
    if h_rows or v_rows:
        value = slot.astype(F32)
        scratch[0][...] = value[:, 0:128]
        scratch[1][...] = value[:, 128:D]
    if h_rows:
        shared = i > 0 and plan.h_rows[i - 1] and plan.h_first[i - 1] + plan.h_rows[i - 1] > h_first
        for j in range(5):
            for half in range(2):
                cols = slice(128 * half, 128 * half + 128)
                first = D * j + h_first
                value = scratch[half][pl.ds(h_off + j, h_rows, stride=5)]
                if shared:
                    heads[first : first + 1, cols] = heads[first : first + 1, cols] + value[0:1]
                    if h_rows > 1:
                        heads[first + 1 : first + h_rows, cols] = value[1:h_rows]
                else:
                    heads[first : first + h_rows, cols] = value
    if v_rows:
        shared = v_first and plan.v_first[i - 1] + plan.v_rows[i - 1] > v_first
        shared = shared or (i > 0 and plan.v_rows[i - 1] > 0 and v_first == 0)
        for half in range(2):
            cols = slice(128 * half, 128 * half + 128)
            value = scratch[half][v_off : v_off + v_rows]
            if shared:
                vectors[v_first : v_first + 1, cols] = vectors[v_first : v_first + 1, cols] + value[0:1]
                if v_rows > 1:
                    vectors[v_first + 1 : v_first + v_rows, cols] = value[1:v_rows]
            else:
                vectors[v_first : v_first + v_rows, cols] = value


def split3(value):
    hi = value.astype(BF).astype(F32)
    mid = (value - hi).astype(BF).astype(F32)
    return hi, mid, value - hi - mid


def gather_kernel(plan, p_ref, ints_ref, imp_ref, w, wh, vec, both, rw, slots, slot128, shifted, rolled, scratch, whf, vecf, send, recv):
    n = plan.n
    depth = n // 4
    core, me, near_x, near_y = neighbours(n)
    barrier = greet(core, me, near_x, near_y, n)
    place_shard(plan, me, p_ref, slot128, shifted, rolled)
    pl.semaphore_wait(barrier, depth + 3)
    half = rw.shape[1]
    started = []

    def copy(src, dst, slot, to):
        c = pltpu.make_async_remote_copy(
            src_ref=src, dst_ref=dst, send_sem=send.at[slot], recv_sem=recv.at[slot], device_id=to, device_id_type=MESH
        )
        c.start()
        started.append(c)
        return c

    mine = pl.multiple_of(core * half, half)
    theirs = pl.multiple_of((1 - core) * half, half)
    number = iter(range(1 << 20))
    ints_copy = copy(ints_ref.at[:, pl.ds(theirs, half)], both.at[core], next(number), at(1 - core, me))
    rows = plan.slot
    total = jnp.sum(imp_ref[...].astype(F32), axis=1, keepdims=True)
    lane = lax.broadcasted_iota(jnp.int32, (1, D), 1)
    hi, mid, lo = split3(total)
    left = slot128[pl.ds(0, rows, stride=2)]
    right = slot128[pl.ds(1, rows, stride=2)]
    own = jnp.concatenate([left, right], 1)
    last = jnp.where(lane == 0, hi, jnp.where(lane == 1, mid, jnp.where(lane == 2, lo, 0.0)))
    last_row = lax.broadcasted_iota(jnp.int32, (rows, D), 0) == rows - 1
    slots[core, me] = jnp.where(last_row, last, own).astype(BF)

    def column(index, k):
        return (index + n - 4 * k) % n

    def send_slot(origin, to, lo=0, hi=rows):
        ref = slots.at[core, origin, pl.ds(lo, hi - lo)]
        return copy(ref, ref, next(number), to)

    near_xy = near_x + near_y - me
    cut = rows // 2
    z_in, x_in, y_in, d_in, s_in = {}, {}, {}, {}, []
    for k in sorted(range(1, depth), key=lambda k: (min(k, depth - k), k)):
        z_in[k] = send_slot(me, at(core, (me + 4 * k) % n))
    order = [0] + list(z_in)
    for k in order:
        if k:
            z_in[k].wait_recv()
        x_in[k] = send_slot(column(me, k), at(core, near_x))
        y_in[k] = send_slot(column(me, k), at(core, near_y))
        s_in.append(send_slot(column(me, k), at(1 - core, me)))
    for k in order:
        x_in[k].wait_recv()
        first = send_slot(column(near_x, k), at(core, near_y), 0, cut)
        s_in.append(send_slot(column(near_x, k), at(1 - core, me)))
        y_in[k].wait_recv()
        second = send_slot(column(near_y, k), at(core, near_x), cut, rows)
        s_in.append(send_slot(column(near_y, k), at(1 - core, me)))
        d_in[k] = (first, second)
    for k in order:
        for c in d_in[k]:
            c.wait_recv()
        s_in.append(send_slot(column(near_xy, k), at(1 - core, me)))
    ints_copy.wait_recv()
    both[core] = ints_ref[:, pl.ds(mine, half)]
    for c in s_in:
        c.wait_recv()
    for c in started:
        c.wait_send()
    for t in range(2):
        vecf[...] = jnp.zeros(vecf.shape, F32)
        for i in range(n):
            unpack_rows(plan, i, slots[t, i], w.at[t], whf, vecf, [scratch.at[0], scratch.at[1]])
        for j in range(5):
            wh[t, :, D * j : D * j + D] = whf[D * j : D * j + D].astype(BF)
        vec[t] = vecf[...].astype(BF)
    total = jnp.zeros((1, D), F32)
    for i in range(n):
        tail = slots[0, i, rows - 16 : rows].astype(F32)
        total = total + tail[15:16]
    weight_sum = jnp.sum(jnp.where(lane < 3, total, 0.0), axis=1, keepdims=True)
    rw[...] = jnp.broadcast_to(imp_ref[:, pl.ds(mine, half)].astype(F32) / weight_sum, (8, half))


def gather(plan, p128, ints, imp):
    n, rows = plan.n, plan.slot
    half = ints.shape[1] // 2
    vm = pl.BlockSpec(memory_space=pltpu.VMEM)
    height = p128.shape[0]
    tall = max(2 * rows, height + 40) + 80
    copies = 1 + (n // 4 - 1) + 2 * (n // 4) + 2 * (n // 4) + n
    return pl.pallas_call(
        functools.partial(gather_kernel, plan),
        out_shape=(
            jax.ShapeDtypeStruct((2, A_ROWS, D), BF),
            jax.ShapeDtypeStruct((2, D, HPAD), BF),
            jax.ShapeDtypeStruct((2, 128, D), BF),
            jax.ShapeDtypeStruct((2, 8, half), jnp.int32),
            jax.ShapeDtypeStruct((8, half), F32),
        ),
        in_specs=[vm] * 3,
        out_specs=(vm,) * 5,
        scratch_shapes=[
            pltpu.VMEM((2, n, rows, D), BF),
            pltpu.VMEM((tall, 128), F32),
            pltpu.VMEM((height + 128, 128), F32),
            pltpu.VMEM((height + 40, 128), F32),
            pltpu.VMEM((2, rows, 128), F32),
            pltpu.VMEM((HPAD, D), F32),
            pltpu.VMEM((128, D), F32),
            pltpu.SemaphoreType.DMA((copies,)),
            pltpu.SemaphoreType.DMA((copies,)),
        ],
        compiler_params=pltpu.CompilerParams(
            collective_id=0, has_side_effects=True, vmem_limit_bytes=48 * 1024 * 1024
        ),
    )(p128, ints, imp)


def chunks(height):
    step = max(c for c in range(8, 113, 8) if height % c == 0)
    return [(lo, lo + step) for lo in range(0, height, step)]


def lay_flat(plan, me, slot128, flat, rolled):
    height = rolled.shape[0] - 40
    start = me * plan.length
    shift = start % 128
    first = start // 128
    base = plan.at(plan.a_base, me)
    row = lax.broadcasted_iota(jnp.int32, (height + 8, 128), 0)
    flat[...] = jnp.zeros(flat.shape, F32)

    @pl.when(plan.at(plan.a_rows, me) > 0)
    def _():
        rows = slot128[pl.ds(first - 2 * base, height + 8)]
        flat[16 : 24 + height] = jnp.where(row + first < 2 * A_ROWS, rows, 0.0)

    v_start = (A_ROWS * D + D * HEADS) // 128
    v_rows, v_off, v_first = (plan.at(t, me) for t in (plan.v_rows, plan.v_off, plan.v_first))
    tall_v = min(height, -(-2 * max(plan.v_rows) // 8) * 8)

    @pl.when(v_rows > 0)
    def _():
        inside = plan.at([max(0, v_start - i * plan.length // 128) for i in range(plan.n)], me)
        source = 2 * v_off + first + inside - v_start - 2 * v_first
        to = pl.ds(16 + inside, tall_v)
        flat[to] = flat[to] + slot128[pl.ds(source, tall_v)]

    h_first, h_rows, h_off = (plan.at(t, me) for t in (plan.h_first, plan.h_rows, plan.h_off))

    @pl.when(h_rows > 0)
    def _():
        tall_h = plan.image
        source = slot128.at[pl.ds(pl.multiple_of(2 * h_off, 8), 10 * plan.heads + 6)]
        it = lax.broadcasted_iota(jnp.int32, (16, 128), 0)
        lane = lax.broadcasted_iota(jnp.int32, (16, 128), 1)
        rolled[0 : tall_h + 8] = jnp.zeros((tall_h + 8, 128), F32)
        for k in range(plan.heads):
            row, turn = HEADS * k // 128, HEADS * k % 128
            kept = (it * 128 + lane < HEADS) & (k < h_rows)
            value = pltpu.roll(jnp.where(kept, source[10 * k : 10 * k + 16], 0.0), turn, 1)
            above = jnp.concatenate([jnp.zeros((8, 128), F32), value], 0)[7:23]
            rolled[row : row + 16] = rolled[row : row + 16] + jnp.where(lane >= turn, value, above)
        begin = A_ROWS * D + HEADS * h_first - 128 * first + 128 * 16
        turn = begin % 128
        slot128[0:8] = jnp.zeros((8, 128), F32)
        slot128[8 : 8 + tall_h] = pltpu.roll(rolled[0:tall_h], turn, 1)
        lane = lax.broadcasted_iota(jnp.int32, (tall_h, 128), 1)
        moved = jnp.where(lane >= turn, slot128[8 : 8 + tall_h], slot128[7 : 7 + tall_h])
        to = pl.ds(begin // 128, tall_h)
        flat[to] = flat[to] + moved

    rolled[0 : height + 8] = pltpu.roll(flat[16 : 24 + height], (128 - shift) % 128, 1)
    for lo, hi in chunks(height):
        lane = lax.broadcasted_iota(jnp.int32, (hi - lo, 128), 1)
        flat[lo:hi] = jnp.where(lane < 128 - shift, rolled[lo:hi], rolled[lo + 1 : hi + 1])


def pack_slots(plan, core, gw, gh, gv, rgw, rgh, rgv, slots, sums, vsum, scratch):
    total = gv[core].astype(F32) + rgv[...]
    for kind in range(3):
        vsum[kind * (BLOCKS + 1) : (kind + 1) * (BLOCKS + 1)] = total[kind, 0 : BLOCKS + 1]
    sums[...] = gh[core].astype(F32) + rgh[...].astype(F32)
    for i in range(plan.n):
        base, rows = plan.a_base[i], plan.a_rows[i]
        h_rows, h_off, h_first = plan.h_rows[i], plan.h_off[i], plan.h_first[i]
        v_rows, v_off, v_first = plan.v_rows[i], plan.v_off[i], plan.v_first[i]
        slots[i, rows : plan.slot] = jnp.zeros((plan.slot - rows, D), BF)
        if rows:
            added = gw[core, base : base + rows].astype(F32) + rgw[base : base + rows].astype(F32)
            slots[i, 0:rows] = added.astype(BF)
        if h_rows or v_rows:
            scratch[...] = jnp.zeros(scratch.shape, F32)
            for half in range(2):
                for j in range(5 if h_rows else 0):
                    cols = slice(D * j + 128 * half, D * j + 128 * half + 128)
                    scratch[half, pl.ds(h_off + j, h_rows, stride=5)] = sums[h_first : h_first + h_rows, cols]
                if v_rows:
                    scratch[half, v_off : v_off + v_rows] = vsum[v_first : v_first + v_rows, 128 * half : 128 * half + 128]
            whole = jnp.concatenate([scratch[0], scratch[1]], 1)
            slots[i, rows : plan.slot] = whole[rows:].astype(BF)


def segment_bounds():
    first = [0] + [(CAT + j * D) * D for j in range(BLOCKS + 1)]
    return list(zip(first, first[1:] + [A_ROWS * D + D * HEADS]))


class Rows:
    def __init__(self, ref):
        self.ref, self.height = ref, ref.shape[0]

    def chunks(self):
        return chunks(self.height)

    def get(self, lo, hi):
        return self.ref[lo:hi]

    def put(self, lo, hi, value):
        self.ref[lo:hi] = value


class Flat:
    def __init__(self, ref, buffer):
        self.ref, self.buffer, self.length = ref, buffer, ref.shape[1]
        self.whole = self.length // 1024 * 8
        self.height = -(-self.length // 1024) * 8

    def chunks(self):
        step = next(s for s in range(64, 0, -8) if self.whole % s == 0)
        return [(lo, lo + step) for lo in range(0, self.whole, step)] + [(self.whole, self.height)]

    def ends(self):
        rows = (self.length - 128 * self.whole) // 128
        return rows, self.length % 128, 128 * self.whole, 128 * (self.whole + rows)

    def get(self, lo, hi):
        if hi <= self.whole:
            return self.ref[0:1, 128 * lo : 128 * hi].reshape(hi - lo, 128)
        rows, lanes, first, last = self.ends()
        self.buffer[...] = jnp.zeros((8, 128), F32)
        if rows:
            self.buffer[0:rows] = self.ref[0:1, first:last].reshape(rows, 128)
        if lanes:
            self.buffer[rows : rows + 1, 0:lanes] = self.ref[0:1, last : self.length]
        return self.buffer[...]

    def put(self, lo, hi, value):
        if hi <= self.whole:
            self.ref[0:1, 128 * lo : 128 * hi] = value.reshape(1, 128 * (hi - lo))
            return
        rows, lanes, first, last = self.ends()
        if rows:
            self.ref[0:1, first:last] = value[0:rows].reshape(1, 128 * rows)
        if lanes:
            self.ref[0:1, last : self.length] = value[rows : rows + 1, 0:lanes]


def update_shard(plan, me, p_ref, m_ref, v_ref, outs, flat, squares, sq_in, push, to_plane, to_z):
    first_out, second_out, new_out, norm_out = outs
    height = p_ref.height
    start = me * plan.length
    correction = 1.0 - 0.5**STEP
    bounds = segment_bounds()

    def place(lo, hi):
        shape = (hi - lo, 128)
        return 128 * lo + 128 * lax.broadcasted_iota(jnp.int32, shape, 0) + lax.broadcasted_iota(jnp.int32, shape, 1)

    for lo, hi in p_ref.chunks():
        spot = place(lo, hi)
        grad = jnp.where(spot < plan.length, flat[lo:hi], 0.0)
        first_new = 0.5 * m_ref.get(lo, hi) + 0.5 * grad
        second_new = 0.5 * v_ref.get(lo, hi) + 0.5 * grad * grad
        first_out.put(lo, hi, first_new)
        second_out.put(lo, hi, second_new)
        decay = jnp.where(spot < bounds[-1][1] - start, 0.01 * p_ref.get(lo, hi), 0.0)
        update = first_new / correction / (jnp.sqrt(second_new / correction) + 1e-06) + decay
        flat[lo:hi] = jnp.where(spot < plan.length, update, 0.0)
        new_out.put(lo, hi, p_ref.get(lo, hi) - 0.5 * update)
    squares[...] = jnp.zeros(squares.shape, F32)

    def each_segment(body):
        for j, (first, last) in enumerate(bounds):
            pl.when((first < start + plan.length) & (last > start))(lambda j=j, first=first, last=last: body(j, first, last))

    def square_sums(j, first, last):
        weight, change = jnp.zeros((8, 128), F32), jnp.zeros((8, 128), F32)
        for lo, hi in p_ref.chunks():
            spot = place(lo, hi)
            inside = (spot >= first - start) & (spot < last - start)
            p, u = jnp.where(inside, p_ref.get(lo, hi), 0.0), jnp.where(inside, flat[lo:hi], 0.0)
            weight = weight + jnp.sum((p * p).reshape(-1, 8, 128), axis=0)
            change = change + jnp.sum((u * u).reshape(-1, 8, 128), axis=0)
        squares[0, j : j + 1] = jnp.sum(weight, axis=0, keepdims=True)
        squares[0, 16 + j : 17 + j] = jnp.sum(change, axis=0, keepdims=True)

    each_segment(square_sums)
    total = squares[0]
    for hop, targets in enumerate((to_plane, to_z)):
        lands = range(3) if hop == 0 else range(3, 3 + len(to_z))
        for c in [push(squares.at[hop], sq_in.at[k], to) for k, to in zip(lands, targets)]:
            c.wait_recv()
        for k in lands:
            total = total + sq_in[k]
        squares[hop + 1] = total
    norm = jnp.sqrt(jnp.sum(total, axis=1, keepdims=True))
    squares[3] = jnp.broadcast_to(norm, (32, 128))
    line = jnp.sqrt(jnp.sum(jnp.concatenate([total, jnp.zeros((96, 128), F32)], 0).T, axis=0, keepdims=True))
    norm_out[0:1] = line[:, 0:MATS]
    norm_out[1:2] = pltpu.roll(line, 112, 1)[:, 0:MATS]

    def scaled(j, first, last):
        ratio = squares[3, j : j + 1] / squares[3, 16 + j : 17 + j]
        for lo, hi in p_ref.chunks():
            spot = place(lo, hi)
            inside = (spot >= first - start) & (spot < last - start)
            new_out.put(lo, hi, jnp.where(inside, p_ref.get(lo, hi) - 0.5 * ratio * flat[lo:hi], new_out.get(lo, hi)))

    each_segment(scaled)


def reduce_kernel(
    plan, gw, gh, gv, st, ig, p_ref, m_ref, v_ref,
    st_out, ig_out, first_out, second_out, new_out, norm_out,
    rgw, rgh, rgv, slots, sums, vsum, scratch, in_d, in_x, in_y, in_z, slot128, flat, rolled, squares, sq_in,
    send, recv, local,
):
    n, rows = plan.n, plan.slot
    depth, cut = n // 4, plan.slot // 2
    core, me, near_x, near_y = neighbours(n)
    near_xy = near_x + near_y - me
    barrier = greet(core, me, near_x, near_y, n)
    pl.semaphore_wait(barrier, depth + 3)
    half = st.shape[1]
    number = iter(range(1 << 20))
    started = []

    def copy(src, dst, to):
        slot = next(number)
        c = pltpu.make_async_remote_copy(
            src_ref=src, dst_ref=dst, send_sem=send.at[slot], recv_sem=recv.at[slot], device_id=to, device_id_type=MESH
        )
        c.start()
        started.append(c)
        return c

    def column(index, k):
        return (index + n - 4 * k) % n

    sibling = at(1 - core, me)
    early = [
        copy(gw.at[1 - core], rgw, sibling),
        copy(gh.at[1 - core], rgh, sibling),
        copy(gv.at[1 - core], rgv, sibling),
    ]
    mine = pl.ds(pl.multiple_of(core * half, half), half)
    late = [
        copy(st.at[1 - core], st_out.at[mine], sibling),
        copy(ig.at[1 - core], ig_out.at[mine], sibling),
    ]
    stay = [
        pltpu.make_async_copy(st.at[core], st_out.at[mine], local.at[0]),
        pltpu.make_async_copy(ig.at[core], ig_out.at[mine], local.at[1]),
    ]
    for c in stay:
        c.start()
    for c in early:
        c.wait_recv()
    pack_slots(plan, core, gw, gh, gv, rgw, rgh, rgv, slots, sums, vsum, scratch)
    order = list(range(1, depth)) + [0]
    to_x, to_y = at(core, near_x), at(core, near_y)
    halves = {}
    for k in order:
        diagonal = column(near_xy, k)
        halves[k] = (
            copy(slots.at[diagonal, pl.ds(0, cut)], in_d.at[k, pl.ds(0, cut)], to_y),
            copy(slots.at[diagonal, pl.ds(cut, rows - cut)], in_d.at[k, pl.ds(cut, rows - cut)], to_x),
        )
    fulls = {}
    for k in order:
        ox, oy = column(near_x, k), column(near_y, k)
        halves[k][0].wait_recv()
        slots[ox, 0:cut] = (slots[ox, 0:cut].astype(F32) + in_d[k, 0:cut].astype(F32)).astype(BF)
        first = copy(slots.at[ox], in_x.at[k], to_x)
        halves[k][1].wait_recv()
        slots[oy, cut:rows] = (slots[oy, cut:rows].astype(F32) + in_d[k, cut:rows].astype(F32)).astype(BF)
        fulls[k] = (first, copy(slots.at[oy], in_y.at[k], to_y))
    along = {}
    for k in order:
        own = column(me, k)
        for c in fulls[k]:
            c.wait_recv()
        if k:
            total = slots[own].astype(F32) + in_x[k].astype(F32) + in_y[k].astype(F32)
            slots[own] = total.astype(BF)
            along[k] = copy(slots.at[own], in_z.at[k], at(core, own))
    for c in along.values():
        c.wait_recv()
    total = slots[me].astype(F32) + in_x[0].astype(F32) + in_y[0].astype(F32)
    for k in along:
        total = total + in_z[k].astype(F32)
    slot128[...] = jnp.zeros(slot128.shape, F32)
    slot128[pl.ds(0, rows, stride=2)] = total[:, 0:128]
    slot128[pl.ds(1, rows, stride=2)] = total[:, 128:D]
    lay_flat(plan, me, slot128, flat, rolled)

    to_z = [at(core, column(me, k)) for k in range(1, depth)]
    outs = (Rows(first_out), Rows(second_out), Rows(new_out), norm_out)
    to_plane = [to_x, to_y, at(core, near_xy)]
    update_shard(plan, me, Rows(p_ref), Rows(m_ref), Rows(v_ref), outs, flat, squares, sq_in, copy, to_plane, to_z)
    for c in late:
        c.wait_recv()
    for c in stay:
        c.wait()
    for c in started:
        c.wait_send()


def reduce_and_update(plan, gw, gh, gv, st, ig, p128, m128, v128):
    n, rows = plan.n, plan.slot
    depth = n // 4
    half = st.shape[1]
    height = p128.shape[0]
    vm = pl.BlockSpec(memory_space=pltpu.VMEM)
    hbm = pl.BlockSpec(memory_space=pl.ANY)
    copies = 5 + 2 * depth + 2 * depth + (depth - 1) + (depth - 1) + 3
    flat32 = jax.ShapeDtypeStruct((height, 128), F32)
    return pl.pallas_call(
        functools.partial(reduce_kernel, plan),
        out_shape=(
            jax.ShapeDtypeStruct((2 * half, D), BF),
            jax.ShapeDtypeStruct((2 * half, D), F32),
            flat32,
            flat32,
            flat32,
            jax.ShapeDtypeStruct((2, MATS), F32),
        ),
        in_specs=[vm] * 3 + [hbm] * 2 + [vm] * 3,
        out_specs=(hbm, hbm, vm, vm, vm, vm),
        scratch_shapes=[
            pltpu.VMEM((A_ROWS, D), BF),
            pltpu.VMEM((D, HPAD), BF),
            pltpu.VMEM(gv.shape[1:], F32),
            pltpu.VMEM((n, rows, D), BF),
            pltpu.VMEM((D, HPAD), F32),
            pltpu.VMEM((40, D), F32),
            pltpu.VMEM((2, rows, 128), F32),
            pltpu.VMEM((depth, rows, D), BF),
            pltpu.VMEM((depth, rows, D), BF),
            pltpu.VMEM((depth, rows, D), BF),
            pltpu.VMEM((depth, rows, D), BF),
            pltpu.VMEM((max(2 * rows, height + 48) + 80, 128), F32),
            pltpu.VMEM((height + 128, 128), F32),
            pltpu.VMEM((height + 40, 128), F32),
            pltpu.VMEM((4, 32, 128), F32),
            pltpu.VMEM((2 + depth, 32, 128), F32),
            pltpu.SemaphoreType.DMA((copies,)),
            pltpu.SemaphoreType.DMA((copies,)),
            pltpu.SemaphoreType.DMA((2,)),
        ],
        compiler_params=pltpu.CompilerParams(
            collective_id=1, has_side_effects=True, vmem_limit_bytes=48 * 1024 * 1024
        ),
    )(gw, gh, gv, st, ig, p128, m128, v128)


class Copies:
    def __init__(self, send, recv):
        self.send, self.recv, self.made, self.sent = send, recv, [], set()

    def add(self, src, dst, to, recv_slot=None, only=None):
        self.made.append((src, dst, to, recv_slot, only))
        return len(self.made) - 1

    def get(self, number):
        src, dst, to, recv_slot, _ = self.made[number]
        return pltpu.make_async_remote_copy(
            src_ref=src(), dst_ref=dst(), send_sem=self.send.at[number],
            recv_sem=self.recv.at[number] if recv_slot is None else recv_slot(),
            device_id=to(), device_id_type=MESH,
        )

    def start(self, *numbers):
        for number in numbers:
            self.get(number).start()

    def arrive(self, *numbers):
        for number in numbers:
            self.get(number).wait_recv()

    def leave(self, *numbers):
        for number in numbers:
            only = self.made[number][4]
            if number not in self.sent and only is None:
                self.get(number).wait_send()
            elif number not in self.sent:
                pl.when(only())(lambda number=number: self.get(number).wait_send())
            self.sent.add(number)


def fused_fits(plan):
    depth, half = plan.n // 4, plan.slot // 2
    plain = [b + plan.slot <= A_ROWS for b, h, v in zip(plan.a_base, plan.h_rows, plan.v_rows) if not (h or v)]
    vectors = [rows for rows in plan.v_rows if rows]
    return (
        all(plain)
        and vectors == [3 * (BLOCKS + 1)]
        and plan.n % 4 == 0
        and half >= 32
        and 4 * half <= HPAD
        and 2 * depth * plan.slot <= (BLOCKS + 1) * D
        and depth == 4
        and max(plan.a_rows) <= plan.slot
    )


def train_kernel(
    plan, x_ref, codes_ref, targets_ref, visits_ref, imp_ref, p_ref, m_ref, v_ref,
    st_out, ig_out, first_out, second_out, new_out, norm_out,
    w, wh, vec, both, away, rw, eye, wct, wt, wht, vt, gsb, xt, mix, xh, gp, rstd, stream, ex, br, dm, acc, lg, dl,
    gw, gh, gv, packed, st_stage, slot128, flat, rolled, vsum, vacc, vin, owned, squares, sq_in, tail,
    send, recv, z_recv, own_recv, local, ready,
):
    n, rows = plan.n, plan.slot
    depth, hrows = n // 4, plan.slot // 2
    cut = hrows // 32 * 16
    core, me, near_x, near_y = neighbours(n)
    near_xy = near_x + near_y - me
    width = both.shape[2]
    params_in, first_new, second_new, new = (Flat(ref, tail) for ref in (p_ref, first_out, second_out, new_out))
    moments = [
        pltpu.make_async_copy(src, dst, local.at[3 + i])
        for i, (src, dst) in enumerate(((m_ref, first_out), (v_ref, second_out)))
    ]
    z_me, j_me = me // 4, me % 4
    copies = Copies(send, recv)
    scratch = [slot128.at[0:rows], slot128.at[rows : 2 * rows]]
    barrier = greet(core, me, near_x, near_y, n, True)
    mine = pl.multiple_of(core * width, width)
    theirs = pl.multiple_of((1 - core) * width, width)
    x_copy = pltpu.make_async_copy(x_ref.at[pl.ds(mine, width)], st_stage.at[0], local.at[0])
    x_copy.start()
    for c in moments:
        c.start()
    for to, half in ((both.at[core], mine), (away, theirs)):
        cols = pl.ds(half, width)
        to[0:1] = codes_ref[:, cols]
        to[1:2] = targets_ref[0, :, cols]
        to[2:6] = visits_ref[:, cols]
        to[6:7] = targets_ref[1, :, cols]
        to[7:8] = targets_ref[2, :, cols]
    height = params_in.height
    for lo, hi in params_in.chunks():
        slot128[lo:hi] = params_in.get(lo, hi)
    place_shard(plan, me, slot128.at[0:height], slot128, flat, rolled)

    spare = (BLOCKS + 1) * D

    def slot_part(t, i, lo, count):
        row = pl.multiple_of(spare + rows * (t * depth + i // 4) + lo, 16)
        return xh.at[pl.ds(row, count), pl.ds(pl.multiple_of((i % 4) * D, D), D)]

    def column(index, k):
        return (index + n - 4 * k) % n

    def sibling():
        return at(1 - core, me)

    def same(make, to):
        return copies.add(make, make, to)

    low = core * hrows
    other_low = (1 - core) * hrows
    order = [0] + sorted(range(1, depth), key=lambda k: (min(k, depth - k), k))
    to_x, to_y, to_d = (lambda: at(core, near_x)), (lambda: at(core, near_y)), (lambda: at(core, near_xy))
    swap_ints = copies.add(lambda: away, lambda: both.at[core], sibling)

    def arrival(t, number):
        return own_recv.at[t * (depth + 2) + number]

    own_targets = [(lambda: near_x), (lambda: near_y)] + [lambda k=k: (me + 4 * k) % n for k in order[1:]]
    own_sends = [copies.add(lambda: slot_part(core, me, 0, rows), lambda: slot_part(core, me, 0, rows), sibling, lambda: arrival(core, 0))]
    for number, target in enumerate(own_targets, 1):
        for h in range(2):
            make = lambda h=h: slot_part(core, me, h * hrows, hrows)
            own_sends.append(
                copies.add(make, make, lambda h=h, target=target: at(h, target()), lambda number=number: arrival(core, number))
            )
    own_sends = own_sends[3 + 2 :] + own_sends[1:5] + own_sends[:1]

    def own_arrive(t, number, make):
        pltpu.make_async_remote_copy(
            src_ref=make(), dst_ref=make(), send_sem=send.at[0], recv_sem=arrival(t, number), device_id=sibling(), device_id_type=MESH
        ).wait_recv()

    gathers = []
    for t in range(2):
        g = {}
        for k in order:
            if k:
                g["x", k] = same(lambda t=t, k=k: slot_part(t, column(me, k), low, hrows), to_x)
                g["y", k] = same(lambda t=t, k=k: slot_part(t, column(me, k), low, hrows), to_y)
            g["d", k] = (
                same(lambda t=t, k=k: slot_part(t, column(near_x, k), low, cut), to_y),
                same(lambda t=t, k=k: slot_part(t, column(near_y, k), low + cut, hrows - cut), to_x),
            )
            g["s", k] = [
                same(lambda t=t, k=k, index=index: slot_part(t, column(index, k), low, hrows), sibling) if index is not me or k else None
                for index in (me, near_x, near_y, near_xy)
            ]
        gathers.append(g)

    def gather_0(t):
        pl.when(core == t)(lambda: copies.start(*own_sends))

    def gather_1(t):
        g = gathers[t]
        for number, k in enumerate(order[1:], 3):
            own_arrive(t, number, lambda: slot_part(t, me, low, hrows))
            copies.start(g["x", k], g["y", k], g["s", k][0])

    def gather_2(t):
        g = gathers[t]
        for k in order:
            if k:
                copies.arrive(g["x", k])
            else:
                own_arrive(t, 1, lambda: slot_part(t, me, low, hrows))
            copies.start(g["d", k][0], g["s", k][1])
            if k:
                copies.arrive(g["y", k])
            else:
                own_arrive(t, 2, lambda: slot_part(t, me, low, hrows))
            copies.start(g["d", k][1], g["s", k][2])

    def gather_3(t):
        g = gathers[t]
        for k in order:
            copies.arrive(*g["d", k])
            copies.start(g["s", k][3])

    def gather_4(t):
        g = gathers[t]
        pl.when(core != t)(lambda: own_arrive(t, 0, lambda: slot_part(t, me, 0, rows)))
        for k in order:
            copies.arrive(*(c for c in g["s", k] if c is not None))

    def unpack(t):
        lg[4 * D : 5 * D, 128:D] = jnp.zeros((D, 128), F32)
        vsum[...] = jnp.zeros(vsum.shape, F32)
        for i in range(n):
            row, lane = spare + rows * (t * depth + i // 4), (i % 4) * D
            unpack_rows(plan, i, xh[row : row + rows, lane : lane + D], w.at[t], lg, vsum, scratch)
        for j in range(5):
            wh[t, :, D * j : D * j + D] = lg[D * j : D * j + D].astype(BF)
        vec[t] = vsum[...].astype(BF)

    total = jnp.sum(imp_ref[...].astype(F32), axis=1, keepdims=True)
    lane_d = lax.broadcasted_iota(jnp.int32, (1, D), 1)
    hi, mid, lo = split3(total)
    left = slot128[pl.ds(0, rows, stride=2)]
    right = slot128[pl.ds(1, rows, stride=2)]
    own = jnp.concatenate([left, right], 1)
    last = jnp.where(lane_d == 0, hi, jnp.where(lane_d == 1, mid, jnp.where(lane_d == 2, lo, 0.0)))
    last_row = lax.broadcasted_iota(jnp.int32, (rows, D), 0) == rows - 1
    slot_part(core, me, 0, rows)[...] = jnp.where(last_row, last, own).astype(BF)
    pl.semaphore_wait(barrier, depth + 3 + 2 + depth - 1)
    gather_0(0)
    copies.start(swap_ints)
    eye[...] = identity(D)
    x_copy.wait()
    for c in range(0, width, CB):
        xt[0, 0:D, c : c + CB] = nt(eye[...], st_stage[0, c : c + CB, :]).astype(BF)
    gather_1(0)
    gather_0(1)
    gather_2(0)
    gather_3(0)
    copies.arrive(swap_ints)
    gather_4(0)
    unpack(0)
    total = jnp.zeros((1, D), F32)
    for i in range(n):
        row, lane = spare + rows * (i // 4), (i % 4) * D
        total = total + xh[row + rows - 16 : row + rows, lane : lane + D].astype(F32)[15:16]
    weight_sum = jnp.sum(jnp.where(lane_d < 3, total, 0.0), axis=1, keepdims=True)
    rw[...] = jnp.broadcast_to(imp_ref[:, pl.ds(mine, width)].astype(F32) / weight_sum, (8, width))

    fwd = (eye, w, wh, vec, wct, wt, vt, gsb, xt, mix, xh, gp, rstd, stream, both, width)

    def during_forward(k):
        pl.when(k == 1)(lambda: gather_1(1))
        pl.when(k == 4)(lambda: gather_2(1))
        pl.when(k == 7)(lambda: gather_3(1))

    def emit_states(t):
        for c in range(0, width, CB):
            st_stage[t, c : c + CB, :] = nt(eye[...], xt[t + 1, 0:D, c : c + CB]).astype(BF)

    forward_tower(0, fwd, during_forward)
    gather_4(1)
    copies.leave(*range(len(copies.made)))
    unpack(1)
    forward_tower(1, fwd, None)
    emit_states(0)
    emit_states(1)
    out_rows = pl.ds(mine, width)
    st_copy = copies.add(lambda: st_stage.at[1 - core], lambda: st_out.at[out_rows], sibling)
    copies.start(st_copy)
    st_stay = pltpu.make_async_copy(st_stage.at[core], st_out.at[out_rows], local.at[1])
    st_stay.start()

    packed_of = [i for i in range(n) if plan.h_rows[i] or plan.v_rows[i]]
    owner = plan.v_rows.index(3 * (BLOCKS + 1))

    early = (2, 3)

    def piece(t, zz, b, lo, count):
        if t == 1 and zz in early:
            arena, first, q = dl, 0, 7 * early.index(zz) + b
        elif t == 1:
            arena, first, q = mix, BLOCKS * (D + 16), 7 * zz + b
        else:
            arena, first, q = xh, spare, 7 * zz + b
        row = pl.multiple_of(first + hrows * (q // 4) + lo, 16)
        return arena.at[pl.ds(row, count), pl.ds(pl.multiple_of((q % 4) * D, D), D)]

    def block(t, zz, b):
        return piece(t, zz, b, 0, hrows)

    def z_in(h, k):
        return st_stage.at[0, pl.ds(pl.multiple_of(hrows * (h * (depth - 1) + k - 1), 16), hrows)]

    def z_out(t, zz):
        if t == 1 and zz in early:
            return st_stage.at[1, pl.ds(hrows * early.index(zz), hrows)]
        return block(t, zz, j_me)

    def slot_half(t, i, lo):
        if i in packed_of:
            return packed.at[packed_of.index(i), pl.ds(pl.multiple_of(lo, 16), hrows)]
        return gw.at[t, pl.ds(pl.multiple_of(plan.a_base[i] + lo, 16), hrows)]

    j_x, j_y, j_d = near_x % 4, near_y % 4, near_xy % 4
    direct = ((0, 0),)
    jobs = {}
    for t in range(2):
        for zz in range(depth):
            job = {}
            job["swap"] = [
                copies.add(lambda t=t, i=4 * zz + j: slot_half(t, i, other_low), lambda t=t, zz=zz, j=j: block(t, zz, j), sibling)
                for j in range(4)
            ]
            if (t, zz) in direct:
                job["d"] = [copies.add(lambda t=t, zz=zz: block(t, zz, j_d), lambda t=t, zz=zz: block(t, zz, 4), to_d)]
            else:
                job["d"] = [
                    copies.add(
                        lambda t=t, zz=zz, lo=lo, count=count: piece(t, zz, j_d, lo, count),
                        lambda t=t, zz=zz, lo=lo, count=count: piece(t, zz, 4, lo, count),
                        to,
                    )
                    for to, lo, count in ((to_y, 0, cut), (to_x, cut, hrows - cut))
                ]
            job["x"] = copies.add(lambda t=t, zz=zz: block(t, zz, j_x), lambda t=t, zz=zz: block(t, zz, 5), to_x)
            job["y"] = copies.add(lambda t=t, zz=zz: block(t, zz, j_y), lambda t=t, zz=zz: block(t, zz, 6), to_y)
            job["z"] = copies.add(
                lambda t=t, zz=zz: z_out(t, zz),
                lambda zz=zz: z_in(core, (zz + depth - z_me) % depth),
                lambda t=t, zz=zz: at(t, 4 * zz + j_me),
                lambda zz=zz: z_recv.at[core * depth + (zz + depth - z_me) % depth],
                lambda zz=zz: z_me != zz,
            )
            jobs[t, zz] = job

    def pack(t, planes):
        wanted = [i for i in packed_of if i // 4 in planes]
        for i in wanted:
            a_rows, h_rows, h_off, h_first = plan.a_rows[i], plan.h_rows[i], plan.h_off[i], plan.h_first[i]
            to = packed.at[packed_of.index(i)]
            for part in scratch:
                part[...] = jnp.zeros(part.shape, F32)
            lo16, hi16 = h_first // 16 * 16, -(-(h_first + h_rows) // 16) * 16
            for half in range(2):
                for j in range(5 if h_rows else 0):
                    cols = slice(D * j + 128 * half, D * j + 128 * half + 128)
                    value = gh[t, lo16:hi16, cols].astype(F32)[h_first - lo16 : h_first - lo16 + h_rows]
                    scratch[half][pl.ds(h_off + j, h_rows, stride=5)] = value
            whole = jnp.concatenate([scratch[0][...], scratch[1][...]], 1)
            to[a_rows:rows] = whole[a_rows:].astype(BF)
            if a_rows:
                to[0:a_rows] = gw[t, plan.a_base[i] : plan.a_base[i] + a_rows]

    def plus(*refs):
        value = refs[0][...].astype(F32)
        for ref in refs[1:]:
            value = value + ref[...].astype(F32)
        return value

    def sum_0(t, zz):
        copies.start(*jobs[t, zz]["swap"])

    def sum_1(t, zz):
        job = jobs[t, zz]
        for j in range(4):
            copies.arrive(job["swap"][j])
            target = block(t, zz, j)
            target[...] = plus(slot_half(t, 4 * zz + j, low), target).astype(BF)
        copies.start(*job["d"])
        if (t, zz) in direct:
            copies.start(job["x"], job["y"])

    def sum_2(t, zz):
        job = jobs[t, zz]
        for side, copy, j, lo, count in (("x", job["d"][0], j_x, 0, cut), ("y", job["d"][1], j_y, cut, hrows - cut)):
            copies.arrive(copy)
            target = piece(t, zz, j, lo, count)
            target[...] = plus(target, piece(t, zz, 4, lo, count)).astype(BF)
            copies.start(job[side])

    def sum_3(t, zz):
        job = jobs[t, zz]
        copies.arrive(job["x"], job["y"])
        value = plus(block(t, zz, j_me), block(t, zz, 5), block(t, zz, 6))
        if (t, zz) in direct:
            copies.arrive(*job["d"])
            value = value + block(t, zz, 4)[...].astype(F32)

        @pl.when(z_me != zz)
        def _():
            z_out(t, zz)[...] = value.astype(BF)
            copies.start(job["z"])

        @pl.when((z_me == zz) & (core == t))
        def _():
            final(core)[...] = value

        @pl.when((z_me == zz) & (core != t))
        def _():
            outgo[...] = value
            copies.start(hand_over)

    def sum_4():
        copies.arrive(hand_over)
        for h in range(2):
            for k in range(1, depth):
                src = z_in(h, k)
                pltpu.make_async_remote_copy(
                    src_ref=src, dst_ref=src, send_sem=send.at[0], recv_sem=z_recv.at[h * depth + k], device_id=sibling(), device_id_type=MESH
                ).wait_recv()
                final(h)[...] = final(h)[...] + src[...].astype(F32)

    def final(h):
        return owned.at[h]

    outgo = owned.at[2]

    def vector_step(step):
        sources = [gv.at[1 - core], vacc.at[0], vacc.at[1]]
        along = [lambda k=k: at(core, (me + 4 * k) % n) for k in range(1, depth)]
        targets = [[sibling], [to_x, to_y, to_d], along]
        if step:
            base = gv[core] if step == 1 else vacc[step - 2]
            for number, k in vector_copies[-1]:
                copies.arrive(number)
                base = base + vin[k]
            vacc[step - 1] = base
        if step < 3:
            started = []
            for k, to in enumerate(targets[step], (0, 1, 4)[step]):
                number = copies.add(lambda step=step: sources[step], lambda k=k: vin.at[k], to)
                copies.start(number)
                started.append((number, k))
            vector_copies.append(started)

    vector_copies = []
    hand_over = copies.add(lambda: outgo, lambda: final(core), sibling)
    peers = [(1 - core, me), (core, near_x), (core, near_y), (core, near_xy)] + [(1 - core, (me + 4 * k) % n) for k in range(1, depth)] + [(core, (me + 4 * k) % n) for k in range(1, depth)]

    bwd = (eye, w, wh, vec, wht, vt, gsb, xt, mix, xh, gp, rstd, stream, ex, br, dm, acc, lg, dl, both, rw, gw, gh, gv, dm, width)
    ig_copies = [copies.add(lambda: dm, lambda: ig_out.at[out_rows], sibling, None, lambda t=t: core != t) for t in range(2)]

    def ig_local():
        return pltpu.make_async_copy(dm, ig_out.at[out_rows], local.at[2])

    def emit_inputs(t):
        pl.when(core == t)(lambda: ig_local().start())
        pl.when(core != t)(lambda: copies.start(ig_copies[t]))

    def free_inputs(t):
        pl.when(core == t)(lambda: ig_local().wait())
        pl.when(core != t)(lambda: copies.get(ig_copies[t]).wait_send())

    def signal_ready(which):
        for to_core, to_index in peers:
            pl.semaphore_signal(ready.at[which], inc=1, device_id=at(to_core, to_index), device_id_type=MESH)

    def wait_ready(which):
        pl.semaphore_wait(ready.at[which], len(peers))

    def schedule(i, steps):
        for step in sorted({s[0] for s in steps}):

            def run(step=step):
                for s, f, *args in steps:
                    if s == step:
                        f(*args)

            pl.when(i == step)(run)

    def after_head_1():
        copies.leave(st_copy)
        st_stay.wait()
        signal_ready(0)

    def during_backward_1(i):
        schedule(i, [
            (1, wait_ready, 0), (1, pack, 1, (3,)), (1, sum_0, 1, 3),
            (2, sum_1, 1, 3),
            (4, pack, 1, (2,)), (4, sum_0, 1, 2), (4, sum_2, 1, 3),
            (5, sum_1, 1, 2),
            (7, sum_2, 1, 2), (7, sum_3, 1, 3),
        ])

    ex[...] = jnp.zeros_like(ex)
    backward_tower(1, bwd, after_head_1, during_backward_1, None, lambda: sum_3(1, 2))
    emit_inputs(1)
    signal_ready(1)
    for zz in early:
        job = jobs[1, zz]
        copies.leave(*job["swap"], *job["d"], job["x"], job["y"])

    def after_head_0():
        wait_ready(1)
        sum_0(1, 1)
        sum_0(1, 0)
        pack(0, (3,))
        sum_0(0, 3)

    def during_backward_0(i):
        schedule(i, [
            (0, sum_1, 1, 1), (0, sum_1, 1, 0),
            (1, sum_1, 0, 3),
            (3, sum_2, 1, 1), (3, sum_2, 1, 0),
            (4, pack, 0, (2,)), (4, sum_0, 0, 2), (4, sum_2, 0, 3),
            (5, sum_1, 0, 2),
            (7, sum_3, 1, 1), (7, sum_3, 1, 0),
            (8, sum_0, 0, 1), (8, sum_2, 0, 2), (8, sum_3, 0, 3),
            (9, sum_1, 0, 1),
        ])

    def after_weights():
        sum_0(0, 0)
        vector_step(0)
        sum_2(0, 1)

    backward_tower(0, bwd, after_head_0, during_backward_0, lambda: free_inputs(1), after_weights)
    emit_inputs(0)
    sum_1(0, 0)
    vector_step(1)
    sum_3(0, 2)
    sum_3(0, 1)
    sum_3(0, 0)
    vector_step(2)
    sum_4()
    vector_step(3)

    slot128[...] = jnp.zeros(slot128.shape, F32)
    for h in range(2):
        slot128[pl.ds(2 * hrows * h, hrows, stride=2)] = final(h)[:, 0:128]
        slot128[pl.ds(2 * hrows * h + 1, hrows, stride=2)] = final(h)[:, 128:D]

    @pl.when(me == owner)
    def _():
        for kind in range(3):
            first = 2 * (plan.v_off[owner] + kind * (BLOCKS + 1))
            for h in range(2):
                value = vacc[2, kind, 0 : BLOCKS + 1, 128 * h : 128 * h + 128]
                slot128[pl.ds(first + h, BLOCKS + 1, stride=2)] = value

    def push(src, dst, to):
        number = copies.add(lambda: src, lambda: dst, lambda: to)
        copies.start(number)
        return copies.get(number)

    lay_flat(plan, me, slot128, flat, rolled)
    for c in moments:
        c.wait()
    update_shard(
        plan, me, params_in, first_new, second_new, (first_new, second_new, new, norm_out),
        flat, squares, sq_in, push, [to_x(), to_y(), to_d()], [at(core, (me + 4 * k) % n) for k in range(1, depth)],
    )
    copies.arrive(st_copy)
    pl.when(core == 0)(lambda: copies.arrive(ig_copies[0]))
    pl.when(core == 1)(lambda: copies.arrive(ig_copies[1]))
    free_inputs(0)
    copies.sent.update(ig_copies)
    copies.leave(*range(len(copies.made)))


def train(plan, latent, codes, targets, visits, imp, params, first, second):
    n, rows = plan.n, plan.slot
    depth, hrows = n // 4, rows // 2
    width = codes.shape[1] // 2
    height = -(-params.shape[1] // 1024) * 8
    vm = pl.BlockSpec(memory_space=pltpu.VMEM)
    hbm = pl.BlockSpec(memory_space=pl.ANY)
    packed = sum(1 for h, v in zip(plan.h_rows, plan.v_rows) if h or v)
    return pl.pallas_call(
        functools.partial(train_kernel, plan),
        out_shape=(
            jax.ShapeDtypeStruct((2 * width, D), BF),
            jax.ShapeDtypeStruct((2 * width, D), F32),
            jax.ShapeDtypeStruct(params.shape, F32),
            jax.ShapeDtypeStruct(params.shape, F32),
            jax.ShapeDtypeStruct(params.shape, F32),
            jax.ShapeDtypeStruct((2, MATS), F32),
        ),
        in_specs=[hbm] + [vm] * 5 + [hbm] * 2,
        out_specs=(hbm, hbm, vm, vm, vm, vm),
        scratch_shapes=[
            pltpu.VMEM((2, A_ROWS, D), BF),
            pltpu.VMEM((2, D, HPAD), BF),
            pltpu.VMEM((2, 128, D), BF),
            pltpu.VMEM((2, 8, width), jnp.int32),
            pltpu.VMEM((8, width), jnp.int32),
            pltpu.VMEM((8, width), F32),
            *work_scratch(width),
            pltpu.VMEM((2, A_ROWS, D), BF),
            pltpu.VMEM((2, D, HPAD), BF),
            pltpu.VMEM((2, 3, 16, D), F32),
            pltpu.VMEM((packed, rows, D), BF),
            pltpu.VMEM((2, width, D), BF),
            pltpu.VMEM((max(2 * rows, height + 48) + 80, 128), F32),
            pltpu.VMEM((height + 128, 128), F32),
            pltpu.VMEM((height + 40, 128), F32),
            pltpu.VMEM((128, D), F32),
            pltpu.VMEM((3, 3, 16, D), F32),
            pltpu.VMEM((3 + depth, 3, 16, D), F32),
            pltpu.VMEM((3, hrows, D), F32),
            pltpu.VMEM((4, 32, 128), F32),
            pltpu.VMEM((2 + depth, 32, 128), F32),
            pltpu.VMEM((8, 128), F32),
            pltpu.SemaphoreType.DMA((11 * n,)),
            pltpu.SemaphoreType.DMA((11 * n,)),
            pltpu.SemaphoreType.DMA((2 * depth,)),
            pltpu.SemaphoreType.DMA((2 * (depth + 2),)),
            pltpu.SemaphoreType.DMA((5,)),
            pltpu.SemaphoreType.REGULAR((2,)),
        ],
        compiler_params=pltpu.CompilerParams(
            collective_id=2, has_side_effects=True, vmem_limit_bytes=63 * 1024 * 1024
        ),
    )(latent, codes, targets, visits, imp, params, first, second)


def on_device(latent, codes, targets, visits, importance, params, first_moment, second_moment):
    me = lax.axis_index("tower")
    row_count = latent.shape[0]
    half = row_count // 2
    shard_len = params.shape[1]
    plan = Plan(lax.axis_size("dp"), shard_len)
    if fused_fits(plan):
        states_out, inputs_out, first, second, new, norms = train(
            plan, latent, codes, targets.transpose(1, 0, 2), visits[0].T, importance[None], params, first_moment, second_moment
        )
    else:
        height = -(-plan.rows128 // 8) * 8
        p128, m128, v128 = (
            jnp.pad(v, ((0, 0), (0, 128 * height - shard_len))).reshape(height, 128)
            for v in (params, first_moment, second_moment)
        )
        ints = jnp.concatenate([codes, targets[0, :1], visits[0].T, targets[0, 1:]], 0)
        x = lax.dynamic_slice_in_dim(latent, me * half, half, 0)
        w, wh, vec, both, rw = gather(plan, p128, ints, importance[None])
        st, ig, gw, gh, gv = compute(x, both, rw, w, wh, vec)
        states_out, inputs_out, *flat, norms = reduce_and_update(plan, gw, gh, gv, st, ig, p128, m128, v128)
        first, second, new = (v.reshape(1, -1)[:, :shard_len] for v in flat)
    return (states_out[None], inputs_out[None], first, second, new, new.astype(BF), norms[None])


def solution(mesh):
    in_specs = (
        P("dp", None),
        P("tower", "dp"),
        P("tower", None, "dp"),
        P("tower", "dp", None),
        P("dp"),
        P("tower", "dp"),
        P("tower", "dp"),
        P("tower", "dp"),
    )
    out_specs = (
        P("tower", "dp", None),
        P("tower", "dp", None),
        P("tower", "dp"),
        P("tower", "dp"),
        P("tower", "dp"),
        P("tower", "dp"),
        P("tower", None, None),
    )
    return jax.shard_map(
        on_device, mesh=mesh, in_specs=in_specs, out_specs=out_specs, check_vma=False
    )
```

```python
import functools

import jax
import jax.numpy as jnp
from jax import lax
from jax.experimental import pallas as pl
from jax.experimental.pallas import tpu as pltpu
from jax.sharding import PartitionSpec as P

D = 256
CODES = 32
BINS = 601
BLOCKS = 10
STEP = 5
HEADS = 1238
MATS = 12
P_SIZE = 1054464
HPAD = 1280
CAT = D + CODES
A_ROWS = CAT + BLOCKS * D
BF = jnp.bfloat16
F32 = jnp.float32
GELU_C = 0.7978845608028654
GELU_K = 0.044715


def nn(a, b):
    return jnp.dot(a, b, preferred_element_type=F32)


def nt(a, b):
    return lax.dot_general(a, b, (((1,), (1,)), ((), ())), preferred_element_type=F32)


def identity(n):
    return (lax.broadcasted_iota(jnp.int32, (n, n), 0) == lax.broadcasted_iota(jnp.int32, (n, n), 1)).astype(BF)


ZETA = (GELU_C * GELU_K) ** (1.0 / 3.0)
B0 = GELU_C / ZETA
E0 = 0.5 / ZETA


def wide(v, cs):
    return jnp.concatenate([v] * ((cs.stop - cs.start) // v.shape[1]), 1)


def norm_act(src, cs, gs, unit, gp, rstd, out):
    for r in range(0, D, 32):
        rs = slice(r, r + 32)
        xh = src[rs, cs] * rstd
        z = xh * wide(gs[rs, 0:128], cs) + wide(gs[rs, 128:256], cs)
        z2 = z * z
        t = jnp.tanh(z * (z2 + B0))
        q = t * E0 + E0
        a = z * q
        out(rs, a)
        unit[rs, cs] = xh.astype(BF)
        gp[rs, cs] = (q + (a * (1.0 - t)) * (z2 * 3.0 + B0)).astype(BF)


def broadcast_vectors(vt, rows):
    k = lax.broadcasted_iota(jnp.int32, (128, 128), 0)
    picks = jnp.concatenate([(k == row).astype(BF) for row in rows], 1)
    return nn(vt, picks)


def head_stage(cs, lg, dl, ints, rw):
    width = rw.shape[1]
    it8 = lax.broadcasted_iota(jnp.int32, (8, width), 0)
    low = -jnp.inf
    b75, b150, b154 = lg[600:608], lg[1200:1208], lg[1232:1240]

    def top(block):
        return jnp.max(block, axis=0, keepdims=True)

    def top_range(lo, hi):
        best = lg[lo : lo + 8]
        for r in range(lo + 8, hi, 8):
            best = jnp.maximum(best, lg[r : r + 8])
        return best

    max_v = top(jnp.maximum(top_range(0, 600), jnp.where(it8 < 1, b75, low)))
    max_r = top(
        jnp.maximum(
            jnp.maximum(top_range(608, 1200), jnp.where(it8 >= 1, b75, low)),
            jnp.where(it8 < 2, b150, low),
        )
    )
    max_c = top(
        jnp.maximum(
            jnp.maximum(top_range(1208, 1232), jnp.where(it8 >= 2, b150, low)),
            jnp.where(it8 < 2, b154, low),
        )
    )
    in_policy = (it8 >= 2) & (it8 < 6)
    max_p = top(jnp.where(in_policy, b154, low))

    def exp_range(lo, hi, best):
        acc = jnp.zeros((8, width), F32)
        for r in range(lo, hi, 8):
            e = jnp.exp(lg[r : r + 8] - best)
            lg[r : r + 8] = e
            acc = acc + e
        return acc

    e75 = jnp.exp(b75 - jnp.where(it8 < 1, max_v, max_r))
    e150 = jnp.exp(b150 - jnp.where(it8 < 2, max_r, max_c))
    e154 = jnp.exp(b154 - jnp.where(it8 < 2, max_c, max_p))

    def total(acc):
        return rw / jnp.sum(acc, axis=0, keepdims=True)

    inv_v = total(exp_range(0, 600, max_v) + jnp.where(it8 < 1, e75, 0.0))
    inv_r = total(exp_range(608, 1200, max_r) + jnp.where(it8 >= 1, e75, 0.0) + jnp.where(it8 < 2, e150, 0.0))
    inv_c = total(exp_range(1208, 1232, max_c) + jnp.where(it8 >= 2, e150, 0.0) + jnp.where(it8 < 2, e154, 0.0))
    inv_p = total(jnp.where(in_policy, e154, 0.0))
    hit_v = ints[1:2]
    hit_r = ints[6:7] + BINS
    hit_c = ints[7:8] + 2 * BINS
    counts = jnp.where(in_policy, ints.astype(F32), 0.0)
    share = counts * (rw / jnp.sum(counts, axis=0, keepdims=True))

    def minus(value, lo, *hits):
        at = lax.broadcasted_iota(jnp.int32, value.shape, 0)
        for hit in hits:
            value = value - jnp.where(at == hit - lo, rw, 0.0)
        return value

    d75 = minus(e75 * jnp.where(it8 < 1, inv_v, inv_r), 600, hit_v, hit_r)
    d150 = minus(e150 * jnp.where(it8 < 2, inv_r, inv_c), 1200, hit_r, hit_c)
    d154 = minus(e154 * jnp.where(it8 < 2, inv_c, inv_p), 1232, hit_c) - share
    d154 = jnp.where(it8 < 6, d154, 0.0)

    def emit(lo, hi, inv, hit):
        for r in range(lo, hi, 16):
            dl[r : r + 16, cs] = minus(lg[r : r + 16] * inv, r, hit).astype(BF)

    def pair(first, second):
        return jnp.concatenate([first, second], 0).astype(BF)

    emit(0, 592, inv_v, hit_v)
    dl[592:608, cs] = pair(minus(lg[592:600] * inv_v, 592, hit_v), d75)
    emit(608, 1200, inv_r, hit_r)
    dl[1200:1216, cs] = pair(d150, minus(lg[1208:1216] * inv_c, 1208, hit_c))
    emit(1216, 1232, inv_c, hit_c)
    dl[1232:1248, cs] = pair(d154, jnp.zeros_like(d154))
    dl[1248:HPAD, cs] = jnp.zeros((HPAD - 1248, width), BF)


CB = 256
GROUP = 2


def saved_views(t, mix, xh):
    def mixed(k):
        return mix.at[pl.ds(pl.multiple_of((t * BLOCKS + k - 1) * (D + 16), 16), D + 16)]

    def unit(k):
        return xh.at[pl.ds(pl.multiple_of((t * (BLOCKS + 1) + k) * D, D), D)]

    return mixed, unit


def column_groups(width):
    blocks = [slice(c, c + CB) for c in range(0, width, CB)]
    per = min(GROUP, len(blocks))
    return blocks, per, [slice(c, c + per * CB) for c in range(0, width, per * CB)]


def forward_tower(t, refs, during=None):
    (eye, w, wh, vec, wt, vt, gsb, xt, mix, xh, gp, rstd, stream, mean, ints, width) = refs
    blocks, per, groups = column_groups(width)
    mixed, unit = saved_views(t, mix, xh)
    first_bias = 2 * (BLOCKS + 1)
    ones = jnp.ones((16, D), BF)

    def mean_rows(slot):
        value = nn(ones, wt[slot, 0:D])[0:8] * (1.0 / D)
        high = value.astype(BF).astype(F32)
        wt[slot, D : D + 16] = jnp.concatenate([high, value - high], 0).astype(BF)

    def vectors(k):
        gsb[k % 2] = broadcast_vectors(vt[...], (k, k + BLOCKS + 1)) * ZETA

    def prefetch(k):
        vectors(k)
        row = pl.multiple_of(CAT + jnp.minimum(k - 1, BLOCKS - 1) * D, 32)
        wt[k % 2, 0:D, 0:D] = nt(eye[...], w[t, pl.ds(row, D)]).astype(BF)
        at_row = lax.broadcasted_iota(jnp.int32, (128, 128), 0) == k + first_bias
        at_lane = lax.broadcasted_iota(jnp.int32, (128, 128), 1) == 0
        wt[k % 2, 0:D, D:384] = nn(vt[...], (at_row & at_lane).astype(BF)).astype(BF)
        mean_rows(k % 2)

    def row_of(k):
        return pl.ds(t * (BLOCKS + 1) + k, 1)

    def stage(k, c):
        def keep(rs, a):
            mixed(k)[rs, blocks[c]] = a.astype(BF)

        norm_act(stream, blocks[c], gsb.at[k % 2], unit(k), gp.at[t, k], rstd[row_of(k), blocks[c]], keep)

    def spread(square, k, cs):
        var = jnp.sum(square, axis=0, keepdims=True) * (1.0 / D)
        rstd[row_of(k), cs] = lax.rsqrt(var + 1e-05)

    def add(k, cs, out, fresh):
        shift = out[D : D + 1] + out[D + 8 : D + 9]
        square = jnp.zeros((8, out.shape[1]), F32)
        for r in range(0, D, 32):
            value = out[r : r + 32] - shift
            if not fresh:
                value = stream[r : r + 32, cs] + value
            stream[r : r + 32, cs] = value
            square = square + jnp.sum((value * value).reshape(4, 8, -1), axis=0)
        if not fresh:
            mean[0:1, cs] = mean[0:1, cs] + shift
        spread(square, k + 1, cs)

    def centre(cs):
        total = jnp.zeros((8, CB), F32)
        for r in range(0, D, 32):
            total = total + jnp.sum(stream[r : r + 32, cs].reshape(4, 8, -1), axis=0)
        middle = jnp.sum(total, axis=0, keepdims=True) * (1.0 / D)
        mean[0:1, cs] = middle
        square = jnp.zeros((8, CB), F32)
        for r in range(0, D, 32):
            value = stream[r : r + 32, cs] - middle
            stream[r : r + 32, cs] = value
            square = square + jnp.sum((value * value).reshape(4, 8, -1), axis=0)
        spread(square, 1, cs)

    vt[...] = nt(eye[...], vec[t]).astype(BF)
    vectors(0)
    wt[0, 0:D, 0:D] = nt(eye[...], w[t, 0:D]).astype(BF)
    tile = first_bias // 16 * 16
    picked = lax.broadcasted_iota(jnp.int32, (16, D), 0) == first_bias - tile
    bias = jnp.where(picked, vec[t, tile : tile + 16].astype(F32), 0.0).astype(BF)
    rest = jnp.concatenate([w[t, D:CAT], bias, jnp.zeros((128 - CODES - 16, D), BF)], 0)
    wt[0, 0:D, D:384] = nt(eye[...], rest).astype(BF)
    mean_rows(0)
    for cs in blocks:
        it = lax.broadcasted_iota(jnp.int32, (CODES, CB), 0)
        xt[t, D:CAT, cs] = (it == ints[t, 0:1, cs]).astype(BF)
        xt[t, CAT : CAT + 16, cs] = jnp.ones((16, CB), BF)
    first = [nn(wt[0, :, 0 : CAT + 16], xt[t, :, cs]) for cs in groups]
    prefetch(1)
    for group, cs in enumerate(groups):
        add(-1, cs, first[group], True)
    for cs in blocks:

        def keep(rs, a):
            stream[rs, cs] = a

        norm_act(stream, cs, gsb.at[0], unit(0), gp.at[t, 0], rstd[row_of(0), cs], keep)
        centre(cs)

    def layer(k, more):
        mixed(k)[D : D + 16, :] = jnp.ones((16, width), BF)
        for group, cs in enumerate(groups):
            out = nn(wt[k % 2, :, 0 : D + 16], mixed(k)[:, cs])
            ahead = group + 1 < len(groups)
            if ahead or more:
                for c in range(per):
                    stage(k if ahead else k + 1, (group + 1) % len(groups) * per + c)
            add(k, cs, out, False)
        if more:
            prefetch(k + 2)

    prefetch(2)
    for c in range(per):
        stage(1, c)

    @pl.loop(1, BLOCKS)
    def _(k):
        if during is not None:
            during(k)
        layer(k, True)

    layer(BLOCKS, False)
    for cs in blocks:
        xt[t + 1, 0:D, cs] = (stream[:, cs] + mean[0:1, cs]).astype(BF)


def backward_tower(t, refs, after_head=None, during=None, before_product=None, after_weights=None):
    (eye, w, wh, vec, wht, vt, gsb, xt, mix, xh, gp, rstd, ds, ex, br, dm, acc, lg, dl, ints, rw, gw, gh, gv, ig, width) = refs
    blocks = [slice(c, c + CB) for c in range(0, width, CB)]
    last = len(blocks) - 1
    mixed, unit = saved_views(t, mix, xh)
    vt[...] = nt(eye[...], vec[t]).astype(BF)
    for h in range(0, HPAD, D):
        wht[h : h + D, :] = nt(eye[...], wh[t, :, h : h + D]).astype(BF)

    @pl.loop(0, width // CB)
    def _(c):
        cs = pl.ds(pl.multiple_of(c * CB, CB), CB)
        lg[...] = nn(wht[...], xt[t + 1, 0:D, cs])
        head_stage(cs, lg, dl, ints[t, :, cs], rw[0:1, cs])
        value = nn(wh[t], dl[:, cs]) + ex[:, cs]
        ds[:, cs] = value
        br[BLOCKS % 2, :, cs] = value.astype(BF)

    for h in range(0, HPAD, D):
        gh[t, :, h : h + D] = nt(xt[t + 1, 0:D, :], dl[h : h + D]).astype(BF)
    if after_head is not None:
        after_head()
    acc[...] = jnp.zeros(acc.shape, F32)
    ones = jnp.ones((16, 128), BF)

    def part(c):
        return dm.at[c * D : c * D + D]

    def gains(k):
        gsb[k % 2, :, 0:128] = broadcast_vectors(vt[...], (k,)) * ZETA

    def row_sums(k):
        for kind in range(2):
            gv[t, kind, pl.ds(k, 1), :] = nt(ones, acc[k % 2, kind].astype(BF))[0:1] * ZETA
        acc[k % 2] = jnp.zeros(acc.shape[1:], F32)

    def product(k, c):
        row = pl.multiple_of(CAT + (k - 1) * D, 32)
        part(c)[...] = nn(w[t, pl.ds(row, D)], br[k % 2, :, blocks[c]])

    def slopes(k, c):
        cs, grad, sums = blocks[c], part(c), acc.at[k % 2]
        s1 = jnp.zeros((8, CB), F32)
        s2 = jnp.zeros((8, CB), F32)
        for r in range(0, D, 32):
            rs = slice(r, r + 32)
            g = wide(gsb[k % 2, rs, 0:128], cs)
            dy = grad[rs, :] * gp[t, k, rs, cs].astype(F32)
            prod = dy * unit(k)[rs, cs].astype(F32)
            back = dy * g
            grad[rs, :] = back
            s1 = s1 + jnp.sum(back.reshape(4, 8, CB), axis=0)
            s2 = s2 + jnp.sum((prod * g).reshape(4, 8, CB), axis=0)
            sums[0, rs] = sums[0, rs] + (prod[:, 0:128] + prod[:, 128:CB])
            sums[1, rs] = sums[1, rs] + (dy[:, 0:128] + dy[:, 128:CB])
        return [jnp.sum(s, axis=0, keepdims=True) * (1.0 / D) for s in (s1, s2)]

    def stage(k, c, first):
        cs = blocks[c]
        means = slopes(k, c)
        scale = rstd[pl.ds(t * (BLOCKS + 1) + k, 1), cs]
        m1, m2 = (jnp.broadcast_to(m * scale, (32, CB)).astype(BF) for m in means)
        for r in range(0, D, 32):
            rs = slice(r, r + 32)
            back = part(c)[rs, :] * scale - (m1 + unit(k)[rs, cs] * m2).astype(F32)
            if first:
                br[0, rs, cs] = back.astype(BF)
            else:
                value = ds[rs, cs] + back
                ds[rs, cs] = value
                br[(k + 1) % 2, rs, cs] = value.astype(BF)

    if before_product is not None:
        before_product()
    gains(BLOCKS)
    gains(BLOCKS - 1)
    product(BLOCKS, 0)

    @pl.loop(0, BLOCKS)
    def _(i):
        k = BLOCKS - i
        if during is not None:
            during(i)
        for c in range(last + 1):
            if c < last:
                product(k, c + 1)
            stage(k, c, False)
            if c == 0:
                full = nt(mixed(k)[...], br[k % 2])
                row = pl.multiple_of(CAT + (k - 1) * D, 32)
                gw[t, pl.ds(row, D), :] = full[0:D].astype(BF)
                gv[t, 2, pl.ds(k, 1), :] = full[D : D + 1]
                product(k - 1, 0)
        gains(k - 2)
        row_sums(k)

    for c, cs in enumerate(blocks):
        part(c)[...] = ds[:, cs]
        stage(0, c, True)
    full = nt(xt[t], br[0])
    gw[t, 0:CAT, :] = full[0:CAT].astype(BF)
    gv[t, 2, 0:1, :] = full[CAT : CAT + 1]
    row_sums(0)
    if after_weights is not None:
        after_weights()
    for cs in blocks:
        back = nn(w[t, 0:D], br[0, :, cs])
        ex[:, cs] = back
        ig[cs, :] = back.T


def compute_kernel(x_ref, ints, rw, w, wh, vec, st, ig, gw, gh, gv, eye, wt, wht, vt, gsb, xt, mix, xh, gp, rstd, mean, stream, ex, br, dm, acc, lg, dl):
    width = x_ref.shape[0]
    eye[...] = identity(D)
    for c in range(0, width, CB):
        cs = slice(c, c + CB)
        xt[0, 0:D, cs] = nt(eye[...], x_ref[cs, :]).astype(BF)
    fwd = (eye, w, wh, vec, wt, vt, gsb, xt, mix, xh, gp, rstd, stream, mean, ints, width)
    @pl.loop(0, 2)
    def _(t):
        forward_tower(t, fwd)

        @pl.loop(0, width // CB)
        def _(c):
            cs = pl.ds(pl.multiple_of(c * CB, CB), CB)
            st[t, cs, :] = nt(eye[...], xt[t + 1, 0:D, cs]).astype(BF)

    ex[...] = jnp.zeros_like(ex)

    @pl.loop(0, 2)
    def _(i):
        t = 1 - i
        backward_tower(
            t,
            (eye, w, wh, vec, wht, vt, gsb, xt, mix, xh, gp, rstd, stream, ex, br, dm, acc, lg, dl, ints, rw, gw, gh, gv, ig.at[t], width),
        )


def work_scratch(width):
    return [
        pltpu.VMEM((D, D), BF),
        pltpu.VMEM((2, D + 16, 384), BF),
        pltpu.VMEM((HPAD, D), BF),
        pltpu.VMEM((D, 128), BF),
        pltpu.VMEM((2, D, 256), F32),
        pltpu.VMEM((3, CAT + 16, width), BF),
        pltpu.VMEM((2 * BLOCKS * (D + 16), width), BF),
        pltpu.VMEM((2 * (BLOCKS + 1) * D, width), BF),
        pltpu.VMEM((2, BLOCKS + 1, D, width), BF),
        pltpu.VMEM((24, width), F32),
        pltpu.VMEM((8, width), F32),
        pltpu.VMEM((D, width), F32),
        pltpu.VMEM((D, width), F32),
        pltpu.VMEM((2, D, width), BF),
        pltpu.VMEM((width // CB * D, CB), F32),
        pltpu.VMEM((2, 2, D, 128), F32),
        pltpu.VMEM((HPAD, CB), F32),
        pltpu.VMEM((HPAD, width), BF),
    ]


def compute(x, ints, rw, w, wh, vec):
    width = x.shape[0]
    vm = pl.BlockSpec(memory_space=pltpu.VMEM)
    return pl.pallas_call(
        compute_kernel,
        out_shape=(
            jax.ShapeDtypeStruct((2, width, D), BF),
            jax.ShapeDtypeStruct((2, width, D), F32),
            jax.ShapeDtypeStruct((2, A_ROWS, D), BF),
            jax.ShapeDtypeStruct((2, D, HPAD), BF),
            jax.ShapeDtypeStruct((2, 3, 16, D), F32),
        ),
        in_specs=[vm] * 6,
        out_specs=(vm,) * 5,
        scratch_shapes=work_scratch(width),
        compiler_params=pltpu.CompilerParams(vmem_limit_bytes=62 * 1024 * 1024),
    )(x, ints, rw, w, wh, vec)


class Plan:
    def __init__(self, n, length):
        self.n, self.length = n, length
        self.rows128 = -(-length // 128)
        block_end, head_end = A_ROWS * D, A_ROWS * D + D * HEADS
        self.a_base, self.a_rows, self.h_first, self.h_rows, self.h_off, self.v_first, self.v_rows, self.v_off = ([] for _ in range(8))
        used = 0
        for i in range(n):
            lo, hi = i * length, (i + 1) * length
            base = min(lo, block_end) // D // 16 * 16
            top = -(-min(hi, block_end) // D)
            a_rows = -(-(top - base) // 16) * 16 if lo < block_end else 0
            first = min(max(lo - block_end, 0), D * HEADS) // HEADS
            last = -(-min(max(hi - block_end, 0), D * HEADS) // HEADS)
            h_rows = last - first if hi > block_end and lo < head_end else 0
            v_first = max(lo - head_end, 0) // D
            v_rows = -(-(hi - head_end) // D) - v_first if hi > head_end else 0
            self.a_base.append(base)
            self.a_rows.append(a_rows)
            self.h_first.append(first)
            self.h_rows.append(h_rows)
            self.h_off.append(a_rows)
            self.v_first.append(v_first)
            self.v_rows.append(v_rows)
            self.v_off.append(a_rows + 5 * h_rows)
            used = max(used, a_rows + 5 * h_rows + v_rows)
        self.heads = max(self.h_rows)
        self.image = (HEADS * self.heads // 128 + 24) // 8 * 8
        self.slot = -(-(used + 1) // 32) * 32

    def at(self, table, me):
        value = jnp.int32(table[0])
        for i in range(1, self.n):
            if table[i] != table[i - 1]:
                value = value + (me >= i).astype(jnp.int32) * (table[i] - table[i - 1])
        return value


MESH = pl.DeviceIdType.MESH


def neighbours(n):
    core = lax.axis_index("tower")
    me = lax.axis_index("dp")
    near_x = me + 1 - 2 * (me % 2)
    near_y = me + 2 - 4 * ((me // 2) % 2)
    return core, me, near_x, near_y


def at(core, index):
    return {"tower": core, "dp": index}


def greet(core, me, near_x, near_y, n, crossed=False):
    barrier = pltpu.get_barrier_semaphore()
    pl.semaphore_signal(barrier, inc=1, device_id=at(1 - core, me), device_id_type=MESH)
    for near in (near_x, near_y, near_x + near_y - me):
        pl.semaphore_signal(barrier, inc=1, device_id=at(core, near), device_id_type=MESH)
    for k in range(1, n // 4):
        pl.semaphore_signal(barrier, inc=1, device_id=at(core, (me + 4 * k) % n), device_id_type=MESH)
    for near in [near_x, near_y] + [(me + 4 * k) % n for k in range(1, n // 4)] if crossed else []:
        pl.semaphore_signal(barrier, inc=1, device_id=at(1 - core, near), device_id_type=MESH)
    return barrier


def place_shard(plan, me, p_ref, slot128, shifted, rolled):
    rows = plan.rows128
    start = me * plan.length
    shift = start % 128
    first = start // 128
    tall = shifted.shape[0]
    height = p_ref.shape[0]
    lane = lax.broadcasted_iota(jnp.int32, (height, 128), 1)
    rolled[0:8] = jnp.zeros((8, 128), F32)
    rolled[8 : 8 + height] = pltpu.roll(p_ref[...], shift, 1)
    shifted[...] = jnp.zeros((tall, 128), F32)
    moved = jnp.where(lane >= shift, rolled[8 : 8 + height], rolled[7 : 7 + height])
    shifted[16 : 16 + height] = moved
    slot128[...] = jnp.zeros(slot128.shape, F32)
    row = lax.broadcasted_iota(jnp.int32, (height, 128), 0)
    base = plan.at(plan.a_base, me)

    @pl.when(plan.at(plan.a_rows, me) > 0)
    def _():
        slot128[pl.ds(first - 2 * base, height)] = jnp.where(row + first < 2 * A_ROWS, moved, 0.0)

    v_start = (A_ROWS * D + D * HEADS) // 128
    v_rows, v_off, v_first = (plan.at(t, me) for t in (plan.v_rows, plan.v_off, plan.v_first))
    tall_v = min(height, -(-2 * max(plan.v_rows) // 8) * 8)

    @pl.when(v_rows > 0)
    def _():
        inside = plan.at([max(0, v_start - i * plan.length // 128) for i in range(plan.n)], me)
        to = 2 * v_off + first + inside - v_start - 2 * v_first
        slot128[pl.ds(to, tall_v)] = shifted[pl.ds(16 + inside, tall_v)]

    h_first, h_rows, h_off = (plan.at(t, me) for t in (plan.h_first, plan.h_rows, plan.h_off))

    @pl.when(h_rows > 0)
    def _():
        tall_h = plan.image
        begin = A_ROWS * D + HEADS * h_first - 128 * first + 128 * 16
        turn = begin % 128
        rolled[0:tall_h] = pltpu.roll(shifted[pl.ds(begin // 128, tall_h)], (128 - turn) % 128, 1)
        rolled[tall_h : tall_h + 8] = jnp.zeros((8, 128), F32)
        lane = lax.broadcasted_iota(jnp.int32, (tall_h, 128), 1)
        shifted[0:tall_h] = jnp.where(lane < 128 - turn, rolled[0:tall_h], rolled[1 : tall_h + 1])
        to = slot128.at[pl.ds(pl.multiple_of(2 * h_off, 8), 10 * plan.heads)]
        it = lax.broadcasted_iota(jnp.int32, (10, 128), 0)
        lane = lax.broadcasted_iota(jnp.int32, (10, 128), 1)
        for k in range(plan.heads):
            row, turn = HEADS * k // 128, HEADS * k % 128
            window = pltpu.roll(shifted[row : row + 16], (128 - turn) % 128, 1)
            value = jnp.where(lane < 128 - turn, window[0:10], window[1:11])
            kept = (it * 128 + lane < HEADS) & (k < h_rows)
            to[10 * k : 10 * k + 10] = to[10 * k : 10 * k + 10] + jnp.where(kept, value, 0.0)


def unpack_rows(plan, i, slot, w, heads, vectors, scratch):
    base, rows = plan.a_base[i], plan.a_rows[i]
    if rows:
        shared = i > 0 and base < plan.a_base[i - 1] + plan.a_rows[i - 1]
        lo = 0
        if shared:
            w[base : base + 16] = w[base : base + 16] + slot[0:16]
            lo = 16
        if rows > lo:
            w[base + lo : base + rows] = slot[lo:rows]
    h_rows, h_off, h_first = plan.h_rows[i], plan.h_off[i], plan.h_first[i]
    v_rows, v_off, v_first = plan.v_rows[i], plan.v_off[i], plan.v_first[i]
    if h_rows or v_rows:
        value = slot.astype(F32)
        scratch[0][...] = value[:, 0:128]
        scratch[1][...] = value[:, 128:D]
    if h_rows:
        shared = i > 0 and plan.h_rows[i - 1] and plan.h_first[i - 1] + plan.h_rows[i - 1] > h_first
        for j in range(5):
            for half in range(2):
                cols = slice(128 * half, 128 * half + 128)
                first = D * j + h_first
                value = scratch[half][pl.ds(h_off + j, h_rows, stride=5)]
                if shared:
                    heads[first : first + 1, cols] = heads[first : first + 1, cols] + value[0:1]
                    if h_rows > 1:
                        heads[first + 1 : first + h_rows, cols] = value[1:h_rows]
                else:
                    heads[first : first + h_rows, cols] = value
    if v_rows:
        shared = v_first and plan.v_first[i - 1] + plan.v_rows[i - 1] > v_first
        shared = shared or (i > 0 and plan.v_rows[i - 1] > 0 and v_first == 0)
        for half in range(2):
            cols = slice(128 * half, 128 * half + 128)
            value = scratch[half][v_off : v_off + v_rows]
            if shared:
                vectors[v_first : v_first + 1, cols] = vectors[v_first : v_first + 1, cols] + value[0:1]
                if v_rows > 1:
                    vectors[v_first + 1 : v_first + v_rows, cols] = value[1:v_rows]
            else:
                vectors[v_first : v_first + v_rows, cols] = value


def split3(value):
    hi = value.astype(BF).astype(F32)
    mid = (value - hi).astype(BF).astype(F32)
    return hi, mid, value - hi - mid


def gather_kernel(plan, p_ref, ints_ref, imp_ref, w, wh, vec, both, rw, slots, slot128, shifted, rolled, scratch, whf, vecf, send, recv):
    n = plan.n
    depth = n // 4
    core, me, near_x, near_y = neighbours(n)
    barrier = greet(core, me, near_x, near_y, n)
    place_shard(plan, me, p_ref, slot128, shifted, rolled)
    pl.semaphore_wait(barrier, depth + 3)
    half = rw.shape[1]
    started = []

    def copy(src, dst, slot, to):
        c = pltpu.make_async_remote_copy(
            src_ref=src, dst_ref=dst, send_sem=send.at[slot], recv_sem=recv.at[slot], device_id=to, device_id_type=MESH
        )
        c.start()
        started.append(c)
        return c

    mine = pl.multiple_of(core * half, half)
    theirs = pl.multiple_of((1 - core) * half, half)
    number = iter(range(1 << 20))
    ints_copy = copy(ints_ref.at[:, pl.ds(theirs, half)], both.at[core], next(number), at(1 - core, me))
    rows = plan.slot
    total = jnp.sum(imp_ref[...].astype(F32), axis=1, keepdims=True)
    lane = lax.broadcasted_iota(jnp.int32, (1, D), 1)
    hi, mid, lo = split3(total)
    left = slot128[pl.ds(0, rows, stride=2)]
    right = slot128[pl.ds(1, rows, stride=2)]
    own = jnp.concatenate([left, right], 1)
    last = jnp.where(lane == 0, hi, jnp.where(lane == 1, mid, jnp.where(lane == 2, lo, 0.0)))
    last_row = lax.broadcasted_iota(jnp.int32, (rows, D), 0) == rows - 1
    slots[core, me] = jnp.where(last_row, last, own).astype(BF)

    def column(index, k):
        return (index + n - 4 * k) % n

    def send_slot(origin, to, lo=0, hi=rows):
        ref = slots.at[core, origin, pl.ds(lo, hi - lo)]
        return copy(ref, ref, next(number), to)

    near_xy = near_x + near_y - me
    cut = rows // 2
    z_in, x_in, y_in, d_in, s_in = {}, {}, {}, {}, []
    for k in sorted(range(1, depth), key=lambda k: (min(k, depth - k), k)):
        z_in[k] = send_slot(me, at(core, (me + 4 * k) % n))
    order = [0] + list(z_in)
    for k in order:
        if k:
            z_in[k].wait_recv()
        x_in[k] = send_slot(column(me, k), at(core, near_x))
        y_in[k] = send_slot(column(me, k), at(core, near_y))
        s_in.append(send_slot(column(me, k), at(1 - core, me)))
    for k in order:
        x_in[k].wait_recv()
        first = send_slot(column(near_x, k), at(core, near_y), 0, cut)
        s_in.append(send_slot(column(near_x, k), at(1 - core, me)))
        y_in[k].wait_recv()
        second = send_slot(column(near_y, k), at(core, near_x), cut, rows)
        s_in.append(send_slot(column(near_y, k), at(1 - core, me)))
        d_in[k] = (first, second)
    for k in order:
        for c in d_in[k]:
            c.wait_recv()
        s_in.append(send_slot(column(near_xy, k), at(1 - core, me)))
    ints_copy.wait_recv()
    both[core] = ints_ref[:, pl.ds(mine, half)]
    for c in s_in:
        c.wait_recv()
    for c in started:
        c.wait_send()
    for t in range(2):
        vecf[...] = jnp.zeros(vecf.shape, F32)
        for i in range(n):
            unpack_rows(plan, i, slots[t, i], w.at[t], whf, vecf, [scratch.at[0], scratch.at[1]])
        for j in range(5):
            wh[t, :, D * j : D * j + D] = whf[D * j : D * j + D].astype(BF)
        vec[t] = vecf[...].astype(BF)
    total = jnp.zeros((1, D), F32)
    for i in range(n):
        tail = slots[0, i, rows - 16 : rows].astype(F32)
        total = total + tail[15:16]
    weight_sum = jnp.sum(jnp.where(lane < 3, total, 0.0), axis=1, keepdims=True)
    rw[...] = jnp.broadcast_to(imp_ref[:, pl.ds(mine, half)].astype(F32) / weight_sum, (8, half))


def gather(plan, p128, ints, imp):
    n, rows = plan.n, plan.slot
    half = ints.shape[1] // 2
    vm = pl.BlockSpec(memory_space=pltpu.VMEM)
    height = p128.shape[0]
    tall = max(2 * rows, height + 40) + 80
    copies = 1 + (n // 4 - 1) + 2 * (n // 4) + 2 * (n // 4) + n
    return pl.pallas_call(
        functools.partial(gather_kernel, plan),
        out_shape=(
            jax.ShapeDtypeStruct((2, A_ROWS, D), BF),
            jax.ShapeDtypeStruct((2, D, HPAD), BF),
            jax.ShapeDtypeStruct((2, 128, D), BF),
            jax.ShapeDtypeStruct((2, 8, half), jnp.int32),
            jax.ShapeDtypeStruct((8, half), F32),
        ),
        in_specs=[vm] * 3,
        out_specs=(vm,) * 5,
        scratch_shapes=[
            pltpu.VMEM((2, n, rows, D), BF),
            pltpu.VMEM((tall, 128), F32),
            pltpu.VMEM((height + 128, 128), F32),
            pltpu.VMEM((height + 40, 128), F32),
            pltpu.VMEM((2, rows, 128), F32),
            pltpu.VMEM((HPAD, D), F32),
            pltpu.VMEM((128, D), F32),
            pltpu.SemaphoreType.DMA((copies,)),
            pltpu.SemaphoreType.DMA((copies,)),
        ],
        compiler_params=pltpu.CompilerParams(
            collective_id=0, has_side_effects=True, vmem_limit_bytes=48 * 1024 * 1024
        ),
    )(p128, ints, imp)


def chunks(height):
    step = max(c for c in range(8, 113, 8) if height % c == 0)
    return [(lo, lo + step) for lo in range(0, height, step)]


def lay_flat(plan, me, slot128, flat, rolled):
    height = rolled.shape[0] - 40
    start = me * plan.length
    shift = start % 128
    first = start // 128
    base = plan.at(plan.a_base, me)
    row = lax.broadcasted_iota(jnp.int32, (height + 8, 128), 0)
    flat[...] = jnp.zeros(flat.shape, F32)

    @pl.when(plan.at(plan.a_rows, me) > 0)
    def _():
        rows = slot128[pl.ds(first - 2 * base, height + 8)]
        flat[16 : 24 + height] = jnp.where(row + first < 2 * A_ROWS, rows, 0.0)

    v_start = (A_ROWS * D + D * HEADS) // 128
    v_rows, v_off, v_first = (plan.at(t, me) for t in (plan.v_rows, plan.v_off, plan.v_first))
    tall_v = min(height, -(-2 * max(plan.v_rows) // 8) * 8)

    @pl.when(v_rows > 0)
    def _():
        inside = plan.at([max(0, v_start - i * plan.length // 128) for i in range(plan.n)], me)
        source = 2 * v_off + first + inside - v_start - 2 * v_first
        to = pl.ds(16 + inside, tall_v)
        flat[to] = flat[to] + slot128[pl.ds(source, tall_v)]

    h_first, h_rows, h_off = (plan.at(t, me) for t in (plan.h_first, plan.h_rows, plan.h_off))

    @pl.when(h_rows > 0)
    def _():
        tall_h = plan.image
        source = slot128.at[pl.ds(pl.multiple_of(2 * h_off, 8), 10 * plan.heads + 6)]
        it = lax.broadcasted_iota(jnp.int32, (16, 128), 0)
        lane = lax.broadcasted_iota(jnp.int32, (16, 128), 1)
        rolled[0 : tall_h + 8] = jnp.zeros((tall_h + 8, 128), F32)
        for k in range(plan.heads):
            row, turn = HEADS * k // 128, HEADS * k % 128
            kept = (it * 128 + lane < HEADS) & (k < h_rows)
            value = pltpu.roll(jnp.where(kept, source[10 * k : 10 * k + 16], 0.0), turn, 1)
            above = jnp.concatenate([jnp.zeros((8, 128), F32), value], 0)[7:23]
            rolled[row : row + 16] = rolled[row : row + 16] + jnp.where(lane >= turn, value, above)
        begin = A_ROWS * D + HEADS * h_first - 128 * first + 128 * 16
        turn = begin % 128
        slot128[0:8] = jnp.zeros((8, 128), F32)
        slot128[8 : 8 + tall_h] = pltpu.roll(rolled[0:tall_h], turn, 1)
        lane = lax.broadcasted_iota(jnp.int32, (tall_h, 128), 1)
        moved = jnp.where(lane >= turn, slot128[8 : 8 + tall_h], slot128[7 : 7 + tall_h])
        to = pl.ds(begin // 128, tall_h)
        flat[to] = flat[to] + moved

    rolled[0 : height + 8] = pltpu.roll(flat[16 : 24 + height], (128 - shift) % 128, 1)
    for lo, hi in chunks(height):
        lane = lax.broadcasted_iota(jnp.int32, (hi - lo, 128), 1)
        flat[lo:hi] = jnp.where(lane < 128 - shift, rolled[lo:hi], rolled[lo + 1 : hi + 1])


def pack_slots(plan, core, gw, gh, gv, rgw, rgh, rgv, slots, sums, vsum, scratch):
    total = gv[core].astype(F32) + rgv[...]
    for kind in range(3):
        vsum[kind * (BLOCKS + 1) : (kind + 1) * (BLOCKS + 1)] = total[kind, 0 : BLOCKS + 1]
    sums[...] = gh[core].astype(F32) + rgh[...].astype(F32)
    for i in range(plan.n):
        base, rows = plan.a_base[i], plan.a_rows[i]
        h_rows, h_off, h_first = plan.h_rows[i], plan.h_off[i], plan.h_first[i]
        v_rows, v_off, v_first = plan.v_rows[i], plan.v_off[i], plan.v_first[i]
        slots[i, rows : plan.slot] = jnp.zeros((plan.slot - rows, D), BF)
        if rows:
            added = gw[core, base : base + rows].astype(F32) + rgw[base : base + rows].astype(F32)
            slots[i, 0:rows] = added.astype(BF)
        if h_rows or v_rows:
            scratch[...] = jnp.zeros(scratch.shape, F32)
            for half in range(2):
                for j in range(5 if h_rows else 0):
                    cols = slice(D * j + 128 * half, D * j + 128 * half + 128)
                    scratch[half, pl.ds(h_off + j, h_rows, stride=5)] = sums[h_first : h_first + h_rows, cols]
                if v_rows:
                    scratch[half, v_off : v_off + v_rows] = vsum[v_first : v_first + v_rows, 128 * half : 128 * half + 128]
            whole = jnp.concatenate([scratch[0], scratch[1]], 1)
            slots[i, rows : plan.slot] = whole[rows:].astype(BF)


def segment_bounds():
    first = [0] + [(CAT + j * D) * D for j in range(BLOCKS + 1)]
    return list(zip(first, first[1:] + [A_ROWS * D + D * HEADS]))


class Rows:
    def __init__(self, ref):
        self.ref, self.height = ref, ref.shape[0]

    def chunks(self):
        return chunks(self.height)

    def get(self, lo, hi):
        return self.ref[lo:hi]

    def put(self, lo, hi, value):
        self.ref[lo:hi] = value


class Flat:
    def __init__(self, ref, buffer):
        self.ref, self.buffer, self.length = ref, buffer, ref.shape[1]
        self.whole = self.length // 1024 * 8
        self.height = -(-self.length // 1024) * 8

    def chunks(self):
        step = next(s for s in range(64, 0, -8) if self.whole % s == 0)
        return [(lo, lo + step) for lo in range(0, self.whole, step)] + [(self.whole, self.height)]

    def ends(self):
        rows = (self.length - 128 * self.whole) // 128
        return rows, self.length % 128, 128 * self.whole, 128 * (self.whole + rows)

    def get(self, lo, hi):
        if hi <= self.whole:
            return self.ref[0:1, 128 * lo : 128 * hi].reshape(hi - lo, 128)
        rows, lanes, first, last = self.ends()
        self.buffer[...] = jnp.zeros((8, 128), F32)
        if rows:
            self.buffer[0:rows] = self.ref[0:1, first:last].reshape(rows, 128)
        if lanes:
            self.buffer[rows : rows + 1, 0:lanes] = self.ref[0:1, last : self.length]
        return self.buffer[...]

    def put(self, lo, hi, value):
        if hi <= self.whole:
            self.ref[0:1, 128 * lo : 128 * hi] = value.reshape(1, 128 * (hi - lo))
            return
        rows, lanes, first, last = self.ends()
        if rows:
            self.ref[0:1, first:last] = value[0:rows].reshape(1, 128 * rows)
        if lanes:
            self.ref[0:1, last : self.length] = value[rows : rows + 1, 0:lanes]


def update_shard(plan, me, p_ref, m_ref, v_ref, outs, flat, squares, sq_in, push, to_plane, to_z):
    first_out, second_out, new_out, norm_out = outs
    height = p_ref.height
    start = me * plan.length
    correction = 1.0 - 0.5**STEP
    bounds = segment_bounds()

    def place(lo, hi):
        shape = (hi - lo, 128)
        return 128 * lo + 128 * lax.broadcasted_iota(jnp.int32, shape, 0) + lax.broadcasted_iota(jnp.int32, shape, 1)

    for lo, hi in p_ref.chunks():
        spot = place(lo, hi)
        grad = jnp.where(spot < plan.length, flat[lo:hi], 0.0)
        first_new = 0.5 * m_ref.get(lo, hi) + 0.5 * grad
        second_new = 0.5 * v_ref.get(lo, hi) + 0.5 * grad * grad
        first_out.put(lo, hi, first_new)
        second_out.put(lo, hi, second_new)
        decay = jnp.where(spot < bounds[-1][1] - start, 0.01 * p_ref.get(lo, hi), 0.0)
        update = first_new / correction / (jnp.sqrt(second_new / correction) + 1e-06) + decay
        flat[lo:hi] = jnp.where(spot < plan.length, update, 0.0)
        new_out.put(lo, hi, p_ref.get(lo, hi) - 0.5 * update)
    squares[...] = jnp.zeros(squares.shape, F32)

    def each_segment(body):
        for j, (first, last) in enumerate(bounds):
            pl.when((first < start + plan.length) & (last > start))(lambda j=j, first=first, last=last: body(j, first, last))

    def square_sums(j, first, last):
        weight, change = jnp.zeros((8, 128), F32), jnp.zeros((8, 128), F32)
        for lo, hi in p_ref.chunks():
            spot = place(lo, hi)
            inside = (spot >= first - start) & (spot < last - start)
            p, u = jnp.where(inside, p_ref.get(lo, hi), 0.0), jnp.where(inside, flat[lo:hi], 0.0)
            weight = weight + jnp.sum((p * p).reshape(-1, 8, 128), axis=0)
            change = change + jnp.sum((u * u).reshape(-1, 8, 128), axis=0)
        squares[0, j : j + 1] = jnp.sum(weight, axis=0, keepdims=True)
        squares[0, 16 + j : 17 + j] = jnp.sum(change, axis=0, keepdims=True)

    each_segment(square_sums)
    total = squares[0]
    for hop, targets in enumerate((to_plane, to_z)):
        lands = range(3) if hop == 0 else range(3, 3 + len(to_z))
        for c in [push(squares.at[hop], sq_in.at[k], to) for k, to in zip(lands, targets)]:
            c.wait_recv()
        for k in lands:
            total = total + sq_in[k]
        squares[hop + 1] = total
    norm = jnp.sqrt(jnp.sum(total, axis=1, keepdims=True))
    squares[3] = jnp.broadcast_to(norm, (32, 128))
    line = jnp.sqrt(jnp.sum(jnp.concatenate([total, jnp.zeros((96, 128), F32)], 0).T, axis=0, keepdims=True))
    norm_out[0:1] = line[:, 0:MATS]
    norm_out[1:2] = pltpu.roll(line, 112, 1)[:, 0:MATS]

    def scaled(j, first, last):
        ratio = squares[3, j : j + 1] / squares[3, 16 + j : 17 + j]
        for lo, hi in p_ref.chunks():
            spot = place(lo, hi)
            inside = (spot >= first - start) & (spot < last - start)
            new_out.put(lo, hi, jnp.where(inside, p_ref.get(lo, hi) - 0.5 * ratio * flat[lo:hi], new_out.get(lo, hi)))

    each_segment(scaled)


def reduce_kernel(
    plan, gw, gh, gv, st, ig, p_ref, m_ref, v_ref,
    st_out, ig_out, first_out, second_out, new_out, norm_out,
    rgw, rgh, rgv, slots, sums, vsum, scratch, in_d, in_x, in_y, in_z, slot128, flat, rolled, squares, sq_in,
    send, recv, local,
):
    n, rows = plan.n, plan.slot
    depth, cut = n // 4, plan.slot // 2
    core, me, near_x, near_y = neighbours(n)
    near_xy = near_x + near_y - me
    barrier = greet(core, me, near_x, near_y, n)
    pl.semaphore_wait(barrier, depth + 3)
    half = st.shape[1]
    number = iter(range(1 << 20))
    started = []

    def copy(src, dst, to):
        slot = next(number)
        c = pltpu.make_async_remote_copy(
            src_ref=src, dst_ref=dst, send_sem=send.at[slot], recv_sem=recv.at[slot], device_id=to, device_id_type=MESH
        )
        c.start()
        started.append(c)
        return c

    def column(index, k):
        return (index + n - 4 * k) % n

    sibling = at(1 - core, me)
    early = [
        copy(gw.at[1 - core], rgw, sibling),
        copy(gh.at[1 - core], rgh, sibling),
        copy(gv.at[1 - core], rgv, sibling),
    ]
    mine = pl.ds(pl.multiple_of(core * half, half), half)
    late = [
        copy(st.at[1 - core], st_out.at[mine], sibling),
        copy(ig.at[1 - core], ig_out.at[mine], sibling),
    ]
    stay = [
        pltpu.make_async_copy(st.at[core], st_out.at[mine], local.at[0]),
        pltpu.make_async_copy(ig.at[core], ig_out.at[mine], local.at[1]),
    ]
    for c in stay:
        c.start()
    for c in early:
        c.wait_recv()
    pack_slots(plan, core, gw, gh, gv, rgw, rgh, rgv, slots, sums, vsum, scratch)
    order = list(range(1, depth)) + [0]
    to_x, to_y = at(core, near_x), at(core, near_y)
    halves = {}
    for k in order:
        diagonal = column(near_xy, k)
        halves[k] = (
            copy(slots.at[diagonal, pl.ds(0, cut)], in_d.at[k, pl.ds(0, cut)], to_y),
            copy(slots.at[diagonal, pl.ds(cut, rows - cut)], in_d.at[k, pl.ds(cut, rows - cut)], to_x),
        )
    fulls = {}
    for k in order:
        ox, oy = column(near_x, k), column(near_y, k)
        halves[k][0].wait_recv()
        slots[ox, 0:cut] = (slots[ox, 0:cut].astype(F32) + in_d[k, 0:cut].astype(F32)).astype(BF)
        first = copy(slots.at[ox], in_x.at[k], to_x)
        halves[k][1].wait_recv()
        slots[oy, cut:rows] = (slots[oy, cut:rows].astype(F32) + in_d[k, cut:rows].astype(F32)).astype(BF)
        fulls[k] = (first, copy(slots.at[oy], in_y.at[k], to_y))
    along = {}
    for k in order:
        own = column(me, k)
        for c in fulls[k]:
            c.wait_recv()
        if k:
            total = slots[own].astype(F32) + in_x[k].astype(F32) + in_y[k].astype(F32)
            slots[own] = total.astype(BF)
            along[k] = copy(slots.at[own], in_z.at[k], at(core, own))
    for c in along.values():
        c.wait_recv()
    total = slots[me].astype(F32) + in_x[0].astype(F32) + in_y[0].astype(F32)
    for k in along:
        total = total + in_z[k].astype(F32)
    slot128[...] = jnp.zeros(slot128.shape, F32)
    slot128[pl.ds(0, rows, stride=2)] = total[:, 0:128]
    slot128[pl.ds(1, rows, stride=2)] = total[:, 128:D]
    lay_flat(plan, me, slot128, flat, rolled)

    to_z = [at(core, column(me, k)) for k in range(1, depth)]
    outs = (Rows(first_out), Rows(second_out), Rows(new_out), norm_out)
    to_plane = [to_x, to_y, at(core, near_xy)]
    update_shard(plan, me, Rows(p_ref), Rows(m_ref), Rows(v_ref), outs, flat, squares, sq_in, copy, to_plane, to_z)
    for c in late:
        c.wait_recv()
    for c in stay:
        c.wait()
    for c in started:
        c.wait_send()


def reduce_and_update(plan, gw, gh, gv, st, ig, p128, m128, v128):
    n, rows = plan.n, plan.slot
    depth = n // 4
    half = st.shape[1]
    height = p128.shape[0]
    vm = pl.BlockSpec(memory_space=pltpu.VMEM)
    hbm = pl.BlockSpec(memory_space=pl.ANY)
    copies = 5 + 2 * depth + 2 * depth + (depth - 1) + (depth - 1) + 3
    flat32 = jax.ShapeDtypeStruct((height, 128), F32)
    return pl.pallas_call(
        functools.partial(reduce_kernel, plan),
        out_shape=(
            jax.ShapeDtypeStruct((2 * half, D), BF),
            jax.ShapeDtypeStruct((2 * half, D), F32),
            flat32,
            flat32,
            flat32,
            jax.ShapeDtypeStruct((2, MATS), F32),
        ),
        in_specs=[vm] * 3 + [hbm] * 2 + [vm] * 3,
        out_specs=(hbm, hbm, vm, vm, vm, vm),
        scratch_shapes=[
            pltpu.VMEM((A_ROWS, D), BF),
            pltpu.VMEM((D, HPAD), BF),
            pltpu.VMEM(gv.shape[1:], F32),
            pltpu.VMEM((n, rows, D), BF),
            pltpu.VMEM((D, HPAD), F32),
            pltpu.VMEM((40, D), F32),
            pltpu.VMEM((2, rows, 128), F32),
            pltpu.VMEM((depth, rows, D), BF),
            pltpu.VMEM((depth, rows, D), BF),
            pltpu.VMEM((depth, rows, D), BF),
            pltpu.VMEM((depth, rows, D), BF),
            pltpu.VMEM((max(2 * rows, height + 48) + 80, 128), F32),
            pltpu.VMEM((height + 128, 128), F32),
            pltpu.VMEM((height + 40, 128), F32),
            pltpu.VMEM((4, 32, 128), F32),
            pltpu.VMEM((2 + depth, 32, 128), F32),
            pltpu.SemaphoreType.DMA((copies,)),
            pltpu.SemaphoreType.DMA((copies,)),
            pltpu.SemaphoreType.DMA((2,)),
        ],
        compiler_params=pltpu.CompilerParams(
            collective_id=1, has_side_effects=True, vmem_limit_bytes=48 * 1024 * 1024
        ),
    )(gw, gh, gv, st, ig, p128, m128, v128)


class Copies:
    def __init__(self, send, recv):
        self.send, self.recv, self.made, self.sent = send, recv, [], set()

    def add(self, src, dst, to, recv_slot=None, only=None):
        self.made.append((src, dst, to, recv_slot, only))
        return len(self.made) - 1

    def get(self, number):
        src, dst, to, recv_slot, _ = self.made[number]
        return pltpu.make_async_remote_copy(
            src_ref=src(), dst_ref=dst(), send_sem=self.send.at[number],
            recv_sem=self.recv.at[number] if recv_slot is None else recv_slot(),
            device_id=to(), device_id_type=MESH,
        )

    def start(self, *numbers):
        for number in numbers:
            self.get(number).start()

    def arrive(self, *numbers):
        for number in numbers:
            self.get(number).wait_recv()

    def leave(self, *numbers):
        for number in numbers:
            only = self.made[number][4]
            if number not in self.sent and only is None:
                self.get(number).wait_send()
            elif number not in self.sent:
                pl.when(only())(lambda number=number: self.get(number).wait_send())
            self.sent.add(number)


def fused_fits(plan):
    depth, half = plan.n // 4, plan.slot // 2
    plain = [b + plan.slot <= A_ROWS for b, h, v in zip(plan.a_base, plan.h_rows, plan.v_rows) if not (h or v)]
    vectors = [rows for rows in plan.v_rows if rows]
    return (
        all(plain)
        and vectors == [3 * (BLOCKS + 1)]
        and plan.n % 4 == 0
        and half >= 32
        and 4 * half <= HPAD
        and 2 * depth * plan.slot <= (BLOCKS + 1) * D
        and depth == 4
        and max(plan.a_rows) <= plan.slot
    )


def train_kernel(
    plan, x_ref, codes_ref, targets_ref, visits_ref, imp_ref, p_ref, m_ref, v_ref,
    st_out, ig_out, first_out, second_out, new_out, norm_out,
    w, wh, vec, both, away, rw, eye, wt, wht, vt, gsb, xt, mix, xh, gp, rstd, mean, stream, ex, br, dm, acc, lg, dl,
    gw, gh, gv, packed, st_stage, slot128, flat, rolled, vsum, vacc, vin, owned, squares, sq_in, tail,
    send, recv, z_recv, own_recv, local, ready,
):
    n, rows = plan.n, plan.slot
    depth, hrows = n // 4, plan.slot // 2
    cut = hrows // 32 * 16
    core, me, near_x, near_y = neighbours(n)
    near_xy = near_x + near_y - me
    width = both.shape[2]
    params_in, first_new, second_new, new = (Flat(ref, tail) for ref in (p_ref, first_out, second_out, new_out))
    moments = [
        pltpu.make_async_copy(src, dst, local.at[3 + i])
        for i, (src, dst) in enumerate(((m_ref, first_out), (v_ref, second_out)))
    ]
    z_me, j_me = me // 4, me % 4
    copies = Copies(send, recv)
    scratch = [slot128.at[0:rows], slot128.at[rows : 2 * rows]]
    barrier = greet(core, me, near_x, near_y, n, True)
    mine = pl.multiple_of(core * width, width)
    theirs = pl.multiple_of((1 - core) * width, width)
    x_copy = pltpu.make_async_copy(x_ref.at[pl.ds(mine, width)], st_stage.at[0], local.at[0])
    x_copy.start()
    for c in moments:
        c.start()
    for to, half in ((both.at[core], mine), (away, theirs)):
        cols = pl.ds(half, width)
        to[0:1] = codes_ref[:, cols]
        to[1:2] = targets_ref[0, :, cols]
        to[2:6] = visits_ref[:, cols]
        to[6:7] = targets_ref[1, :, cols]
        to[7:8] = targets_ref[2, :, cols]
    height = params_in.height
    for lo, hi in params_in.chunks():
        slot128[lo:hi] = params_in.get(lo, hi)
    place_shard(plan, me, slot128.at[0:height], slot128, flat, rolled)

    spare = (BLOCKS + 1) * D

    def slot_part(t, i, lo, count):
        row = pl.multiple_of(spare + rows * (t * depth + i // 4) + lo, 16)
        return xh.at[pl.ds(row, count), pl.ds(pl.multiple_of((i % 4) * D, D), D)]

    def column(index, k):
        return (index + n - 4 * k) % n

    def sibling():
        return at(1 - core, me)

    def same(make, to):
        return copies.add(make, make, to)

    low = core * hrows
    other_low = (1 - core) * hrows
    order = [0] + sorted(range(1, depth), key=lambda k: (min(k, depth - k), k))
    to_x, to_y, to_d = (lambda: at(core, near_x)), (lambda: at(core, near_y)), (lambda: at(core, near_xy))
    swap_ints = copies.add(lambda: away, lambda: both.at[core], sibling)

    def arrival(t, number):
        return own_recv.at[t * (depth + 2) + number]

    own_targets = [(lambda: near_x), (lambda: near_y)] + [lambda k=k: (me + 4 * k) % n for k in order[1:]]
    own_sends = [copies.add(lambda: slot_part(core, me, 0, rows), lambda: slot_part(core, me, 0, rows), sibling, lambda: arrival(core, 0))]
    for number, target in enumerate(own_targets, 1):
        for h in range(2):
            make = lambda h=h: slot_part(core, me, h * hrows, hrows)
            own_sends.append(
                copies.add(make, make, lambda h=h, target=target: at(h, target()), lambda number=number: arrival(core, number))
            )
    own_sends = own_sends[3 + 2 :] + own_sends[1:5] + own_sends[:1]

    def own_arrive(t, number, make):
        pltpu.make_async_remote_copy(
            src_ref=make(), dst_ref=make(), send_sem=send.at[0], recv_sem=arrival(t, number), device_id=sibling(), device_id_type=MESH
        ).wait_recv()

    gathers = []
    for t in range(2):
        g = {}
        for k in order:
            if k:
                g["x", k] = same(lambda t=t, k=k: slot_part(t, column(me, k), low, hrows), to_x)
                g["y", k] = same(lambda t=t, k=k: slot_part(t, column(me, k), low, hrows), to_y)
            g["d", k] = (
                same(lambda t=t, k=k: slot_part(t, column(near_x, k), low, cut), to_y),
                same(lambda t=t, k=k: slot_part(t, column(near_y, k), low + cut, hrows - cut), to_x),
            )
            g["s", k] = [
                same(lambda t=t, k=k, index=index: slot_part(t, column(index, k), low, hrows), sibling) if index is not me or k else None
                for index in (me, near_x, near_y, near_xy)
            ]
        gathers.append(g)

    def gather_0(t):
        pl.when(core == t)(lambda: copies.start(*own_sends))

    def gather_1(t):
        g = gathers[t]
        for number, k in enumerate(order[1:], 3):
            own_arrive(t, number, lambda: slot_part(t, me, low, hrows))
            copies.start(g["x", k], g["y", k], g["s", k][0])

    def gather_2(t):
        g = gathers[t]
        for k in order:
            if k:
                copies.arrive(g["x", k])
            else:
                own_arrive(t, 1, lambda: slot_part(t, me, low, hrows))
            copies.start(g["d", k][0], g["s", k][1])
            if k:
                copies.arrive(g["y", k])
            else:
                own_arrive(t, 2, lambda: slot_part(t, me, low, hrows))
            copies.start(g["d", k][1], g["s", k][2])

    def gather_3(t):
        g = gathers[t]
        for k in order:
            copies.arrive(*g["d", k])
            copies.start(g["s", k][3])

    def gather_4(t):
        g = gathers[t]
        pl.when(core != t)(lambda: own_arrive(t, 0, lambda: slot_part(t, me, 0, rows)))
        for k in order:
            copies.arrive(*(c for c in g["s", k] if c is not None))

    def unpack(t):
        lg[4 * D : 5 * D, 128:D] = jnp.zeros((D, 128), F32)
        vsum[...] = jnp.zeros(vsum.shape, F32)
        for i in range(n):
            row, lane = spare + rows * (t * depth + i // 4), (i % 4) * D
            unpack_rows(plan, i, xh[row : row + rows, lane : lane + D], w.at[t], lg, vsum, scratch)
        for j in range(5):
            wh[t, :, D * j : D * j + D] = lg[D * j : D * j + D].astype(BF)
        vec[t] = vsum[...].astype(BF)

    total = jnp.sum(imp_ref[...].astype(F32), axis=1, keepdims=True)
    lane_d = lax.broadcasted_iota(jnp.int32, (1, D), 1)
    hi, mid, lo = split3(total)
    left = slot128[pl.ds(0, rows, stride=2)]
    right = slot128[pl.ds(1, rows, stride=2)]
    own = jnp.concatenate([left, right], 1)
    last = jnp.where(lane_d == 0, hi, jnp.where(lane_d == 1, mid, jnp.where(lane_d == 2, lo, 0.0)))
    last_row = lax.broadcasted_iota(jnp.int32, (rows, D), 0) == rows - 1
    slot_part(core, me, 0, rows)[...] = jnp.where(last_row, last, own).astype(BF)
    pl.semaphore_wait(barrier, depth + 3 + 2 + depth - 1)
    gather_0(0)
    copies.start(swap_ints)
    eye[...] = identity(D)
    x_copy.wait()
    for c in range(0, width, CB):
        xt[0, 0:D, c : c + CB] = nt(eye[...], st_stage[0, c : c + CB, :]).astype(BF)
    gather_1(0)
    gather_0(1)
    gather_2(0)
    gather_3(0)
    copies.arrive(swap_ints)
    gather_4(0)
    unpack(0)
    total = jnp.zeros((1, D), F32)
    for i in range(n):
        row, lane = spare + rows * (i // 4), (i % 4) * D
        total = total + xh[row + rows - 16 : row + rows, lane : lane + D].astype(F32)[15:16]
    weight_sum = jnp.sum(jnp.where(lane_d < 3, total, 0.0), axis=1, keepdims=True)
    rw[...] = jnp.broadcast_to(imp_ref[:, pl.ds(mine, width)].astype(F32) / weight_sum, (8, width))

    fwd = (eye, w, wh, vec, wt, vt, gsb, xt, mix, xh, gp, rstd, stream, mean, both, width)

    def during_forward(k):
        pl.when(k == 1)(lambda: gather_1(1))
        pl.when(k == 4)(lambda: gather_2(1))
        pl.when(k == 7)(lambda: gather_3(1))

    def emit_states(t):
        for c in range(0, width, CB):
            st_stage[t, c : c + CB, :] = nt(eye[...], xt[t + 1, 0:D, c : c + CB]).astype(BF)

    forward_tower(0, fwd, during_forward)
    gather_4(1)
    copies.leave(*range(len(copies.made)))
    unpack(1)
    forward_tower(1, fwd, None)
    emit_states(0)
    emit_states(1)
    out_rows = pl.ds(mine, width)
    st_copy = copies.add(lambda: st_stage.at[1 - core], lambda: st_out.at[out_rows], sibling)
    copies.start(st_copy)
    st_stay = pltpu.make_async_copy(st_stage.at[core], st_out.at[out_rows], local.at[1])
    st_stay.start()

    packed_of = [i for i in range(n) if plan.h_rows[i] or plan.v_rows[i]]
    owner = plan.v_rows.index(3 * (BLOCKS + 1))

    early = (2, 3)

    def piece(t, zz, b, lo, count):
        if t == 1 and zz in early:
            arena, first, q = dl, 0, 7 * early.index(zz) + b
        elif t == 1:
            arena, first, q = mix, BLOCKS * (D + 16), 7 * zz + b
        else:
            arena, first, q = xh, spare, 7 * zz + b
        row = pl.multiple_of(first + hrows * (q // 4) + lo, 16)
        return arena.at[pl.ds(row, count), pl.ds(pl.multiple_of((q % 4) * D, D), D)]

    def block(t, zz, b):
        return piece(t, zz, b, 0, hrows)

    def z_in(h, k):
        return st_stage.at[0, pl.ds(pl.multiple_of(hrows * (h * (depth - 1) + k - 1), 16), hrows)]

    def z_out(t, zz):
        if t == 1 and zz in early:
            return st_stage.at[1, pl.ds(hrows * early.index(zz), hrows)]
        return block(t, zz, j_me)

    def slot_half(t, i, lo):
        if i in packed_of:
            return packed.at[packed_of.index(i), pl.ds(pl.multiple_of(lo, 16), hrows)]
        return gw.at[t, pl.ds(pl.multiple_of(plan.a_base[i] + lo, 16), hrows)]

    j_x, j_y, j_d = near_x % 4, near_y % 4, near_xy % 4
    direct = ((0, 0),)
    jobs = {}
    for t in range(2):
        for zz in range(depth):
            job = {}
            job["swap"] = [
                copies.add(lambda t=t, i=4 * zz + j: slot_half(t, i, other_low), lambda t=t, zz=zz, j=j: block(t, zz, j), sibling)
                for j in range(4)
            ]
            if (t, zz) in direct:
                job["d"] = [copies.add(lambda t=t, zz=zz: block(t, zz, j_d), lambda t=t, zz=zz: block(t, zz, 4), to_d)]
            else:
                job["d"] = [
                    copies.add(
                        lambda t=t, zz=zz, lo=lo, count=count: piece(t, zz, j_d, lo, count),
                        lambda t=t, zz=zz, lo=lo, count=count: piece(t, zz, 4, lo, count),
                        to,
                    )
                    for to, lo, count in ((to_y, 0, cut), (to_x, cut, hrows - cut))
                ]
            job["x"] = copies.add(lambda t=t, zz=zz: block(t, zz, j_x), lambda t=t, zz=zz: block(t, zz, 5), to_x)
            job["y"] = copies.add(lambda t=t, zz=zz: block(t, zz, j_y), lambda t=t, zz=zz: block(t, zz, 6), to_y)
            job["z"] = copies.add(
                lambda t=t, zz=zz: z_out(t, zz),
                lambda zz=zz: z_in(core, (zz + depth - z_me) % depth),
                lambda t=t, zz=zz: at(t, 4 * zz + j_me),
                lambda zz=zz: z_recv.at[core * depth + (zz + depth - z_me) % depth],
                lambda zz=zz: z_me != zz,
            )
            jobs[t, zz] = job

    def pack(t, planes):
        wanted = [i for i in packed_of if i // 4 in planes]
        for i in wanted:
            a_rows, h_rows, h_off, h_first = plan.a_rows[i], plan.h_rows[i], plan.h_off[i], plan.h_first[i]
            to = packed.at[packed_of.index(i)]
            for part in scratch:
                part[...] = jnp.zeros(part.shape, F32)
            lo16, hi16 = h_first // 16 * 16, -(-(h_first + h_rows) // 16) * 16
            for half in range(2):
                for j in range(5 if h_rows else 0):
                    cols = slice(D * j + 128 * half, D * j + 128 * half + 128)
                    value = gh[t, lo16:hi16, cols].astype(F32)[h_first - lo16 : h_first - lo16 + h_rows]
                    scratch[half][pl.ds(h_off + j, h_rows, stride=5)] = value
            whole = jnp.concatenate([scratch[0][...], scratch[1][...]], 1)
            to[a_rows:rows] = whole[a_rows:].astype(BF)
            if a_rows:
                to[0:a_rows] = gw[t, plan.a_base[i] : plan.a_base[i] + a_rows]

    def plus(*refs):
        value = refs[0][...].astype(F32)
        for ref in refs[1:]:
            value = value + ref[...].astype(F32)
        return value

    def sum_0(t, zz):
        copies.start(*jobs[t, zz]["swap"])

    def sum_1(t, zz):
        job = jobs[t, zz]
        for j in range(4):
            copies.arrive(job["swap"][j])
            target = block(t, zz, j)
            target[...] = plus(slot_half(t, 4 * zz + j, low), target).astype(BF)
        copies.start(*job["d"])
        if (t, zz) in direct:
            copies.start(job["x"], job["y"])

    def sum_2(t, zz):
        job = jobs[t, zz]
        for side, copy, j, lo, count in (("x", job["d"][0], j_x, 0, cut), ("y", job["d"][1], j_y, cut, hrows - cut)):
            copies.arrive(copy)
            target = piece(t, zz, j, lo, count)
            target[...] = plus(target, piece(t, zz, 4, lo, count)).astype(BF)
            copies.start(job[side])

    def sum_3(t, zz):
        job = jobs[t, zz]
        copies.arrive(job["x"], job["y"])
        value = plus(block(t, zz, j_me), block(t, zz, 5), block(t, zz, 6))
        if (t, zz) in direct:
            copies.arrive(*job["d"])
            value = value + block(t, zz, 4)[...].astype(F32)

        @pl.when(z_me != zz)
        def _():
            z_out(t, zz)[...] = value.astype(BF)
            copies.start(job["z"])

        @pl.when((z_me == zz) & (core == t))
        def _():
            final(core)[...] = value

        @pl.when((z_me == zz) & (core != t))
        def _():
            outgo[...] = value
            copies.start(hand_over)

    def sum_4():
        copies.arrive(hand_over)
        for h in range(2):
            for k in range(1, depth):
                src = z_in(h, k)
                pltpu.make_async_remote_copy(
                    src_ref=src, dst_ref=src, send_sem=send.at[0], recv_sem=z_recv.at[h * depth + k], device_id=sibling(), device_id_type=MESH
                ).wait_recv()
                final(h)[...] = final(h)[...] + src[...].astype(F32)

    def final(h):
        return owned.at[h]

    outgo = owned.at[2]

    def vector_step(step):
        sources = [gv.at[1 - core], vacc.at[0], vacc.at[1]]
        along = [lambda k=k: at(core, (me + 4 * k) % n) for k in range(1, depth)]
        targets = [[sibling], [to_x, to_y, to_d], along]
        if step:
            base = gv[core] if step == 1 else vacc[step - 2]
            for number, k in vector_copies[-1]:
                copies.arrive(number)
                base = base + vin[k]
            vacc[step - 1] = base
        if step < 3:
            started = []
            for k, to in enumerate(targets[step], (0, 1, 4)[step]):
                number = copies.add(lambda step=step: sources[step], lambda k=k: vin.at[k], to)
                copies.start(number)
                started.append((number, k))
            vector_copies.append(started)

    vector_copies = []
    hand_over = copies.add(lambda: outgo, lambda: final(core), sibling)
    peers = [(1 - core, me), (core, near_x), (core, near_y), (core, near_xy)] + [(1 - core, (me + 4 * k) % n) for k in range(1, depth)] + [(core, (me + 4 * k) % n) for k in range(1, depth)]

    bwd = (eye, w, wh, vec, wht, vt, gsb, xt, mix, xh, gp, rstd, stream, ex, br, dm, acc, lg, dl, both, rw, gw, gh, gv, dm, width)
    ig_copies = [copies.add(lambda: dm, lambda: ig_out.at[out_rows], sibling, None, lambda t=t: core != t) for t in range(2)]

    def ig_local():
        return pltpu.make_async_copy(dm, ig_out.at[out_rows], local.at[2])

    def emit_inputs(t):
        pl.when(core == t)(lambda: ig_local().start())
        pl.when(core != t)(lambda: copies.start(ig_copies[t]))

    def free_inputs(t):
        pl.when(core == t)(lambda: ig_local().wait())
        pl.when(core != t)(lambda: copies.get(ig_copies[t]).wait_send())

    def signal_ready(which):
        for to_core, to_index in peers:
            pl.semaphore_signal(ready.at[which], inc=1, device_id=at(to_core, to_index), device_id_type=MESH)

    def wait_ready(which):
        pl.semaphore_wait(ready.at[which], len(peers))

    def schedule(i, steps):
        for step in sorted({s[0] for s in steps}):

            def run(step=step):
                for s, f, *args in steps:
                    if s == step:
                        f(*args)

            pl.when(i == step)(run)

    def after_head_1():
        copies.leave(st_copy)
        st_stay.wait()
        signal_ready(0)

    def during_backward_1(i):
        schedule(i, [
            (1, wait_ready, 0), (1, pack, 1, (3,)), (1, sum_0, 1, 3),
            (2, sum_1, 1, 3),
            (4, pack, 1, (2,)), (4, sum_0, 1, 2), (4, sum_2, 1, 3),
            (5, sum_1, 1, 2),
            (7, sum_2, 1, 2), (7, sum_3, 1, 3),
        ])

    ex[...] = jnp.zeros_like(ex)
    backward_tower(1, bwd, after_head_1, during_backward_1, None, lambda: sum_3(1, 2))
    emit_inputs(1)
    signal_ready(1)
    for zz in early:
        job = jobs[1, zz]
        copies.leave(*job["swap"], *job["d"], job["x"], job["y"])

    def after_head_0():
        wait_ready(1)
        sum_0(1, 1)
        sum_0(1, 0)
        pack(0, (3,))
        sum_0(0, 3)

    def during_backward_0(i):
        schedule(i, [
            (0, sum_1, 1, 1), (0, sum_1, 1, 0),
            (1, sum_1, 0, 3),
            (3, sum_2, 1, 1), (3, sum_2, 1, 0),
            (4, pack, 0, (2,)), (4, sum_0, 0, 2), (4, sum_2, 0, 3),
            (5, sum_1, 0, 2),
            (7, sum_3, 1, 1), (7, sum_3, 1, 0),
            (8, sum_0, 0, 1), (8, sum_2, 0, 2), (8, sum_3, 0, 3),
            (9, sum_1, 0, 1),
        ])

    def after_weights():
        sum_0(0, 0)
        vector_step(0)
        sum_2(0, 1)

    backward_tower(0, bwd, after_head_0, during_backward_0, lambda: free_inputs(1), after_weights)
    emit_inputs(0)
    sum_1(0, 0)
    vector_step(1)
    sum_3(0, 2)
    sum_3(0, 1)
    sum_3(0, 0)
    vector_step(2)
    sum_4()
    vector_step(3)

    slot128[...] = jnp.zeros(slot128.shape, F32)
    for h in range(2):
        slot128[pl.ds(2 * hrows * h, hrows, stride=2)] = final(h)[:, 0:128]
        slot128[pl.ds(2 * hrows * h + 1, hrows, stride=2)] = final(h)[:, 128:D]

    @pl.when(me == owner)
    def _():
        for kind in range(3):
            first = 2 * (plan.v_off[owner] + kind * (BLOCKS + 1))
            for h in range(2):
                value = vacc[2, kind, 0 : BLOCKS + 1, 128 * h : 128 * h + 128]
                slot128[pl.ds(first + h, BLOCKS + 1, stride=2)] = value

    def push(src, dst, to):
        number = copies.add(lambda: src, lambda: dst, lambda: to)
        copies.start(number)
        return copies.get(number)

    lay_flat(plan, me, slot128, flat, rolled)
    for c in moments:
        c.wait()
    update_shard(
        plan, me, params_in, first_new, second_new, (first_new, second_new, new, norm_out),
        flat, squares, sq_in, push, [to_x(), to_y(), to_d()], [at(core, (me + 4 * k) % n) for k in range(1, depth)],
    )
    copies.arrive(st_copy)
    pl.when(core == 0)(lambda: copies.arrive(ig_copies[0]))
    pl.when(core == 1)(lambda: copies.arrive(ig_copies[1]))
    free_inputs(0)
    copies.sent.update(ig_copies)
    copies.leave(*range(len(copies.made)))


def finish_kernel(st, ig, first, second, new, norms, st_out, ig_out, first_out, second_out, new_out, low_out, norms_out, sem):
    half = st.shape[0] // 2
    pairs = [(first, first_out), (second, second_out)]
    for src, dst in ((ig, ig_out), (st, st_out)):
        pairs += [(src.at[pl.ds(lo, half)], dst.at[pl.ds(lo, half)]) for lo in (0, half)]
    moves = [pltpu.make_async_copy(src, dst, sem.at[i]) for i, (src, dst) in enumerate(pairs)]
    for move in moves:
        move.start()
    size = new.shape[1]
    for lo in range(0, size, 8192):
        hi = min(lo + 8192, size)
        value = new[0:1, lo:hi]
        new_out[0:1, lo:hi] = value
        low_out[0:1, lo:hi] = value.astype(BF)
    norms_out[...] = norms[...]
    for move in moves:
        move.wait()


def finish(st, ig, first, second, new, norms):
    vm = pl.BlockSpec(memory_space=pltpu.VMEM)
    hbm = pl.BlockSpec(memory_space=pl.ANY)
    arrays = (st, ig, first, second, new)
    shapes = [jax.ShapeDtypeStruct(v.shape, v.dtype) for v in arrays]
    return pl.pallas_call(
        finish_kernel,
        out_shape=(*shapes, jax.ShapeDtypeStruct(new.shape, BF), jax.ShapeDtypeStruct(norms.shape, F32)),
        in_specs=[hbm] * 4 + [vm] * 2,
        out_specs=(hbm,) * 4 + (vm,) * 3,
        scratch_shapes=[pltpu.SemaphoreType.DMA((6,))],
        compiler_params=pltpu.CompilerParams(vmem_limit_bytes=62 * 1024 * 1024),
    )(st, ig, first, second, new, norms)


def train(plan, latent, codes, targets, visits, imp, params, first, second):
    n, rows = plan.n, plan.slot
    depth, hrows = n // 4, rows // 2
    width = codes.shape[1] // 2
    height = -(-params.shape[1] // 1024) * 8
    vm = pl.BlockSpec(memory_space=pltpu.VMEM)
    hbm = pl.BlockSpec(memory_space=pl.ANY)
    packed = sum(1 for h, v in zip(plan.h_rows, plan.v_rows) if h or v)
    return pl.pallas_call(
        functools.partial(train_kernel, plan),
        out_shape=(
            jax.ShapeDtypeStruct((2 * width, D), BF),
            jax.ShapeDtypeStruct((2 * width, D), F32),
            jax.ShapeDtypeStruct(params.shape, F32),
            jax.ShapeDtypeStruct(params.shape, F32),
            jax.ShapeDtypeStruct(params.shape, F32),
            jax.ShapeDtypeStruct((2, MATS), F32),
        ),
        in_specs=[hbm] + [vm] * 5 + [hbm] * 2,
        out_specs=(hbm, hbm, vm, vm, vm, vm),
        scratch_shapes=[
            pltpu.VMEM((2, A_ROWS, D), BF),
            pltpu.VMEM((2, D, HPAD), BF),
            pltpu.VMEM((2, 128, D), BF),
            pltpu.VMEM((2, 8, width), jnp.int32),
            pltpu.VMEM((8, width), jnp.int32),
            pltpu.VMEM((8, width), F32),
            *work_scratch(width),
            pltpu.VMEM((2, A_ROWS, D), BF),
            pltpu.VMEM((2, D, HPAD), BF),
            pltpu.VMEM((2, 3, 16, D), F32),
            pltpu.VMEM((packed, rows, D), BF),
            pltpu.VMEM((2, width, D), BF),
            pltpu.VMEM((max(2 * rows, height + 48) + 80, 128), F32),
            pltpu.VMEM((height + 128, 128), F32),
            pltpu.VMEM((height + 40, 128), F32),
            pltpu.VMEM((128, D), F32),
            pltpu.VMEM((3, 3, 16, D), F32),
            pltpu.VMEM((3 + depth, 3, 16, D), F32),
            pltpu.VMEM((3, hrows, D), F32),
            pltpu.VMEM((4, 32, 128), F32),
            pltpu.VMEM((2 + depth, 32, 128), F32),
            pltpu.VMEM((8, 128), F32),
            pltpu.SemaphoreType.DMA((11 * n,)),
            pltpu.SemaphoreType.DMA((11 * n,)),
            pltpu.SemaphoreType.DMA((2 * depth,)),
            pltpu.SemaphoreType.DMA((2 * (depth + 2),)),
            pltpu.SemaphoreType.DMA((5,)),
            pltpu.SemaphoreType.REGULAR((2,)),
        ],
        compiler_params=pltpu.CompilerParams(
            collective_id=2, has_side_effects=True, vmem_limit_bytes=63 * 1024 * 1024
        ),
    )(latent, codes, targets, visits, imp, params, first, second)


def on_device(latent, codes, targets, visits, importance, params, first_moment, second_moment):
    me = lax.axis_index("tower")
    row_count = latent.shape[0]
    half = row_count // 2
    shard_len = params.shape[1]
    plan = Plan(lax.axis_size("dp"), shard_len)
    if fused_fits(plan):
        states_out, inputs_out, first, second, new, norms = train(
            plan, latent, codes, targets.transpose(1, 0, 2), visits[0].T, importance[None], params, first_moment, second_moment
        )
        states_out, inputs_out, first, second, new, low, norms = finish(states_out, inputs_out, first, second, new, norms)
    else:
        height = -(-plan.rows128 // 8) * 8
        p128, m128, v128 = (
            jnp.pad(v, ((0, 0), (0, 128 * height - shard_len))).reshape(height, 128)
            for v in (params, first_moment, second_moment)
        )
        ints = jnp.concatenate([codes, targets[0, :1], visits[0].T, targets[0, 1:]], 0)
        x = lax.dynamic_slice_in_dim(latent, me * half, half, 0)
        w, wh, vec, both, rw = gather(plan, p128, ints, importance[None])
        st, ig, gw, gh, gv = compute(x, both, rw, w, wh, vec)
        states_out, inputs_out, *flat, norms = reduce_and_update(plan, gw, gh, gv, st, ig, p128, m128, v128)
        first, second, new = (v.reshape(1, -1)[:, :shard_len] for v in flat)
        low = new.astype(BF)
    return (states_out[None], inputs_out[None], first, second, new, low, norms[None])


def solution(mesh):
    in_specs = (
        P("dp", None),
        P("tower", "dp"),
        P("tower", None, "dp"),
        P("tower", "dp", None),
        P("dp"),
        P("tower", "dp"),
        P("tower", "dp"),
        P("tower", "dp"),
    )
    out_specs = (
        P("tower", "dp", None),
        P("tower", "dp", None),
        P("tower", "dp"),
        P("tower", "dp"),
        P("tower", "dp"),
        P("tower", "dp"),
        P("tower", None, None),
    )
    return jax.shard_map(
        on_device, mesh=mesh, in_specs=in_specs, out_specs=out_specs, check_vma=False
    )
```

```python
import functools

import jax
import jax.numpy as jnp
from jax import lax
from jax.experimental import pallas as pl
from jax.experimental.pallas import tpu as pltpu
from jax.sharding import PartitionSpec as P

D = 256
CODES = 32
BINS = 601
BLOCKS = 10
STEP = 5
HEADS = 1238
MATS = 12
P_SIZE = 1054464
HPAD = 1280
CAT = D + CODES
A_ROWS = CAT + BLOCKS * D
BF = jnp.bfloat16
F32 = jnp.float32
GELU_C = 0.7978845608028654
GELU_K = 0.044715


def nn(a, b):
    return jnp.dot(a, b, preferred_element_type=F32)


def nt(a, b):
    return lax.dot_general(a, b, (((1,), (1,)), ((), ())), preferred_element_type=F32)


def identity(n):
    return (lax.broadcasted_iota(jnp.int32, (n, n), 0) == lax.broadcasted_iota(jnp.int32, (n, n), 1)).astype(BF)


ZETA = (GELU_C * GELU_K) ** (1.0 / 3.0)
B0 = GELU_C / ZETA
E0 = 0.5 / ZETA


def wide(v, cs):
    return jnp.concatenate([v] * ((cs.stop - cs.start) // v.shape[1]), 1)


def norm_act(src, cs, gs, unit, gp, rstd, out):
    for r in range(0, D, 32):
        rs = slice(r, r + 32)
        xh = src[rs, cs] * rstd
        z = xh * wide(gs[rs, 0:128], cs) + wide(gs[rs, 128:256], cs)
        z2 = z * z
        t = jnp.tanh(z * (z2 + B0))
        q = t * E0 + E0
        a = z * q
        out(rs, a)
        unit[rs, cs] = xh.astype(BF)
        gp[rs, cs] = (q + (a * (1.0 - t)) * (z2 * 3.0 + B0)).astype(BF)


def broadcast_vectors(vt, rows):
    k = lax.broadcasted_iota(jnp.int32, (128, 128), 0)
    picks = jnp.concatenate([(k == row).astype(BF) for row in rows], 1)
    return nn(vt, picks)


def head_stage(cs, lg, dl, ints, rw):
    width = rw.shape[1]
    it8 = lax.broadcasted_iota(jnp.int32, (8, width), 0)
    low = -jnp.inf
    b75, b150, b154 = lg[600:608], lg[1200:1208], lg[1232:1240]

    def top(block):
        return jnp.max(block, axis=0, keepdims=True)

    def top_range(lo, hi):
        best = lg[lo : lo + 8]
        for r in range(lo + 8, hi, 8):
            best = jnp.maximum(best, lg[r : r + 8])
        return best

    max_v = top(jnp.maximum(top_range(0, 600), jnp.where(it8 < 1, b75, low)))
    max_r = top(
        jnp.maximum(
            jnp.maximum(top_range(608, 1200), jnp.where(it8 >= 1, b75, low)),
            jnp.where(it8 < 2, b150, low),
        )
    )
    max_c = top(
        jnp.maximum(
            jnp.maximum(top_range(1208, 1232), jnp.where(it8 >= 2, b150, low)),
            jnp.where(it8 < 2, b154, low),
        )
    )
    in_policy = (it8 >= 2) & (it8 < 6)
    max_p = top(jnp.where(in_policy, b154, low))

    def exp_range(lo, hi, best):
        acc = jnp.zeros((8, width), F32)
        for r in range(lo, hi, 8):
            e = jnp.exp(lg[r : r + 8] - best)
            lg[r : r + 8] = e
            acc = acc + e
        return acc

    e75 = jnp.exp(b75 - jnp.where(it8 < 1, max_v, max_r))
    e150 = jnp.exp(b150 - jnp.where(it8 < 2, max_r, max_c))
    e154 = jnp.exp(b154 - jnp.where(it8 < 2, max_c, max_p))

    def total(acc):
        return rw / jnp.sum(acc, axis=0, keepdims=True)

    inv_v = total(exp_range(0, 600, max_v) + jnp.where(it8 < 1, e75, 0.0))
    inv_r = total(exp_range(608, 1200, max_r) + jnp.where(it8 >= 1, e75, 0.0) + jnp.where(it8 < 2, e150, 0.0))
    inv_c = total(exp_range(1208, 1232, max_c) + jnp.where(it8 >= 2, e150, 0.0) + jnp.where(it8 < 2, e154, 0.0))
    inv_p = total(jnp.where(in_policy, e154, 0.0))
    hit_v = ints[1:2]
    hit_r = ints[6:7] + BINS
    hit_c = ints[7:8] + 2 * BINS
    counts = jnp.where(in_policy, ints.astype(F32), 0.0)
    share = counts * (rw / jnp.sum(counts, axis=0, keepdims=True))

    def minus(value, lo, *hits):
        at = lax.broadcasted_iota(jnp.int32, value.shape, 0)
        for hit in hits:
            value = value - jnp.where(at == hit - lo, rw, 0.0)
        return value

    d75 = minus(e75 * jnp.where(it8 < 1, inv_v, inv_r), 600, hit_v, hit_r)
    d150 = minus(e150 * jnp.where(it8 < 2, inv_r, inv_c), 1200, hit_r, hit_c)
    d154 = minus(e154 * jnp.where(it8 < 2, inv_c, inv_p), 1232, hit_c) - share
    d154 = jnp.where(it8 < 6, d154, 0.0)

    def emit(lo, hi, inv, hit):
        for r in range(lo, hi, 16):
            dl[r : r + 16, cs] = minus(lg[r : r + 16] * inv, r, hit).astype(BF)

    def pair(first, second):
        return jnp.concatenate([first, second], 0).astype(BF)

    emit(0, 592, inv_v, hit_v)
    dl[592:608, cs] = pair(minus(lg[592:600] * inv_v, 592, hit_v), d75)
    emit(608, 1200, inv_r, hit_r)
    dl[1200:1216, cs] = pair(d150, minus(lg[1208:1216] * inv_c, 1208, hit_c))
    emit(1216, 1232, inv_c, hit_c)
    dl[1232:1248, cs] = pair(d154, jnp.zeros_like(d154))
    dl[1248:HPAD, cs] = jnp.zeros((HPAD - 1248, width), BF)


CB = 256
GROUP = 2


def saved_views(t, mix, xh):
    def mixed(k):
        return mix.at[pl.ds(pl.multiple_of((t * BLOCKS + k - 1) * (D + 16), 16), D + 16)]

    def unit(k):
        return xh.at[pl.ds(pl.multiple_of((t * (BLOCKS + 1) + k) * D, D), D)]

    return mixed, unit


def column_groups(width):
    blocks = [slice(c, c + CB) for c in range(0, width, CB)]
    per = min(GROUP, len(blocks))
    return blocks, per, [slice(c, c + per * CB) for c in range(0, width, per * CB)]


def forward_tower(t, refs, during=None, before_last=None):
    (eye, w, wh, vec, wt, vt, gsb, xt, mix, xh, gp, rstd, stream, mean, ints, width) = refs
    blocks, per, groups = column_groups(width)
    mixed, unit = saved_views(t, mix, xh)
    first_bias = 2 * (BLOCKS + 1)
    ones = jnp.ones((16, D), BF)

    def mean_rows(slot):
        value = nn(ones, wt[slot, 0:D])[0:8] * (1.0 / D)
        high = value.astype(BF).astype(F32)
        wt[slot, D : D + 16] = jnp.concatenate([high, value - high], 0).astype(BF)

    def vectors(k):
        gsb[k % 2] = broadcast_vectors(vt[...], (k, k + BLOCKS + 1)) * ZETA

    def prefetch(k):
        vectors(k)
        row = pl.multiple_of(CAT + jnp.minimum(k - 1, BLOCKS - 1) * D, 32)
        wt[k % 2, 0:D, 0:D] = nt(eye[...], w[t, pl.ds(row, D)]).astype(BF)
        at_row = lax.broadcasted_iota(jnp.int32, (128, 128), 0) == k + first_bias
        at_lane = lax.broadcasted_iota(jnp.int32, (128, 128), 1) == 0
        wt[k % 2, 0:D, D:384] = nn(vt[...], (at_row & at_lane).astype(BF)).astype(BF)
        mean_rows(k % 2)

    def row_of(k):
        return pl.ds(t * (BLOCKS + 1) + k, 1)

    def stage(k, c):
        def keep(rs, a):
            mixed(k)[rs, blocks[c]] = a.astype(BF)

        norm_act(stream, blocks[c], gsb.at[k % 2], unit(k), gp.at[t, k], rstd[row_of(k), blocks[c]], keep)

    def spread(square, k, cs):
        var = jnp.sum(square, axis=0, keepdims=True) * (1.0 / D)
        rstd[row_of(k), cs] = lax.rsqrt(var + 1e-05)

    def add(k, cs, out, fresh):
        shift = out[D : D + 1] + out[D + 8 : D + 9]
        square = jnp.zeros((8, out.shape[1]), F32)
        for r in range(0, D, 32):
            value = out[r : r + 32] - shift
            if not fresh:
                value = stream[r : r + 32, cs] + value
            stream[r : r + 32, cs] = value
            square = square + jnp.sum((value * value).reshape(4, 8, -1), axis=0)
        if not fresh:
            mean[0:1, cs] = mean[0:1, cs] + shift
        spread(square, k + 1, cs)

    def centre(cs):
        total = jnp.zeros((8, CB), F32)
        for r in range(0, D, 32):
            total = total + jnp.sum(stream[r : r + 32, cs].reshape(4, 8, -1), axis=0)
        middle = jnp.sum(total, axis=0, keepdims=True) * (1.0 / D)
        mean[0:1, cs] = middle
        square = jnp.zeros((8, CB), F32)
        for r in range(0, D, 32):
            value = stream[r : r + 32, cs] - middle
            stream[r : r + 32, cs] = value
            square = square + jnp.sum((value * value).reshape(4, 8, -1), axis=0)
        spread(square, 1, cs)

    vt[...] = nt(eye[...], vec[t]).astype(BF)
    vectors(0)
    wt[0, 0:D, 0:D] = nt(eye[...], w[t, 0:D]).astype(BF)
    tile = first_bias // 16 * 16
    picked = lax.broadcasted_iota(jnp.int32, (16, D), 0) == first_bias - tile
    bias = jnp.where(picked, vec[t, tile : tile + 16].astype(F32), 0.0).astype(BF)
    rest = jnp.concatenate([w[t, D:CAT], bias, jnp.zeros((128 - CODES - 16, D), BF)], 0)
    wt[0, 0:D, D:384] = nt(eye[...], rest).astype(BF)
    mean_rows(0)
    for cs in blocks:
        it = lax.broadcasted_iota(jnp.int32, (CODES, CB), 0)
        xt[t, D:CAT, cs] = (it == ints[t, 0:1, cs]).astype(BF)
        xt[t, CAT : CAT + 16, cs] = jnp.ones((16, CB), BF)
    first = [nn(wt[0, :, 0 : CAT + 16], xt[t, :, cs]) for cs in groups]
    prefetch(1)
    for group, cs in enumerate(groups):
        add(-1, cs, first[group], True)
    for cs in blocks:

        def keep(rs, a):
            stream[rs, cs] = a

        norm_act(stream, cs, gsb.at[0], unit(0), gp.at[t, 0], rstd[row_of(0), cs], keep)
        centre(cs)

    def layer(k, more):
        mixed(k)[D : D + 16, :] = jnp.ones((16, width), BF)
        for group, cs in enumerate(groups):
            out = nn(wt[k % 2, :, 0 : D + 16], mixed(k)[:, cs])
            ahead = group + 1 < len(groups)
            if ahead or more:
                for c in range(per):
                    stage(k if ahead else k + 1, (group + 1) % len(groups) * per + c)
            add(k, cs, out, False)
        if more:
            prefetch(k + 2)

    prefetch(2)
    for c in range(per):
        stage(1, c)

    @pl.loop(1, BLOCKS)
    def _(k):
        if during is not None:
            during(k)
        layer(k, True)

    if before_last is not None:
        before_last()
    layer(BLOCKS, False)
    for cs in blocks:
        xt[t + 1, 0:D, cs] = (stream[:, cs] + mean[0:1, cs]).astype(BF)


def backward_tower(t, refs, after_head=None, during=None, before_product=None, after_weights=None):
    (eye, w, wh, vec, wht, vt, gsb, xt, mix, xh, gp, rstd, ds, ex, br, dm, acc, lg, dl, ints, rw, gw, gh, gv, ig, width) = refs
    blocks = [slice(c, c + CB) for c in range(0, width, CB)]
    last = len(blocks) - 1
    mixed, unit = saved_views(t, mix, xh)
    vt[...] = nt(eye[...], vec[t]).astype(BF)
    for h in range(0, HPAD, D):
        wht[h : h + D, :] = nt(eye[...], wh[t, :, h : h + D]).astype(BF)

    @pl.loop(0, width // CB)
    def _(c):
        cs = pl.ds(pl.multiple_of(c * CB, CB), CB)
        lg[...] = nn(wht[...], xt[t + 1, 0:D, cs])
        head_stage(cs, lg, dl, ints[t, :, cs], rw[0:1, cs])
        value = nn(wh[t], dl[:, cs]) + ex[:, cs]
        ds[:, cs] = value
        br[BLOCKS % 2, :, cs] = value.astype(BF)

    for h in range(0, HPAD, D):
        gh[t, :, h : h + D] = nt(xt[t + 1, 0:D, :], dl[h : h + D]).astype(BF)
    if after_head is not None:
        after_head()
    acc[...] = jnp.zeros(acc.shape, F32)
    ones = jnp.ones((16, 128), BF)

    def part(c):
        return dm.at[c * D : c * D + D]

    def gains(k):
        gsb[k % 2, :, 0:128] = broadcast_vectors(vt[...], (k,)) * ZETA

    def row_sums(k):
        for kind in range(2):
            gv[t, kind, pl.ds(k, 1), :] = nt(ones, acc[k % 2, kind].astype(BF))[0:1] * ZETA
        acc[k % 2] = jnp.zeros(acc.shape[1:], F32)

    def product(k, c):
        row = pl.multiple_of(CAT + (k - 1) * D, 32)
        part(c)[...] = nn(w[t, pl.ds(row, D)], br[k % 2, :, blocks[c]])

    def slopes(k, c):
        cs, grad, sums = blocks[c], part(c), acc.at[k % 2]
        s1 = jnp.zeros((8, CB), F32)
        s2 = jnp.zeros((8, CB), F32)
        for r in range(0, D, 32):
            rs = slice(r, r + 32)
            g = wide(gsb[k % 2, rs, 0:128], cs)
            dy = grad[rs, :] * gp[t, k, rs, cs].astype(F32)
            prod = dy * unit(k)[rs, cs].astype(F32)
            back = dy * g
            grad[rs, :] = back
            s1 = s1 + jnp.sum(back.reshape(4, 8, CB), axis=0)
            s2 = s2 + jnp.sum((prod * g).reshape(4, 8, CB), axis=0)
            sums[0, rs] = sums[0, rs] + (prod[:, 0:128] + prod[:, 128:CB])
            sums[1, rs] = sums[1, rs] + (dy[:, 0:128] + dy[:, 128:CB])
        return [jnp.sum(s, axis=0, keepdims=True) * (1.0 / D) for s in (s1, s2)]

    def stage(k, c, first):
        cs = blocks[c]
        means = slopes(k, c)
        scale = rstd[pl.ds(t * (BLOCKS + 1) + k, 1), cs]
        m1, m2 = (jnp.broadcast_to(m * scale, (32, CB)).astype(BF) for m in means)
        for r in range(0, D, 32):
            rs = slice(r, r + 32)
            back = part(c)[rs, :] * scale - (m1 + unit(k)[rs, cs] * m2).astype(F32)
            if first:
                br[0, rs, cs] = back.astype(BF)
            else:
                value = ds[rs, cs] + back
                ds[rs, cs] = value
                br[(k + 1) % 2, rs, cs] = value.astype(BF)

    if before_product is not None:
        before_product()
    gains(BLOCKS)
    gains(BLOCKS - 1)
    product(BLOCKS, 0)

    @pl.loop(0, BLOCKS)
    def _(i):
        k = BLOCKS - i
        if during is not None:
            during(i)
        for c in range(last + 1):
            if c < last:
                product(k, c + 1)
            stage(k, c, False)
            if c == 0:
                full = nt(mixed(k)[...], br[k % 2])
                row = pl.multiple_of(CAT + (k - 1) * D, 32)
                gw[t, pl.ds(row, D), :] = full[0:D].astype(BF)
                gv[t, 2, pl.ds(k, 1), :] = full[D : D + 1]
                product(k - 1, 0)
        gains(k - 2)
        row_sums(k)

    for c, cs in enumerate(blocks):
        part(c)[...] = ds[:, cs]
        stage(0, c, True)
    full = nt(xt[t], br[0])
    gw[t, 0:CAT, :] = full[0:CAT].astype(BF)
    gv[t, 2, 0:1, :] = full[CAT : CAT + 1]
    row_sums(0)
    if after_weights is not None:
        after_weights()
    for cs in blocks:
        back = nn(w[t, 0:D], br[0, :, cs])
        ex[:, cs] = back
        ig[cs, :] = back.T


def compute_kernel(x_ref, ints, rw, w, wh, vec, st, ig, gw, gh, gv, eye, wt, wht, vt, gsb, xt, mix, xh, gp, rstd, mean, stream, ex, br, dm, acc, lg, dl):
    width = x_ref.shape[0]
    eye[...] = identity(D)
    for c in range(0, width, CB):
        cs = slice(c, c + CB)
        xt[0, 0:D, cs] = nt(eye[...], x_ref[cs, :]).astype(BF)
    fwd = (eye, w, wh, vec, wt, vt, gsb, xt, mix, xh, gp, rstd, stream, mean, ints, width)
    @pl.loop(0, 2)
    def _(t):
        forward_tower(t, fwd)

        @pl.loop(0, width // CB)
        def _(c):
            cs = pl.ds(pl.multiple_of(c * CB, CB), CB)
            st[t, cs, :] = nt(eye[...], xt[t + 1, 0:D, cs]).astype(BF)

    ex[...] = jnp.zeros_like(ex)

    @pl.loop(0, 2)
    def _(i):
        t = 1 - i
        backward_tower(
            t,
            (eye, w, wh, vec, wht, vt, gsb, xt, mix, xh, gp, rstd, stream, ex, br, dm, acc, lg, dl, ints, rw, gw, gh, gv, ig.at[t], width),
        )


def work_scratch(width):
    return [
        pltpu.VMEM((D, D), BF),
        pltpu.VMEM((2, D + 16, 384), BF),
        pltpu.VMEM((HPAD, D), BF),
        pltpu.VMEM((D, 128), BF),
        pltpu.VMEM((2, D, 256), F32),
        pltpu.VMEM((3, CAT + 16, width), BF),
        pltpu.VMEM((2 * BLOCKS * (D + 16), width), BF),
        pltpu.VMEM((2 * (BLOCKS + 1) * D, width), BF),
        pltpu.VMEM((2, BLOCKS + 1, D, width), BF),
        pltpu.VMEM((24, width), F32),
        pltpu.VMEM((8, width), F32),
        pltpu.VMEM((D, width), F32),
        pltpu.VMEM((D, width), F32),
        pltpu.VMEM((2, D, width), BF),
        pltpu.VMEM((width // CB * D, CB), F32),
        pltpu.VMEM((2, 2, D, 128), F32),
        pltpu.VMEM((HPAD, CB), F32),
        pltpu.VMEM((HPAD, width), BF),
    ]


def compute(x, ints, rw, w, wh, vec):
    width = x.shape[0]
    vm = pl.BlockSpec(memory_space=pltpu.VMEM)
    return pl.pallas_call(
        compute_kernel,
        out_shape=(
            jax.ShapeDtypeStruct((2, width, D), BF),
            jax.ShapeDtypeStruct((2, width, D), F32),
            jax.ShapeDtypeStruct((2, A_ROWS, D), BF),
            jax.ShapeDtypeStruct((2, D, HPAD), BF),
            jax.ShapeDtypeStruct((2, 3, 16, D), F32),
        ),
        in_specs=[vm] * 6,
        out_specs=(vm,) * 5,
        scratch_shapes=work_scratch(width),
        compiler_params=pltpu.CompilerParams(vmem_limit_bytes=62 * 1024 * 1024),
    )(x, ints, rw, w, wh, vec)


class Plan:
    def __init__(self, n, length):
        self.n, self.length = n, length
        self.rows128 = -(-length // 128)
        block_end, head_end = A_ROWS * D, A_ROWS * D + D * HEADS
        self.a_base, self.a_rows, self.h_first, self.h_rows, self.h_off, self.v_first, self.v_rows, self.v_off = ([] for _ in range(8))
        used = 0
        for i in range(n):
            lo, hi = i * length, (i + 1) * length
            base = min(lo, block_end) // D // 16 * 16
            top = -(-min(hi, block_end) // D)
            a_rows = -(-(top - base) // 16) * 16 if lo < block_end else 0
            first = min(max(lo - block_end, 0), D * HEADS) // HEADS
            last = -(-min(max(hi - block_end, 0), D * HEADS) // HEADS)
            h_rows = last - first if hi > block_end and lo < head_end else 0
            v_first = max(lo - head_end, 0) // D
            v_rows = -(-(hi - head_end) // D) - v_first if hi > head_end else 0
            self.a_base.append(base)
            self.a_rows.append(a_rows)
            self.h_first.append(first)
            self.h_rows.append(h_rows)
            self.h_off.append(a_rows)
            self.v_first.append(v_first)
            self.v_rows.append(v_rows)
            self.v_off.append(a_rows + 5 * h_rows)
            used = max(used, a_rows + 5 * h_rows + v_rows)
        self.heads = max(self.h_rows)
        self.image = (HEADS * self.heads // 128 + 24) // 8 * 8
        self.slot = -(-(used + 1) // 32) * 32

    def at(self, table, me):
        value = jnp.int32(table[0])
        for i in range(1, self.n):
            if table[i] != table[i - 1]:
                value = value + (me >= i).astype(jnp.int32) * (table[i] - table[i - 1])
        return value


MESH = pl.DeviceIdType.MESH


def neighbours(n):
    core = lax.axis_index("tower")
    me = lax.axis_index("dp")
    near_x = me + 1 - 2 * (me % 2)
    near_y = me + 2 - 4 * ((me // 2) % 2)
    return core, me, near_x, near_y


def at(core, index):
    return {"tower": core, "dp": index}


def greet(core, me, near_x, near_y, n, crossed=False):
    barrier = pltpu.get_barrier_semaphore()
    pl.semaphore_signal(barrier, inc=1, device_id=at(1 - core, me), device_id_type=MESH)
    for near in (near_x, near_y, near_x + near_y - me):
        pl.semaphore_signal(barrier, inc=1, device_id=at(core, near), device_id_type=MESH)
    for k in range(1, n // 4):
        pl.semaphore_signal(barrier, inc=1, device_id=at(core, (me + 4 * k) % n), device_id_type=MESH)
    for near in [near_x, near_y] + [(me + 4 * k) % n for k in range(1, n // 4)] if crossed else []:
        pl.semaphore_signal(barrier, inc=1, device_id=at(1 - core, near), device_id_type=MESH)
    return barrier


def place_shard(plan, me, p_ref, slot128, shifted, rolled):
    rows = plan.rows128
    start = me * plan.length
    shift = start % 128
    first = start // 128
    tall = shifted.shape[0]
    height = p_ref.shape[0]
    lane = lax.broadcasted_iota(jnp.int32, (height, 128), 1)
    rolled[0:8] = jnp.zeros((8, 128), F32)
    rolled[8 : 8 + height] = pltpu.roll(p_ref[...], shift, 1)
    shifted[...] = jnp.zeros((tall, 128), F32)
    moved = jnp.where(lane >= shift, rolled[8 : 8 + height], rolled[7 : 7 + height])
    shifted[16 : 16 + height] = moved
    slot128[...] = jnp.zeros(slot128.shape, F32)
    row = lax.broadcasted_iota(jnp.int32, (height, 128), 0)
    base = plan.at(plan.a_base, me)

    @pl.when(plan.at(plan.a_rows, me) > 0)
    def _():
        slot128[pl.ds(first - 2 * base, height)] = jnp.where(row + first < 2 * A_ROWS, moved, 0.0)

    v_start = (A_ROWS * D + D * HEADS) // 128
    v_rows, v_off, v_first = (plan.at(t, me) for t in (plan.v_rows, plan.v_off, plan.v_first))
    tall_v = min(height, -(-2 * max(plan.v_rows) // 8) * 8)

    @pl.when(v_rows > 0)
    def _():
        inside = plan.at([max(0, v_start - i * plan.length // 128) for i in range(plan.n)], me)
        to = 2 * v_off + first + inside - v_start - 2 * v_first
        slot128[pl.ds(to, tall_v)] = shifted[pl.ds(16 + inside, tall_v)]

    h_first, h_rows, h_off = (plan.at(t, me) for t in (plan.h_first, plan.h_rows, plan.h_off))

    @pl.when(h_rows > 0)
    def _():
        tall_h = plan.image
        begin = A_ROWS * D + HEADS * h_first - 128 * first + 128 * 16
        turn = begin % 128
        rolled[0:tall_h] = pltpu.roll(shifted[pl.ds(begin // 128, tall_h)], (128 - turn) % 128, 1)
        rolled[tall_h : tall_h + 8] = jnp.zeros((8, 128), F32)
        lane = lax.broadcasted_iota(jnp.int32, (tall_h, 128), 1)
        shifted[0:tall_h] = jnp.where(lane < 128 - turn, rolled[0:tall_h], rolled[1 : tall_h + 1])
        to = slot128.at[pl.ds(pl.multiple_of(2 * h_off, 8), 10 * plan.heads)]
        it = lax.broadcasted_iota(jnp.int32, (10, 128), 0)
        lane = lax.broadcasted_iota(jnp.int32, (10, 128), 1)
        for k in range(plan.heads):
            row, turn = HEADS * k // 128, HEADS * k % 128
            window = pltpu.roll(shifted[row : row + 16], (128 - turn) % 128, 1)
            value = jnp.where(lane < 128 - turn, window[0:10], window[1:11])
            kept = (it * 128 + lane < HEADS) & (k < h_rows)
            to[10 * k : 10 * k + 10] = to[10 * k : 10 * k + 10] + jnp.where(kept, value, 0.0)


def unpack_rows(plan, i, slot, w, heads, vectors, scratch):
    base, rows = plan.a_base[i], plan.a_rows[i]
    if rows:
        shared = i > 0 and base < plan.a_base[i - 1] + plan.a_rows[i - 1]
        lo = 0
        if shared:
            w[base : base + 16] = w[base : base + 16] + slot[0:16]
            lo = 16
        if rows > lo:
            w[base + lo : base + rows] = slot[lo:rows]
    h_rows, h_off, h_first = plan.h_rows[i], plan.h_off[i], plan.h_first[i]
    v_rows, v_off, v_first = plan.v_rows[i], plan.v_off[i], plan.v_first[i]
    if h_rows or v_rows:
        value = slot.astype(F32)
        scratch[0][...] = value[:, 0:128]
        scratch[1][...] = value[:, 128:D]
    if h_rows:
        shared = i > 0 and plan.h_rows[i - 1] and plan.h_first[i - 1] + plan.h_rows[i - 1] > h_first
        for j in range(5):
            for half in range(2):
                cols = slice(128 * half, 128 * half + 128)
                first = D * j + h_first
                value = scratch[half][pl.ds(h_off + j, h_rows, stride=5)]
                if shared:
                    heads[first : first + 1, cols] = heads[first : first + 1, cols] + value[0:1]
                    if h_rows > 1:
                        heads[first + 1 : first + h_rows, cols] = value[1:h_rows]
                else:
                    heads[first : first + h_rows, cols] = value
    if v_rows:
        shared = v_first and plan.v_first[i - 1] + plan.v_rows[i - 1] > v_first
        shared = shared or (i > 0 and plan.v_rows[i - 1] > 0 and v_first == 0)
        for half in range(2):
            cols = slice(128 * half, 128 * half + 128)
            value = scratch[half][v_off : v_off + v_rows]
            if shared:
                vectors[v_first : v_first + 1, cols] = vectors[v_first : v_first + 1, cols] + value[0:1]
                if v_rows > 1:
                    vectors[v_first + 1 : v_first + v_rows, cols] = value[1:v_rows]
            else:
                vectors[v_first : v_first + v_rows, cols] = value


def split3(value):
    hi = value.astype(BF).astype(F32)
    mid = (value - hi).astype(BF).astype(F32)
    return hi, mid, value - hi - mid


def gather_kernel(plan, p_ref, ints_ref, imp_ref, w, wh, vec, both, rw, slots, slot128, shifted, rolled, scratch, whf, vecf, send, recv):
    n = plan.n
    depth = n // 4
    core, me, near_x, near_y = neighbours(n)
    barrier = greet(core, me, near_x, near_y, n)
    place_shard(plan, me, p_ref, slot128, shifted, rolled)
    pl.semaphore_wait(barrier, depth + 3)
    half = rw.shape[1]
    started = []

    def copy(src, dst, slot, to):
        c = pltpu.make_async_remote_copy(
            src_ref=src, dst_ref=dst, send_sem=send.at[slot], recv_sem=recv.at[slot], device_id=to, device_id_type=MESH
        )
        c.start()
        started.append(c)
        return c

    mine = pl.multiple_of(core * half, half)
    theirs = pl.multiple_of((1 - core) * half, half)
    number = iter(range(1 << 20))
    ints_copy = copy(ints_ref.at[:, pl.ds(theirs, half)], both.at[core], next(number), at(1 - core, me))
    rows = plan.slot
    total = jnp.sum(imp_ref[...].astype(F32), axis=1, keepdims=True)
    lane = lax.broadcasted_iota(jnp.int32, (1, D), 1)
    hi, mid, lo = split3(total)
    left = slot128[pl.ds(0, rows, stride=2)]
    right = slot128[pl.ds(1, rows, stride=2)]
    own = jnp.concatenate([left, right], 1)
    last = jnp.where(lane == 0, hi, jnp.where(lane == 1, mid, jnp.where(lane == 2, lo, 0.0)))
    last_row = lax.broadcasted_iota(jnp.int32, (rows, D), 0) == rows - 1
    slots[core, me] = jnp.where(last_row, last, own).astype(BF)

    def column(index, k):
        return (index + n - 4 * k) % n

    def send_slot(origin, to, lo=0, hi=rows):
        ref = slots.at[core, origin, pl.ds(lo, hi - lo)]
        return copy(ref, ref, next(number), to)

    near_xy = near_x + near_y - me
    cut = rows // 2
    z_in, x_in, y_in, d_in, s_in = {}, {}, {}, {}, []
    for k in sorted(range(1, depth), key=lambda k: (min(k, depth - k), k)):
        z_in[k] = send_slot(me, at(core, (me + 4 * k) % n))
    order = [0] + list(z_in)
    for k in order:
        if k:
            z_in[k].wait_recv()
        x_in[k] = send_slot(column(me, k), at(core, near_x))
        y_in[k] = send_slot(column(me, k), at(core, near_y))
        s_in.append(send_slot(column(me, k), at(1 - core, me)))
    for k in order:
        x_in[k].wait_recv()
        first = send_slot(column(near_x, k), at(core, near_y), 0, cut)
        s_in.append(send_slot(column(near_x, k), at(1 - core, me)))
        y_in[k].wait_recv()
        second = send_slot(column(near_y, k), at(core, near_x), cut, rows)
        s_in.append(send_slot(column(near_y, k), at(1 - core, me)))
        d_in[k] = (first, second)
    for k in order:
        for c in d_in[k]:
            c.wait_recv()
        s_in.append(send_slot(column(near_xy, k), at(1 - core, me)))
    ints_copy.wait_recv()
    both[core] = ints_ref[:, pl.ds(mine, half)]
    for c in s_in:
        c.wait_recv()
    for c in started:
        c.wait_send()
    for t in range(2):
        vecf[...] = jnp.zeros(vecf.shape, F32)
        for i in range(n):
            unpack_rows(plan, i, slots[t, i], w.at[t], whf, vecf, [scratch.at[0], scratch.at[1]])
        for j in range(5):
            wh[t, :, D * j : D * j + D] = whf[D * j : D * j + D].astype(BF)
        vec[t] = vecf[...].astype(BF)
    total = jnp.zeros((1, D), F32)
    for i in range(n):
        tail = slots[0, i, rows - 16 : rows].astype(F32)
        total = total + tail[15:16]
    weight_sum = jnp.sum(jnp.where(lane < 3, total, 0.0), axis=1, keepdims=True)
    rw[...] = jnp.broadcast_to(imp_ref[:, pl.ds(mine, half)].astype(F32) / weight_sum, (8, half))


def gather(plan, p128, ints, imp):
    n, rows = plan.n, plan.slot
    half = ints.shape[1] // 2
    vm = pl.BlockSpec(memory_space=pltpu.VMEM)
    height = p128.shape[0]
    tall = max(2 * rows, height + 40) + 80
    copies = 1 + (n // 4 - 1) + 2 * (n // 4) + 2 * (n // 4) + n
    return pl.pallas_call(
        functools.partial(gather_kernel, plan),
        out_shape=(
            jax.ShapeDtypeStruct((2, A_ROWS, D), BF),
            jax.ShapeDtypeStruct((2, D, HPAD), BF),
            jax.ShapeDtypeStruct((2, 128, D), BF),
            jax.ShapeDtypeStruct((2, 8, half), jnp.int32),
            jax.ShapeDtypeStruct((8, half), F32),
        ),
        in_specs=[vm] * 3,
        out_specs=(vm,) * 5,
        scratch_shapes=[
            pltpu.VMEM((2, n, rows, D), BF),
            pltpu.VMEM((tall, 128), F32),
            pltpu.VMEM((height + 128, 128), F32),
            pltpu.VMEM((height + 40, 128), F32),
            pltpu.VMEM((2, rows, 128), F32),
            pltpu.VMEM((HPAD, D), F32),
            pltpu.VMEM((128, D), F32),
            pltpu.SemaphoreType.DMA((copies,)),
            pltpu.SemaphoreType.DMA((copies,)),
        ],
        compiler_params=pltpu.CompilerParams(
            collective_id=0, has_side_effects=True, vmem_limit_bytes=48 * 1024 * 1024
        ),
    )(p128, ints, imp)


def chunks(height):
    step = max(c for c in range(8, 113, 8) if height % c == 0)
    return [(lo, lo + step) for lo in range(0, height, step)]


def lay_flat(plan, me, slot128, flat, rolled):
    height = rolled.shape[0] - 40
    start = me * plan.length
    shift = start % 128
    first = start // 128
    base = plan.at(plan.a_base, me)
    row = lax.broadcasted_iota(jnp.int32, (height + 8, 128), 0)
    flat[...] = jnp.zeros(flat.shape, F32)

    @pl.when(plan.at(plan.a_rows, me) > 0)
    def _():
        rows = slot128[pl.ds(first - 2 * base, height + 8)]
        flat[16 : 24 + height] = jnp.where(row + first < 2 * A_ROWS, rows, 0.0)

    v_start = (A_ROWS * D + D * HEADS) // 128
    v_rows, v_off, v_first = (plan.at(t, me) for t in (plan.v_rows, plan.v_off, plan.v_first))
    tall_v = min(height, -(-2 * max(plan.v_rows) // 8) * 8)

    @pl.when(v_rows > 0)
    def _():
        inside = plan.at([max(0, v_start - i * plan.length // 128) for i in range(plan.n)], me)
        source = 2 * v_off + first + inside - v_start - 2 * v_first
        to = pl.ds(16 + inside, tall_v)
        flat[to] = flat[to] + slot128[pl.ds(source, tall_v)]

    h_first, h_rows, h_off = (plan.at(t, me) for t in (plan.h_first, plan.h_rows, plan.h_off))

    @pl.when(h_rows > 0)
    def _():
        tall_h = plan.image
        source = slot128.at[pl.ds(pl.multiple_of(2 * h_off, 8), 10 * plan.heads + 6)]
        it = lax.broadcasted_iota(jnp.int32, (16, 128), 0)
        lane = lax.broadcasted_iota(jnp.int32, (16, 128), 1)
        rolled[0 : tall_h + 8] = jnp.zeros((tall_h + 8, 128), F32)
        for k in range(plan.heads):
            row, turn = HEADS * k // 128, HEADS * k % 128
            kept = (it * 128 + lane < HEADS) & (k < h_rows)
            value = pltpu.roll(jnp.where(kept, source[10 * k : 10 * k + 16], 0.0), turn, 1)
            above = jnp.concatenate([jnp.zeros((8, 128), F32), value], 0)[7:23]
            rolled[row : row + 16] = rolled[row : row + 16] + jnp.where(lane >= turn, value, above)
        begin = A_ROWS * D + HEADS * h_first - 128 * first + 128 * 16
        turn = begin % 128
        slot128[0:8] = jnp.zeros((8, 128), F32)
        slot128[8 : 8 + tall_h] = pltpu.roll(rolled[0:tall_h], turn, 1)
        lane = lax.broadcasted_iota(jnp.int32, (tall_h, 128), 1)
        moved = jnp.where(lane >= turn, slot128[8 : 8 + tall_h], slot128[7 : 7 + tall_h])
        to = pl.ds(begin // 128, tall_h)
        flat[to] = flat[to] + moved

    rolled[0 : height + 8] = pltpu.roll(flat[16 : 24 + height], (128 - shift) % 128, 1)
    for lo, hi in chunks(height):
        lane = lax.broadcasted_iota(jnp.int32, (hi - lo, 128), 1)
        flat[lo:hi] = jnp.where(lane < 128 - shift, rolled[lo:hi], rolled[lo + 1 : hi + 1])


def pack_slots(plan, core, gw, gh, gv, rgw, rgh, rgv, slots, sums, vsum, scratch):
    total = gv[core].astype(F32) + rgv[...]
    for kind in range(3):
        vsum[kind * (BLOCKS + 1) : (kind + 1) * (BLOCKS + 1)] = total[kind, 0 : BLOCKS + 1]
    sums[...] = gh[core].astype(F32) + rgh[...].astype(F32)
    for i in range(plan.n):
        base, rows = plan.a_base[i], plan.a_rows[i]
        h_rows, h_off, h_first = plan.h_rows[i], plan.h_off[i], plan.h_first[i]
        v_rows, v_off, v_first = plan.v_rows[i], plan.v_off[i], plan.v_first[i]
        slots[i, rows : plan.slot] = jnp.zeros((plan.slot - rows, D), BF)
        if rows:
            added = gw[core, base : base + rows].astype(F32) + rgw[base : base + rows].astype(F32)
            slots[i, 0:rows] = added.astype(BF)
        if h_rows or v_rows:
            scratch[...] = jnp.zeros(scratch.shape, F32)
            for half in range(2):
                for j in range(5 if h_rows else 0):
                    cols = slice(D * j + 128 * half, D * j + 128 * half + 128)
                    scratch[half, pl.ds(h_off + j, h_rows, stride=5)] = sums[h_first : h_first + h_rows, cols]
                if v_rows:
                    scratch[half, v_off : v_off + v_rows] = vsum[v_first : v_first + v_rows, 128 * half : 128 * half + 128]
            whole = jnp.concatenate([scratch[0], scratch[1]], 1)
            slots[i, rows : plan.slot] = whole[rows:].astype(BF)


def segment_bounds():
    first = [0] + [(CAT + j * D) * D for j in range(BLOCKS + 1)]
    return list(zip(first, first[1:] + [A_ROWS * D + D * HEADS]))


class Rows:
    def __init__(self, ref):
        self.ref, self.height = ref, ref.shape[0]

    def chunks(self):
        return chunks(self.height)

    def get(self, lo, hi):
        return self.ref[lo:hi]

    def put(self, lo, hi, value):
        self.ref[lo:hi] = value


class Flat:
    def __init__(self, ref, buffer):
        self.ref, self.buffer, self.length = ref, buffer, ref.shape[1]
        self.whole = self.length // 1024 * 8
        self.height = -(-self.length // 1024) * 8

    def chunks(self):
        step = next(s for s in range(64, 0, -8) if self.whole % s == 0)
        return [(lo, lo + step) for lo in range(0, self.whole, step)] + [(self.whole, self.height)]

    def ends(self):
        rows = (self.length - 128 * self.whole) // 128
        return rows, self.length % 128, 128 * self.whole, 128 * (self.whole + rows)

    def get(self, lo, hi):
        if hi <= self.whole:
            return self.ref[0:1, 128 * lo : 128 * hi].reshape(hi - lo, 128)
        rows, lanes, first, last = self.ends()
        self.buffer[...] = jnp.zeros((8, 128), F32)
        if rows:
            self.buffer[0:rows] = self.ref[0:1, first:last].reshape(rows, 128)
        if lanes:
            self.buffer[rows : rows + 1, 0:lanes] = self.ref[0:1, last : self.length]
        return self.buffer[...]

    def put(self, lo, hi, value):
        if hi <= self.whole:
            self.ref[0:1, 128 * lo : 128 * hi] = value.reshape(1, 128 * (hi - lo))
            return
        rows, lanes, first, last = self.ends()
        if rows:
            self.ref[0:1, first:last] = value[0:rows].reshape(1, 128 * rows)
        if lanes:
            self.ref[0:1, last : self.length] = value[rows : rows + 1, 0:lanes]


def update_shard(plan, me, p_ref, m_ref, v_ref, outs, flat, squares, sq_in, push, to_plane, to_z):
    first_out, second_out, new_out, norm_out = outs
    height = p_ref.height
    start = me * plan.length
    correction = 1.0 - 0.5**STEP
    bounds = segment_bounds()

    def place(lo, hi):
        shape = (hi - lo, 128)
        return 128 * lo + 128 * lax.broadcasted_iota(jnp.int32, shape, 0) + lax.broadcasted_iota(jnp.int32, shape, 1)

    for lo, hi in p_ref.chunks():
        spot = place(lo, hi)
        grad = jnp.where(spot < plan.length, flat[lo:hi], 0.0)
        first_new = 0.5 * m_ref.get(lo, hi) + 0.5 * grad
        second_new = 0.5 * v_ref.get(lo, hi) + 0.5 * grad * grad
        first_out.put(lo, hi, first_new)
        second_out.put(lo, hi, second_new)
        decay = jnp.where(spot < bounds[-1][1] - start, 0.01 * p_ref.get(lo, hi), 0.0)
        update = first_new / correction / (jnp.sqrt(second_new / correction) + 1e-06) + decay
        flat[lo:hi] = jnp.where(spot < plan.length, update, 0.0)
        new_out.put(lo, hi, p_ref.get(lo, hi) - 0.5 * update)
    squares[...] = jnp.zeros(squares.shape, F32)

    def each_segment(body):
        for j, (first, last) in enumerate(bounds):
            pl.when((first < start + plan.length) & (last > start))(lambda j=j, first=first, last=last: body(j, first, last))

    def square_sums(j, first, last):
        weight, change = jnp.zeros((8, 128), F32), jnp.zeros((8, 128), F32)
        for lo, hi in p_ref.chunks():
            spot = place(lo, hi)
            inside = (spot >= first - start) & (spot < last - start)
            p, u = jnp.where(inside, p_ref.get(lo, hi), 0.0), jnp.where(inside, flat[lo:hi], 0.0)
            weight = weight + jnp.sum((p * p).reshape(-1, 8, 128), axis=0)
            change = change + jnp.sum((u * u).reshape(-1, 8, 128), axis=0)
        squares[0, j : j + 1] = jnp.sum(weight, axis=0, keepdims=True)
        squares[0, 16 + j : 17 + j] = jnp.sum(change, axis=0, keepdims=True)

    each_segment(square_sums)
    total = squares[0]
    for hop, targets in enumerate((to_plane, to_z)):
        lands = range(3) if hop == 0 else range(3, 3 + len(to_z))
        for c in [push(squares.at[hop], sq_in.at[k], to) for k, to in zip(lands, targets)]:
            c.wait_recv()
        for k in lands:
            total = total + sq_in[k]
        squares[hop + 1] = total
    norm = jnp.sqrt(jnp.sum(total, axis=1, keepdims=True))
    squares[3] = jnp.broadcast_to(norm, (32, 128))
    line = jnp.sqrt(jnp.sum(jnp.concatenate([total, jnp.zeros((96, 128), F32)], 0).T, axis=0, keepdims=True))
    norm_out[0:1] = line[:, 0:MATS]
    norm_out[1:2] = pltpu.roll(line, 112, 1)[:, 0:MATS]

    def scaled(j, first, last):
        ratio = squares[3, j : j + 1] / squares[3, 16 + j : 17 + j]
        for lo, hi in p_ref.chunks():
            spot = place(lo, hi)
            inside = (spot >= first - start) & (spot < last - start)
            new_out.put(lo, hi, jnp.where(inside, p_ref.get(lo, hi) - 0.5 * ratio * flat[lo:hi], new_out.get(lo, hi)))

    each_segment(scaled)


def reduce_kernel(
    plan, gw, gh, gv, st, ig, p_ref, m_ref, v_ref,
    st_out, ig_out, first_out, second_out, new_out, norm_out,
    rgw, rgh, rgv, slots, sums, vsum, scratch, in_d, in_x, in_y, in_z, slot128, flat, rolled, squares, sq_in,
    send, recv, local,
):
    n, rows = plan.n, plan.slot
    depth, cut = n // 4, plan.slot // 2
    core, me, near_x, near_y = neighbours(n)
    near_xy = near_x + near_y - me
    barrier = greet(core, me, near_x, near_y, n)
    pl.semaphore_wait(barrier, depth + 3)
    half = st.shape[1]
    number = iter(range(1 << 20))
    started = []

    def copy(src, dst, to):
        slot = next(number)
        c = pltpu.make_async_remote_copy(
            src_ref=src, dst_ref=dst, send_sem=send.at[slot], recv_sem=recv.at[slot], device_id=to, device_id_type=MESH
        )
        c.start()
        started.append(c)
        return c

    def column(index, k):
        return (index + n - 4 * k) % n

    sibling = at(1 - core, me)
    early = [
        copy(gw.at[1 - core], rgw, sibling),
        copy(gh.at[1 - core], rgh, sibling),
        copy(gv.at[1 - core], rgv, sibling),
    ]
    mine = pl.ds(pl.multiple_of(core * half, half), half)
    late = [
        copy(st.at[1 - core], st_out.at[mine], sibling),
        copy(ig.at[1 - core], ig_out.at[mine], sibling),
    ]
    stay = [
        pltpu.make_async_copy(st.at[core], st_out.at[mine], local.at[0]),
        pltpu.make_async_copy(ig.at[core], ig_out.at[mine], local.at[1]),
    ]
    for c in stay:
        c.start()
    for c in early:
        c.wait_recv()
    pack_slots(plan, core, gw, gh, gv, rgw, rgh, rgv, slots, sums, vsum, scratch)
    order = list(range(1, depth)) + [0]
    to_x, to_y = at(core, near_x), at(core, near_y)
    halves = {}
    for k in order:
        diagonal = column(near_xy, k)
        halves[k] = (
            copy(slots.at[diagonal, pl.ds(0, cut)], in_d.at[k, pl.ds(0, cut)], to_y),
            copy(slots.at[diagonal, pl.ds(cut, rows - cut)], in_d.at[k, pl.ds(cut, rows - cut)], to_x),
        )
    fulls = {}
    for k in order:
        ox, oy = column(near_x, k), column(near_y, k)
        halves[k][0].wait_recv()
        slots[ox, 0:cut] = (slots[ox, 0:cut].astype(F32) + in_d[k, 0:cut].astype(F32)).astype(BF)
        first = copy(slots.at[ox], in_x.at[k], to_x)
        halves[k][1].wait_recv()
        slots[oy, cut:rows] = (slots[oy, cut:rows].astype(F32) + in_d[k, cut:rows].astype(F32)).astype(BF)
        fulls[k] = (first, copy(slots.at[oy], in_y.at[k], to_y))
    along = {}
    for k in order:
        own = column(me, k)
        for c in fulls[k]:
            c.wait_recv()
        if k:
            total = slots[own].astype(F32) + in_x[k].astype(F32) + in_y[k].astype(F32)
            slots[own] = total.astype(BF)
            along[k] = copy(slots.at[own], in_z.at[k], at(core, own))
    for c in along.values():
        c.wait_recv()
    total = slots[me].astype(F32) + in_x[0].astype(F32) + in_y[0].astype(F32)
    for k in along:
        total = total + in_z[k].astype(F32)
    slot128[...] = jnp.zeros(slot128.shape, F32)
    slot128[pl.ds(0, rows, stride=2)] = total[:, 0:128]
    slot128[pl.ds(1, rows, stride=2)] = total[:, 128:D]
    lay_flat(plan, me, slot128, flat, rolled)

    to_z = [at(core, column(me, k)) for k in range(1, depth)]
    outs = (Rows(first_out), Rows(second_out), Rows(new_out), norm_out)
    to_plane = [to_x, to_y, at(core, near_xy)]
    update_shard(plan, me, Rows(p_ref), Rows(m_ref), Rows(v_ref), outs, flat, squares, sq_in, copy, to_plane, to_z)
    for c in late:
        c.wait_recv()
    for c in stay:
        c.wait()
    for c in started:
        c.wait_send()


def reduce_and_update(plan, gw, gh, gv, st, ig, p128, m128, v128):
    n, rows = plan.n, plan.slot
    depth = n // 4
    half = st.shape[1]
    height = p128.shape[0]
    vm = pl.BlockSpec(memory_space=pltpu.VMEM)
    hbm = pl.BlockSpec(memory_space=pl.ANY)
    copies = 5 + 2 * depth + 2 * depth + (depth - 1) + (depth - 1) + 3
    flat32 = jax.ShapeDtypeStruct((height, 128), F32)
    return pl.pallas_call(
        functools.partial(reduce_kernel, plan),
        out_shape=(
            jax.ShapeDtypeStruct((2 * half, D), BF),
            jax.ShapeDtypeStruct((2 * half, D), F32),
            flat32,
            flat32,
            flat32,
            jax.ShapeDtypeStruct((2, MATS), F32),
        ),
        in_specs=[vm] * 3 + [hbm] * 2 + [vm] * 3,
        out_specs=(hbm, hbm, vm, vm, vm, vm),
        scratch_shapes=[
            pltpu.VMEM((A_ROWS, D), BF),
            pltpu.VMEM((D, HPAD), BF),
            pltpu.VMEM(gv.shape[1:], F32),
            pltpu.VMEM((n, rows, D), BF),
            pltpu.VMEM((D, HPAD), F32),
            pltpu.VMEM((40, D), F32),
            pltpu.VMEM((2, rows, 128), F32),
            pltpu.VMEM((depth, rows, D), BF),
            pltpu.VMEM((depth, rows, D), BF),
            pltpu.VMEM((depth, rows, D), BF),
            pltpu.VMEM((depth, rows, D), BF),
            pltpu.VMEM((max(2 * rows, height + 48) + 80, 128), F32),
            pltpu.VMEM((height + 128, 128), F32),
            pltpu.VMEM((height + 40, 128), F32),
            pltpu.VMEM((4, 32, 128), F32),
            pltpu.VMEM((2 + depth, 32, 128), F32),
            pltpu.SemaphoreType.DMA((copies,)),
            pltpu.SemaphoreType.DMA((copies,)),
            pltpu.SemaphoreType.DMA((2,)),
        ],
        compiler_params=pltpu.CompilerParams(
            collective_id=1, has_side_effects=True, vmem_limit_bytes=48 * 1024 * 1024
        ),
    )(gw, gh, gv, st, ig, p128, m128, v128)


class Copies:
    def __init__(self, send, recv):
        self.send, self.recv, self.made, self.sent = send, recv, [], set()

    def add(self, src, dst, to, recv_slot=None, only=None):
        self.made.append((src, dst, to, recv_slot, only))
        return len(self.made) - 1

    def get(self, number):
        src, dst, to, recv_slot, _ = self.made[number]
        return pltpu.make_async_remote_copy(
            src_ref=src(), dst_ref=dst(), send_sem=self.send.at[number],
            recv_sem=self.recv.at[number] if recv_slot is None else recv_slot(),
            device_id=to(), device_id_type=MESH,
        )

    def start(self, *numbers):
        for number in numbers:
            self.get(number).start()

    def arrive(self, *numbers):
        for number in numbers:
            self.get(number).wait_recv()

    def leave(self, *numbers):
        for number in numbers:
            only = self.made[number][4]
            if number not in self.sent and only is None:
                self.get(number).wait_send()
            elif number not in self.sent:
                pl.when(only())(lambda number=number: self.get(number).wait_send())
            self.sent.add(number)


def fused_fits(plan):
    depth, half = plan.n // 4, plan.slot // 2
    plain = [b + plan.slot <= A_ROWS for b, h, v in zip(plan.a_base, plan.h_rows, plan.v_rows) if not (h or v)]
    vectors = [rows for rows in plan.v_rows if rows]
    return (
        all(plain)
        and vectors == [3 * (BLOCKS + 1)]
        and plan.n % 4 == 0
        and half >= 32
        and 4 * half <= HPAD
        and 2 * depth * plan.slot <= (BLOCKS + 1) * D
        and depth == 4
        and max(plan.a_rows) <= plan.slot
    )


def train_kernel(
    plan, x_ref, codes_ref, targets_ref, visits_ref, imp_ref, p_ref, m_ref, v_ref,
    st_out, ig_out, first_out, second_out, new_out, norm_out,
    w, wh, vec, both, away, rw, eye, wt, wht, vt, gsb, xt, mix, xh, gp, rstd, mean, stream, ex, br, dm, acc, lg, dl,
    gw, gh, gv, packed, st_stage, slot128, flat, rolled, vsum, vacc, vin, owned, squares, sq_in, tail,
    send, recv, z_recv, own_recv, local, ready,
):
    n, rows = plan.n, plan.slot
    depth, hrows = n // 4, plan.slot // 2
    cut = hrows // 32 * 16
    core, me, near_x, near_y = neighbours(n)
    near_xy = near_x + near_y - me
    width = both.shape[2]
    params_in, first_new, second_new, new = (Flat(ref, tail) for ref in (p_ref, first_out, second_out, new_out))
    moments = [
        pltpu.make_async_copy(src, dst, local.at[3 + i])
        for i, (src, dst) in enumerate(((m_ref, first_out), (v_ref, second_out)))
    ]
    z_me, j_me = me // 4, me % 4
    copies = Copies(send, recv)
    scratch = [slot128.at[0:rows], slot128.at[rows : 2 * rows]]
    barrier = greet(core, me, near_x, near_y, n, True)
    mine = pl.multiple_of(core * width, width)
    theirs = pl.multiple_of((1 - core) * width, width)
    x_copy = pltpu.make_async_copy(x_ref.at[pl.ds(mine, width)], st_stage.at[0], local.at[0])
    x_copy.start()
    for c in moments:
        c.start()
    for to, half in ((both.at[core], mine), (away, theirs)):
        cols = pl.ds(half, width)
        to[0:1] = codes_ref[:, cols]
        to[1:2] = targets_ref[0, :, cols]
        to[2:6] = visits_ref[:, cols]
        to[6:7] = targets_ref[1, :, cols]
        to[7:8] = targets_ref[2, :, cols]
    height = params_in.height
    for lo, hi in params_in.chunks():
        slot128[lo:hi] = params_in.get(lo, hi)
    place_shard(plan, me, slot128.at[0:height], slot128, flat, rolled)

    spare = (BLOCKS + 1) * D

    def slot_part(t, i, lo, count):
        row = pl.multiple_of(spare + rows * (t * depth + i // 4) + lo, 16)
        return xh.at[pl.ds(row, count), pl.ds(pl.multiple_of((i % 4) * D, D), D)]

    def column(index, k):
        return (index + n - 4 * k) % n

    def sibling():
        return at(1 - core, me)

    def same(make, to):
        return copies.add(make, make, to)

    low = core * hrows
    other_low = (1 - core) * hrows
    order = [0] + sorted(range(1, depth), key=lambda k: (min(k, depth - k), k))
    to_x, to_y, to_d = (lambda: at(core, near_x)), (lambda: at(core, near_y)), (lambda: at(core, near_xy))
    swap_ints = copies.add(lambda: away, lambda: both.at[core], sibling)

    def arrival(t, number):
        return own_recv.at[t * (depth + 2) + number]

    own_targets = [(lambda: near_x), (lambda: near_y)] + [lambda k=k: (me + 4 * k) % n for k in order[1:]]
    own_sends = [copies.add(lambda: slot_part(core, me, 0, rows), lambda: slot_part(core, me, 0, rows), sibling, lambda: arrival(core, 0))]
    for number, target in enumerate(own_targets, 1):
        for h in range(2):
            make = lambda h=h: slot_part(core, me, h * hrows, hrows)
            own_sends.append(
                copies.add(make, make, lambda h=h, target=target: at(h, target()), lambda number=number: arrival(core, number))
            )
    own_sends = own_sends[3 + 2 :] + own_sends[1:5] + own_sends[:1]

    def own_arrive(t, number, make):
        pltpu.make_async_remote_copy(
            src_ref=make(), dst_ref=make(), send_sem=send.at[0], recv_sem=arrival(t, number), device_id=sibling(), device_id_type=MESH
        ).wait_recv()

    gathers = []
    for t in range(2):
        g = {}
        for k in order:
            if k:
                g["x", k] = same(lambda t=t, k=k: slot_part(t, column(me, k), low, hrows), to_x)
                g["y", k] = same(lambda t=t, k=k: slot_part(t, column(me, k), low, hrows), to_y)
            g["d", k] = (
                same(lambda t=t, k=k: slot_part(t, column(near_x, k), low, cut), to_y),
                same(lambda t=t, k=k: slot_part(t, column(near_y, k), low + cut, hrows - cut), to_x),
            )
            g["s", k] = [
                same(lambda t=t, k=k, index=index: slot_part(t, column(index, k), low, hrows), sibling) if index is not me or k else None
                for index in (me, near_x, near_y, near_xy)
            ]
        gathers.append(g)

    def gather_0(t):
        pl.when(core == t)(lambda: copies.start(*own_sends))

    def gather_1(t):
        g = gathers[t]
        for number, k in enumerate(order[1:], 3):
            own_arrive(t, number, lambda: slot_part(t, me, low, hrows))
            copies.start(g["x", k], g["y", k], g["s", k][0])

    def gather_2(t):
        g = gathers[t]
        for k in order:
            if k:
                copies.arrive(g["x", k])
            else:
                own_arrive(t, 1, lambda: slot_part(t, me, low, hrows))
            copies.start(g["d", k][0], g["s", k][1])
            if k:
                copies.arrive(g["y", k])
            else:
                own_arrive(t, 2, lambda: slot_part(t, me, low, hrows))
            copies.start(g["d", k][1], g["s", k][2])

    def gather_3(t):
        g = gathers[t]
        for k in order:
            copies.arrive(*g["d", k])
            copies.start(g["s", k][3])

    def gather_4(t):
        g = gathers[t]
        pl.when(core != t)(lambda: own_arrive(t, 0, lambda: slot_part(t, me, 0, rows)))
        for k in order:
            copies.arrive(*(c for c in g["s", k] if c is not None))

    def unpack(t):
        lg[4 * D : 5 * D, 128:D] = jnp.zeros((D, 128), F32)
        vsum[...] = jnp.zeros(vsum.shape, F32)
        for i in range(n):
            row, lane = spare + rows * (t * depth + i // 4), (i % 4) * D
            unpack_rows(plan, i, xh[row : row + rows, lane : lane + D], w.at[t], lg, vsum, scratch)
        for j in range(5):
            wh[t, :, D * j : D * j + D] = lg[D * j : D * j + D].astype(BF)
        vec[t] = vsum[...].astype(BF)

    total = jnp.sum(imp_ref[...].astype(F32), axis=1, keepdims=True)
    lane_d = lax.broadcasted_iota(jnp.int32, (1, D), 1)
    hi, mid, lo = split3(total)
    left = slot128[pl.ds(0, rows, stride=2)]
    right = slot128[pl.ds(1, rows, stride=2)]
    own = jnp.concatenate([left, right], 1)
    last = jnp.where(lane_d == 0, hi, jnp.where(lane_d == 1, mid, jnp.where(lane_d == 2, lo, 0.0)))
    last_row = lax.broadcasted_iota(jnp.int32, (rows, D), 0) == rows - 1
    slot_part(core, me, 0, rows)[...] = jnp.where(last_row, last, own).astype(BF)
    pl.semaphore_wait(barrier, depth + 3 + 2 + depth - 1)
    gather_0(0)
    copies.start(swap_ints)
    eye[...] = identity(D)
    x_copy.wait()
    for c in range(0, width, CB):
        xt[0, 0:D, c : c + CB] = nt(eye[...], st_stage[0, c : c + CB, :]).astype(BF)
    gather_1(0)
    gather_0(1)
    gather_2(0)
    gather_3(0)
    copies.arrive(swap_ints)
    gather_4(0)
    unpack(0)
    total = jnp.zeros((1, D), F32)
    for i in range(n):
        row, lane = spare + rows * (i // 4), (i % 4) * D
        total = total + xh[row + rows - 16 : row + rows, lane : lane + D].astype(F32)[15:16]
    weight_sum = jnp.sum(jnp.where(lane_d < 3, total, 0.0), axis=1, keepdims=True)
    rw[...] = jnp.broadcast_to(imp_ref[:, pl.ds(mine, width)].astype(F32) / weight_sum, (8, width))

    fwd = (eye, w, wh, vec, wt, vt, gsb, xt, mix, xh, gp, rstd, stream, mean, both, width)

    def during_forward(k):
        pl.when(k == 6)(lambda: gather_2(1))

    def emit_states(t):
        for c in range(0, width, CB):
            st_stage[t, c : c + CB, :] = nt(eye[...], xt[t + 1, 0:D, c : c + CB]).astype(BF)

    gather_1(1)
    forward_tower(0, fwd, during_forward, lambda: gather_3(1))
    gather_4(1)
    copies.leave(*range(len(copies.made)))
    unpack(1)
    forward_tower(1, fwd)
    emit_states(0)
    emit_states(1)
    out_rows = pl.ds(mine, width)
    st_copy = copies.add(lambda: st_stage.at[1 - core], lambda: st_out.at[out_rows], sibling)
    copies.start(st_copy)
    st_stay = pltpu.make_async_copy(st_stage.at[core], st_out.at[out_rows], local.at[1])
    st_stay.start()

    packed_of = [i for i in range(n) if plan.h_rows[i] or plan.v_rows[i]]
    owner = plan.v_rows.index(3 * (BLOCKS + 1))

    early = (2, 3)

    def piece(t, zz, b, lo, count):
        if t == 1 and zz in early:
            arena, first, q = dl, 0, 7 * early.index(zz) + b
        elif t == 1:
            arena, first, q = mix, BLOCKS * (D + 16), 7 * zz + b
        else:
            arena, first, q = xh, spare, 7 * zz + b
        row = pl.multiple_of(first + hrows * (q // 4) + lo, 16)
        return arena.at[pl.ds(row, count), pl.ds(pl.multiple_of((q % 4) * D, D), D)]

    def block(t, zz, b):
        return piece(t, zz, b, 0, hrows)

    def z_in(h, k):
        return st_stage.at[0, pl.ds(pl.multiple_of(hrows * (h * (depth - 1) + k - 1), 16), hrows)]

    def z_out(t, zz):
        if t == 1 and zz in early:
            return st_stage.at[1, pl.ds(hrows * early.index(zz), hrows)]
        return block(t, zz, j_me)

    def slot_half(t, i, lo):
        if i in packed_of:
            return packed.at[packed_of.index(i), pl.ds(pl.multiple_of(lo, 16), hrows)]
        return gw.at[t, pl.ds(pl.multiple_of(plan.a_base[i] + lo, 16), hrows)]

    j_x, j_y, j_d = near_x % 4, near_y % 4, near_xy % 4
    direct = ((0, 0), (0, 1), (0, 2), (1, 2), (1, 3))
    jobs = {}
    for t in range(2):
        for zz in range(depth):
            job = {}
            job["swap"] = [
                copies.add(lambda t=t, i=4 * zz + j: slot_half(t, i, other_low), lambda t=t, zz=zz, j=j: block(t, zz, j), sibling)
                for j in range(4)
            ]
            if (t, zz) in direct:
                job["d"] = [copies.add(lambda t=t, zz=zz: block(t, zz, j_d), lambda t=t, zz=zz: block(t, zz, 4), to_d)]
            else:
                job["d"] = [
                    copies.add(
                        lambda t=t, zz=zz, lo=lo, count=count: piece(t, zz, j_d, lo, count),
                        lambda t=t, zz=zz, lo=lo, count=count: piece(t, zz, 4, lo, count),
                        to,
                    )
                    for to, lo, count in ((to_y, 0, cut), (to_x, cut, hrows - cut))
                ]
            job["x"] = copies.add(lambda t=t, zz=zz: block(t, zz, j_x), lambda t=t, zz=zz: block(t, zz, 5), to_x)
            job["y"] = copies.add(lambda t=t, zz=zz: block(t, zz, j_y), lambda t=t, zz=zz: block(t, zz, 6), to_y)
            job["z"] = copies.add(
                lambda t=t, zz=zz: z_out(t, zz),
                lambda zz=zz: z_in(core, (zz + depth - z_me) % depth),
                lambda t=t, zz=zz: at(t, 4 * zz + j_me),
                lambda zz=zz: z_recv.at[core * depth + (zz + depth - z_me) % depth],
                lambda zz=zz: z_me != zz,
            )
            jobs[t, zz] = job

    def pack(t, planes):
        wanted = [i for i in packed_of if i // 4 in planes]
        for i in wanted:
            a_rows, h_rows, h_off, h_first = plan.a_rows[i], plan.h_rows[i], plan.h_off[i], plan.h_first[i]
            to = packed.at[packed_of.index(i)]
            for part in scratch:
                part[...] = jnp.zeros(part.shape, F32)
            lo16, hi16 = h_first // 16 * 16, -(-(h_first + h_rows) // 16) * 16
            for half in range(2):
                for j in range(5 if h_rows else 0):
                    cols = slice(D * j + 128 * half, D * j + 128 * half + 128)
                    value = gh[t, lo16:hi16, cols].astype(F32)[h_first - lo16 : h_first - lo16 + h_rows]
                    scratch[half][pl.ds(h_off + j, h_rows, stride=5)] = value
            whole = jnp.concatenate([scratch[0][...], scratch[1][...]], 1)
            to[a_rows:rows] = whole[a_rows:].astype(BF)
            if a_rows:
                to[0:a_rows] = gw[t, plan.a_base[i] : plan.a_base[i] + a_rows]

    def plus(*refs):
        value = refs[0][...].astype(F32)
        for ref in refs[1:]:
            value = value + ref[...].astype(F32)
        return value

    def sum_0(t, zz):
        copies.start(*jobs[t, zz]["swap"])

    def sum_1(t, zz):
        job = jobs[t, zz]
        for j in range(4):
            copies.arrive(job["swap"][j])
            target = block(t, zz, j)
            target[...] = plus(slot_half(t, 4 * zz + j, low), target).astype(BF)
        copies.start(*job["d"])
        if (t, zz) in direct:
            copies.start(job["x"], job["y"])

    def sum_2(t, zz):
        job = jobs[t, zz]
        for side, copy, j, lo, count in (("x", job["d"][0], j_x, 0, cut), ("y", job["d"][1], j_y, cut, hrows - cut)):
            copies.arrive(copy)
            target = piece(t, zz, j, lo, count)
            target[...] = plus(target, piece(t, zz, 4, lo, count)).astype(BF)
            copies.start(job[side])

    def sum_3(t, zz):
        job = jobs[t, zz]
        copies.arrive(job["x"], job["y"])
        value = plus(block(t, zz, j_me), block(t, zz, 5), block(t, zz, 6))
        if (t, zz) in direct:
            copies.arrive(*job["d"])
            value = value + block(t, zz, 4)[...].astype(F32)

        @pl.when(z_me != zz)
        def _():
            z_out(t, zz)[...] = value.astype(BF)
            copies.start(job["z"])

        @pl.when((z_me == zz) & (core == t))
        def _():
            final(core)[...] = value

        @pl.when((z_me == zz) & (core != t))
        def _():
            outgo[...] = value
            copies.start(hand_over)

    def sum_4():
        copies.arrive(hand_over)
        for h in range(2):
            for k in range(1, depth):
                src = z_in(h, k)
                pltpu.make_async_remote_copy(
                    src_ref=src, dst_ref=src, send_sem=send.at[0], recv_sem=z_recv.at[h * depth + k], device_id=sibling(), device_id_type=MESH
                ).wait_recv()
                final(h)[...] = final(h)[...] + src[...].astype(F32)

    def final(h):
        return owned.at[h]

    outgo = owned.at[2]

    def vector_step(step):
        sources = [gv.at[1 - core], vacc.at[0], vacc.at[1]]
        along = [lambda k=k: at(core, (me + 4 * k) % n) for k in range(1, depth)]
        targets = [[sibling], [to_x, to_y, to_d], along]
        if step:
            base = gv[core] if step == 1 else vacc[step - 2]
            for number, k in vector_copies[-1]:
                copies.arrive(number)
                base = base + vin[k]
            vacc[step - 1] = base
        if step < 3:
            started = []
            for k, to in enumerate(targets[step], (0, 1, 4)[step]):
                number = copies.add(lambda step=step: sources[step], lambda k=k: vin.at[k], to)
                copies.start(number)
                started.append((number, k))
            vector_copies.append(started)

    vector_copies = []
    hand_over = copies.add(lambda: outgo, lambda: final(core), sibling)
    peers = [(1 - core, me), (core, near_x), (core, near_y), (core, near_xy)] + [(1 - core, (me + 4 * k) % n) for k in range(1, depth)] + [(core, (me + 4 * k) % n) for k in range(1, depth)]

    bwd = (eye, w, wh, vec, wht, vt, gsb, xt, mix, xh, gp, rstd, stream, ex, br, dm, acc, lg, dl, both, rw, gw, gh, gv, dm, width)
    ig_copies = [copies.add(lambda: dm, lambda: ig_out.at[out_rows], sibling, None, lambda t=t: core != t) for t in range(2)]

    def ig_local():
        return pltpu.make_async_copy(dm, ig_out.at[out_rows], local.at[2])

    def emit_inputs(t):
        pl.when(core == t)(lambda: ig_local().start())
        pl.when(core != t)(lambda: copies.start(ig_copies[t]))

    def free_inputs(t):
        pl.when(core == t)(lambda: ig_local().wait())
        pl.when(core != t)(lambda: copies.get(ig_copies[t]).wait_send())

    def signal_ready(which):
        for to_core, to_index in peers:
            pl.semaphore_signal(ready.at[which], inc=1, device_id=at(to_core, to_index), device_id_type=MESH)

    def wait_ready(which):
        pl.semaphore_wait(ready.at[which], len(peers))

    def schedule(i, steps):
        for step in sorted({s[0] for s in steps}):

            def run(step=step):
                for s, f, *args in steps:
                    if s == step:
                        f(*args)

            pl.when(i == step)(run)

    def after_head_1():
        copies.leave(st_copy)
        st_stay.wait()
        signal_ready(0)

    def during_backward_1(i):
        schedule(i, [
            (2, wait_ready, 0), (2, pack, 1, (3,)), (2, sum_0, 1, 3),
            (4, sum_1, 1, 3), (4, pack, 1, (2,)), (4, sum_0, 1, 2),
            (6, sum_1, 1, 2),
            (8, sum_3, 1, 3),
        ])

    ex[...] = jnp.zeros_like(ex)
    backward_tower(1, bwd, after_head_1, during_backward_1, None, lambda: sum_3(1, 2))
    emit_inputs(1)
    signal_ready(1)
    for zz in early:
        job = jobs[1, zz]
        copies.leave(*job["swap"], *job["d"], job["x"], job["y"])

    def after_head_0():
        wait_ready(1)
        sum_0(1, 1)
        sum_0(1, 0)
        pack(0, (3,))
        sum_0(0, 3)

    def during_backward_0(i):
        schedule(i, [
            (1, sum_1, 1, 1), (1, sum_1, 1, 0),
            (2, sum_1, 0, 3),
            (4, sum_2, 1, 1), (4, sum_2, 1, 0), (4, pack, 0, (2,)), (4, sum_0, 0, 2),
            (5, sum_2, 0, 3),
            (6, sum_1, 0, 2),
            (8, sum_3, 1, 1), (8, sum_3, 1, 0), (8, sum_0, 0, 1),
            (9, sum_3, 0, 3), (9, sum_1, 0, 1),
        ])

    def after_weights():
        sum_0(0, 0)
        vector_step(0)

    backward_tower(0, bwd, after_head_0, during_backward_0, lambda: free_inputs(1), after_weights)
    emit_inputs(0)
    sum_1(0, 0)
    vector_step(1)
    sum_3(0, 2)
    sum_3(0, 1)
    sum_3(0, 0)
    vector_step(2)
    sum_4()
    vector_step(3)

    slot128[...] = jnp.zeros(slot128.shape, F32)
    for h in range(2):
        slot128[pl.ds(2 * hrows * h, hrows, stride=2)] = final(h)[:, 0:128]
        slot128[pl.ds(2 * hrows * h + 1, hrows, stride=2)] = final(h)[:, 128:D]

    @pl.when(me == owner)
    def _():
        for kind in range(3):
            first = 2 * (plan.v_off[owner] + kind * (BLOCKS + 1))
            for h in range(2):
                value = vacc[2, kind, 0 : BLOCKS + 1, 128 * h : 128 * h + 128]
                slot128[pl.ds(first + h, BLOCKS + 1, stride=2)] = value

    def push(src, dst, to):
        number = copies.add(lambda: src, lambda: dst, lambda: to)
        copies.start(number)
        return copies.get(number)

    lay_flat(plan, me, slot128, flat, rolled)
    for c in moments:
        c.wait()
    update_shard(
        plan, me, params_in, first_new, second_new, (first_new, second_new, new, norm_out),
        flat, squares, sq_in, push, [to_x(), to_y(), to_d()], [at(core, (me + 4 * k) % n) for k in range(1, depth)],
    )
    copies.arrive(st_copy)
    pl.when(core == 0)(lambda: copies.arrive(ig_copies[0]))
    pl.when(core == 1)(lambda: copies.arrive(ig_copies[1]))
    free_inputs(0)
    copies.sent.update(ig_copies)
    copies.leave(*range(len(copies.made)))


def finish_kernel(st, ig, first, second, new, norms, st_out, ig_out, first_out, second_out, new_out, low_out, norms_out, *rest):
    *held, into, outof = rest
    moves = []
    for src, dst, mid, parts in zip((new, ig, st, first, second), (new_out, ig_out, st_out, first_out, second_out), held, (1, 4, 2, 1, 1)):
        rows = src.shape[0] // parts
        for i in range(parts):
            at_rows = pl.ds(i * rows, rows)
            number = len(moves)
            moves.append(
                (
                    pltpu.make_async_copy(src.at[at_rows], mid.at[at_rows], into.at[number]),
                    pltpu.make_async_copy(mid.at[at_rows], dst.at[at_rows], outof.at[number]),
                )
            )
    for load, _ in moves:
        load.start()
    for load, store in moves:
        load.wait()
        store.start()
    size = new.shape[1]
    for lo in range(0, size, 8192):
        hi = min(lo + 8192, size)
        low_out[0:1, lo:hi] = held[0][0:1, lo:hi].astype(BF)
    norms_out[...] = norms[...]
    for _, store in moves:
        store.wait()


def finish(st, ig, first, second, new, norms):
    vm = pl.BlockSpec(memory_space=pltpu.VMEM)
    hbm = pl.BlockSpec(memory_space=pl.ANY)
    arrays = (st, ig, first, second, new)
    shapes = [jax.ShapeDtypeStruct(v.shape, v.dtype) for v in arrays]
    return pl.pallas_call(
        finish_kernel,
        out_shape=(*shapes, jax.ShapeDtypeStruct(new.shape, BF), jax.ShapeDtypeStruct(norms.shape, F32)),
        in_specs=[hbm] * 5 + [vm],
        out_specs=(hbm,) * 5 + (vm,) * 2,
        scratch_shapes=[pltpu.VMEM(v.shape, v.dtype) for v in (new, ig, st, first, second)] + [pltpu.SemaphoreType.DMA((9,))] * 2,
        compiler_params=pltpu.CompilerParams(vmem_limit_bytes=62 * 1024 * 1024),
    )(st, ig, first, second, new, norms)


def train(plan, latent, codes, targets, visits, imp, params, first, second):
    n, rows = plan.n, plan.slot
    depth, hrows = n // 4, rows // 2
    width = codes.shape[1] // 2
    height = -(-params.shape[1] // 1024) * 8
    vm = pl.BlockSpec(memory_space=pltpu.VMEM)
    hbm = pl.BlockSpec(memory_space=pl.ANY)
    packed = sum(1 for h, v in zip(plan.h_rows, plan.v_rows) if h or v)
    return pl.pallas_call(
        functools.partial(train_kernel, plan),
        out_shape=(
            jax.ShapeDtypeStruct((2 * width, D), BF),
            jax.ShapeDtypeStruct((2 * width, D), F32),
            jax.ShapeDtypeStruct(params.shape, F32),
            jax.ShapeDtypeStruct(params.shape, F32),
            jax.ShapeDtypeStruct(params.shape, F32),
            jax.ShapeDtypeStruct((2, MATS), F32),
        ),
        in_specs=[hbm] + [vm] * 5 + [hbm] * 2,
        out_specs=(hbm, hbm, vm, vm, vm, vm),
        scratch_shapes=[
            pltpu.VMEM((2, A_ROWS, D), BF),
            pltpu.VMEM((2, D, HPAD), BF),
            pltpu.VMEM((2, 128, D), BF),
            pltpu.VMEM((2, 8, width), jnp.int32),
            pltpu.VMEM((8, width), jnp.int32),
            pltpu.VMEM((8, width), F32),
            *work_scratch(width),
            pltpu.VMEM((2, A_ROWS, D), BF),
            pltpu.VMEM((2, D, HPAD), BF),
            pltpu.VMEM((2, 3, 16, D), F32),
            pltpu.VMEM((packed, rows, D), BF),
            pltpu.VMEM((2, width, D), BF),
            pltpu.VMEM((max(2 * rows, height + 48) + 80, 128), F32),
            pltpu.VMEM((height + 128, 128), F32),
            pltpu.VMEM((height + 40, 128), F32),
            pltpu.VMEM((128, D), F32),
            pltpu.VMEM((3, 3, 16, D), F32),
            pltpu.VMEM((3 + depth, 3, 16, D), F32),
            pltpu.VMEM((3, hrows, D), F32),
            pltpu.VMEM((4, 32, 128), F32),
            pltpu.VMEM((2 + depth, 32, 128), F32),
            pltpu.VMEM((8, 128), F32),
            pltpu.SemaphoreType.DMA((11 * n,)),
            pltpu.SemaphoreType.DMA((11 * n,)),
            pltpu.SemaphoreType.DMA((2 * depth,)),
            pltpu.SemaphoreType.DMA((2 * (depth + 2),)),
            pltpu.SemaphoreType.DMA((5,)),
            pltpu.SemaphoreType.REGULAR((2,)),
        ],
        compiler_params=pltpu.CompilerParams(
            collective_id=2, has_side_effects=True, vmem_limit_bytes=63 * 1024 * 1024
        ),
    )(latent, codes, targets, visits, imp, params, first, second)


def on_device(latent, codes, targets, visits, importance, params, first_moment, second_moment):
    me = lax.axis_index("tower")
    row_count = latent.shape[0]
    half = row_count // 2
    shard_len = params.shape[1]
    plan = Plan(lax.axis_size("dp"), shard_len)
    if fused_fits(plan):
        states_out, inputs_out, first, second, new, norms = train(
            plan, latent, codes, targets.transpose(1, 0, 2), visits[0].T, importance[None], params, first_moment, second_moment
        )
        states_out, inputs_out, first, second, new, low, norms = finish(states_out, inputs_out, first, second, new, norms)
    else:
        height = -(-plan.rows128 // 8) * 8
        p128, m128, v128 = (
            jnp.pad(v, ((0, 0), (0, 128 * height - shard_len))).reshape(height, 128)
            for v in (params, first_moment, second_moment)
        )
        ints = jnp.concatenate([codes, targets[0, :1], visits[0].T, targets[0, 1:]], 0)
        x = lax.dynamic_slice_in_dim(latent, me * half, half, 0)
        w, wh, vec, both, rw = gather(plan, p128, ints, importance[None])
        st, ig, gw, gh, gv = compute(x, both, rw, w, wh, vec)
        states_out, inputs_out, *flat, norms = reduce_and_update(plan, gw, gh, gv, st, ig, p128, m128, v128)
        first, second, new = (v.reshape(1, -1)[:, :shard_len] for v in flat)
        low = new.astype(BF)
    return (states_out[None], inputs_out[None], first, second, new, low, norms[None])


def solution(mesh):
    in_specs = (
        P("dp", None),
        P("tower", "dp"),
        P("tower", None, "dp"),
        P("tower", "dp", None),
        P("dp"),
        P("tower", "dp"),
        P("tower", "dp"),
        P("tower", "dp"),
    )
    out_specs = (
        P("tower", "dp", None),
        P("tower", "dp", None),
        P("tower", "dp"),
        P("tower", "dp"),
        P("tower", "dp"),
        P("tower", "dp"),
        P("tower", None, None),
    )
    return jax.shard_map(
        on_device, mesh=mesh, in_specs=in_specs, out_specs=out_specs, check_vma=False
    )
```

```python
import functools

import jax
import jax.numpy as jnp
from jax import lax
from jax.experimental import pallas as pl
from jax.experimental.pallas import tpu as pltpu
from jax.sharding import PartitionSpec as P

D = 256
CODES = 32
BINS = 601
BLOCKS = 10
STEP = 5
HEADS = 1238
MATS = 12
P_SIZE = 1054464
HPAD = 1280
CAT = D + CODES
A_ROWS = CAT + BLOCKS * D
BF = jnp.bfloat16
F32 = jnp.float32
GELU_C = 0.7978845608028654
GELU_K = 0.044715


def nn(a, b):
    return jnp.dot(a, b, preferred_element_type=F32)


def nt(a, b):
    return lax.dot_general(a, b, (((1,), (1,)), ((), ())), preferred_element_type=F32)


def identity(n):
    return (lax.broadcasted_iota(jnp.int32, (n, n), 0) == lax.broadcasted_iota(jnp.int32, (n, n), 1)).astype(BF)


ZETA = (GELU_C * GELU_K) ** (1.0 / 3.0)
B0 = GELU_C / ZETA
E0 = 0.5 / ZETA


def wide(v, cs):
    return jnp.concatenate([v] * ((cs.stop - cs.start) // v.shape[1]), 1)


def norm_act(src, cs, gs, unit, gp, rstd, out):
    for r in range(0, D, 32):
        rs = slice(r, r + 32)
        xh = src[rs, cs] * rstd
        z = xh * wide(gs[rs, 0:128], cs) + wide(gs[rs, 128:256], cs)
        z2 = z * z
        t = jnp.tanh(z * (z2 + B0))
        q = t * E0 + E0
        a = z * q
        out(rs, a)
        unit[rs, cs] = xh.astype(BF)
        gp[rs, cs] = (q + (a * (1.0 - t)) * (z2 * 3.0 + B0)).astype(BF)


def broadcast_vectors(vt, rows):
    k = lax.broadcasted_iota(jnp.int32, (128, 128), 0)
    picks = jnp.concatenate([(k == row).astype(BF) for row in rows], 1)
    return nn(vt, picks)


def head_stage(cs, lg, dl, ints, rw):
    width = rw.shape[1]
    it8 = lax.broadcasted_iota(jnp.int32, (8, width), 0)
    low = -jnp.inf
    b75, b150, b154 = lg[600:608], lg[1200:1208], lg[1232:1240]

    def top(block):
        return jnp.max(block, axis=0, keepdims=True)

    def steps(lo, hi, step):
        return [(r, min(r + step, hi)) for r in range(lo, hi, step)]

    def folded(value):
        return value.reshape(-1, 8, width)

    def top_range(lo, hi):
        best = None
        for r, end in steps(lo, hi, 40):
            part = jnp.max(folded(lg[r:end]), axis=0)
            best = part if best is None else jnp.maximum(best, part)
        return best

    max_v = top(jnp.maximum(top_range(0, 600), jnp.where(it8 < 1, b75, low)))
    max_r = top(
        jnp.maximum(
            jnp.maximum(top_range(608, 1200), jnp.where(it8 >= 1, b75, low)),
            jnp.where(it8 < 2, b150, low),
        )
    )
    max_c = top(
        jnp.maximum(
            jnp.maximum(top_range(1208, 1232), jnp.where(it8 >= 2, b150, low)),
            jnp.where(it8 < 2, b154, low),
        )
    )
    in_policy = (it8 >= 2) & (it8 < 6)
    max_p = top(jnp.where(in_policy, b154, low))

    def exp_range(lo, hi, best):
        acc = jnp.zeros((8, width), F32)
        for r, end in steps(lo, hi, 40):
            e = jnp.exp(lg[r:end] - best)
            lg[r:end] = e
            acc = acc + jnp.sum(folded(e), axis=0)
        return acc

    e75 = jnp.exp(b75 - jnp.where(it8 < 1, max_v, max_r))
    e150 = jnp.exp(b150 - jnp.where(it8 < 2, max_r, max_c))
    e154 = jnp.exp(b154 - jnp.where(it8 < 2, max_c, max_p))

    def total(acc):
        return rw / jnp.sum(acc, axis=0, keepdims=True)

    inv_v = total(exp_range(0, 600, max_v) + jnp.where(it8 < 1, e75, 0.0))
    inv_r = total(exp_range(608, 1200, max_r) + jnp.where(it8 >= 1, e75, 0.0) + jnp.where(it8 < 2, e150, 0.0))
    inv_c = total(exp_range(1208, 1232, max_c) + jnp.where(it8 >= 2, e150, 0.0) + jnp.where(it8 < 2, e154, 0.0))
    inv_p = total(jnp.where(in_policy, e154, 0.0))
    hit_v = ints[1:2]
    hit_r = ints[6:7] + BINS
    hit_c = ints[7:8] + 2 * BINS
    counts = jnp.where(in_policy, ints.astype(F32), 0.0)
    share = counts * (rw / jnp.sum(counts, axis=0, keepdims=True))

    def minus(value, lo, *hits):
        at = lax.broadcasted_iota(jnp.int32, value.shape, 0)
        for hit in hits:
            value = value - jnp.where(at == hit - lo, rw, 0.0)
        return value

    d75 = minus(e75 * jnp.where(it8 < 1, inv_v, inv_r), 600, hit_v, hit_r)
    d150 = minus(e150 * jnp.where(it8 < 2, inv_r, inv_c), 1200, hit_r, hit_c)
    d154 = minus(e154 * jnp.where(it8 < 2, inv_c, inv_p), 1232, hit_c) - share
    d154 = jnp.where(it8 < 6, d154, 0.0)

    def emit(lo, hi, inv, hit):
        for r, end in steps(lo, hi, 80):
            dl[r:end, cs] = minus(lg[r:end] * inv, r, hit).astype(BF)

    def pair(first, second):
        return jnp.concatenate([first, second], 0).astype(BF)

    emit(0, 592, inv_v, hit_v)
    dl[592:608, cs] = pair(minus(lg[592:600] * inv_v, 592, hit_v), d75)
    emit(608, 1200, inv_r, hit_r)
    dl[1200:1216, cs] = pair(d150, minus(lg[1208:1216] * inv_c, 1208, hit_c))
    emit(1216, 1232, inv_c, hit_c)
    dl[1232:1248, cs] = pair(d154, jnp.zeros_like(d154))
    dl[1248:HPAD, cs] = jnp.zeros((HPAD - 1248, width), BF)


CB = 256
GROUP = 2


def saved_views(t, mix, xh):
    def mixed(k):
        return mix.at[pl.ds(pl.multiple_of((t * BLOCKS + k - 1) * (D + 16), 16), D + 16)]

    def unit(k):
        return xh.at[pl.ds(pl.multiple_of((t * (BLOCKS + 1) + k) * D, D), D)]

    return mixed, unit


def column_groups(width):
    blocks = [slice(c, c + CB) for c in range(0, width, CB)]
    per = min(GROUP, len(blocks))
    return blocks, per, [slice(c, c + per * CB) for c in range(0, width, per * CB)]


def forward_tower(t, refs, during=None, before_last=None):
    (eye, w, wh, vec, wt, vt, gsb, xt, mix, xh, gp, rstd, stream, mean, ints, width) = refs
    blocks, per, groups = column_groups(width)
    mixed, unit = saved_views(t, mix, xh)
    first_bias = 2 * (BLOCKS + 1)
    ones = jnp.ones((16, D), BF)

    def mean_rows(slot):
        value = nn(ones, wt[slot, 0:D])[0:8] * (1.0 / D)
        high = value.astype(BF).astype(F32)
        wt[slot, D : D + 16] = jnp.concatenate([high, value - high], 0).astype(BF)

    def vectors(k):
        gsb[k % 2] = broadcast_vectors(vt[...], (k, k + BLOCKS + 1)) * ZETA

    def prefetch(k):
        vectors(k)
        row = pl.multiple_of(CAT + jnp.minimum(k - 1, BLOCKS - 1) * D, 32)
        wt[k % 2, 0:D, 0:D] = nt(eye[...], w[t, pl.ds(row, D)]).astype(BF)
        at_row = lax.broadcasted_iota(jnp.int32, (128, 128), 0) == k + first_bias
        at_lane = lax.broadcasted_iota(jnp.int32, (128, 128), 1) == 0
        wt[k % 2, 0:D, D:384] = nn(vt[...], (at_row & at_lane).astype(BF)).astype(BF)
        mean_rows(k % 2)

    def row_of(k):
        return pl.ds(t * (BLOCKS + 1) + k, 1)

    def stage(k, c):
        def keep(rs, a):
            mixed(k)[rs, blocks[c]] = a.astype(BF)

        norm_act(stream, blocks[c], gsb.at[k % 2], unit(k), gp.at[t, k], rstd[row_of(k), blocks[c]], keep)

    def spread(square, k, cs):
        var = jnp.sum(square, axis=0, keepdims=True) * (1.0 / D)
        rstd[row_of(k), cs] = lax.rsqrt(var + 1e-05)

    def add(k, cs, out, fresh):
        shift = out[D : D + 1] + out[D + 8 : D + 9]
        square = jnp.zeros((8, out.shape[1]), F32)
        for r in range(0, D, 32):
            value = out[r : r + 32] - shift
            if not fresh:
                value = stream[r : r + 32, cs] + value
            stream[r : r + 32, cs] = value
            square = square + jnp.sum((value * value).reshape(4, 8, -1), axis=0)
        if not fresh:
            mean[0:1, cs] = mean[0:1, cs] + shift
        spread(square, k + 1, cs)

    def centre(cs):
        total = jnp.zeros((8, CB), F32)
        for r in range(0, D, 32):
            total = total + jnp.sum(stream[r : r + 32, cs].reshape(4, 8, -1), axis=0)
        middle = jnp.sum(total, axis=0, keepdims=True) * (1.0 / D)
        mean[0:1, cs] = middle
        square = jnp.zeros((8, CB), F32)
        for r in range(0, D, 32):
            value = stream[r : r + 32, cs] - middle
            stream[r : r + 32, cs] = value
            square = square + jnp.sum((value * value).reshape(4, 8, -1), axis=0)
        spread(square, 1, cs)

    vt[...] = nt(eye[...], vec[t]).astype(BF)
    vectors(0)
    wt[0, 0:D, 0:D] = nt(eye[...], w[t, 0:D]).astype(BF)
    tile = first_bias // 16 * 16
    picked = lax.broadcasted_iota(jnp.int32, (16, D), 0) == first_bias - tile
    bias = jnp.where(picked, vec[t, tile : tile + 16].astype(F32), 0.0).astype(BF)
    rest = jnp.concatenate([w[t, D:CAT], bias, jnp.zeros((128 - CODES - 16, D), BF)], 0)
    wt[0, 0:D, D:384] = nt(eye[...], rest).astype(BF)
    mean_rows(0)
    for cs in blocks:
        it = lax.broadcasted_iota(jnp.int32, (CODES, CB), 0)
        xt[t, D:CAT, cs] = (it == ints[t, 0:1, cs]).astype(BF)
        xt[t, CAT : CAT + 16, cs] = jnp.ones((16, CB), BF)
    first = [nn(wt[0, :, 0 : CAT + 16], xt[t, :, cs]) for cs in groups]
    prefetch(1)
    for group, cs in enumerate(groups):
        add(-1, cs, first[group], True)
    for cs in blocks:

        def keep(rs, a):
            stream[rs, cs] = a

        norm_act(stream, cs, gsb.at[0], unit(0), gp.at[t, 0], rstd[row_of(0), cs], keep)
        centre(cs)

    def layer(k, more):
        mixed(k)[D : D + 16, :] = jnp.ones((16, width), BF)
        for group, cs in enumerate(groups):
            out = nn(wt[k % 2, :, 0 : D + 16], mixed(k)[:, cs])
            ahead = group + 1 < len(groups)
            if ahead or more:
                for c in range(per):
                    stage(k if ahead else k + 1, (group + 1) % len(groups) * per + c)
            add(k, cs, out, False)
        if more:
            prefetch(k + 2)

    prefetch(2)
    for c in range(per):
        stage(1, c)

    @pl.loop(1, BLOCKS)
    def _(k):
        if during is not None:
            during(k)
        layer(k, True)

    if before_last is not None:
        before_last()
    layer(BLOCKS, False)
    for cs in blocks:
        xt[t + 1, 0:D, cs] = (stream[:, cs] + mean[0:1, cs]).astype(BF)


def backward_tower(t, refs, after_head=None, during=None, before_product=None, after_weights=None):
    (eye, w, wh, vec, wht, vt, gsb, xt, mix, xh, gp, rstd, ds, ex, br, dm, acc, lg, dl, ints, rw, gw, gh, gv, ig, width) = refs
    blocks = [slice(c, c + CB) for c in range(0, width, CB)]
    last = len(blocks) - 1
    mixed, unit = saved_views(t, mix, xh)
    vt[...] = nt(eye[...], vec[t]).astype(BF)
    for h in range(0, HPAD, D):
        wht[h : h + D, :] = nt(eye[...], wh[t, :, h : h + D]).astype(BF)

    def softmax_block(c):
        cs = pl.ds(pl.multiple_of(c * CB, CB), CB)
        lg[...] = nn(wht[...], xt[t + 1, 0:D, cs])
        return cs

    def states_block(c):
        cs = pl.ds(pl.multiple_of(c * CB, CB), CB)
        return cs, nn(wh[t], dl[:, cs])

    def keep_states(cs, product):
        value = product + ex[:, cs]
        ds[:, cs] = value
        br[BLOCKS % 2, :, cs] = value.astype(BF)

    cs = softmax_block(0)
    head_stage(cs, lg, dl, ints[t, :, cs], rw[0:1, cs])

    @pl.loop(1, width // CB)
    def _(c):
        cs = softmax_block(c)
        before, product = states_block(c - 1)
        head_stage(cs, lg, dl, ints[t, :, cs], rw[0:1, cs])
        keep_states(before, product)

    keep_states(*states_block(width // CB - 1))
    for h in range(0, HPAD, D):
        gh[t, :, h : h + D] = nt(xt[t + 1, 0:D, :], dl[h : h + D]).astype(BF)
    if after_head is not None:
        after_head()
    acc[...] = jnp.zeros(acc.shape, F32)
    ones = jnp.ones((16, 128), BF)

    def part(c):
        return dm.at[c * D : c * D + D]

    def gains(k):
        gsb[k % 2, :, 0:128] = broadcast_vectors(vt[...], (k,)) * ZETA

    def row_sums(k):
        for kind in range(2):
            gv[t, kind, pl.ds(k, 1), :] = nt(ones, acc[k % 2, kind].astype(BF))[0:1] * ZETA
        acc[k % 2] = jnp.zeros(acc.shape[1:], F32)

    def product(k, c):
        row = pl.multiple_of(CAT + (k - 1) * D, 32)
        part(c)[...] = nn(w[t, pl.ds(row, D)], br[k % 2, :, blocks[c]])

    def slopes(k, c):
        cs, grad, sums = blocks[c], part(c), acc.at[k % 2]
        s1 = jnp.zeros((8, CB), F32)
        s2 = jnp.zeros((8, CB), F32)
        for r in range(0, D, 32):
            rs = slice(r, r + 32)
            g = wide(gsb[k % 2, rs, 0:128], cs)
            dy = grad[rs, :] * gp[t, k, rs, cs].astype(F32)
            prod = dy * unit(k)[rs, cs].astype(F32)
            back = dy * g
            grad[rs, :] = back
            s1 = s1 + jnp.sum(back.reshape(4, 8, CB), axis=0)
            s2 = s2 + jnp.sum((prod * g).reshape(4, 8, CB), axis=0)
            sums[0, rs] = sums[0, rs] + (prod[:, 0:128] + prod[:, 128:CB])
            sums[1, rs] = sums[1, rs] + (dy[:, 0:128] + dy[:, 128:CB])
        return [jnp.sum(s, axis=0, keepdims=True) * (1.0 / D) for s in (s1, s2)]

    def stage(k, c, first):
        cs = blocks[c]
        means = slopes(k, c)
        scale = rstd[pl.ds(t * (BLOCKS + 1) + k, 1), cs]
        m1, m2 = (jnp.broadcast_to(m * scale, (32, CB)).astype(BF) for m in means)
        for r in range(0, D, 32):
            rs = slice(r, r + 32)
            back = part(c)[rs, :] * scale - (m1 + unit(k)[rs, cs] * m2).astype(F32)
            if first:
                br[0, rs, cs] = back.astype(BF)
            else:
                value = ds[rs, cs] + back
                ds[rs, cs] = value
                br[(k + 1) % 2, rs, cs] = value.astype(BF)

    if before_product is not None:
        before_product()
    gains(BLOCKS)
    gains(BLOCKS - 1)
    product(BLOCKS, 0)

    @pl.loop(0, BLOCKS)
    def _(i):
        k = BLOCKS - i
        if during is not None:
            during(i)
        for c in range(last + 1):
            if c < last:
                product(k, c + 1)
            stage(k, c, False)
            if c == 0:
                full = nt(mixed(k)[...], br[k % 2])
                row = pl.multiple_of(CAT + (k - 1) * D, 32)
                gw[t, pl.ds(row, D), :] = full[0:D].astype(BF)
                gv[t, 2, pl.ds(k, 1), :] = full[D : D + 1]
                product(k - 1, 0)
        gains(k - 2)
        row_sums(k)

    for c, cs in enumerate(blocks):
        part(c)[...] = ds[:, cs]
        stage(0, c, True)
    full = nt(xt[t], br[0])
    gw[t, 0:CAT, :] = full[0:CAT].astype(BF)
    gv[t, 2, 0:1, :] = full[CAT : CAT + 1]
    row_sums(0)
    if after_weights is not None:
        after_weights()
    for cs in blocks:
        back = nn(w[t, 0:D], br[0, :, cs])
        ex[:, cs] = back
        ig[cs, :] = back.T


def compute_kernel(x_ref, ints, rw, w, wh, vec, st, ig, gw, gh, gv, eye, wt, wht, vt, gsb, xt, mix, xh, gp, rstd, mean, stream, ex, br, dm, acc, lg, dl):
    width = x_ref.shape[0]
    eye[...] = identity(D)
    for c in range(0, width, CB):
        cs = slice(c, c + CB)
        xt[0, 0:D, cs] = nt(eye[...], x_ref[cs, :]).astype(BF)
    fwd = (eye, w, wh, vec, wt, vt, gsb, xt, mix, xh, gp, rstd, stream, mean, ints, width)
    @pl.loop(0, 2)
    def _(t):
        forward_tower(t, fwd)

        @pl.loop(0, width // CB)
        def _(c):
            cs = pl.ds(pl.multiple_of(c * CB, CB), CB)
            st[t, cs, :] = nt(eye[...], xt[t + 1, 0:D, cs]).astype(BF)

    ex[...] = jnp.zeros_like(ex)

    @pl.loop(0, 2)
    def _(i):
        t = 1 - i
        backward_tower(
            t,
            (eye, w, wh, vec, wht, vt, gsb, xt, mix, xh, gp, rstd, stream, ex, br, dm, acc, lg, dl, ints, rw, gw, gh, gv, ig.at[t], width),
        )


def work_scratch(width):
    return [
        pltpu.VMEM((D, D), BF),
        pltpu.VMEM((2, D + 16, 384), BF),
        pltpu.VMEM((HPAD, D), BF),
        pltpu.VMEM((D, 128), BF),
        pltpu.VMEM((2, D, 256), F32),
        pltpu.VMEM((3, CAT + 16, width), BF),
        pltpu.VMEM((2 * BLOCKS * (D + 16), width), BF),
        pltpu.VMEM((2 * (BLOCKS + 1) * D, width), BF),
        pltpu.VMEM((2, BLOCKS + 1, D, width), BF),
        pltpu.VMEM((24, width), F32),
        pltpu.VMEM((8, width), F32),
        pltpu.VMEM((D, width), F32),
        pltpu.VMEM((D, width), F32),
        pltpu.VMEM((2, D, width), BF),
        pltpu.VMEM((width // CB * D, CB), F32),
        pltpu.VMEM((2, 2, D, 128), F32),
        pltpu.VMEM((HPAD, CB), F32),
        pltpu.VMEM((HPAD, width), BF),
    ]


def compute(x, ints, rw, w, wh, vec):
    width = x.shape[0]
    vm = pl.BlockSpec(memory_space=pltpu.VMEM)
    return pl.pallas_call(
        compute_kernel,
        out_shape=(
            jax.ShapeDtypeStruct((2, width, D), BF),
            jax.ShapeDtypeStruct((2, width, D), F32),
            jax.ShapeDtypeStruct((2, A_ROWS, D), BF),
            jax.ShapeDtypeStruct((2, D, HPAD), BF),
            jax.ShapeDtypeStruct((2, 3, 16, D), F32),
        ),
        in_specs=[vm] * 6,
        out_specs=(vm,) * 5,
        scratch_shapes=work_scratch(width),
        compiler_params=pltpu.CompilerParams(vmem_limit_bytes=62 * 1024 * 1024),
    )(x, ints, rw, w, wh, vec)


class Plan:
    def __init__(self, n, length):
        self.n, self.length = n, length
        self.rows128 = -(-length // 128)
        block_end, head_end = A_ROWS * D, A_ROWS * D + D * HEADS
        self.a_base, self.a_rows, self.h_first, self.h_rows, self.h_off, self.v_first, self.v_rows, self.v_off = ([] for _ in range(8))
        used = 0
        for i in range(n):
            lo, hi = i * length, (i + 1) * length
            base = min(lo, block_end) // D // 16 * 16
            top = -(-min(hi, block_end) // D)
            a_rows = -(-(top - base) // 16) * 16 if lo < block_end else 0
            first = min(max(lo - block_end, 0), D * HEADS) // HEADS
            last = -(-min(max(hi - block_end, 0), D * HEADS) // HEADS)
            h_rows = last - first if hi > block_end and lo < head_end else 0
            v_first = max(lo - head_end, 0) // D
            v_rows = -(-(hi - head_end) // D) - v_first if hi > head_end else 0
            self.a_base.append(base)
            self.a_rows.append(a_rows)
            self.h_first.append(first)
            self.h_rows.append(h_rows)
            self.h_off.append(a_rows)
            self.v_first.append(v_first)
            self.v_rows.append(v_rows)
            self.v_off.append(a_rows + 5 * h_rows)
            used = max(used, a_rows + 5 * h_rows + v_rows)
        self.heads = max(self.h_rows)
        self.image = (HEADS * self.heads // 128 + 24) // 8 * 8
        self.slot = -(-(used + 1) // 32) * 32

    def at(self, table, me):
        value = jnp.int32(table[0])
        for i in range(1, self.n):
            if table[i] != table[i - 1]:
                value = value + (me >= i).astype(jnp.int32) * (table[i] - table[i - 1])
        return value


MESH = pl.DeviceIdType.MESH


def neighbours(n):
    core = lax.axis_index("tower")
    me = lax.axis_index("dp")
    near_x = me + 1 - 2 * (me % 2)
    near_y = me + 2 - 4 * ((me // 2) % 2)
    return core, me, near_x, near_y


def at(core, index):
    return {"tower": core, "dp": index}


def greet(core, me, near_x, near_y, n, crossed=False):
    barrier = pltpu.get_barrier_semaphore()
    pl.semaphore_signal(barrier, inc=1, device_id=at(1 - core, me), device_id_type=MESH)
    for near in (near_x, near_y, near_x + near_y - me):
        pl.semaphore_signal(barrier, inc=1, device_id=at(core, near), device_id_type=MESH)
    for k in range(1, n // 4):
        pl.semaphore_signal(barrier, inc=1, device_id=at(core, (me + 4 * k) % n), device_id_type=MESH)
    for near in [near_x, near_y] + [(me + 4 * k) % n for k in range(1, n // 4)] if crossed else []:
        pl.semaphore_signal(barrier, inc=1, device_id=at(1 - core, near), device_id_type=MESH)
    return barrier


def place_shard(plan, me, p_ref, slot128, shifted, rolled):
    rows = plan.rows128
    start = me * plan.length
    shift = start % 128
    first = start // 128
    tall = shifted.shape[0]
    height = p_ref.shape[0]
    lane = lax.broadcasted_iota(jnp.int32, (height, 128), 1)
    rolled[0:8] = jnp.zeros((8, 128), F32)
    rolled[8 : 8 + height] = pltpu.roll(p_ref[...], shift, 1)
    shifted[...] = jnp.zeros((tall, 128), F32)
    moved = jnp.where(lane >= shift, rolled[8 : 8 + height], rolled[7 : 7 + height])
    shifted[16 : 16 + height] = moved
    slot128[...] = jnp.zeros(slot128.shape, F32)
    row = lax.broadcasted_iota(jnp.int32, (height, 128), 0)
    base = plan.at(plan.a_base, me)

    @pl.when(plan.at(plan.a_rows, me) > 0)
    def _():
        slot128[pl.ds(first - 2 * base, height)] = jnp.where(row + first < 2 * A_ROWS, moved, 0.0)

    v_start = (A_ROWS * D + D * HEADS) // 128
    v_rows, v_off, v_first = (plan.at(t, me) for t in (plan.v_rows, plan.v_off, plan.v_first))
    tall_v = min(height, -(-2 * max(plan.v_rows) // 8) * 8)

    @pl.when(v_rows > 0)
    def _():
        inside = plan.at([max(0, v_start - i * plan.length // 128) for i in range(plan.n)], me)
        to = 2 * v_off + first + inside - v_start - 2 * v_first
        slot128[pl.ds(to, tall_v)] = shifted[pl.ds(16 + inside, tall_v)]

    h_first, h_rows, h_off = (plan.at(t, me) for t in (plan.h_first, plan.h_rows, plan.h_off))

    @pl.when(h_rows > 0)
    def _():
        tall_h = plan.image
        begin = A_ROWS * D + HEADS * h_first - 128 * first + 128 * 16
        turn = begin % 128
        rolled[0:tall_h] = pltpu.roll(shifted[pl.ds(begin // 128, tall_h)], (128 - turn) % 128, 1)
        rolled[tall_h : tall_h + 8] = jnp.zeros((8, 128), F32)
        lane = lax.broadcasted_iota(jnp.int32, (tall_h, 128), 1)
        shifted[0:tall_h] = jnp.where(lane < 128 - turn, rolled[0:tall_h], rolled[1 : tall_h + 1])
        to = slot128.at[pl.ds(pl.multiple_of(2 * h_off, 8), 10 * plan.heads)]
        it = lax.broadcasted_iota(jnp.int32, (10, 128), 0)
        lane = lax.broadcasted_iota(jnp.int32, (10, 128), 1)
        for k in range(plan.heads):
            row, turn = HEADS * k // 128, HEADS * k % 128
            window = pltpu.roll(shifted[row : row + 16], (128 - turn) % 128, 1)
            value = jnp.where(lane < 128 - turn, window[0:10], window[1:11])
            kept = (it * 128 + lane < HEADS) & (k < h_rows)
            to[10 * k : 10 * k + 10] = to[10 * k : 10 * k + 10] + jnp.where(kept, value, 0.0)


def unpack_rows(plan, i, slot, w, heads, vectors, scratch):
    base, rows = plan.a_base[i], plan.a_rows[i]
    if rows:
        shared = i > 0 and base < plan.a_base[i - 1] + plan.a_rows[i - 1]
        lo = 0
        if shared:
            w[base : base + 16] = w[base : base + 16] + slot[0:16]
            lo = 16
        if rows > lo:
            w[base + lo : base + rows] = slot[lo:rows]
    h_rows, h_off, h_first = plan.h_rows[i], plan.h_off[i], plan.h_first[i]
    v_rows, v_off, v_first = plan.v_rows[i], plan.v_off[i], plan.v_first[i]
    if h_rows or v_rows:
        value = slot.astype(F32)
        scratch[0][...] = value[:, 0:128]
        scratch[1][...] = value[:, 128:D]
    if h_rows:
        shared = i > 0 and plan.h_rows[i - 1] and plan.h_first[i - 1] + plan.h_rows[i - 1] > h_first
        for j in range(5):
            for half in range(2):
                cols = slice(128 * half, 128 * half + 128)
                first = D * j + h_first
                value = scratch[half][pl.ds(h_off + j, h_rows, stride=5)]
                if shared:
                    heads[first : first + 1, cols] = heads[first : first + 1, cols] + value[0:1]
                    if h_rows > 1:
                        heads[first + 1 : first + h_rows, cols] = value[1:h_rows]
                else:
                    heads[first : first + h_rows, cols] = value
    if v_rows:
        shared = v_first and plan.v_first[i - 1] + plan.v_rows[i - 1] > v_first
        shared = shared or (i > 0 and plan.v_rows[i - 1] > 0 and v_first == 0)
        for half in range(2):
            cols = slice(128 * half, 128 * half + 128)
            value = scratch[half][v_off : v_off + v_rows]
            if shared:
                vectors[v_first : v_first + 1, cols] = vectors[v_first : v_first + 1, cols] + value[0:1]
                if v_rows > 1:
                    vectors[v_first + 1 : v_first + v_rows, cols] = value[1:v_rows]
            else:
                vectors[v_first : v_first + v_rows, cols] = value


def split3(value):
    hi = value.astype(BF).astype(F32)
    mid = (value - hi).astype(BF).astype(F32)
    return hi, mid, value - hi - mid


def gather_kernel(plan, p_ref, ints_ref, imp_ref, w, wh, vec, both, rw, slots, slot128, shifted, rolled, scratch, whf, vecf, send, recv):
    n = plan.n
    depth = n // 4
    core, me, near_x, near_y = neighbours(n)
    barrier = greet(core, me, near_x, near_y, n)
    place_shard(plan, me, p_ref, slot128, shifted, rolled)
    pl.semaphore_wait(barrier, depth + 3)
    half = rw.shape[1]
    started = []

    def copy(src, dst, slot, to):
        c = pltpu.make_async_remote_copy(
            src_ref=src, dst_ref=dst, send_sem=send.at[slot], recv_sem=recv.at[slot], device_id=to, device_id_type=MESH
        )
        c.start()
        started.append(c)
        return c

    mine = pl.multiple_of(core * half, half)
    theirs = pl.multiple_of((1 - core) * half, half)
    number = iter(range(1 << 20))
    ints_copy = copy(ints_ref.at[:, pl.ds(theirs, half)], both.at[core], next(number), at(1 - core, me))
    rows = plan.slot
    total = jnp.sum(imp_ref[...].astype(F32), axis=1, keepdims=True)
    lane = lax.broadcasted_iota(jnp.int32, (1, D), 1)
    hi, mid, lo = split3(total)
    left = slot128[pl.ds(0, rows, stride=2)]
    right = slot128[pl.ds(1, rows, stride=2)]
    own = jnp.concatenate([left, right], 1)
    last = jnp.where(lane == 0, hi, jnp.where(lane == 1, mid, jnp.where(lane == 2, lo, 0.0)))
    last_row = lax.broadcasted_iota(jnp.int32, (rows, D), 0) == rows - 1
    slots[core, me] = jnp.where(last_row, last, own).astype(BF)

    def column(index, k):
        return (index + n - 4 * k) % n

    def send_slot(origin, to, lo=0, hi=rows):
        ref = slots.at[core, origin, pl.ds(lo, hi - lo)]
        return copy(ref, ref, next(number), to)

    near_xy = near_x + near_y - me
    cut = rows // 2
    z_in, x_in, y_in, d_in, s_in = {}, {}, {}, {}, []
    for k in sorted(range(1, depth), key=lambda k: (min(k, depth - k), k)):
        z_in[k] = send_slot(me, at(core, (me + 4 * k) % n))
    order = [0] + list(z_in)
    for k in order:
        if k:
            z_in[k].wait_recv()
        x_in[k] = send_slot(column(me, k), at(core, near_x))
        y_in[k] = send_slot(column(me, k), at(core, near_y))
        s_in.append(send_slot(column(me, k), at(1 - core, me)))
    for k in order:
        x_in[k].wait_recv()
        first = send_slot(column(near_x, k), at(core, near_y), 0, cut)
        s_in.append(send_slot(column(near_x, k), at(1 - core, me)))
        y_in[k].wait_recv()
        second = send_slot(column(near_y, k), at(core, near_x), cut, rows)
        s_in.append(send_slot(column(near_y, k), at(1 - core, me)))
        d_in[k] = (first, second)
    for k in order:
        for c in d_in[k]:
            c.wait_recv()
        s_in.append(send_slot(column(near_xy, k), at(1 - core, me)))
    ints_copy.wait_recv()
    both[core] = ints_ref[:, pl.ds(mine, half)]
    for c in s_in:
        c.wait_recv()
    for c in started:
        c.wait_send()
    for t in range(2):
        vecf[...] = jnp.zeros(vecf.shape, F32)
        for i in range(n):
            unpack_rows(plan, i, slots[t, i], w.at[t], whf, vecf, [scratch.at[0], scratch.at[1]])
        for j in range(5):
            wh[t, :, D * j : D * j + D] = whf[D * j : D * j + D].astype(BF)
        vec[t] = vecf[...].astype(BF)
    total = jnp.zeros((1, D), F32)
    for i in range(n):
        tail = slots[0, i, rows - 16 : rows].astype(F32)
        total = total + tail[15:16]
    weight_sum = jnp.sum(jnp.where(lane < 3, total, 0.0), axis=1, keepdims=True)
    rw[...] = jnp.broadcast_to(imp_ref[:, pl.ds(mine, half)].astype(F32) / weight_sum, (8, half))


def gather(plan, p128, ints, imp):
    n, rows = plan.n, plan.slot
    half = ints.shape[1] // 2
    vm = pl.BlockSpec(memory_space=pltpu.VMEM)
    height = p128.shape[0]
    tall = max(2 * rows, height + 40) + 80
    copies = 1 + (n // 4 - 1) + 2 * (n // 4) + 2 * (n // 4) + n
    return pl.pallas_call(
        functools.partial(gather_kernel, plan),
        out_shape=(
            jax.ShapeDtypeStruct((2, A_ROWS, D), BF),
            jax.ShapeDtypeStruct((2, D, HPAD), BF),
            jax.ShapeDtypeStruct((2, 128, D), BF),
            jax.ShapeDtypeStruct((2, 8, half), jnp.int32),
            jax.ShapeDtypeStruct((8, half), F32),
        ),
        in_specs=[vm] * 3,
        out_specs=(vm,) * 5,
        scratch_shapes=[
            pltpu.VMEM((2, n, rows, D), BF),
            pltpu.VMEM((tall, 128), F32),
            pltpu.VMEM((height + 128, 128), F32),
            pltpu.VMEM((height + 40, 128), F32),
            pltpu.VMEM((2, rows, 128), F32),
            pltpu.VMEM((HPAD, D), F32),
            pltpu.VMEM((128, D), F32),
            pltpu.SemaphoreType.DMA((copies,)),
            pltpu.SemaphoreType.DMA((copies,)),
        ],
        compiler_params=pltpu.CompilerParams(
            collective_id=0, has_side_effects=True, vmem_limit_bytes=48 * 1024 * 1024
        ),
    )(p128, ints, imp)


def chunks(height):
    step = max(c for c in range(8, 113, 8) if height % c == 0)
    return [(lo, lo + step) for lo in range(0, height, step)]


def lay_flat(plan, me, slot128, flat, rolled):
    height = rolled.shape[0] - 40
    start = me * plan.length
    shift = start % 128
    first = start // 128
    base = plan.at(plan.a_base, me)
    row = lax.broadcasted_iota(jnp.int32, (height + 8, 128), 0)
    flat[...] = jnp.zeros(flat.shape, F32)

    @pl.when(plan.at(plan.a_rows, me) > 0)
    def _():
        rows = slot128[pl.ds(first - 2 * base, height + 8)]
        flat[16 : 24 + height] = jnp.where(row + first < 2 * A_ROWS, rows, 0.0)

    v_start = (A_ROWS * D + D * HEADS) // 128
    v_rows, v_off, v_first = (plan.at(t, me) for t in (plan.v_rows, plan.v_off, plan.v_first))
    tall_v = min(height, -(-2 * max(plan.v_rows) // 8) * 8)

    @pl.when(v_rows > 0)
    def _():
        inside = plan.at([max(0, v_start - i * plan.length // 128) for i in range(plan.n)], me)
        source = 2 * v_off + first + inside - v_start - 2 * v_first
        to = pl.ds(16 + inside, tall_v)
        flat[to] = flat[to] + slot128[pl.ds(source, tall_v)]

    h_first, h_rows, h_off = (plan.at(t, me) for t in (plan.h_first, plan.h_rows, plan.h_off))

    @pl.when(h_rows > 0)
    def _():
        tall_h = plan.image
        source = slot128.at[pl.ds(pl.multiple_of(2 * h_off, 8), 10 * plan.heads + 6)]
        it = lax.broadcasted_iota(jnp.int32, (16, 128), 0)
        lane = lax.broadcasted_iota(jnp.int32, (16, 128), 1)
        rolled[0 : tall_h + 8] = jnp.zeros((tall_h + 8, 128), F32)
        for k in range(plan.heads):
            row, turn = HEADS * k // 128, HEADS * k % 128
            kept = (it * 128 + lane < HEADS) & (k < h_rows)
            value = pltpu.roll(jnp.where(kept, source[10 * k : 10 * k + 16], 0.0), turn, 1)
            above = jnp.concatenate([jnp.zeros((8, 128), F32), value], 0)[7:23]
            rolled[row : row + 16] = rolled[row : row + 16] + jnp.where(lane >= turn, value, above)
        begin = A_ROWS * D + HEADS * h_first - 128 * first + 128 * 16
        turn = begin % 128
        slot128[0:8] = jnp.zeros((8, 128), F32)
        slot128[8 : 8 + tall_h] = pltpu.roll(rolled[0:tall_h], turn, 1)
        lane = lax.broadcasted_iota(jnp.int32, (tall_h, 128), 1)
        moved = jnp.where(lane >= turn, slot128[8 : 8 + tall_h], slot128[7 : 7 + tall_h])
        to = pl.ds(begin // 128, tall_h)
        flat[to] = flat[to] + moved

    rolled[0 : height + 8] = pltpu.roll(flat[16 : 24 + height], (128 - shift) % 128, 1)
    for lo, hi in chunks(height):
        lane = lax.broadcasted_iota(jnp.int32, (hi - lo, 128), 1)
        flat[lo:hi] = jnp.where(lane < 128 - shift, rolled[lo:hi], rolled[lo + 1 : hi + 1])


def pack_slots(plan, core, gw, gh, gv, rgw, rgh, rgv, slots, sums, vsum, scratch):
    total = gv[core].astype(F32) + rgv[...]
    for kind in range(3):
        vsum[kind * (BLOCKS + 1) : (kind + 1) * (BLOCKS + 1)] = total[kind, 0 : BLOCKS + 1]
    sums[...] = gh[core].astype(F32) + rgh[...].astype(F32)
    for i in range(plan.n):
        base, rows = plan.a_base[i], plan.a_rows[i]
        h_rows, h_off, h_first = plan.h_rows[i], plan.h_off[i], plan.h_first[i]
        v_rows, v_off, v_first = plan.v_rows[i], plan.v_off[i], plan.v_first[i]
        slots[i, rows : plan.slot] = jnp.zeros((plan.slot - rows, D), BF)
        if rows:
            added = gw[core, base : base + rows].astype(F32) + rgw[base : base + rows].astype(F32)
            slots[i, 0:rows] = added.astype(BF)
        if h_rows or v_rows:
            scratch[...] = jnp.zeros(scratch.shape, F32)
            for half in range(2):
                for j in range(5 if h_rows else 0):
                    cols = slice(D * j + 128 * half, D * j + 128 * half + 128)
                    scratch[half, pl.ds(h_off + j, h_rows, stride=5)] = sums[h_first : h_first + h_rows, cols]
                if v_rows:
                    scratch[half, v_off : v_off + v_rows] = vsum[v_first : v_first + v_rows, 128 * half : 128 * half + 128]
            whole = jnp.concatenate([scratch[0], scratch[1]], 1)
            slots[i, rows : plan.slot] = whole[rows:].astype(BF)


def segment_bounds():
    first = [0] + [(CAT + j * D) * D for j in range(BLOCKS + 1)]
    return list(zip(first, first[1:] + [A_ROWS * D + D * HEADS]))


class Rows:
    def __init__(self, ref):
        self.ref, self.height = ref, ref.shape[0]

    def chunks(self):
        return chunks(self.height)

    def get(self, lo, hi):
        return self.ref[lo:hi]

    def put(self, lo, hi, value):
        self.ref[lo:hi] = value


class Flat:
    def __init__(self, ref, buffer):
        self.ref, self.buffer, self.length = ref, buffer, ref.shape[1]
        self.whole = self.length // 1024 * 8
        self.height = -(-self.length // 1024) * 8

    def chunks(self):
        step = next(s for s in range(64, 0, -8) if self.whole % s == 0)
        return [(lo, lo + step) for lo in range(0, self.whole, step)] + [(self.whole, self.height)]

    def ends(self):
        rows = (self.length - 128 * self.whole) // 128
        return rows, self.length % 128, 128 * self.whole, 128 * (self.whole + rows)

    def get(self, lo, hi):
        if hi <= self.whole:
            return self.ref[0:1, 128 * lo : 128 * hi].reshape(hi - lo, 128)
        rows, lanes, first, last = self.ends()
        self.buffer[...] = jnp.zeros((8, 128), F32)
        if rows:
            self.buffer[0:rows] = self.ref[0:1, first:last].reshape(rows, 128)
        if lanes:
            self.buffer[rows : rows + 1, 0:lanes] = self.ref[0:1, last : self.length]
        return self.buffer[...]

    def put(self, lo, hi, value):
        if hi <= self.whole:
            self.ref[0:1, 128 * lo : 128 * hi] = value.reshape(1, 128 * (hi - lo))
            return
        rows, lanes, first, last = self.ends()
        if rows:
            self.ref[0:1, first:last] = value[0:rows].reshape(1, 128 * rows)
        if lanes:
            self.ref[0:1, last : self.length] = value[rows : rows + 1, 0:lanes]


def update_shard(plan, me, p_ref, m_ref, v_ref, outs, flat, squares, sq_in, push, to_plane, to_z):
    first_out, second_out, new_out, norm_out = outs
    height = p_ref.height
    start = me * plan.length
    correction = 1.0 - 0.5**STEP
    bounds = segment_bounds()

    def place(lo, hi):
        shape = (hi - lo, 128)
        return 128 * lo + 128 * lax.broadcasted_iota(jnp.int32, shape, 0) + lax.broadcasted_iota(jnp.int32, shape, 1)

    for lo, hi in p_ref.chunks():
        spot = place(lo, hi)
        grad = jnp.where(spot < plan.length, flat[lo:hi], 0.0)
        first_new = 0.5 * m_ref.get(lo, hi) + 0.5 * grad
        second_new = 0.5 * v_ref.get(lo, hi) + 0.5 * grad * grad
        first_out.put(lo, hi, first_new)
        second_out.put(lo, hi, second_new)
        decay = jnp.where(spot < bounds[-1][1] - start, 0.01 * p_ref.get(lo, hi), 0.0)
        update = first_new / correction / (jnp.sqrt(second_new / correction) + 1e-06) + decay
        flat[lo:hi] = jnp.where(spot < plan.length, update, 0.0)
        new_out.put(lo, hi, p_ref.get(lo, hi) - 0.5 * update)
    squares[...] = jnp.zeros(squares.shape, F32)

    def each_segment(body):
        for j, (first, last) in enumerate(bounds):
            pl.when((first < start + plan.length) & (last > start))(lambda j=j, first=first, last=last: body(j, first, last))

    def square_sums(j, first, last):
        weight, change = jnp.zeros((8, 128), F32), jnp.zeros((8, 128), F32)
        for lo, hi in p_ref.chunks():
            spot = place(lo, hi)
            inside = (spot >= first - start) & (spot < last - start)
            p, u = jnp.where(inside, p_ref.get(lo, hi), 0.0), jnp.where(inside, flat[lo:hi], 0.0)
            weight = weight + jnp.sum((p * p).reshape(-1, 8, 128), axis=0)
            change = change + jnp.sum((u * u).reshape(-1, 8, 128), axis=0)
        squares[0, j : j + 1] = jnp.sum(weight, axis=0, keepdims=True)
        squares[0, 16 + j : 17 + j] = jnp.sum(change, axis=0, keepdims=True)

    each_segment(square_sums)
    total = squares[0]
    for hop, targets in enumerate((to_plane, to_z)):
        lands = range(3) if hop == 0 else range(3, 3 + len(to_z))
        for c in [push(squares.at[hop], sq_in.at[k], to) for k, to in zip(lands, targets)]:
            c.wait_recv()
        for k in lands:
            total = total + sq_in[k]
        squares[hop + 1] = total
    norm = jnp.sqrt(jnp.sum(total, axis=1, keepdims=True))
    squares[3] = jnp.broadcast_to(norm, (32, 128))
    line = jnp.sqrt(jnp.sum(jnp.concatenate([total, jnp.zeros((96, 128), F32)], 0).T, axis=0, keepdims=True))
    norm_out[0:1] = line[:, 0:MATS]
    norm_out[1:2] = pltpu.roll(line, 112, 1)[:, 0:MATS]

    def scaled(j, first, last):
        ratio = squares[3, j : j + 1] / squares[3, 16 + j : 17 + j]
        for lo, hi in p_ref.chunks():
            spot = place(lo, hi)
            inside = (spot >= first - start) & (spot < last - start)
            new_out.put(lo, hi, jnp.where(inside, p_ref.get(lo, hi) - 0.5 * ratio * flat[lo:hi], new_out.get(lo, hi)))

    each_segment(scaled)


def reduce_kernel(
    plan, gw, gh, gv, st, ig, p_ref, m_ref, v_ref,
    st_out, ig_out, first_out, second_out, new_out, norm_out,
    rgw, rgh, rgv, slots, sums, vsum, scratch, in_d, in_x, in_y, in_z, slot128, flat, rolled, squares, sq_in,
    send, recv, local,
):
    n, rows = plan.n, plan.slot
    depth, cut = n // 4, plan.slot // 2
    core, me, near_x, near_y = neighbours(n)
    near_xy = near_x + near_y - me
    barrier = greet(core, me, near_x, near_y, n)
    pl.semaphore_wait(barrier, depth + 3)
    half = st.shape[1]
    number = iter(range(1 << 20))
    started = []

    def copy(src, dst, to):
        slot = next(number)
        c = pltpu.make_async_remote_copy(
            src_ref=src, dst_ref=dst, send_sem=send.at[slot], recv_sem=recv.at[slot], device_id=to, device_id_type=MESH
        )
        c.start()
        started.append(c)
        return c

    def column(index, k):
        return (index + n - 4 * k) % n

    sibling = at(1 - core, me)
    early = [
        copy(gw.at[1 - core], rgw, sibling),
        copy(gh.at[1 - core], rgh, sibling),
        copy(gv.at[1 - core], rgv, sibling),
    ]
    mine = pl.ds(pl.multiple_of(core * half, half), half)
    late = [
        copy(st.at[1 - core], st_out.at[mine], sibling),
        copy(ig.at[1 - core], ig_out.at[mine], sibling),
    ]
    stay = [
        pltpu.make_async_copy(st.at[core], st_out.at[mine], local.at[0]),
        pltpu.make_async_copy(ig.at[core], ig_out.at[mine], local.at[1]),
    ]
    for c in stay:
        c.start()
    for c in early:
        c.wait_recv()
    pack_slots(plan, core, gw, gh, gv, rgw, rgh, rgv, slots, sums, vsum, scratch)
    order = list(range(1, depth)) + [0]
    to_x, to_y = at(core, near_x), at(core, near_y)
    halves = {}
    for k in order:
        diagonal = column(near_xy, k)
        halves[k] = (
            copy(slots.at[diagonal, pl.ds(0, cut)], in_d.at[k, pl.ds(0, cut)], to_y),
            copy(slots.at[diagonal, pl.ds(cut, rows - cut)], in_d.at[k, pl.ds(cut, rows - cut)], to_x),
        )
    fulls = {}
    for k in order:
        ox, oy = column(near_x, k), column(near_y, k)
        halves[k][0].wait_recv()
        slots[ox, 0:cut] = (slots[ox, 0:cut].astype(F32) + in_d[k, 0:cut].astype(F32)).astype(BF)
        first = copy(slots.at[ox], in_x.at[k], to_x)
        halves[k][1].wait_recv()
        slots[oy, cut:rows] = (slots[oy, cut:rows].astype(F32) + in_d[k, cut:rows].astype(F32)).astype(BF)
        fulls[k] = (first, copy(slots.at[oy], in_y.at[k], to_y))
    along = {}
    for k in order:
        own = column(me, k)
        for c in fulls[k]:
            c.wait_recv()
        if k:
            total = slots[own].astype(F32) + in_x[k].astype(F32) + in_y[k].astype(F32)
            slots[own] = total.astype(BF)
            along[k] = copy(slots.at[own], in_z.at[k], at(core, own))
    for c in along.values():
        c.wait_recv()
    total = slots[me].astype(F32) + in_x[0].astype(F32) + in_y[0].astype(F32)
    for k in along:
        total = total + in_z[k].astype(F32)
    slot128[...] = jnp.zeros(slot128.shape, F32)
    slot128[pl.ds(0, rows, stride=2)] = total[:, 0:128]
    slot128[pl.ds(1, rows, stride=2)] = total[:, 128:D]
    lay_flat(plan, me, slot128, flat, rolled)

    to_z = [at(core, column(me, k)) for k in range(1, depth)]
    outs = (Rows(first_out), Rows(second_out), Rows(new_out), norm_out)
    to_plane = [to_x, to_y, at(core, near_xy)]
    update_shard(plan, me, Rows(p_ref), Rows(m_ref), Rows(v_ref), outs, flat, squares, sq_in, copy, to_plane, to_z)
    for c in late:
        c.wait_recv()
    for c in stay:
        c.wait()
    for c in started:
        c.wait_send()


def reduce_and_update(plan, gw, gh, gv, st, ig, p128, m128, v128):
    n, rows = plan.n, plan.slot
    depth = n // 4
    half = st.shape[1]
    height = p128.shape[0]
    vm = pl.BlockSpec(memory_space=pltpu.VMEM)
    hbm = pl.BlockSpec(memory_space=pl.ANY)
    copies = 5 + 2 * depth + 2 * depth + (depth - 1) + (depth - 1) + 3
    flat32 = jax.ShapeDtypeStruct((height, 128), F32)
    return pl.pallas_call(
        functools.partial(reduce_kernel, plan),
        out_shape=(
            jax.ShapeDtypeStruct((2 * half, D), BF),
            jax.ShapeDtypeStruct((2 * half, D), F32),
            flat32,
            flat32,
            flat32,
            jax.ShapeDtypeStruct((2, MATS), F32),
        ),
        in_specs=[vm] * 3 + [hbm] * 2 + [vm] * 3,
        out_specs=(hbm, hbm, vm, vm, vm, vm),
        scratch_shapes=[
            pltpu.VMEM((A_ROWS, D), BF),
            pltpu.VMEM((D, HPAD), BF),
            pltpu.VMEM(gv.shape[1:], F32),
            pltpu.VMEM((n, rows, D), BF),
            pltpu.VMEM((D, HPAD), F32),
            pltpu.VMEM((40, D), F32),
            pltpu.VMEM((2, rows, 128), F32),
            pltpu.VMEM((depth, rows, D), BF),
            pltpu.VMEM((depth, rows, D), BF),
            pltpu.VMEM((depth, rows, D), BF),
            pltpu.VMEM((depth, rows, D), BF),
            pltpu.VMEM((max(2 * rows, height + 48) + 80, 128), F32),
            pltpu.VMEM((height + 128, 128), F32),
            pltpu.VMEM((height + 40, 128), F32),
            pltpu.VMEM((4, 32, 128), F32),
            pltpu.VMEM((2 + depth, 32, 128), F32),
            pltpu.SemaphoreType.DMA((copies,)),
            pltpu.SemaphoreType.DMA((copies,)),
            pltpu.SemaphoreType.DMA((2,)),
        ],
        compiler_params=pltpu.CompilerParams(
            collective_id=1, has_side_effects=True, vmem_limit_bytes=48 * 1024 * 1024
        ),
    )(gw, gh, gv, st, ig, p128, m128, v128)


class Copies:
    def __init__(self, send, recv):
        self.send, self.recv, self.made, self.sent = send, recv, [], set()

    def add(self, src, dst, to, recv_slot=None, only=None):
        self.made.append((src, dst, to, recv_slot, only))
        return len(self.made) - 1

    def get(self, number):
        src, dst, to, recv_slot, _ = self.made[number]
        return pltpu.make_async_remote_copy(
            src_ref=src(), dst_ref=dst(), send_sem=self.send.at[number],
            recv_sem=self.recv.at[number] if recv_slot is None else recv_slot(),
            device_id=to(), device_id_type=MESH,
        )

    def start(self, *numbers):
        for number in numbers:
            self.get(number).start()

    def arrive(self, *numbers):
        for number in numbers:
            self.get(number).wait_recv()

    def leave(self, *numbers):
        for number in numbers:
            only = self.made[number][4]
            if number not in self.sent and only is None:
                self.get(number).wait_send()
            elif number not in self.sent:
                pl.when(only())(lambda number=number: self.get(number).wait_send())
            self.sent.add(number)


def fused_fits(plan):
    depth, half = plan.n // 4, plan.slot // 2
    plain = [b + plan.slot <= A_ROWS for b, h, v in zip(plan.a_base, plan.h_rows, plan.v_rows) if not (h or v)]
    vectors = [rows for rows in plan.v_rows if rows]
    return (
        all(plain)
        and vectors == [3 * (BLOCKS + 1)]
        and plan.n % 4 == 0
        and half >= 32
        and 4 * half <= HPAD
        and 2 * depth * plan.slot <= (BLOCKS + 1) * D
        and depth == 4
        and max(plan.a_rows) <= plan.slot
    )


def train_kernel(
    plan, x_ref, codes_ref, targets_ref, visits_ref, imp_ref, p_ref, m_ref, v_ref,
    st_out, ig_out, first_out, second_out, new_out, norm_out,
    w, wh, vec, both, away, rw, eye, wt, wht, vt, gsb, xt, mix, xh, gp, rstd, mean, stream, ex, br, dm, acc, lg, dl,
    gw, gh, gv, packed, st_stage, slot128, flat, rolled, vsum, vacc, vin, owned, squares, sq_in, tail,
    send, recv, z_recv, own_recv, local, ready,
):
    n, rows = plan.n, plan.slot
    depth, hrows = n // 4, plan.slot // 2
    cut = hrows // 32 * 16
    core, me, near_x, near_y = neighbours(n)
    near_xy = near_x + near_y - me
    width = both.shape[2]
    params_in, first_new, second_new, new = (Flat(ref, tail) for ref in (p_ref, first_out, second_out, new_out))
    moments = [
        pltpu.make_async_copy(src, dst, local.at[3 + i])
        for i, (src, dst) in enumerate(((m_ref, first_out), (v_ref, second_out)))
    ]
    z_me, j_me = me // 4, me % 4
    copies = Copies(send, recv)
    scratch = [slot128.at[0:rows], slot128.at[rows : 2 * rows]]
    barrier = greet(core, me, near_x, near_y, n, True)
    mine = pl.multiple_of(core * width, width)
    theirs = pl.multiple_of((1 - core) * width, width)
    x_copy = pltpu.make_async_copy(x_ref.at[pl.ds(mine, width)], st_stage.at[0], local.at[0])
    x_copy.start()
    for c in moments:
        c.start()
    for to, half in ((both.at[core], mine), (away, theirs)):
        cols = pl.ds(half, width)
        to[0:1] = codes_ref[:, cols]
        to[1:2] = targets_ref[0, :, cols]
        to[2:6] = visits_ref[:, cols]
        to[6:7] = targets_ref[1, :, cols]
        to[7:8] = targets_ref[2, :, cols]
    height = params_in.height
    for lo, hi in params_in.chunks():
        slot128[lo:hi] = params_in.get(lo, hi)
    place_shard(plan, me, slot128.at[0:height], slot128, flat, rolled)

    spare = (BLOCKS + 1) * D

    def slot_part(t, i, lo, count):
        row = pl.multiple_of(spare + rows * (t * depth + i // 4) + lo, 16)
        return xh.at[pl.ds(row, count), pl.ds(pl.multiple_of((i % 4) * D, D), D)]

    def column(index, k):
        return (index + n - 4 * k) % n

    def sibling():
        return at(1 - core, me)

    def same(make, to):
        return copies.add(make, make, to)

    low = core * hrows
    other_low = (1 - core) * hrows
    order = [0] + sorted(range(1, depth), key=lambda k: (min(k, depth - k), k))
    to_x, to_y, to_d = (lambda: at(core, near_x)), (lambda: at(core, near_y)), (lambda: at(core, near_xy))
    swap_ints = copies.add(lambda: away, lambda: both.at[core], sibling)

    def arrival(t, number):
        return own_recv.at[t * (depth + 2) + number]

    own_targets = [(lambda: near_x), (lambda: near_y)] + [lambda k=k: (me + 4 * k) % n for k in order[1:]]
    own_sends = [copies.add(lambda: slot_part(core, me, 0, rows), lambda: slot_part(core, me, 0, rows), sibling, lambda: arrival(core, 0))]
    for number, target in enumerate(own_targets, 1):
        for h in range(2):
            make = lambda h=h: slot_part(core, me, h * hrows, hrows)
            own_sends.append(
                copies.add(make, make, lambda h=h, target=target: at(h, target()), lambda number=number: arrival(core, number))
            )
    own_sends = own_sends[3 + 2 :] + own_sends[1:5] + own_sends[:1]

    def own_arrive(t, number, make):
        pltpu.make_async_remote_copy(
            src_ref=make(), dst_ref=make(), send_sem=send.at[0], recv_sem=arrival(t, number), device_id=sibling(), device_id_type=MESH
        ).wait_recv()

    gathers = []
    for t in range(2):
        g = {}
        for k in order:
            if k:
                g["x", k] = same(lambda t=t, k=k: slot_part(t, column(me, k), low, hrows), to_x)
                g["y", k] = same(lambda t=t, k=k: slot_part(t, column(me, k), low, hrows), to_y)
            g["d", k] = (
                same(lambda t=t, k=k: slot_part(t, column(near_x, k), low, cut), to_y),
                same(lambda t=t, k=k: slot_part(t, column(near_y, k), low + cut, hrows - cut), to_x),
            )
            g["s", k] = [
                same(lambda t=t, k=k, index=index: slot_part(t, column(index, k), low, hrows), sibling) if index is not me or k else None
                for index in (me, near_x, near_y, near_xy)
            ]
        gathers.append(g)

    def gather_0(t):
        pl.when(core == t)(lambda: copies.start(*own_sends))

    def gather_1(t):
        g = gathers[t]
        for number, k in enumerate(order[1:], 3):
            own_arrive(t, number, lambda: slot_part(t, me, low, hrows))
            copies.start(g["x", k], g["y", k], g["s", k][0])

    def gather_2(t):
        g = gathers[t]
        for k in order:
            if k:
                copies.arrive(g["x", k])
            else:
                own_arrive(t, 1, lambda: slot_part(t, me, low, hrows))
            copies.start(g["d", k][0], g["s", k][1])
            if k:
                copies.arrive(g["y", k])
            else:
                own_arrive(t, 2, lambda: slot_part(t, me, low, hrows))
            copies.start(g["d", k][1], g["s", k][2])

    def gather_3(t):
        g = gathers[t]
        for k in order:
            copies.arrive(*g["d", k])
            copies.start(g["s", k][3])

    def gather_4(t):
        g = gathers[t]
        pl.when(core != t)(lambda: own_arrive(t, 0, lambda: slot_part(t, me, 0, rows)))
        for k in order:
            copies.arrive(*(c for c in g["s", k] if c is not None))

    def unpack(t):
        lg[4 * D : 5 * D, 128:D] = jnp.zeros((D, 128), F32)
        vsum[...] = jnp.zeros(vsum.shape, F32)
        for i in range(n):
            row, lane = spare + rows * (t * depth + i // 4), (i % 4) * D
            unpack_rows(plan, i, xh[row : row + rows, lane : lane + D], w.at[t], lg, vsum, scratch)
        for j in range(5):
            wh[t, :, D * j : D * j + D] = lg[D * j : D * j + D].astype(BF)
        vec[t] = vsum[...].astype(BF)

    total = jnp.sum(imp_ref[...].astype(F32), axis=1, keepdims=True)
    lane_d = lax.broadcasted_iota(jnp.int32, (1, D), 1)
    hi, mid, lo = split3(total)
    left = slot128[pl.ds(0, rows, stride=2)]
    right = slot128[pl.ds(1, rows, stride=2)]
    own = jnp.concatenate([left, right], 1)
    last = jnp.where(lane_d == 0, hi, jnp.where(lane_d == 1, mid, jnp.where(lane_d == 2, lo, 0.0)))
    last_row = lax.broadcasted_iota(jnp.int32, (rows, D), 0) == rows - 1
    slot_part(core, me, 0, rows)[...] = jnp.where(last_row, last, own).astype(BF)
    pl.semaphore_wait(barrier, depth + 3 + 2 + depth - 1)
    gather_0(0)
    copies.start(swap_ints)
    eye[...] = identity(D)
    x_copy.wait()
    for c in range(0, width, CB):
        xt[0, 0:D, c : c + CB] = nt(eye[...], st_stage[0, c : c + CB, :]).astype(BF)
    gather_1(0)
    gather_0(1)
    gather_2(0)
    gather_3(0)
    copies.arrive(swap_ints)
    gather_4(0)
    unpack(0)
    total = jnp.zeros((1, D), F32)
    for i in range(n):
        row, lane = spare + rows * (i // 4), (i % 4) * D
        total = total + xh[row + rows - 16 : row + rows, lane : lane + D].astype(F32)[15:16]
    weight_sum = jnp.sum(jnp.where(lane_d < 3, total, 0.0), axis=1, keepdims=True)
    rw[...] = jnp.broadcast_to(imp_ref[:, pl.ds(mine, width)].astype(F32) / weight_sum, (8, width))

    fwd = (eye, w, wh, vec, wt, vt, gsb, xt, mix, xh, gp, rstd, stream, mean, both, width)

    def during_forward(k):
        pl.when(k == 6)(lambda: gather_2(1))

    def emit_states(t):
        for c in range(0, width, CB):
            st_stage[t, c : c + CB, :] = nt(eye[...], xt[t + 1, 0:D, c : c + CB]).astype(BF)

    gather_1(1)
    forward_tower(0, fwd, during_forward, lambda: gather_3(1))
    gather_4(1)
    copies.leave(*range(len(copies.made)))
    unpack(1)
    forward_tower(1, fwd)
    emit_states(0)
    emit_states(1)
    out_rows = pl.ds(mine, width)
    st_copy = copies.add(lambda: st_stage.at[1 - core], lambda: st_out.at[out_rows], sibling)
    copies.start(st_copy)
    st_stay = pltpu.make_async_copy(st_stage.at[core], st_out.at[out_rows], local.at[1])
    st_stay.start()

    packed_of = [i for i in range(n) if plan.h_rows[i] or plan.v_rows[i]]
    owner = plan.v_rows.index(3 * (BLOCKS + 1))

    early = (2, 3)

    def piece(t, zz, b, lo, count):
        if t == 1 and zz in early:
            arena, first, q = dl, 0, 7 * early.index(zz) + b
        elif t == 1:
            arena, first, q = mix, BLOCKS * (D + 16), 7 * zz + b
        else:
            arena, first, q = xh, spare, 7 * zz + b
        row = pl.multiple_of(first + hrows * (q // 4) + lo, 16)
        return arena.at[pl.ds(row, count), pl.ds(pl.multiple_of((q % 4) * D, D), D)]

    def block(t, zz, b):
        return piece(t, zz, b, 0, hrows)

    def z_in(h, k):
        return st_stage.at[0, pl.ds(pl.multiple_of(hrows * (h * (depth - 1) + k - 1), 16), hrows)]

    def z_out(t, zz):
        if t == 1 and zz in early:
            return st_stage.at[1, pl.ds(hrows * early.index(zz), hrows)]
        return block(t, zz, j_me)

    def slot_half(t, i, lo):
        if i in packed_of:
            return packed.at[packed_of.index(i), pl.ds(pl.multiple_of(lo, 16), hrows)]
        return gw.at[t, pl.ds(pl.multiple_of(plan.a_base[i] + lo, 16), hrows)]

    j_x, j_y, j_d = near_x % 4, near_y % 4, near_xy % 4
    direct = ((0, 0), (0, 1), (0, 2), (1, 2), (1, 3))
    jobs = {}
    for t in range(2):
        for zz in range(depth):
            job = {}
            job["swap"] = [
                copies.add(lambda t=t, i=4 * zz + j: slot_half(t, i, other_low), lambda t=t, zz=zz, j=j: block(t, zz, j), sibling)
                for j in range(4)
            ]
            if (t, zz) in direct:
                job["d"] = [copies.add(lambda t=t, zz=zz: block(t, zz, j_d), lambda t=t, zz=zz: block(t, zz, 4), to_d)]
            else:
                job["d"] = [
                    copies.add(
                        lambda t=t, zz=zz, lo=lo, count=count: piece(t, zz, j_d, lo, count),
                        lambda t=t, zz=zz, lo=lo, count=count: piece(t, zz, 4, lo, count),
                        to,
                    )
                    for to, lo, count in ((to_y, 0, cut), (to_x, cut, hrows - cut))
                ]
            job["x"] = copies.add(lambda t=t, zz=zz: block(t, zz, j_x), lambda t=t, zz=zz: block(t, zz, 5), to_x)
            job["y"] = copies.add(lambda t=t, zz=zz: block(t, zz, j_y), lambda t=t, zz=zz: block(t, zz, 6), to_y)
            job["z"] = copies.add(
                lambda t=t, zz=zz: z_out(t, zz),
                lambda zz=zz: z_in(core, (zz + depth - z_me) % depth),
                lambda t=t, zz=zz: at(t, 4 * zz + j_me),
                lambda zz=zz: z_recv.at[core * depth + (zz + depth - z_me) % depth],
                lambda zz=zz: z_me != zz,
            )
            jobs[t, zz] = job

    def pack(t, planes):
        wanted = [i for i in packed_of if i // 4 in planes]
        for i in wanted:
            a_rows, h_rows, h_off, h_first = plan.a_rows[i], plan.h_rows[i], plan.h_off[i], plan.h_first[i]
            to = packed.at[packed_of.index(i)]
            for part in scratch:
                part[...] = jnp.zeros(part.shape, F32)
            lo16, hi16 = h_first // 16 * 16, -(-(h_first + h_rows) // 16) * 16
            for half in range(2):
                for j in range(5 if h_rows else 0):
                    cols = slice(D * j + 128 * half, D * j + 128 * half + 128)
                    value = gh[t, lo16:hi16, cols].astype(F32)[h_first - lo16 : h_first - lo16 + h_rows]
                    scratch[half][pl.ds(h_off + j, h_rows, stride=5)] = value
            whole = jnp.concatenate([scratch[0][...], scratch[1][...]], 1)
            to[a_rows:rows] = whole[a_rows:].astype(BF)
            if a_rows:
                to[0:a_rows] = gw[t, plan.a_base[i] : plan.a_base[i] + a_rows]

    def plus(*refs):
        value = refs[0][...].astype(F32)
        for ref in refs[1:]:
            value = value + ref[...].astype(F32)
        return value

    def sum_0(t, zz):
        copies.start(*jobs[t, zz]["swap"])

    def sum_1(t, zz):
        job = jobs[t, zz]
        for j in range(4):
            copies.arrive(job["swap"][j])
            target = block(t, zz, j)
            target[...] = plus(slot_half(t, 4 * zz + j, low), target).astype(BF)
        copies.start(*job["d"])
        if (t, zz) in direct:
            copies.start(job["x"], job["y"])

    def sum_2(t, zz):
        job = jobs[t, zz]
        for side, copy, j, lo, count in (("x", job["d"][0], j_x, 0, cut), ("y", job["d"][1], j_y, cut, hrows - cut)):
            copies.arrive(copy)
            target = piece(t, zz, j, lo, count)
            target[...] = plus(target, piece(t, zz, 4, lo, count)).astype(BF)
            copies.start(job[side])

    def sum_3(t, zz):
        job = jobs[t, zz]
        copies.arrive(job["x"], job["y"])
        value = plus(block(t, zz, j_me), block(t, zz, 5), block(t, zz, 6))
        if (t, zz) in direct:
            copies.arrive(*job["d"])
            value = value + block(t, zz, 4)[...].astype(F32)

        @pl.when(z_me != zz)
        def _():
            z_out(t, zz)[...] = value.astype(BF)
            copies.start(job["z"])

        @pl.when((z_me == zz) & (core == t))
        def _():
            final(core)[...] = value

        @pl.when((z_me == zz) & (core != t))
        def _():
            outgo[...] = value
            copies.start(hand_over)

    def sum_4():
        copies.arrive(hand_over)
        for h in range(2):
            for k in range(1, depth):
                src = z_in(h, k)
                pltpu.make_async_remote_copy(
                    src_ref=src, dst_ref=src, send_sem=send.at[0], recv_sem=z_recv.at[h * depth + k], device_id=sibling(), device_id_type=MESH
                ).wait_recv()
                final(h)[...] = final(h)[...] + src[...].astype(F32)

    def final(h):
        return owned.at[h]

    outgo = owned.at[2]

    def vector_step(step):
        sources = [gv.at[1 - core], vacc.at[0], vacc.at[1]]
        along = [lambda k=k: at(core, (me + 4 * k) % n) for k in range(1, depth)]
        targets = [[sibling], [to_x, to_y, to_d], along]
        if step:
            base = gv[core] if step == 1 else vacc[step - 2]
            for number, k in vector_copies[-1]:
                copies.arrive(number)
                base = base + vin[k]
            vacc[step - 1] = base
        if step < 3:
            started = []
            for k, to in enumerate(targets[step], (0, 1, 4)[step]):
                number = copies.add(lambda step=step: sources[step], lambda k=k: vin.at[k], to)
                copies.start(number)
                started.append((number, k))
            vector_copies.append(started)

    vector_copies = []
    hand_over = copies.add(lambda: outgo, lambda: final(core), sibling)
    peers = [(1 - core, me), (core, near_x), (core, near_y), (core, near_xy)] + [(1 - core, (me + 4 * k) % n) for k in range(1, depth)] + [(core, (me + 4 * k) % n) for k in range(1, depth)]

    bwd = (eye, w, wh, vec, wht, vt, gsb, xt, mix, xh, gp, rstd, stream, ex, br, dm, acc, lg, dl, both, rw, gw, gh, gv, dm, width)
    ig_copies = [copies.add(lambda: dm, lambda: ig_out.at[out_rows], sibling, None, lambda t=t: core != t) for t in range(2)]

    def ig_local():
        return pltpu.make_async_copy(dm, ig_out.at[out_rows], local.at[2])

    def emit_inputs(t):
        pl.when(core == t)(lambda: ig_local().start())
        pl.when(core != t)(lambda: copies.start(ig_copies[t]))

    def free_inputs(t):
        pl.when(core == t)(lambda: ig_local().wait())
        pl.when(core != t)(lambda: copies.get(ig_copies[t]).wait_send())

    def signal_ready(which):
        for to_core, to_index in peers:
            pl.semaphore_signal(ready.at[which], inc=1, device_id=at(to_core, to_index), device_id_type=MESH)

    def wait_ready(which):
        pl.semaphore_wait(ready.at[which], len(peers))

    def schedule(i, steps):
        for step in sorted({s[0] for s in steps}):

            def run(step=step):
                for s, f, *args in steps:
                    if s == step:
                        f(*args)

            pl.when(i == step)(run)

    def after_head_1():
        copies.leave(st_copy)
        st_stay.wait()
        signal_ready(0)

    def during_backward_1(i):
        schedule(i, [
            (2, wait_ready, 0), (2, pack, 1, (3,)), (2, sum_0, 1, 3),
            (4, sum_1, 1, 3), (4, pack, 1, (2,)), (4, sum_0, 1, 2),
            (6, sum_1, 1, 2),
            (8, sum_3, 1, 3),
        ])

    ex[...] = jnp.zeros_like(ex)
    backward_tower(1, bwd, after_head_1, during_backward_1, None, lambda: sum_3(1, 2))
    emit_inputs(1)
    signal_ready(1)
    for zz in early:
        job = jobs[1, zz]
        copies.leave(*job["swap"], *job["d"], job["x"], job["y"])

    def after_head_0():
        wait_ready(1)
        sum_0(1, 1)
        sum_0(1, 0)
        pack(0, (3,))
        sum_0(0, 3)

    def during_backward_0(i):
        schedule(i, [
            (1, sum_1, 1, 1), (1, sum_1, 1, 0),
            (2, sum_1, 0, 3),
            (4, sum_2, 1, 1), (4, sum_2, 1, 0), (4, pack, 0, (2,)), (4, sum_0, 0, 2),
            (5, sum_2, 0, 3),
            (6, sum_1, 0, 2),
            (8, sum_3, 1, 1), (8, sum_3, 1, 0), (8, sum_0, 0, 1),
            (9, sum_3, 0, 3), (9, sum_1, 0, 1),
        ])

    def after_weights():
        sum_0(0, 0)
        vector_step(0)

    backward_tower(0, bwd, after_head_0, during_backward_0, lambda: free_inputs(1), after_weights)
    emit_inputs(0)
    sum_1(0, 0)
    vector_step(1)
    sum_3(0, 2)
    sum_3(0, 1)
    sum_3(0, 0)
    vector_step(2)
    sum_4()
    vector_step(3)

    slot128[...] = jnp.zeros(slot128.shape, F32)
    for h in range(2):
        slot128[pl.ds(2 * hrows * h, hrows, stride=2)] = final(h)[:, 0:128]
        slot128[pl.ds(2 * hrows * h + 1, hrows, stride=2)] = final(h)[:, 128:D]

    @pl.when(me == owner)
    def _():
        for kind in range(3):
            first = 2 * (plan.v_off[owner] + kind * (BLOCKS + 1))
            for h in range(2):
                value = vacc[2, kind, 0 : BLOCKS + 1, 128 * h : 128 * h + 128]
                slot128[pl.ds(first + h, BLOCKS + 1, stride=2)] = value

    def push(src, dst, to):
        number = copies.add(lambda: src, lambda: dst, lambda: to)
        copies.start(number)
        return copies.get(number)

    lay_flat(plan, me, slot128, flat, rolled)
    for c in moments:
        c.wait()
    update_shard(
        plan, me, params_in, first_new, second_new, (first_new, second_new, new, norm_out),
        flat, squares, sq_in, push, [to_x(), to_y(), to_d()], [at(core, (me + 4 * k) % n) for k in range(1, depth)],
    )
    copies.arrive(st_copy)
    pl.when(core == 0)(lambda: copies.arrive(ig_copies[0]))
    pl.when(core == 1)(lambda: copies.arrive(ig_copies[1]))
    free_inputs(0)
    copies.sent.update(ig_copies)
    copies.leave(*range(len(copies.made)))


def finish_kernel(st, ig, first, second, new, norms, st_out, ig_out, first_out, second_out, new_out, low_out, norms_out, *rest):
    *held, into, outof = rest
    moves = []
    for src, dst, mid, parts in zip((new, ig, st, first, second), (new_out, ig_out, st_out, first_out, second_out), held, (1, 8, 4, 1, 1)):
        rows = src.shape[0] // parts
        for i in range(parts):
            at_rows = pl.ds(i * rows, rows)
            number = len(moves)
            moves.append(
                (
                    pltpu.make_async_copy(src.at[at_rows], mid.at[at_rows], into.at[number]),
                    pltpu.make_async_copy(mid.at[at_rows], dst.at[at_rows], outof.at[number]),
                )
            )
    for load, _ in moves:
        load.start()
    for load, store in moves:
        load.wait()
        store.start()
    size = new.shape[1]
    for lo in range(0, size, 8192):
        hi = min(lo + 8192, size)
        low_out[0:1, lo:hi] = held[0][0:1, lo:hi].astype(BF)
    norms_out[...] = norms[...]
    for _, store in moves:
        store.wait()


def finish(st, ig, first, second, new, norms):
    vm = pl.BlockSpec(memory_space=pltpu.VMEM)
    hbm = pl.BlockSpec(memory_space=pl.ANY)
    arrays = (st, ig, first, second, new)
    shapes = [jax.ShapeDtypeStruct(v.shape, v.dtype) for v in arrays]
    return pl.pallas_call(
        finish_kernel,
        out_shape=(*shapes, jax.ShapeDtypeStruct(new.shape, BF), jax.ShapeDtypeStruct(norms.shape, F32)),
        in_specs=[hbm] * 5 + [vm],
        out_specs=(hbm,) * 5 + (vm,) * 2,
        scratch_shapes=[pltpu.VMEM(v.shape, v.dtype) for v in (new, ig, st, first, second)] + [pltpu.SemaphoreType.DMA((15,))] * 2,
        compiler_params=pltpu.CompilerParams(vmem_limit_bytes=62 * 1024 * 1024),
    )(st, ig, first, second, new, norms)


def train(plan, latent, codes, targets, visits, imp, params, first, second):
    n, rows = plan.n, plan.slot
    depth, hrows = n // 4, rows // 2
    width = codes.shape[1] // 2
    height = -(-params.shape[1] // 1024) * 8
    vm = pl.BlockSpec(memory_space=pltpu.VMEM)
    hbm = pl.BlockSpec(memory_space=pl.ANY)
    packed = sum(1 for h, v in zip(plan.h_rows, plan.v_rows) if h or v)
    return pl.pallas_call(
        functools.partial(train_kernel, plan),
        out_shape=(
            jax.ShapeDtypeStruct((2 * width, D), BF),
            jax.ShapeDtypeStruct((2 * width, D), F32),
            jax.ShapeDtypeStruct(params.shape, F32),
            jax.ShapeDtypeStruct(params.shape, F32),
            jax.ShapeDtypeStruct(params.shape, F32),
            jax.ShapeDtypeStruct((2, MATS), F32),
        ),
        in_specs=[hbm] + [vm] * 5 + [hbm] * 2,
        out_specs=(hbm, hbm, vm, vm, vm, vm),
        scratch_shapes=[
            pltpu.VMEM((2, A_ROWS, D), BF),
            pltpu.VMEM((2, D, HPAD), BF),
            pltpu.VMEM((2, 128, D), BF),
            pltpu.VMEM((2, 8, width), jnp.int32),
            pltpu.VMEM((8, width), jnp.int32),
            pltpu.VMEM((8, width), F32),
            *work_scratch(width),
            pltpu.VMEM((2, A_ROWS, D), BF),
            pltpu.VMEM((2, D, HPAD), BF),
            pltpu.VMEM((2, 3, 16, D), F32),
            pltpu.VMEM((packed, rows, D), BF),
            pltpu.VMEM((2, width, D), BF),
            pltpu.VMEM((max(2 * rows, height + 48) + 80, 128), F32),
            pltpu.VMEM((height + 128, 128), F32),
            pltpu.VMEM((height + 40, 128), F32),
            pltpu.VMEM((128, D), F32),
            pltpu.VMEM((3, 3, 16, D), F32),
            pltpu.VMEM((3 + depth, 3, 16, D), F32),
            pltpu.VMEM((3, hrows, D), F32),
            pltpu.VMEM((4, 32, 128), F32),
            pltpu.VMEM((2 + depth, 32, 128), F32),
            pltpu.VMEM((8, 128), F32),
            pltpu.SemaphoreType.DMA((11 * n,)),
            pltpu.SemaphoreType.DMA((11 * n,)),
            pltpu.SemaphoreType.DMA((2 * depth,)),
            pltpu.SemaphoreType.DMA((2 * (depth + 2),)),
            pltpu.SemaphoreType.DMA((5,)),
            pltpu.SemaphoreType.REGULAR((2,)),
        ],
        compiler_params=pltpu.CompilerParams(
            collective_id=2, has_side_effects=True, vmem_limit_bytes=63 * 1024 * 1024
        ),
    )(latent, codes, targets, visits, imp, params, first, second)


def on_device(latent, codes, targets, visits, importance, params, first_moment, second_moment):
    me = lax.axis_index("tower")
    row_count = latent.shape[0]
    half = row_count // 2
    shard_len = params.shape[1]
    plan = Plan(lax.axis_size("dp"), shard_len)
    if fused_fits(plan):
        states_out, inputs_out, first, second, new, norms = train(
            plan, latent, codes, targets.transpose(1, 0, 2), visits[0].T, importance[None], params, first_moment, second_moment
        )
        states_out, inputs_out, first, second, new, low, norms = finish(states_out, inputs_out, first, second, new, norms)
    else:
        height = -(-plan.rows128 // 8) * 8
        p128, m128, v128 = (
            jnp.pad(v, ((0, 0), (0, 128 * height - shard_len))).reshape(height, 128)
            for v in (params, first_moment, second_moment)
        )
        ints = jnp.concatenate([codes, targets[0, :1], visits[0].T, targets[0, 1:]], 0)
        x = lax.dynamic_slice_in_dim(latent, me * half, half, 0)
        w, wh, vec, both, rw = gather(plan, p128, ints, importance[None])
        st, ig, gw, gh, gv = compute(x, both, rw, w, wh, vec)
        states_out, inputs_out, *flat, norms = reduce_and_update(plan, gw, gh, gv, st, ig, p128, m128, v128)
        first, second, new = (v.reshape(1, -1)[:, :shard_len] for v in flat)
        low = new.astype(BF)
    return (states_out[None], inputs_out[None], first, second, new, low, norms[None])


def solution(mesh):
    in_specs = (
        P("dp", None),
        P("tower", "dp"),
        P("tower", None, "dp"),
        P("tower", "dp", None),
        P("dp"),
        P("tower", "dp"),
        P("tower", "dp"),
        P("tower", "dp"),
    )
    out_specs = (
        P("tower", "dp", None),
        P("tower", "dp", None),
        P("tower", "dp"),
        P("tower", "dp"),
        P("tower", "dp"),
        P("tower", "dp"),
        P("tower", None, None),
    )
    return jax.shard_map(
        on_device, mesh=mesh, in_specs=in_specs, out_specs=out_specs, check_vma=False
    )
```

```python
import functools

import jax
import jax.numpy as jnp
from jax import lax
from jax.experimental import pallas as pl
from jax.experimental.pallas import tpu as pltpu
from jax.sharding import PartitionSpec as P

D = 256
CODES = 32
BINS = 601
BLOCKS = 10
STEP = 5
HEADS = 1238
MATS = 12
P_SIZE = 1054464
HPAD = 1280
CAT = D + CODES
A_ROWS = CAT + BLOCKS * D
BF = jnp.bfloat16
F32 = jnp.float32
GELU_C = 0.7978845608028654
GELU_K = 0.044715


def nn(a, b):
    return jnp.dot(a, b, preferred_element_type=F32)


def nt(a, b):
    return lax.dot_general(a, b, (((1,), (1,)), ((), ())), preferred_element_type=F32)


def identity(n):
    return (lax.broadcasted_iota(jnp.int32, (n, n), 0) == lax.broadcasted_iota(jnp.int32, (n, n), 1)).astype(BF)


ZETA = (GELU_C * GELU_K) ** (1.0 / 3.0)
B0 = GELU_C / ZETA
E0 = 0.5 / ZETA


def wide(v, cs):
    return jnp.concatenate([v] * ((cs.stop - cs.start) // v.shape[1]), 1)


def norm_act(src, cs, gs, unit, gp, rstd, out):
    for r in range(0, D, 32):
        rs = slice(r, r + 32)
        xh = src[rs, cs] * rstd
        z = xh * wide(gs[rs, 0:128], cs) + wide(gs[rs, 128:256], cs)
        z2 = z * z
        t = jnp.tanh(z * (z2 + B0))
        q = t * E0 + E0
        a = z * q
        out(rs, a)
        unit[rs, cs] = xh.astype(BF)
        gp[rs, cs] = (q + (a * (1.0 - t)) * (z2 * 3.0 + B0)).astype(BF)


def broadcast_vectors(vt, rows):
    k = lax.broadcasted_iota(jnp.int32, (128, 128), 0)
    picks = jnp.concatenate([(k == row).astype(BF) for row in rows], 1)
    return nn(vt, picks)


def head_stage(cs, lg, dl, ints, rw):
    width = rw.shape[1]
    it8 = lax.broadcasted_iota(jnp.int32, (8, width), 0)
    low = -jnp.inf
    b75, b150, b154 = lg[600:608], lg[1200:1208], lg[1232:1240]

    def top(block):
        return jnp.max(block, axis=0, keepdims=True)

    def steps(lo, hi, step):
        return [(r, min(r + step, hi)) for r in range(lo, hi, step)]

    def folded(value):
        return value.reshape(-1, 8, width)

    def top_range(lo, hi):
        best = None
        for r, end in steps(lo, hi, 40):
            part = jnp.max(folded(lg[r:end]), axis=0)
            best = part if best is None else jnp.maximum(best, part)
        return best

    max_v = top(jnp.maximum(top_range(0, 600), jnp.where(it8 < 1, b75, low)))
    max_r = top(
        jnp.maximum(
            jnp.maximum(top_range(608, 1200), jnp.where(it8 >= 1, b75, low)),
            jnp.where(it8 < 2, b150, low),
        )
    )
    max_c = top(
        jnp.maximum(
            jnp.maximum(top_range(1208, 1232), jnp.where(it8 >= 2, b150, low)),
            jnp.where(it8 < 2, b154, low),
        )
    )
    in_policy = (it8 >= 2) & (it8 < 6)
    max_p = top(jnp.where(in_policy, b154, low))

    def exp_range(lo, hi, best):
        acc = jnp.zeros((8, width), F32)
        for r, end in steps(lo, hi, 40):
            e = jnp.exp(lg[r:end] - best)
            lg[r:end] = e
            acc = acc + jnp.sum(folded(e), axis=0)
        return acc

    e75 = jnp.exp(b75 - jnp.where(it8 < 1, max_v, max_r))
    e150 = jnp.exp(b150 - jnp.where(it8 < 2, max_r, max_c))
    e154 = jnp.exp(b154 - jnp.where(it8 < 2, max_c, max_p))

    def total(acc):
        return rw / jnp.sum(acc, axis=0, keepdims=True)

    inv_v = total(exp_range(0, 600, max_v) + jnp.where(it8 < 1, e75, 0.0))
    inv_r = total(exp_range(608, 1200, max_r) + jnp.where(it8 >= 1, e75, 0.0) + jnp.where(it8 < 2, e150, 0.0))
    inv_c = total(exp_range(1208, 1232, max_c) + jnp.where(it8 >= 2, e150, 0.0) + jnp.where(it8 < 2, e154, 0.0))
    inv_p = total(jnp.where(in_policy, e154, 0.0))
    hit_v = ints[1:2]
    hit_r = ints[6:7] + BINS
    hit_c = ints[7:8] + 2 * BINS
    counts = jnp.where(in_policy, ints.astype(F32), 0.0)
    share = counts * (rw / jnp.sum(counts, axis=0, keepdims=True))

    def minus(value, lo, *hits):
        at = lax.broadcasted_iota(jnp.int32, value.shape, 0)
        for hit in hits:
            value = value - jnp.where(at == hit - lo, rw, 0.0)
        return value

    d75 = minus(e75 * jnp.where(it8 < 1, inv_v, inv_r), 600, hit_v, hit_r)
    d150 = minus(e150 * jnp.where(it8 < 2, inv_r, inv_c), 1200, hit_r, hit_c)
    d154 = minus(e154 * jnp.where(it8 < 2, inv_c, inv_p), 1232, hit_c) - share
    d154 = jnp.where(it8 < 6, d154, 0.0)

    def emit(lo, hi, inv, hit):
        for r, end in steps(lo, hi, 80):
            dl[r:end, cs] = minus(lg[r:end] * inv, r, hit).astype(BF)

    def pair(first, second):
        return jnp.concatenate([first, second], 0).astype(BF)

    emit(0, 592, inv_v, hit_v)
    dl[592:608, cs] = pair(minus(lg[592:600] * inv_v, 592, hit_v), d75)
    emit(608, 1200, inv_r, hit_r)
    dl[1200:1216, cs] = pair(d150, minus(lg[1208:1216] * inv_c, 1208, hit_c))
    emit(1216, 1232, inv_c, hit_c)
    dl[1232:1248, cs] = pair(d154, jnp.zeros_like(d154))
    dl[1248:HPAD, cs] = jnp.zeros((HPAD - 1248, width), BF)


CB = 256
GROUP = 2


def saved_views(t, mix, xh):
    def mixed(k):
        return mix.at[pl.ds(pl.multiple_of((t * BLOCKS + k - 1) * (D + 16), 16), D + 16)]

    def unit(k):
        return xh.at[pl.ds(pl.multiple_of((t * (BLOCKS + 1) + k) * D, D), D)]

    return mixed, unit


def column_groups(width):
    blocks = [slice(c, c + CB) for c in range(0, width, CB)]
    per = min(GROUP, len(blocks))
    return blocks, per, [slice(c, c + per * CB) for c in range(0, width, per * CB)]


def forward_tower(t, refs, during=None, before_last=None, beside=None):
    (eye, w, wh, vec, wt, vt, gsb, xt, mix, xh, gp, rstd, stream, mean, ints, width) = refs
    blocks, per, groups = column_groups(width)
    mixed, unit = saved_views(t, mix, xh)
    first_bias = 2 * (BLOCKS + 1)
    ones = jnp.ones((16, D), BF)

    def mean_rows(slot):
        value = nn(ones, wt[slot, 0:D])[0:8] * (1.0 / D)
        high = value.astype(BF).astype(F32)
        wt[slot, D : D + 16] = jnp.concatenate([high, value - high], 0).astype(BF)

    def vectors(k):
        gsb[k % 2] = broadcast_vectors(vt[...], (k, k + BLOCKS + 1)) * ZETA

    def prefetch(k):
        vectors(k)
        row = pl.multiple_of(CAT + jnp.minimum(k - 1, BLOCKS - 1) * D, 32)
        wt[k % 2, 0:D, 0:D] = nt(eye[...], w[t, pl.ds(row, D)]).astype(BF)
        at_row = lax.broadcasted_iota(jnp.int32, (128, 128), 0) == k + first_bias
        at_lane = lax.broadcasted_iota(jnp.int32, (128, 128), 1) == 0
        wt[k % 2, 0:D, D:384] = nn(vt[...], (at_row & at_lane).astype(BF)).astype(BF)
        mean_rows(k % 2)

    def row_of(k):
        return pl.ds(t * (BLOCKS + 1) + k, 1)

    def stage(k, c):
        def keep(rs, a):
            mixed(k)[rs, blocks[c]] = a.astype(BF)

        norm_act(stream, blocks[c], gsb.at[k % 2], unit(k), gp.at[t, k], rstd[row_of(k), blocks[c]], keep)

    def spread(square, k, cs):
        var = jnp.sum(square, axis=0, keepdims=True) * (1.0 / D)
        rstd[row_of(k), cs] = lax.rsqrt(var + 1e-05)

    def add(k, cs, out, fresh):
        shift = out[D : D + 1] + out[D + 8 : D + 9]
        square = jnp.zeros((8, out.shape[1]), F32)
        for r in range(0, D, 32):
            value = out[r : r + 32] - shift
            if not fresh:
                value = stream[r : r + 32, cs] + value
            stream[r : r + 32, cs] = value
            square = square + jnp.sum((value * value).reshape(4, 8, -1), axis=0)
        if not fresh:
            mean[0:1, cs] = mean[0:1, cs] + shift
        spread(square, k + 1, cs)

    def centre(cs):
        total = jnp.zeros((8, CB), F32)
        for r in range(0, D, 32):
            total = total + jnp.sum(stream[r : r + 32, cs].reshape(4, 8, -1), axis=0)
        middle = jnp.sum(total, axis=0, keepdims=True) * (1.0 / D)
        mean[0:1, cs] = middle
        square = jnp.zeros((8, CB), F32)
        for r in range(0, D, 32):
            value = stream[r : r + 32, cs] - middle
            stream[r : r + 32, cs] = value
            square = square + jnp.sum((value * value).reshape(4, 8, -1), axis=0)
        spread(square, 1, cs)

    vt[...] = nt(eye[...], vec[t]).astype(BF)
    vectors(0)
    wt[0, 0:D, 0:D] = nt(eye[...], w[t, 0:D]).astype(BF)
    tile = first_bias // 16 * 16
    picked = lax.broadcasted_iota(jnp.int32, (16, D), 0) == first_bias - tile
    bias = jnp.where(picked, vec[t, tile : tile + 16].astype(F32), 0.0).astype(BF)
    rest = jnp.concatenate([w[t, D:CAT], bias, jnp.zeros((128 - CODES - 16, D), BF)], 0)
    wt[0, 0:D, D:384] = nt(eye[...], rest).astype(BF)
    mean_rows(0)
    for cs in blocks:
        it = lax.broadcasted_iota(jnp.int32, (CODES, CB), 0)
        xt[t, D:CAT, cs] = (it == ints[t, 0:1, cs]).astype(BF)
        xt[t, CAT : CAT + 16, cs] = jnp.ones((16, CB), BF)
    first = [nn(wt[0, :, 0 : CAT + 16], xt[t, :, cs]) for cs in groups]
    prefetch(1)
    for group, cs in enumerate(groups):
        add(-1, cs, first[group], True)
    for cs in blocks:

        def keep(rs, a):
            stream[rs, cs] = a

        norm_act(stream, cs, gsb.at[0], unit(0), gp.at[t, 0], rstd[row_of(0), cs], keep)
        centre(cs)

    def layer(k, more):
        mixed(k)[D : D + 16, :] = jnp.ones((16, width), BF)
        if more and beside is not None:
            beside(k)
        for group, cs in enumerate(groups):
            out = nn(wt[k % 2, :, 0 : D + 16], mixed(k)[:, cs])
            ahead = group + 1 < len(groups)
            if ahead or more:
                for c in range(per):
                    stage(k if ahead else k + 1, (group + 1) % len(groups) * per + c)
            add(k, cs, out, False)
        if more:
            prefetch(k + 2)

    prefetch(2)
    for c in range(per):
        stage(1, c)

    @pl.loop(1, BLOCKS)
    def _(k):
        if during is not None:
            during(k)
        layer(k, True)

    if before_last is not None:
        before_last()
    layer(BLOCKS, False)
    for cs in blocks:
        xt[t + 1, 0:D, cs] = (stream[:, cs] + mean[0:1, cs]).astype(BF)


def transposed_head(eye, wh, wht, h):
    at_rows = pl.ds(pl.multiple_of(h * D, D), D)
    wht[at_rows, :] = nt(eye[...], wh[:, at_rows]).astype(BF)


def backward_tower(t, refs, after_head=None, during=None, before_product=None, after_weights=None, transposed=False, beside=None):
    (eye, w, wh, vec, wht, vt, gsb, xt, mix, xh, gp, rstd, ds, ex, br, dm, acc, lg, dl, ints, rw, gw, gh, gv, ig, width) = refs
    blocks = [slice(c, c + CB) for c in range(0, width, CB)]
    last = len(blocks) - 1
    mixed, unit = saved_views(t, mix, xh)
    vt[...] = nt(eye[...], vec[t]).astype(BF)
    for h in range(0 if transposed else HPAD // D):
        transposed_head(eye, wh.at[t], wht, h)

    def softmax_block(c):
        cs = pl.ds(pl.multiple_of(c * CB, CB), CB)
        lg[...] = nn(wht[...], xt[t + 1, 0:D, cs])
        return cs

    def states_block(c):
        cs = pl.ds(pl.multiple_of(c * CB, CB), CB)
        return cs, nn(wh[t], dl[:, cs])

    def keep_states(cs, product):
        value = product + ex[:, cs]
        ds[:, cs] = value
        br[BLOCKS % 2, :, cs] = value.astype(BF)

    cs = softmax_block(0)
    head_stage(cs, lg, dl, ints[t, :, cs], rw[0:1, cs])

    @pl.loop(1, width // CB)
    def _(c):
        cs = softmax_block(c)
        before, product = states_block(c - 1)
        head_stage(cs, lg, dl, ints[t, :, cs], rw[0:1, cs])
        keep_states(before, product)

    keep_states(*states_block(width // CB - 1))
    for h in range(0, HPAD, D):
        gh[t, :, h : h + D] = nt(xt[t + 1, 0:D, :], dl[h : h + D]).astype(BF)
    if after_head is not None:
        after_head()
    acc[...] = jnp.zeros(acc.shape, F32)
    ones = jnp.ones((16, 128), BF)

    def part(c):
        return dm.at[c * D : c * D + D]

    def gains(k):
        gsb[k % 2, :, 0:128] = broadcast_vectors(vt[...], (k,)) * ZETA

    def row_sums(k):
        for kind in range(2):
            gv[t, kind, pl.ds(k, 1), :] = nt(ones, acc[k % 2, kind].astype(BF))[0:1] * ZETA
        acc[k % 2] = jnp.zeros(acc.shape[1:], F32)

    def product(k, c):
        row = pl.multiple_of(CAT + (k - 1) * D, 32)
        part(c)[...] = nn(w[t, pl.ds(row, D)], br[k % 2, :, blocks[c]])

    def slopes(k, c):
        cs, grad, sums = blocks[c], part(c), acc.at[k % 2]
        s1 = jnp.zeros((8, CB), F32)
        s2 = jnp.zeros((8, CB), F32)
        for r in range(0, D, 32):
            rs = slice(r, r + 32)
            g = wide(gsb[k % 2, rs, 0:128], cs)
            dy = grad[rs, :] * gp[t, k, rs, cs].astype(F32)
            prod = dy * unit(k)[rs, cs].astype(F32)
            back = dy * g
            grad[rs, :] = back
            s1 = s1 + jnp.sum(back.reshape(4, 8, CB), axis=0)
            s2 = s2 + jnp.sum((prod * g).reshape(4, 8, CB), axis=0)
            sums[0, rs] = sums[0, rs] + (prod[:, 0:128] + prod[:, 128:CB])
            sums[1, rs] = sums[1, rs] + (dy[:, 0:128] + dy[:, 128:CB])
        return [jnp.sum(s, axis=0, keepdims=True) * (1.0 / D) for s in (s1, s2)]

    def stage(k, c, first):
        cs = blocks[c]
        means = slopes(k, c)
        scale = rstd[pl.ds(t * (BLOCKS + 1) + k, 1), cs]
        m1, m2 = (jnp.broadcast_to(m * scale, (32, CB)).astype(BF) for m in means)
        for r in range(0, D, 32):
            rs = slice(r, r + 32)
            back = part(c)[rs, :] * scale - (m1 + unit(k)[rs, cs] * m2).astype(F32)
            if first:
                br[0, rs, cs] = back.astype(BF)
            else:
                value = ds[rs, cs] + back
                ds[rs, cs] = value
                br[(k + 1) % 2, rs, cs] = value.astype(BF)

    if before_product is not None:
        before_product()
    gains(BLOCKS)
    gains(BLOCKS - 1)
    product(BLOCKS, 0)

    @pl.loop(0, BLOCKS)
    def _(i):
        k = BLOCKS - i
        if during is not None:
            during(i)
        if beside is not None:
            beside(i)
        for c in range(last + 1):
            if c < last:
                product(k, c + 1)
            stage(k, c, False)
            if c == 0:
                full = nt(mixed(k)[...], br[k % 2])
                row = pl.multiple_of(CAT + (k - 1) * D, 32)
                gw[t, pl.ds(row, D), :] = full[0:D].astype(BF)
                gv[t, 2, pl.ds(k, 1), :] = full[D : D + 1]
                product(k - 1, 0)
        gains(k - 2)
        row_sums(k)

    for c, cs in enumerate(blocks):
        part(c)[...] = ds[:, cs]
        stage(0, c, True)
    full = nt(xt[t], br[0])
    gw[t, 0:CAT, :] = full[0:CAT].astype(BF)
    gv[t, 2, 0:1, :] = full[CAT : CAT + 1]
    row_sums(0)
    if after_weights is not None:
        after_weights()
    for cs in blocks:
        back = nn(w[t, 0:D], br[0, :, cs])
        ex[:, cs] = back
        ig[cs, :] = back.T


def compute_kernel(x_ref, ints, rw, w, wh, vec, st, ig, gw, gh, gv, eye, wt, wht, vt, gsb, xt, mix, xh, gp, rstd, mean, stream, ex, br, dm, acc, lg, dl):
    width = x_ref.shape[0]
    eye[...] = identity(D)
    for c in range(0, width, CB):
        cs = slice(c, c + CB)
        xt[0, 0:D, cs] = nt(eye[...], x_ref[cs, :]).astype(BF)
    fwd = (eye, w, wh, vec, wt, vt, gsb, xt, mix, xh, gp, rstd, stream, mean, ints, width)
    @pl.loop(0, 2)
    def _(t):
        forward_tower(t, fwd)

        @pl.loop(0, width // CB)
        def _(c):
            cs = pl.ds(pl.multiple_of(c * CB, CB), CB)
            st[t, cs, :] = nt(eye[...], xt[t + 1, 0:D, cs]).astype(BF)

    ex[...] = jnp.zeros_like(ex)

    @pl.loop(0, 2)
    def _(i):
        t = 1 - i
        backward_tower(
            t,
            (eye, w, wh, vec, wht, vt, gsb, xt, mix, xh, gp, rstd, stream, ex, br, dm, acc, lg, dl, ints, rw, gw, gh, gv, ig.at[t], width),
        )


def work_scratch(width):
    return [
        pltpu.VMEM((D, D), BF),
        pltpu.VMEM((2, D + 16, 384), BF),
        pltpu.VMEM((HPAD, D), BF),
        pltpu.VMEM((D, 128), BF),
        pltpu.VMEM((2, D, 256), F32),
        pltpu.VMEM((3, CAT + 16, width), BF),
        pltpu.VMEM((2 * BLOCKS * (D + 16), width), BF),
        pltpu.VMEM((2 * (BLOCKS + 1) * D, width), BF),
        pltpu.VMEM((2, BLOCKS + 1, D, width), BF),
        pltpu.VMEM((24, width), F32),
        pltpu.VMEM((8, width), F32),
        pltpu.VMEM((D, width), F32),
        pltpu.VMEM((D, width), F32),
        pltpu.VMEM((2, D, width), BF),
        pltpu.VMEM((width // CB * D, CB), F32),
        pltpu.VMEM((2, 2, D, 128), F32),
        pltpu.VMEM((HPAD, CB), F32),
        pltpu.VMEM((HPAD, width), BF),
    ]


def compute(x, ints, rw, w, wh, vec):
    width = x.shape[0]
    vm = pl.BlockSpec(memory_space=pltpu.VMEM)
    return pl.pallas_call(
        compute_kernel,
        out_shape=(
            jax.ShapeDtypeStruct((2, width, D), BF),
            jax.ShapeDtypeStruct((2, width, D), F32),
            jax.ShapeDtypeStruct((2, A_ROWS, D), BF),
            jax.ShapeDtypeStruct((2, D, HPAD), BF),
            jax.ShapeDtypeStruct((2, 3, 16, D), F32),
        ),
        in_specs=[vm] * 6,
        out_specs=(vm,) * 5,
        scratch_shapes=work_scratch(width),
        compiler_params=pltpu.CompilerParams(vmem_limit_bytes=62 * 1024 * 1024),
    )(x, ints, rw, w, wh, vec)


class Plan:
    def __init__(self, n, length):
        self.n, self.length = n, length
        self.rows128 = -(-length // 128)
        block_end, head_end = A_ROWS * D, A_ROWS * D + D * HEADS
        self.a_base, self.a_rows, self.h_first, self.h_rows, self.h_off, self.v_first, self.v_rows, self.v_off = ([] for _ in range(8))
        used = 0
        for i in range(n):
            lo, hi = i * length, (i + 1) * length
            base = min(lo, block_end) // D // 16 * 16
            top = -(-min(hi, block_end) // D)
            a_rows = -(-(top - base) // 16) * 16 if lo < block_end else 0
            first = min(max(lo - block_end, 0), D * HEADS) // HEADS
            last = -(-min(max(hi - block_end, 0), D * HEADS) // HEADS)
            h_rows = last - first if hi > block_end and lo < head_end else 0
            v_first = max(lo - head_end, 0) // D
            v_rows = -(-(hi - head_end) // D) - v_first if hi > head_end else 0
            self.a_base.append(base)
            self.a_rows.append(a_rows)
            self.h_first.append(first)
            self.h_rows.append(h_rows)
            self.h_off.append(a_rows)
            self.v_first.append(v_first)
            self.v_rows.append(v_rows)
            self.v_off.append(a_rows + 5 * h_rows)
            used = max(used, a_rows + 5 * h_rows + v_rows)
        self.heads = max(self.h_rows)
        self.image = (HEADS * self.heads // 128 + 24) // 8 * 8
        self.slot = -(-(used + 1) // 32) * 32

    def at(self, table, me):
        value = jnp.int32(table[0])
        for i in range(1, self.n):
            if table[i] != table[i - 1]:
                value = value + (me >= i).astype(jnp.int32) * (table[i] - table[i - 1])
        return value


MESH = pl.DeviceIdType.MESH


def neighbours(n):
    core = lax.axis_index("tower")
    me = lax.axis_index("dp")
    near_x = me + 1 - 2 * (me % 2)
    near_y = me + 2 - 4 * ((me // 2) % 2)
    return core, me, near_x, near_y


def at(core, index):
    return {"tower": core, "dp": index}


def greet(core, me, near_x, near_y, n, crossed=False):
    barrier = pltpu.get_barrier_semaphore()
    pl.semaphore_signal(barrier, inc=1, device_id=at(1 - core, me), device_id_type=MESH)
    for near in (near_x, near_y, near_x + near_y - me):
        pl.semaphore_signal(barrier, inc=1, device_id=at(core, near), device_id_type=MESH)
    for k in range(1, n // 4):
        pl.semaphore_signal(barrier, inc=1, device_id=at(core, (me + 4 * k) % n), device_id_type=MESH)
    for near in [near_x, near_y] + [(me + 4 * k) % n for k in range(1, n // 4)] if crossed else []:
        pl.semaphore_signal(barrier, inc=1, device_id=at(1 - core, near), device_id_type=MESH)
    return barrier


def place_shard(plan, me, p_ref, slot128, shifted, rolled):
    rows = plan.rows128
    start = me * plan.length
    shift = start % 128
    first = start // 128
    tall = shifted.shape[0]
    height = p_ref.shape[0]
    lane = lax.broadcasted_iota(jnp.int32, (height, 128), 1)
    rolled[0:8] = jnp.zeros((8, 128), F32)
    rolled[8 : 8 + height] = pltpu.roll(p_ref[...], shift, 1)
    shifted[...] = jnp.zeros((tall, 128), F32)
    moved = jnp.where(lane >= shift, rolled[8 : 8 + height], rolled[7 : 7 + height])
    shifted[16 : 16 + height] = moved
    slot128[...] = jnp.zeros(slot128.shape, F32)
    row = lax.broadcasted_iota(jnp.int32, (height, 128), 0)
    base = plan.at(plan.a_base, me)

    @pl.when(plan.at(plan.a_rows, me) > 0)
    def _():
        slot128[pl.ds(first - 2 * base, height)] = jnp.where(row + first < 2 * A_ROWS, moved, 0.0)

    v_start = (A_ROWS * D + D * HEADS) // 128
    v_rows, v_off, v_first = (plan.at(t, me) for t in (plan.v_rows, plan.v_off, plan.v_first))
    tall_v = min(height, -(-2 * max(plan.v_rows) // 8) * 8)

    @pl.when(v_rows > 0)
    def _():
        inside = plan.at([max(0, v_start - i * plan.length // 128) for i in range(plan.n)], me)
        to = 2 * v_off + first + inside - v_start - 2 * v_first
        slot128[pl.ds(to, tall_v)] = shifted[pl.ds(16 + inside, tall_v)]

    h_first, h_rows, h_off = (plan.at(t, me) for t in (plan.h_first, plan.h_rows, plan.h_off))

    @pl.when(h_rows > 0)
    def _():
        tall_h = plan.image
        begin = A_ROWS * D + HEADS * h_first - 128 * first + 128 * 16
        turn = begin % 128
        rolled[0:tall_h] = pltpu.roll(shifted[pl.ds(begin // 128, tall_h)], (128 - turn) % 128, 1)
        rolled[tall_h : tall_h + 8] = jnp.zeros((8, 128), F32)
        lane = lax.broadcasted_iota(jnp.int32, (tall_h, 128), 1)
        shifted[0:tall_h] = jnp.where(lane < 128 - turn, rolled[0:tall_h], rolled[1 : tall_h + 1])
        to = slot128.at[pl.ds(pl.multiple_of(2 * h_off, 8), 10 * plan.heads)]
        it = lax.broadcasted_iota(jnp.int32, (10, 128), 0)
        lane = lax.broadcasted_iota(jnp.int32, (10, 128), 1)
        for k in range(plan.heads):
            row, turn = HEADS * k // 128, HEADS * k % 128
            window = pltpu.roll(shifted[row : row + 16], (128 - turn) % 128, 1)
            value = jnp.where(lane < 128 - turn, window[0:10], window[1:11])
            kept = (it * 128 + lane < HEADS) & (k < h_rows)
            to[10 * k : 10 * k + 10] = to[10 * k : 10 * k + 10] + jnp.where(kept, value, 0.0)


def unpack_rows(plan, i, slot, w, heads, vectors, scratch):
    base, rows = plan.a_base[i], plan.a_rows[i]
    if rows:
        shared = i > 0 and base < plan.a_base[i - 1] + plan.a_rows[i - 1]
        lo = 0
        if shared:
            w[base : base + 16] = w[base : base + 16] + slot[0:16]
            lo = 16
        if rows > lo:
            w[base + lo : base + rows] = slot[lo:rows]
    h_rows, h_off, h_first = plan.h_rows[i], plan.h_off[i], plan.h_first[i]
    v_rows, v_off, v_first = plan.v_rows[i], plan.v_off[i], plan.v_first[i]
    if h_rows or v_rows:
        value = slot.astype(F32)
        scratch[0][...] = value[:, 0:128]
        scratch[1][...] = value[:, 128:D]
    if h_rows:
        shared = i > 0 and plan.h_rows[i - 1] and plan.h_first[i - 1] + plan.h_rows[i - 1] > h_first
        for j in range(5):
            for half in range(2):
                cols = slice(128 * half, 128 * half + 128)
                first = D * j + h_first
                value = scratch[half][pl.ds(h_off + j, h_rows, stride=5)]
                if shared:
                    heads[first : first + 1, cols] = heads[first : first + 1, cols] + value[0:1]
                    if h_rows > 1:
                        heads[first + 1 : first + h_rows, cols] = value[1:h_rows]
                else:
                    heads[first : first + h_rows, cols] = value
    if v_rows:
        shared = v_first and plan.v_first[i - 1] + plan.v_rows[i - 1] > v_first
        shared = shared or (i > 0 and plan.v_rows[i - 1] > 0 and v_first == 0)
        for half in range(2):
            cols = slice(128 * half, 128 * half + 128)
            value = scratch[half][v_off : v_off + v_rows]
            if shared:
                vectors[v_first : v_first + 1, cols] = vectors[v_first : v_first + 1, cols] + value[0:1]
                if v_rows > 1:
                    vectors[v_first + 1 : v_first + v_rows, cols] = value[1:v_rows]
            else:
                vectors[v_first : v_first + v_rows, cols] = value


def split3(value):
    hi = value.astype(BF).astype(F32)
    mid = (value - hi).astype(BF).astype(F32)
    return hi, mid, value - hi - mid


def gather_kernel(plan, p_ref, ints_ref, imp_ref, w, wh, vec, both, rw, slots, slot128, shifted, rolled, scratch, whf, vecf, send, recv):
    n = plan.n
    depth = n // 4
    core, me, near_x, near_y = neighbours(n)
    barrier = greet(core, me, near_x, near_y, n)
    place_shard(plan, me, p_ref, slot128, shifted, rolled)
    pl.semaphore_wait(barrier, depth + 3)
    half = rw.shape[1]
    started = []

    def copy(src, dst, slot, to):
        c = pltpu.make_async_remote_copy(
            src_ref=src, dst_ref=dst, send_sem=send.at[slot], recv_sem=recv.at[slot], device_id=to, device_id_type=MESH
        )
        c.start()
        started.append(c)
        return c

    mine = pl.multiple_of(core * half, half)
    theirs = pl.multiple_of((1 - core) * half, half)
    number = iter(range(1 << 20))
    ints_copy = copy(ints_ref.at[:, pl.ds(theirs, half)], both.at[core], next(number), at(1 - core, me))
    rows = plan.slot
    total = jnp.sum(imp_ref[...].astype(F32), axis=1, keepdims=True)
    lane = lax.broadcasted_iota(jnp.int32, (1, D), 1)
    hi, mid, lo = split3(total)
    left = slot128[pl.ds(0, rows, stride=2)]
    right = slot128[pl.ds(1, rows, stride=2)]
    own = jnp.concatenate([left, right], 1)
    last = jnp.where(lane == 0, hi, jnp.where(lane == 1, mid, jnp.where(lane == 2, lo, 0.0)))
    last_row = lax.broadcasted_iota(jnp.int32, (rows, D), 0) == rows - 1
    slots[core, me] = jnp.where(last_row, last, own).astype(BF)

    def column(index, k):
        return (index + n - 4 * k) % n

    def send_slot(origin, to, lo=0, hi=rows):
        ref = slots.at[core, origin, pl.ds(lo, hi - lo)]
        return copy(ref, ref, next(number), to)

    near_xy = near_x + near_y - me
    cut = rows // 2
    z_in, x_in, y_in, d_in, s_in = {}, {}, {}, {}, []
    for k in sorted(range(1, depth), key=lambda k: (min(k, depth - k), k)):
        z_in[k] = send_slot(me, at(core, (me + 4 * k) % n))
    order = [0] + list(z_in)
    for k in order:
        if k:
            z_in[k].wait_recv()
        x_in[k] = send_slot(column(me, k), at(core, near_x))
        y_in[k] = send_slot(column(me, k), at(core, near_y))
        s_in.append(send_slot(column(me, k), at(1 - core, me)))
    for k in order:
        x_in[k].wait_recv()
        first = send_slot(column(near_x, k), at(core, near_y), 0, cut)
        s_in.append(send_slot(column(near_x, k), at(1 - core, me)))
        y_in[k].wait_recv()
        second = send_slot(column(near_y, k), at(core, near_x), cut, rows)
        s_in.append(send_slot(column(near_y, k), at(1 - core, me)))
        d_in[k] = (first, second)
    for k in order:
        for c in d_in[k]:
            c.wait_recv()
        s_in.append(send_slot(column(near_xy, k), at(1 - core, me)))
    ints_copy.wait_recv()
    both[core] = ints_ref[:, pl.ds(mine, half)]
    for c in s_in:
        c.wait_recv()
    for c in started:
        c.wait_send()
    for t in range(2):
        vecf[...] = jnp.zeros(vecf.shape, F32)
        for i in range(n):
            unpack_rows(plan, i, slots[t, i], w.at[t], whf, vecf, [scratch.at[0], scratch.at[1]])
        for j in range(5):
            wh[t, :, D * j : D * j + D] = whf[D * j : D * j + D].astype(BF)
        vec[t] = vecf[...].astype(BF)
    total = jnp.zeros((1, D), F32)
    for i in range(n):
        tail = slots[0, i, rows - 16 : rows].astype(F32)
        total = total + tail[15:16]
    weight_sum = jnp.sum(jnp.where(lane < 3, total, 0.0), axis=1, keepdims=True)
    rw[...] = jnp.broadcast_to(imp_ref[:, pl.ds(mine, half)].astype(F32) / weight_sum, (8, half))


def gather(plan, p128, ints, imp):
    n, rows = plan.n, plan.slot
    half = ints.shape[1] // 2
    vm = pl.BlockSpec(memory_space=pltpu.VMEM)
    height = p128.shape[0]
    tall = max(2 * rows, height + 40) + 80
    copies = 1 + (n // 4 - 1) + 2 * (n // 4) + 2 * (n // 4) + n
    return pl.pallas_call(
        functools.partial(gather_kernel, plan),
        out_shape=(
            jax.ShapeDtypeStruct((2, A_ROWS, D), BF),
            jax.ShapeDtypeStruct((2, D, HPAD), BF),
            jax.ShapeDtypeStruct((2, 128, D), BF),
            jax.ShapeDtypeStruct((2, 8, half), jnp.int32),
            jax.ShapeDtypeStruct((8, half), F32),
        ),
        in_specs=[vm] * 3,
        out_specs=(vm,) * 5,
        scratch_shapes=[
            pltpu.VMEM((2, n, rows, D), BF),
            pltpu.VMEM((tall, 128), F32),
            pltpu.VMEM((height + 128, 128), F32),
            pltpu.VMEM((height + 40, 128), F32),
            pltpu.VMEM((2, rows, 128), F32),
            pltpu.VMEM((HPAD, D), F32),
            pltpu.VMEM((128, D), F32),
            pltpu.SemaphoreType.DMA((copies,)),
            pltpu.SemaphoreType.DMA((copies,)),
        ],
        compiler_params=pltpu.CompilerParams(
            collective_id=0, has_side_effects=True, vmem_limit_bytes=48 * 1024 * 1024
        ),
    )(p128, ints, imp)


def chunks(height):
    step = max(c for c in range(8, 113, 8) if height % c == 0)
    return [(lo, lo + step) for lo in range(0, height, step)]


def lay_flat(plan, me, slot128, flat, rolled):
    height = rolled.shape[0] - 40
    start = me * plan.length
    shift = start % 128
    first = start // 128
    base = plan.at(plan.a_base, me)
    row = lax.broadcasted_iota(jnp.int32, (height + 8, 128), 0)
    flat[...] = jnp.zeros(flat.shape, F32)

    @pl.when(plan.at(plan.a_rows, me) > 0)
    def _():
        rows = slot128[pl.ds(first - 2 * base, height + 8)]
        flat[16 : 24 + height] = jnp.where(row + first < 2 * A_ROWS, rows, 0.0)

    v_start = (A_ROWS * D + D * HEADS) // 128
    v_rows, v_off, v_first = (plan.at(t, me) for t in (plan.v_rows, plan.v_off, plan.v_first))
    tall_v = min(height, -(-2 * max(plan.v_rows) // 8) * 8)

    @pl.when(v_rows > 0)
    def _():
        inside = plan.at([max(0, v_start - i * plan.length // 128) for i in range(plan.n)], me)
        source = 2 * v_off + first + inside - v_start - 2 * v_first
        to = pl.ds(16 + inside, tall_v)
        flat[to] = flat[to] + slot128[pl.ds(source, tall_v)]

    h_first, h_rows, h_off = (plan.at(t, me) for t in (plan.h_first, plan.h_rows, plan.h_off))

    @pl.when(h_rows > 0)
    def _():
        tall_h = plan.image
        source = slot128.at[pl.ds(pl.multiple_of(2 * h_off, 8), 10 * plan.heads + 6)]
        it = lax.broadcasted_iota(jnp.int32, (16, 128), 0)
        lane = lax.broadcasted_iota(jnp.int32, (16, 128), 1)
        rolled[0 : tall_h + 8] = jnp.zeros((tall_h + 8, 128), F32)
        for k in range(plan.heads):
            row, turn = HEADS * k // 128, HEADS * k % 128
            kept = (it * 128 + lane < HEADS) & (k < h_rows)
            value = pltpu.roll(jnp.where(kept, source[10 * k : 10 * k + 16], 0.0), turn, 1)
            above = jnp.concatenate([jnp.zeros((8, 128), F32), value], 0)[7:23]
            rolled[row : row + 16] = rolled[row : row + 16] + jnp.where(lane >= turn, value, above)
        begin = A_ROWS * D + HEADS * h_first - 128 * first + 128 * 16
        turn = begin % 128
        slot128[0:8] = jnp.zeros((8, 128), F32)
        slot128[8 : 8 + tall_h] = pltpu.roll(rolled[0:tall_h], turn, 1)
        lane = lax.broadcasted_iota(jnp.int32, (tall_h, 128), 1)
        moved = jnp.where(lane >= turn, slot128[8 : 8 + tall_h], slot128[7 : 7 + tall_h])
        to = pl.ds(begin // 128, tall_h)
        flat[to] = flat[to] + moved

    rolled[0 : height + 8] = pltpu.roll(flat[16 : 24 + height], (128 - shift) % 128, 1)
    for lo, hi in chunks(height):
        lane = lax.broadcasted_iota(jnp.int32, (hi - lo, 128), 1)
        flat[lo:hi] = jnp.where(lane < 128 - shift, rolled[lo:hi], rolled[lo + 1 : hi + 1])


def pack_slots(plan, core, gw, gh, gv, rgw, rgh, rgv, slots, sums, vsum, scratch):
    total = gv[core].astype(F32) + rgv[...]
    for kind in range(3):
        vsum[kind * (BLOCKS + 1) : (kind + 1) * (BLOCKS + 1)] = total[kind, 0 : BLOCKS + 1]
    sums[...] = gh[core].astype(F32) + rgh[...].astype(F32)
    for i in range(plan.n):
        base, rows = plan.a_base[i], plan.a_rows[i]
        h_rows, h_off, h_first = plan.h_rows[i], plan.h_off[i], plan.h_first[i]
        v_rows, v_off, v_first = plan.v_rows[i], plan.v_off[i], plan.v_first[i]
        slots[i, rows : plan.slot] = jnp.zeros((plan.slot - rows, D), BF)
        if rows:
            added = gw[core, base : base + rows].astype(F32) + rgw[base : base + rows].astype(F32)
            slots[i, 0:rows] = added.astype(BF)
        if h_rows or v_rows:
            scratch[...] = jnp.zeros(scratch.shape, F32)
            for half in range(2):
                for j in range(5 if h_rows else 0):
                    cols = slice(D * j + 128 * half, D * j + 128 * half + 128)
                    scratch[half, pl.ds(h_off + j, h_rows, stride=5)] = sums[h_first : h_first + h_rows, cols]
                if v_rows:
                    scratch[half, v_off : v_off + v_rows] = vsum[v_first : v_first + v_rows, 128 * half : 128 * half + 128]
            whole = jnp.concatenate([scratch[0], scratch[1]], 1)
            slots[i, rows : plan.slot] = whole[rows:].astype(BF)


def segment_bounds():
    first = [0] + [(CAT + j * D) * D for j in range(BLOCKS + 1)]
    return list(zip(first, first[1:] + [A_ROWS * D + D * HEADS]))


class Rows:
    def __init__(self, ref):
        self.ref, self.height = ref, ref.shape[0]

    def chunks(self):
        return chunks(self.height)

    def get(self, lo, hi):
        return self.ref[lo:hi]

    def put(self, lo, hi, value):
        self.ref[lo:hi] = value


class Flat:
    def __init__(self, ref, buffer):
        self.ref, self.buffer, self.length = ref, buffer, ref.shape[1]
        self.whole = self.length // 1024 * 8
        self.height = -(-self.length // 1024) * 8

    def chunks(self):
        step = next(s for s in range(64, 0, -8) if self.whole % s == 0)
        return [(lo, lo + step) for lo in range(0, self.whole, step)] + [(self.whole, self.height)]

    def ends(self):
        rows = (self.length - 128 * self.whole) // 128
        return rows, self.length % 128, 128 * self.whole, 128 * (self.whole + rows)

    def get(self, lo, hi):
        if hi <= self.whole:
            return self.ref[0:1, 128 * lo : 128 * hi].reshape(hi - lo, 128)
        rows, lanes, first, last = self.ends()
        self.buffer[...] = jnp.zeros((8, 128), F32)
        if rows:
            self.buffer[0:rows] = self.ref[0:1, first:last].reshape(rows, 128)
        if lanes:
            self.buffer[rows : rows + 1, 0:lanes] = self.ref[0:1, last : self.length]
        return self.buffer[...]

    def put(self, lo, hi, value):
        if hi <= self.whole:
            self.ref[0:1, 128 * lo : 128 * hi] = value.reshape(1, 128 * (hi - lo))
            return
        rows, lanes, first, last = self.ends()
        if rows:
            self.ref[0:1, first:last] = value[0:rows].reshape(1, 128 * rows)
        if lanes:
            self.ref[0:1, last : self.length] = value[rows : rows + 1, 0:lanes]


def update_shard(plan, me, p_ref, m_ref, v_ref, outs, flat, squares, sq_in, push, to_plane, to_z):
    first_out, second_out, new_out, norm_out = outs
    height = p_ref.height
    start = me * plan.length
    correction = 1.0 - 0.5**STEP
    bounds = segment_bounds()

    def place(lo, hi):
        shape = (hi - lo, 128)
        return 128 * lo + 128 * lax.broadcasted_iota(jnp.int32, shape, 0) + lax.broadcasted_iota(jnp.int32, shape, 1)

    for lo, hi in p_ref.chunks():
        spot = place(lo, hi)
        grad = jnp.where(spot < plan.length, flat[lo:hi], 0.0)
        first_new = 0.5 * m_ref.get(lo, hi) + 0.5 * grad
        second_new = 0.5 * v_ref.get(lo, hi) + 0.5 * grad * grad
        first_out.put(lo, hi, first_new)
        second_out.put(lo, hi, second_new)
        decay = jnp.where(spot < bounds[-1][1] - start, 0.01 * p_ref.get(lo, hi), 0.0)
        update = first_new / correction / (jnp.sqrt(second_new / correction) + 1e-06) + decay
        flat[lo:hi] = jnp.where(spot < plan.length, update, 0.0)
        new_out.put(lo, hi, p_ref.get(lo, hi) - 0.5 * update)
    squares[...] = jnp.zeros(squares.shape, F32)

    def each_segment(body):
        for j, (first, last) in enumerate(bounds):
            pl.when((first < start + plan.length) & (last > start))(lambda j=j, first=first, last=last: body(j, first, last))

    def square_sums(j, first, last):
        weight, change = jnp.zeros((8, 128), F32), jnp.zeros((8, 128), F32)
        for lo, hi in p_ref.chunks():
            spot = place(lo, hi)
            inside = (spot >= first - start) & (spot < last - start)
            p, u = jnp.where(inside, p_ref.get(lo, hi), 0.0), jnp.where(inside, flat[lo:hi], 0.0)
            weight = weight + jnp.sum((p * p).reshape(-1, 8, 128), axis=0)
            change = change + jnp.sum((u * u).reshape(-1, 8, 128), axis=0)
        squares[0, j : j + 1] = jnp.sum(weight, axis=0, keepdims=True)
        squares[0, 16 + j : 17 + j] = jnp.sum(change, axis=0, keepdims=True)

    each_segment(square_sums)
    total = squares[0]
    for hop, targets in enumerate((to_plane, to_z)):
        lands = range(3) if hop == 0 else range(3, 3 + len(to_z))
        for c in [push(squares.at[hop], sq_in.at[k], to) for k, to in zip(lands, targets)]:
            c.wait_recv()
        for k in lands:
            total = total + sq_in[k]
        squares[hop + 1] = total
    norm = jnp.sqrt(jnp.sum(total, axis=1, keepdims=True))
    squares[3] = jnp.broadcast_to(norm, (32, 128))
    line = jnp.sqrt(jnp.sum(jnp.concatenate([total, jnp.zeros((96, 128), F32)], 0).T, axis=0, keepdims=True))
    norm_out[0:1] = line[:, 0:MATS]
    norm_out[1:2] = pltpu.roll(line, 112, 1)[:, 0:MATS]

    def scaled(j, first, last):
        ratio = squares[3, j : j + 1] / squares[3, 16 + j : 17 + j]
        for lo, hi in p_ref.chunks():
            spot = place(lo, hi)
            inside = (spot >= first - start) & (spot < last - start)
            new_out.put(lo, hi, jnp.where(inside, p_ref.get(lo, hi) - 0.5 * ratio * flat[lo:hi], new_out.get(lo, hi)))

    each_segment(scaled)


def reduce_kernel(
    plan, gw, gh, gv, st, ig, p_ref, m_ref, v_ref,
    st_out, ig_out, first_out, second_out, new_out, norm_out,
    rgw, rgh, rgv, slots, sums, vsum, scratch, in_d, in_x, in_y, in_z, slot128, flat, rolled, squares, sq_in,
    send, recv, local,
):
    n, rows = plan.n, plan.slot
    depth, cut = n // 4, plan.slot // 2
    core, me, near_x, near_y = neighbours(n)
    near_xy = near_x + near_y - me
    barrier = greet(core, me, near_x, near_y, n)
    pl.semaphore_wait(barrier, depth + 3)
    half = st.shape[1]
    number = iter(range(1 << 20))
    started = []

    def copy(src, dst, to):
        slot = next(number)
        c = pltpu.make_async_remote_copy(
            src_ref=src, dst_ref=dst, send_sem=send.at[slot], recv_sem=recv.at[slot], device_id=to, device_id_type=MESH
        )
        c.start()
        started.append(c)
        return c

    def column(index, k):
        return (index + n - 4 * k) % n

    sibling = at(1 - core, me)
    early = [
        copy(gw.at[1 - core], rgw, sibling),
        copy(gh.at[1 - core], rgh, sibling),
        copy(gv.at[1 - core], rgv, sibling),
    ]
    mine = pl.ds(pl.multiple_of(core * half, half), half)
    late = [
        copy(st.at[1 - core], st_out.at[mine], sibling),
        copy(ig.at[1 - core], ig_out.at[mine], sibling),
    ]
    stay = [
        pltpu.make_async_copy(st.at[core], st_out.at[mine], local.at[0]),
        pltpu.make_async_copy(ig.at[core], ig_out.at[mine], local.at[1]),
    ]
    for c in stay:
        c.start()
    for c in early:
        c.wait_recv()
    pack_slots(plan, core, gw, gh, gv, rgw, rgh, rgv, slots, sums, vsum, scratch)
    order = list(range(1, depth)) + [0]
    to_x, to_y = at(core, near_x), at(core, near_y)
    halves = {}
    for k in order:
        diagonal = column(near_xy, k)
        halves[k] = (
            copy(slots.at[diagonal, pl.ds(0, cut)], in_d.at[k, pl.ds(0, cut)], to_y),
            copy(slots.at[diagonal, pl.ds(cut, rows - cut)], in_d.at[k, pl.ds(cut, rows - cut)], to_x),
        )
    fulls = {}
    for k in order:
        ox, oy = column(near_x, k), column(near_y, k)
        halves[k][0].wait_recv()
        slots[ox, 0:cut] = (slots[ox, 0:cut].astype(F32) + in_d[k, 0:cut].astype(F32)).astype(BF)
        first = copy(slots.at[ox], in_x.at[k], to_x)
        halves[k][1].wait_recv()
        slots[oy, cut:rows] = (slots[oy, cut:rows].astype(F32) + in_d[k, cut:rows].astype(F32)).astype(BF)
        fulls[k] = (first, copy(slots.at[oy], in_y.at[k], to_y))
    along = {}
    for k in order:
        own = column(me, k)
        for c in fulls[k]:
            c.wait_recv()
        if k:
            total = slots[own].astype(F32) + in_x[k].astype(F32) + in_y[k].astype(F32)
            slots[own] = total.astype(BF)
            along[k] = copy(slots.at[own], in_z.at[k], at(core, own))
    for c in along.values():
        c.wait_recv()
    total = slots[me].astype(F32) + in_x[0].astype(F32) + in_y[0].astype(F32)
    for k in along:
        total = total + in_z[k].astype(F32)
    slot128[...] = jnp.zeros(slot128.shape, F32)
    slot128[pl.ds(0, rows, stride=2)] = total[:, 0:128]
    slot128[pl.ds(1, rows, stride=2)] = total[:, 128:D]
    lay_flat(plan, me, slot128, flat, rolled)

    to_z = [at(core, column(me, k)) for k in range(1, depth)]
    outs = (Rows(first_out), Rows(second_out), Rows(new_out), norm_out)
    to_plane = [to_x, to_y, at(core, near_xy)]
    update_shard(plan, me, Rows(p_ref), Rows(m_ref), Rows(v_ref), outs, flat, squares, sq_in, copy, to_plane, to_z)
    for c in late:
        c.wait_recv()
    for c in stay:
        c.wait()
    for c in started:
        c.wait_send()


def reduce_and_update(plan, gw, gh, gv, st, ig, p128, m128, v128):
    n, rows = plan.n, plan.slot
    depth = n // 4
    half = st.shape[1]
    height = p128.shape[0]
    vm = pl.BlockSpec(memory_space=pltpu.VMEM)
    hbm = pl.BlockSpec(memory_space=pl.ANY)
    copies = 5 + 2 * depth + 2 * depth + (depth - 1) + (depth - 1) + 3
    flat32 = jax.ShapeDtypeStruct((height, 128), F32)
    return pl.pallas_call(
        functools.partial(reduce_kernel, plan),
        out_shape=(
            jax.ShapeDtypeStruct((2 * half, D), BF),
            jax.ShapeDtypeStruct((2 * half, D), F32),
            flat32,
            flat32,
            flat32,
            jax.ShapeDtypeStruct((2, MATS), F32),
        ),
        in_specs=[vm] * 3 + [hbm] * 2 + [vm] * 3,
        out_specs=(hbm, hbm, vm, vm, vm, vm),
        scratch_shapes=[
            pltpu.VMEM((A_ROWS, D), BF),
            pltpu.VMEM((D, HPAD), BF),
            pltpu.VMEM(gv.shape[1:], F32),
            pltpu.VMEM((n, rows, D), BF),
            pltpu.VMEM((D, HPAD), F32),
            pltpu.VMEM((40, D), F32),
            pltpu.VMEM((2, rows, 128), F32),
            pltpu.VMEM((depth, rows, D), BF),
            pltpu.VMEM((depth, rows, D), BF),
            pltpu.VMEM((depth, rows, D), BF),
            pltpu.VMEM((depth, rows, D), BF),
            pltpu.VMEM((max(2 * rows, height + 48) + 80, 128), F32),
            pltpu.VMEM((height + 128, 128), F32),
            pltpu.VMEM((height + 40, 128), F32),
            pltpu.VMEM((4, 32, 128), F32),
            pltpu.VMEM((2 + depth, 32, 128), F32),
            pltpu.SemaphoreType.DMA((copies,)),
            pltpu.SemaphoreType.DMA((copies,)),
            pltpu.SemaphoreType.DMA((2,)),
        ],
        compiler_params=pltpu.CompilerParams(
            collective_id=1, has_side_effects=True, vmem_limit_bytes=48 * 1024 * 1024
        ),
    )(gw, gh, gv, st, ig, p128, m128, v128)


class Copies:
    def __init__(self, send, recv):
        self.send, self.recv, self.made, self.sent = send, recv, [], set()

    def add(self, src, dst, to, recv_slot=None, only=None):
        self.made.append((src, dst, to, recv_slot, only))
        return len(self.made) - 1

    def get(self, number):
        src, dst, to, recv_slot, _ = self.made[number]
        return pltpu.make_async_remote_copy(
            src_ref=src(), dst_ref=dst(), send_sem=self.send.at[number],
            recv_sem=self.recv.at[number] if recv_slot is None else recv_slot(),
            device_id=to(), device_id_type=MESH,
        )

    def start(self, *numbers):
        for number in numbers:
            self.get(number).start()

    def arrive(self, *numbers):
        for number in numbers:
            self.get(number).wait_recv()

    def leave(self, *numbers):
        for number in numbers:
            only = self.made[number][4]
            if number not in self.sent and only is None:
                self.get(number).wait_send()
            elif number not in self.sent:
                pl.when(only())(lambda number=number: self.get(number).wait_send())
            self.sent.add(number)


def fused_fits(plan):
    depth, half = plan.n // 4, plan.slot // 2
    plain = [b + plan.slot <= A_ROWS for b, h, v in zip(plan.a_base, plan.h_rows, plan.v_rows) if not (h or v)]
    vectors = [rows for rows in plan.v_rows if rows]
    return (
        all(plain)
        and vectors == [3 * (BLOCKS + 1)]
        and plan.n % 4 == 0
        and half >= 32
        and 4 * half <= HPAD
        and 2 * depth * plan.slot <= (BLOCKS + 1) * D
        and depth == 4
        and max(plan.a_rows) <= plan.slot
    )


def train_kernel(
    plan, x_ref, codes_ref, targets_ref, visits_ref, imp_ref, p_ref, m_ref, v_ref,
    st_out, ig_out, first_out, second_out, new_out, norm_out,
    w, wh, vec, both, away, rw, eye, wt, wht, vt, gsb, xt, mix, xh, gp, rstd, mean, stream, ex, br, dm, acc, lg, dl,
    gw, gh, gv, packed, st_stage, slot128, flat, rolled, vsum, vacc, vin, owned, squares, sq_in, tail,
    send, recv, z_recv, own_recv, local, ready,
):
    n, rows = plan.n, plan.slot
    depth, hrows = n // 4, plan.slot // 2
    cut = hrows // 32 * 16
    core, me, near_x, near_y = neighbours(n)
    near_xy = near_x + near_y - me
    width = both.shape[2]
    params_in, first_new, second_new, new = (Flat(ref, tail) for ref in (p_ref, first_out, second_out, new_out))
    moments = [
        pltpu.make_async_copy(src, dst, local.at[3 + i])
        for i, (src, dst) in enumerate(((m_ref, first_out), (v_ref, second_out)))
    ]
    z_me, j_me = me // 4, me % 4
    copies = Copies(send, recv)
    scratch = [slot128.at[0:rows], slot128.at[rows : 2 * rows]]
    barrier = greet(core, me, near_x, near_y, n, True)
    mine = pl.multiple_of(core * width, width)
    theirs = pl.multiple_of((1 - core) * width, width)
    x_copy = pltpu.make_async_copy(x_ref.at[pl.ds(mine, width)], st_stage.at[0], local.at[0])
    x_copy.start()
    for c in moments:
        c.start()
    for to, half in ((both.at[core], mine), (away, theirs)):
        cols = pl.ds(half, width)
        to[0:1] = codes_ref[:, cols]
        to[1:2] = targets_ref[0, :, cols]
        to[2:6] = visits_ref[:, cols]
        to[6:7] = targets_ref[1, :, cols]
        to[7:8] = targets_ref[2, :, cols]
    height = params_in.height
    for lo, hi in params_in.chunks():
        slot128[lo:hi] = params_in.get(lo, hi)
    place_shard(plan, me, slot128.at[0:height], slot128, flat, rolled)

    spare = (BLOCKS + 1) * D

    def slot_part(t, i, lo, count):
        row = pl.multiple_of(spare + rows * (t * depth + i // 4) + lo, 16)
        return xh.at[pl.ds(row, count), pl.ds(pl.multiple_of((i % 4) * D, D), D)]

    def column(index, k):
        return (index + n - 4 * k) % n

    def sibling():
        return at(1 - core, me)

    def same(make, to):
        return copies.add(make, make, to)

    low = core * hrows
    other_low = (1 - core) * hrows
    order = [0] + sorted(range(1, depth), key=lambda k: (min(k, depth - k), k))
    to_x, to_y, to_d = (lambda: at(core, near_x)), (lambda: at(core, near_y)), (lambda: at(core, near_xy))
    swap_ints = copies.add(lambda: away, lambda: both.at[core], sibling)

    def arrival(t, number):
        return own_recv.at[t * (depth + 2) + number]

    own_targets = [(lambda: near_x), (lambda: near_y)] + [lambda k=k: (me + 4 * k) % n for k in order[1:]]
    own_sends = [copies.add(lambda: slot_part(core, me, 0, rows), lambda: slot_part(core, me, 0, rows), sibling, lambda: arrival(core, 0))]
    for number, target in enumerate(own_targets, 1):
        for h in range(2):
            make = lambda h=h: slot_part(core, me, h * hrows, hrows)
            own_sends.append(
                copies.add(make, make, lambda h=h, target=target: at(h, target()), lambda number=number: arrival(core, number))
            )
    own_sends = own_sends[3 + 2 :] + own_sends[1:5] + own_sends[:1]

    def own_arrive(t, number, make):
        pltpu.make_async_remote_copy(
            src_ref=make(), dst_ref=make(), send_sem=send.at[0], recv_sem=arrival(t, number), device_id=sibling(), device_id_type=MESH
        ).wait_recv()

    gathers = []
    for t in range(2):
        g = {}
        for k in order:
            if k:
                g["x", k] = same(lambda t=t, k=k: slot_part(t, column(me, k), low, hrows), to_x)
                g["y", k] = same(lambda t=t, k=k: slot_part(t, column(me, k), low, hrows), to_y)
            g["d", k] = (
                same(lambda t=t, k=k: slot_part(t, column(near_x, k), low, cut), to_y),
                same(lambda t=t, k=k: slot_part(t, column(near_y, k), low + cut, hrows - cut), to_x),
            )
            g["s", k] = [
                same(lambda t=t, k=k, index=index: slot_part(t, column(index, k), low, hrows), sibling) if index is not me or k else None
                for index in (me, near_x, near_y, near_xy)
            ]
        gathers.append(g)

    def gather_0(t):
        pl.when(core == t)(lambda: copies.start(*own_sends))

    def gather_1(t):
        g = gathers[t]
        for number, k in enumerate(order[1:], 3):
            own_arrive(t, number, lambda: slot_part(t, me, low, hrows))
            copies.start(g["x", k], g["y", k], g["s", k][0])

    def gather_2(t):
        g = gathers[t]
        for k in order:
            if k:
                copies.arrive(g["x", k])
            else:
                own_arrive(t, 1, lambda: slot_part(t, me, low, hrows))
            copies.start(g["d", k][0], g["s", k][1])
            if k:
                copies.arrive(g["y", k])
            else:
                own_arrive(t, 2, lambda: slot_part(t, me, low, hrows))
            copies.start(g["d", k][1], g["s", k][2])

    def gather_3(t):
        g = gathers[t]
        for k in order:
            copies.arrive(*g["d", k])
            copies.start(g["s", k][3])

    def gather_4(t):
        g = gathers[t]
        pl.when(core != t)(lambda: own_arrive(t, 0, lambda: slot_part(t, me, 0, rows)))
        for k in order:
            copies.arrive(*(c for c in g["s", k] if c is not None))

    def unpack(t):
        lg[4 * D : 5 * D, 128:D] = jnp.zeros((D, 128), F32)
        vsum[...] = jnp.zeros(vsum.shape, F32)
        for i in range(n):
            row, lane = spare + rows * (t * depth + i // 4), (i % 4) * D
            unpack_rows(plan, i, xh[row : row + rows, lane : lane + D], w.at[t], lg, vsum, scratch)
        for j in range(5):
            wh[t, :, D * j : D * j + D] = lg[D * j : D * j + D].astype(BF)
        vec[t] = vsum[...].astype(BF)

    total = jnp.sum(imp_ref[...].astype(F32), axis=1, keepdims=True)
    lane_d = lax.broadcasted_iota(jnp.int32, (1, D), 1)
    hi, mid, lo = split3(total)
    left = slot128[pl.ds(0, rows, stride=2)]
    right = slot128[pl.ds(1, rows, stride=2)]
    own = jnp.concatenate([left, right], 1)
    last = jnp.where(lane_d == 0, hi, jnp.where(lane_d == 1, mid, jnp.where(lane_d == 2, lo, 0.0)))
    last_row = lax.broadcasted_iota(jnp.int32, (rows, D), 0) == rows - 1
    slot_part(core, me, 0, rows)[...] = jnp.where(last_row, last, own).astype(BF)
    pl.semaphore_wait(barrier, depth + 3 + 2 + depth - 1)
    gather_0(0)
    copies.start(swap_ints)
    eye[...] = identity(D)
    x_copy.wait()
    for c in range(0, width, CB):
        xt[0, 0:D, c : c + CB] = nt(eye[...], st_stage[0, c : c + CB, :]).astype(BF)
    gather_1(0)
    gather_0(1)
    gather_2(0)
    gather_3(0)
    copies.arrive(swap_ints)
    gather_4(0)
    unpack(0)
    total = jnp.zeros((1, D), F32)
    for i in range(n):
        row, lane = spare + rows * (i // 4), (i % 4) * D
        total = total + xh[row + rows - 16 : row + rows, lane : lane + D].astype(F32)[15:16]
    weight_sum = jnp.sum(jnp.where(lane_d < 3, total, 0.0), axis=1, keepdims=True)
    rw[...] = jnp.broadcast_to(imp_ref[:, pl.ds(mine, width)].astype(F32) / weight_sum, (8, width))

    fwd = (eye, w, wh, vec, wt, vt, gsb, xt, mix, xh, gp, rstd, stream, mean, both, width)

    def during_forward(k):
        pl.when(k == 6)(lambda: gather_2(1))

    def emit_states(t, c):
        at_rows = pl.ds(pl.multiple_of(c * CB, CB), CB)
        st_stage[t, at_rows, :] = nt(eye[...], xt[t + 1, 0:D, at_rows]).astype(BF)

    def beside_forward(k):
        transposed_head(eye, wh.at[1], wht, (k - 1) % (HPAD // D))
        emit_states(0, (k - 1) % (width // CB))

    def beside_backward(i):
        transposed_head(eye, wh.at[0], wht, i % (HPAD // D))

    gather_1(1)
    forward_tower(0, fwd, during_forward, lambda: gather_3(1))
    gather_4(1)
    copies.leave(*range(len(copies.made)))
    unpack(1)
    forward_tower(1, fwd, None, None, beside_forward)
    for c in range(width // CB):
        emit_states(1, c)
    out_rows = pl.ds(mine, width)
    st_copy = copies.add(lambda: st_stage.at[1 - core], lambda: st_out.at[out_rows], sibling)
    copies.start(st_copy)
    st_stay = pltpu.make_async_copy(st_stage.at[core], st_out.at[out_rows], local.at[1])
    st_stay.start()

    packed_of = [i for i in range(n) if plan.h_rows[i] or plan.v_rows[i]]
    owner = plan.v_rows.index(3 * (BLOCKS + 1))

    early = (2, 3)

    def piece(t, zz, b, lo, count):
        if t == 1 and zz in early:
            arena, first, q = dl, 0, 7 * early.index(zz) + b
        elif t == 1:
            arena, first, q = mix, BLOCKS * (D + 16), 7 * zz + b
        else:
            arena, first, q = xh, spare, 7 * zz + b
        row = pl.multiple_of(first + hrows * (q // 4) + lo, 16)
        return arena.at[pl.ds(row, count), pl.ds(pl.multiple_of((q % 4) * D, D), D)]

    def block(t, zz, b):
        return piece(t, zz, b, 0, hrows)

    def z_in(h, k):
        return st_stage.at[0, pl.ds(pl.multiple_of(hrows * (h * (depth - 1) + k - 1), 16), hrows)]

    def z_out(t, zz):
        if t == 1 and zz in early:
            return st_stage.at[1, pl.ds(hrows * early.index(zz), hrows)]
        return block(t, zz, j_me)

    def slot_half(t, i, lo):
        if i in packed_of:
            return packed.at[packed_of.index(i), pl.ds(pl.multiple_of(lo, 16), hrows)]
        return gw.at[t, pl.ds(pl.multiple_of(plan.a_base[i] + lo, 16), hrows)]

    j_x, j_y, j_d = near_x % 4, near_y % 4, near_xy % 4
    direct = ((0, 0), (0, 1), (0, 2), (1, 2), (1, 3))
    jobs = {}
    for t in range(2):
        for zz in range(depth):
            job = {}
            job["swap"] = [
                copies.add(lambda t=t, i=4 * zz + j: slot_half(t, i, other_low), lambda t=t, zz=zz, j=j: block(t, zz, j), sibling)
                for j in range(4)
            ]
            if (t, zz) in direct:
                job["d"] = [copies.add(lambda t=t, zz=zz: block(t, zz, j_d), lambda t=t, zz=zz: block(t, zz, 4), to_d)]
            else:
                job["d"] = [
                    copies.add(
                        lambda t=t, zz=zz, lo=lo, count=count: piece(t, zz, j_d, lo, count),
                        lambda t=t, zz=zz, lo=lo, count=count: piece(t, zz, 4, lo, count),
                        to,
                    )
                    for to, lo, count in ((to_y, 0, cut), (to_x, cut, hrows - cut))
                ]
            job["x"] = copies.add(lambda t=t, zz=zz: block(t, zz, j_x), lambda t=t, zz=zz: block(t, zz, 5), to_x)
            job["y"] = copies.add(lambda t=t, zz=zz: block(t, zz, j_y), lambda t=t, zz=zz: block(t, zz, 6), to_y)
            job["z"] = copies.add(
                lambda t=t, zz=zz: z_out(t, zz),
                lambda zz=zz: z_in(core, (zz + depth - z_me) % depth),
                lambda t=t, zz=zz: at(t, 4 * zz + j_me),
                lambda zz=zz: z_recv.at[core * depth + (zz + depth - z_me) % depth],
                lambda zz=zz: z_me != zz,
            )
            jobs[t, zz] = job

    def pack(t, planes):
        wanted = [i for i in packed_of if i // 4 in planes]
        for i in wanted:
            a_rows, h_rows, h_off, h_first = plan.a_rows[i], plan.h_rows[i], plan.h_off[i], plan.h_first[i]
            to = packed.at[packed_of.index(i)]
            for part in scratch:
                part[...] = jnp.zeros(part.shape, F32)
            lo16, hi16 = h_first // 16 * 16, -(-(h_first + h_rows) // 16) * 16
            for half in range(2):
                for j in range(5 if h_rows else 0):
                    cols = slice(D * j + 128 * half, D * j + 128 * half + 128)
                    value = gh[t, lo16:hi16, cols].astype(F32)[h_first - lo16 : h_first - lo16 + h_rows]
                    scratch[half][pl.ds(h_off + j, h_rows, stride=5)] = value
            whole = jnp.concatenate([scratch[0][...], scratch[1][...]], 1)
            to[a_rows:rows] = whole[a_rows:].astype(BF)
            if a_rows:
                to[0:a_rows] = gw[t, plan.a_base[i] : plan.a_base[i] + a_rows]

    def plus(*refs):
        value = refs[0][...].astype(F32)
        for ref in refs[1:]:
            value = value + ref[...].astype(F32)
        return value

    def sum_0(t, zz):
        copies.start(*jobs[t, zz]["swap"])

    def sum_1(t, zz):
        job = jobs[t, zz]
        for j in range(4):
            copies.arrive(job["swap"][j])
            target = block(t, zz, j)
            target[...] = plus(slot_half(t, 4 * zz + j, low), target).astype(BF)
        copies.start(*job["d"])
        if (t, zz) in direct:
            copies.start(job["x"], job["y"])

    def sum_2(t, zz):
        job = jobs[t, zz]
        for side, copy, j, lo, count in (("x", job["d"][0], j_x, 0, cut), ("y", job["d"][1], j_y, cut, hrows - cut)):
            copies.arrive(copy)
            target = piece(t, zz, j, lo, count)
            target[...] = plus(target, piece(t, zz, 4, lo, count)).astype(BF)
            copies.start(job[side])

    def sum_3(t, zz):
        job = jobs[t, zz]
        copies.arrive(job["x"], job["y"])
        value = plus(block(t, zz, j_me), block(t, zz, 5), block(t, zz, 6))
        if (t, zz) in direct:
            copies.arrive(*job["d"])
            value = value + block(t, zz, 4)[...].astype(F32)

        @pl.when(z_me != zz)
        def _():
            z_out(t, zz)[...] = value.astype(BF)
            copies.start(job["z"])

        @pl.when((z_me == zz) & (core == t))
        def _():
            final(core)[...] = value

        @pl.when((z_me == zz) & (core != t))
        def _():
            outgo[...] = value
            copies.start(hand_over)

    def sum_4():
        copies.arrive(hand_over)
        for h in range(2):
            for k in range(1, depth):
                src = z_in(h, k)
                pltpu.make_async_remote_copy(
                    src_ref=src, dst_ref=src, send_sem=send.at[0], recv_sem=z_recv.at[h * depth + k], device_id=sibling(), device_id_type=MESH
                ).wait_recv()
                final(h)[...] = final(h)[...] + src[...].astype(F32)

    def final(h):
        return owned.at[h]

    outgo = owned.at[2]

    def vector_step(step):
        sources = [gv.at[1 - core], vacc.at[0], vacc.at[1]]
        along = [lambda k=k: at(core, (me + 4 * k) % n) for k in range(1, depth)]
        targets = [[sibling], [to_x, to_y, to_d], along]
        if step:
            base = gv[core] if step == 1 else vacc[step - 2]
            for number, k in vector_copies[-1]:
                copies.arrive(number)
                base = base + vin[k]
            vacc[step - 1] = base
        if step < 3:
            started = []
            for k, to in enumerate(targets[step], (0, 1, 4)[step]):
                number = copies.add(lambda step=step: sources[step], lambda k=k: vin.at[k], to)
                copies.start(number)
                started.append((number, k))
            vector_copies.append(started)

    vector_copies = []
    hand_over = copies.add(lambda: outgo, lambda: final(core), sibling)
    peers = [(1 - core, me), (core, near_x), (core, near_y), (core, near_xy)] + [(1 - core, (me + 4 * k) % n) for k in range(1, depth)] + [(core, (me + 4 * k) % n) for k in range(1, depth)]

    bwd = (eye, w, wh, vec, wht, vt, gsb, xt, mix, xh, gp, rstd, stream, ex, br, dm, acc, lg, dl, both, rw, gw, gh, gv, dm, width)
    ig_copies = [copies.add(lambda: dm, lambda: ig_out.at[out_rows], sibling, None, lambda t=t: core != t) for t in range(2)]

    def ig_local():
        return pltpu.make_async_copy(dm, ig_out.at[out_rows], local.at[2])

    def emit_inputs(t):
        pl.when(core == t)(lambda: ig_local().start())
        pl.when(core != t)(lambda: copies.start(ig_copies[t]))

    def free_inputs(t):
        pl.when(core == t)(lambda: ig_local().wait())
        pl.when(core != t)(lambda: copies.get(ig_copies[t]).wait_send())

    def signal_ready(which):
        for to_core, to_index in peers:
            pl.semaphore_signal(ready.at[which], inc=1, device_id=at(to_core, to_index), device_id_type=MESH)

    def wait_ready(which):
        pl.semaphore_wait(ready.at[which], len(peers))

    def schedule(i, steps):
        for step in sorted({s[0] for s in steps}):

            def run(step=step):
                for s, f, *args in steps:
                    if s == step:
                        f(*args)

            pl.when(i == step)(run)

    def after_head_1():
        copies.leave(st_copy)
        st_stay.wait()
        signal_ready(0)

    def during_backward_1(i):
        schedule(i, [
            (2, wait_ready, 0), (2, pack, 1, (3,)), (2, sum_0, 1, 3),
            (4, sum_1, 1, 3), (4, pack, 1, (2,)), (4, sum_0, 1, 2),
            (6, sum_1, 1, 2),
            (8, sum_3, 1, 3),
        ])

    ex[...] = jnp.zeros_like(ex)
    backward_tower(1, bwd, after_head_1, during_backward_1, None, lambda: sum_3(1, 2), True, beside_backward)
    emit_inputs(1)
    signal_ready(1)
    for zz in early:
        job = jobs[1, zz]
        copies.leave(*job["swap"], *job["d"], job["x"], job["y"])

    def after_head_0():
        wait_ready(1)
        sum_0(1, 1)
        sum_0(1, 0)
        pack(0, (3,))
        sum_0(0, 3)

    def during_backward_0(i):
        schedule(i, [
            (1, sum_1, 1, 1), (1, sum_1, 1, 0),
            (2, sum_1, 0, 3),
            (4, sum_2, 1, 1), (4, sum_2, 1, 0), (4, pack, 0, (2,)), (4, sum_0, 0, 2),
            (5, sum_2, 0, 3),
            (6, sum_1, 0, 2),
            (8, sum_3, 1, 1), (8, sum_3, 1, 0), (8, sum_0, 0, 1),
            (9, sum_3, 0, 3), (9, sum_1, 0, 1),
        ])

    def after_weights():
        sum_0(0, 0)
        vector_step(0)

    backward_tower(0, bwd, after_head_0, during_backward_0, lambda: free_inputs(1), after_weights, True)
    emit_inputs(0)
    sum_1(0, 0)
    vector_step(1)
    sum_3(0, 2)
    sum_3(0, 1)
    sum_3(0, 0)
    vector_step(2)
    sum_4()
    vector_step(3)

    slot128[...] = jnp.zeros(slot128.shape, F32)
    for h in range(2):
        slot128[pl.ds(2 * hrows * h, hrows, stride=2)] = final(h)[:, 0:128]
        slot128[pl.ds(2 * hrows * h + 1, hrows, stride=2)] = final(h)[:, 128:D]

    @pl.when(me == owner)
    def _():
        for kind in range(3):
            first = 2 * (plan.v_off[owner] + kind * (BLOCKS + 1))
            for h in range(2):
                value = vacc[2, kind, 0 : BLOCKS + 1, 128 * h : 128 * h + 128]
                slot128[pl.ds(first + h, BLOCKS + 1, stride=2)] = value

    def push(src, dst, to):
        number = copies.add(lambda: src, lambda: dst, lambda: to)
        copies.start(number)
        return copies.get(number)

    lay_flat(plan, me, slot128, flat, rolled)
    for c in moments:
        c.wait()
    update_shard(
        plan, me, params_in, first_new, second_new, (first_new, second_new, new, norm_out),
        flat, squares, sq_in, push, [to_x(), to_y(), to_d()], [at(core, (me + 4 * k) % n) for k in range(1, depth)],
    )
    copies.arrive(st_copy)
    pl.when(core == 0)(lambda: copies.arrive(ig_copies[0]))
    pl.when(core == 1)(lambda: copies.arrive(ig_copies[1]))
    free_inputs(0)
    copies.sent.update(ig_copies)
    copies.leave(*range(len(copies.made)))


def finish_kernel(st, ig, first, second, new, norms, st_out, ig_out, first_out, second_out, new_out, low_out, norms_out, *rest):
    *held, into, outof = rest
    moves = []
    for src, dst, mid, parts in zip((new, ig, st, first, second), (new_out, ig_out, st_out, first_out, second_out), held, (1, 8, 4, 1, 1)):
        rows = src.shape[0] // parts
        for i in range(parts):
            at_rows = pl.ds(i * rows, rows)
            number = len(moves)
            moves.append(
                (
                    pltpu.make_async_copy(src.at[at_rows], mid.at[at_rows], into.at[number]),
                    pltpu.make_async_copy(mid.at[at_rows], dst.at[at_rows], outof.at[number]),
                )
            )
    for load, _ in moves:
        load.start()
    for load, store in moves:
        load.wait()
        store.start()
    size = new.shape[1]
    for lo in range(0, size, 8192):
        hi = min(lo + 8192, size)
        low_out[0:1, lo:hi] = held[0][0:1, lo:hi].astype(BF)
    norms_out[...] = norms[...]
    for _, store in moves:
        store.wait()


def finish(st, ig, first, second, new, norms):
    vm = pl.BlockSpec(memory_space=pltpu.VMEM)
    hbm = pl.BlockSpec(memory_space=pl.ANY)
    arrays = (st, ig, first, second, new)
    shapes = [jax.ShapeDtypeStruct(v.shape, v.dtype) for v in arrays]
    return pl.pallas_call(
        finish_kernel,
        out_shape=(*shapes, jax.ShapeDtypeStruct(new.shape, BF), jax.ShapeDtypeStruct(norms.shape, F32)),
        in_specs=[hbm] * 5 + [vm],
        out_specs=(hbm,) * 5 + (vm,) * 2,
        scratch_shapes=[pltpu.VMEM(v.shape, v.dtype) for v in (new, ig, st, first, second)] + [pltpu.SemaphoreType.DMA((15,))] * 2,
        compiler_params=pltpu.CompilerParams(vmem_limit_bytes=62 * 1024 * 1024),
    )(st, ig, first, second, new, norms)


def train(plan, latent, codes, targets, visits, imp, params, first, second):
    n, rows = plan.n, plan.slot
    depth, hrows = n // 4, rows // 2
    width = codes.shape[1] // 2
    height = -(-params.shape[1] // 1024) * 8
    vm = pl.BlockSpec(memory_space=pltpu.VMEM)
    hbm = pl.BlockSpec(memory_space=pl.ANY)
    packed = sum(1 for h, v in zip(plan.h_rows, plan.v_rows) if h or v)
    return pl.pallas_call(
        functools.partial(train_kernel, plan),
        out_shape=(
            jax.ShapeDtypeStruct((2 * width, D), BF),
            jax.ShapeDtypeStruct((2 * width, D), F32),
            jax.ShapeDtypeStruct(params.shape, F32),
            jax.ShapeDtypeStruct(params.shape, F32),
            jax.ShapeDtypeStruct(params.shape, F32),
            jax.ShapeDtypeStruct((2, MATS), F32),
        ),
        in_specs=[hbm] + [vm] * 5 + [hbm] * 2,
        out_specs=(hbm, hbm, vm, vm, vm, vm),
        scratch_shapes=[
            pltpu.VMEM((2, A_ROWS, D), BF),
            pltpu.VMEM((2, D, HPAD), BF),
            pltpu.VMEM((2, 128, D), BF),
            pltpu.VMEM((2, 8, width), jnp.int32),
            pltpu.VMEM((8, width), jnp.int32),
            pltpu.VMEM((8, width), F32),
            *work_scratch(width),
            pltpu.VMEM((2, A_ROWS, D), BF),
            pltpu.VMEM((2, D, HPAD), BF),
            pltpu.VMEM((2, 3, 16, D), F32),
            pltpu.VMEM((packed, rows, D), BF),
            pltpu.VMEM((2, width, D), BF),
            pltpu.VMEM((max(2 * rows, height + 48) + 80, 128), F32),
            pltpu.VMEM((height + 128, 128), F32),
            pltpu.VMEM((height + 40, 128), F32),
            pltpu.VMEM((128, D), F32),
            pltpu.VMEM((3, 3, 16, D), F32),
            pltpu.VMEM((3 + depth, 3, 16, D), F32),
            pltpu.VMEM((3, hrows, D), F32),
            pltpu.VMEM((4, 32, 128), F32),
            pltpu.VMEM((2 + depth, 32, 128), F32),
            pltpu.VMEM((8, 128), F32),
            pltpu.SemaphoreType.DMA((11 * n,)),
            pltpu.SemaphoreType.DMA((11 * n,)),
            pltpu.SemaphoreType.DMA((2 * depth,)),
            pltpu.SemaphoreType.DMA((2 * (depth + 2),)),
            pltpu.SemaphoreType.DMA((5,)),
            pltpu.SemaphoreType.REGULAR((2,)),
        ],
        compiler_params=pltpu.CompilerParams(
            collective_id=2, has_side_effects=True, vmem_limit_bytes=63 * 1024 * 1024
        ),
    )(latent, codes, targets, visits, imp, params, first, second)


def on_device(latent, codes, targets, visits, importance, params, first_moment, second_moment):
    me = lax.axis_index("tower")
    row_count = latent.shape[0]
    half = row_count // 2
    shard_len = params.shape[1]
    plan = Plan(lax.axis_size("dp"), shard_len)
    if fused_fits(plan):
        states_out, inputs_out, first, second, new, norms = train(
            plan, latent, codes, targets.transpose(1, 0, 2), visits[0].T, importance[None], params, first_moment, second_moment
        )
        states_out, inputs_out, first, second, new, low, norms = finish(states_out, inputs_out, first, second, new, norms)
    else:
        height = -(-plan.rows128 // 8) * 8
        p128, m128, v128 = (
            jnp.pad(v, ((0, 0), (0, 128 * height - shard_len))).reshape(height, 128)
            for v in (params, first_moment, second_moment)
        )
        ints = jnp.concatenate([codes, targets[0, :1], visits[0].T, targets[0, 1:]], 0)
        x = lax.dynamic_slice_in_dim(latent, me * half, half, 0)
        w, wh, vec, both, rw = gather(plan, p128, ints, importance[None])
        st, ig, gw, gh, gv = compute(x, both, rw, w, wh, vec)
        states_out, inputs_out, *flat, norms = reduce_and_update(plan, gw, gh, gv, st, ig, p128, m128, v128)
        first, second, new = (v.reshape(1, -1)[:, :shard_len] for v in flat)
        low = new.astype(BF)
    return (states_out[None], inputs_out[None], first, second, new, low, norms[None])


def solution(mesh):
    in_specs = (
        P("dp", None),
        P("tower", "dp"),
        P("tower", None, "dp"),
        P("tower", "dp", None),
        P("dp"),
        P("tower", "dp"),
        P("tower", "dp"),
        P("tower", "dp"),
    )
    out_specs = (
        P("tower", "dp", None),
        P("tower", "dp", None),
        P("tower", "dp"),
        P("tower", "dp"),
        P("tower", "dp"),
        P("tower", "dp"),
        P("tower", None, None),
    )
    return jax.shard_map(
        on_device, mesh=mesh, in_specs=in_specs, out_specs=out_specs, check_vma=False
    )
```

```python
import functools

import jax
import jax.numpy as jnp
from jax import lax
from jax.experimental import pallas as pl
from jax.experimental.pallas import tpu as pltpu
from jax.sharding import PartitionSpec as P

D = 256
CODES = 32
BINS = 601
BLOCKS = 10
STEP = 5
HEADS = 1238
MATS = 12
P_SIZE = 1054464
HPAD = 1280
CAT = D + CODES
A_ROWS = CAT + BLOCKS * D
BF = jnp.bfloat16
F32 = jnp.float32
GELU_C = 0.7978845608028654
GELU_K = 0.044715


def nn(a, b):
    return jnp.dot(a, b, preferred_element_type=F32)


def nt(a, b):
    return lax.dot_general(a, b, (((1,), (1,)), ((), ())), preferred_element_type=F32)


def identity(n):
    return (lax.broadcasted_iota(jnp.int32, (n, n), 0) == lax.broadcasted_iota(jnp.int32, (n, n), 1)).astype(BF)


ZETA = (GELU_C * GELU_K) ** (1.0 / 3.0)
B0 = GELU_C / ZETA
E0 = 0.5 / ZETA


def wide(v, cs):
    return jnp.concatenate([v] * ((cs.stop - cs.start) // v.shape[1]), 1)


def norm_act(src, cs, gs, unit, gp, rstd, out):
    for r in range(0, D, 32):
        rs = slice(r, r + 32)
        xh = src[rs, cs] * rstd
        z = xh * wide(gs[rs, 0:128], cs) + wide(gs[rs, 128:256], cs)
        z2 = z * z
        t = jnp.tanh(z * (z2 + B0))
        q = t * E0 + E0
        a = z * q
        out(rs, a)
        unit[rs, cs] = xh.astype(BF)
        gp[rs, cs] = (q + (a * (1.0 - t)) * (z2 * 3.0 + B0)).astype(BF)


def broadcast_vectors(vt, rows):
    k = lax.broadcasted_iota(jnp.int32, (128, 128), 0)
    picks = jnp.concatenate([(k == row).astype(BF) for row in rows], 1)
    return nn(vt, picks)


def head_stage(cs, lg, dl, ints, rw):
    width = rw.shape[1]
    it8 = lax.broadcasted_iota(jnp.int32, (8, width), 0)
    low = -jnp.inf
    b75, b150, b154 = lg[600:608], lg[1200:1208], lg[1232:1240]

    def top(block):
        return jnp.max(block, axis=0, keepdims=True)

    def steps(lo, hi, step):
        return [(r, min(r + step, hi)) for r in range(lo, hi, step)]

    def folded(value):
        return value.reshape(-1, 8, width)

    def top_range(lo, hi):
        best = None
        for r, end in steps(lo, hi, 40):
            part = jnp.max(folded(lg[r:end]), axis=0)
            best = part if best is None else jnp.maximum(best, part)
        return best

    max_v = top(jnp.maximum(top_range(0, 600), jnp.where(it8 < 1, b75, low)))
    max_r = top(
        jnp.maximum(
            jnp.maximum(top_range(608, 1200), jnp.where(it8 >= 1, b75, low)),
            jnp.where(it8 < 2, b150, low),
        )
    )
    max_c = top(
        jnp.maximum(
            jnp.maximum(top_range(1208, 1232), jnp.where(it8 >= 2, b150, low)),
            jnp.where(it8 < 2, b154, low),
        )
    )
    in_policy = (it8 >= 2) & (it8 < 6)
    max_p = top(jnp.where(in_policy, b154, low))

    def exp_range(lo, hi, best):
        acc = jnp.zeros((8, width), F32)
        for r, end in steps(lo, hi, 40):
            e = jnp.exp(lg[r:end] - best)
            lg[r:end] = e
            acc = acc + jnp.sum(folded(e), axis=0)
        return acc

    e75 = jnp.exp(b75 - jnp.where(it8 < 1, max_v, max_r))
    e150 = jnp.exp(b150 - jnp.where(it8 < 2, max_r, max_c))
    e154 = jnp.exp(b154 - jnp.where(it8 < 2, max_c, max_p))

    def total(acc):
        return rw / jnp.sum(acc, axis=0, keepdims=True)

    inv_v = total(exp_range(0, 600, max_v) + jnp.where(it8 < 1, e75, 0.0))
    inv_r = total(exp_range(608, 1200, max_r) + jnp.where(it8 >= 1, e75, 0.0) + jnp.where(it8 < 2, e150, 0.0))
    inv_c = total(exp_range(1208, 1232, max_c) + jnp.where(it8 >= 2, e150, 0.0) + jnp.where(it8 < 2, e154, 0.0))
    inv_p = total(jnp.where(in_policy, e154, 0.0))
    hit_v = ints[1:2]
    hit_r = ints[6:7] + BINS
    hit_c = ints[7:8] + 2 * BINS
    counts = jnp.where(in_policy, ints.astype(F32), 0.0)
    share = counts * (rw / jnp.sum(counts, axis=0, keepdims=True))

    def minus(value, lo, *hits):
        at = lax.broadcasted_iota(jnp.int32, value.shape, 0)
        for hit in hits:
            value = value - jnp.where(at == hit - lo, rw, 0.0)
        return value

    d75 = minus(e75 * jnp.where(it8 < 1, inv_v, inv_r), 600, hit_v, hit_r)
    d150 = minus(e150 * jnp.where(it8 < 2, inv_r, inv_c), 1200, hit_r, hit_c)
    d154 = minus(e154 * jnp.where(it8 < 2, inv_c, inv_p), 1232, hit_c) - share
    d154 = jnp.where(it8 < 6, d154, 0.0)

    def emit(lo, hi, inv, hit):
        for r, end in steps(lo, hi, 80):
            dl[r:end, cs] = minus(lg[r:end] * inv, r, hit).astype(BF)

    def pair(first, second):
        return jnp.concatenate([first, second], 0).astype(BF)

    emit(0, 592, inv_v, hit_v)
    dl[592:608, cs] = pair(minus(lg[592:600] * inv_v, 592, hit_v), d75)
    emit(608, 1200, inv_r, hit_r)
    dl[1200:1216, cs] = pair(d150, minus(lg[1208:1216] * inv_c, 1208, hit_c))
    emit(1216, 1232, inv_c, hit_c)
    dl[1232:1248, cs] = pair(d154, jnp.zeros_like(d154))
    dl[1248:HPAD, cs] = jnp.zeros((HPAD - 1248, width), BF)


CB = 256
GROUP = 2


def saved_views(t, mix, xh):
    def mixed(k):
        return mix.at[pl.ds(pl.multiple_of((t * BLOCKS + k - 1) * (D + 16), 16), D + 16)]

    def unit(k):
        return xh.at[pl.ds(pl.multiple_of((t * (BLOCKS + 1) + k) * D, D), D)]

    return mixed, unit


def column_groups(width):
    blocks = [slice(c, c + CB) for c in range(0, width, CB)]
    per = min(GROUP, len(blocks))
    return blocks, per, [slice(c, c + per * CB) for c in range(0, width, per * CB)]


def forward_tower(t, refs, during=None, before_last=None):
    (eye, w, wh, vec, wt, vt, gsb, xt, mix, xh, gp, rstd, stream, mean, ints, width) = refs
    blocks, per, groups = column_groups(width)
    mixed, unit = saved_views(t, mix, xh)
    first_bias = 2 * (BLOCKS + 1)
    ones = jnp.ones((16, D), BF)

    def mean_rows(slot):
        value = nn(ones, wt[slot, 0:D])[0:8] * (1.0 / D)
        high = value.astype(BF).astype(F32)
        wt[slot, D : D + 16] = jnp.concatenate([high, value - high], 0).astype(BF)

    def vectors(k):
        gsb[k % 2] = broadcast_vectors(vt[...], (k, k + BLOCKS + 1)) * ZETA

    def prefetch(k):
        vectors(k)
        row = pl.multiple_of(CAT + jnp.minimum(k - 1, BLOCKS - 1) * D, 32)
        wt[k % 2, 0:D, 0:D] = nt(eye[...], w[t, pl.ds(row, D)]).astype(BF)
        at_row = lax.broadcasted_iota(jnp.int32, (128, 128), 0) == k + first_bias
        at_lane = lax.broadcasted_iota(jnp.int32, (128, 128), 1) == 0
        wt[k % 2, 0:D, D:384] = nn(vt[...], (at_row & at_lane).astype(BF)).astype(BF)
        mean_rows(k % 2)

    def row_of(k):
        return pl.ds(t * (BLOCKS + 1) + k, 1)

    def stage(k, c):
        def keep(rs, a):
            mixed(k)[rs, blocks[c]] = a.astype(BF)

        norm_act(stream, blocks[c], gsb.at[k % 2], unit(k), gp.at[t, k], rstd[row_of(k), blocks[c]], keep)

    def spread(square, k, cs):
        var = jnp.sum(square, axis=0, keepdims=True) * (1.0 / D)
        rstd[row_of(k), cs] = lax.rsqrt(var + 1e-05)

    def add(k, cs, out, fresh):
        shift = out[D : D + 1] + out[D + 8 : D + 9]
        square = jnp.zeros((8, out.shape[1]), F32)
        for r in range(0, D, 32):
            value = out[r : r + 32] - shift
            if not fresh:
                value = stream[r : r + 32, cs] + value
            stream[r : r + 32, cs] = value
            square = square + jnp.sum((value * value).reshape(4, 8, -1), axis=0)
        if not fresh:
            mean[0:1, cs] = mean[0:1, cs] + shift
        spread(square, k + 1, cs)

    def centre(cs):
        total = jnp.zeros((8, CB), F32)
        for r in range(0, D, 32):
            total = total + jnp.sum(stream[r : r + 32, cs].reshape(4, 8, -1), axis=0)
        middle = jnp.sum(total, axis=0, keepdims=True) * (1.0 / D)
        mean[0:1, cs] = middle
        square = jnp.zeros((8, CB), F32)
        for r in range(0, D, 32):
            value = stream[r : r + 32, cs] - middle
            stream[r : r + 32, cs] = value
            square = square + jnp.sum((value * value).reshape(4, 8, -1), axis=0)
        spread(square, 1, cs)

    vt[...] = nt(eye[...], vec[t]).astype(BF)
    vectors(0)
    wt[0, 0:D, 0:D] = nt(eye[...], w[t, 0:D]).astype(BF)
    tile = first_bias // 16 * 16
    picked = lax.broadcasted_iota(jnp.int32, (16, D), 0) == first_bias - tile
    bias = jnp.where(picked, vec[t, tile : tile + 16].astype(F32), 0.0).astype(BF)
    rest = jnp.concatenate([w[t, D:CAT], bias, jnp.zeros((128 - CODES - 16, D), BF)], 0)
    wt[0, 0:D, D:384] = nt(eye[...], rest).astype(BF)
    mean_rows(0)
    for cs in blocks:
        it = lax.broadcasted_iota(jnp.int32, (CODES, CB), 0)
        xt[t, D:CAT, cs] = (it == ints[t, 0:1, cs]).astype(BF)
        xt[t, CAT : CAT + 16, cs] = jnp.ones((16, CB), BF)
    first = [nn(wt[0, :, 0 : CAT + 16], xt[t, :, cs]) for cs in groups]
    prefetch(1)
    for group, cs in enumerate(groups):
        add(-1, cs, first[group], True)
    for cs in blocks:

        def keep(rs, a):
            stream[rs, cs] = a

        norm_act(stream, cs, gsb.at[0], unit(0), gp.at[t, 0], rstd[row_of(0), cs], keep)
        centre(cs)

    def layer(k, more):
        mixed(k)[D : D + 16, :] = jnp.ones((16, width), BF)
        for group, cs in enumerate(groups):
            out = nn(wt[k % 2, :, 0 : D + 16], mixed(k)[:, cs])
            ahead = group + 1 < len(groups)
            if ahead or more:
                for c in range(per):
                    stage(k if ahead else k + 1, (group + 1) % len(groups) * per + c)
            add(k, cs, out, False)
        if more:
            prefetch(k + 2)

    prefetch(2)
    for c in range(per):
        stage(1, c)

    @pl.loop(1, BLOCKS)
    def _(k):
        if during is not None:
            during(k)
        layer(k, True)

    if before_last is not None:
        before_last()
    layer(BLOCKS, False)
    for cs in blocks:
        xt[t + 1, 0:D, cs] = (stream[:, cs] + mean[0:1, cs]).astype(BF)


def backward_tower(t, refs, after_head=None, during=None, before_product=None, after_weights=None):
    (eye, w, wh, vec, wht, vt, gsb, xt, mix, xh, gp, rstd, ds, ex, br, dm, acc, lg, dl, ints, rw, gw, gh, gv, ig, width) = refs
    blocks = [slice(c, c + CB) for c in range(0, width, CB)]
    last = len(blocks) - 1
    mixed, unit = saved_views(t, mix, xh)
    vt[...] = nt(eye[...], vec[t]).astype(BF)
    for h in range(0, HPAD, D):
        wht[h : h + D, :] = nt(eye[...], wh[t, :, h : h + D]).astype(BF)

    def softmax_block(c):
        cs = pl.ds(pl.multiple_of(c * CB, CB), CB)
        lg[...] = nn(wht[...], xt[t + 1, 0:D, cs])
        return cs

    def states_block(c):
        cs = pl.ds(pl.multiple_of(c * CB, CB), CB)
        return cs, nn(wh[t], dl[:, cs])

    def keep_states(cs, product):
        value = product + ex[:, cs]
        ds[:, cs] = value
        br[BLOCKS % 2, :, cs] = value.astype(BF)

    cs = softmax_block(0)
    head_stage(cs, lg, dl, ints[t, :, cs], rw[0:1, cs])

    @pl.loop(1, width // CB)
    def _(c):
        cs = softmax_block(c)
        before, product = states_block(c - 1)
        head_stage(cs, lg, dl, ints[t, :, cs], rw[0:1, cs])
        keep_states(before, product)

    keep_states(*states_block(width // CB - 1))
    for h in range(0, HPAD, D):
        gh[t, :, h : h + D] = nt(xt[t + 1, 0:D, :], dl[h : h + D]).astype(BF)
    if after_head is not None:
        after_head()
    acc[...] = jnp.zeros(acc.shape, F32)
    ones = jnp.ones((16, 128), BF)

    def part(c):
        return dm.at[c * D : c * D + D]

    def gains(k):
        gsb[k % 2, :, 0:128] = broadcast_vectors(vt[...], (k,)) * ZETA

    def row_sums(k):
        for kind in range(2):
            gv[t, kind, pl.ds(k, 1), :] = nt(ones, acc[k % 2, kind].astype(BF))[0:1] * ZETA
        acc[k % 2] = jnp.zeros(acc.shape[1:], F32)

    def product(k, c):
        row = pl.multiple_of(CAT + (k - 1) * D, 32)
        part(c)[...] = nn(w[t, pl.ds(row, D)], br[k % 2, :, blocks[c]])

    def slopes(k, c):
        cs, grad, sums = blocks[c], part(c), acc.at[k % 2]
        s1 = jnp.zeros((8, CB), F32)
        s2 = jnp.zeros((8, CB), F32)
        for r in range(0, D, 32):
            rs = slice(r, r + 32)
            g = wide(gsb[k % 2, rs, 0:128], cs)
            dy = grad[rs, :] * gp[t, k, rs, cs].astype(F32)
            prod = dy * unit(k)[rs, cs].astype(F32)
            back = dy * g
            grad[rs, :] = back
            s1 = s1 + jnp.sum(back.reshape(4, 8, CB), axis=0)
            s2 = s2 + jnp.sum((prod * g).reshape(4, 8, CB), axis=0)
            sums[0, rs] = sums[0, rs] + (prod[:, 0:128] + prod[:, 128:CB])
            sums[1, rs] = sums[1, rs] + (dy[:, 0:128] + dy[:, 128:CB])
        return [jnp.sum(s, axis=0, keepdims=True) * (1.0 / D) for s in (s1, s2)]

    def stage(k, c, first):
        cs = blocks[c]
        means = slopes(k, c)
        scale = rstd[pl.ds(t * (BLOCKS + 1) + k, 1), cs]
        m1, m2 = (jnp.broadcast_to(m * scale, (32, CB)).astype(BF) for m in means)
        for r in range(0, D, 32):
            rs = slice(r, r + 32)
            back = part(c)[rs, :] * scale - (m1 + unit(k)[rs, cs] * m2).astype(F32)
            if first:
                br[0, rs, cs] = back.astype(BF)
            else:
                value = ds[rs, cs] + back
                ds[rs, cs] = value
                br[(k + 1) % 2, rs, cs] = value.astype(BF)

    if before_product is not None:
        before_product()
    gains(BLOCKS)
    gains(BLOCKS - 1)
    product(BLOCKS, 0)

    @pl.loop(0, BLOCKS)
    def _(i):
        k = BLOCKS - i
        if during is not None:
            during(i)
        for c in range(last + 1):
            if c < last:
                product(k, c + 1)
            stage(k, c, False)
            if c == 0:
                full = nt(mixed(k)[...], br[k % 2])
                row = pl.multiple_of(CAT + (k - 1) * D, 32)
                gw[t, pl.ds(row, D), :] = full[0:D].astype(BF)
                gv[t, 2, pl.ds(k, 1), :] = full[D : D + 1]
                product(k - 1, 0)
        gains(k - 2)
        row_sums(k)

    for c, cs in enumerate(blocks):
        part(c)[...] = ds[:, cs]
        stage(0, c, True)
    full = nt(xt[t], br[0])
    gw[t, 0:CAT, :] = full[0:CAT].astype(BF)
    gv[t, 2, 0:1, :] = full[CAT : CAT + 1]
    row_sums(0)
    if after_weights is not None:
        after_weights()
    for cs in blocks:
        back = nn(w[t, 0:D], br[0, :, cs])
        ex[:, cs] = back
        ig[cs, :] = back.T


def compute_kernel(x_ref, ints, rw, w, wh, vec, st, ig, gw, gh, gv, eye, wt, wht, vt, gsb, xt, mix, xh, gp, rstd, mean, stream, ex, br, dm, acc, lg, dl):
    width = x_ref.shape[0]
    eye[...] = identity(D)
    for c in range(0, width, CB):
        cs = slice(c, c + CB)
        xt[0, 0:D, cs] = nt(eye[...], x_ref[cs, :]).astype(BF)
    fwd = (eye, w, wh, vec, wt, vt, gsb, xt, mix, xh, gp, rstd, stream, mean, ints, width)
    @pl.loop(0, 2)
    def _(t):
        forward_tower(t, fwd)

        @pl.loop(0, width // CB)
        def _(c):
            cs = pl.ds(pl.multiple_of(c * CB, CB), CB)
            st[t, cs, :] = nt(eye[...], xt[t + 1, 0:D, cs]).astype(BF)

    ex[...] = jnp.zeros_like(ex)

    @pl.loop(0, 2)
    def _(i):
        t = 1 - i
        backward_tower(
            t,
            (eye, w, wh, vec, wht, vt, gsb, xt, mix, xh, gp, rstd, stream, ex, br, dm, acc, lg, dl, ints, rw, gw, gh, gv, ig.at[t], width),
        )


def work_scratch(width):
    return [
        pltpu.VMEM((D, D), BF),
        pltpu.VMEM((2, D + 16, 384), BF),
        pltpu.VMEM((HPAD, D), BF),
        pltpu.VMEM((D, 128), BF),
        pltpu.VMEM((2, D, 256), F32),
        pltpu.VMEM((3, CAT + 16, width), BF),
        pltpu.VMEM((2 * BLOCKS * (D + 16), width), BF),
        pltpu.VMEM((2 * (BLOCKS + 1) * D, width), BF),
        pltpu.VMEM((2, BLOCKS + 1, D, width), BF),
        pltpu.VMEM((24, width), F32),
        pltpu.VMEM((8, width), F32),
        pltpu.VMEM((D, width), F32),
        pltpu.VMEM((D, width), F32),
        pltpu.VMEM((2, D, width), BF),
        pltpu.VMEM((width // CB * D, CB), F32),
        pltpu.VMEM((2, 2, D, 128), F32),
        pltpu.VMEM((HPAD, CB), F32),
        pltpu.VMEM((HPAD, width), BF),
    ]


def compute(x, ints, rw, w, wh, vec):
    width = x.shape[0]
    vm = pl.BlockSpec(memory_space=pltpu.VMEM)
    return pl.pallas_call(
        compute_kernel,
        out_shape=(
            jax.ShapeDtypeStruct((2, width, D), BF),
            jax.ShapeDtypeStruct((2, width, D), F32),
            jax.ShapeDtypeStruct((2, A_ROWS, D), BF),
            jax.ShapeDtypeStruct((2, D, HPAD), BF),
            jax.ShapeDtypeStruct((2, 3, 16, D), F32),
        ),
        in_specs=[vm] * 6,
        out_specs=(vm,) * 5,
        scratch_shapes=work_scratch(width),
        compiler_params=pltpu.CompilerParams(vmem_limit_bytes=62 * 1024 * 1024),
    )(x, ints, rw, w, wh, vec)


class Plan:
    def __init__(self, n, length):
        self.n, self.length = n, length
        self.rows128 = -(-length // 128)
        block_end, head_end = A_ROWS * D, A_ROWS * D + D * HEADS
        self.a_base, self.a_rows, self.h_first, self.h_rows, self.h_off, self.v_first, self.v_rows, self.v_off = ([] for _ in range(8))
        used = 0
        for i in range(n):
            lo, hi = i * length, (i + 1) * length
            base = min(lo, block_end) // D // 16 * 16
            top = -(-min(hi, block_end) // D)
            a_rows = -(-(top - base) // 16) * 16 if lo < block_end else 0
            first = min(max(lo - block_end, 0), D * HEADS) // HEADS
            last = -(-min(max(hi - block_end, 0), D * HEADS) // HEADS)
            h_rows = last - first if hi > block_end and lo < head_end else 0
            v_first = max(lo - head_end, 0) // D
            v_rows = -(-(hi - head_end) // D) - v_first if hi > head_end else 0
            self.a_base.append(base)
            self.a_rows.append(a_rows)
            self.h_first.append(first)
            self.h_rows.append(h_rows)
            self.h_off.append(a_rows)
            self.v_first.append(v_first)
            self.v_rows.append(v_rows)
            self.v_off.append(a_rows + 5 * h_rows)
            used = max(used, a_rows + 5 * h_rows + v_rows)
        self.heads = max(self.h_rows)
        self.image = (HEADS * self.heads // 128 + 24) // 8 * 8
        self.slot = -(-(used + 1) // 32) * 32

    def at(self, table, me):
        value = jnp.int32(table[0])
        for i in range(1, self.n):
            if table[i] != table[i - 1]:
                value = value + (me >= i).astype(jnp.int32) * (table[i] - table[i - 1])
        return value


MESH = pl.DeviceIdType.MESH


def neighbours(n):
    core = lax.axis_index("tower")
    me = lax.axis_index("dp")
    near_x = me + 1 - 2 * (me % 2)
    near_y = me + 2 - 4 * ((me // 2) % 2)
    return core, me, near_x, near_y


def at(core, index):
    return {"tower": core, "dp": index}


def greet(core, me, near_x, near_y, n, crossed=False):
    barrier = pltpu.get_barrier_semaphore()
    pl.semaphore_signal(barrier, inc=1, device_id=at(1 - core, me), device_id_type=MESH)
    for near in (near_x, near_y, near_x + near_y - me):
        pl.semaphore_signal(barrier, inc=1, device_id=at(core, near), device_id_type=MESH)
    for k in range(1, n // 4):
        pl.semaphore_signal(barrier, inc=1, device_id=at(core, (me + 4 * k) % n), device_id_type=MESH)
    for near in [near_x, near_y] + [(me + 4 * k) % n for k in range(1, n // 4)] if crossed else []:
        pl.semaphore_signal(barrier, inc=1, device_id=at(1 - core, near), device_id_type=MESH)
    return barrier


def place_shard(plan, me, p_ref, slot128, shifted, rolled):
    rows = plan.rows128
    start = me * plan.length
    shift = start % 128
    first = start // 128
    tall = shifted.shape[0]
    height = p_ref.shape[0]
    lane = lax.broadcasted_iota(jnp.int32, (height, 128), 1)
    rolled[0:8] = jnp.zeros((8, 128), F32)
    rolled[8 : 8 + height] = pltpu.roll(p_ref[...], shift, 1)
    shifted[...] = jnp.zeros((tall, 128), F32)
    moved = jnp.where(lane >= shift, rolled[8 : 8 + height], rolled[7 : 7 + height])
    shifted[16 : 16 + height] = moved
    slot128[...] = jnp.zeros(slot128.shape, F32)
    row = lax.broadcasted_iota(jnp.int32, (height, 128), 0)
    base = plan.at(plan.a_base, me)

    @pl.when(plan.at(plan.a_rows, me) > 0)
    def _():
        slot128[pl.ds(first - 2 * base, height)] = jnp.where(row + first < 2 * A_ROWS, moved, 0.0)

    v_start = (A_ROWS * D + D * HEADS) // 128
    v_rows, v_off, v_first = (plan.at(t, me) for t in (plan.v_rows, plan.v_off, plan.v_first))
    tall_v = min(height, -(-2 * max(plan.v_rows) // 8) * 8)

    @pl.when(v_rows > 0)
    def _():
        inside = plan.at([max(0, v_start - i * plan.length // 128) for i in range(plan.n)], me)
        to = 2 * v_off + first + inside - v_start - 2 * v_first
        slot128[pl.ds(to, tall_v)] = shifted[pl.ds(16 + inside, tall_v)]

    h_first, h_rows, h_off = (plan.at(t, me) for t in (plan.h_first, plan.h_rows, plan.h_off))

    @pl.when(h_rows > 0)
    def _():
        tall_h = plan.image
        begin = A_ROWS * D + HEADS * h_first - 128 * first + 128 * 16
        turn = begin % 128
        rolled[0:tall_h] = pltpu.roll(shifted[pl.ds(begin // 128, tall_h)], (128 - turn) % 128, 1)
        rolled[tall_h : tall_h + 8] = jnp.zeros((8, 128), F32)
        lane = lax.broadcasted_iota(jnp.int32, (tall_h, 128), 1)
        shifted[0:tall_h] = jnp.where(lane < 128 - turn, rolled[0:tall_h], rolled[1 : tall_h + 1])
        to = slot128.at[pl.ds(pl.multiple_of(2 * h_off, 8), 10 * plan.heads)]
        it = lax.broadcasted_iota(jnp.int32, (10, 128), 0)
        lane = lax.broadcasted_iota(jnp.int32, (10, 128), 1)
        for k in range(plan.heads):
            row, turn = HEADS * k // 128, HEADS * k % 128
            window = pltpu.roll(shifted[row : row + 16], (128 - turn) % 128, 1)
            value = jnp.where(lane < 128 - turn, window[0:10], window[1:11])
            kept = (it * 128 + lane < HEADS) & (k < h_rows)
            to[10 * k : 10 * k + 10] = to[10 * k : 10 * k + 10] + jnp.where(kept, value, 0.0)


def unpack_rows(plan, i, slot, w, heads, vectors, scratch):
    base, rows = plan.a_base[i], plan.a_rows[i]
    if rows:
        shared = i > 0 and base < plan.a_base[i - 1] + plan.a_rows[i - 1]
        lo = 0
        if shared:
            w[base : base + 16] = w[base : base + 16] + slot[0:16]
            lo = 16
        if rows > lo:
            w[base + lo : base + rows] = slot[lo:rows]
    h_rows, h_off, h_first = plan.h_rows[i], plan.h_off[i], plan.h_first[i]
    v_rows, v_off, v_first = plan.v_rows[i], plan.v_off[i], plan.v_first[i]
    if h_rows or v_rows:
        value = slot.astype(F32)
        scratch[0][...] = value[:, 0:128]
        scratch[1][...] = value[:, 128:D]
    if h_rows:
        shared = i > 0 and plan.h_rows[i - 1] and plan.h_first[i - 1] + plan.h_rows[i - 1] > h_first
        for j in range(5):
            for half in range(2):
                cols = slice(128 * half, 128 * half + 128)
                first = D * j + h_first
                value = scratch[half][pl.ds(h_off + j, h_rows, stride=5)]
                if shared:
                    heads[first : first + 1, cols] = heads[first : first + 1, cols] + value[0:1]
                    if h_rows > 1:
                        heads[first + 1 : first + h_rows, cols] = value[1:h_rows]
                else:
                    heads[first : first + h_rows, cols] = value
    if v_rows:
        shared = v_first and plan.v_first[i - 1] + plan.v_rows[i - 1] > v_first
        shared = shared or (i > 0 and plan.v_rows[i - 1] > 0 and v_first == 0)
        for half in range(2):
            cols = slice(128 * half, 128 * half + 128)
            value = scratch[half][v_off : v_off + v_rows]
            if shared:
                vectors[v_first : v_first + 1, cols] = vectors[v_first : v_first + 1, cols] + value[0:1]
                if v_rows > 1:
                    vectors[v_first + 1 : v_first + v_rows, cols] = value[1:v_rows]
            else:
                vectors[v_first : v_first + v_rows, cols] = value


def split3(value):
    hi = value.astype(BF).astype(F32)
    mid = (value - hi).astype(BF).astype(F32)
    return hi, mid, value - hi - mid


def gather_kernel(plan, p_ref, ints_ref, imp_ref, w, wh, vec, both, rw, slots, slot128, shifted, rolled, scratch, whf, vecf, send, recv):
    n = plan.n
    depth = n // 4
    core, me, near_x, near_y = neighbours(n)
    barrier = greet(core, me, near_x, near_y, n)
    place_shard(plan, me, p_ref, slot128, shifted, rolled)
    pl.semaphore_wait(barrier, depth + 3)
    half = rw.shape[1]
    started = []

    def copy(src, dst, slot, to):
        c = pltpu.make_async_remote_copy(
            src_ref=src, dst_ref=dst, send_sem=send.at[slot], recv_sem=recv.at[slot], device_id=to, device_id_type=MESH
        )
        c.start()
        started.append(c)
        return c

    mine = pl.multiple_of(core * half, half)
    theirs = pl.multiple_of((1 - core) * half, half)
    number = iter(range(1 << 20))
    ints_copy = copy(ints_ref.at[:, pl.ds(theirs, half)], both.at[core], next(number), at(1 - core, me))
    rows = plan.slot
    total = jnp.sum(imp_ref[...].astype(F32), axis=1, keepdims=True)
    lane = lax.broadcasted_iota(jnp.int32, (1, D), 1)
    hi, mid, lo = split3(total)
    left = slot128[pl.ds(0, rows, stride=2)]
    right = slot128[pl.ds(1, rows, stride=2)]
    own = jnp.concatenate([left, right], 1)
    last = jnp.where(lane == 0, hi, jnp.where(lane == 1, mid, jnp.where(lane == 2, lo, 0.0)))
    last_row = lax.broadcasted_iota(jnp.int32, (rows, D), 0) == rows - 1
    slots[core, me] = jnp.where(last_row, last, own).astype(BF)

    def column(index, k):
        return (index + n - 4 * k) % n

    def send_slot(origin, to, lo=0, hi=rows):
        ref = slots.at[core, origin, pl.ds(lo, hi - lo)]
        return copy(ref, ref, next(number), to)

    near_xy = near_x + near_y - me
    cut = rows // 2
    z_in, x_in, y_in, d_in, s_in = {}, {}, {}, {}, []
    for k in sorted(range(1, depth), key=lambda k: (min(k, depth - k), k)):
        z_in[k] = send_slot(me, at(core, (me + 4 * k) % n))
    order = [0] + list(z_in)
    for k in order:
        if k:
            z_in[k].wait_recv()
        x_in[k] = send_slot(column(me, k), at(core, near_x))
        y_in[k] = send_slot(column(me, k), at(core, near_y))
        s_in.append(send_slot(column(me, k), at(1 - core, me)))
    for k in order:
        x_in[k].wait_recv()
        first = send_slot(column(near_x, k), at(core, near_y), 0, cut)
        s_in.append(send_slot(column(near_x, k), at(1 - core, me)))
        y_in[k].wait_recv()
        second = send_slot(column(near_y, k), at(core, near_x), cut, rows)
        s_in.append(send_slot(column(near_y, k), at(1 - core, me)))
        d_in[k] = (first, second)
    for k in order:
        for c in d_in[k]:
            c.wait_recv()
        s_in.append(send_slot(column(near_xy, k), at(1 - core, me)))
    ints_copy.wait_recv()
    both[core] = ints_ref[:, pl.ds(mine, half)]
    for c in s_in:
        c.wait_recv()
    for c in started:
        c.wait_send()
    for t in range(2):
        vecf[...] = jnp.zeros(vecf.shape, F32)
        for i in range(n):
            unpack_rows(plan, i, slots[t, i], w.at[t], whf, vecf, [scratch.at[0], scratch.at[1]])
        for j in range(5):
            wh[t, :, D * j : D * j + D] = whf[D * j : D * j + D].astype(BF)
        vec[t] = vecf[...].astype(BF)
    total = jnp.zeros((1, D), F32)
    for i in range(n):
        tail = slots[0, i, rows - 16 : rows].astype(F32)
        total = total + tail[15:16]
    weight_sum = jnp.sum(jnp.where(lane < 3, total, 0.0), axis=1, keepdims=True)
    rw[...] = jnp.broadcast_to(imp_ref[:, pl.ds(mine, half)].astype(F32) / weight_sum, (8, half))


def gather(plan, p128, ints, imp):
    n, rows = plan.n, plan.slot
    half = ints.shape[1] // 2
    vm = pl.BlockSpec(memory_space=pltpu.VMEM)
    height = p128.shape[0]
    tall = max(2 * rows, height + 40) + 80
    copies = 1 + (n // 4 - 1) + 2 * (n // 4) + 2 * (n // 4) + n
    return pl.pallas_call(
        functools.partial(gather_kernel, plan),
        out_shape=(
            jax.ShapeDtypeStruct((2, A_ROWS, D), BF),
            jax.ShapeDtypeStruct((2, D, HPAD), BF),
            jax.ShapeDtypeStruct((2, 128, D), BF),
            jax.ShapeDtypeStruct((2, 8, half), jnp.int32),
            jax.ShapeDtypeStruct((8, half), F32),
        ),
        in_specs=[vm] * 3,
        out_specs=(vm,) * 5,
        scratch_shapes=[
            pltpu.VMEM((2, n, rows, D), BF),
            pltpu.VMEM((tall, 128), F32),
            pltpu.VMEM((height + 128, 128), F32),
            pltpu.VMEM((height + 40, 128), F32),
            pltpu.VMEM((2, rows, 128), F32),
            pltpu.VMEM((HPAD, D), F32),
            pltpu.VMEM((128, D), F32),
            pltpu.SemaphoreType.DMA((copies,)),
            pltpu.SemaphoreType.DMA((copies,)),
        ],
        compiler_params=pltpu.CompilerParams(
            collective_id=0, has_side_effects=True, vmem_limit_bytes=48 * 1024 * 1024
        ),
    )(p128, ints, imp)


def chunks(height):
    step = max(c for c in range(8, 113, 8) if height % c == 0)
    return [(lo, lo + step) for lo in range(0, height, step)]


def lay_flat(plan, me, slot128, flat, rolled):
    height = rolled.shape[0] - 40
    start = me * plan.length
    shift = start % 128
    first = start // 128
    base = plan.at(plan.a_base, me)
    row = lax.broadcasted_iota(jnp.int32, (height + 8, 128), 0)
    flat[...] = jnp.zeros(flat.shape, F32)

    @pl.when(plan.at(plan.a_rows, me) > 0)
    def _():
        rows = slot128[pl.ds(first - 2 * base, height + 8)]
        flat[16 : 24 + height] = jnp.where(row + first < 2 * A_ROWS, rows, 0.0)

    v_start = (A_ROWS * D + D * HEADS) // 128
    v_rows, v_off, v_first = (plan.at(t, me) for t in (plan.v_rows, plan.v_off, plan.v_first))
    tall_v = min(height, -(-2 * max(plan.v_rows) // 8) * 8)

    @pl.when(v_rows > 0)
    def _():
        inside = plan.at([max(0, v_start - i * plan.length // 128) for i in range(plan.n)], me)
        source = 2 * v_off + first + inside - v_start - 2 * v_first
        to = pl.ds(16 + inside, tall_v)
        flat[to] = flat[to] + slot128[pl.ds(source, tall_v)]

    h_first, h_rows, h_off = (plan.at(t, me) for t in (plan.h_first, plan.h_rows, plan.h_off))

    @pl.when(h_rows > 0)
    def _():
        tall_h = plan.image
        source = slot128.at[pl.ds(pl.multiple_of(2 * h_off, 8), 10 * plan.heads + 6)]
        it = lax.broadcasted_iota(jnp.int32, (16, 128), 0)
        lane = lax.broadcasted_iota(jnp.int32, (16, 128), 1)
        rolled[0 : tall_h + 8] = jnp.zeros((tall_h + 8, 128), F32)
        for k in range(plan.heads):
            row, turn = HEADS * k // 128, HEADS * k % 128
            kept = (it * 128 + lane < HEADS) & (k < h_rows)
            value = pltpu.roll(jnp.where(kept, source[10 * k : 10 * k + 16], 0.0), turn, 1)
            above = jnp.concatenate([jnp.zeros((8, 128), F32), value], 0)[7:23]
            rolled[row : row + 16] = rolled[row : row + 16] + jnp.where(lane >= turn, value, above)
        begin = A_ROWS * D + HEADS * h_first - 128 * first + 128 * 16
        turn = begin % 128
        slot128[0:8] = jnp.zeros((8, 128), F32)
        slot128[8 : 8 + tall_h] = pltpu.roll(rolled[0:tall_h], turn, 1)
        lane = lax.broadcasted_iota(jnp.int32, (tall_h, 128), 1)
        moved = jnp.where(lane >= turn, slot128[8 : 8 + tall_h], slot128[7 : 7 + tall_h])
        to = pl.ds(begin // 128, tall_h)
        flat[to] = flat[to] + moved

    rolled[0 : height + 8] = pltpu.roll(flat[16 : 24 + height], (128 - shift) % 128, 1)
    for lo, hi in chunks(height):
        lane = lax.broadcasted_iota(jnp.int32, (hi - lo, 128), 1)
        flat[lo:hi] = jnp.where(lane < 128 - shift, rolled[lo:hi], rolled[lo + 1 : hi + 1])


def pack_slots(plan, core, gw, gh, gv, rgw, rgh, rgv, slots, sums, vsum, scratch):
    total = gv[core].astype(F32) + rgv[...]
    for kind in range(3):
        vsum[kind * (BLOCKS + 1) : (kind + 1) * (BLOCKS + 1)] = total[kind, 0 : BLOCKS + 1]
    sums[...] = gh[core].astype(F32) + rgh[...].astype(F32)
    for i in range(plan.n):
        base, rows = plan.a_base[i], plan.a_rows[i]
        h_rows, h_off, h_first = plan.h_rows[i], plan.h_off[i], plan.h_first[i]
        v_rows, v_off, v_first = plan.v_rows[i], plan.v_off[i], plan.v_first[i]
        slots[i, rows : plan.slot] = jnp.zeros((plan.slot - rows, D), BF)
        if rows:
            added = gw[core, base : base + rows].astype(F32) + rgw[base : base + rows].astype(F32)
            slots[i, 0:rows] = added.astype(BF)
        if h_rows or v_rows:
            scratch[...] = jnp.zeros(scratch.shape, F32)
            for half in range(2):
                for j in range(5 if h_rows else 0):
                    cols = slice(D * j + 128 * half, D * j + 128 * half + 128)
                    scratch[half, pl.ds(h_off + j, h_rows, stride=5)] = sums[h_first : h_first + h_rows, cols]
                if v_rows:
                    scratch[half, v_off : v_off + v_rows] = vsum[v_first : v_first + v_rows, 128 * half : 128 * half + 128]
            whole = jnp.concatenate([scratch[0], scratch[1]], 1)
            slots[i, rows : plan.slot] = whole[rows:].astype(BF)


def segment_bounds():
    first = [0] + [(CAT + j * D) * D for j in range(BLOCKS + 1)]
    return list(zip(first, first[1:] + [A_ROWS * D + D * HEADS]))


class Rows:
    def __init__(self, ref):
        self.ref, self.height = ref, ref.shape[0]

    def chunks(self):
        return chunks(self.height)

    def get(self, lo, hi):
        return self.ref[lo:hi]

    def put(self, lo, hi, value):
        self.ref[lo:hi] = value


class Flat:
    def __init__(self, ref, buffer):
        self.ref, self.buffer, self.length = ref, buffer, ref.shape[1]
        self.whole = self.length // 1024 * 8
        self.height = -(-self.length // 1024) * 8

    def chunks(self):
        step = next(s for s in range(64, 0, -8) if self.whole % s == 0)
        return [(lo, lo + step) for lo in range(0, self.whole, step)] + [(self.whole, self.height)]

    def ends(self):
        rows = (self.length - 128 * self.whole) // 128
        return rows, self.length % 128, 128 * self.whole, 128 * (self.whole + rows)

    def get(self, lo, hi):
        if hi <= self.whole:
            return self.ref[0:1, 128 * lo : 128 * hi].reshape(hi - lo, 128)
        rows, lanes, first, last = self.ends()
        self.buffer[...] = jnp.zeros((8, 128), F32)
        if rows:
            self.buffer[0:rows] = self.ref[0:1, first:last].reshape(rows, 128)
        if lanes:
            self.buffer[rows : rows + 1, 0:lanes] = self.ref[0:1, last : self.length]
        return self.buffer[...]

    def put(self, lo, hi, value):
        if hi <= self.whole:
            self.ref[0:1, 128 * lo : 128 * hi] = value.reshape(1, 128 * (hi - lo))
            return
        rows, lanes, first, last = self.ends()
        if rows:
            self.ref[0:1, first:last] = value[0:rows].reshape(1, 128 * rows)
        if lanes:
            self.ref[0:1, last : self.length] = value[rows : rows + 1, 0:lanes]


def update_shard(plan, me, p_ref, m_ref, v_ref, outs, flat, squares, sq_in, push, to_plane, to_z):
    first_out, second_out, new_out, norm_out = outs
    height = p_ref.height
    start = me * plan.length
    correction = 1.0 - 0.5**STEP
    bounds = segment_bounds()

    def place(lo, hi):
        shape = (hi - lo, 128)
        return 128 * lo + 128 * lax.broadcasted_iota(jnp.int32, shape, 0) + lax.broadcasted_iota(jnp.int32, shape, 1)

    for lo, hi in p_ref.chunks():
        spot = place(lo, hi)
        grad = jnp.where(spot < plan.length, flat[lo:hi], 0.0)
        first_new = 0.5 * m_ref.get(lo, hi) + 0.5 * grad
        second_new = 0.5 * v_ref.get(lo, hi) + 0.5 * grad * grad
        first_out.put(lo, hi, first_new)
        second_out.put(lo, hi, second_new)
        decay = jnp.where(spot < bounds[-1][1] - start, 0.01 * p_ref.get(lo, hi), 0.0)
        update = first_new / correction / (jnp.sqrt(second_new / correction) + 1e-06) + decay
        flat[lo:hi] = jnp.where(spot < plan.length, update, 0.0)
        new_out.put(lo, hi, p_ref.get(lo, hi) - 0.5 * update)
    squares[...] = jnp.zeros(squares.shape, F32)

    def each_segment(body):
        for j, (first, last) in enumerate(bounds):
            pl.when((first < start + plan.length) & (last > start))(lambda j=j, first=first, last=last: body(j, first, last))

    def square_sums(j, first, last):
        weight, change = jnp.zeros((8, 128), F32), jnp.zeros((8, 128), F32)
        for lo, hi in p_ref.chunks():
            spot = place(lo, hi)
            inside = (spot >= first - start) & (spot < last - start)
            p, u = jnp.where(inside, p_ref.get(lo, hi), 0.0), jnp.where(inside, flat[lo:hi], 0.0)
            weight = weight + jnp.sum((p * p).reshape(-1, 8, 128), axis=0)
            change = change + jnp.sum((u * u).reshape(-1, 8, 128), axis=0)
        squares[0, j : j + 1] = jnp.sum(weight, axis=0, keepdims=True)
        squares[0, 16 + j : 17 + j] = jnp.sum(change, axis=0, keepdims=True)

    each_segment(square_sums)
    total = squares[0]
    for hop, targets in enumerate((to_plane, to_z)):
        lands = range(3) if hop == 0 else range(3, 3 + len(to_z))
        for c in [push(squares.at[hop], sq_in.at[k], to) for k, to in zip(lands, targets)]:
            c.wait_recv()
        for k in lands:
            total = total + sq_in[k]
        squares[hop + 1] = total
    norm = jnp.sqrt(jnp.sum(total, axis=1, keepdims=True))
    squares[3] = jnp.broadcast_to(norm, (32, 128))
    line = jnp.sqrt(jnp.sum(jnp.concatenate([total, jnp.zeros((96, 128), F32)], 0).T, axis=0, keepdims=True))
    norm_out[0:1] = line[:, 0:MATS]
    norm_out[1:2] = pltpu.roll(line, 112, 1)[:, 0:MATS]

    def scaled(j, first, last):
        ratio = squares[3, j : j + 1] / squares[3, 16 + j : 17 + j]
        for lo, hi in p_ref.chunks():
            spot = place(lo, hi)
            inside = (spot >= first - start) & (spot < last - start)
            new_out.put(lo, hi, jnp.where(inside, p_ref.get(lo, hi) - 0.5 * ratio * flat[lo:hi], new_out.get(lo, hi)))

    each_segment(scaled)


def reduce_kernel(
    plan, gw, gh, gv, st, ig, p_ref, m_ref, v_ref,
    st_out, ig_out, first_out, second_out, new_out, norm_out,
    rgw, rgh, rgv, slots, sums, vsum, scratch, in_d, in_x, in_y, in_z, slot128, flat, rolled, squares, sq_in,
    send, recv, local,
):
    n, rows = plan.n, plan.slot
    depth, cut = n // 4, plan.slot // 2
    core, me, near_x, near_y = neighbours(n)
    near_xy = near_x + near_y - me
    barrier = greet(core, me, near_x, near_y, n)
    pl.semaphore_wait(barrier, depth + 3)
    half = st.shape[1]
    number = iter(range(1 << 20))
    started = []

    def copy(src, dst, to):
        slot = next(number)
        c = pltpu.make_async_remote_copy(
            src_ref=src, dst_ref=dst, send_sem=send.at[slot], recv_sem=recv.at[slot], device_id=to, device_id_type=MESH
        )
        c.start()
        started.append(c)
        return c

    def column(index, k):
        return (index + n - 4 * k) % n

    sibling = at(1 - core, me)
    early = [
        copy(gw.at[1 - core], rgw, sibling),
        copy(gh.at[1 - core], rgh, sibling),
        copy(gv.at[1 - core], rgv, sibling),
    ]
    mine = pl.ds(pl.multiple_of(core * half, half), half)
    late = [
        copy(st.at[1 - core], st_out.at[mine], sibling),
        copy(ig.at[1 - core], ig_out.at[mine], sibling),
    ]
    stay = [
        pltpu.make_async_copy(st.at[core], st_out.at[mine], local.at[0]),
        pltpu.make_async_copy(ig.at[core], ig_out.at[mine], local.at[1]),
    ]
    for c in stay:
        c.start()
    for c in early:
        c.wait_recv()
    pack_slots(plan, core, gw, gh, gv, rgw, rgh, rgv, slots, sums, vsum, scratch)
    order = list(range(1, depth)) + [0]
    to_x, to_y = at(core, near_x), at(core, near_y)
    halves = {}
    for k in order:
        diagonal = column(near_xy, k)
        halves[k] = (
            copy(slots.at[diagonal, pl.ds(0, cut)], in_d.at[k, pl.ds(0, cut)], to_y),
            copy(slots.at[diagonal, pl.ds(cut, rows - cut)], in_d.at[k, pl.ds(cut, rows - cut)], to_x),
        )
    fulls = {}
    for k in order:
        ox, oy = column(near_x, k), column(near_y, k)
        halves[k][0].wait_recv()
        slots[ox, 0:cut] = (slots[ox, 0:cut].astype(F32) + in_d[k, 0:cut].astype(F32)).astype(BF)
        first = copy(slots.at[ox], in_x.at[k], to_x)
        halves[k][1].wait_recv()
        slots[oy, cut:rows] = (slots[oy, cut:rows].astype(F32) + in_d[k, cut:rows].astype(F32)).astype(BF)
        fulls[k] = (first, copy(slots.at[oy], in_y.at[k], to_y))
    along = {}
    for k in order:
        own = column(me, k)
        for c in fulls[k]:
            c.wait_recv()
        if k:
            total = slots[own].astype(F32) + in_x[k].astype(F32) + in_y[k].astype(F32)
            slots[own] = total.astype(BF)
            along[k] = copy(slots.at[own], in_z.at[k], at(core, own))
    for c in along.values():
        c.wait_recv()
    total = slots[me].astype(F32) + in_x[0].astype(F32) + in_y[0].astype(F32)
    for k in along:
        total = total + in_z[k].astype(F32)
    slot128[...] = jnp.zeros(slot128.shape, F32)
    slot128[pl.ds(0, rows, stride=2)] = total[:, 0:128]
    slot128[pl.ds(1, rows, stride=2)] = total[:, 128:D]
    lay_flat(plan, me, slot128, flat, rolled)

    to_z = [at(core, column(me, k)) for k in range(1, depth)]
    outs = (Rows(first_out), Rows(second_out), Rows(new_out), norm_out)
    to_plane = [to_x, to_y, at(core, near_xy)]
    update_shard(plan, me, Rows(p_ref), Rows(m_ref), Rows(v_ref), outs, flat, squares, sq_in, copy, to_plane, to_z)
    for c in late:
        c.wait_recv()
    for c in stay:
        c.wait()
    for c in started:
        c.wait_send()


def reduce_and_update(plan, gw, gh, gv, st, ig, p128, m128, v128):
    n, rows = plan.n, plan.slot
    depth = n // 4
    half = st.shape[1]
    height = p128.shape[0]
    vm = pl.BlockSpec(memory_space=pltpu.VMEM)
    hbm = pl.BlockSpec(memory_space=pl.ANY)
    copies = 5 + 2 * depth + 2 * depth + (depth - 1) + (depth - 1) + 3
    flat32 = jax.ShapeDtypeStruct((height, 128), F32)
    return pl.pallas_call(
        functools.partial(reduce_kernel, plan),
        out_shape=(
            jax.ShapeDtypeStruct((2 * half, D), BF),
            jax.ShapeDtypeStruct((2 * half, D), F32),
            flat32,
            flat32,
            flat32,
            jax.ShapeDtypeStruct((2, MATS), F32),
        ),
        in_specs=[vm] * 3 + [hbm] * 2 + [vm] * 3,
        out_specs=(hbm, hbm, vm, vm, vm, vm),
        scratch_shapes=[
            pltpu.VMEM((A_ROWS, D), BF),
            pltpu.VMEM((D, HPAD), BF),
            pltpu.VMEM(gv.shape[1:], F32),
            pltpu.VMEM((n, rows, D), BF),
            pltpu.VMEM((D, HPAD), F32),
            pltpu.VMEM((40, D), F32),
            pltpu.VMEM((2, rows, 128), F32),
            pltpu.VMEM((depth, rows, D), BF),
            pltpu.VMEM((depth, rows, D), BF),
            pltpu.VMEM((depth, rows, D), BF),
            pltpu.VMEM((depth, rows, D), BF),
            pltpu.VMEM((max(2 * rows, height + 48) + 80, 128), F32),
            pltpu.VMEM((height + 128, 128), F32),
            pltpu.VMEM((height + 40, 128), F32),
            pltpu.VMEM((4, 32, 128), F32),
            pltpu.VMEM((2 + depth, 32, 128), F32),
            pltpu.SemaphoreType.DMA((copies,)),
            pltpu.SemaphoreType.DMA((copies,)),
            pltpu.SemaphoreType.DMA((2,)),
        ],
        compiler_params=pltpu.CompilerParams(
            collective_id=1, has_side_effects=True, vmem_limit_bytes=48 * 1024 * 1024
        ),
    )(gw, gh, gv, st, ig, p128, m128, v128)


class Copies:
    def __init__(self, send, recv):
        self.send, self.recv, self.made, self.sent = send, recv, [], set()

    def add(self, src, dst, to, recv_slot=None, only=None):
        self.made.append((src, dst, to, recv_slot, only))
        return len(self.made) - 1

    def get(self, number):
        src, dst, to, recv_slot, _ = self.made[number]
        return pltpu.make_async_remote_copy(
            src_ref=src(), dst_ref=dst(), send_sem=self.send.at[number],
            recv_sem=self.recv.at[number] if recv_slot is None else recv_slot(),
            device_id=to(), device_id_type=MESH,
        )

    def start(self, *numbers):
        for number in numbers:
            self.get(number).start()

    def arrive(self, *numbers):
        for number in numbers:
            self.get(number).wait_recv()

    def leave(self, *numbers):
        for number in numbers:
            only = self.made[number][4]
            if number not in self.sent and only is None:
                self.get(number).wait_send()
            elif number not in self.sent:
                pl.when(only())(lambda number=number: self.get(number).wait_send())
            self.sent.add(number)


def fused_fits(plan):
    depth, half = plan.n // 4, plan.slot // 2
    plain = [b + plan.slot <= A_ROWS for b, h, v in zip(plan.a_base, plan.h_rows, plan.v_rows) if not (h or v)]
    vectors = [rows for rows in plan.v_rows if rows]
    return (
        all(plain)
        and vectors == [3 * (BLOCKS + 1)]
        and plan.n % 4 == 0
        and half >= 32
        and 4 * half <= HPAD
        and 2 * depth * plan.slot <= (BLOCKS + 1) * D
        and depth == 4
        and max(plan.a_rows) <= plan.slot
    )


def train_kernel(
    plan, x_ref, codes_ref, targets_ref, visits_ref, imp_ref, p_ref, m_ref, v_ref,
    st_out, ig_out, first_out, second_out, new_out, norm_out,
    w, wh, vec, both, away, rw, eye, wt, wht, vt, gsb, xt, mix, xh, gp, rstd, mean, stream, ex, br, dm, acc, lg, dl,
    gw, gh, gv, packed, st_stage, slot128, flat, rolled, vsum, vacc, vin, owned, squares, sq_in, tail,
    send, recv, z_recv, own_recv, local, ready,
):
    n, rows = plan.n, plan.slot
    depth, hrows = n // 4, plan.slot // 2
    cut = hrows // 32 * 16
    core, me, near_x, near_y = neighbours(n)
    near_xy = near_x + near_y - me
    width = both.shape[2]
    params_in, first_new, second_new, new = (Flat(ref, tail) for ref in (p_ref, first_out, second_out, new_out))
    moments = [
        pltpu.make_async_copy(src, dst, local.at[3 + i])
        for i, (src, dst) in enumerate(((m_ref, first_out), (v_ref, second_out)))
    ]
    z_me, j_me = me // 4, me % 4
    copies = Copies(send, recv)
    scratch = [slot128.at[0:rows], slot128.at[rows : 2 * rows]]
    barrier = greet(core, me, near_x, near_y, n, True)
    mine = pl.multiple_of(core * width, width)
    theirs = pl.multiple_of((1 - core) * width, width)
    x_copy = pltpu.make_async_copy(x_ref.at[pl.ds(mine, width)], st_stage.at[0], local.at[0])
    x_copy.start()
    for c in moments:
        c.start()
    for to, half in ((both.at[core], mine), (away, theirs)):
        cols = pl.ds(half, width)
        to[0:1] = codes_ref[:, cols]
        to[1:2] = targets_ref[0, :, cols]
        to[2:6] = visits_ref[:, cols]
        to[6:7] = targets_ref[1, :, cols]
        to[7:8] = targets_ref[2, :, cols]
    height = params_in.height
    for lo, hi in params_in.chunks():
        slot128[lo:hi] = params_in.get(lo, hi)
    place_shard(plan, me, slot128.at[0:height], slot128, flat, rolled)

    spare = (BLOCKS + 1) * D

    def slot_part(t, i, lo, count):
        row = pl.multiple_of(spare + rows * (t * depth + i // 4) + lo, 16)
        return xh.at[pl.ds(row, count), pl.ds(pl.multiple_of((i % 4) * D, D), D)]

    def column(index, k):
        return (index + n - 4 * k) % n

    def sibling():
        return at(1 - core, me)

    def same(make, to):
        return copies.add(make, make, to)

    low = core * hrows
    other_low = (1 - core) * hrows
    order = [0] + sorted(range(1, depth), key=lambda k: (min(k, depth - k), k))
    to_x, to_y, to_d = (lambda: at(core, near_x)), (lambda: at(core, near_y)), (lambda: at(core, near_xy))
    swap_ints = copies.add(lambda: away, lambda: both.at[core], sibling)

    def arrival(t, number):
        return own_recv.at[t * (depth + 2) + number]

    own_targets = [(lambda: near_x), (lambda: near_y)] + [lambda k=k: (me + 4 * k) % n for k in order[1:]]
    own_sends = [copies.add(lambda: slot_part(core, me, 0, rows), lambda: slot_part(core, me, 0, rows), sibling, lambda: arrival(core, 0))]
    for number, target in enumerate(own_targets, 1):
        for h in range(2):
            make = lambda h=h: slot_part(core, me, h * hrows, hrows)
            own_sends.append(
                copies.add(make, make, lambda h=h, target=target: at(h, target()), lambda number=number: arrival(core, number))
            )
    own_sends = own_sends[3 + 2 :] + own_sends[1:5] + own_sends[:1]

    def own_arrive(t, number, make):
        pltpu.make_async_remote_copy(
            src_ref=make(), dst_ref=make(), send_sem=send.at[0], recv_sem=arrival(t, number), device_id=sibling(), device_id_type=MESH
        ).wait_recv()

    gathers = []
    for t in range(2):
        g = {}
        for k in order:
            if k:
                g["x", k] = same(lambda t=t, k=k: slot_part(t, column(me, k), low, hrows), to_x)
                g["y", k] = same(lambda t=t, k=k: slot_part(t, column(me, k), low, hrows), to_y)
            g["d", k] = (
                same(lambda t=t, k=k: slot_part(t, column(near_x, k), low, cut), to_y),
                same(lambda t=t, k=k: slot_part(t, column(near_y, k), low + cut, hrows - cut), to_x),
            )
            g["s", k] = [
                same(lambda t=t, k=k, index=index: slot_part(t, column(index, k), low, hrows), sibling) if index is not me or k else None
                for index in (me, near_x, near_y, near_xy)
            ]
        gathers.append(g)

    def gather_0(t):
        pl.when(core == t)(lambda: copies.start(*own_sends))

    def gather_1(t):
        g = gathers[t]
        for number, k in enumerate(order[1:], 3):
            own_arrive(t, number, lambda: slot_part(t, me, low, hrows))
            copies.start(g["x", k], g["y", k], g["s", k][0])

    def gather_2(t):
        g = gathers[t]
        for k in order:
            if k:
                copies.arrive(g["x", k])
            else:
                own_arrive(t, 1, lambda: slot_part(t, me, low, hrows))
            copies.start(g["d", k][0], g["s", k][1])
            if k:
                copies.arrive(g["y", k])
            else:
                own_arrive(t, 2, lambda: slot_part(t, me, low, hrows))
            copies.start(g["d", k][1], g["s", k][2])

    def gather_3(t):
        g = gathers[t]
        for k in order:
            copies.arrive(*g["d", k])
            copies.start(g["s", k][3])

    def gather_4(t):
        g = gathers[t]
        pl.when(core != t)(lambda: own_arrive(t, 0, lambda: slot_part(t, me, 0, rows)))
        for k in order:
            copies.arrive(*(c for c in g["s", k] if c is not None))

    def unpack(t):
        lg[4 * D : 5 * D, 128:D] = jnp.zeros((D, 128), F32)
        vsum[...] = jnp.zeros(vsum.shape, F32)
        for i in range(n):
            row, lane = spare + rows * (t * depth + i // 4), (i % 4) * D
            unpack_rows(plan, i, xh[row : row + rows, lane : lane + D], w.at[t], lg, vsum, scratch)
        for j in range(5):
            wh[t, :, D * j : D * j + D] = lg[D * j : D * j + D].astype(BF)
        vec[t] = vsum[...].astype(BF)

    total = jnp.sum(imp_ref[...].astype(F32), axis=1, keepdims=True)
    lane_d = lax.broadcasted_iota(jnp.int32, (1, D), 1)
    hi, mid, lo = split3(total)
    left = slot128[pl.ds(0, rows, stride=2)]
    right = slot128[pl.ds(1, rows, stride=2)]
    own = jnp.concatenate([left, right], 1)
    last = jnp.where(lane_d == 0, hi, jnp.where(lane_d == 1, mid, jnp.where(lane_d == 2, lo, 0.0)))
    last_row = lax.broadcasted_iota(jnp.int32, (rows, D), 0) == rows - 1
    slot_part(core, me, 0, rows)[...] = jnp.where(last_row, last, own).astype(BF)
    pl.semaphore_wait(barrier, depth + 3 + 2 + depth - 1)
    gather_0(0)
    copies.start(swap_ints)
    eye[...] = identity(D)
    x_copy.wait()
    for c in range(0, width, CB):
        xt[0, 0:D, c : c + CB] = nt(eye[...], st_stage[0, c : c + CB, :]).astype(BF)
    gather_1(0)
    gather_0(1)
    gather_2(0)
    gather_3(0)
    copies.arrive(swap_ints)
    gather_4(0)
    unpack(0)
    total = jnp.zeros((1, D), F32)
    for i in range(n):
        row, lane = spare + rows * (i // 4), (i % 4) * D
        total = total + xh[row + rows - 16 : row + rows, lane : lane + D].astype(F32)[15:16]
    weight_sum = jnp.sum(jnp.where(lane_d < 3, total, 0.0), axis=1, keepdims=True)
    rw[...] = jnp.broadcast_to(imp_ref[:, pl.ds(mine, width)].astype(F32) / weight_sum, (8, width))

    fwd = (eye, w, wh, vec, wt, vt, gsb, xt, mix, xh, gp, rstd, stream, mean, both, width)

    def during_forward(k):
        pl.when(k == 6)(lambda: gather_2(1))

    def emit_states(t):
        for c in range(0, width, CB):
            st_stage[t, c : c + CB, :] = nt(eye[...], xt[t + 1, 0:D, c : c + CB]).astype(BF)

    gather_1(1)
    forward_tower(0, fwd, during_forward, lambda: gather_3(1))
    gather_4(1)
    copies.leave(*range(len(copies.made)))
    unpack(1)
    forward_tower(1, fwd)
    emit_states(0)
    emit_states(1)
    out_rows = pl.ds(mine, width)
    st_copy = copies.add(lambda: st_stage.at[1 - core], lambda: st_out.at[out_rows], sibling)
    copies.start(st_copy)
    st_stay = pltpu.make_async_copy(st_stage.at[core], st_out.at[out_rows], local.at[1])
    st_stay.start()

    packed_of = [i for i in range(n) if plan.h_rows[i] or plan.v_rows[i]]
    owner = plan.v_rows.index(3 * (BLOCKS + 1))

    early = (2, 3)

    def piece(t, zz, b, lo, count):
        if t == 1 and zz in early:
            arena, first, q = dl, 0, 7 * early.index(zz) + b
        elif t == 1:
            arena, first, q = mix, BLOCKS * (D + 16), 7 * zz + b
        else:
            arena, first, q = xh, spare, 7 * zz + b
        row = pl.multiple_of(first + hrows * (q // 4) + lo, 16)
        return arena.at[pl.ds(row, count), pl.ds(pl.multiple_of((q % 4) * D, D), D)]

    def block(t, zz, b):
        return piece(t, zz, b, 0, hrows)

    def z_in(h, k, lo=0, count=hrows):
        return st_stage.at[0, pl.ds(pl.multiple_of(hrows * (h * (depth - 1) + k - 1) + lo, 16), count)]

    def z_out(t, zz, lo, count):
        if t == 1 and zz in early:
            return st_stage.at[1, pl.ds(hrows * early.index(zz) + lo, count)]
        return piece(t, zz, j_me, lo, count)

    def job_pieces(t, zz):
        return [(0, cut), (cut, hrows - cut)] if (t, zz) == (0, 0) else [(0, hrows)]

    def slot_half(t, i, lo):
        if i in packed_of:
            return packed.at[packed_of.index(i), pl.ds(pl.multiple_of(lo, 16), hrows)]
        return gw.at[t, pl.ds(pl.multiple_of(plan.a_base[i] + lo, 16), hrows)]

    j_x, j_y, j_d = near_x % 4, near_y % 4, near_xy % 4
    direct = ((0, 0), (0, 1), (0, 2), (1, 2), (1, 3))
    jobs = {}
    for t in range(2):
        for zz in range(depth):
            job = {}
            job["swap"] = [
                copies.add(lambda t=t, i=4 * zz + j: slot_half(t, i, other_low), lambda t=t, zz=zz, j=j: block(t, zz, j), sibling)
                for j in range(4)
            ]
            pieces = job_pieces(t, zz)
            for side, b, j, to in (("x", 5, j_x, to_x), ("y", 6, j_y, to_y), ("d", 4, j_d, to_d)):
                job[side] = [
                    copies.add(
                        lambda t=t, zz=zz, j=j, lo=lo, count=count: piece(t, zz, j, lo, count),
                        lambda t=t, zz=zz, b=b, lo=lo, count=count: piece(t, zz, b, lo, count),
                        to,
                    )
                    for lo, count in pieces
                    if side != "d" or (t, zz) in direct
                ]
            if (t, zz) not in direct:
                job["d"] = [
                    copies.add(
                        lambda t=t, zz=zz, lo=lo, count=count: piece(t, zz, j_d, lo, count),
                        lambda t=t, zz=zz, lo=lo, count=count: piece(t, zz, 4, lo, count),
                        to,
                    )
                    for to, lo, count in ((to_y, 0, cut), (to_x, cut, hrows - cut))
                ]
            job["z"] = [
                copies.add(
                    lambda t=t, zz=zz, lo=lo, count=count: z_out(t, zz, lo, count),
                    lambda zz=zz, lo=lo, count=count: z_in(core, (zz + depth - z_me) % depth, lo, count),
                    lambda t=t, zz=zz: at(t, 4 * zz + j_me),
                    lambda zz=zz, part=part: z_recv.at[(2 * part + core) * depth + (zz + depth - z_me) % depth],
                    lambda zz=zz: z_me != zz,
                )
                for part, (lo, count) in enumerate(pieces)
            ]
            jobs[t, zz] = job

    def pack(t, planes):
        wanted = [i for i in packed_of if i // 4 in planes]
        for i in wanted:
            a_rows, h_rows, h_off, h_first = plan.a_rows[i], plan.h_rows[i], plan.h_off[i], plan.h_first[i]
            to = packed.at[packed_of.index(i)]
            for part in scratch:
                part[...] = jnp.zeros(part.shape, F32)
            lo16, hi16 = h_first // 16 * 16, -(-(h_first + h_rows) // 16) * 16
            for half in range(2):
                for j in range(5 if h_rows else 0):
                    cols = slice(D * j + 128 * half, D * j + 128 * half + 128)
                    value = gh[t, lo16:hi16, cols].astype(F32)[h_first - lo16 : h_first - lo16 + h_rows]
                    scratch[half][pl.ds(h_off + j, h_rows, stride=5)] = value
            whole = jnp.concatenate([scratch[0][...], scratch[1][...]], 1)
            to[a_rows:rows] = whole[a_rows:].astype(BF)
            if a_rows:
                to[0:a_rows] = gw[t, plan.a_base[i] : plan.a_base[i] + a_rows]

    def plus(*refs):
        value = refs[0][...].astype(F32)
        for ref in refs[1:]:
            value = value + ref[...].astype(F32)
        return value

    def sum_0(t, zz):
        copies.start(*jobs[t, zz]["swap"])

    def sum_1(t, zz):
        job = jobs[t, zz]
        for j in range(4):
            copies.arrive(job["swap"][j])
            target = block(t, zz, j)
            target[...] = plus(slot_half(t, 4 * zz + j, low), target).astype(BF)
        if (t, zz) in direct:
            for x, y, d in zip(job["x"], job["y"], job["d"]):
                copies.start(x, y, d)
        else:
            copies.start(*job["d"])

    def sum_2(t, zz):
        job = jobs[t, zz]
        for side, copy, j, lo, count in (("x", job["d"][0], j_x, 0, cut), ("y", job["d"][1], j_y, cut, hrows - cut)):
            copies.arrive(copy)
            target = piece(t, zz, j, lo, count)
            target[...] = plus(target, piece(t, zz, 4, lo, count)).astype(BF)
            copies.start(*job[side])

    def sum_3(t, zz):
        job = jobs[t, zz]
        pieces = job_pieces(t, zz)
        for part, (lo, count) in enumerate(pieces):
            copies.arrive(job["x"][part], job["y"][part])
            value = plus(*(piece(t, zz, b, lo, count) for b in (j_me, 5, 6)))
            if (t, zz) in direct:
                copies.arrive(job["d"][part])
                value = value + piece(t, zz, 4, lo, count)[...].astype(F32)
            last = part == len(pieces) - 1

            @pl.when(z_me != zz)
            def _():
                z_out(t, zz, lo, count)[...] = value.astype(BF)
                copies.start(job["z"][part])

            @pl.when((z_me == zz) & (core == t))
            def _():
                owned[core, lo : lo + count] = value

            @pl.when((z_me == zz) & (core != t))
            def _():
                owned[2, lo : lo + count] = value
                if last:
                    copies.start(hand_over)

    def z_wait(h, k, part, lo, count):
        src = z_in(h, k, lo, count)
        pltpu.make_async_remote_copy(
            src_ref=src, dst_ref=src, send_sem=send.at[0], recv_sem=z_recv.at[(2 * part + h) * depth + k],
            device_id=sibling(), device_id_type=MESH,
        ).wait_recv()

    def sum_4():
        copies.arrive(hand_over)
        in_pieces = (z_me == 0) & (core == 0)
        for h in range(2):
            for k in range(1, depth):

                @pl.when(in_pieces)
                def _():
                    for part, (lo, count) in enumerate(job_pieces(0, 0)):
                        z_wait(h, k, part, lo, count)

                @pl.when((z_me != 0) | (core != 0))
                def _():
                    z_wait(h, k, 0, 0, hrows)

                final(h)[...] = final(h)[...] + z_in(h, k)[...].astype(F32)

    def final(h):
        return owned.at[h]

    outgo = owned.at[2]

    def vector_step(step):
        sources = [gv.at[1 - core], vacc.at[0], vacc.at[1]]
        along = [lambda k=k: at(core, (me + 4 * k) % n) for k in range(1, depth)]
        targets = [[sibling], [to_x, to_y, to_d], along]
        if step:
            base = gv[core] if step == 1 else vacc[step - 2]
            for number, k in vector_copies[-1]:
                copies.arrive(number)
                base = base + vin[k]
            vacc[step - 1] = base
        if step < 3:
            started = []
            for k, to in enumerate(targets[step], (0, 1, 4)[step]):
                number = copies.add(lambda step=step: sources[step], lambda k=k: vin.at[k], to)
                copies.start(number)
                started.append((number, k))
            vector_copies.append(started)

    vector_copies = []
    hand_over = copies.add(lambda: outgo, lambda: final(core), sibling)
    peers = [(1 - core, me), (core, near_x), (core, near_y), (core, near_xy)] + [(1 - core, (me + 4 * k) % n) for k in range(1, depth)] + [(core, (me + 4 * k) % n) for k in range(1, depth)]

    bwd = (eye, w, wh, vec, wht, vt, gsb, xt, mix, xh, gp, rstd, stream, ex, br, dm, acc, lg, dl, both, rw, gw, gh, gv, dm, width)
    ig_copies = [copies.add(lambda: dm, lambda: ig_out.at[out_rows], sibling, None, lambda t=t: core != t) for t in range(2)]

    def ig_local():
        return pltpu.make_async_copy(dm, ig_out.at[out_rows], local.at[2])

    def emit_inputs(t):
        pl.when(core == t)(lambda: ig_local().start())
        pl.when(core != t)(lambda: copies.start(ig_copies[t]))

    def free_inputs(t):
        pl.when(core == t)(lambda: ig_local().wait())
        pl.when(core != t)(lambda: copies.get(ig_copies[t]).wait_send())

    def signal_ready(which):
        for to_core, to_index in peers:
            pl.semaphore_signal(ready.at[which], inc=1, device_id=at(to_core, to_index), device_id_type=MESH)

    def wait_ready(which):
        pl.semaphore_wait(ready.at[which], len(peers))

    def schedule(i, steps):
        for step in sorted({s[0] for s in steps}):

            def run(step=step):
                for s, f, *args in steps:
                    if s == step:
                        f(*args)

            pl.when(i == step)(run)

    def after_head_1():
        copies.leave(st_copy)
        st_stay.wait()
        signal_ready(0)

    def during_backward_1(i):
        schedule(i, [
            (2, wait_ready, 0), (2, pack, 1, (3,)), (2, sum_0, 1, 3),
            (4, sum_1, 1, 3), (4, pack, 1, (2,)), (4, sum_0, 1, 2),
            (6, sum_1, 1, 2),
            (8, sum_3, 1, 3),
        ])

    ex[...] = jnp.zeros_like(ex)
    backward_tower(1, bwd, after_head_1, during_backward_1, None, lambda: sum_3(1, 2))
    emit_inputs(1)
    signal_ready(1)
    for zz in early:
        job = jobs[1, zz]
        copies.leave(*job["swap"], *job["d"], *job["x"], *job["y"])

    def after_head_0():
        wait_ready(1)
        sum_0(1, 1)
        sum_0(1, 0)
        pack(0, (3,))
        sum_0(0, 3)

    def during_backward_0(i):
        schedule(i, [
            (1, sum_1, 1, 1), (1, sum_1, 1, 0),
            (2, sum_1, 0, 3),
            (4, sum_2, 1, 1), (4, sum_2, 1, 0), (4, pack, 0, (2,)), (4, sum_0, 0, 2),
            (5, sum_2, 0, 3),
            (6, sum_1, 0, 2),
            (8, sum_3, 1, 1), (8, sum_3, 1, 0), (8, sum_0, 0, 1),
            (9, sum_3, 0, 3), (9, sum_1, 0, 1),
        ])

    def after_weights():
        sum_0(0, 0)
        vector_step(0)

    backward_tower(0, bwd, after_head_0, during_backward_0, lambda: free_inputs(1), after_weights)
    emit_inputs(0)
    sum_1(0, 0)
    vector_step(1)
    sum_3(0, 2)
    sum_3(0, 1)
    sum_3(0, 0)
    vector_step(2)
    sum_4()
    vector_step(3)

    slot128[...] = jnp.zeros(slot128.shape, F32)
    for h in range(2):
        slot128[pl.ds(2 * hrows * h, hrows, stride=2)] = final(h)[:, 0:128]
        slot128[pl.ds(2 * hrows * h + 1, hrows, stride=2)] = final(h)[:, 128:D]

    @pl.when(me == owner)
    def _():
        for kind in range(3):
            first = 2 * (plan.v_off[owner] + kind * (BLOCKS + 1))
            for h in range(2):
                value = vacc[2, kind, 0 : BLOCKS + 1, 128 * h : 128 * h + 128]
                slot128[pl.ds(first + h, BLOCKS + 1, stride=2)] = value

    def push(src, dst, to):
        number = copies.add(lambda: src, lambda: dst, lambda: to)
        copies.start(number)
        return copies.get(number)

    lay_flat(plan, me, slot128, flat, rolled)
    for c in moments:
        c.wait()
    update_shard(
        plan, me, params_in, first_new, second_new, (first_new, second_new, new, norm_out),
        flat, squares, sq_in, push, [to_x(), to_y(), to_d()], [at(core, (me + 4 * k) % n) for k in range(1, depth)],
    )
    copies.arrive(st_copy)
    pl.when(core == 0)(lambda: copies.arrive(ig_copies[0]))
    pl.when(core == 1)(lambda: copies.arrive(ig_copies[1]))
    free_inputs(0)
    copies.sent.update(ig_copies)
    assert len(copies.made) <= 11 * n
    copies.leave(*range(len(copies.made)))


def finish_kernel(st, ig, first, second, new, norms, st_out, ig_out, first_out, second_out, new_out, low_out, norms_out, *rest):
    *held, into, outof = rest
    moves = []
    for src, dst, mid, parts in zip((new, ig, st, first, second), (new_out, ig_out, st_out, first_out, second_out), held, (1, 8, 4, 1, 1)):
        rows = src.shape[0] // parts
        for i in range(parts):
            at_rows = pl.ds(i * rows, rows)
            number = len(moves)
            moves.append(
                (
                    pltpu.make_async_copy(src.at[at_rows], mid.at[at_rows], into.at[number]),
                    pltpu.make_async_copy(mid.at[at_rows], dst.at[at_rows], outof.at[number]),
                )
            )
    for load, _ in moves:
        load.start()
    for load, store in moves:
        load.wait()
        store.start()
    size = new.shape[1]
    for lo in range(0, size, 8192):
        hi = min(lo + 8192, size)
        low_out[0:1, lo:hi] = held[0][0:1, lo:hi].astype(BF)
    norms_out[...] = norms[...]
    for _, store in moves:
        store.wait()


def finish(st, ig, first, second, new, norms):
    vm = pl.BlockSpec(memory_space=pltpu.VMEM)
    hbm = pl.BlockSpec(memory_space=pl.ANY)
    arrays = (st, ig, first, second, new)
    shapes = [jax.ShapeDtypeStruct(v.shape, v.dtype) for v in arrays]
    return pl.pallas_call(
        finish_kernel,
        out_shape=(*shapes, jax.ShapeDtypeStruct(new.shape, BF), jax.ShapeDtypeStruct(norms.shape, F32)),
        in_specs=[hbm] * 5 + [vm],
        out_specs=(hbm,) * 5 + (vm,) * 2,
        scratch_shapes=[pltpu.VMEM(v.shape, v.dtype) for v in (new, ig, st, first, second)] + [pltpu.SemaphoreType.DMA((15,))] * 2,
        compiler_params=pltpu.CompilerParams(vmem_limit_bytes=62 * 1024 * 1024),
    )(st, ig, first, second, new, norms)


def train(plan, latent, codes, targets, visits, imp, params, first, second):
    n, rows = plan.n, plan.slot
    depth, hrows = n // 4, rows // 2
    width = codes.shape[1] // 2
    height = -(-params.shape[1] // 1024) * 8
    vm = pl.BlockSpec(memory_space=pltpu.VMEM)
    hbm = pl.BlockSpec(memory_space=pl.ANY)
    packed = sum(1 for h, v in zip(plan.h_rows, plan.v_rows) if h or v)
    return pl.pallas_call(
        functools.partial(train_kernel, plan),
        out_shape=(
            jax.ShapeDtypeStruct((2 * width, D), BF),
            jax.ShapeDtypeStruct((2 * width, D), F32),
            jax.ShapeDtypeStruct(params.shape, F32),
            jax.ShapeDtypeStruct(params.shape, F32),
            jax.ShapeDtypeStruct(params.shape, F32),
            jax.ShapeDtypeStruct((2, MATS), F32),
        ),
        in_specs=[hbm] + [vm] * 5 + [hbm] * 2,
        out_specs=(hbm, hbm, vm, vm, vm, vm),
        scratch_shapes=[
            pltpu.VMEM((2, A_ROWS, D), BF),
            pltpu.VMEM((2, D, HPAD), BF),
            pltpu.VMEM((2, 128, D), BF),
            pltpu.VMEM((2, 8, width), jnp.int32),
            pltpu.VMEM((8, width), jnp.int32),
            pltpu.VMEM((8, width), F32),
            *work_scratch(width),
            pltpu.VMEM((2, A_ROWS, D), BF),
            pltpu.VMEM((2, D, HPAD), BF),
            pltpu.VMEM((2, 3, 16, D), F32),
            pltpu.VMEM((packed, rows, D), BF),
            pltpu.VMEM((2, width, D), BF),
            pltpu.VMEM((max(2 * rows, height + 48) + 80, 128), F32),
            pltpu.VMEM((height + 128, 128), F32),
            pltpu.VMEM((height + 40, 128), F32),
            pltpu.VMEM((128, D), F32),
            pltpu.VMEM((3, 3, 16, D), F32),
            pltpu.VMEM((3 + depth, 3, 16, D), F32),
            pltpu.VMEM((3, hrows, D), F32),
            pltpu.VMEM((4, 32, 128), F32),
            pltpu.VMEM((2 + depth, 32, 128), F32),
            pltpu.VMEM((8, 128), F32),
            pltpu.SemaphoreType.DMA((11 * n,)),
            pltpu.SemaphoreType.DMA((11 * n,)),
            pltpu.SemaphoreType.DMA((4 * depth,)),
            pltpu.SemaphoreType.DMA((2 * (depth + 2),)),
            pltpu.SemaphoreType.DMA((5,)),
            pltpu.SemaphoreType.REGULAR((2,)),
        ],
        compiler_params=pltpu.CompilerParams(
            collective_id=2, has_side_effects=True, vmem_limit_bytes=63 * 1024 * 1024
        ),
    )(latent, codes, targets, visits, imp, params, first, second)


def on_device(latent, codes, targets, visits, importance, params, first_moment, second_moment):
    me = lax.axis_index("tower")
    row_count = latent.shape[0]
    half = row_count // 2
    shard_len = params.shape[1]
    plan = Plan(lax.axis_size("dp"), shard_len)
    if fused_fits(plan):
        states_out, inputs_out, first, second, new, norms = train(
            plan, latent, codes, targets.transpose(1, 0, 2), visits[0].T, importance[None], params, first_moment, second_moment
        )
        states_out, inputs_out, first, second, new, low, norms = finish(states_out, inputs_out, first, second, new, norms)
    else:
        height = -(-plan.rows128 // 8) * 8
        p128, m128, v128 = (
            jnp.pad(v, ((0, 0), (0, 128 * height - shard_len))).reshape(height, 128)
            for v in (params, first_moment, second_moment)
        )
        ints = jnp.concatenate([codes, targets[0, :1], visits[0].T, targets[0, 1:]], 0)
        x = lax.dynamic_slice_in_dim(latent, me * half, half, 0)
        w, wh, vec, both, rw = gather(plan, p128, ints, importance[None])
        st, ig, gw, gh, gv = compute(x, both, rw, w, wh, vec)
        states_out, inputs_out, *flat, norms = reduce_and_update(plan, gw, gh, gv, st, ig, p128, m128, v128)
        first, second, new = (v.reshape(1, -1)[:, :shard_len] for v in flat)
        low = new.astype(BF)
    return (states_out[None], inputs_out[None], first, second, new, low, norms[None])


def solution(mesh):
    in_specs = (
        P("dp", None),
        P("tower", "dp"),
        P("tower", None, "dp"),
        P("tower", "dp", None),
        P("dp"),
        P("tower", "dp"),
        P("tower", "dp"),
        P("tower", "dp"),
    )
    out_specs = (
        P("tower", "dp", None),
        P("tower", "dp", None),
        P("tower", "dp"),
        P("tower", "dp"),
        P("tower", "dp"),
        P("tower", "dp"),
        P("tower", None, None),
    )
    return jax.shard_map(
        on_device, mesh=mesh, in_specs=in_specs, out_specs=out_specs, check_vma=False
    )
```

```python
import functools

import jax
import jax.numpy as jnp
from jax import lax
from jax.experimental import pallas as pl
from jax.experimental.pallas import tpu as pltpu
from jax.sharding import PartitionSpec as P

D = 256
CODES = 32
BINS = 601
BLOCKS = 10
STEP = 5
HEADS = 1238
MATS = 12
P_SIZE = 1054464
HPAD = 1280
CAT = D + CODES
A_ROWS = CAT + BLOCKS * D
BF = jnp.bfloat16
F32 = jnp.float32
GELU_C = 0.7978845608028654
GELU_K = 0.044715


def nn(a, b):
    return jnp.dot(a, b, preferred_element_type=F32)


def nt(a, b):
    return lax.dot_general(a, b, (((1,), (1,)), ((), ())), preferred_element_type=F32)


def identity(n):
    return (lax.broadcasted_iota(jnp.int32, (n, n), 0) == lax.broadcasted_iota(jnp.int32, (n, n), 1)).astype(BF)


ZETA = (GELU_C * GELU_K) ** (1.0 / 3.0)
B0 = GELU_C / ZETA
E0 = 0.5 / ZETA


def wide(v, cs):
    return jnp.concatenate([v] * ((cs.stop - cs.start) // v.shape[1]), 1)


def norm_act(src, cs, gs, unit, gp, rstd, out):
    for r in range(0, D, 32):
        rs = slice(r, r + 32)
        xh = src[rs, cs] * rstd
        z = xh * wide(gs[rs, 0:128], cs) + wide(gs[rs, 128:256], cs)
        z2 = z * z
        t = jnp.tanh(z * (z2 + B0))
        q = t * E0 + E0
        a = z * q
        out(rs, a)
        unit[rs, cs] = xh.astype(BF)
        gp[rs, cs] = (q + (a * (1.0 - t)) * (z2 * 3.0 + B0)).astype(BF)


def broadcast_vectors(vt, rows):
    k = lax.broadcasted_iota(jnp.int32, (128, 128), 0)
    picks = jnp.concatenate([(k == row).astype(BF) for row in rows], 1)
    return nn(vt, picks)


def head_stage(cs, lg, dl, ints, rw):
    width = rw.shape[1]
    it8 = lax.broadcasted_iota(jnp.int32, (8, width), 0)
    low = -jnp.inf
    b75, b150, b154 = lg[600:608], lg[1200:1208], lg[1232:1240]

    def top(block):
        return jnp.max(block, axis=0, keepdims=True)

    def steps(lo, hi, step):
        return [(r, min(r + step, hi)) for r in range(lo, hi, step)]

    def folded(value):
        return value.reshape(-1, 8, width)

    def top_range(lo, hi):
        best = None
        for r, end in steps(lo, hi, 40):
            part = jnp.max(folded(lg[r:end]), axis=0)
            best = part if best is None else jnp.maximum(best, part)
        return best

    max_v = top(jnp.maximum(top_range(0, 600), jnp.where(it8 < 1, b75, low)))
    max_r = top(
        jnp.maximum(
            jnp.maximum(top_range(608, 1200), jnp.where(it8 >= 1, b75, low)),
            jnp.where(it8 < 2, b150, low),
        )
    )
    max_c = top(
        jnp.maximum(
            jnp.maximum(top_range(1208, 1232), jnp.where(it8 >= 2, b150, low)),
            jnp.where(it8 < 2, b154, low),
        )
    )
    in_policy = (it8 >= 2) & (it8 < 6)
    max_p = top(jnp.where(in_policy, b154, low))

    def exp_range(lo, hi, best):
        acc = jnp.zeros((8, width), F32)
        for r, end in steps(lo, hi, 40):
            e = jnp.exp(lg[r:end] - best)
            lg[r:end] = e
            acc = acc + jnp.sum(folded(e), axis=0)
        return acc

    e75 = jnp.exp(b75 - jnp.where(it8 < 1, max_v, max_r))
    e150 = jnp.exp(b150 - jnp.where(it8 < 2, max_r, max_c))
    e154 = jnp.exp(b154 - jnp.where(it8 < 2, max_c, max_p))

    def total(acc):
        return rw / jnp.sum(acc, axis=0, keepdims=True)

    inv_v = total(exp_range(0, 600, max_v) + jnp.where(it8 < 1, e75, 0.0))
    inv_r = total(exp_range(608, 1200, max_r) + jnp.where(it8 >= 1, e75, 0.0) + jnp.where(it8 < 2, e150, 0.0))
    inv_c = total(exp_range(1208, 1232, max_c) + jnp.where(it8 >= 2, e150, 0.0) + jnp.where(it8 < 2, e154, 0.0))
    inv_p = total(jnp.where(in_policy, e154, 0.0))
    hit_v = ints[1:2]
    hit_r = ints[6:7] + BINS
    hit_c = ints[7:8] + 2 * BINS
    counts = jnp.where(in_policy, ints.astype(F32), 0.0)
    share = counts * (rw / jnp.sum(counts, axis=0, keepdims=True))

    def minus(value, lo, *hits):
        at = lax.broadcasted_iota(jnp.int32, value.shape, 0)
        for hit in hits:
            value = value - jnp.where(at == hit - lo, rw, 0.0)
        return value

    d75 = minus(e75 * jnp.where(it8 < 1, inv_v, inv_r), 600, hit_v, hit_r)
    d150 = minus(e150 * jnp.where(it8 < 2, inv_r, inv_c), 1200, hit_r, hit_c)
    d154 = minus(e154 * jnp.where(it8 < 2, inv_c, inv_p), 1232, hit_c) - share
    d154 = jnp.where(it8 < 6, d154, 0.0)

    def emit(lo, hi, inv, hit):
        for r, end in steps(lo, hi, 80):
            dl[r:end, cs] = minus(lg[r:end] * inv, r, hit).astype(BF)

    def pair(first, second):
        return jnp.concatenate([first, second], 0).astype(BF)

    emit(0, 592, inv_v, hit_v)
    dl[592:608, cs] = pair(minus(lg[592:600] * inv_v, 592, hit_v), d75)
    emit(608, 1200, inv_r, hit_r)
    dl[1200:1216, cs] = pair(d150, minus(lg[1208:1216] * inv_c, 1208, hit_c))
    emit(1216, 1232, inv_c, hit_c)
    dl[1232:1248, cs] = pair(d154, jnp.zeros_like(d154))
    dl[1248:HPAD, cs] = jnp.zeros((HPAD - 1248, width), BF)


CB = 256
GROUP = 2


def saved_views(t, mix, xh):
    def mixed(k):
        return mix.at[pl.ds(pl.multiple_of((t * BLOCKS + k - 1) * (D + 16), 16), D + 16)]

    def unit(k):
        return xh.at[pl.ds(pl.multiple_of((t * (BLOCKS + 1) + k) * D, D), D)]

    return mixed, unit


def column_groups(width):
    blocks = [slice(c, c + CB) for c in range(0, width, CB)]
    per = min(GROUP, len(blocks))
    return blocks, per, [slice(c, c + per * CB) for c in range(0, width, per * CB)]


def forward_tower(t, refs, during=None, before_last=None):
    (eye, w, wh, vec, wt, vt, gsb, xt, mix, xh, gp, rstd, stream, mean, ints, width) = refs
    blocks, per, groups = column_groups(width)
    mixed, unit = saved_views(t, mix, xh)
    first_bias = 2 * (BLOCKS + 1)
    ones = jnp.ones((16, D), BF)

    def mean_rows(slot):
        value = nn(ones, wt[slot, 0:D])[0:8] * (1.0 / D)
        high = value.astype(BF).astype(F32)
        wt[slot, D : D + 16] = jnp.concatenate([high, value - high], 0).astype(BF)

    def vectors(k):
        gsb[k % 2] = broadcast_vectors(vt[...], (k, k + BLOCKS + 1)) * ZETA

    def prefetch(k):
        vectors(k)
        row = pl.multiple_of(CAT + jnp.minimum(k - 1, BLOCKS - 1) * D, 32)
        wt[k % 2, 0:D, 0:D] = nt(eye[...], w[t, pl.ds(row, D)]).astype(BF)
        at_row = lax.broadcasted_iota(jnp.int32, (128, 128), 0) == k + first_bias
        at_lane = lax.broadcasted_iota(jnp.int32, (128, 128), 1) == 0
        wt[k % 2, 0:D, D:384] = nn(vt[...], (at_row & at_lane).astype(BF)).astype(BF)
        mean_rows(k % 2)

    def row_of(k):
        return pl.ds(t * (BLOCKS + 1) + k, 1)

    def stage(k, c):
        def keep(rs, a):
            mixed(k)[rs, blocks[c]] = a.astype(BF)

        norm_act(stream, blocks[c], gsb.at[k % 2], unit(k), gp.at[t, k], rstd[row_of(k), blocks[c]], keep)

    def spread(square, k, cs):
        var = jnp.sum(square, axis=0, keepdims=True) * (1.0 / D)
        rstd[row_of(k), cs] = lax.rsqrt(var + 1e-05)

    def add(k, cs, out, fresh):
        shift = out[D : D + 1] + out[D + 8 : D + 9]
        square = jnp.zeros((8, out.shape[1]), F32)
        for r in range(0, D, 32):
            value = out[r : r + 32] - shift
            if not fresh:
                value = stream[r : r + 32, cs] + value
            stream[r : r + 32, cs] = value
            square = square + jnp.sum((value * value).reshape(4, 8, -1), axis=0)
        if not fresh:
            mean[0:1, cs] = mean[0:1, cs] + shift
        spread(square, k + 1, cs)

    def centre(cs):
        total = jnp.zeros((8, CB), F32)
        for r in range(0, D, 32):
            total = total + jnp.sum(stream[r : r + 32, cs].reshape(4, 8, -1), axis=0)
        middle = jnp.sum(total, axis=0, keepdims=True) * (1.0 / D)
        mean[0:1, cs] = middle
        square = jnp.zeros((8, CB), F32)
        for r in range(0, D, 32):
            value = stream[r : r + 32, cs] - middle
            stream[r : r + 32, cs] = value
            square = square + jnp.sum((value * value).reshape(4, 8, -1), axis=0)
        spread(square, 1, cs)

    vt[...] = nt(eye[...], vec[t]).astype(BF)
    vectors(0)
    wt[0, 0:D, 0:D] = nt(eye[...], w[t, 0:D]).astype(BF)
    tile = first_bias // 16 * 16
    picked = lax.broadcasted_iota(jnp.int32, (16, D), 0) == first_bias - tile
    bias = jnp.where(picked, vec[t, tile : tile + 16].astype(F32), 0.0).astype(BF)
    rest = jnp.concatenate([w[t, D:CAT], bias, jnp.zeros((128 - CODES - 16, D), BF)], 0)
    wt[0, 0:D, D:384] = nt(eye[...], rest).astype(BF)
    mean_rows(0)
    for cs in blocks:
        it = lax.broadcasted_iota(jnp.int32, (CODES, CB), 0)
        xt[t, D:CAT, cs] = (it == ints[t, 0:1, cs]).astype(BF)
        xt[t, CAT : CAT + 16, cs] = jnp.ones((16, CB), BF)
    first = [nn(wt[0, :, 0 : CAT + 16], xt[t, :, cs]) for cs in groups]
    prefetch(1)
    for group, cs in enumerate(groups):
        add(-1, cs, first[group], True)
    for cs in blocks:

        def keep(rs, a):
            stream[rs, cs] = a

        norm_act(stream, cs, gsb.at[0], unit(0), gp.at[t, 0], rstd[row_of(0), cs], keep)
        centre(cs)

    def layer(k, more):
        mixed(k)[D : D + 16, :] = jnp.ones((16, width), BF)
        for group, cs in enumerate(groups):
            out = nn(wt[k % 2, :, 0 : D + 16], mixed(k)[:, cs])
            ahead = group + 1 < len(groups)
            if ahead or more:
                for c in range(per):
                    stage(k if ahead else k + 1, (group + 1) % len(groups) * per + c)
            add(k, cs, out, False)
        if more:
            prefetch(k + 2)

    prefetch(2)
    for c in range(per):
        stage(1, c)

    @pl.loop(1, BLOCKS)
    def _(k):
        if during is not None:
            during(k)
        layer(k, True)

    if before_last is not None:
        before_last()
    layer(BLOCKS, False)
    for cs in blocks:
        xt[t + 1, 0:D, cs] = (stream[:, cs] + mean[0:1, cs]).astype(BF)


def backward_tower(t, refs, after_head=None, during=None, before_product=None, after_weights=None):
    (eye, w, wh, vec, wht, vt, gsb, xt, mix, xh, gp, rstd, ds, ex, br, dm, acc, lg, dl, ints, rw, gw, gh, gv, ig, width) = refs
    blocks = [slice(c, c + CB) for c in range(0, width, CB)]
    last = len(blocks) - 1
    mixed, unit = saved_views(t, mix, xh)
    vt[...] = nt(eye[...], vec[t]).astype(BF)
    for h in range(0, HPAD, D):
        wht[h : h + D, :] = nt(eye[...], wh[t, :, h : h + D]).astype(BF)

    def softmax_block(c):
        cs = pl.ds(pl.multiple_of(c * CB, CB), CB)
        lg[...] = nn(wht[...], xt[t + 1, 0:D, cs])
        return cs

    def states_block(c):
        cs = pl.ds(pl.multiple_of(c * CB, CB), CB)
        return cs, nn(wh[t], dl[:, cs])

    def keep_states(cs, product):
        value = product + ex[:, cs]
        ds[:, cs] = value
        br[BLOCKS % 2, :, cs] = value.astype(BF)

    cs = softmax_block(0)
    head_stage(cs, lg, dl, ints[t, :, cs], rw[0:1, cs])

    @pl.loop(1, width // CB)
    def _(c):
        cs = softmax_block(c)
        before, product = states_block(c - 1)
        head_stage(cs, lg, dl, ints[t, :, cs], rw[0:1, cs])
        keep_states(before, product)

    keep_states(*states_block(width // CB - 1))
    for h in range(0, HPAD, D):
        gh[t, :, h : h + D] = nt(xt[t + 1, 0:D, :], dl[h : h + D]).astype(BF)
    if after_head is not None:
        after_head()
    acc[...] = jnp.zeros(acc.shape, F32)
    ones = jnp.ones((16, 128), BF)

    def part(c):
        return dm.at[c * D : c * D + D]

    def gains(k):
        gsb[k % 2, :, 0:128] = broadcast_vectors(vt[...], (k,)) * ZETA

    def row_sums(k):
        for kind in range(2):
            gv[t, kind, pl.ds(k, 1), :] = nt(ones, acc[k % 2, kind].astype(BF))[0:1] * ZETA
        acc[k % 2] = jnp.zeros(acc.shape[1:], F32)

    def product(k, c):
        row = pl.multiple_of(CAT + (k - 1) * D, 32)
        part(c)[...] = nn(w[t, pl.ds(row, D)], br[k % 2, :, blocks[c]])

    def slopes(k, c):
        cs, grad, sums = blocks[c], part(c), acc.at[k % 2]
        s1 = jnp.zeros((8, CB), F32)
        s2 = jnp.zeros((8, CB), F32)
        for r in range(0, D, 32):
            rs = slice(r, r + 32)
            g = wide(gsb[k % 2, rs, 0:128], cs)
            dy = grad[rs, :] * gp[t, k, rs, cs].astype(F32)
            prod = dy * unit(k)[rs, cs].astype(F32)
            back = dy * g
            grad[rs, :] = back
            s1 = s1 + jnp.sum(back.reshape(4, 8, CB), axis=0)
            s2 = s2 + jnp.sum((prod * g).reshape(4, 8, CB), axis=0)
            sums[0, rs] = sums[0, rs] + (prod[:, 0:128] + prod[:, 128:CB])
            sums[1, rs] = sums[1, rs] + (dy[:, 0:128] + dy[:, 128:CB])
        return [jnp.sum(s, axis=0, keepdims=True) * (1.0 / D) for s in (s1, s2)]

    def stage(k, c, first):
        cs = blocks[c]
        means = slopes(k, c)
        scale = rstd[pl.ds(t * (BLOCKS + 1) + k, 1), cs]
        m1, m2 = (jnp.broadcast_to(m * scale, (32, CB)).astype(BF) for m in means)
        for r in range(0, D, 32):
            rs = slice(r, r + 32)
            back = part(c)[rs, :] * scale - (m1 + unit(k)[rs, cs] * m2).astype(F32)
            if first:
                br[0, rs, cs] = back.astype(BF)
            else:
                value = ds[rs, cs] + back
                ds[rs, cs] = value
                br[(k + 1) % 2, rs, cs] = value.astype(BF)

    if before_product is not None:
        before_product()
    gains(BLOCKS)
    gains(BLOCKS - 1)
    product(BLOCKS, 0)

    @pl.loop(0, BLOCKS)
    def _(i):
        k = BLOCKS - i
        if during is not None:
            during(i)
        for c in range(last + 1):
            if c < last:
                product(k, c + 1)
            stage(k, c, False)
            if c == 0:
                full = nt(mixed(k)[...], br[k % 2])
                row = pl.multiple_of(CAT + (k - 1) * D, 32)
                gw[t, pl.ds(row, D), :] = full[0:D].astype(BF)
                gv[t, 2, pl.ds(k, 1), :] = full[D : D + 1]
                product(k - 1, 0)
        gains(k - 2)
        row_sums(k)

    for c, cs in enumerate(blocks):
        part(c)[...] = ds[:, cs]
        stage(0, c, True)
    full = nt(xt[t], br[0])
    gw[t, 0:CAT, :] = full[0:CAT].astype(BF)
    gv[t, 2, 0:1, :] = full[CAT : CAT + 1]
    row_sums(0)
    if after_weights is not None:
        after_weights()
    for cs in blocks:
        back = nn(w[t, 0:D], br[0, :, cs])
        ex[:, cs] = back
        ig[cs, :] = back.T


def compute_kernel(x_ref, ints, rw, w, wh, vec, st, ig, gw, gh, gv, eye, wt, wht, vt, gsb, xt, mix, xh, gp, rstd, mean, stream, ex, br, dm, acc, lg, dl):
    width = x_ref.shape[0]
    eye[...] = identity(D)
    for c in range(0, width, CB):
        cs = slice(c, c + CB)
        xt[0, 0:D, cs] = nt(eye[...], x_ref[cs, :]).astype(BF)
    fwd = (eye, w, wh, vec, wt, vt, gsb, xt, mix, xh, gp, rstd, stream, mean, ints, width)
    @pl.loop(0, 2)
    def _(t):
        forward_tower(t, fwd)

        @pl.loop(0, width // CB)
        def _(c):
            cs = pl.ds(pl.multiple_of(c * CB, CB), CB)
            st[t, cs, :] = nt(eye[...], xt[t + 1, 0:D, cs]).astype(BF)

    ex[...] = jnp.zeros_like(ex)

    @pl.loop(0, 2)
    def _(i):
        t = 1 - i
        backward_tower(
            t,
            (eye, w, wh, vec, wht, vt, gsb, xt, mix, xh, gp, rstd, stream, ex, br, dm, acc, lg, dl, ints, rw, gw, gh, gv, ig.at[t], width),
        )


def work_scratch(width):
    return [
        pltpu.VMEM((D, D), BF),
        pltpu.VMEM((2, D + 16, 384), BF),
        pltpu.VMEM((HPAD, D), BF),
        pltpu.VMEM((D, 128), BF),
        pltpu.VMEM((2, D, 256), F32),
        pltpu.VMEM((3, CAT + 16, width), BF),
        pltpu.VMEM((2 * BLOCKS * (D + 16), width), BF),
        pltpu.VMEM((2 * (BLOCKS + 1) * D, width), BF),
        pltpu.VMEM((2, BLOCKS + 1, D, width), BF),
        pltpu.VMEM((24, width), F32),
        pltpu.VMEM((8, width), F32),
        pltpu.VMEM((D, width), F32),
        pltpu.VMEM((D, width), F32),
        pltpu.VMEM((2, D, width), BF),
        pltpu.VMEM((width // CB * D, CB), F32),
        pltpu.VMEM((2, 2, D, 128), F32),
        pltpu.VMEM((HPAD, CB), F32),
        pltpu.VMEM((HPAD, width), BF),
    ]


def compute(x, ints, rw, w, wh, vec):
    width = x.shape[0]
    vm = pl.BlockSpec(memory_space=pltpu.VMEM)
    return pl.pallas_call(
        compute_kernel,
        out_shape=(
            jax.ShapeDtypeStruct((2, width, D), BF),
            jax.ShapeDtypeStruct((2, width, D), F32),
            jax.ShapeDtypeStruct((2, A_ROWS, D), BF),
            jax.ShapeDtypeStruct((2, D, HPAD), BF),
            jax.ShapeDtypeStruct((2, 3, 16, D), F32),
        ),
        in_specs=[vm] * 6,
        out_specs=(vm,) * 5,
        scratch_shapes=work_scratch(width),
        compiler_params=pltpu.CompilerParams(vmem_limit_bytes=62 * 1024 * 1024),
    )(x, ints, rw, w, wh, vec)


class Plan:
    def __init__(self, n, length):
        self.n, self.length = n, length
        self.rows128 = -(-length // 128)
        block_end, head_end = A_ROWS * D, A_ROWS * D + D * HEADS
        self.a_base, self.a_rows, self.h_first, self.h_rows, self.h_off, self.v_first, self.v_rows, self.v_off = ([] for _ in range(8))
        used = 0
        for i in range(n):
            lo, hi = i * length, (i + 1) * length
            base = min(lo, block_end) // D // 16 * 16
            top = -(-min(hi, block_end) // D)
            a_rows = -(-(top - base) // 16) * 16 if lo < block_end else 0
            first = min(max(lo - block_end, 0), D * HEADS) // HEADS
            last = -(-min(max(hi - block_end, 0), D * HEADS) // HEADS)
            h_rows = last - first if hi > block_end and lo < head_end else 0
            v_first = max(lo - head_end, 0) // D
            v_rows = -(-(hi - head_end) // D) - v_first if hi > head_end else 0
            self.a_base.append(base)
            self.a_rows.append(a_rows)
            self.h_first.append(first)
            self.h_rows.append(h_rows)
            self.h_off.append(a_rows)
            self.v_first.append(v_first)
            self.v_rows.append(v_rows)
            self.v_off.append(a_rows + 5 * h_rows)
            used = max(used, a_rows + 5 * h_rows + v_rows)
        self.heads = max(self.h_rows)
        self.image = (HEADS * self.heads // 128 + 24) // 8 * 8
        self.slot = -(-(used + 1) // 32) * 32

    def at(self, table, me):
        value = jnp.int32(table[0])
        for i in range(1, self.n):
            if table[i] != table[i - 1]:
                value = value + (me >= i).astype(jnp.int32) * (table[i] - table[i - 1])
        return value


MESH = pl.DeviceIdType.MESH


def neighbours(n):
    core = lax.axis_index("tower")
    me = lax.axis_index("dp")
    near_x = me + 1 - 2 * (me % 2)
    near_y = me + 2 - 4 * ((me // 2) % 2)
    return core, me, near_x, near_y


def at(core, index):
    return {"tower": core, "dp": index}


def greet(core, me, near_x, near_y, n, crossed=False):
    barrier = pltpu.get_barrier_semaphore()
    pl.semaphore_signal(barrier, inc=1, device_id=at(1 - core, me), device_id_type=MESH)
    for near in (near_x, near_y, near_x + near_y - me):
        pl.semaphore_signal(barrier, inc=1, device_id=at(core, near), device_id_type=MESH)
    for k in range(1, n // 4):
        pl.semaphore_signal(barrier, inc=1, device_id=at(core, (me + 4 * k) % n), device_id_type=MESH)
    for near in [near_x, near_y] + [(me + 4 * k) % n for k in range(1, n // 4)] if crossed else []:
        pl.semaphore_signal(barrier, inc=1, device_id=at(1 - core, near), device_id_type=MESH)
    return barrier


def place_shard(plan, me, p_ref, slot128, shifted, rolled):
    rows = plan.rows128
    start = me * plan.length
    shift = start % 128
    first = start // 128
    tall = shifted.shape[0]
    height = p_ref.shape[0]
    lane = lax.broadcasted_iota(jnp.int32, (height, 128), 1)
    rolled[0:8] = jnp.zeros((8, 128), F32)
    rolled[8 : 8 + height] = pltpu.roll(p_ref[...], shift, 1)
    shifted[...] = jnp.zeros((tall, 128), F32)
    moved = jnp.where(lane >= shift, rolled[8 : 8 + height], rolled[7 : 7 + height])
    shifted[16 : 16 + height] = moved
    slot128[...] = jnp.zeros(slot128.shape, F32)
    row = lax.broadcasted_iota(jnp.int32, (height, 128), 0)
    base = plan.at(plan.a_base, me)

    @pl.when(plan.at(plan.a_rows, me) > 0)
    def _():
        slot128[pl.ds(first - 2 * base, height)] = jnp.where(row + first < 2 * A_ROWS, moved, 0.0)

    v_start = (A_ROWS * D + D * HEADS) // 128
    v_rows, v_off, v_first = (plan.at(t, me) for t in (plan.v_rows, plan.v_off, plan.v_first))
    tall_v = min(height, -(-2 * max(plan.v_rows) // 8) * 8)

    @pl.when(v_rows > 0)
    def _():
        inside = plan.at([max(0, v_start - i * plan.length // 128) for i in range(plan.n)], me)
        to = 2 * v_off + first + inside - v_start - 2 * v_first
        slot128[pl.ds(to, tall_v)] = shifted[pl.ds(16 + inside, tall_v)]

    h_first, h_rows, h_off = (plan.at(t, me) for t in (plan.h_first, plan.h_rows, plan.h_off))

    @pl.when(h_rows > 0)
    def _():
        tall_h = plan.image
        begin = A_ROWS * D + HEADS * h_first - 128 * first + 128 * 16
        turn = begin % 128
        rolled[0:tall_h] = pltpu.roll(shifted[pl.ds(begin // 128, tall_h)], (128 - turn) % 128, 1)
        rolled[tall_h : tall_h + 8] = jnp.zeros((8, 128), F32)
        lane = lax.broadcasted_iota(jnp.int32, (tall_h, 128), 1)
        shifted[0:tall_h] = jnp.where(lane < 128 - turn, rolled[0:tall_h], rolled[1 : tall_h + 1])
        to = slot128.at[pl.ds(pl.multiple_of(2 * h_off, 8), 10 * plan.heads)]
        it = lax.broadcasted_iota(jnp.int32, (10, 128), 0)
        lane = lax.broadcasted_iota(jnp.int32, (10, 128), 1)
        for k in range(plan.heads):
            row, turn = HEADS * k // 128, HEADS * k % 128
            window = pltpu.roll(shifted[row : row + 16], (128 - turn) % 128, 1)
            value = jnp.where(lane < 128 - turn, window[0:10], window[1:11])
            kept = (it * 128 + lane < HEADS) & (k < h_rows)
            to[10 * k : 10 * k + 10] = to[10 * k : 10 * k + 10] + jnp.where(kept, value, 0.0)


def unpack_rows(plan, i, slot, w, heads, vectors, scratch):
    base, rows = plan.a_base[i], plan.a_rows[i]
    if rows:
        shared = i > 0 and base < plan.a_base[i - 1] + plan.a_rows[i - 1]
        lo = 0
        if shared:
            w[base : base + 16] = w[base : base + 16] + slot[0:16]
            lo = 16
        if rows > lo:
            w[base + lo : base + rows] = slot[lo:rows]
    h_rows, h_off, h_first = plan.h_rows[i], plan.h_off[i], plan.h_first[i]
    v_rows, v_off, v_first = plan.v_rows[i], plan.v_off[i], plan.v_first[i]
    if h_rows or v_rows:
        value = slot.astype(F32)
        scratch[0][...] = value[:, 0:128]
        scratch[1][...] = value[:, 128:D]
    if h_rows:
        shared = i > 0 and plan.h_rows[i - 1] and plan.h_first[i - 1] + plan.h_rows[i - 1] > h_first
        for j in range(5):
            for half in range(2):
                cols = slice(128 * half, 128 * half + 128)
                first = D * j + h_first
                value = scratch[half][pl.ds(h_off + j, h_rows, stride=5)]
                if shared:
                    heads[first : first + 1, cols] = heads[first : first + 1, cols] + value[0:1]
                    if h_rows > 1:
                        heads[first + 1 : first + h_rows, cols] = value[1:h_rows]
                else:
                    heads[first : first + h_rows, cols] = value
    if v_rows:
        shared = v_first and plan.v_first[i - 1] + plan.v_rows[i - 1] > v_first
        shared = shared or (i > 0 and plan.v_rows[i - 1] > 0 and v_first == 0)
        for half in range(2):
            cols = slice(128 * half, 128 * half + 128)
            value = scratch[half][v_off : v_off + v_rows]
            if shared:
                vectors[v_first : v_first + 1, cols] = vectors[v_first : v_first + 1, cols] + value[0:1]
                if v_rows > 1:
                    vectors[v_first + 1 : v_first + v_rows, cols] = value[1:v_rows]
            else:
                vectors[v_first : v_first + v_rows, cols] = value


def split3(value):
    hi = value.astype(BF).astype(F32)
    mid = (value - hi).astype(BF).astype(F32)
    return hi, mid, value - hi - mid


def gather_kernel(plan, p_ref, ints_ref, imp_ref, w, wh, vec, both, rw, slots, slot128, shifted, rolled, scratch, whf, vecf, send, recv):
    n = plan.n
    depth = n // 4
    core, me, near_x, near_y = neighbours(n)
    barrier = greet(core, me, near_x, near_y, n)
    place_shard(plan, me, p_ref, slot128, shifted, rolled)
    pl.semaphore_wait(barrier, depth + 3)
    half = rw.shape[1]
    started = []

    def copy(src, dst, slot, to):
        c = pltpu.make_async_remote_copy(
            src_ref=src, dst_ref=dst, send_sem=send.at[slot], recv_sem=recv.at[slot], device_id=to, device_id_type=MESH
        )
        c.start()
        started.append(c)
        return c

    mine = pl.multiple_of(core * half, half)
    theirs = pl.multiple_of((1 - core) * half, half)
    number = iter(range(1 << 20))
    ints_copy = copy(ints_ref.at[:, pl.ds(theirs, half)], both.at[core], next(number), at(1 - core, me))
    rows = plan.slot
    total = jnp.sum(imp_ref[...].astype(F32), axis=1, keepdims=True)
    lane = lax.broadcasted_iota(jnp.int32, (1, D), 1)
    hi, mid, lo = split3(total)
    left = slot128[pl.ds(0, rows, stride=2)]
    right = slot128[pl.ds(1, rows, stride=2)]
    own = jnp.concatenate([left, right], 1)
    last = jnp.where(lane == 0, hi, jnp.where(lane == 1, mid, jnp.where(lane == 2, lo, 0.0)))
    last_row = lax.broadcasted_iota(jnp.int32, (rows, D), 0) == rows - 1
    slots[core, me] = jnp.where(last_row, last, own).astype(BF)

    def column(index, k):
        return (index + n - 4 * k) % n

    def send_slot(origin, to, lo=0, hi=rows):
        ref = slots.at[core, origin, pl.ds(lo, hi - lo)]
        return copy(ref, ref, next(number), to)

    near_xy = near_x + near_y - me
    cut = rows // 2
    z_in, x_in, y_in, d_in, s_in = {}, {}, {}, {}, []
    for k in sorted(range(1, depth), key=lambda k: (min(k, depth - k), k)):
        z_in[k] = send_slot(me, at(core, (me + 4 * k) % n))
    order = [0] + list(z_in)
    for k in order:
        if k:
            z_in[k].wait_recv()
        x_in[k] = send_slot(column(me, k), at(core, near_x))
        y_in[k] = send_slot(column(me, k), at(core, near_y))
        s_in.append(send_slot(column(me, k), at(1 - core, me)))
    for k in order:
        x_in[k].wait_recv()
        first = send_slot(column(near_x, k), at(core, near_y), 0, cut)
        s_in.append(send_slot(column(near_x, k), at(1 - core, me)))
        y_in[k].wait_recv()
        second = send_slot(column(near_y, k), at(core, near_x), cut, rows)
        s_in.append(send_slot(column(near_y, k), at(1 - core, me)))
        d_in[k] = (first, second)
    for k in order:
        for c in d_in[k]:
            c.wait_recv()
        s_in.append(send_slot(column(near_xy, k), at(1 - core, me)))
    ints_copy.wait_recv()
    both[core] = ints_ref[:, pl.ds(mine, half)]
    for c in s_in:
        c.wait_recv()
    for c in started:
        c.wait_send()
    for t in range(2):
        vecf[...] = jnp.zeros(vecf.shape, F32)
        for i in range(n):
            unpack_rows(plan, i, slots[t, i], w.at[t], whf, vecf, [scratch.at[0], scratch.at[1]])
        for j in range(5):
            wh[t, :, D * j : D * j + D] = whf[D * j : D * j + D].astype(BF)
        vec[t] = vecf[...].astype(BF)
    total = jnp.zeros((1, D), F32)
    for i in range(n):
        tail = slots[0, i, rows - 16 : rows].astype(F32)
        total = total + tail[15:16]
    weight_sum = jnp.sum(jnp.where(lane < 3, total, 0.0), axis=1, keepdims=True)
    rw[...] = jnp.broadcast_to(imp_ref[:, pl.ds(mine, half)].astype(F32) / weight_sum, (8, half))


def gather(plan, p128, ints, imp):
    n, rows = plan.n, plan.slot
    half = ints.shape[1] // 2
    vm = pl.BlockSpec(memory_space=pltpu.VMEM)
    height = p128.shape[0]
    tall = max(2 * rows, height + 40) + 80
    copies = 1 + (n // 4 - 1) + 2 * (n // 4) + 2 * (n // 4) + n
    return pl.pallas_call(
        functools.partial(gather_kernel, plan),
        out_shape=(
            jax.ShapeDtypeStruct((2, A_ROWS, D), BF),
            jax.ShapeDtypeStruct((2, D, HPAD), BF),
            jax.ShapeDtypeStruct((2, 128, D), BF),
            jax.ShapeDtypeStruct((2, 8, half), jnp.int32),
            jax.ShapeDtypeStruct((8, half), F32),
        ),
        in_specs=[vm] * 3,
        out_specs=(vm,) * 5,
        scratch_shapes=[
            pltpu.VMEM((2, n, rows, D), BF),
            pltpu.VMEM((tall, 128), F32),
            pltpu.VMEM((height + 128, 128), F32),
            pltpu.VMEM((height + 40, 128), F32),
            pltpu.VMEM((2, rows, 128), F32),
            pltpu.VMEM((HPAD, D), F32),
            pltpu.VMEM((128, D), F32),
            pltpu.SemaphoreType.DMA((copies,)),
            pltpu.SemaphoreType.DMA((copies,)),
        ],
        compiler_params=pltpu.CompilerParams(
            collective_id=0, has_side_effects=True, vmem_limit_bytes=48 * 1024 * 1024
        ),
    )(p128, ints, imp)


def chunks(height):
    step = max(c for c in range(8, 113, 8) if height % c == 0)
    return [(lo, lo + step) for lo in range(0, height, step)]


def lay_flat(plan, me, slot128, flat, rolled):
    height = rolled.shape[0] - 40
    start = me * plan.length
    shift = start % 128
    first = start // 128
    base = plan.at(plan.a_base, me)
    row = lax.broadcasted_iota(jnp.int32, (height + 8, 128), 0)
    flat[...] = jnp.zeros(flat.shape, F32)

    @pl.when(plan.at(plan.a_rows, me) > 0)
    def _():
        rows = slot128[pl.ds(first - 2 * base, height + 8)]
        flat[16 : 24 + height] = jnp.where(row + first < 2 * A_ROWS, rows, 0.0)

    v_start = (A_ROWS * D + D * HEADS) // 128
    v_rows, v_off, v_first = (plan.at(t, me) for t in (plan.v_rows, plan.v_off, plan.v_first))
    tall_v = min(height, -(-2 * max(plan.v_rows) // 8) * 8)

    @pl.when(v_rows > 0)
    def _():
        inside = plan.at([max(0, v_start - i * plan.length // 128) for i in range(plan.n)], me)
        source = 2 * v_off + first + inside - v_start - 2 * v_first
        to = pl.ds(16 + inside, tall_v)
        flat[to] = flat[to] + slot128[pl.ds(source, tall_v)]

    h_first, h_rows, h_off = (plan.at(t, me) for t in (plan.h_first, plan.h_rows, plan.h_off))

    @pl.when(h_rows > 0)
    def _():
        tall_h = plan.image
        source = slot128.at[pl.ds(pl.multiple_of(2 * h_off, 8), 10 * plan.heads + 6)]
        it = lax.broadcasted_iota(jnp.int32, (16, 128), 0)
        lane = lax.broadcasted_iota(jnp.int32, (16, 128), 1)
        rolled[0 : tall_h + 8] = jnp.zeros((tall_h + 8, 128), F32)
        for k in range(plan.heads):
            row, turn = HEADS * k // 128, HEADS * k % 128
            kept = (it * 128 + lane < HEADS) & (k < h_rows)
            value = pltpu.roll(jnp.where(kept, source[10 * k : 10 * k + 16], 0.0), turn, 1)
            above = jnp.concatenate([jnp.zeros((8, 128), F32), value], 0)[7:23]
            rolled[row : row + 16] = rolled[row : row + 16] + jnp.where(lane >= turn, value, above)
        begin = A_ROWS * D + HEADS * h_first - 128 * first + 128 * 16
        turn = begin % 128
        slot128[0:8] = jnp.zeros((8, 128), F32)
        slot128[8 : 8 + tall_h] = pltpu.roll(rolled[0:tall_h], turn, 1)
        lane = lax.broadcasted_iota(jnp.int32, (tall_h, 128), 1)
        moved = jnp.where(lane >= turn, slot128[8 : 8 + tall_h], slot128[7 : 7 + tall_h])
        to = pl.ds(begin // 128, tall_h)
        flat[to] = flat[to] + moved

    rolled[0 : height + 8] = pltpu.roll(flat[16 : 24 + height], (128 - shift) % 128, 1)
    for lo, hi in chunks(height):
        lane = lax.broadcasted_iota(jnp.int32, (hi - lo, 128), 1)
        flat[lo:hi] = jnp.where(lane < 128 - shift, rolled[lo:hi], rolled[lo + 1 : hi + 1])


def pack_slots(plan, core, gw, gh, gv, rgw, rgh, rgv, slots, sums, vsum, scratch):
    total = gv[core].astype(F32) + rgv[...]
    for kind in range(3):
        vsum[kind * (BLOCKS + 1) : (kind + 1) * (BLOCKS + 1)] = total[kind, 0 : BLOCKS + 1]
    sums[...] = gh[core].astype(F32) + rgh[...].astype(F32)
    for i in range(plan.n):
        base, rows = plan.a_base[i], plan.a_rows[i]
        h_rows, h_off, h_first = plan.h_rows[i], plan.h_off[i], plan.h_first[i]
        v_rows, v_off, v_first = plan.v_rows[i], plan.v_off[i], plan.v_first[i]
        slots[i, rows : plan.slot] = jnp.zeros((plan.slot - rows, D), BF)
        if rows:
            added = gw[core, base : base + rows].astype(F32) + rgw[base : base + rows].astype(F32)
            slots[i, 0:rows] = added.astype(BF)
        if h_rows or v_rows:
            scratch[...] = jnp.zeros(scratch.shape, F32)
            for half in range(2):
                for j in range(5 if h_rows else 0):
                    cols = slice(D * j + 128 * half, D * j + 128 * half + 128)
                    scratch[half, pl.ds(h_off + j, h_rows, stride=5)] = sums[h_first : h_first + h_rows, cols]
                if v_rows:
                    scratch[half, v_off : v_off + v_rows] = vsum[v_first : v_first + v_rows, 128 * half : 128 * half + 128]
            whole = jnp.concatenate([scratch[0], scratch[1]], 1)
            slots[i, rows : plan.slot] = whole[rows:].astype(BF)


def segment_bounds():
    first = [0] + [(CAT + j * D) * D for j in range(BLOCKS + 1)]
    return list(zip(first, first[1:] + [A_ROWS * D + D * HEADS]))


class Rows:
    def __init__(self, ref):
        self.ref, self.height = ref, ref.shape[0]

    def chunks(self):
        return chunks(self.height)

    def get(self, lo, hi):
        return self.ref[lo:hi]

    def put(self, lo, hi, value):
        self.ref[lo:hi] = value


class Flat:
    def __init__(self, ref, buffer):
        self.ref, self.buffer, self.length = ref, buffer, ref.shape[1]
        self.whole = self.length // 1024 * 8
        self.height = -(-self.length // 1024) * 8

    def chunks(self):
        step = next(s for s in range(64, 0, -8) if self.whole % s == 0)
        return [(lo, lo + step) for lo in range(0, self.whole, step)] + [(self.whole, self.height)]

    def ends(self):
        rows = (self.length - 128 * self.whole) // 128
        return rows, self.length % 128, 128 * self.whole, 128 * (self.whole + rows)

    def get(self, lo, hi):
        if hi <= self.whole:
            return self.ref[0:1, 128 * lo : 128 * hi].reshape(hi - lo, 128)
        rows, lanes, first, last = self.ends()
        self.buffer[...] = jnp.zeros((8, 128), F32)
        if rows:
            self.buffer[0:rows] = self.ref[0:1, first:last].reshape(rows, 128)
        if lanes:
            self.buffer[rows : rows + 1, 0:lanes] = self.ref[0:1, last : self.length]
        return self.buffer[...]

    def put(self, lo, hi, value):
        if hi <= self.whole:
            self.ref[0:1, 128 * lo : 128 * hi] = value.reshape(1, 128 * (hi - lo))
            return
        rows, lanes, first, last = self.ends()
        if rows:
            self.ref[0:1, first:last] = value[0:rows].reshape(1, 128 * rows)
        if lanes:
            self.ref[0:1, last : self.length] = value[rows : rows + 1, 0:lanes]


def update_shard(plan, me, p_ref, m_ref, v_ref, outs, flat, squares, sq_in, push, to_plane, to_z):
    first_out, second_out, new_out, norm_out = outs
    height = p_ref.height
    start = me * plan.length
    correction = 1.0 - 0.5**STEP
    bounds = segment_bounds()

    def place(lo, hi):
        shape = (hi - lo, 128)
        return 128 * lo + 128 * lax.broadcasted_iota(jnp.int32, shape, 0) + lax.broadcasted_iota(jnp.int32, shape, 1)

    for lo, hi in p_ref.chunks():
        spot = place(lo, hi)
        grad = jnp.where(spot < plan.length, flat[lo:hi], 0.0)
        first_new = 0.5 * m_ref.get(lo, hi) + 0.5 * grad
        second_new = 0.5 * v_ref.get(lo, hi) + 0.5 * grad * grad
        first_out.put(lo, hi, first_new)
        second_out.put(lo, hi, second_new)
        decay = jnp.where(spot < bounds[-1][1] - start, 0.01 * p_ref.get(lo, hi), 0.0)
        update = first_new / correction / (jnp.sqrt(second_new / correction) + 1e-06) + decay
        flat[lo:hi] = jnp.where(spot < plan.length, update, 0.0)
        new_out.put(lo, hi, p_ref.get(lo, hi) - 0.5 * update)
    squares[...] = jnp.zeros(squares.shape, F32)

    def each_segment(body):
        for j, (first, last) in enumerate(bounds):
            pl.when((first < start + plan.length) & (last > start))(lambda j=j, first=first, last=last: body(j, first, last))

    def square_sums(j, first, last):
        weight, change = jnp.zeros((8, 128), F32), jnp.zeros((8, 128), F32)
        for lo, hi in p_ref.chunks():
            spot = place(lo, hi)
            inside = (spot >= first - start) & (spot < last - start)
            p, u = jnp.where(inside, p_ref.get(lo, hi), 0.0), jnp.where(inside, flat[lo:hi], 0.0)
            weight = weight + jnp.sum((p * p).reshape(-1, 8, 128), axis=0)
            change = change + jnp.sum((u * u).reshape(-1, 8, 128), axis=0)
        squares[0, j : j + 1] = jnp.sum(weight, axis=0, keepdims=True)
        squares[0, 16 + j : 17 + j] = jnp.sum(change, axis=0, keepdims=True)

    each_segment(square_sums)
    total = squares[0]
    for hop, targets in enumerate((to_plane, to_z)):
        lands = range(3) if hop == 0 else range(3, 3 + len(to_z))
        for c in [push(squares.at[hop], sq_in.at[k], to) for k, to in zip(lands, targets)]:
            c.wait_recv()
        for k in lands:
            total = total + sq_in[k]
        squares[hop + 1] = total
    norm = jnp.sqrt(jnp.sum(total, axis=1, keepdims=True))
    squares[3] = jnp.broadcast_to(norm, (32, 128))
    line = jnp.sqrt(jnp.sum(jnp.concatenate([total, jnp.zeros((96, 128), F32)], 0).T, axis=0, keepdims=True))
    norm_out[0:1] = line[:, 0:MATS]
    norm_out[1:2] = pltpu.roll(line, 112, 1)[:, 0:MATS]

    def scaled(j, first, last):
        ratio = squares[3, j : j + 1] / squares[3, 16 + j : 17 + j]
        for lo, hi in p_ref.chunks():
            spot = place(lo, hi)
            inside = (spot >= first - start) & (spot < last - start)
            new_out.put(lo, hi, jnp.where(inside, p_ref.get(lo, hi) - 0.5 * ratio * flat[lo:hi], new_out.get(lo, hi)))

    each_segment(scaled)


def reduce_kernel(
    plan, gw, gh, gv, st, ig, p_ref, m_ref, v_ref,
    st_out, ig_out, first_out, second_out, new_out, norm_out,
    rgw, rgh, rgv, slots, sums, vsum, scratch, in_d, in_x, in_y, in_z, slot128, flat, rolled, squares, sq_in,
    send, recv, local,
):
    n, rows = plan.n, plan.slot
    depth, cut = n // 4, plan.slot // 2
    core, me, near_x, near_y = neighbours(n)
    near_xy = near_x + near_y - me
    barrier = greet(core, me, near_x, near_y, n)
    pl.semaphore_wait(barrier, depth + 3)
    half = st.shape[1]
    number = iter(range(1 << 20))
    started = []

    def copy(src, dst, to):
        slot = next(number)
        c = pltpu.make_async_remote_copy(
            src_ref=src, dst_ref=dst, send_sem=send.at[slot], recv_sem=recv.at[slot], device_id=to, device_id_type=MESH
        )
        c.start()
        started.append(c)
        return c

    def column(index, k):
        return (index + n - 4 * k) % n

    sibling = at(1 - core, me)
    early = [
        copy(gw.at[1 - core], rgw, sibling),
        copy(gh.at[1 - core], rgh, sibling),
        copy(gv.at[1 - core], rgv, sibling),
    ]
    mine = pl.ds(pl.multiple_of(core * half, half), half)
    late = [
        copy(st.at[1 - core], st_out.at[mine], sibling),
        copy(ig.at[1 - core], ig_out.at[mine], sibling),
    ]
    stay = [
        pltpu.make_async_copy(st.at[core], st_out.at[mine], local.at[0]),
        pltpu.make_async_copy(ig.at[core], ig_out.at[mine], local.at[1]),
    ]
    for c in stay:
        c.start()
    for c in early:
        c.wait_recv()
    pack_slots(plan, core, gw, gh, gv, rgw, rgh, rgv, slots, sums, vsum, scratch)
    order = list(range(1, depth)) + [0]
    to_x, to_y = at(core, near_x), at(core, near_y)
    halves = {}
    for k in order:
        diagonal = column(near_xy, k)
        halves[k] = (
            copy(slots.at[diagonal, pl.ds(0, cut)], in_d.at[k, pl.ds(0, cut)], to_y),
            copy(slots.at[diagonal, pl.ds(cut, rows - cut)], in_d.at[k, pl.ds(cut, rows - cut)], to_x),
        )
    fulls = {}
    for k in order:
        ox, oy = column(near_x, k), column(near_y, k)
        halves[k][0].wait_recv()
        slots[ox, 0:cut] = (slots[ox, 0:cut].astype(F32) + in_d[k, 0:cut].astype(F32)).astype(BF)
        first = copy(slots.at[ox], in_x.at[k], to_x)
        halves[k][1].wait_recv()
        slots[oy, cut:rows] = (slots[oy, cut:rows].astype(F32) + in_d[k, cut:rows].astype(F32)).astype(BF)
        fulls[k] = (first, copy(slots.at[oy], in_y.at[k], to_y))
    along = {}
    for k in order:
        own = column(me, k)
        for c in fulls[k]:
            c.wait_recv()
        if k:
            total = slots[own].astype(F32) + in_x[k].astype(F32) + in_y[k].astype(F32)
            slots[own] = total.astype(BF)
            along[k] = copy(slots.at[own], in_z.at[k], at(core, own))
    for c in along.values():
        c.wait_recv()
    total = slots[me].astype(F32) + in_x[0].astype(F32) + in_y[0].astype(F32)
    for k in along:
        total = total + in_z[k].astype(F32)
    slot128[...] = jnp.zeros(slot128.shape, F32)
    slot128[pl.ds(0, rows, stride=2)] = total[:, 0:128]
    slot128[pl.ds(1, rows, stride=2)] = total[:, 128:D]
    lay_flat(plan, me, slot128, flat, rolled)

    to_z = [at(core, column(me, k)) for k in range(1, depth)]
    outs = (Rows(first_out), Rows(second_out), Rows(new_out), norm_out)
    to_plane = [to_x, to_y, at(core, near_xy)]
    update_shard(plan, me, Rows(p_ref), Rows(m_ref), Rows(v_ref), outs, flat, squares, sq_in, copy, to_plane, to_z)
    for c in late:
        c.wait_recv()
    for c in stay:
        c.wait()
    for c in started:
        c.wait_send()


def reduce_and_update(plan, gw, gh, gv, st, ig, p128, m128, v128):
    n, rows = plan.n, plan.slot
    depth = n // 4
    half = st.shape[1]
    height = p128.shape[0]
    vm = pl.BlockSpec(memory_space=pltpu.VMEM)
    hbm = pl.BlockSpec(memory_space=pl.ANY)
    copies = 5 + 2 * depth + 2 * depth + (depth - 1) + (depth - 1) + 3
    flat32 = jax.ShapeDtypeStruct((height, 128), F32)
    return pl.pallas_call(
        functools.partial(reduce_kernel, plan),
        out_shape=(
            jax.ShapeDtypeStruct((2 * half, D), BF),
            jax.ShapeDtypeStruct((2 * half, D), F32),
            flat32,
            flat32,
            flat32,
            jax.ShapeDtypeStruct((2, MATS), F32),
        ),
        in_specs=[vm] * 3 + [hbm] * 2 + [vm] * 3,
        out_specs=(hbm, hbm, vm, vm, vm, vm),
        scratch_shapes=[
            pltpu.VMEM((A_ROWS, D), BF),
            pltpu.VMEM((D, HPAD), BF),
            pltpu.VMEM(gv.shape[1:], F32),
            pltpu.VMEM((n, rows, D), BF),
            pltpu.VMEM((D, HPAD), F32),
            pltpu.VMEM((40, D), F32),
            pltpu.VMEM((2, rows, 128), F32),
            pltpu.VMEM((depth, rows, D), BF),
            pltpu.VMEM((depth, rows, D), BF),
            pltpu.VMEM((depth, rows, D), BF),
            pltpu.VMEM((depth, rows, D), BF),
            pltpu.VMEM((max(2 * rows, height + 48) + 80, 128), F32),
            pltpu.VMEM((height + 128, 128), F32),
            pltpu.VMEM((height + 40, 128), F32),
            pltpu.VMEM((4, 32, 128), F32),
            pltpu.VMEM((2 + depth, 32, 128), F32),
            pltpu.SemaphoreType.DMA((copies,)),
            pltpu.SemaphoreType.DMA((copies,)),
            pltpu.SemaphoreType.DMA((2,)),
        ],
        compiler_params=pltpu.CompilerParams(
            collective_id=1, has_side_effects=True, vmem_limit_bytes=48 * 1024 * 1024
        ),
    )(gw, gh, gv, st, ig, p128, m128, v128)


class Copies:
    def __init__(self, send, recv):
        self.send, self.recv, self.made, self.sent = send, recv, [], set()

    def add(self, src, dst, to, recv_slot=None, only=None):
        self.made.append((src, dst, to, recv_slot, only))
        return len(self.made) - 1

    def get(self, number):
        src, dst, to, recv_slot, _ = self.made[number]
        return pltpu.make_async_remote_copy(
            src_ref=src(), dst_ref=dst(), send_sem=self.send.at[number],
            recv_sem=self.recv.at[number] if recv_slot is None else recv_slot(),
            device_id=to(), device_id_type=MESH,
        )

    def start(self, *numbers):
        for number in numbers:
            self.get(number).start()

    def arrive(self, *numbers):
        for number in numbers:
            self.get(number).wait_recv()

    def leave(self, *numbers):
        for number in numbers:
            only = self.made[number][4]
            if number not in self.sent and only is None:
                self.get(number).wait_send()
            elif number not in self.sent:
                pl.when(only())(lambda number=number: self.get(number).wait_send())
            self.sent.add(number)


def fused_fits(plan):
    depth, half = plan.n // 4, plan.slot // 2
    plain = [b + plan.slot <= A_ROWS for b, h, v in zip(plan.a_base, plan.h_rows, plan.v_rows) if not (h or v)]
    vectors = [rows for rows in plan.v_rows if rows]
    return (
        all(plain)
        and vectors == [3 * (BLOCKS + 1)]
        and plan.n % 4 == 0
        and half >= 32
        and 4 * half <= HPAD
        and 2 * depth * plan.slot <= (BLOCKS + 1) * D
        and depth == 4
        and max(plan.a_rows) <= plan.slot
    )


def train_kernel(
    plan, x_ref, codes_ref, targets_ref, visits_ref, imp_ref, p_ref, m_ref, v_ref,
    st_out, ig_out, first_out, second_out, new_out, norm_out,
    w, wh, vec, both, away, rw, eye, wt, wht, vt, gsb, xt, mix, xh, gp, rstd, mean, stream, ex, br, dm, acc, lg, dl,
    gw, gh, gv, packed, st_stage, slot128, flat, rolled, vsum, vacc, vin, owned, squares, sq_in, tail,
    send, recv, z_recv, own_recv, local, ready,
):
    n, rows = plan.n, plan.slot
    depth, hrows = n // 4, plan.slot // 2
    cut = hrows // 32 * 16
    core, me, near_x, near_y = neighbours(n)
    near_xy = near_x + near_y - me
    width = both.shape[2]
    params_in, first_new, second_new, new = (Flat(ref, tail) for ref in (p_ref, first_out, second_out, new_out))
    moments = [
        pltpu.make_async_copy(src, dst, local.at[3 + i])
        for i, (src, dst) in enumerate(((m_ref, first_out), (v_ref, second_out)))
    ]
    z_me, j_me = me // 4, me % 4
    copies = Copies(send, recv)
    scratch = [slot128.at[0:rows], slot128.at[rows : 2 * rows]]
    barrier = greet(core, me, near_x, near_y, n, True)
    mine = pl.multiple_of(core * width, width)
    theirs = pl.multiple_of((1 - core) * width, width)
    x_copy = pltpu.make_async_copy(x_ref.at[pl.ds(mine, width)], st_stage.at[0], local.at[0])
    x_copy.start()
    for c in moments:
        c.start()
    for to, half in ((both.at[core], mine), (away, theirs)):
        cols = pl.ds(half, width)
        to[0:1] = codes_ref[:, cols]
        to[1:2] = targets_ref[0, :, cols]
        to[2:6] = visits_ref[:, cols]
        to[6:7] = targets_ref[1, :, cols]
        to[7:8] = targets_ref[2, :, cols]
    height = params_in.height
    for lo, hi in params_in.chunks():
        slot128[lo:hi] = params_in.get(lo, hi)
    place_shard(plan, me, slot128.at[0:height], slot128, flat, rolled)

    spare = (BLOCKS + 1) * D

    def slot_part(t, i, lo, count):
        row = pl.multiple_of(spare + rows * (t * depth + i // 4) + lo, 16)
        return xh.at[pl.ds(row, count), pl.ds(pl.multiple_of((i % 4) * D, D), D)]

    def column(index, k):
        return (index + n - 4 * k) % n

    def sibling():
        return at(1 - core, me)

    def same(make, to):
        return copies.add(make, make, to)

    low = core * hrows
    other_low = (1 - core) * hrows
    order = [0] + sorted(range(1, depth), key=lambda k: (min(k, depth - k), k))
    to_x, to_y, to_d = (lambda: at(core, near_x)), (lambda: at(core, near_y)), (lambda: at(core, near_xy))
    swap_ints = copies.add(lambda: away, lambda: both.at[core], sibling)

    def arrival(t, number):
        return own_recv.at[t * (depth + 2) + number]

    own_targets = [(lambda: near_x), (lambda: near_y)] + [lambda k=k: (me + 4 * k) % n for k in order[1:]]
    own_sends = [copies.add(lambda: slot_part(core, me, 0, rows), lambda: slot_part(core, me, 0, rows), sibling, lambda: arrival(core, 0))]
    for number, target in enumerate(own_targets, 1):
        for h in range(2):
            make = lambda h=h: slot_part(core, me, h * hrows, hrows)
            own_sends.append(
                copies.add(make, make, lambda h=h, target=target: at(h, target()), lambda number=number: arrival(core, number))
            )
    own_sends = own_sends[3 + 2 :] + own_sends[1:5] + own_sends[:1]

    def own_arrive(t, number, make):
        pltpu.make_async_remote_copy(
            src_ref=make(), dst_ref=make(), send_sem=send.at[0], recv_sem=arrival(t, number), device_id=sibling(), device_id_type=MESH
        ).wait_recv()

    gathers = []
    for t in range(2):
        g = {}
        for k in order:
            if k:
                g["x", k] = same(lambda t=t, k=k: slot_part(t, column(me, k), low, hrows), to_x)
                g["y", k] = same(lambda t=t, k=k: slot_part(t, column(me, k), low, hrows), to_y)
            g["d", k] = (
                same(lambda t=t, k=k: slot_part(t, column(near_x, k), low, cut), to_y),
                same(lambda t=t, k=k: slot_part(t, column(near_y, k), low + cut, hrows - cut), to_x),
            )
            g["s", k] = [
                same(lambda t=t, k=k, index=index: slot_part(t, column(index, k), low, hrows), sibling) if index is not me or k else None
                for index in (me, near_x, near_y, near_xy)
            ]
        gathers.append(g)

    def gather_0(t):
        pl.when(core == t)(lambda: copies.start(*own_sends))

    def gather_1(t):
        g = gathers[t]
        for number, k in enumerate(order[1:], 3):
            own_arrive(t, number, lambda: slot_part(t, me, low, hrows))
            copies.start(g["x", k], g["y", k], g["s", k][0])

    def gather_2(t):
        g = gathers[t]
        for k in order:
            if k:
                copies.arrive(g["x", k])
            else:
                own_arrive(t, 1, lambda: slot_part(t, me, low, hrows))
            copies.start(g["d", k][0], g["s", k][1])
            if k:
                copies.arrive(g["y", k])
            else:
                own_arrive(t, 2, lambda: slot_part(t, me, low, hrows))
            copies.start(g["d", k][1], g["s", k][2])

    def gather_3(t):
        g = gathers[t]
        for k in order:
            copies.arrive(*g["d", k])
            copies.start(g["s", k][3])

    def gather_4(t):
        g = gathers[t]
        pl.when(core != t)(lambda: own_arrive(t, 0, lambda: slot_part(t, me, 0, rows)))
        for k in order:
            copies.arrive(*(c for c in g["s", k] if c is not None))

    def unpack(t):
        lg[4 * D : 5 * D, 128:D] = jnp.zeros((D, 128), F32)
        vsum[...] = jnp.zeros(vsum.shape, F32)
        for i in range(n):
            row, lane = spare + rows * (t * depth + i // 4), (i % 4) * D
            unpack_rows(plan, i, xh[row : row + rows, lane : lane + D], w.at[t], lg, vsum, scratch)
        for j in range(5):
            wh[t, :, D * j : D * j + D] = lg[D * j : D * j + D].astype(BF)
        vec[t] = vsum[...].astype(BF)

    total = jnp.sum(imp_ref[...].astype(F32), axis=1, keepdims=True)
    lane_d = lax.broadcasted_iota(jnp.int32, (1, D), 1)
    hi, mid, lo = split3(total)
    left = slot128[pl.ds(0, rows, stride=2)]
    right = slot128[pl.ds(1, rows, stride=2)]
    own = jnp.concatenate([left, right], 1)
    last = jnp.where(lane_d == 0, hi, jnp.where(lane_d == 1, mid, jnp.where(lane_d == 2, lo, 0.0)))
    last_row = lax.broadcasted_iota(jnp.int32, (rows, D), 0) == rows - 1
    slot_part(core, me, 0, rows)[...] = jnp.where(last_row, last, own).astype(BF)
    pl.semaphore_wait(barrier, depth + 3 + 2 + depth - 1)
    gather_0(0)
    copies.start(swap_ints)
    eye[...] = identity(D)
    x_copy.wait()
    for c in range(0, width, CB):
        xt[0, 0:D, c : c + CB] = nt(eye[...], st_stage[0, c : c + CB, :]).astype(BF)
    gather_1(0)
    gather_0(1)
    gather_2(0)
    gather_3(0)
    copies.arrive(swap_ints)
    gather_4(0)
    unpack(0)
    total = jnp.zeros((1, D), F32)
    for i in range(n):
        row, lane = spare + rows * (i // 4), (i % 4) * D
        total = total + xh[row + rows - 16 : row + rows, lane : lane + D].astype(F32)[15:16]
    weight_sum = jnp.sum(jnp.where(lane_d < 3, total, 0.0), axis=1, keepdims=True)
    rw[...] = jnp.broadcast_to(imp_ref[:, pl.ds(mine, width)].astype(F32) / weight_sum, (8, width))

    fwd = (eye, w, wh, vec, wt, vt, gsb, xt, mix, xh, gp, rstd, stream, mean, both, width)

    def during_forward(k):
        pl.when(k == 6)(lambda: gather_2(1))

    def emit_states(t):
        for c in range(0, width, CB):
            st_stage[t, c : c + CB, :] = nt(eye[...], xt[t + 1, 0:D, c : c + CB]).astype(BF)

    gather_1(1)
    forward_tower(0, fwd, during_forward, lambda: gather_3(1))
    gather_4(1)
    copies.leave(*range(len(copies.made)))
    unpack(1)
    forward_tower(1, fwd)
    emit_states(0)
    emit_states(1)
    out_rows = pl.ds(mine, width)
    st_copy = copies.add(lambda: st_stage.at[1 - core], lambda: st_out.at[out_rows], sibling)
    copies.start(st_copy)
    st_stay = pltpu.make_async_copy(st_stage.at[core], st_out.at[out_rows], local.at[1])
    st_stay.start()

    packed_of = [i for i in range(n) if plan.h_rows[i] or plan.v_rows[i]]
    owner = plan.v_rows.index(3 * (BLOCKS + 1))

    early = (2, 3)

    def piece(t, zz, b, lo, count):
        if t == 1 and zz in early:
            arena, first, q = dl, 0, 7 * early.index(zz) + b
        elif t == 1:
            arena, first, q = mix, BLOCKS * (D + 16), 7 * zz + b
        else:
            arena, first, q = xh, spare, 7 * zz + b
        row = pl.multiple_of(first + hrows * (q // 4) + lo, 16)
        return arena.at[pl.ds(row, count), pl.ds(pl.multiple_of((q % 4) * D, D), D)]

    def block(t, zz, b):
        return piece(t, zz, b, 0, hrows)

    def z_in(h, k, lo=0, count=hrows):
        return st_stage.at[0, pl.ds(pl.multiple_of(hrows * (h * (depth - 1) + k - 1) + lo, 16), count)]

    def z_out(t, zz, lo, count):
        if t == 1 and zz in early:
            return st_stage.at[1, pl.ds(hrows * early.index(zz) + lo, count)]
        return piece(t, zz, j_me, lo, count)

    def job_pieces(t, zz):
        return [(0, cut), (cut, hrows - cut)] if (t, zz) == (0, 0) else [(0, hrows)]

    def slot_half(t, i, lo):
        if i in packed_of:
            return packed.at[packed_of.index(i), pl.ds(pl.multiple_of(lo, 16), hrows)]
        return gw.at[t, pl.ds(pl.multiple_of(plan.a_base[i] + lo, 16), hrows)]

    j_x, j_y, j_d = near_x % 4, near_y % 4, near_xy % 4
    direct = ((0, 0), (0, 1), (0, 2), (1, 2), (1, 3))
    jobs = {}
    for t in range(2):
        for zz in range(depth):
            job = {}
            job["swap"] = [
                copies.add(lambda t=t, i=4 * zz + j: slot_half(t, i, other_low), lambda t=t, zz=zz, j=j: block(t, zz, j), sibling)
                for j in range(4)
            ]
            pieces = job_pieces(t, zz)
            for side, b, j, to in (("x", 5, j_x, to_x), ("y", 6, j_y, to_y), ("d", 4, j_d, to_d)):
                job[side] = [
                    copies.add(
                        lambda t=t, zz=zz, j=j, lo=lo, count=count: piece(t, zz, j, lo, count),
                        lambda t=t, zz=zz, b=b, lo=lo, count=count: piece(t, zz, b, lo, count),
                        to,
                    )
                    for lo, count in pieces
                    if side != "d" or (t, zz) in direct
                ]
            if (t, zz) not in direct:
                job["d"] = [
                    copies.add(
                        lambda t=t, zz=zz, lo=lo, count=count: piece(t, zz, j_d, lo, count),
                        lambda t=t, zz=zz, lo=lo, count=count: piece(t, zz, 4, lo, count),
                        to,
                    )
                    for to, lo, count in ((to_y, 0, cut), (to_x, cut, hrows - cut))
                ]
            job["z"] = [
                copies.add(
                    lambda t=t, zz=zz, lo=lo, count=count: z_out(t, zz, lo, count),
                    lambda zz=zz, lo=lo, count=count: z_in(core, (zz + depth - z_me) % depth, lo, count),
                    lambda t=t, zz=zz: at(t, 4 * zz + j_me),
                    lambda zz=zz, part=part: z_recv.at[(2 * part + core) * depth + (zz + depth - z_me) % depth],
                    lambda zz=zz: z_me != zz,
                )
                for part, (lo, count) in enumerate(pieces)
            ]
            jobs[t, zz] = job

    def pack(t, planes):
        wanted = [i for i in packed_of if i // 4 in planes]
        for i in wanted:
            a_rows, h_rows, h_off, h_first = plan.a_rows[i], plan.h_rows[i], plan.h_off[i], plan.h_first[i]
            to = packed.at[packed_of.index(i)]
            for part in scratch:
                part[...] = jnp.zeros(part.shape, F32)
            lo16, hi16 = h_first // 16 * 16, -(-(h_first + h_rows) // 16) * 16
            for half in range(2):
                for j in range(5 if h_rows else 0):
                    cols = slice(D * j + 128 * half, D * j + 128 * half + 128)
                    value = gh[t, lo16:hi16, cols].astype(F32)[h_first - lo16 : h_first - lo16 + h_rows]
                    scratch[half][pl.ds(h_off + j, h_rows, stride=5)] = value
            whole = jnp.concatenate([scratch[0][...], scratch[1][...]], 1)
            to[a_rows:rows] = whole[a_rows:].astype(BF)
            if a_rows:
                to[0:a_rows] = gw[t, plan.a_base[i] : plan.a_base[i] + a_rows]

    def plus(*refs):
        value = refs[0][...].astype(F32)
        for ref in refs[1:]:
            value = value + ref[...].astype(F32)
        return value

    def sum_0(t, zz):
        copies.start(*jobs[t, zz]["swap"])

    def sum_1(t, zz):
        job = jobs[t, zz]
        for j in range(4):
            copies.arrive(job["swap"][j])
            target = block(t, zz, j)
            target[...] = plus(slot_half(t, 4 * zz + j, low), target).astype(BF)
        if (t, zz) in direct:
            for x, y, d in zip(job["x"], job["y"], job["d"]):
                copies.start(x, y, d)
        else:
            copies.start(*job["d"])

    def sum_2(t, zz):
        job = jobs[t, zz]
        for side, copy, j, lo, count in (("x", job["d"][0], j_x, 0, cut), ("y", job["d"][1], j_y, cut, hrows - cut)):
            copies.arrive(copy)
            target = piece(t, zz, j, lo, count)
            target[...] = plus(target, piece(t, zz, 4, lo, count)).astype(BF)
            copies.start(*job[side])

    def sum_3(t, zz):
        job = jobs[t, zz]
        pieces = job_pieces(t, zz)
        for part, (lo, count) in enumerate(pieces):
            copies.arrive(job["x"][part], job["y"][part])
            value = plus(*(piece(t, zz, b, lo, count) for b in (j_me, 5, 6)))
            if (t, zz) in direct:
                copies.arrive(job["d"][part])
                value = value + piece(t, zz, 4, lo, count)[...].astype(F32)
            last = part == len(pieces) - 1

            @pl.when(z_me != zz)
            def _():
                z_out(t, zz, lo, count)[...] = value.astype(BF)
                copies.start(job["z"][part])

            @pl.when((z_me == zz) & (core == t))
            def _():
                owned[core, lo : lo + count] = value

            @pl.when((z_me == zz) & (core != t))
            def _():
                owned[2, lo : lo + count] = value
                if last:
                    copies.start(hand_over)

    def z_wait(h, k, part, lo, count):
        src = z_in(h, k, lo, count)
        pltpu.make_async_remote_copy(
            src_ref=src, dst_ref=src, send_sem=send.at[0], recv_sem=z_recv.at[(2 * part + h) * depth + k],
            device_id=sibling(), device_id_type=MESH,
        ).wait_recv()

    def sum_4():
        copies.arrive(hand_over)
        in_pieces = (z_me == 0) & (core == 0)
        for h in range(2):
            for k in range(1, depth):

                @pl.when(in_pieces)
                def _():
                    for part, (lo, count) in enumerate(job_pieces(0, 0)):
                        z_wait(h, k, part, lo, count)

                @pl.when((z_me != 0) | (core != 0))
                def _():
                    z_wait(h, k, 0, 0, hrows)

                final(h)[...] = final(h)[...] + z_in(h, k)[...].astype(F32)

    def final(h):
        return owned.at[h]

    outgo = owned.at[2]

    def vector_step(step):
        sources = [gv.at[1 - core], vacc.at[0], vacc.at[1]]
        along = [lambda k=k: at(core, (me + 4 * k) % n) for k in range(1, depth)]
        targets = [[sibling], [to_x, to_y, to_d], along]
        if step:
            base = gv[core] if step == 1 else vacc[step - 2]
            for number, k in vector_copies[-1]:
                copies.arrive(number)
                base = base + vin[k]
            vacc[step - 1] = base
        if step < 3:
            started = []
            for k, to in enumerate(targets[step], (0, 1, 4)[step]):
                number = copies.add(lambda step=step: sources[step], lambda k=k: vin.at[k], to)
                copies.start(number)
                started.append((number, k))
            vector_copies.append(started)

    vector_copies = []
    hand_over = copies.add(lambda: outgo, lambda: final(core), sibling)
    peers = [(1 - core, me), (core, near_x), (core, near_y), (core, near_xy)] + [(1 - core, (me + 4 * k) % n) for k in range(1, depth)] + [(core, (me + 4 * k) % n) for k in range(1, depth)]

    bwd = (eye, w, wh, vec, wht, vt, gsb, xt, mix, xh, gp, rstd, stream, ex, br, dm, acc, lg, dl, both, rw, gw, gh, gv, dm, width)
    ig_copies = [copies.add(lambda: dm, lambda: ig_out.at[out_rows], sibling, None, lambda t=t: core != t) for t in range(2)]

    def ig_local():
        return pltpu.make_async_copy(dm, ig_out.at[out_rows], local.at[2])

    def emit_inputs(t):
        pl.when(core == t)(lambda: ig_local().start())
        pl.when(core != t)(lambda: copies.start(ig_copies[t]))

    def free_inputs(t):
        pl.when(core == t)(lambda: ig_local().wait())
        pl.when(core != t)(lambda: copies.get(ig_copies[t]).wait_send())

    def signal_ready(which):
        for to_core, to_index in peers:
            pl.semaphore_signal(ready.at[which], inc=1, device_id=at(to_core, to_index), device_id_type=MESH)

    def wait_ready(which):
        pl.semaphore_wait(ready.at[which], len(peers))

    def schedule(i, steps):
        for step in sorted({s[0] for s in steps}):

            def run(step=step):
                for s, f, *args in steps:
                    if s == step:
                        f(*args)

            pl.when(i == step)(run)

    def after_head_1():
        copies.leave(st_copy)
        st_stay.wait()
        signal_ready(0)

    def during_backward_1(i):
        schedule(i, [
            (2, wait_ready, 0), (2, pack, 1, (3,)), (2, sum_0, 1, 3),
            (4, sum_1, 1, 3), (4, pack, 1, (2,)), (4, sum_0, 1, 2),
            (6, sum_1, 1, 2),
            (8, sum_3, 1, 3),
        ])

    ex[...] = jnp.zeros_like(ex)
    backward_tower(1, bwd, after_head_1, during_backward_1, None, lambda: sum_3(1, 2))
    emit_inputs(1)
    signal_ready(1)
    for zz in early:
        job = jobs[1, zz]
        copies.leave(*job["swap"], *job["d"], *job["x"], *job["y"])

    def after_head_0():
        wait_ready(1)
        sum_0(1, 1)
        sum_0(1, 0)
        pack(0, (3,))
        sum_0(0, 3)

    def during_backward_0(i):
        schedule(i, [
            (1, sum_1, 1, 1), (1, sum_1, 1, 0),
            (2, sum_1, 0, 3),
            (4, sum_2, 1, 1), (4, sum_2, 1, 0), (4, pack, 0, (2,)), (4, sum_0, 0, 2),
            (5, sum_2, 0, 3),
            (6, sum_1, 0, 2),
            (8, sum_3, 1, 1), (8, sum_3, 1, 0), (8, sum_0, 0, 1),
            (9, sum_3, 0, 3), (9, sum_1, 0, 1),
        ])

    def after_weights():
        sum_0(0, 0)
        vector_step(0)

    backward_tower(0, bwd, after_head_0, during_backward_0, lambda: free_inputs(1), after_weights)
    sum_1(0, 0)
    vector_step(1)
    emit_inputs(0)
    sum_3(0, 2)
    sum_3(0, 1)
    sum_3(0, 0)
    vector_step(2)
    sum_4()
    vector_step(3)

    slot128[...] = jnp.zeros(slot128.shape, F32)
    for h in range(2):
        slot128[pl.ds(2 * hrows * h, hrows, stride=2)] = final(h)[:, 0:128]
        slot128[pl.ds(2 * hrows * h + 1, hrows, stride=2)] = final(h)[:, 128:D]

    @pl.when(me == owner)
    def _():
        for kind in range(3):
            first = 2 * (plan.v_off[owner] + kind * (BLOCKS + 1))
            for h in range(2):
                value = vacc[2, kind, 0 : BLOCKS + 1, 128 * h : 128 * h + 128]
                slot128[pl.ds(first + h, BLOCKS + 1, stride=2)] = value

    def push(src, dst, to):
        number = copies.add(lambda: src, lambda: dst, lambda: to)
        copies.start(number)
        return copies.get(number)

    lay_flat(plan, me, slot128, flat, rolled)
    for c in moments:
        c.wait()
    update_shard(
        plan, me, params_in, first_new, second_new, (first_new, second_new, new, norm_out),
        flat, squares, sq_in, push, [to_x(), to_y(), to_d()], [at(core, (me + 4 * k) % n) for k in range(1, depth)],
    )
    copies.arrive(st_copy)
    pl.when(core == 0)(lambda: copies.arrive(ig_copies[0]))
    pl.when(core == 1)(lambda: copies.arrive(ig_copies[1]))
    free_inputs(0)
    copies.sent.update(ig_copies)
    assert len(copies.made) <= 11 * n
    copies.leave(*range(len(copies.made)))


def finish_kernel(st, ig, first, second, new, norms, st_out, ig_out, first_out, second_out, new_out, low_out, norms_out, *rest):
    *held, into, outof = rest
    moves = []
    for src, dst, mid, parts in zip((new, ig, st, first, second), (new_out, ig_out, st_out, first_out, second_out), held, (1, 8, 4, 1, 1)):
        rows = src.shape[0] // parts
        for i in range(parts):
            at_rows = pl.ds(i * rows, rows)
            number = len(moves)
            moves.append(
                (
                    pltpu.make_async_copy(src.at[at_rows], mid.at[at_rows], into.at[number]),
                    pltpu.make_async_copy(mid.at[at_rows], dst.at[at_rows], outof.at[number]),
                )
            )
    for load, _ in moves:
        load.start()
    for load, store in moves:
        load.wait()
        store.start()
    size = new.shape[1]
    for lo in range(0, size, 8192):
        hi = min(lo + 8192, size)
        low_out[0:1, lo:hi] = held[0][0:1, lo:hi].astype(BF)
    norms_out[...] = norms[...]
    for _, store in moves:
        store.wait()


def finish(st, ig, first, second, new, norms):
    vm = pl.BlockSpec(memory_space=pltpu.VMEM)
    hbm = pl.BlockSpec(memory_space=pl.ANY)
    arrays = (st, ig, first, second, new)
    shapes = [jax.ShapeDtypeStruct(v.shape, v.dtype) for v in arrays]
    return pl.pallas_call(
        finish_kernel,
        out_shape=(*shapes, jax.ShapeDtypeStruct(new.shape, BF), jax.ShapeDtypeStruct(norms.shape, F32)),
        in_specs=[hbm] * 5 + [vm],
        out_specs=(hbm,) * 5 + (vm,) * 2,
        scratch_shapes=[pltpu.VMEM(v.shape, v.dtype) for v in (new, ig, st, first, second)] + [pltpu.SemaphoreType.DMA((15,))] * 2,
        compiler_params=pltpu.CompilerParams(vmem_limit_bytes=62 * 1024 * 1024),
    )(st, ig, first, second, new, norms)


def train(plan, latent, codes, targets, visits, imp, params, first, second):
    n, rows = plan.n, plan.slot
    depth, hrows = n // 4, rows // 2
    width = codes.shape[1] // 2
    height = -(-params.shape[1] // 1024) * 8
    vm = pl.BlockSpec(memory_space=pltpu.VMEM)
    hbm = pl.BlockSpec(memory_space=pl.ANY)
    packed = sum(1 for h, v in zip(plan.h_rows, plan.v_rows) if h or v)
    return pl.pallas_call(
        functools.partial(train_kernel, plan),
        out_shape=(
            jax.ShapeDtypeStruct((2 * width, D), BF),
            jax.ShapeDtypeStruct((2 * width, D), F32),
            jax.ShapeDtypeStruct(params.shape, F32),
            jax.ShapeDtypeStruct(params.shape, F32),
            jax.ShapeDtypeStruct(params.shape, F32),
            jax.ShapeDtypeStruct((2, MATS), F32),
        ),
        in_specs=[hbm] + [vm] * 5 + [hbm] * 2,
        out_specs=(hbm, hbm, vm, vm, vm, vm),
        scratch_shapes=[
            pltpu.VMEM((2, A_ROWS, D), BF),
            pltpu.VMEM((2, D, HPAD), BF),
            pltpu.VMEM((2, 128, D), BF),
            pltpu.VMEM((2, 8, width), jnp.int32),
            pltpu.VMEM((8, width), jnp.int32),
            pltpu.VMEM((8, width), F32),
            *work_scratch(width),
            pltpu.VMEM((2, A_ROWS, D), BF),
            pltpu.VMEM((2, D, HPAD), BF),
            pltpu.VMEM((2, 3, 16, D), F32),
            pltpu.VMEM((packed, rows, D), BF),
            pltpu.VMEM((2, width, D), BF),
            pltpu.VMEM((max(2 * rows, height + 48) + 80, 128), F32),
            pltpu.VMEM((height + 128, 128), F32),
            pltpu.VMEM((height + 40, 128), F32),
            pltpu.VMEM((128, D), F32),
            pltpu.VMEM((3, 3, 16, D), F32),
            pltpu.VMEM((3 + depth, 3, 16, D), F32),
            pltpu.VMEM((3, hrows, D), F32),
            pltpu.VMEM((4, 32, 128), F32),
            pltpu.VMEM((2 + depth, 32, 128), F32),
            pltpu.VMEM((8, 128), F32),
            pltpu.SemaphoreType.DMA((11 * n,)),
            pltpu.SemaphoreType.DMA((11 * n,)),
            pltpu.SemaphoreType.DMA((4 * depth,)),
            pltpu.SemaphoreType.DMA((2 * (depth + 2),)),
            pltpu.SemaphoreType.DMA((5,)),
            pltpu.SemaphoreType.REGULAR((2,)),
        ],
        compiler_params=pltpu.CompilerParams(
            collective_id=2, has_side_effects=True, vmem_limit_bytes=63 * 1024 * 1024
        ),
    )(latent, codes, targets, visits, imp, params, first, second)


def on_device(latent, codes, targets, visits, importance, params, first_moment, second_moment):
    me = lax.axis_index("tower")
    row_count = latent.shape[0]
    half = row_count // 2
    shard_len = params.shape[1]
    plan = Plan(lax.axis_size("dp"), shard_len)
    if fused_fits(plan):
        states_out, inputs_out, first, second, new, norms = train(
            plan, latent, codes, targets.transpose(1, 0, 2), visits[0].T, importance[None], params, first_moment, second_moment
        )
        states_out, inputs_out, first, second, new, low, norms = finish(states_out, inputs_out, first, second, new, norms)
    else:
        height = -(-plan.rows128 // 8) * 8
        p128, m128, v128 = (
            jnp.pad(v, ((0, 0), (0, 128 * height - shard_len))).reshape(height, 128)
            for v in (params, first_moment, second_moment)
        )
        ints = jnp.concatenate([codes, targets[0, :1], visits[0].T, targets[0, 1:]], 0)
        x = lax.dynamic_slice_in_dim(latent, me * half, half, 0)
        w, wh, vec, both, rw = gather(plan, p128, ints, importance[None])
        st, ig, gw, gh, gv = compute(x, both, rw, w, wh, vec)
        states_out, inputs_out, *flat, norms = reduce_and_update(plan, gw, gh, gv, st, ig, p128, m128, v128)
        first, second, new = (v.reshape(1, -1)[:, :shard_len] for v in flat)
        low = new.astype(BF)
    return (states_out[None], inputs_out[None], first, second, new, low, norms[None])


def solution(mesh):
    in_specs = (
        P("dp", None),
        P("tower", "dp"),
        P("tower", None, "dp"),
        P("tower", "dp", None),
        P("dp"),
        P("tower", "dp"),
        P("tower", "dp"),
        P("tower", "dp"),
    )
    out_specs = (
        P("tower", "dp", None),
        P("tower", "dp", None),
        P("tower", "dp"),
        P("tower", "dp"),
        P("tower", "dp"),
        P("tower", "dp"),
        P("tower", None, None),
    )
    return jax.shard_map(
        on_device, mesh=mesh, in_specs=in_specs, out_specs=out_specs, check_vma=False
    )
```
